32 devices in a mesh: dp: 8 (over y, x, core), branch: 4 (over z).
Axes of the slice: x: 2, y: 2, z: 4, core: 2. Of those that a mesh axis runs over, the one named last changes fastest.
Arguments:
- frames: bfloat16 [8, 16, 14, 14, 832], P('dp', None, None, None, 'branch'), may hold values from -200 to 200
- lengths: int32 [8], P('dp'), may hold values from 2 to 16, as said below
- cotangent: bfloat16 [8, 8, 7, 7, 832], P('dp'), may hold values from -6 to 6
- pointwise: bfloat16 [2, 832, 576], replicated, may hold values from -0.21875 to 0.21875
- conv_mid: bfloat16 [2, 27, 160, 320], replicated, may hold values from -0.09375 to 0.09375
- conv_small: bfloat16 [2, 27, 32, 128], replicated, may hold values from -0.21875 to 0.21875
- gains: float32 [2, 1024], replicated, may hold values from 0.5 to 1.5
- shifts: float32 [2, 1024], replicated, may hold values from -2 to 2
Outputs:
- activations: bfloat16 [8, 8, 7, 7, 832], P('dp')
- input_grad: bfloat16 [8, 16, 14, 14, 832], P('dp', None, None, None, 'branch')
- pointwise_grad: float32 [2, 832, 576], replicated
- mid_grad: float32 [2, 27, 160, 320], replicated
- small_grad: float32 [2, 27, 32, 128], replicated
- gain_grad: float32 [2, 1024], replicated
- shift_grad: float32 [2, 1024], replicated
The draws below stay inside these ranges and needn't reach their ends.
Inputs may be any that keep to these rules, and one draw needn't show every extreme that they name: `lengths`: every length is even; some clip has all 16 frames.
All inputs are finite; a program needn't handle non-finite values.
Results may differ from the reference program's by a relative error of at most 0.013.
Values may be sent and summed in bfloat16 or wider, within the bound.
No kernel may reach another device: no remote copies, remote signals or barrier semaphores. Data moves between devices by JAX's collectives and lax.ppermute only.
A program may use at most 384 MiB of HBM per device.

```python
import jax
import jax.numpy as jnp
from jax import lax

DIRECT = 256
MID_IN = 160
MID_OUT = 320
SMALL_IN = 32
SMALL_OUT = 128
TAPS = 27
BLOCKS = 2
FRAMES = 16
SIDE = 14
CHANNELS = 832
SQUEEZED = 576
NORMED = 1024
CLIPS = 8


def draw_frames(key, part):
    key = jax.random.fold_in(key, 5)
    first_key, second_key, third_key = jax.random.split(key, 3)
    rising = 2.0 ** (2.0 * jnp.arange(CLIPS, dtype=jnp.float32) / max(CLIPS - 1, 1))
    clip_scale = rising * jax.random.uniform(first_key, (CLIPS,), jnp.float32, 0.8, 1.25)
    channel_scale = 10.0 ** jax.random.uniform(second_key, (CHANNELS,), jnp.float32)
    full_shape = (CLIPS, FRAMES, SIDE, SIDE, CHANNELS)
    pattern = jnp.clip(jax.random.normal(third_key, full_shape, jnp.float32), -4.0, 4.0)
    values = pattern * clip_scale[:, None, None, None, None] * channel_scale
    return values.astype(jnp.bfloat16)


def draw_lengths(key, part):
    key = jax.random.fold_in(key, 11)
    halves = jax.random.randint(key, (CLIPS,), 1, FRAMES // 2 + 1)
    return (2 * halves).at[0].set(FRAMES).astype(jnp.int32)


def block_levels(key, shape, cuts, least, top_value):
    loudness = 1.0
    for position, parts in cuts:
        heights = jax.random.uniform(jax.random.fold_in(jax.random.fold_in(key, 6), position), (parts,), jnp.float32, least / len(cuts), top_value / len(cuts))
        loudness = loudness * jnp.repeat(jnp.exp(heights), shape[position] // parts).reshape((-1,) + (1,) * (len(shape) - 1 - position))
    return loudness


def scatter_about(key, shape, scale, reach, pieces=(), held_as=jnp.bfloat16):
    level = block_levels(key, shape, pieces, -0.22, 0.18) if pieces else 1.0
    values = jax.random.normal(key, shape, jnp.float32) * scale * level
    return jnp.minimum(jnp.maximum(values, -reach), reach).astype(held_as)


def setup_inputs(seed: int = 0) -> dict:
    seeds = jax.random.split(jax.random.key(seed), 9)
    frames = draw_frames(jax.random.fold_in(seeds[8], 71), 0)
    lengths = draw_lengths(jax.random.fold_in(seeds[8], 71), 0)
    cotangent = scatter_about(seeds[2], (CLIPS, FRAMES // 2, SIDE // 2, SIDE // 2, CHANNELS), 1.0, 6.0, ((0, 8),))
    pointwise = scatter_about(seeds[3], (BLOCKS, CHANNELS, SQUEEZED), CHANNELS ** -0.5, 0.21875)
    conv_mid = scatter_about(seeds[4], (BLOCKS, TAPS, MID_IN, MID_OUT), (TAPS * MID_IN) ** -0.5, 0.09375)
    conv_small = scatter_about(seeds[5], (BLOCKS, TAPS, SMALL_IN, SMALL_OUT), (TAPS * SMALL_IN) ** -0.5, 0.21875)
    gains = jnp.clip(1.0 + 0.1 * jax.random.normal(seeds[6], (BLOCKS, NORMED), jnp.float32), 0.5, 1.5)
    shifts = scatter_about(seeds[7], (BLOCKS, NORMED), 0.5, 2.0, (), jnp.float32)
    return dict(frames=frames, lengths=lengths, cotangent=cotangent, pointwise=pointwise, conv_mid=conv_mid, conv_small=conv_small, gains=gains, shifts=shifts)


@jax.custom_vjp
def low(v):
    return lax.optimization_barrier(v.astype(jnp.bfloat16)).astype(jnp.float32)

@jax.custom_vjp
def low_back(v):
    return v

def low_keep(v):
    return (low(v), None)

def low_pass(kept, grad):
    return (grad,)

def back_keep(v):
    return (v, None)

def back_low(kept, grad):
    return (low(grad),)
low.defvjp(low_keep, low_pass)
low_back.defvjp(back_keep, back_low)
highest = lax.Precision.HIGHEST

def box_sum(values):
    for dimension in (1, 2, 3):
        extent = values.shape[dimension]
        widths = [(0, 0)] * 5
        widths[dimension] = (1, 1)
        padded = jnp.pad(values, widths)
        values = lax.slice_in_dim(padded, 0, extent, axis=dimension) + lax.slice_in_dim(padded, 1, extent + 1, axis=dimension) + lax.slice_in_dim(padded, 2, extent + 2, axis=dimension)
    return values

def pool_mean(values, frame_mask):
    counts = box_sum(jnp.broadcast_to(frame_mask, values.shape[:4] + (1,)))
    return box_sum(values) / jnp.maximum(counts, 1.0)

def normalize(pre_act, gain_vec, shift_vec, frame_mask, voxel_count):
    masked_sum = lax.optimization_barrier(jnp.sum(pre_act * frame_mask, axis=(0, 1, 2, 3)))
    square = lax.optimization_barrier(jnp.sum(pre_act * pre_act * frame_mask, axis=(0, 1, 2, 3)))
    center = masked_sum / voxel_count
    spread = square / voxel_count - center * center
    scaled = (pre_act - center) * lax.rsqrt(spread + 1e-05)
    return jax.nn.silu(gain_vec * scaled + shift_vec) * frame_mask

def convolve(values, kernel):
    kernel_five = kernel.reshape(3, 3, 3, kernel.shape[1], kernel.shape[2])
    return lax.conv_general_dilated(values, kernel_five, (1, 1, 1), 'SAME', dimension_numbers=('NDHWC', 'DHWIO', 'NDHWC'), precision=highest)

def inception(inputs, frame_mask, voxel_count, pointwise_w, mid_kernel, small_kernel, gain_vec, shift_vec):
    first_cut = DIRECT
    second_cut = DIRECT + MID_IN
    third_cut = DIRECT + MID_IN + SMALL_IN
    direct = low_back(jnp.dot(inputs, pointwise_w[:, :third_cut], precision=highest))
    before_pool = low_back(jnp.dot(inputs, pointwise_w[:, third_cut:], precision=highest))
    first_pre = jnp.concatenate([direct, pool_mean(before_pool, frame_mask)], axis=-1)
    first_act = low(normalize(first_pre, gain_vec[:SQUEEZED], shift_vec[:SQUEEZED], frame_mask, voxel_count))
    middle = low_back(convolve(first_act[..., first_cut:second_cut], mid_kernel))
    smaller = low_back(convolve(first_act[..., second_cut:third_cut], small_kernel))
    second_pre = jnp.concatenate([middle, smaller], axis=-1)
    second_act = low(normalize(second_pre, gain_vec[SQUEEZED:], shift_vec[SQUEEZED:], frame_mask, voxel_count))
    return jnp.concatenate([first_act[..., :first_cut], second_act, first_act[..., third_cut:]], axis=-1)

def forward(inputs, pointwise_w, mid_kernel, small_kernel, gain_vec, shift_vec, lengths):
    frame_ids = jnp.arange(FRAMES, dtype=jnp.int32)
    mask_first = (frame_ids[None, :] < lengths[:, None]).astype(jnp.float32)[:, :, None, None, None]
    count_first = jnp.sum(lengths).astype(jnp.float32) * (SIDE * SIDE)
    hidden = inception(inputs * mask_first, mask_first, count_first, pointwise_w[0], mid_kernel[0], small_kernel[0], gain_vec[0], shift_vec[0])
    grouped = hidden.reshape(CLIPS, FRAMES // 2, 2, SIDE // 2, 2, SIDE // 2, 2, hidden.shape[-1])
    pooled = low(lax.optimization_barrier(jnp.mean(grouped, axis=(2, 4, 6))))
    halves = lengths // 2
    mask_second = (frame_ids[None, :FRAMES // 2] < halves[:, None]).astype(jnp.float32)[:, :, None, None, None]
    count_second = jnp.sum(halves).astype(jnp.float32) * (SIDE // 2 * (SIDE // 2))
    return inception(pooled, mask_second, count_second, pointwise_w[1], mid_kernel[1], small_kernel[1], gain_vec[1], shift_vec[1])

def reference(frames, lengths, cotangent, pointwise, conv_mid, conv_small, gains, shifts):

    def wrapped(inputs, pointwise_w, mid_kernel, small_kernel, gain_vec, shift_vec):
        return forward(inputs, pointwise_w, mid_kernel, small_kernel, gain_vec, shift_vec, lengths)
    outputs, pullback = jax.vjp(wrapped, frames.astype(jnp.float32), pointwise.astype(jnp.float32), conv_mid.astype(jnp.float32), conv_small.astype(jnp.float32), gains, shifts)
    gradients = pullback(cotangent.astype(jnp.float32))
    return (outputs.astype(jnp.bfloat16), gradients[0].astype(jnp.bfloat16), gradients[1], gradients[2], gradients[3], gradients[4], gradients[5])
```

```python
import functools

import jax
import jax.numpy as jnp
from jax import lax
from jax.experimental import pallas as pl
from jax.experimental.pallas import tpu as pltpu
from jax.sharding import PartitionSpec as P

DIRECT = 256
MID_IN = 160
MID_OUT = 320
SMALL_IN = 32
SMALL_OUT = 128
TAPS = 27
CHANNELS = 832
SQUEEZED = 576
PITCH = 16
REDUCED = 256
POOLED = 128
FIRST = 640
SECOND = 512
OUTER = 896
TAP_ROWS = 432
EPSILON = 1e-05
F32 = jnp.float32
BF16 = jnp.bfloat16
VMEM_BYTES = 58 * 2**20


def call(body, out_shape, scratch=(), scalars=0, flops=10**9):
    def run(*operands):
        specs = [
            pl.BlockSpec(memory_space=pltpu.SMEM if number < scalars else pltpu.VMEM)
            for number in range(len(operands))
        ]
        return pl.pallas_call(
            body,
            out_shape=out_shape,
            in_specs=specs,
            out_specs=jax.tree.map(lambda _: pl.BlockSpec(memory_space=pltpu.VMEM), out_shape),
            scratch_shapes=list(scratch),
            compiler_params=pltpu.CompilerParams(vmem_limit_bytes=VMEM_BYTES),
            cost_estimate=pl.CostEstimate(
                flops=flops, bytes_accessed=16 * 2**20, transcendentals=0
            ),
        )(*operands)

    return run


def shape(dims, dtype):
    return jax.ShapeDtypeStruct(tuple(dims), dtype)


def rows_at(start, size):
    return pl.ds(pl.multiple_of(start, 16), size)


def frame_flag(frame, length):
    return jnp.where(frame < length, 1.0, 0.0).astype(F32)


def row_geometry(side, width):
    row = lax.broadcasted_iota(jnp.int32, (side * PITCH, width), 0)
    column, line = (row & (PITCH - 1), row >> 4)
    valid = jnp.where(column < side, 1.0, 0.0)

    def near(place):
        return 3.0 - jnp.where(place == 0, 1.0, 0.0) - jnp.where(place == side - 1, 1.0, 0.0)

    return (valid, near(line) * near(column))


def plane_box(values):
    rows = values.shape[0]
    across = values + pltpu.roll(values, 1, 0) + pltpu.roll(values, rows - 1, 0)
    edge = jnp.zeros((PITCH, values.shape[1]), values.dtype)
    return (
        across
        + jnp.concatenate([across[PITCH:], edge], axis=0)
        + jnp.concatenate([edge, across[:-PITCH]], axis=0)
    )


def box_scale(frame, length, window):
    frames = frame_flag(frame, length) + frame_flag(frame + 1, length)
    frames = frames + jnp.where(frame > 0, frame_flag(frame - 1, length), 0.0)
    return 1.0 / jnp.maximum(frames * window, 1.0)


def sigmoid(value):
    return 0.5 * jnp.tanh(0.5 * value) + 0.5


def silu(value):
    return value * sigmoid(value)


def silu_slope(value):
    gate = sigmoid(value)
    return gate * (1.0 + value * (1.0 - gate))


def partial_sum(values):
    rows, width = values.shape
    return jnp.sum(values.reshape(rows // 8, 8, width), axis=0)


def moments(total, square, count):
    center = total / count
    return (center, lax.rsqrt(square / count - center * center + EPSILON))


def total_of(gathered):
    total = gathered[0]
    for number in range(1, gathered.shape[0]):
        total = total + gathered[number]
    return total


def pool_matrix(side, transposed):
    wide = 2 * side
    few, many = (side * PITCH, 2 * wide * PITCH)
    dims = (many, few) if transposed else (few, many)
    coarse = lax.broadcasted_iota(jnp.int32, dims, 1 if transposed else 0)
    fine = lax.broadcasted_iota(jnp.int32, dims, 0 if transposed else 1)
    fine = jnp.where(fine >= wide * PITCH, fine - wide * PITCH, fine)
    same = (
        ((fine >> 4) >> 1 == coarse >> 4)
        & ((fine & (PITCH - 1)) >> 1 == coarse & (PITCH - 1))
        & ((fine & (PITCH - 1)) < wide)
    )
    return jnp.where(same, 0.125, 0.0).astype(BF16)


class Grid:
    def __init__(self, frames, side):
        self.frames, self.side = (frames, side)
        self.frame_rows = side * PITCH
        self.rows = frames * self.frame_rows
        self.pitch = (side + 1) * PITCH
        self.lead = self.pitch + PITCH
        self.padded = (frames + 2) * self.pitch + 2 * PITCH
        self.group = 2 if side > 8 else 4


def zero_rows(ref):
    rows = ref.shape[0]
    step = 16
    while rows % (step * 2) == 0 and step < 256:
        step = step * 2

    @pl.loop(0, rows // step)
    def _(number):
        ref[rows_at(number * step, step), :] = jnp.zeros((step, ref.shape[1]), ref.dtype)


def store_taps(grid, taps_ref, frame, act):
    rows = grid.frame_rows
    at = rows_at(grid.lead + frame * grid.pitch, rows)
    taps_ref[at, 0:REDUCED] = pltpu.roll(act, 1, 0).astype(BF16)
    taps_ref[at, REDUCED : 2 * REDUCED] = act.astype(BF16)
    taps_ref[at, 2 * REDUCED : 3 * REDUCED] = pltpu.roll(act, rows - 1, 0).astype(BF16)


def convolve(grid, taps_ref, kernel_ref, acc_ref, e_ref, sums_ref, length, valid):
    group_rows = grid.group * grid.pitch
    sums_ref[...] = jnp.zeros_like(sums_ref)
    wide_valid = jnp.concatenate([valid] * (SECOND // 128), axis=1)

    @pl.loop(0, grid.frames // grid.group)
    def _(group):
        base = grid.lead + group * group_rows
        for tap in range(9):
            start = base + (tap // 3 - 1) * grid.pitch + (tap % 3 - 1) * PITCH
            part = jnp.dot(
                taps_ref[rows_at(start, group_rows), :], kernel_ref[tap], preferred_element_type=F32
            )
            acc_ref[...] = part if tap == 0 else acc_ref[...] + part
        for number in range(grid.group):
            frame = group * grid.group + number
            values = acc_ref[number * grid.pitch : number * grid.pitch + grid.frame_rows, :]
            e_ref[rows_at(frame * grid.frame_rows, grid.frame_rows), :] = values
            masked = values * (wide_valid * frame_flag(frame, length))
            sums_ref[0:8] += partial_sum(masked)
            sums_ref[8:16] += partial_sum(masked * values)


def write_sums(out_ref, sums_ref, lo, hi):
    for number in range(2):
        out_ref[number : number + 1, lo:hi] = jnp.sum(
            sums_ref[8 * number : 8 * number + 8], axis=0, keepdims=True
        )


def first_pointwise(grid, local, parts, count_ref, x_ref, p_ref, mid_ref, pool_ref, direct_ref, sums_ref, u_ref):
    rows = local * grid.frame_rows
    wide = 2 * grid.frame_rows
    count = count_ref[0]

    @pl.loop(0, local // 2)
    def _(pair):
        at = rows_at(pair * wide, wide)
        total = jnp.dot(x_ref[0, at, :], p_ref[0], preferred_element_type=F32)
        for part in range(1, parts):
            total = total + jnp.dot(x_ref[part, at, :], p_ref[part], preferred_element_type=F32)
        u_ref[at, :] = total

    def summed(pair, carry):
        values = u_ref[rows_at(pair * wide, wide), :]
        return (carry[0] + partial_sum(values), carry[1] + partial_sum(values * values))

    zero = jnp.zeros((8, FIRST), F32)
    total, square = lax.fori_loop(0, local // 2, summed, (zero, zero))
    total = jnp.sum(total, axis=0, keepdims=True)
    square = jnp.sum(square, axis=0, keepdims=True)
    sums_ref[0:1, :] = total[:, :SECOND]
    sums_ref[1:2, :] = square[:, :SECOND]
    sums_ref[2:3, :] = jnp.full((1, SECOND), count, F32)
    offset = (total / jnp.full((1, FIRST), jnp.maximum(count, 1.0), F32)).astype(BF16)
    wide_offset = offset.astype(F32)
    tail = jnp.broadcast_to(wide_offset, (PITCH, FIRST)).astype(BF16)
    places = ((direct_ref, 0, DIRECT), (mid_ref, DIRECT, 2 * DIRECT), (pool_ref, SECOND, FIRST))
    for ref, lo, hi in places:
        ref[rows : rows + PITCH, :] = tail[:, lo:hi]

    @pl.loop(0, local)
    def _(frame):
        at = rows_at(frame * grid.frame_rows, grid.frame_rows)
        for ref, lo, hi in places:
            ref[at, :] = (u_ref[at, lo:hi] - wide_offset[:, lo:hi]).astype(BF16)


def each_frame(grid, local, parts, place, refs, visit):
    rows = local * grid.frame_rows
    for step, ref in enumerate(refs):
        source = lax.rem(place - step + parts, parts)
        offset = ref[rows : rows + PITCH, :].astype(F32)[0:1]

        @pl.loop(0, local)
        def _(number):
            at = rows_at(number * grid.frame_rows, grid.frame_rows)
            visit(source * local + number, ref[at, :].astype(F32) + offset)


def first_convolve(grid, local, parts, length_ref, place_ref, *refs):
    mids, sums, (gain_ref, shift_ref, kernel_ref), rest = (
        refs[:parts],
        refs[parts : 2 * parts],
        refs[2 * parts : 2 * parts + 3],
        refs[2 * parts + 3 :],
    )
    h_ref, taps_ref, e_ref, out_sums_ref, moment_ref, acc_ref, sums_ref = rest
    length = length_ref[0]
    total = sums[0][...]
    for ref in sums[1:]:
        total = total + ref[...]
    count = total[2:3]
    center, inverse = moments(total[0:1], total[1:2], count)
    moment_ref[0:1, :] = center
    moment_ref[1:2, :] = inverse
    moment_ref[2:3, :] = count
    center, inverse = (center[:, DIRECT:SECOND], inverse[:, DIRECT:SECOND])
    valid, _ = row_geometry(grid.side, 128)
    wide_valid = jnp.concatenate([valid, valid], axis=1)
    zero_rows(taps_ref)

    def visit(frame, values):
        scaled = (values - center) * inverse
        h_ref[rows_at(frame * grid.frame_rows, grid.frame_rows), :] = scaled.astype(BF16)
        act = silu(gain_ref[...] * scaled + shift_ref[...])
        store_taps(grid, taps_ref, frame, act * (wide_valid * frame_flag(frame, length)))

    each_frame(grid, local, parts, place_ref[0], mids, visit)
    convolve(grid, taps_ref, kernel_ref, acc_ref, e_ref, sums_ref, length, valid)
    write_sums(out_sums_ref, sums_ref, 0, SECOND)


def pool_planes(grid, plane_ref, q_ref, lo, sums_ref, length, valid, window):
    rows = grid.frame_rows
    sums_ref[...] = jnp.zeros_like(sums_ref)

    @pl.loop(0, grid.frames)
    def _(frame):
        start = frame * rows
        values = (
            plane_ref[rows_at(start, rows), :]
            + plane_ref[rows_at(start + rows, rows), :]
            + plane_ref[rows_at(start + 2 * rows, rows), :]
        ) * box_scale(frame, length, window)
        q_ref[rows_at(start, rows), lo : lo + POOLED] = values
        masked = values * (valid * frame_flag(frame, length))
        sums_ref[0:8] += partial_sum(masked)
        sums_ref[8:16] += partial_sum(masked * values)


def first_pool(grid, local, parts, length_ref, place_ref, *refs):
    pools, (q_ref, out_sums_ref, plane_ref, sums_ref) = (refs[:parts], refs[parts:])
    length = length_ref[0]
    valid, window = row_geometry(grid.side, POOLED)
    rows = grid.frame_rows
    plane_ref[0:rows] = jnp.zeros((rows, POOLED), F32)
    plane_ref[grid.rows + rows : grid.rows + 2 * rows] = jnp.zeros((rows, POOLED), F32)

    def visit(frame, values):
        plane_ref[rows_at((frame + 1) * rows, rows), :] = plane_box(values)

    each_frame(grid, local, parts, place_ref[0], pools, visit)
    pool_planes(grid, plane_ref, q_ref, 0, sums_ref, length, valid, window)
    write_sums(out_sums_ref, sums_ref, 0, POOLED)


def outer_moments(first_moment, second_sums, pool_at):
    count = first_moment[2:3, 0:1]
    total = total_of(second_sums)
    center, inverse = moments(total[0:1], total[1:2], first_moment[2:3, 0:128][:, 0:1])
    return (center, inverse, count)


def first_output(grid, small, local, parts, length_ref, place_ref, *refs):
    directs, rest = (refs[:parts], refs[parts:])
    q_ref, e_ref, moment_ref, sums_ref, gain_ref, shift_ref, pooled_ref, h_ref, outer_ref = rest
    length = length_ref[0]
    valid, _ = row_geometry(grid.side, 128)
    wide_valid = jnp.concatenate([valid] * (OUTER // 128), axis=1)
    total = total_of(sums_ref)
    count = jnp.concatenate([moment_ref[2:3, 0:128]] * 7, axis=1)
    center, inverse = moments(total[0:1], total[1:2], count[:, :FIRST])
    center = jnp.concatenate([moment_ref[0:1, :DIRECT], center], axis=1)
    inverse = jnp.concatenate([moment_ref[1:2, :DIRECT], inverse], axis=1)
    outer_ref[0:1, :] = center
    outer_ref[1:2, :] = inverse
    outer_ref[2:3, :] = count
    matrix = pool_matrix(small.side, False)
    rows = grid.frame_rows
    local_rows = local * rows
    for step, ref in enumerate(directs):
        source = lax.rem(place_ref[0] - step + parts, parts)
        offset = ref[local_rows : local_rows + PITCH, :].astype(F32)[0:1]

        @pl.loop(0, local // 2)
        def _(pair):
            acts = []
            for number in range(2):
                frame = source * local + 2 * pair + number
                at = rows_at(frame * rows, rows)
                direct = ref[rows_at((2 * pair + number) * rows, rows), :].astype(F32) + offset
                values = jnp.concatenate([direct, e_ref[at, :], q_ref[at, :]], axis=1)
                scaled = (values - center) * inverse
                h_ref[at, :] = scaled.astype(BF16)
                act = silu(gain_ref[...] * scaled + shift_ref[...])
                acts.append((act * (wide_valid * frame_flag(frame, length))).astype(BF16))
            coarse = source * (local // 2) + pair
            pooled_ref[rows_at(coarse * small.frame_rows, small.frame_rows), :] = jnp.dot(
                matrix, jnp.concatenate(acts, axis=0), preferred_element_type=F32
            ).astype(BF16)


def second_pointwise(grid, length_ref, count_ref, x_ref, p_ref, q_ref, out_sums_ref, plane_ref, sums_ref, pool_sums_ref):
    length = length_ref[0]
    rows = grid.frame_rows
    wide = 2 * rows
    valid, window = row_geometry(grid.side, POOLED)
    sums_ref[...] = jnp.zeros_like(sums_ref)
    plane_ref[0:rows] = jnp.zeros((rows, POOLED), F32)
    plane_ref[grid.rows + rows : grid.rows + 2 * rows] = jnp.zeros((rows, POOLED), F32)

    @pl.loop(0, grid.frames // 2)
    def _(pair):
        at = rows_at(pair * wide, wide)
        values = jnp.dot(x_ref[at, :], p_ref[...], preferred_element_type=F32)
        q_ref[at, 0:SECOND] = values[:, :SECOND]
        sums_ref[0:8] += partial_sum(values[:, :SECOND])
        sums_ref[8:16] += partial_sum(values[:, :SECOND] * values[:, :SECOND])
        for number in range(2):
            plane_ref[rows_at((2 * pair + number + 1) * rows, rows), :] = plane_box(
                values[number * rows : (number + 1) * rows, SECOND:]
            )

    pool_planes(grid, plane_ref, q_ref, SECOND, pool_sums_ref, length, valid, window)
    write_sums(out_sums_ref, sums_ref, 0, SECOND)
    write_sums(out_sums_ref, pool_sums_ref, SECOND, FIRST)
    out_sums_ref[2:3, :] = jnp.full((1, FIRST), count_ref[0], F32)


def second_convolve(grid, length_ref, q_ref, sums_in_ref, gain_ref, shift_ref, kernel_ref, h_ref, taps_ref, e_ref, out_sums_ref, moment_ref, acc_ref, sums_ref):
    length = length_ref[0]
    total = total_of(sums_in_ref)
    count = total[2:3]
    center, inverse = moments(total[0:1], total[1:2], count)
    moment_ref[0:1, :] = center
    moment_ref[1:2, :] = inverse
    moment_ref[2:3, :] = count
    center, inverse = (center[:, DIRECT:SECOND], inverse[:, DIRECT:SECOND])
    valid, _ = row_geometry(grid.side, 128)
    wide_valid = jnp.concatenate([valid, valid], axis=1)
    zero_rows(taps_ref)

    @pl.loop(0, grid.frames)
    def _(frame):
        at = rows_at(frame * grid.frame_rows, grid.frame_rows)
        scaled = (q_ref[at, DIRECT:SECOND] - center) * inverse
        h_ref[at, :] = scaled.astype(BF16)
        act = silu(gain_ref[...] * scaled + shift_ref[...])
        store_taps(grid, taps_ref, frame, act * (wide_valid * frame_flag(frame, length)))

    convolve(grid, taps_ref, kernel_ref, acc_ref, e_ref, sums_ref, length, valid)
    write_sums(out_sums_ref, sums_ref, 0, SECOND)


def second_output(grid, length_ref, q_ref, e_ref, moment_ref, sums_in_ref, gain_ref, shift_ref, cot_ref, act_ref, h_ref, outer_ref, out_sums_ref, sums_ref):
    length = length_ref[0]
    valid, _ = row_geometry(grid.side, 128)
    wide_valid = jnp.concatenate([valid] * (OUTER // 128), axis=1)
    total = total_of(sums_in_ref)
    count = jnp.concatenate([moment_ref[2:3, 0:128]] * 7, axis=1)
    center, inverse = moments(total[0:1], total[1:2], count[:, :SECOND])
    center = jnp.concatenate([moment_ref[0:1, :DIRECT], center, moment_ref[0:1, SECOND:]], axis=1)
    inverse = jnp.concatenate([moment_ref[1:2, :DIRECT], inverse, moment_ref[1:2, SECOND:]], axis=1)
    outer_ref[0:1, :] = center
    outer_ref[1:2, :] = inverse
    outer_ref[2:3, :] = count
    sums_ref[...] = jnp.zeros_like(sums_ref)

    @pl.loop(0, grid.frames)
    def _(frame):
        at = rows_at(frame * grid.frame_rows, grid.frame_rows)
        values = jnp.concatenate([q_ref[at, :DIRECT], e_ref[at, :], q_ref[at, SECOND:]], axis=1)
        scaled = (values - center) * inverse
        h_ref[at, :] = scaled.astype(BF16)
        mask = wide_valid * frame_flag(frame, length)
        shifted = gain_ref[...] * scaled + shift_ref[...]
        gate = sigmoid(shifted)
        act_ref[at, :] = (shifted * gate * mask).astype(BF16)
        slope = gate * (1.0 + shifted * (1.0 - gate))
        error = cot_ref[at, :].astype(F32) * slope * mask
        sums_ref[0:8] += partial_sum(error)
        sums_ref[8:16] += partial_sum(error * scaled)

    write_sums(out_sums_ref, sums_ref, 0, OUTER)


def outer_gradient(grid, small, grad_ref, matrix, frame, lo, hi):
    if small is None:
        return grad_ref[rows_at(frame * grid.frame_rows, grid.frame_rows), lo:hi].astype(F32)
    coarse = grad_ref[rows_at((frame // 2) * small.frame_rows, small.frame_rows), lo:hi]
    return jnp.dot(matrix, coarse, preferred_element_type=F32)


def spread_matrix(grid, small):
    return None if small is None else pool_matrix(small.side, True)[: grid.frame_rows]


def first_outer_sums(grid, small, length_ref, h_ref, gain_ref, shift_ref, grad_ref, out_sums_ref, sums_ref):
    length = length_ref[0]
    valid, _ = row_geometry(grid.side, 128)
    wide_valid = jnp.concatenate([valid] * (OUTER // 128), axis=1)
    matrix = spread_matrix(grid, small)
    sums_ref[...] = jnp.zeros_like(sums_ref)

    @pl.loop(0, grid.frames)
    def _(frame):
        at = rows_at(frame * grid.frame_rows, grid.frame_rows)
        scaled = h_ref[at, :].astype(F32)
        slope = silu_slope(gain_ref[...] * scaled + shift_ref[...])
        grad = outer_gradient(grid, small, grad_ref, matrix, frame, 0, OUTER)
        error = grad * slope * (wide_valid * frame_flag(frame, length))
        sums_ref[0:8] += partial_sum(error)
        sums_ref[8:16] += partial_sum(error * scaled)

    write_sums(out_sums_ref, sums_ref, 0, OUTER)


def conv_back(grid, small, length_ref, h_ref, outer_ref, sums_in_ref, gain_ref, shift_ref, grad_ref, kernel_ref, reduced_ref, reduced_gain_ref, reduced_shift_ref, d_ref, r_ref, out_sums_ref, total_ref, acc_ref, sums_ref):
    length = length_ref[0]
    valid, _ = row_geometry(grid.side, 128)
    total = total_of(sums_in_ref)
    total_ref[...] = total
    lo, hi = (DIRECT, DIRECT + SECOND)
    count = outer_ref[2:3, lo:hi]
    mean_r = total[0:1, lo:hi] / count
    mean_rh = total[1:2, lo:hi] / count
    gain, shift = (gain_ref[:, lo:hi], shift_ref[:, lo:hi])
    factor = gain * outer_ref[1:2, lo:hi]
    wide_valid = jnp.concatenate([valid] * (SECOND // 128), axis=1)
    matrix = spread_matrix(grid, small)
    zero_rows(d_ref)

    @pl.loop(0, grid.frames)
    def _(frame):
        at = rows_at(frame * grid.frame_rows, grid.frame_rows)
        scaled = h_ref[at, lo:hi].astype(F32)
        grad = outer_gradient(grid, small, grad_ref, matrix, frame, lo, hi)
        error = grad * silu_slope(gain * scaled + shift)
        back = factor * (error - mean_r - scaled * mean_rh)
        d_ref[rows_at(grid.lead + frame * grid.pitch, grid.frame_rows), :] = (
            back * (wide_valid * frame_flag(frame, length))
        ).astype(BF16)

    group_rows = grid.group * grid.pitch
    sums_ref[...] = jnp.zeros_like(sums_ref)
    reduced_valid = jnp.concatenate([valid, valid], axis=1)

    @pl.loop(0, grid.frames // grid.group)
    def _(group):
        base = grid.lead + group * group_rows
        for tap in range(9):
            start = base - (tap // 3 - 1) * grid.pitch - (tap % 3 - 1) * PITCH
            part = lax.dot_general(
                d_ref[rows_at(start, group_rows), :],
                kernel_ref[tap],
                (((1,), (1,)), ((), ())),
                preferred_element_type=F32,
            )
            acc_ref[...] = part if tap == 0 else acc_ref[...] + part
        for number in range(grid.group):
            frame = group * grid.group + number
            rows = grid.frame_rows
            lines = slice(number * grid.pitch, number * grid.pitch + rows)
            back = (
                pltpu.roll(acc_ref[lines, 0:REDUCED], rows - 1, 0)
                + acc_ref[lines, REDUCED : 2 * REDUCED]
                + pltpu.roll(acc_ref[lines, 2 * REDUCED : 3 * REDUCED], 1, 0)
            )
            at = rows_at(frame * rows, rows)
            scaled = reduced_ref[at, :].astype(F32)
            slope = silu_slope(reduced_gain_ref[...] * scaled + reduced_shift_ref[...])
            error = back * slope * (reduced_valid * frame_flag(frame, length))
            r_ref[at, :] = error.astype(BF16)
            sums_ref[0:8] += partial_sum(error)
            sums_ref[8:16] += partial_sum(error * scaled)

    write_sums(out_sums_ref, sums_ref, 0, REDUCED)


def kernel_grads(grid, slots, first_ref, taps_ref, d_ref, out_ref, acc_ref):
    group_rows = grid.group * grid.pitch
    acc_ref[...] = jnp.zeros_like(acc_ref)

    @pl.loop(0, grid.frames // grid.group)
    def _(group):
        base = grid.lead + group * group_rows
        right = d_ref[rows_at(base, group_rows), :]
        for slot in range(slots):
            tap = jnp.minimum(first_ref[0] + slot, TAPS - 1)
            start = base + (tap // 9 - 1) * grid.pitch + (lax.rem(tap // 3, 3) - 1) * PITCH
            lanes = pl.ds(pl.multiple_of(lax.rem(tap, 3) * REDUCED, REDUCED), REDUCED)
            left = taps_ref[rows_at(start, group_rows), lanes]
            acc_ref[slot] += lax.dot_general(
                left, right, (((0,), (0,)), ((), ())), preferred_element_type=F32
            )

    for slot in range(slots):
        base = slot * TAP_ROWS
        for tile in range(2):
            out_ref[base + MID_IN * tile : base + MID_IN * (tile + 1), :] = acc_ref[
                slot, 0:MID_IN, 128 * tile : 128 * (tile + 1)
            ].astype(BF16)
        half = MID_IN // 2
        folded = acc_ref[slot, 0:half, 256:384] + pltpu.roll(
            acc_ref[slot, half:MID_IN, 256:384], 64, 1
        )
        base = base + 2 * MID_IN
        out_ref[base : base + half, :] = folded.astype(BF16)
        base = base + half
        out_ref[base : base + SMALL_IN, :] = acc_ref[
            slot, MID_IN : MID_IN + SMALL_IN, 384:512
        ].astype(BF16)
    used = slots * TAP_ROWS
    if out_ref.shape[0] > used:
        out_ref[used:, :] = jnp.zeros((out_ref.shape[0] - used, 128), BF16)


def point_back(grid, small, kept, length_ref, place_ref, h_ref, outer_ref, total_ref, gain_ref, shift_ref, grad_ref, reduced_ref, r_ref, moment_ref, sums_in_ref, reduced_gain_ref, x_ref, p_ref, dx_ref, dp_ref, reduced_total_ref, du_ref, plane_ref, acc_ref):
    length = length_ref[0]
    rows = grid.frame_rows
    valid, window = row_geometry(grid.side, 128)
    matrix = spread_matrix(grid, small)
    total = total_of(sums_in_ref)
    reduced_total_ref[...] = total
    count = outer_ref[2:3, 0:128]
    count = jnp.concatenate([count, count], axis=1)
    mid_r, mid_rh = (total[0:1] / count, total[1:2] / count)
    mid_factor = reduced_gain_ref[...] * moment_ref[1:2, DIRECT:SECOND]
    two = jnp.concatenate([valid, valid], axis=1)
    plane_ref[0:rows] = jnp.zeros((rows, POOLED), F32)
    plane_ref[grid.rows + rows : grid.rows + 2 * rows] = jnp.zeros((rows, POOLED), F32)

    def section(frame, lo, hi, mask):
        at = rows_at(frame * rows, rows)
        scaled = h_ref[at, lo:hi].astype(F32)
        gain, shift = (gain_ref[:, lo:hi], shift_ref[:, lo:hi])
        grad = outer_gradient(grid, small, grad_ref, matrix, frame, lo, hi)
        error = grad * silu_slope(gain * scaled + shift)
        size = outer_ref[2:3, lo:hi]
        inner = error - total_ref[0:1, lo:hi] / size - scaled * (total_ref[1:2, lo:hi] / size)
        return (gain * outer_ref[1:2, lo:hi]) * inner * mask

    @pl.loop(0, grid.frames)
    def _(frame):
        at = rows_at(frame * rows, rows)
        flag = frame_flag(frame, length)
        du_ref[at, 0:DIRECT] = section(frame, 0, DIRECT, two * flag).astype(BF16)
        scaled = reduced_ref[at, :].astype(F32)
        inner = r_ref[at, :].astype(F32) - mid_r - scaled * mid_rh
        du_ref[at, DIRECT:SECOND] = (mid_factor * inner * (two * flag)).astype(BF16)
        pool = section(frame, OUTER - POOLED, OUTER, valid * flag)
        plane_ref[rows_at((frame + 1) * rows, rows), :] = plane_box(
            pool * box_scale(frame, length, window)
        )

    wide = 2 * rows
    acc_ref[...] = jnp.zeros_like(acc_ref)

    @pl.loop(0, grid.frames // 2)
    def _(pair):
        start = pair * wide
        at = rows_at(start, wide)
        pool = (
            plane_ref[at, :]
            + plane_ref[rows_at(start + rows, wide), :]
            + plane_ref[rows_at(start + 2 * rows, wide), :]
        ) * jnp.concatenate([valid, valid], axis=0)
        du = jnp.concatenate([du_ref[at, 0:SECOND], pool.astype(BF16)], axis=1)
        dx_ref[at, :] = lax.dot_general(
            du, p_ref[...], (((1,), (1,)), ((), ())), preferred_element_type=F32
        ).astype(BF16)
        acc_ref[...] += lax.dot_general(
            x_ref[at, :], du, (((0,), (0,)), ((), ())), preferred_element_type=F32
        )

    first = pl.multiple_of(place_ref[0] * kept, 16) if kept < acc_ref.shape[0] else 0
    own = acc_ref[pl.ds(first, kept), :]
    for tile in range(FIRST // 128):
        dp_ref[kept * tile : kept * (tile + 1), :] = own[:, 128 * tile : 128 * (tile + 1)].astype(
            BF16
        )
    used = (FIRST // 128) * kept
    if dp_ref.shape[0] > used:
        dp_ref[used:, :] = jnp.zeros((dp_ref.shape[0] - used, 128), BF16)


def unpack_taps(first_ref, second_ref, mid_ref, small_ref):
    half = MID_IN // 2
    for number, ref in enumerate((first_ref, second_ref)):
        values = ref[0].astype(F32)
        folded = values[2 * MID_IN : 2 * MID_IN + half]
        mid_ref[number, 0, :, 0:128] = values[0:MID_IN]
        mid_ref[number, 0, :, 128:256] = values[MID_IN : 2 * MID_IN]
        mid_ref[number, 0, 0:half, 256:320] = folded[:, 0:64]
        mid_ref[number, 0, half:MID_IN, 256:320] = pltpu.roll(folded, 64, 1)[:, 0:64]
        small_ref[number, 0] = values[2 * MID_IN + half : TAP_ROWS]


def unpack_point(parts, first_ref, second_ref, out_ref):
    kept = CHANNELS // parts
    for part in range(parts):
        for tile in range(FIRST // 128):
            values = first_ref[part, kept * tile : kept * (tile + 1), :].astype(F32)
            at = slice(kept * part, kept * (part + 1))
            place_columns(out_ref, 0, at, tile, values)
    kept = OUTER // parts
    for part in range(parts):
        for tile in range(FIRST // 128):
            start = kept * part
            while start < kept * (part + 1):
                stop = kept * (part + 1)
                if start < SQUEEZED:
                    stop, moved = (min(stop, SQUEEZED), 0)
                elif start < FIRST:
                    start = min(stop, FIRST)
                    continue
                else:
                    moved = 64
                source = kept * tile + start - kept * part
                values = second_ref[part, source : source + stop - start, :].astype(F32)
                place_columns(out_ref, 1, slice(start - moved, stop - moved), tile, values)
                start = stop


def place_columns(out_ref, block, at, tile, values):
    if tile < 3:
        out_ref[block, at, 128 * tile : 128 * (tile + 1)] = values
    elif tile == 3:
        out_ref[block, at, 384:448] = values[:, 0:64]
    else:
        out_ref[block, at, 448:576] = values


def outer_vector(values):
    gap = jnp.zeros((64,), F32)
    return jnp.concatenate(
        [values[:256], values[576:896], gap, values[896:1024], values[448:576]]
    ).reshape(1, OUTER)


def reduced_vector(values):
    return jnp.pad(values[256:448], (0, 64)).reshape(1, REDUCED)


def norm_vector(outer, reduced):
    return jnp.concatenate(
        [outer[:256], reduced[:192], outer[768:896], outer[256:576], outer[640:768]]
    )


def wide_kernels(conv_mid, conv_small):
    mid = jnp.pad(conv_mid, ((0, 0), (0, 96), (0, 192)))
    small = jnp.pad(conv_small, ((0, 0), (160, 64), (384, 0)))
    return (mid + small).reshape(9, 3 * REDUCED, SECOND)


def point_columns(point):
    gap = jnp.zeros((point.shape[0], 64), point.dtype)
    return jnp.concatenate([point[:, :448], gap, point[:, 448:]], axis=1)


def round_up(value, unit):
    return -(-value // unit) * unit


def spread_over(values, axis, size):
    received = [values]
    for step in range(1, size):
        perm = [(source, (source + step) % size) for source in range(size)]
        received.append(lax.ppermute(values, axis, perm))
    return received


def after(values, earlier):
    return lax.optimization_barrier((values, earlier))[0]


def summed_everywhere(packed):
    share = lax.psum_scatter(packed, "dp", scatter_dimension=0, tiled=True)
    whole = lax.all_gather(share, ("branch", "dp"), axis=0, tiled=True)
    return whole.reshape(-1, packed.shape[0], 128)


def on_device(frames, lengths, cotangent, pointwise, conv_mid, conv_small, gains, shifts):
    parts = lax.axis_size("branch")
    clips = lax.axis_size("dp")
    place = lax.axis_index("branch").astype(jnp.int32)
    count_frames, side = (frames.shape[1], frames.shape[2])
    grid, small = (Grid(count_frames, side), Grid(count_frames // 2, side // 2))
    local = count_frames // parts
    own_channels = frames.shape[-1]
    length = lengths.astype(jnp.int32)
    half_length = length // 2
    place_one = place.reshape(1)

    ids = jnp.arange(count_frames, dtype=jnp.int32)
    mask = (ids < length[0]).astype(BF16)[:, None, None, None]
    own = jnp.pad(frames[0] * mask, ((0, 0), (0, 0), (0, PITCH - side), (0, 0)))
    own = own.reshape(grid.rows, own_channels)
    by_frames = lax.all_to_all(
        own.reshape(parts, local * grid.frame_rows, own_channels), "branch", 0, 0, tiled=True
    )

    columns = [point_columns(pointwise[0]), point_columns(pointwise[1])]
    point_first = columns[0].reshape(parts, own_channels, FIRST)
    point_own = lax.dynamic_slice_in_dim(columns[0], place * own_channels, own_channels, 0)
    point_second = jnp.concatenate(
        [columns[1][:576], jnp.zeros((64, FIRST), BF16), columns[1][576:]], axis=0
    )
    kernels = [wide_kernels(conv_mid[number], conv_small[number]) for number in range(2)]
    outer_gain = [outer_vector(gains[number]) for number in range(2)]
    outer_shift = [outer_vector(shifts[number]) for number in range(2)]
    reduced_gain = [reduced_vector(gains[number]) for number in range(2)]
    reduced_shift = [reduced_vector(shifts[number]) for number in range(2)]
    cot = cotangent[0]
    cot = jnp.concatenate(
        [cot[..., :576], jnp.zeros(cot.shape[:3] + (64,), BF16), cot[..., 576:]], axis=-1
    )
    cot = jnp.pad(cot, ((0, 0), (0, 0), (0, PITCH - small.side), (0, 0))).reshape(small.rows, OUTER)

    local_rows = local * grid.frame_rows
    valid_frames = jnp.clip(length - place * local, 0, local)
    local_count = valid_frames.astype(F32) * float(side * side)
    mid, pool, direct, sums = call(
        functools.partial(first_pointwise, grid, local, parts),
        (
            shape((local_rows + PITCH, REDUCED), BF16),
            shape((local_rows + PITCH, POOLED), BF16),
            shape((local_rows + PITCH, DIRECT), BF16),
            shape((3, SECOND), F32),
        ),
        [pltpu.VMEM((local_rows, FIRST), F32)],
        scalars=1,
    )(local_count, by_frames, point_first)
    mids = spread_over(mid, "branch", parts)
    sums = jnp.sum(lax.all_gather(sums, "dp"), axis=0)
    all_sums = spread_over(sums, "branch", parts)
    pools = spread_over(after(pool, mids), "branch", parts)
    directs = spread_over(after(direct, pools), "branch", parts)
    group_rows = grid.group * grid.pitch
    h_reduced, taps, e, e_sums, moment = call(
        functools.partial(first_convolve, grid, local, parts),
        (
            shape((grid.rows, REDUCED), BF16),
            shape((grid.padded, 3 * REDUCED), BF16),
            shape((grid.rows, SECOND), F32),
            shape((2, SECOND), F32),
            shape((3, SECOND), F32),
        ),
        [pltpu.VMEM((group_rows, SECOND), F32), pltpu.VMEM((16, SECOND), F32)],
        scalars=2,
        flops=2 * 10**10,
    )(length, place_one, *mids, *all_sums, reduced_gain[0], reduced_shift[0], kernels[0])
    q_pool, pool_sums = call(
        functools.partial(first_pool, grid, local, parts),
        (shape((grid.rows, POOLED), F32), shape((2, POOLED), F32)),
        [
            pltpu.VMEM((grid.rows + 2 * grid.frame_rows, POOLED), F32),
            pltpu.VMEM((16, POOLED), F32),
        ],
        scalars=2,
    )(length, place_one, *pools)
    second_sums = lax.all_gather(jnp.concatenate([e_sums, pool_sums], axis=1), "dp")
    pooled, h_outer, outer = call(
        functools.partial(first_output, grid, small, local, parts),
        (
            shape((small.rows, OUTER), BF16),
            shape((grid.rows, OUTER), BF16),
            shape((3, OUTER), F32),
        ),
        scalars=2,
    )(length, place_one, *directs, q_pool, e, moment, second_sums, outer_gain[0], outer_shift[0])

    small_count = half_length.astype(F32) * float(small.side * small.side)
    q_small, sums_small = call(
        functools.partial(second_pointwise, small),
        (shape((small.rows, FIRST), F32), shape((3, FIRST), F32)),
        [
            pltpu.VMEM((small.rows + 2 * small.frame_rows, POOLED), F32),
            pltpu.VMEM((16, SECOND), F32),
            pltpu.VMEM((16, POOLED), F32),
        ],
        scalars=2,
    )(half_length, small_count, pooled, point_second)
    sums_small = lax.all_gather(sums_small, "dp")
    small_group = small.group * small.pitch
    h_reduced_small, taps_small, e_small, e_sums_small, moment_small = call(
        functools.partial(second_convolve, small),
        (
            shape((small.rows, REDUCED), BF16),
            shape((small.padded, 3 * REDUCED), BF16),
            shape((small.rows, SECOND), F32),
            shape((2, SECOND), F32),
            shape((3, FIRST), F32),
        ),
        [pltpu.VMEM((small_group, SECOND), F32), pltpu.VMEM((16, SECOND), F32)],
        scalars=1,
    )(half_length, q_small, sums_small, reduced_gain[1], reduced_shift[1], kernels[1])
    e_sums_small = lax.all_gather(e_sums_small, "dp")
    act, h_outer_small, outer_small, outer_sums_small = call(
        functools.partial(second_output, small),
        (
            shape((small.rows, OUTER), BF16),
            shape((small.rows, OUTER), BF16),
            shape((3, OUTER), F32),
            shape((2, OUTER), F32),
        ),
        [pltpu.VMEM((16, OUTER), F32)],
        scalars=1,
    )(half_length, q_small, e_small, moment_small, e_sums_small, outer_gain[1], outer_shift[1], cot)

    slots = -(-TAPS // parts)
    tap_rows = round_up(slots * TAP_ROWS, 16 * clips)
    first_tap = place_one * slots

    def back(at, coarse, number, span, h_out, outer_moment, outer_sums, grad, h_red, taps_of, moment_of, x, point, kept):
        gathered = lax.all_gather(outer_sums, "dp")
        rows = at.group * at.pitch
        d_low, r_low, sums_low, total = call(
            functools.partial(conv_back, at, coarse),
            (
                shape((at.padded, SECOND), BF16),
                shape((at.rows, REDUCED), BF16),
                shape((2, REDUCED), F32),
                shape((2, OUTER), F32),
            ),
            [pltpu.VMEM((rows, 3 * REDUCED), F32), pltpu.VMEM((16, REDUCED), F32)],
            scalars=1,
            flops=2 * 10**10 if coarse is not None else 10**9,
        )(
            span,
            h_out,
            outer_moment,
            gathered,
            outer_gain[number],
            outer_shift[number],
            grad,
            kernels[number],
            h_red,
            reduced_gain[number],
            reduced_shift[number],
        )
        packed_taps = call(
            functools.partial(kernel_grads, at, slots),
            shape((tap_rows, 128), BF16),
            [pltpu.VMEM((slots, REDUCED, SECOND), F32)],
            scalars=1,
        )(first_tap, taps_of, d_low)
        gathered = lax.all_gather(sums_low, "dp")
        point_rows = round_up(kept * (FIRST // 128), 16 * clips)
        dx, packed_point, reduced_total = call(
            functools.partial(point_back, at, coarse, kept),
            (
                shape((at.rows, x.shape[1]), BF16),
                shape((point_rows, 128), BF16),
                shape((2, REDUCED), F32),
            ),
            [
                pltpu.VMEM((at.rows, SECOND), BF16),
                pltpu.VMEM((at.rows + 2 * at.frame_rows, POOLED), F32),
                pltpu.VMEM((x.shape[1], FIRST), F32),
            ],
            scalars=2,
        )(
            span,
            place_one,
            h_out,
            outer_moment,
            total,
            outer_gain[number],
            outer_shift[number],
            grad,
            h_red,
            r_low,
            moment_of,
            gathered,
            reduced_gain[number],
            x,
            point,
        )
        norms = [norm_vector(total[row], reduced_total[row]) for row in range(2)]
        return (dx, packed_taps, packed_point, norms)

    dx_small, taps_packed_small, point_packed_small, norms_small = back(
        small, None, 1, half_length, h_outer_small, outer_small, outer_sums_small, cot,
        h_reduced_small, taps_small, moment_small, pooled, point_second, OUTER // parts,
    )
    outer_sums = call(
        functools.partial(first_outer_sums, grid, small),
        shape((2, OUTER), F32),
        [pltpu.VMEM((16, OUTER), F32)],
        scalars=1,
    )(length, h_outer, outer_gain[0], outer_shift[0], dx_small)
    dx, taps_packed, point_packed, norms = back(
        grid, small, 0, length, h_outer, outer, outer_sums, dx_small,
        h_reduced, taps, moment, own, point_own, own_channels,
    )

    taps_small_whole = summed_everywhere(taps_packed_small)
    point_small_whole = summed_everywhere(point_packed_small)
    taps_whole = summed_everywhere(taps_packed)
    point_whole = summed_everywhere(point_packed)
    block = pl.BlockSpec((1, TAP_ROWS, 128), lambda tap: (tap // slots, tap % slots, 0))
    mid_grad, small_grad = pl.pallas_call(
        unpack_taps,
        grid=(TAPS,),
        in_specs=[block, block],
        out_specs=(
            pl.BlockSpec((2, 1, MID_IN, MID_OUT), lambda tap: (0, tap, 0, 0)),
            pl.BlockSpec((2, 1, SMALL_IN, SMALL_OUT), lambda tap: (0, tap, 0, 0)),
        ),
        out_shape=(
            shape((2, TAPS, MID_IN, MID_OUT), F32),
            shape((2, TAPS, SMALL_IN, SMALL_OUT), F32),
        ),
    )(taps_whole, taps_small_whole)
    point_grad = call(
        functools.partial(unpack_point, parts), shape((2, CHANNELS, SQUEEZED), F32)
    )(point_whole, point_small_whole)
    act = act.reshape(1, small.frames, small.side, PITCH, OUTER)[:, :, :, : small.side]
    act = jnp.concatenate([act[..., :576], act[..., 640:]], axis=-1)
    input_grad = dx.reshape(1, grid.frames, side, PITCH, own_channels)[:, :, :, :side]
    input_grad = input_grad * mask[None]
    gain_grad = jnp.stack([norms[1], norms_small[1]])
    shift_grad = jnp.stack([norms[0], norms_small[0]])
    return (act, input_grad, point_grad, mid_grad, small_grad, gain_grad, shift_grad)


def solution(mesh):
    split = P("dp", None, None, None, "branch")
    whole = P("dp", None, None, None, None)
    return jax.shard_map(
        on_device,
        mesh=mesh,
        in_specs=(split, P("dp"), whole, P(), P(), P(), P(), P()),
        out_specs=(whole, split, P(), P(), P(), P(), P()),
        check_vma=False,
    )
```

```python
import functools

import jax
import jax.numpy as jnp
from jax import lax
from jax.experimental import pallas as pl
from jax.experimental.pallas import tpu as pltpu
from jax.sharding import PartitionSpec as P

DIRECT = 256
MID_IN = 160
MID_OUT = 320
SMALL_IN = 32
SMALL_OUT = 128
TAPS = 27
CHANNELS = 832
SQUEEZED = 576
PITCH = 16
REDUCED = 256
POOLED = 128
FIRST = 640
SECOND = 512
OUTER = 896
TAP_ROWS = 432
EPSILON = 1e-05
F32 = jnp.float32
BF16 = jnp.bfloat16
VMEM_BYTES = 58 * 2**20


def call(body, out_shape, scratch=(), scalars=0, flops=10**9, out_space=pltpu.VMEM, aliases=None):
    aliases = aliases or {}

    def run(*operands):
        specs = [
            pl.BlockSpec(
                memory_space=pl.ANY
                if number in aliases
                else pltpu.SMEM
                if number < scalars
                else pltpu.VMEM
            )
            for number in range(len(operands))
        ]
        return pl.pallas_call(
            body,
            out_shape=out_shape,
            in_specs=specs,
            out_specs=jax.tree.map(lambda _: pl.BlockSpec(memory_space=out_space), out_shape),
            input_output_aliases=aliases,
            scratch_shapes=list(scratch),
            compiler_params=pltpu.CompilerParams(vmem_limit_bytes=VMEM_BYTES),
            cost_estimate=pl.CostEstimate(
                flops=flops, bytes_accessed=16 * 2**20, transcendentals=0
            ),
        )(*operands)

    return run


def shape(dims, dtype):
    return jax.ShapeDtypeStruct(tuple(dims), dtype)


def rows_at(start, size):
    return pl.ds(pl.multiple_of(start, 16), size)


def frame_flag(frame, length):
    return jnp.where(frame < length, 1.0, 0.0).astype(F32)


def row_geometry(side, width):
    row = lax.broadcasted_iota(jnp.int32, (side * PITCH, width), 0)
    column, line = (row & (PITCH - 1), row >> 4)
    valid = jnp.where(column < side, 1.0, 0.0)

    def near(place):
        return 3.0 - jnp.where(place == 0, 1.0, 0.0) - jnp.where(place == side - 1, 1.0, 0.0)

    return (valid, near(line) * near(column))


def plane_box(values):
    rows = values.shape[0]
    across = values + pltpu.roll(values, 1, 0) + pltpu.roll(values, rows - 1, 0)
    edge = jnp.zeros((PITCH, values.shape[1]), values.dtype)
    return (
        across
        + jnp.concatenate([across[PITCH:], edge], axis=0)
        + jnp.concatenate([edge, across[:-PITCH]], axis=0)
    )


def box_scale(frame, length, window):
    frames = frame_flag(frame, length) + frame_flag(frame + 1, length)
    frames = frames + jnp.where(frame > 0, frame_flag(frame - 1, length), 0.0)
    return 1.0 / jnp.maximum(frames * window, 1.0)


def sigmoid(value):
    return 0.5 * jnp.tanh(0.5 * value) + 0.5


def silu(value):
    return value * sigmoid(value)


def silu_slope(value):
    gate = sigmoid(value)
    return gate * (1.0 + value * (1.0 - gate))


def partial_sum(values):
    rows, width = values.shape
    return jnp.sum(values.reshape(rows // 8, 8, width), axis=0)


def moments(total, square, count):
    center = total / count
    return (center, lax.rsqrt(square / count - center * center + EPSILON))


def total_of(gathered):
    total = gathered[0]
    for number in range(1, gathered.shape[0]):
        total = total + gathered[number]
    return total


def pool_matrix(side, transposed):
    wide = 2 * side
    few, many = (side * PITCH, 2 * wide * PITCH)
    dims = (many, few) if transposed else (few, many)
    coarse = lax.broadcasted_iota(jnp.int32, dims, 1 if transposed else 0)
    fine = lax.broadcasted_iota(jnp.int32, dims, 0 if transposed else 1)
    fine = jnp.where(fine >= wide * PITCH, fine - wide * PITCH, fine)
    same = (
        ((fine >> 4) >> 1 == coarse >> 4)
        & ((fine & (PITCH - 1)) >> 1 == coarse & (PITCH - 1))
        & ((fine & (PITCH - 1)) < wide)
    )
    return jnp.where(same, 0.125, 0.0).astype(BF16)


class Grid:
    def __init__(self, frames, side):
        self.frames, self.side = (frames, side)
        self.frame_rows = side * PITCH
        self.rows = frames * self.frame_rows
        self.pitch = (side + 1) * PITCH
        self.lead = self.pitch + PITCH
        self.padded = (frames + 2) * self.pitch + 2 * PITCH
        self.group = 2 if side > 8 else 4


def zero_rows(ref):
    rows = ref.shape[0]
    step = 16
    while rows % (step * 2) == 0 and step < 256:
        step = step * 2

    @pl.loop(0, rows // step)
    def _(number):
        ref[rows_at(number * step, step), :] = jnp.zeros((step, ref.shape[1]), ref.dtype)


def store_taps(grid, taps_ref, frame, act):
    rows = grid.frame_rows
    at = rows_at(grid.lead + frame * grid.pitch, rows)
    taps_ref[at, 0:REDUCED] = pltpu.roll(act, 1, 0).astype(BF16)
    taps_ref[at, REDUCED : 2 * REDUCED] = act.astype(BF16)
    taps_ref[at, 2 * REDUCED : 3 * REDUCED] = pltpu.roll(act, rows - 1, 0).astype(BF16)


def convolve(grid, taps_ref, kernel_ref, acc_ref, e_ref, sums_ref, length, valid):
    group_rows = grid.group * grid.pitch
    sums_ref[...] = jnp.zeros_like(sums_ref)
    wide_valid = jnp.concatenate([valid] * (SECOND // 128), axis=1)

    @pl.loop(0, grid.frames // grid.group)
    def _(group):
        base = grid.lead + group * group_rows
        for tap in range(9):
            start = base + (tap // 3 - 1) * grid.pitch + (tap % 3 - 1) * PITCH
            part = jnp.dot(
                taps_ref[rows_at(start, group_rows), :], kernel_ref[tap], preferred_element_type=F32
            )
            acc_ref[...] = part if tap == 0 else acc_ref[...] + part
        for number in range(grid.group):
            frame = group * grid.group + number
            values = acc_ref[number * grid.pitch : number * grid.pitch + grid.frame_rows, :]
            e_ref[rows_at(frame * grid.frame_rows, grid.frame_rows), :] = values
            masked = values * (wide_valid * frame_flag(frame, length))
            sums_ref[0:8] += partial_sum(masked)
            sums_ref[8:16] += partial_sum(masked * values)


def write_sums(out_ref, sums_ref, lo, hi):
    for number in range(2):
        out_ref[number : number + 1, lo:hi] = jnp.sum(
            sums_ref[8 * number : 8 * number + 8], axis=0, keepdims=True
        )


def first_pointwise(grid, local, parts, count_ref, x_ref, p_ref, mid_ref, pool_ref, direct_ref, sums_ref, u_ref):
    rows = local * grid.frame_rows
    wide = 2 * grid.frame_rows
    count = count_ref[0]
    for part in range(parts):
        product = lax.dot_general(
            x_ref[part], p_ref[part], (((0,), (0,)), ((), ())), preferred_element_type=F32
        )
        u_ref[...] = product if part == 0 else u_ref[...] + product

    def summed(pair, carry):
        values = u_ref[rows_at(pair * wide, wide), :]
        return (carry[0] + partial_sum(values), carry[1] + partial_sum(values * values))

    zero = jnp.zeros((8, FIRST), F32)
    total, square = lax.fori_loop(0, local // 2, summed, (zero, zero))
    total = jnp.sum(total, axis=0, keepdims=True)
    square = jnp.sum(square, axis=0, keepdims=True)
    sums_ref[0:1, :] = total[:, :SECOND]
    sums_ref[1:2, :] = square[:, :SECOND]
    sums_ref[2:3, :] = jnp.full((1, SECOND), count, F32)
    offset = (total / jnp.full((1, FIRST), jnp.maximum(count, 1.0), F32)).astype(BF16)
    wide_offset = offset.astype(F32)
    tail = jnp.broadcast_to(wide_offset, (PITCH, FIRST)).astype(BF16)
    places = ((direct_ref, 0, DIRECT), (mid_ref, DIRECT, 2 * DIRECT), (pool_ref, SECOND, FIRST))
    for ref, lo, hi in places:
        ref[rows : rows + PITCH, :] = tail[:, lo:hi]

    @pl.loop(0, local)
    def _(frame):
        at = rows_at(frame * grid.frame_rows, grid.frame_rows)
        for ref, lo, hi in places:
            ref[at, :] = (u_ref[at, lo:hi] - wide_offset[:, lo:hi]).astype(BF16)


def each_frame(grid, local, parts, place, refs, visit):
    rows = local * grid.frame_rows
    for step, ref in enumerate(refs):
        source = lax.rem(place - step + parts, parts)
        offset = ref[rows : rows + PITCH, :].astype(F32)[0:1]

        @pl.loop(0, local)
        def _(number):
            at = rows_at(number * grid.frame_rows, grid.frame_rows)
            visit(source * local + number, ref[at, :].astype(F32) + offset)


def first_convolve(grid, local, parts, length_ref, place_ref, *refs):
    mids, sums, (gain_ref, shift_ref, kernel_ref), rest = (
        refs[:parts],
        refs[parts : 2 * parts],
        refs[2 * parts : 2 * parts + 3],
        refs[2 * parts + 3 :],
    )
    h_ref, taps_ref, e_ref, out_sums_ref, moment_ref, acc_ref, sums_ref = rest
    length = length_ref[0]
    total = sums[0][...]
    for ref in sums[1:]:
        total = total + ref[...]
    count = total[2:3]
    center, inverse = moments(total[0:1], total[1:2], count)
    moment_ref[0:1, :] = center
    moment_ref[1:2, :] = inverse
    moment_ref[2:3, :] = count
    center, inverse = (center[:, DIRECT:SECOND], inverse[:, DIRECT:SECOND])
    valid, _ = row_geometry(grid.side, 128)
    wide_valid = jnp.concatenate([valid, valid], axis=1)
    zero_rows(taps_ref)

    def visit(frame, values):
        scaled = (values - center) * inverse
        h_ref[rows_at(frame * grid.frame_rows, grid.frame_rows), :] = scaled.astype(BF16)
        act = silu(gain_ref[...] * scaled + shift_ref[...])
        store_taps(grid, taps_ref, frame, act * (wide_valid * frame_flag(frame, length)))

    each_frame(grid, local, parts, place_ref[0], mids, visit)
    convolve(grid, taps_ref, kernel_ref, acc_ref, e_ref, sums_ref, length, valid)
    write_sums(out_sums_ref, sums_ref, 0, SECOND)


def pool_planes(grid, plane_ref, q_ref, lo, sums_ref, length, valid, window):
    rows = grid.frame_rows
    sums_ref[...] = jnp.zeros_like(sums_ref)

    @pl.loop(0, grid.frames)
    def _(frame):
        start = frame * rows
        values = (
            plane_ref[rows_at(start, rows), :]
            + plane_ref[rows_at(start + rows, rows), :]
            + plane_ref[rows_at(start + 2 * rows, rows), :]
        ) * box_scale(frame, length, window)
        q_ref[rows_at(start, rows), lo : lo + POOLED] = values
        masked = values * (valid * frame_flag(frame, length))
        sums_ref[0:8] += partial_sum(masked)
        sums_ref[8:16] += partial_sum(masked * values)


def first_pool(grid, local, parts, length_ref, place_ref, *refs):
    pools, (q_ref, out_sums_ref, plane_ref, sums_ref) = (refs[:parts], refs[parts:])
    length = length_ref[0]
    valid, window = row_geometry(grid.side, POOLED)
    rows = grid.frame_rows
    plane_ref[0:rows] = jnp.zeros((rows, POOLED), F32)
    plane_ref[grid.rows + rows : grid.rows + 2 * rows] = jnp.zeros((rows, POOLED), F32)

    def visit(frame, values):
        plane_ref[rows_at((frame + 1) * rows, rows), :] = plane_box(values)

    each_frame(grid, local, parts, place_ref[0], pools, visit)
    pool_planes(grid, plane_ref, q_ref, 0, sums_ref, length, valid, window)
    write_sums(out_sums_ref, sums_ref, 0, POOLED)


def outer_moments(first_moment, second_sums, pool_at):
    count = first_moment[2:3, 0:1]
    total = total_of(second_sums)
    center, inverse = moments(total[0:1], total[1:2], first_moment[2:3, 0:128][:, 0:1])
    return (center, inverse, count)


def first_output(grid, small, local, parts, length_ref, place_ref, *refs):
    directs, rest = (refs[:parts], refs[parts:])
    q_ref, e_ref, moment_ref, sums_ref, gain_ref, shift_ref, *rest = rest
    pooled_ref, h_ref, slope_ref, outer_ref, pooled_slope_ref, pooled_product_ref = rest
    length = length_ref[0]
    valid, _ = row_geometry(grid.side, 128)
    wide_valid = jnp.concatenate([valid] * (OUTER // 128), axis=1)
    total = total_of(sums_ref)
    count = jnp.concatenate([moment_ref[2:3, 0:128]] * 7, axis=1)
    center, inverse = moments(total[0:1], total[1:2], count[:, :FIRST])
    center = jnp.concatenate([moment_ref[0:1, :DIRECT], center], axis=1)
    inverse = jnp.concatenate([moment_ref[1:2, :DIRECT], inverse], axis=1)
    outer_ref[0:1, :] = center
    outer_ref[1:2, :] = inverse
    outer_ref[2:3, :] = count
    matrix = pool_matrix(small.side, False)
    rows = grid.frame_rows
    local_rows = local * rows
    for step, ref in enumerate(directs):
        source = lax.rem(place_ref[0] - step + parts, parts)
        offset = ref[local_rows : local_rows + PITCH, :].astype(F32)[0:1]

        @pl.loop(0, local // 2)
        def _(pair):
            acts, slopes, products = ([], [], [])
            for number in range(2):
                frame = source * local + 2 * pair + number
                at = rows_at(frame * rows, rows)
                direct = ref[rows_at((2 * pair + number) * rows, rows), :].astype(F32) + offset
                values = jnp.concatenate([direct, e_ref[at, :], q_ref[at, :]], axis=1)
                scaled = (values - center) * inverse
                h_ref[at, :] = scaled.astype(BF16)
                shifted = gain_ref[...] * scaled + shift_ref[...]
                gate = sigmoid(shifted)
                mask = wide_valid * frame_flag(frame, length)
                gate_mask = gate * mask
                act = shifted * gate_mask
                slope = gate_mask + act * (1.0 - gate)
                low_slope = slope.astype(BF16)
                slope_ref[at, :] = low_slope
                acts.append(act.astype(BF16))
                slopes.append(low_slope)
                products.append((slope * scaled).astype(BF16))
            at = rows_at((source * (local // 2) + pair) * small.frame_rows, small.frame_rows)
            for ref_out, pieces in (
                (pooled_ref, acts),
                (pooled_slope_ref, slopes),
                (pooled_product_ref, products),
            ):
                ref_out[at, :] = jnp.dot(
                    matrix, jnp.concatenate(pieces, axis=0), preferred_element_type=F32
                ).astype(BF16)


def second_pointwise(grid, length_ref, count_ref, x_ref, p_ref, q_ref, out_sums_ref, plane_ref, sums_ref, pool_sums_ref):
    length = length_ref[0]
    rows = grid.frame_rows
    wide = 2 * rows
    valid, window = row_geometry(grid.side, POOLED)
    sums_ref[...] = jnp.zeros_like(sums_ref)
    plane_ref[0:rows] = jnp.zeros((rows, POOLED), F32)
    plane_ref[grid.rows + rows : grid.rows + 2 * rows] = jnp.zeros((rows, POOLED), F32)

    @pl.loop(0, grid.frames // 2)
    def _(pair):
        at = rows_at(pair * wide, wide)
        values = jnp.dot(x_ref[at, :], p_ref[...], preferred_element_type=F32)
        q_ref[at, 0:SECOND] = values[:, :SECOND]
        sums_ref[0:8] += partial_sum(values[:, :SECOND])
        sums_ref[8:16] += partial_sum(values[:, :SECOND] * values[:, :SECOND])
        for number in range(2):
            plane_ref[rows_at((2 * pair + number + 1) * rows, rows), :] = plane_box(
                values[number * rows : (number + 1) * rows, SECOND:]
            )

    pool_planes(grid, plane_ref, q_ref, SECOND, pool_sums_ref, length, valid, window)
    write_sums(out_sums_ref, sums_ref, 0, SECOND)
    write_sums(out_sums_ref, pool_sums_ref, SECOND, FIRST)
    out_sums_ref[2:3, :] = jnp.full((1, FIRST), count_ref[0], F32)


def second_convolve(grid, length_ref, q_ref, sums_in_ref, gain_ref, shift_ref, kernel_ref, h_ref, taps_ref, e_ref, out_sums_ref, moment_ref, acc_ref, sums_ref):
    length = length_ref[0]
    total = total_of(sums_in_ref)
    count = total[2:3]
    center, inverse = moments(total[0:1], total[1:2], count)
    moment_ref[0:1, :] = center
    moment_ref[1:2, :] = inverse
    moment_ref[2:3, :] = count
    center, inverse = (center[:, DIRECT:SECOND], inverse[:, DIRECT:SECOND])
    valid, _ = row_geometry(grid.side, 128)
    wide_valid = jnp.concatenate([valid, valid], axis=1)
    zero_rows(taps_ref)

    @pl.loop(0, grid.frames)
    def _(frame):
        at = rows_at(frame * grid.frame_rows, grid.frame_rows)
        scaled = (q_ref[at, DIRECT:SECOND] - center) * inverse
        h_ref[at, :] = scaled.astype(BF16)
        act = silu(gain_ref[...] * scaled + shift_ref[...])
        store_taps(grid, taps_ref, frame, act * (wide_valid * frame_flag(frame, length)))

    convolve(grid, taps_ref, kernel_ref, acc_ref, e_ref, sums_ref, length, valid)
    write_sums(out_sums_ref, sums_ref, 0, SECOND)


def second_output(grid, length_ref, q_ref, e_ref, moment_ref, sums_in_ref, gain_ref, shift_ref, cot_ref, act_ref, h_ref, error_ref, outer_ref, out_sums_ref, sums_ref):
    length = length_ref[0]
    valid, _ = row_geometry(grid.side, 128)
    wide_valid = jnp.concatenate([valid] * (OUTER // 128), axis=1)
    total = total_of(sums_in_ref)
    count = jnp.concatenate([moment_ref[2:3, 0:128]] * 7, axis=1)
    center, inverse = moments(total[0:1], total[1:2], count[:, :SECOND])
    center = jnp.concatenate([moment_ref[0:1, :DIRECT], center, moment_ref[0:1, SECOND:]], axis=1)
    inverse = jnp.concatenate([moment_ref[1:2, :DIRECT], inverse, moment_ref[1:2, SECOND:]], axis=1)
    outer_ref[0:1, :] = center
    outer_ref[1:2, :] = inverse
    outer_ref[2:3, :] = count
    sums_ref[...] = jnp.zeros_like(sums_ref)

    @pl.loop(0, grid.frames)
    def _(frame):
        at = rows_at(frame * grid.frame_rows, grid.frame_rows)
        values = jnp.concatenate([q_ref[at, :DIRECT], e_ref[at, :], q_ref[at, SECOND:]], axis=1)
        scaled = (values - center) * inverse
        h_ref[at, :] = scaled.astype(BF16)
        mask = wide_valid * frame_flag(frame, length)
        shifted = gain_ref[...] * scaled + shift_ref[...]
        gate = sigmoid(shifted)
        act_ref[at, :] = (shifted * gate * mask).astype(BF16)
        slope = gate * (1.0 + shifted * (1.0 - gate))
        error = cot_ref[at, :].astype(F32) * slope * mask
        error_ref[at, :] = error.astype(BF16)
        sums_ref[0:8] += partial_sum(error)
        sums_ref[8:16] += partial_sum(error * scaled)

    write_sums(out_sums_ref, sums_ref, 0, OUTER)


def outer_error(grid, small, slope_ref, grad_ref, matrix, frame, lo, hi):
    values = slope_ref[rows_at(frame * grid.frame_rows, grid.frame_rows), lo:hi].astype(F32)
    if small is None:
        return values
    coarse = grad_ref[rows_at((frame // 2) * small.frame_rows, small.frame_rows), lo:hi]
    return values * jnp.dot(matrix, coarse, preferred_element_type=F32)


def spread_matrix(grid, small):
    return None if small is None else pool_matrix(small.side, True)[: grid.frame_rows]


def second_back(grid, small, length_ref, h_ref, outer_ref, sums_in_ref, gain_ref, slope_ref, *rest):
    grad_ref, d_ref, total_ref = rest if small is not None else (None, *rest)
    length = length_ref[0]
    valid, _ = row_geometry(grid.side, 128)
    total = total_of(sums_in_ref)
    total_ref[...] = total
    lo, hi = (DIRECT, DIRECT + SECOND)
    count = outer_ref[2:3, lo:hi]
    mean_r = total[0:1, lo:hi] / count
    mean_rh = total[1:2, lo:hi] / count
    factor = gain_ref[:, lo:hi] * outer_ref[1:2, lo:hi]
    wide_valid = jnp.concatenate([valid] * (SECOND // 128), axis=1)
    matrix = spread_matrix(grid, small)
    zero_rows(d_ref)

    @pl.loop(0, grid.frames)
    def _(frame):
        at = rows_at(frame * grid.frame_rows, grid.frame_rows)
        scaled = h_ref[at, lo:hi].astype(F32)
        error = outer_error(grid, small, slope_ref, grad_ref, matrix, frame, lo, hi)
        back = factor * (error - mean_r - scaled * mean_rh)
        d_ref[rows_at(grid.lead + frame * grid.pitch, grid.frame_rows), :] = (
            back * (wide_valid * frame_flag(frame, length))
        ).astype(BF16)


def conv_back(grid, length_ref, d_ref, kernel_ref, reduced_ref, reduced_gain_ref, reduced_shift_ref, r_ref, out_sums_ref, acc_ref, sums_ref):
    length = length_ref[0]
    valid, _ = row_geometry(grid.side, 128)
    group_rows = grid.group * grid.pitch
    sums_ref[...] = jnp.zeros_like(sums_ref)
    reduced_valid = jnp.concatenate([valid, valid], axis=1)

    @pl.loop(0, grid.frames // grid.group)
    def _(group):
        base = grid.lead + group * group_rows
        for tap in range(9):
            start = base - (tap // 3 - 1) * grid.pitch - (tap % 3 - 1) * PITCH
            part = lax.dot_general(
                d_ref[rows_at(start, group_rows), :],
                kernel_ref[tap],
                (((1,), (1,)), ((), ())),
                preferred_element_type=F32,
            )
            acc_ref[...] = part if tap == 0 else acc_ref[...] + part
        for number in range(grid.group):
            frame = group * grid.group + number
            rows = grid.frame_rows
            lines = slice(number * grid.pitch, number * grid.pitch + rows)
            back = (
                pltpu.roll(acc_ref[lines, 0:REDUCED], rows - 1, 0)
                + acc_ref[lines, REDUCED : 2 * REDUCED]
                + pltpu.roll(acc_ref[lines, 2 * REDUCED : 3 * REDUCED], 1, 0)
            )
            at = rows_at(frame * rows, rows)
            scaled = reduced_ref[at, :].astype(F32)
            slope = silu_slope(reduced_gain_ref[...] * scaled + reduced_shift_ref[...])
            error = back * slope * (reduced_valid * frame_flag(frame, length))
            r_ref[at, :] = error.astype(BF16)
            sums_ref[0:8] += partial_sum(error)
            sums_ref[8:16] += partial_sum(error * scaled)

    write_sums(out_sums_ref, sums_ref, 0, REDUCED)


def kernel_grads(grid, slots, first_ref, taps_ref, d_ref, out_ref, acc_ref):
    group_rows = grid.group * grid.pitch
    acc_ref[...] = jnp.zeros_like(acc_ref)

    @pl.loop(0, grid.frames // grid.group)
    def _(group):
        base = grid.lead + group * group_rows
        right = d_ref[rows_at(base, group_rows), :]
        for slot in range(slots):
            tap = jnp.minimum(first_ref[0] + slot, TAPS - 1)
            start = base + (tap // 9 - 1) * grid.pitch + (lax.rem(tap // 3, 3) - 1) * PITCH
            lanes = pl.ds(pl.multiple_of(lax.rem(tap, 3) * REDUCED, REDUCED), REDUCED)
            left = taps_ref[rows_at(start, group_rows), lanes]
            acc_ref[slot] += lax.dot_general(
                left, right, (((0,), (0,)), ((), ())), preferred_element_type=F32
            )

    for slot in range(slots):
        base = slot * TAP_ROWS
        for tile in range(2):
            out_ref[base + MID_IN * tile : base + MID_IN * (tile + 1), :] = acc_ref[
                slot, 0:MID_IN, 128 * tile : 128 * (tile + 1)
            ].astype(BF16)
        half = MID_IN // 2
        folded = acc_ref[slot, 0:half, 256:384] + pltpu.roll(
            acc_ref[slot, half:MID_IN, 256:384], 64, 1
        )
        base = base + 2 * MID_IN
        out_ref[base : base + half, :] = folded.astype(BF16)
        base = base + half
        out_ref[base : base + SMALL_IN, :] = acc_ref[
            slot, MID_IN : MID_IN + SMALL_IN, 384:512
        ].astype(BF16)
    used = slots * TAP_ROWS
    if out_ref.shape[0] > used:
        out_ref[used:, :] = jnp.zeros((out_ref.shape[0] - used, 128), BF16)


def point_back(grid, small, kept, length_ref, place_ref, h_ref, outer_ref, total_ref, gain_ref, slope_ref, *rest):
    first = small is not None
    grad_ref, rest = (rest[0], rest[1:]) if first else (None, rest)
    reduced_ref, r_ref, moment_ref, sums_in_ref, reduced_gain_ref, x_ref, p_ref, *rest = rest
    pooled_refs, rest = ((), rest) if first else (rest[:2], rest[2:])
    dx_ref, dp_ref, reduced_total_ref, *rest = rest
    outer_sums_ref, rest = (None, rest) if first else (rest[0], rest[1:])
    du_ref, plane_ref, acc_ref, *rest = rest
    length = length_ref[0]
    rows = grid.frame_rows
    valid, window = row_geometry(grid.side, 128)
    matrix = spread_matrix(grid, small)
    total = total_of(sums_in_ref)
    reduced_total_ref[...] = total
    count = outer_ref[2:3, 0:128]
    count = jnp.concatenate([count, count], axis=1)
    mid_r, mid_rh = (total[0:1] / count, total[1:2] / count)
    mid_factor = reduced_gain_ref[...] * moment_ref[1:2, DIRECT:SECOND]
    two = jnp.concatenate([valid, valid], axis=1)
    plane_ref[0:rows] = jnp.zeros((rows, POOLED), F32)
    plane_ref[grid.rows + rows : grid.rows + 2 * rows] = jnp.zeros((rows, POOLED), F32)

    def section(frame, lo, hi, mask):
        at = rows_at(frame * rows, rows)
        scaled = h_ref[at, lo:hi].astype(F32)
        error = outer_error(grid, small, slope_ref, grad_ref, matrix, frame, lo, hi)
        size = outer_ref[2:3, lo:hi]
        inner = error - total_ref[0:1, lo:hi] / size - scaled * (total_ref[1:2, lo:hi] / size)
        return (gain_ref[:, lo:hi] * outer_ref[1:2, lo:hi]) * inner * mask

    @pl.loop(0, grid.frames)
    def _(frame):
        at = rows_at(frame * rows, rows)
        flag = frame_flag(frame, length)
        du_ref[at, 0:DIRECT] = section(frame, 0, DIRECT, two * flag).astype(BF16)
        scaled = reduced_ref[at, :].astype(F32)
        inner = r_ref[at, :].astype(F32) - mid_r - scaled * mid_rh
        du_ref[at, DIRECT:SECOND] = (mid_factor * inner * (two * flag)).astype(BF16)
        pool = section(frame, OUTER - POOLED, OUTER, valid * flag)
        plane_ref[rows_at((frame + 1) * rows, rows), :] = plane_box(
            pool * box_scale(frame, length, window)
        )

    wide = 2 * rows
    acc_ref[...] = jnp.zeros_like(acc_ref)
    if not first:
        rest[0][...] = jnp.zeros_like(rest[0])

    @pl.loop(0, grid.frames // 2)
    def _(pair):
        start = pair * wide
        at = rows_at(start, wide)
        pool = (
            plane_ref[at, :]
            + plane_ref[rows_at(start + rows, wide), :]
            + plane_ref[rows_at(start + 2 * rows, wide), :]
        ) * jnp.concatenate([valid, valid], axis=0)
        du = jnp.concatenate([du_ref[at, 0:SECOND], pool.astype(BF16)], axis=1)
        dx = lax.dot_general(
            du, p_ref[...], (((1,), (1,)), ((), ())), preferred_element_type=F32
        ).astype(BF16)
        dx_ref[at, :] = dx
        if not first:
            for number, ref in enumerate(pooled_refs):
                rest[0][8 * number : 8 * number + 8] += partial_sum(
                    dx.astype(F32) * ref[at, :].astype(F32)
                )
        acc_ref[...] += lax.dot_general(
            x_ref[at, :], du, (((0,), (0,)), ((), ())), preferred_element_type=F32
        )

    if not first:
        write_sums(outer_sums_ref, rest[0], 0, OUTER)
    start = pl.multiple_of(place_ref[0] * kept, 16) if kept < acc_ref.shape[0] else 0
    own = acc_ref[pl.ds(start, kept), :]
    for tile in range(FIRST // 128):
        dp_ref[kept * tile : kept * (tile + 1), :] = own[:, 128 * tile : 128 * (tile + 1)].astype(
            BF16
        )
    used = (FIRST // 128) * kept
    if dp_ref.shape[0] > used:
        dp_ref[used:, :] = jnp.zeros((dp_ref.shape[0] - used, 128), BF16)


def write_taps(buffer_ref, parts, slots, mid_ref, small_ref):
    half = MID_IN // 2

    @pl.loop(0, TAPS)
    def _(tap):
        base = lax.rem(tap, slots) * TAP_ROWS
        part = tap // slots

        def piece(start, size):
            return buffer_ref[part, rows_at(base + start, size), :].astype(F32)

        folded = piece(2 * MID_IN, half)
        mid_ref[tap, :, 0:128] = piece(0, MID_IN)
        mid_ref[tap, :, 128:256] = piece(MID_IN, MID_IN)
        mid_ref[tap, 0:half, 256:320] = folded[:, 0:64]
        mid_ref[tap, half:MID_IN, 256:320] = pltpu.roll(folded, 64, 1)[:, 0:64]
        small_ref[tap] = piece(2 * MID_IN + half, SMALL_IN)


def write_point(read, parts, kept, point_ref, wide_ref):
    for tile in range(FIRST // 128):
        for part in range(parts):
            start, stop = (kept * part, kept * (part + 1))
            values = read(part, kept * tile, kept)
            if kept * parts == CHANNELS:
                wide_ref[start:stop, :] = values
                continue
            for lo, hi, moved in ((0, 576, 0), (640, OUTER, 64)):
                lo, hi = (max(lo, start), min(hi, stop))
                if lo < hi:
                    wide_ref[lo - moved : hi - moved, :] = values[lo - start : hi - start]
        turned = wide_ref[...].T
        if tile < 3:
            point_ref[128 * tile : 128 * (tile + 1), :] = turned
        elif tile == 3:
            point_ref[384:448, :] = turned[0:64]
        else:
            point_ref[448:576, :] = turned


def copy_out(pairs, sem_ref):
    copies = [
        pltpu.make_async_copy(source, target, sem_ref.at[number])
        for number, (source, target) in enumerate(pairs)
    ]
    for copy in copies:
        copy.start()
    for copy in copies:
        copy.wait()


def unpack_second(parts, slots, tap_rows, buffer_ref, mid_out, small_out, point_out, mid_ref, small_ref, point_ref, wide_ref, sem_ref):
    def read(part, start, size):
        return buffer_ref[part, tap_rows + start : tap_rows + start + size, :].astype(F32)

    write_taps(buffer_ref, parts, slots, mid_ref, small_ref)
    write_point(read, parts, OUTER // parts, point_ref, wide_ref)
    copy_out(
        [(mid_ref, mid_out.at[1]), (small_ref, small_out.at[1]), (point_ref, point_out.at[1])],
        sem_ref,
    )


def reorder(parts, clips, share, place, clip, mine_ref, other_ref, buffer_ref):
    for chip in range(clips // 2):
        for step in range(parts):
            source = (chip * parts + step) * share
            part = lax.rem(place - step + parts, parts)
            for swapped, ref in enumerate((mine_ref, other_ref)):
                owner = clip ^ (2 * chip) ^ swapped
                buffer_ref[part, rows_at(owner * share, share), :] = ref[
                    source : source + share, :
                ]


def unpack_taps(parts, clips, slots, share, place_ref, clip_ref, mine_ref, other_ref, mid_in, small_in, mid_out, small_out, buffer_ref, mid_ref, small_ref, sem_ref):
    reorder(parts, clips, share, place_ref[0], clip_ref[0], mine_ref, other_ref, buffer_ref)
    write_taps(buffer_ref, parts, slots, mid_ref, small_ref)
    copy_out([(mid_ref, mid_out.at[0]), (small_ref, small_out.at[0])], sem_ref)


def unpack_point(parts, clips, share, place_ref, clip_ref, mine_ref, other_ref, point_in, point_out, buffer_ref, point_ref, wide_ref, sem_ref):
    reorder(parts, clips, share, place_ref[0], clip_ref[0], mine_ref, other_ref, buffer_ref)

    def read(part, start, size):
        return buffer_ref[part, start : start + size, :].astype(F32)

    write_point(read, parts, CHANNELS // parts, point_ref, wide_ref)
    copy_out([(point_ref, point_out.at[0])], sem_ref)


def outer_vector(values):
    gap = jnp.zeros((64,), F32)
    return jnp.concatenate(
        [values[:256], values[576:896], gap, values[896:1024], values[448:576]]
    ).reshape(1, OUTER)


def reduced_vector(values):
    return jnp.pad(values[256:448], (0, 64)).reshape(1, REDUCED)


def norm_vector(outer, reduced):
    return jnp.concatenate(
        [outer[:256], reduced[:192], outer[768:896], outer[256:576], outer[640:768]]
    )


def wide_kernels(conv_mid, conv_small):
    mid = jnp.pad(conv_mid, ((0, 0), (0, 96), (0, 192)))
    small = jnp.pad(conv_small, ((0, 0), (160, 64), (384, 0)))
    return (mid + small).reshape(9, 3 * REDUCED, SECOND)


def point_columns(point):
    gap = jnp.zeros((point.shape[0], 64), point.dtype)
    return jnp.concatenate([point[:, :448], gap, point[:, 448:]], axis=1)


def round_up(value, unit):
    return -(-value // unit) * unit


def spread_over(values, axis, size):
    received = [values]
    for step in range(1, size):
        perm = [(source, (source + step) % size) for source in range(size)]
        received.append(lax.ppermute(values, axis, perm))
    return received


def after(values, earlier):
    return lax.optimization_barrier((values, earlier))[0]


def shared_sum(packed, clips):
    pieces = packed.reshape(clips, packed.shape[0] // clips, 128)
    pieces = lax.all_to_all(pieces, "dp", 0, 0, tiled=True)
    return jnp.sum(pieces.astype(F32), axis=0).astype(BF16)


def gather_steps(share, parts, clips):
    column = jnp.concatenate(spread_over(share, "branch", parts), axis=0)
    columns = [column]
    for chip in range(1, clips // 2):
        perm = [(source, source ^ (2 * chip)) for source in range(clips)]
        columns.append(lax.ppermute(column, "dp", perm))
    mine = jnp.concatenate(columns, axis=0)
    other = lax.ppermute(mine, "dp", [(source, source ^ 1) for source in range(clips)])
    return (mine, other)


def on_device(frames, lengths, cotangent, pointwise, conv_mid, conv_small, gains, shifts):
    parts = lax.axis_size("branch")
    clips = lax.axis_size("dp")
    place = lax.axis_index("branch").astype(jnp.int32)
    count_frames, side = (frames.shape[1], frames.shape[2])
    grid, small = (Grid(count_frames, side), Grid(count_frames // 2, side // 2))
    local = count_frames // parts
    own_channels = frames.shape[-1]
    length = lengths.astype(jnp.int32)
    half_length = length // 2
    place_one = place.reshape(1)

    ids = jnp.arange(count_frames, dtype=jnp.int32)
    mask = (ids < length[0]).astype(BF16)[:, None, None, None]
    own = jnp.pad(frames[0] * mask, ((0, 0), (0, 0), (0, PITCH - side), (0, 0)))
    own = own.reshape(grid.rows, own_channels)
    by_frames = lax.all_to_all(
        own.reshape(parts, local * grid.frame_rows, own_channels).transpose(0, 2, 1),
        "branch",
        0,
        0,
        tiled=True,
    )

    columns = [point_columns(pointwise[0]), point_columns(pointwise[1])]
    point_first = columns[0].reshape(parts, own_channels, FIRST)
    point_own = lax.dynamic_slice_in_dim(columns[0], place * own_channels, own_channels, 0)
    point_second = jnp.concatenate(
        [columns[1][:576], jnp.zeros((64, FIRST), BF16), columns[1][576:]], axis=0
    )
    kernels = [wide_kernels(conv_mid[number], conv_small[number]) for number in range(2)]
    outer_gain = [outer_vector(gains[number]) for number in range(2)]
    outer_shift = [outer_vector(shifts[number]) for number in range(2)]
    reduced_gain = [reduced_vector(gains[number]) for number in range(2)]
    reduced_shift = [reduced_vector(shifts[number]) for number in range(2)]
    cot = cotangent[0]
    cot = jnp.concatenate(
        [cot[..., :576], jnp.zeros(cot.shape[:3] + (64,), BF16), cot[..., 576:]], axis=-1
    )
    cot = jnp.pad(cot, ((0, 0), (0, 0), (0, PITCH - small.side), (0, 0))).reshape(small.rows, OUTER)

    local_rows = local * grid.frame_rows
    valid_frames = jnp.clip(length - place * local, 0, local)
    local_count = valid_frames.astype(F32) * float(side * side)
    mid, pool, direct, sums = call(
        functools.partial(first_pointwise, grid, local, parts),
        (
            shape((local_rows + PITCH, REDUCED), BF16),
            shape((local_rows + PITCH, POOLED), BF16),
            shape((local_rows + PITCH, DIRECT), BF16),
            shape((3, SECOND), F32),
        ),
        [pltpu.VMEM((local_rows, FIRST), F32)],
        scalars=1,
    )(local_count, by_frames, point_first)
    mids = spread_over(mid, "branch", parts)
    sums = jnp.sum(lax.all_gather(sums, "dp"), axis=0)
    all_sums = spread_over(sums, "branch", parts)
    pool, direct = after((pool, direct), (mids, all_sums))
    pools = spread_over(pool, "branch", parts)
    directs = spread_over(direct, "branch", parts)
    group_rows = grid.group * grid.pitch
    h_reduced, taps, e, e_sums, moment = call(
        functools.partial(first_convolve, grid, local, parts),
        (
            shape((grid.rows, REDUCED), BF16),
            shape((grid.padded, 3 * REDUCED), BF16),
            shape((grid.rows, SECOND), F32),
            shape((2, SECOND), F32),
            shape((3, SECOND), F32),
        ),
        [pltpu.VMEM((group_rows, SECOND), F32), pltpu.VMEM((16, SECOND), F32)],
        scalars=2,
        flops=2 * 10**10,
    )(length, place_one, *mids, *all_sums, reduced_gain[0], reduced_shift[0], kernels[0])
    q_pool, pool_sums = call(
        functools.partial(first_pool, grid, local, parts),
        (shape((grid.rows, POOLED), F32), shape((2, POOLED), F32)),
        [
            pltpu.VMEM((grid.rows + 2 * grid.frame_rows, POOLED), F32),
            pltpu.VMEM((16, POOLED), F32),
        ],
        scalars=2,
    )(length, place_one, *pools)
    second_sums = lax.all_gather(jnp.concatenate([e_sums, pool_sums], axis=1), "dp")
    pooled, h_outer, slope, outer, pooled_slope, pooled_product = call(
        functools.partial(first_output, grid, small, local, parts),
        (
            shape((small.rows, OUTER), BF16),
            shape((grid.rows, OUTER), BF16),
            shape((grid.rows, OUTER), BF16),
            shape((3, OUTER), F32),
            shape((small.rows, OUTER), BF16),
            shape((small.rows, OUTER), BF16),
        ),
        scalars=2,
    )(length, place_one, *directs, q_pool, e, moment, second_sums, outer_gain[0], outer_shift[0])

    small_count = half_length.astype(F32) * float(small.side * small.side)
    q_small, sums_small = call(
        functools.partial(second_pointwise, small),
        (shape((small.rows, FIRST), F32), shape((3, FIRST), F32)),
        [
            pltpu.VMEM((small.rows + 2 * small.frame_rows, POOLED), F32),
            pltpu.VMEM((16, SECOND), F32),
            pltpu.VMEM((16, POOLED), F32),
        ],
        scalars=2,
    )(half_length, small_count, pooled, point_second)
    sums_small = lax.all_gather(sums_small, "dp")
    small_group = small.group * small.pitch
    h_reduced_small, taps_small, e_small, e_sums_small, moment_small = call(
        functools.partial(second_convolve, small),
        (
            shape((small.rows, REDUCED), BF16),
            shape((small.padded, 3 * REDUCED), BF16),
            shape((small.rows, SECOND), F32),
            shape((2, SECOND), F32),
            shape((3, FIRST), F32),
        ),
        [pltpu.VMEM((small_group, SECOND), F32), pltpu.VMEM((16, SECOND), F32)],
        scalars=1,
    )(half_length, q_small, sums_small, reduced_gain[1], reduced_shift[1], kernels[1])
    e_sums_small = lax.all_gather(e_sums_small, "dp")
    act, h_outer_small, error_small, outer_small, outer_sums_small = call(
        functools.partial(second_output, small),
        (
            shape((small.rows, OUTER), BF16),
            shape((small.rows, OUTER), BF16),
            shape((small.rows, OUTER), BF16),
            shape((3, OUTER), F32),
            shape((2, OUTER), F32),
        ),
        [pltpu.VMEM((16, OUTER), F32)],
        scalars=1,
    )(half_length, q_small, e_small, moment_small, e_sums_small, outer_gain[1], outer_shift[1], cot)

    slots = -(-TAPS // parts)
    tap_rows = round_up(slots * TAP_ROWS, 16 * clips)
    first_tap = place_one * slots

    def back(at, coarse, number, span, h_out, outer_moment, outer_sums, slopes, grad, h_red, taps_of, moment_of, x, point, kept, pooled_pair):
        first = coarse is not None
        gathered = lax.all_gather(outer_sums, "dp")
        rows = at.group * at.pitch
        grads = (grad,) if first else ()
        d_low, total = call(
            functools.partial(second_back, at, coarse),
            (shape((at.padded, SECOND), BF16), shape((2, OUTER), F32)),
            scalars=1,
        )(span, h_out, outer_moment, gathered, outer_gain[number], slopes, *grads)
        packed_taps = call(
            functools.partial(kernel_grads, at, slots),
            shape((tap_rows, 128), BF16),
            [pltpu.VMEM((slots, REDUCED, SECOND), F32)],
            scalars=1,
        )(first_tap, taps_of, d_low)
        r_low, sums_low = call(
            functools.partial(conv_back, at),
            (shape((at.rows, REDUCED), BF16), shape((2, REDUCED), F32)),
            [pltpu.VMEM((rows, 3 * REDUCED), F32), pltpu.VMEM((16, REDUCED), F32)],
            scalars=1,
            flops=2 * 10**10 if first else 10**9,
        )(
            span,
            after(d_low, packed_taps) if first else d_low,
            kernels[number],
            h_red,
            reduced_gain[number],
            reduced_shift[number],
        )
        gathered = lax.all_gather(sums_low, "dp")
        point_rows = round_up(kept * (FIRST // 128), 16 * clips)
        extra_out = () if first else (shape((2, OUTER), F32),)
        extra_scratch = [] if first else [pltpu.VMEM((16, OUTER), F32)]
        dx, packed_point, reduced_total, *next_sums = call(
            functools.partial(point_back, at, coarse, kept),
            (
                shape((at.rows, x.shape[1]), BF16),
                shape((point_rows, 128), BF16),
                shape((2, REDUCED), F32),
                *extra_out,
            ),
            [
                pltpu.VMEM((at.rows, SECOND), BF16),
                pltpu.VMEM((at.rows + 2 * at.frame_rows, POOLED), F32),
                pltpu.VMEM((x.shape[1], FIRST), F32),
                *extra_scratch,
            ],
            scalars=2,
        )(
            span,
            place_one,
            h_out,
            outer_moment,
            total,
            outer_gain[number],
            slopes,
            *grads,
            h_red,
            r_low,
            moment_of,
            gathered,
            reduced_gain[number],
            x,
            point,
            *pooled_pair,
        )
        norms = [norm_vector(total[row], reduced_total[row]) for row in range(2)]
        return (dx, packed_taps, packed_point, norms, next_sums)

    dx_small, taps_packed_small, point_packed_small, norms_small, (outer_sums,) = back(
        small, None, 1, half_length, h_outer_small, outer_small, outer_sums_small, error_small, None,
        h_reduced_small, taps_small, moment_small, pooled, point_second, OUTER // parts,
        (pooled_slope, pooled_product),
    )
    share_small = shared_sum(
        jnp.concatenate(
            [
                taps_packed_small.reshape(clips, -1, 128),
                point_packed_small.reshape(clips, -1, 128),
            ],
            axis=1,
        ).reshape(-1, 128),
        clips,
    )
    whole_small = lax.all_gather(share_small, ("branch", "dp"), axis=0, tiled=True)
    dx, taps_packed, point_packed, norms, _ = back(
        grid, small, 0, length, h_outer, outer, outer_sums, slope, dx_small,
        h_reduced, taps, moment, own, point_own, own_channels, (),
    )
    taps_mine, taps_other = gather_steps(shared_sum(taps_packed, clips), parts, clips)
    point_mine, point_other = gather_steps(shared_sum(point_packed, clips), parts, clips)

    outs = (
        shape((2, TAPS, MID_IN, MID_OUT), F32),
        shape((2, TAPS, SMALL_IN, SMALL_OUT), F32),
        shape((2, SQUEEZED, CHANNELS), F32),
    )
    mid_scratch = pltpu.VMEM((TAPS, MID_IN, MID_OUT), F32)
    small_scratch = pltpu.VMEM((TAPS, SMALL_IN, SMALL_OUT), F32)
    point_scratch = [pltpu.VMEM((SQUEEZED, CHANNELS), F32), pltpu.VMEM((CHANNELS, 128), F32)]
    small_rows = round_up((OUTER // parts) * (FIRST // 128), 16 * clips)
    point_rows = point_packed.shape[0]
    whole_small = whole_small.reshape(parts, clips, -1, 128)
    tap_share = tap_rows // clips
    whole_small = jnp.concatenate(
        [
            whole_small[:, :, :tap_share].reshape(parts, tap_rows, 128),
            whole_small[:, :, tap_share:].reshape(parts, small_rows, 128),
        ],
        axis=1,
    )
    mid_grad, small_grad, point_grad = call(
        functools.partial(unpack_second, parts, slots, tap_rows),
        outs,
        [mid_scratch, small_scratch, *point_scratch, pltpu.SemaphoreType.DMA((3,))],
        out_space=pl.ANY,
    )(whole_small)
    clip_one = lax.axis_index("dp").astype(jnp.int32).reshape(1)
    mid_grad, small_grad = call(
        functools.partial(unpack_taps, parts, clips, slots, tap_share),
        outs[:2],
        [
            pltpu.VMEM((parts, tap_rows, 128), BF16),
            mid_scratch,
            small_scratch,
            pltpu.SemaphoreType.DMA((2,)),
        ],
        scalars=2,
        out_space=pl.ANY,
        aliases={4: 0, 5: 1},
    )(place_one, clip_one, taps_mine, taps_other, mid_grad, small_grad)
    point_grad = call(
        functools.partial(unpack_point, parts, clips, point_rows // clips),
        outs[2],
        [
            pltpu.VMEM((parts, point_rows, 128), BF16),
            *point_scratch,
            pltpu.SemaphoreType.DMA((1,)),
        ],
        scalars=2,
        out_space=pl.ANY,
        aliases={4: 0},
    )(place_one, clip_one, point_mine, point_other, point_grad)
    point_grad = point_grad.swapaxes(1, 2)
    act = act.reshape(1, small.frames, small.side, PITCH, OUTER)[:, :, :, : small.side]
    act = jnp.concatenate([act[..., :576], act[..., 640:]], axis=-1)
    input_grad = dx.reshape(1, grid.frames, side, PITCH, own_channels)[:, :, :, :side]
    input_grad = input_grad * mask[None]
    gain_grad = jnp.stack([norms[1], norms_small[1]])
    shift_grad = jnp.stack([norms[0], norms_small[0]])
    return (act, input_grad, point_grad, mid_grad, small_grad, gain_grad, shift_grad)


def solution(mesh):
    split = P("dp", None, None, None, "branch")
    whole = P("dp", None, None, None, None)
    return jax.shard_map(
        on_device,
        mesh=mesh,
        in_specs=(split, P("dp"), whole, P(), P(), P(), P(), P()),
        out_specs=(whole, split, P(), P(), P(), P(), P()),
        check_vma=False,
    )
```

```python
import functools

import jax
import jax.numpy as jnp
from jax import lax
from jax.experimental import pallas as pl
from jax.experimental.pallas import tpu as pltpu
from jax.sharding import PartitionSpec as P

DIRECT = 256
MID_IN = 160
MID_OUT = 320
SMALL_IN = 32
SMALL_OUT = 128
TAPS = 27
CHANNELS = 832
SQUEEZED = 576
PITCH = 16
REDUCED = 256
POOLED = 128
FIRST = 640
SECOND = 512
OUTER = 896
TAP_ROWS = 432
EPSILON = 1e-05
F32 = jnp.float32
BF16 = jnp.bfloat16
VMEM_BYTES = 58 * 2**20


def call(body, out_shape, scratch=(), scalars=0, flops=10**9, out_space=pltpu.VMEM, aliases=None, far=(), far_out=()):
    aliases = aliases or {}

    def run(*operands):
        specs = [
            pl.BlockSpec(
                memory_space=pl.ANY
                if number in aliases or number in far
                else pltpu.SMEM
                if number < scalars
                else pltpu.VMEM
            )
            for number in range(len(operands))
        ]
        if isinstance(out_shape, tuple):
            out_specs = tuple(
                pl.BlockSpec(memory_space=pl.ANY if number in far_out else out_space)
                for number in range(len(out_shape))
            )
        else:
            out_specs = pl.BlockSpec(memory_space=out_space)
        return pl.pallas_call(
            body,
            out_shape=out_shape,
            in_specs=specs,
            out_specs=out_specs,
            input_output_aliases=aliases,
            scratch_shapes=list(scratch),
            compiler_params=pltpu.CompilerParams(vmem_limit_bytes=VMEM_BYTES),
            cost_estimate=pl.CostEstimate(
                flops=flops, bytes_accessed=16 * 2**20, transcendentals=0
            ),
        )(*operands)

    return run


def shape(dims, dtype):
    return jax.ShapeDtypeStruct(tuple(dims), dtype)


def rows_at(start, size):
    return pl.ds(pl.multiple_of(start, 16), size)


def frames_of(rows, width=128):
    return lax.broadcasted_iota(jnp.int32, (rows, width), 0) & (PITCH - 1)


def frame_mask(rows, length, width=128):
    mask = jnp.where(frames_of(rows) < length, 1.0, 0.0)
    return jnp.concatenate([mask] * (width // 128), axis=1) if width > 128 else mask


def earlier(values):
    return jnp.where(frames_of(*values.shape) > 0, pltpu.roll(values, 1, 0), 0.0)


def later(values):
    rows = values.shape[0]
    return jnp.where(frames_of(*values.shape) < PITCH - 1, pltpu.roll(values, rows - 1, 0), 0.0)


def plane_box(values):
    across = values + earlier(values) + later(values)
    edge = jnp.zeros((PITCH, values.shape[1]), values.dtype)
    return (
        across
        + jnp.concatenate([across[PITCH:], edge], axis=0)
        + jnp.concatenate([edge, across[:-PITCH]], axis=0)
    )


def box_window(side, length):
    frame = frames_of(side * PITCH)
    place = lax.broadcasted_iota(jnp.int32, (side * PITCH, 128), 0) >> 4

    def one(condition):
        return jnp.where(condition, 1.0, 0.0)

    count = one(frame < length) + one(frame + 1 < length) + one((frame > 0) & (frame - 1 < length))
    return count * (3.0 - one(place == 0) - one(place == side - 1))


def box_scale(line, side, window):
    lines = 3.0 - jnp.where(line == 0, 1.0, 0.0) - jnp.where(line == side - 1, 1.0, 0.0)
    return 1.0 / jnp.maximum(window * lines, 1.0)


def sigmoid(value):
    return 0.5 * jnp.tanh(0.5 * value) + 0.5


def silu(value):
    return value * sigmoid(value)


def silu_slope(value):
    gate = sigmoid(value)
    return gate * (1.0 + value * (1.0 - gate))


def partial_sum(values):
    rows, width = values.shape
    return jnp.sum(values.reshape(rows // 8, 8, width), axis=0)


def moments(total, square, count):
    center = total / count
    return (center, lax.rsqrt(square / count - center * center + EPSILON))


def total_of(gathered):
    total = gathered[0]
    for number in range(1, gathered.shape[0]):
        total = total + gathered[number]
    return total


def pool_matrix(side, transposed):
    line = 2 * side * PITCH
    few, many = (side * PITCH, 2 * line)
    dims = (many, few) if transposed else (few, many)
    coarse = lax.broadcasted_iota(jnp.int32, dims, 1 if transposed else 0)
    fine = lax.broadcasted_iota(jnp.int32, dims, 0 if transposed else 1)
    fine = jnp.where(fine >= line, fine - line, fine)
    same = (fine >> 5 == coarse >> 4) & ((fine & (PITCH - 1)) >> 1 == coarse & (PITCH - 1))
    return jnp.where(same, 0.125, 0.0).astype(BF16)


class Grid:
    def __init__(self, side):
        self.side = side
        self.line_rows = side * PITCH
        self.rows = side * self.line_rows
        self.pitch = (side + 1) * PITCH
        self.lead = self.pitch + PITCH
        self.padded = (side + 2) * self.pitch + 2 * PITCH
        self.group = 2 if side % 2 == 0 else side


def zero_rows(ref):
    rows = ref.shape[0]
    step = 16
    while rows % (step * 2) == 0 and step < 256:
        step = step * 2

    @pl.loop(0, rows // step)
    def _(number):
        ref[rows_at(number * step, step), :] = jnp.zeros((step, ref.shape[1]), ref.dtype)


def store_taps(mid_ref, small_ref, at, act):
    before, after_ = (earlier(act), later(act))
    mid_ref[at, 0:128] = before[:, :128].astype(BF16)
    mid_ref[at, 128:256] = act[:, :128].astype(BF16)
    mid_ref[at, 256:384] = after_[:, :128].astype(BF16)
    before, act, after_ = (before[:, 128:], act[:, 128:], after_[:, 128:])
    lane = lax.broadcasted_iota(jnp.int32, act.shape, 1)
    mid_ref[at, 384:512] = jnp.where(
        lane < 32, before, jnp.where(lane < 64, pltpu.roll(act, 32, 1), pltpu.roll(after_, 64, 1))
    ).astype(BF16)
    small_ref[at, :] = jnp.where(
        lane < 32, pltpu.roll(before, 96, 1), jnp.where(lane < 64, act, pltpu.roll(after_, 32, 1))
    ).astype(BF16)


def tap_start(grid, base, tap, sign):
    return base + sign * ((tap // 3 - 1) * grid.pitch + (tap % 3 - 1) * PITCH)


def convolve(grid, taps, kernels, rest_ref, acc_ref, stage_ref, e_ref, stage_sem, sums_ref, length):
    mid_ref, small_ref = taps
    main_ref, last_ref, small_kernel_ref = kernels
    group_rows = grid.group * grid.pitch
    stage_rows = grid.group * grid.line_rows
    groups = grid.side // grid.group
    sums_ref[...] = jnp.zeros_like(sums_ref)
    mask = frame_mask(grid.line_rows, length, SECOND)
    edge = jnp.zeros((grid.pitch, 256), F32)
    rest_ref[PITCH : grid.lead, :] = edge
    end = grid.lead + grid.side * grid.pitch
    rest_ref[end : end + grid.pitch, :] = edge

    @pl.loop(0, groups)
    def _(group):
        base = grid.lead + group * group_rows
        total = None
        for place in range(3):
            part = jnp.dot(
                mid_ref[rows_at(base + (place - 1) * PITCH, group_rows), :],
                last_ref[place],
                preferred_element_type=F32,
            )
            total = part if total is None else total + part
        rest_ref[rows_at(base, group_rows), :] = total

    lane = lax.broadcasted_iota(jnp.int32, (grid.line_rows, 128), 1)

    def staged(group, slot):
        return pltpu.make_async_copy(
            stage_ref.at[slot],
            e_ref.at[rows_at(group * stage_rows, stage_rows), :],
            stage_sem.at[slot],
        )

    @pl.loop(0, groups)
    def _(group):
        base = grid.lead + group * group_rows
        slot = lax.rem(group, 2)
        for tap in range(9):
            part = jnp.dot(
                mid_ref[rows_at(tap_start(grid, base, tap, 1), group_rows), :],
                main_ref[tap],
                preferred_element_type=F32,
            )
            acc_ref[:, 0:256] = part if tap == 0 else acc_ref[:, 0:256] + part
        near = [small_ref[rows_at(tap_start(grid, base, tap, 1), group_rows), :] for tap in range(9)]
        acc_ref[:, 256:384] = jnp.dot(
            jnp.concatenate(near, axis=1), small_kernel_ref[...], preferred_element_type=F32
        )

        @pl.when(group >= 2)
        def _():
            staged(group - 2, slot).wait()

        for number in range(grid.group):
            rows = grid.line_rows
            start = base + number * grid.pitch
            last = (
                rest_ref[rows_at(start - grid.pitch, rows), 0:128]
                + pltpu.roll(rest_ref[rows_at(start, rows), 0:128], 64, 1)
                + rest_ref[rows_at(start + grid.pitch, rows), 128:256]
            )
            lines = slice(number * grid.pitch, number * grid.pitch + rows)
            values = jnp.concatenate(
                [acc_ref[lines, 0:256], jnp.where(lane < 64, last, 0.0), acc_ref[lines, 256:384]],
                axis=1,
            )
            stage_ref[slot, number * rows : (number + 1) * rows, :] = values
            masked = values * mask
            sums_ref[0:8] += partial_sum(masked)
            sums_ref[8:16] += partial_sum(masked * values)
        staged(group, slot).start()

    for group in range(max(groups - 2, 0), groups):
        staged(group, group % 2).wait()


def conv_scratch(grid):
    group_rows = grid.group * grid.pitch
    return [
        pltpu.VMEM((9, 512, 256), BF16),
        pltpu.VMEM((3, 512, 256), BF16),
        pltpu.VMEM((1152, 128), BF16),
        pltpu.VMEM((grid.padded, 512), BF16),
        pltpu.VMEM((grid.padded, 128), BF16),
        pltpu.VMEM((grid.rows, REDUCED), BF16),
        pltpu.VMEM((grid.padded, 256), F32),
        pltpu.VMEM((group_rows, 384), F32),
        pltpu.VMEM((2, grid.group * grid.line_rows, SECOND), F32),
        pltpu.VMEM((16, SECOND), F32),
        pltpu.SemaphoreType.DMA((3,)),
        pltpu.SemaphoreType.DMA((3,)),
        pltpu.SemaphoreType.DMA((2,)),
    ]


def conv_outputs(grid, width):
    return (
        shape((grid.rows, REDUCED), BF16),
        shape((grid.padded, 512), BF16),
        shape((grid.padded, 128), BF16),
        shape((grid.rows, SECOND), F32),
        shape((2, SECOND), F32),
        shape((3, width), F32),
    )


def copies(sources, targets, sem_ref):
    return [
        pltpu.make_async_copy(source, target, sem_ref.at[number])
        for number, (source, target) in enumerate(zip(sources, targets))
    ]


def run_convolution(grid, length, far_kernels, outputs, scratch, fill):
    h_out, mid_out, small_out, e_out, sums_out = outputs
    kernels, (mid_ref, small_ref, h_ref), rest = (scratch[:3], scratch[3:6], scratch[6:])
    rest_ref, acc_ref, stage_ref, sums_ref, in_sem, out_sem, stage_sem = rest
    arriving = copies(far_kernels, kernels, in_sem)
    for copy in arriving:
        copy.start()
    zero_rows(mid_ref)
    zero_rows(small_ref)
    fill(h_ref, mid_ref, small_ref)
    leaving = copies((mid_ref, small_ref, h_ref), (mid_out, small_out, h_out), out_sem)
    for copy in leaving:
        copy.start()
    for copy in arriving:
        copy.wait()
    convolve(
        grid, (mid_ref, small_ref), kernels, rest_ref, acc_ref, stage_ref, e_out, stage_sem, sums_ref, length
    )
    write_sums(sums_out, sums_ref, 0, SECOND)
    for copy in leaving:
        copy.wait()


def write_sums(out_ref, sums_ref, lo, hi):
    for number in range(2):
        out_ref[number : number + 1, lo:hi] = jnp.sum(
            sums_ref[8 * number : 8 * number + 8], axis=0, keepdims=True
        )


def first_pointwise(parts, length_ref, count_ref, x_ref, p_ref, mid_ref, rest_ref, u_ref):
    rows = u_ref.shape[0]
    step = 112 if rows % 112 == 0 else PITCH
    length, count = (length_ref[0], count_ref[0])
    for part in range(parts):
        product = lax.dot_general(
            x_ref[part], p_ref[part], (((0,), (1,)), ((), ())), preferred_element_type=F32
        )
        u_ref[...] = product if part == 0 else u_ref[...] + product
    mask = frame_mask(step, length, FIRST)

    def summed(number, carry):
        return carry + partial_sum(u_ref[rows_at(number * step, step), :] * mask)

    total = lax.fori_loop(0, rows // step, summed, jnp.zeros((8, FIRST), F32))
    total = jnp.sum(total, axis=0, keepdims=True)
    offset = (total / jnp.full((1, FIRST), jnp.maximum(count, 1.0), F32)).astype(BF16)
    wide_offset = offset.astype(F32)
    tail = jnp.broadcast_to(wide_offset, (PITCH, FIRST)).astype(BF16)
    places = ((rest_ref, 0, 0, DIRECT), (mid_ref, 0, DIRECT, SECOND), (rest_ref, DIRECT, SECOND, FIRST))
    for ref, at, lo, hi in places:
        ref[rows : rows + PITCH, at : at + hi - lo] = tail[:, lo:hi]

    @pl.loop(0, rows // step)
    def _(number):
        here = rows_at(number * step, step)
        values = u_ref[here, :] * mask - wide_offset
        for ref, at, lo, hi in places:
            ref[here, at : at + hi - lo] = values[:, lo:hi].astype(BF16)


def each_chunk(local_rows, parts, place, refs, visit):
    step = 112 if local_rows % 112 == 0 else PITCH
    for number, ref in enumerate(refs):
        source = lax.rem(place - number + parts, parts)
        offset = ref[local_rows : local_rows + PITCH, :].astype(F32)[0:1]

        @pl.loop(0, local_rows // step)
        def _(chunk):
            at = rows_at(chunk * step, step)
            visit(source * local_rows + chunk * step, step, ref[at, :].astype(F32) + offset)


def first_sums(local_rows, parts, place_ref, count_ref, *refs):
    mids, (out_sums_ref, sums_ref) = (refs[:parts], refs[parts:])
    sums_ref[...] = jnp.zeros_like(sums_ref)

    def visit(row, size, values):
        sums_ref[0:8] += partial_sum(values)
        sums_ref[8:16] += partial_sum(values * values)

    each_chunk(local_rows, parts, place_ref[0], mids, visit)
    write_sums(out_sums_ref, sums_ref, 0, REDUCED)
    out_sums_ref[2:3, :] = jnp.full((1, REDUCED), count_ref[0], F32)


def reduced_moments(sums_in_ref, moment_ref, lo, hi):
    total = total_of(sums_in_ref)
    count = total[2:3]
    center, inverse = moments(total[0:1], total[1:2], count)
    moment_ref[0:1, :] = center
    moment_ref[1:2, :] = inverse
    moment_ref[2:3, :] = count
    return (center[:, lo:hi], inverse[:, lo:hi])


def first_convolve(grid, block, local_rows, parts, length_ref, place_ref, *refs):
    mids, (sums_in_ref, gain_ref, shift_ref), refs = (refs[:parts], refs[parts : parts + 3], refs[parts + 3 :])
    far_kernels, outputs, moment_ref, scratch = (refs[:3], refs[3:8], refs[8], refs[9:])
    length = length_ref[0]
    center, inverse = reduced_moments(sums_in_ref, moment_ref, 0, REDUCED)
    gain, shift = (gain_ref[block : block + 1], shift_ref[block : block + 1])

    def fill(h_ref, mid_ref, small_ref):
        def visit(row, size, values):
            @pl.when(row < grid.rows)
            def _():
                scaled = (values - center) * inverse
                h_ref[rows_at(row, size), :] = scaled.astype(BF16)
                act = silu(gain * scaled + shift) * frame_mask(size, length, REDUCED)
                line = row // grid.line_rows
                at = grid.lead + line * grid.pitch + row - line * grid.line_rows
                store_taps(mid_ref, small_ref, rows_at(at, size), act)

        each_chunk(local_rows, parts, place_ref[0], mids, visit)

    run_convolution(grid, length, far_kernels, outputs, scratch, fill)


def pool_planes(grid, plane_ref, q_ref, lo, sums_ref, length, window):
    rows = grid.line_rows
    mask = frame_mask(rows, length)
    sums_ref[...] = jnp.zeros_like(sums_ref)

    @pl.loop(0, grid.side)
    def _(line):
        start = line * rows
        values = (
            plane_ref[rows_at(start, rows), :]
            + plane_ref[rows_at(start + rows, rows), :]
            + plane_ref[rows_at(start + 2 * rows, rows), :]
        ) * box_scale(line, grid.side, window)
        q_ref[rows_at(start, rows), lo : lo + POOLED] = values
        masked = values * mask
        sums_ref[0:8] += partial_sum(masked)
        sums_ref[8:16] += partial_sum(masked * values)


def clear_edges(grid, plane_ref):
    rows = grid.line_rows
    plane_ref[0:rows] = jnp.zeros((rows, POOLED), F32)
    plane_ref[grid.rows + rows : grid.rows + 2 * rows] = jnp.zeros((rows, POOLED), F32)


def first_pool(grid, local_rows, parts, length_ref, place_ref, *refs):
    rests, refs = (refs[:parts], refs[parts:])
    q_ref, out_sums_ref, all_ref, plane_ref, sums_ref, pool_sums_ref = refs
    length = length_ref[0]
    rows = grid.line_rows
    clear_edges(grid, plane_ref)
    sums_ref[...] = jnp.zeros_like(sums_ref)

    def visit(row, size, values):
        at = rows_at(row, size)
        all_ref[at, :] = values
        sums_ref[0:8] += partial_sum(values[:, :DIRECT])
        sums_ref[8:16] += partial_sum(values[:, :DIRECT] * values[:, :DIRECT])

    each_chunk(local_rows, parts, place_ref[0], rests, visit)

    @pl.loop(0, grid.side)
    def _(line):
        at = rows_at(line * rows, rows)
        q_ref[at, 0:DIRECT] = all_ref[at, 0:DIRECT]
        plane_ref[rows_at((line + 1) * rows, rows), :] = plane_box(all_ref[at, DIRECT:])

    pool_planes(grid, plane_ref, q_ref, DIRECT, pool_sums_ref, length, box_window(grid.side, length))
    write_sums(out_sums_ref, sums_ref, 0, DIRECT)
    write_sums(out_sums_ref, pool_sums_ref, DIRECT, DIRECT + POOLED)


def outer_moments(center, inverse, count, outer_ref):
    outer_ref[0:1, :] = center
    outer_ref[1:2, :] = inverse
    outer_ref[2:3, :] = jnp.concatenate([count[:, 0:128]] * (OUTER // 128), axis=1)


def first_output(grid, small, block, length_ref, q_far, e_far, moment_ref, e_sums_ref, rest_sums_ref, gain_ref, shift_ref, *refs):
    pooled_ref, h_far, slope_far, outer_ref, pooled_slope_ref, pooled_product_ref, *refs = refs
    q_ref, e_ref, h_ref, slope_ref, q_sem, e_sem, h_sem, slope_sem = refs
    rows = grid.line_rows
    wide = 2 * rows
    pairs = grid.side // 2

    def arriving(pair, slot):
        at = rows_at(pair * wide, wide)
        return [
            pltpu.make_async_copy(q_far.at[at, :], q_ref.at[slot], q_sem.at[slot]),
            pltpu.make_async_copy(e_far.at[at, :], e_ref.at[slot], e_sem.at[slot]),
        ]

    def leaving(pair, slot):
        at = rows_at(pair * wide, wide)
        return [
            pltpu.make_async_copy(h_ref.at[slot], h_far.at[at, :], h_sem.at[slot]),
            pltpu.make_async_copy(slope_ref.at[slot], slope_far.at[at, :], slope_sem.at[slot]),
        ]

    for copy in arriving(0, 0):
        copy.start()
    mask = frame_mask(rows, length_ref[0], OUTER)
    e_total, rest_total = (total_of(e_sums_ref), total_of(rest_sums_ref))
    total = jnp.concatenate(
        [rest_total[0:2, :DIRECT], e_total[0:2], rest_total[0:2, DIRECT:]], axis=1
    )
    count = jnp.concatenate([moment_ref[2:3, 0:128]] * (OUTER // 128), axis=1)
    center, inverse = moments(total[0:1], total[1:2], count)
    outer_moments(center, inverse, count, outer_ref)
    matrix = pool_matrix(small.side, False)
    gain, shift = (gain_ref[block : block + 1], shift_ref[block : block + 1])

    @pl.loop(0, pairs)
    def _(pair):
        slot = lax.rem(pair, 2)

        @pl.when(pair + 1 < pairs)
        def _():
            for copy in arriving(pair + 1, 1 - slot):
                copy.start()

        for copy in arriving(pair, slot):
            copy.wait()

        @pl.when(pair >= 2)
        def _():
            for copy in leaving(pair - 2, slot):
                copy.wait()

        acts, slopes, products = ([], [], [])
        for number in range(2):
            lines = slice(number * rows, (number + 1) * rows)
            values = jnp.concatenate(
                [q_ref[slot, lines, :DIRECT], e_ref[slot, lines, :], q_ref[slot, lines, DIRECT:]],
                axis=1,
            )
            scaled = (values - center) * inverse
            h_ref[slot, lines, :] = scaled.astype(BF16)
            shifted = gain * scaled + shift
            gate = sigmoid(shifted)
            gate_mask = gate * mask
            act = shifted * gate_mask
            slope = gate_mask + act * (1.0 - gate)
            low_slope = slope.astype(BF16)
            slope_ref[slot, lines, :] = low_slope
            acts.append(act.astype(BF16))
            slopes.append(low_slope)
            products.append((slope * scaled).astype(BF16))
        for copy in leaving(pair, slot):
            copy.start()
        at = rows_at(pair * small.line_rows, small.line_rows)
        for ref, pieces in (
            (pooled_ref, acts),
            (pooled_slope_ref, slopes),
            (pooled_product_ref, products),
        ):
            ref[at, :] = jnp.dot(
                matrix, jnp.concatenate(pieces, axis=0), preferred_element_type=F32
            ).astype(BF16)

    for pair in range(max(pairs - 2, 0), pairs):
        for copy in leaving(pair, pair % 2):
            copy.wait()


def second_pointwise(grid, length_ref, count_ref, x_ref, p_ref, q_ref, out_sums_ref, plane_ref, sums_ref, pool_sums_ref):
    length = length_ref[0]
    rows = grid.line_rows
    sums_ref[...] = jnp.zeros_like(sums_ref)
    clear_edges(grid, plane_ref)
    q_ref[...] = lax.dot_general(
        x_ref[...], p_ref[...], (((1,), (1,)), ((), ())), preferred_element_type=F32
    )

    @pl.loop(0, grid.side)
    def _(line):
        values = q_ref[rows_at(line * rows, rows), :]
        sums_ref[0:8] += partial_sum(values[:, :SECOND])
        sums_ref[8:16] += partial_sum(values[:, :SECOND] * values[:, :SECOND])
        plane_ref[rows_at((line + 1) * rows, rows), :] = plane_box(values[:, SECOND:])

    pool_planes(grid, plane_ref, q_ref, SECOND, pool_sums_ref, length, box_window(grid.side, length))
    write_sums(out_sums_ref, sums_ref, 0, SECOND)
    write_sums(out_sums_ref, pool_sums_ref, SECOND, FIRST)
    out_sums_ref[2:3, :] = jnp.full((1, FIRST), count_ref[0], F32)


def second_convolve(grid, block, length_ref, q_ref, sums_in_ref, gain_ref, shift_ref, *refs):
    far_kernels, outputs, moment_ref, scratch = (refs[:3], refs[3:8], refs[8], refs[9:])
    length = length_ref[0]
    center, inverse = reduced_moments(sums_in_ref, moment_ref, DIRECT, SECOND)
    gain, shift = (gain_ref[block : block + 1], shift_ref[block : block + 1])
    mask = frame_mask(grid.line_rows, length, REDUCED)

    def fill(h_ref, mid_ref, small_ref):
        @pl.loop(0, grid.side)
        def _(line):
            at = rows_at(line * grid.line_rows, grid.line_rows)
            scaled = (q_ref[at, DIRECT:SECOND] - center) * inverse
            h_ref[at, :] = scaled.astype(BF16)
            act = silu(gain * scaled + shift) * mask
            store_taps(
                mid_ref, small_ref, rows_at(grid.lead + line * grid.pitch, grid.line_rows), act
            )

    run_convolution(grid, length, far_kernels, outputs, scratch, fill)


def second_output(grid, block, length_ref, q_ref, e_ref, moment_ref, sums_in_ref, gain_ref, shift_ref, cot_ref, act_ref, h_ref, error_ref, outer_ref, out_sums_ref, sums_ref):
    rows = grid.line_rows
    side, frames = (grid.side, cot_ref.shape[1])
    mask = frame_mask(rows, length_ref[0], OUTER)
    total = total_of(sums_in_ref)
    count = moment_ref[2:3, 0:SECOND]
    center, inverse = moments(total[0:1], total[1:2], count)
    center = jnp.concatenate([moment_ref[0:1, :DIRECT], center, moment_ref[0:1, SECOND:]], axis=1)
    inverse = jnp.concatenate([moment_ref[1:2, :DIRECT], inverse, moment_ref[1:2, SECOND:]], axis=1)
    outer_moments(center, inverse, count, outer_ref)
    sums_ref[...] = jnp.zeros_like(sums_ref)
    gain, shift = (gain_ref[block : block + 1], shift_ref[block : block + 1])
    gap = jnp.zeros((rows, 64), F32)
    unused = jnp.zeros((side, PITCH - frames, CHANNELS), F32)

    @pl.loop(0, side)
    def _(line):
        at = rows_at(line * rows, rows)
        places = pl.ds(line * side, side)
        values = jnp.concatenate([q_ref[at, :DIRECT], e_ref[at, :], q_ref[at, SECOND:]], axis=1)
        scaled = (values - center) * inverse
        h_ref[at, :] = scaled.astype(BF16)
        shifted = gain * scaled + shift
        gate = sigmoid(shifted)
        act = (shifted * gate * mask).reshape(side, PITCH, OUTER)[:, :frames].astype(BF16)
        act_ref[places, :, 0:576] = act[:, :, 0:576]
        act_ref[places, :, 576:CHANNELS] = act[:, :, 640:OUTER]
        slope = gate * (1.0 + shifted * (1.0 - gate))
        grad = jnp.concatenate([cot_ref[places].astype(F32), unused], axis=1)
        grad = grad.reshape(rows, CHANNELS)
        grad = jnp.concatenate([grad[:, :576], gap, grad[:, 576:]], axis=1)
        error = grad * slope * mask
        error_ref[at, :] = error.astype(BF16)
        sums_ref[0:8] += partial_sum(error)
        sums_ref[8:16] += partial_sum(error * scaled)

    write_sums(out_sums_ref, sums_ref, 0, OUTER)


def spread_matrix(grid, small):
    return None if small is None else pool_matrix(small.side, True)[: grid.line_rows]


def outer_error(slopes, small, grad_ref, matrix, line, lo, hi):
    values = slopes.astype(F32)
    if small is None:
        return values
    coarse = grad_ref[rows_at((line // 2) * small.line_rows, small.line_rows), lo:hi]
    return values * jnp.dot(matrix, coarse, preferred_element_type=F32)


class Lines:
    def __init__(self, grid, sources, buffers, sem_ref):
        self.step = 2 if grid.side % 2 == 0 else 1
        self.size = self.step * grid.line_rows
        self.steps = grid.side // self.step
        self.sources, self.buffers, self.sem = (sources, buffers, sem_ref)

    def copies(self, step, slot):
        at = rows_at(step * self.size, self.size)
        return [
            pltpu.make_async_copy(
                ref.at[at, pl.ds(lo, hi - lo)],
                buffer.at[slot, :, pl.ds(place, hi - lo)],
                self.sem.at[number, slot],
            )
            for number, ((ref, lo, hi), (buffer, place)) in enumerate(
                zip(self.sources, self.buffers)
            )
        ]

    def first(self):
        for copy in self.copies(0, 0):
            copy.start()

    def run(self, visit):
        @pl.loop(0, self.steps)
        def _(step):
            slot = lax.rem(step, 2)

            @pl.when(step + 1 < self.steps)
            def _():
                for copy in self.copies(step + 1, 1 - slot):
                    copy.start()

            for copy in self.copies(step, slot):
                copy.wait()
            visit(step, slot)

    @staticmethod
    def rows(grid):
        return (2 if grid.side % 2 == 0 else 1) * grid.line_rows


def second_back(grid, small, block, slots, length_ref, first_ref, h_far, outer_ref, sums_in_ref, gain_ref, slope_far, *refs):
    grad_ref, refs = (refs[0], refs[1:]) if small is not None else (None, refs)
    mid_far, few_far, d_far, total_ref, out_ref, *refs = refs
    d_ref, h_ref, slope_ref, mid_ref, few_ref, mid_acc_ref, small_acc_ref, turned_ref, sem_ref, in_sem, out_sem = refs
    lo, hi = (DIRECT, DIRECT + SECOND)
    lines = Lines(grid, ((h_far, lo, hi), (slope_far, lo, hi)), ((h_ref, 0), (slope_ref, 0)), sem_ref)
    lines.first()
    arriving = copies((mid_far, few_far), (mid_ref, few_ref), in_sem)
    for copy in arriving:
        copy.start()
    total = total_of(sums_in_ref)
    total_ref[...] = total
    count = outer_ref[2:3, lo:hi]
    mean_r = total[0:1, lo:hi] / count
    mean_rh = total[1:2, lo:hi] / count
    factor = gain_ref[block : block + 1, lo:hi] * outer_ref[1:2, lo:hi]
    mask = frame_mask(grid.line_rows, length_ref[0], SECOND)
    matrix = spread_matrix(grid, small)
    zero_rows(d_ref)
    rows = grid.line_rows

    def visit(step, slot):
        for number in range(lines.step):
            line = step * lines.step + number
            here = slice(number * rows, (number + 1) * rows)
            scaled = h_ref[slot, here, :].astype(F32)
            error = outer_error(slope_ref[slot, here, :], small, grad_ref, matrix, line, lo, hi)
            back = factor * (error - mean_r - scaled * mean_rh) * mask
            d_ref[rows_at(grid.lead + line * grid.pitch, rows), :] = back.astype(BF16)

    lines.run(visit)
    leaving = pltpu.make_async_copy(d_ref, d_far, out_sem.at[0])
    leaving.start()
    for copy in arriving:
        copy.wait()
    kernel_grads(grid, slots, first_ref, mid_ref, few_ref, d_ref, out_ref, mid_acc_ref, small_acc_ref, turned_ref)
    leaving.wait()


def second_back_scratch(grid, slots):
    rows = Lines.rows(grid)
    return [
        pltpu.VMEM((grid.padded, SECOND), BF16),
        pltpu.VMEM((2, rows, SECOND), BF16),
        pltpu.VMEM((2, rows, SECOND), BF16),
        pltpu.VMEM((grid.padded, 512), BF16),
        pltpu.VMEM((grid.padded, 128), BF16),
        pltpu.VMEM((slots, 384, 256), F32),
        pltpu.VMEM((slots, 128, 128), F32),
        pltpu.VMEM((MID_IN + 128, 128), F32),
        pltpu.SemaphoreType.DMA((2, 2)),
        pltpu.SemaphoreType.DMA((2,)),
        pltpu.SemaphoreType.DMA((1,)),
    ]


def conv_back(grid, block, length_ref, d_ref, reduced_ref, reduced_gain_ref, reduced_shift_ref, *refs):
    far_kernels, (r_ref, out_sums_ref), refs = (refs[:3], refs[3:5], refs[5:])
    kernels, (last_ref, acc_ref, sums_ref, in_sem) = (refs[:3], refs[3:])
    main_ref, rest_ref, small_ref = kernels
    arriving = copies(far_kernels, kernels, in_sem)
    for copy in arriving:
        copy.start()
    rows = grid.line_rows
    group_rows = grid.group * grid.pitch
    sums_ref[...] = jnp.zeros_like(sums_ref)
    mask = frame_mask(rows, length_ref[0], REDUCED)
    gain, shift = (reduced_gain_ref[block : block + 1], reduced_shift_ref[block : block + 1])
    turned = (((1,), (1,)), ((), ()))
    lane = lax.broadcasted_iota(jnp.int32, (rows, 128), 1)
    wide_lane = lax.broadcasted_iota(jnp.int32, (grid.pitch, 128), 1)

    @pl.loop(0, grid.side)
    def _(line):
        place = grid.lead + line * grid.pitch
        here = d_ref[rows_at(place, grid.pitch), 256:384].astype(F32)
        further = d_ref[rows_at(place + grid.pitch, grid.pitch), 256:384].astype(F32)
        at = rows_at(place, grid.pitch)
        last_ref[at, 0:128] = jnp.where(wide_lane < 64, further, pltpu.roll(here, 64, 1)).astype(
            BF16
        )
        last_ref[at, 128:256] = d_ref[rows_at(place - grid.pitch, grid.pitch), 256:384]

    last_ref[grid.lead - PITCH : grid.lead, :] = jnp.zeros((PITCH, 256), BF16)
    end = grid.lead + grid.side * grid.pitch
    last_ref[end : end + PITCH, :] = jnp.zeros((PITCH, 256), BF16)
    for copy in arriving:
        copy.wait()

    @pl.loop(0, grid.side // grid.group)
    def _(group):
        base = grid.lead + group * group_rows
        for tap in range(9):
            part = lax.dot_general(
                d_ref[rows_at(tap_start(grid, base, tap, -1), group_rows), 0:256],
                main_ref[tap],
                turned,
                preferred_element_type=F32,
            )
            acc_ref[:, 0:512] = part if tap == 0 else acc_ref[:, 0:512] + part
        for place in range(3):
            acc_ref[:, 0:512] += lax.dot_general(
                last_ref[rows_at(base - (place - 1) * PITCH, group_rows), :],
                rest_ref[place],
                turned,
                preferred_element_type=F32,
            )
        near = [
            d_ref[rows_at(tap_start(grid, base, tap, -1), group_rows), 384:512] for tap in range(9)
        ]
        acc_ref[:, 512:640] = jnp.dot(
            jnp.concatenate(near, axis=1), small_ref[...], preferred_element_type=F32
        )
        for number in range(grid.group):
            line = group * grid.group + number
            lines = slice(number * grid.pitch, number * grid.pitch + rows)
            rest, small = (acc_ref[lines, 384:512], acc_ref[lines, 512:640])
            one = jnp.where(lane < 32, rest, pltpu.roll(small, 32, 1))
            two = jnp.where(lane < 32, pltpu.roll(rest, 96, 1), small)
            three = jnp.where(lane < 32, pltpu.roll(rest, 64, 1), pltpu.roll(small, 96, 1))
            wide = later(acc_ref[lines, 0:128]) + acc_ref[lines, 128:256]
            wide = wide + earlier(acc_ref[lines, 256:384])
            narrow = jnp.where(lane < 64, later(one) + two + earlier(three), 0.0)
            back = jnp.concatenate([wide, narrow], axis=1)
            at = rows_at(line * rows, rows)
            scaled = reduced_ref[at, :].astype(F32)
            error = back * silu_slope(gain * scaled + shift) * mask
            r_ref[at, :] = error.astype(BF16)
            sums_ref[0:8] += partial_sum(error)
            sums_ref[8:16] += partial_sum(error * scaled)

    write_sums(out_sums_ref, sums_ref, 0, REDUCED)


def kernel_grads(grid, slots, first_ref, mid_ref, small_ref, d_ref, out_ref, mid_acc_ref, small_acc_ref, turned_ref):
    group_rows = grid.group * grid.pitch
    mid_acc_ref[...] = jnp.zeros_like(mid_acc_ref)
    small_acc_ref[...] = jnp.zeros_like(small_acc_ref)

    def neighbour(slot):
        return jnp.minimum(first_ref[0] + slot, TAPS - 1) // 9

    @pl.loop(0, grid.side // grid.group)
    def _(group):
        base = grid.lead + group * group_rows
        left = d_ref[rows_at(base, group_rows), :].T
        for slot in range(slots):
            tap = lax.rem(jnp.minimum(first_ref[0] + slot, TAPS - 1), 9)
            at = rows_at(
                base + (tap // 3 - 1) * grid.pitch + (lax.rem(tap, 3) - 1) * PITCH, group_rows
            )
            lanes = pl.ds(pl.multiple_of(neighbour(slot) * 128, 128), 128)
            right = jnp.concatenate([mid_ref[at, lanes], mid_ref[at, 384:512]], axis=1)
            mid_acc_ref[slot] += jnp.dot(left[0:384], right, preferred_element_type=F32)
            small_acc_ref[slot] += jnp.dot(
                left[384:512], small_ref[at, :], preferred_element_type=F32
            )

    half = MID_IN // 2
    for slot in range(slots):
        base = slot * TAP_ROWS
        rest = pl.ds(pl.multiple_of(neighbour(slot) * 32, 32), 32)
        for tile in range(3):
            lines = slice(128 * tile, 128 * (tile + 1))
            turned_ref[0:128, :] = mid_acc_ref[slot, lines, 0:128].T
            turned_ref[MID_IN : MID_IN + 128, :] = mid_acc_ref[slot, lines, 128:256].T
            turned_ref[128:MID_IN, :] = turned_ref[
                pl.ds(pl.multiple_of(MID_IN + neighbour(slot) * 32, 32), 32), :
            ]
            if tile < 2:
                out_ref[base + MID_IN * tile : base + MID_IN * (tile + 1), :] = turned_ref[
                    0:MID_IN, :
                ].astype(BF16)
            else:
                folded = turned_ref[0:half, :] + pltpu.roll(turned_ref[half:MID_IN, :], 64, 1)
                out_ref[base + 2 * MID_IN : base + 2 * MID_IN + half, :] = folded.astype(BF16)
        turned_ref[0:128, :] = small_acc_ref[slot].T
        base = base + 2 * MID_IN + half
        out_ref[base : base + SMALL_IN, :] = turned_ref[rest, :].astype(BF16)
    used = slots * TAP_ROWS
    if out_ref.shape[0] > used:
        out_ref[used:, :] = jnp.zeros((out_ref.shape[0] - used, 128), BF16)


def point_back(grid, small, block, kept, length_ref, place_ref, h_far, outer_ref, total_ref, gain_ref, slope_far, *refs):
    first = small is not None
    grad_ref, refs = (refs[0], refs[1:]) if first else (None, refs)
    reduced_far, r_far, moment_ref, sums_in_ref, reduced_gain_ref, x_far, p_far, *refs = refs
    pooled_refs, refs = ((), refs) if first else (refs[:2], refs[2:])
    dx_ref, dp_ref, reduced_total_ref, *refs = refs
    outer_sums_ref, refs = (None, refs) if first else (refs[0], refs[1:])
    h_ref, slope_ref, reduced_ref, r_ref, x_ref, p_ref, du_ref, plane_ref, acc_ref, sem_ref, in_sem, *refs = refs
    rows = grid.line_rows
    pool = OUTER - POOLED
    lines = Lines(
        grid,
        (
            (h_far, 0, DIRECT),
            (h_far, pool, OUTER),
            (slope_far, 0, DIRECT),
            (slope_far, pool, OUTER),
            (reduced_far, 0, REDUCED),
            (r_far, 0, REDUCED),
        ),
        ((h_ref, 0), (h_ref, DIRECT), (slope_ref, 0), (slope_ref, DIRECT), (reduced_ref, 0), (r_ref, 0)),
        sem_ref,
    )
    lines.first()
    arriving = copies((x_far, p_far.at[place_ref[0]] if first else p_far), (x_ref, p_ref), in_sem)
    for copy in arriving:
        copy.start()
    length = length_ref[0]
    matrix = spread_matrix(grid, small)
    total = total_of(sums_in_ref)
    reduced_total_ref[...] = total
    count = outer_ref[2:3, 0:REDUCED]
    mid_r, mid_rh = (total[0:1] / count, total[1:2] / count)
    mid_factor = reduced_gain_ref[block : block + 1] * moment_ref[1:2]
    mask = frame_mask(rows, length, REDUCED)
    window = box_window(grid.side, length)
    clear_edges(grid, plane_ref)

    def constants(lo, hi):
        size = outer_ref[2:3, lo:hi]
        return (
            total_ref[0:1, lo:hi] / size,
            total_ref[1:2, lo:hi] / size,
            gain_ref[block : block + 1, lo:hi] * outer_ref[1:2, lo:hi],
        )

    direct_constants, pool_constants = (constants(0, DIRECT), constants(pool, OUTER))

    def visit(step, slot):
        for number in range(lines.step):
            line = step * lines.step + number
            here = slice(number * rows, (number + 1) * rows)
            at = rows_at(line * rows, rows)

            def section(lo, hi, kept_lo, kept_hi, constant):
                scaled = h_ref[slot, here, kept_lo:kept_hi].astype(F32)
                error = outer_error(
                    slope_ref[slot, here, kept_lo:kept_hi], small, grad_ref, matrix, line, lo, hi
                )
                inner = error - constant[0] - scaled * constant[1]
                return constant[2] * inner * mask[:, : hi - lo]

            du_ref[at, 0:DIRECT] = section(0, DIRECT, 0, DIRECT, direct_constants).astype(BF16)
            scaled = reduced_ref[slot, here, :].astype(F32)
            inner = r_ref[slot, here, :].astype(F32) - mid_r - scaled * mid_rh
            du_ref[at, DIRECT:SECOND] = (mid_factor * inner * mask).astype(BF16)
            pooled = section(pool, OUTER, DIRECT, DIRECT + POOLED, pool_constants)
            plane_ref[rows_at((line + 1) * rows, rows), :] = plane_box(
                pooled * box_scale(line, grid.side, window)
            )

    lines.run(visit)
    for copy in arriving:
        copy.wait()
    acc_ref[...] = jnp.zeros_like(acc_ref)
    if not first:
        refs[0][...] = jnp.zeros_like(refs[0])
    wide = lines.size
    pool_mask = frame_mask(wide, length)

    @pl.loop(0, lines.steps)
    def _(step):
        start = step * wide
        at = rows_at(start, wide)
        pooled = (
            plane_ref[at, :]
            + plane_ref[rows_at(start + rows, wide), :]
            + plane_ref[rows_at(start + 2 * rows, wide), :]
        ) * pool_mask
        du = jnp.concatenate([du_ref[at, 0:SECOND], pooled.astype(BF16)], axis=1)
        dx = jnp.dot(du, p_ref[...], preferred_element_type=F32).astype(BF16)
        dx_ref[at, :] = dx
        if not first:
            for number, ref in enumerate(pooled_refs):
                refs[0][8 * number : 8 * number + 8] += partial_sum(
                    dx.astype(F32) * ref[at, :].astype(F32)
                )
        acc_ref[...] += lax.dot_general(
            x_ref[at, :], du, (((0,), (0,)), ((), ())), preferred_element_type=F32
        )

    if not first:
        write_sums(outer_sums_ref, refs[0], 0, OUTER)
    start = pl.multiple_of(place_ref[0] * kept, 16) if kept < acc_ref.shape[0] else 0
    own = acc_ref[pl.ds(start, kept), :]
    for tile in range(FIRST // 128):
        dp_ref[kept * tile : kept * (tile + 1), :] = own[:, 128 * tile : 128 * (tile + 1)].astype(
            BF16
        )
    used = (FIRST // 128) * kept
    if dp_ref.shape[0] > used:
        dp_ref[used:, :] = jnp.zeros((dp_ref.shape[0] - used, 128), BF16)


def write_taps(buffer_ref, parts, slots, mid_ref, small_ref):
    half = MID_IN // 2

    @pl.loop(0, TAPS)
    def _(tap):
        base = lax.rem(tap, slots) * TAP_ROWS
        part = tap // slots

        def piece(start, size):
            return buffer_ref[part, rows_at(base + start, size), :].astype(F32)

        folded = piece(2 * MID_IN, half)
        mid_ref[tap, :, 0:128] = piece(0, MID_IN)
        mid_ref[tap, :, 128:256] = piece(MID_IN, MID_IN)
        mid_ref[tap, 0:half, 256:320] = folded[:, 0:64]
        mid_ref[tap, half:MID_IN, 256:320] = pltpu.roll(folded, 64, 1)[:, 0:64]
        small_ref[tap] = piece(2 * MID_IN + half, SMALL_IN)


def write_point(read, parts, kept, point_ref, wide_ref):
    for tile in range(FIRST // 128):
        for part in range(parts):
            start, stop = (kept * part, kept * (part + 1))
            values = read(part, kept * tile, kept)
            if kept * parts == CHANNELS:
                wide_ref[start:stop, :] = values
                continue
            for lo, hi, moved in ((0, 576, 0), (640, OUTER, 64)):
                lo, hi = (max(lo, start), min(hi, stop))
                if lo < hi:
                    wide_ref[lo - moved : hi - moved, :] = values[lo - start : hi - start]
        turned = wide_ref[...].T
        if tile < 3:
            point_ref[128 * tile : 128 * (tile + 1), :] = turned
        elif tile == 3:
            point_ref[384:448, :] = turned[0:64]
        else:
            point_ref[448:576, :] = turned


def copy_out(pairs, sem_ref):
    copies = [
        pltpu.make_async_copy(source, target, sem_ref.at[number])
        for number, (source, target) in enumerate(pairs)
    ]
    for copy in copies:
        copy.start()
    for copy in copies:
        copy.wait()


def unpack_second(parts, clips, slots, share, shares_ref, mid_out, small_out, point_out, taps_ref, rows_ref, mid_ref, small_ref, point_ref, wide_ref, sem_ref):
    size = shares_ref.shape[1] - share
    for part in range(parts):
        for clip in range(clips):
            taps_ref[part, share * clip : share * (clip + 1), :] = shares_ref[
                part * clips + clip, 0:share, :
            ]
            rows_ref[part, size * clip : size * (clip + 1), :] = shares_ref[
                part * clips + clip, share : share + size, :
            ]

    def read(part, start, size):
        return rows_ref[part, start : start + size, :].astype(F32)

    write_taps(taps_ref, parts, slots, mid_ref, small_ref)
    write_point(read, parts, OUTER // parts, point_ref, wide_ref)
    copy_out(
        [(mid_ref, mid_out.at[1]), (small_ref, small_out.at[1]), (point_ref, point_out.at[1])],
        sem_ref,
    )


def reorder(parts, clips, share, place, clip, mine_ref, other_ref, buffer_ref):
    for chip in range(clips // 2):
        for step in range(parts):
            source = (chip * parts + step) * share
            part = lax.rem(place - step + parts, parts)
            for swapped, ref in enumerate((mine_ref, other_ref)):
                owner = clip ^ (2 * chip) ^ swapped
                buffer_ref[part, rows_at(owner * share, share), :] = ref[
                    source : source + share, :
                ]


def unpack_taps(parts, clips, slots, share, place_ref, clip_ref, mine_ref, other_ref, *refs):
    totals, refs = (refs[:4], refs[4:])
    mid_in, small_in, mid_out, small_out, gain_out, shift_out, buffer_ref, mid_ref, small_ref, sem_ref = refs
    for block in range(2):
        outer_ref, reduced_ref = totals[2 * block : 2 * block + 2]
        for row, out in enumerate((shift_out, gain_out)):
            at, line = (slice(block, block + 1), slice(row, row + 1))
            out[at, 0:256] = outer_ref[line, 0:256]
            out[at, 256:448] = reduced_ref[line, 0:192]
            out[at, 448:576] = outer_ref[line, 768:896]
            out[at, 576:896] = outer_ref[line, 256:576]
            out[at, 896:1024] = outer_ref[line, 640:768]
    reorder(parts, clips, share, place_ref[0], clip_ref[0], mine_ref, other_ref, buffer_ref)
    write_taps(buffer_ref, parts, slots, mid_ref, small_ref)
    copy_out([(mid_ref, mid_out.at[0]), (small_ref, small_out.at[0])], sem_ref)


def unpack_point(parts, clips, share, place_ref, clip_ref, mine_ref, other_ref, point_in, point_out, buffer_ref, point_ref, wide_ref, sem_ref):
    reorder(parts, clips, share, place_ref[0], clip_ref[0], mine_ref, other_ref, buffer_ref)

    def read(part, start, size):
        return buffer_ref[part, start : start + size, :].astype(F32)

    write_point(read, parts, CHANNELS // parts, point_ref, wide_ref)
    copy_out([(point_ref, point_out.at[0])], sem_ref)


def prepare(parts, mid_in, small_in, point_in, gain_in, shift_in, *refs):
    kernels, (point_ref, second_ref, *vectors) = (refs[:8], refs[8:14])
    for block in range(2):
        main_ref, last_ref, few_ref, back_ref = kernels[4 * block : 4 * block + 4]

        @pl.loop(0, 9)
        def _(tap):
            for number in range(3):
                source = 9 * number + tap
                main_ref[tap, 128 * number : 128 * (number + 1), :] = mid_in[block, source, 0:128, 0:256]
                main_ref[tap, 384 + 32 * number : 416 + 32 * number, :] = mid_in[
                    block, source, 128:MID_IN, 0:256
                ]
            main_ref[tap, 480:512, :] = jnp.zeros((32, 256), BF16)
            small = jnp.concatenate(
                [small_in[block, 9 * number + tap] for number in range(3)]
                + [jnp.zeros((32, 128), BF16)],
                axis=0,
            )
            at = pl.ds(pl.multiple_of(tap * 128, 128), 128)
            few_ref[at, :] = small
            back_ref[at, :] = small.astype(F32).T.astype(BF16)

        @pl.loop(0, 3)
        def _(place):
            for number in range(3):
                for rows, start, size in (
                    (slice(0, 128), 128 * number, 128),
                    (slice(128, MID_IN), 384 + 32 * number, 32),
                ):
                    pieces = [
                        mid_in[block, 9 * number + 3 * line + place, rows, 256:MID_OUT].astype(F32)
                        for line in range(3)
                    ]
                    pieces.append(jnp.zeros((size, 64), F32))
                    last_ref[place, start : start + size, :] = jnp.concatenate(
                        pieces, axis=1
                    ).astype(BF16)
            last_ref[place, 480:512, :] = jnp.zeros((32, 256), BF16)

    own = point_ref.shape[2]
    for lo, hi, at in ((0, 448, 0), (448, SQUEEZED, SECOND)):
        values = point_in[0, lo:hi, :].astype(F32)
        for part in range(parts):
            point_ref[part, at : at + hi - lo, :] = values[:, own * part : own * (part + 1)].astype(
                BF16
            )
        values = point_in[1, lo:hi, :].astype(F32)
        gap = jnp.zeros((hi - lo, 64), F32)
        second_ref[at : at + hi - lo, :] = jnp.concatenate(
            [values[:, :576], gap, values[:, 576:]], axis=1
        ).astype(BF16)
    for part in range(parts):
        point_ref[part, 448:SECOND, :] = jnp.zeros((64, own), BF16)
    second_ref[448:SECOND, :] = jnp.zeros((64, OUTER), BF16)
    for source, outer, reduced in ((gain_in, vectors[0], vectors[1]), (shift_in, vectors[2], vectors[3])):
        outer[:, 0:256] = source[:, 0:256]
        outer[:, 256:576] = source[:, 576:896]
        outer[:, 576:640] = jnp.zeros((2, 64), F32)
        outer[:, 640:768] = source[:, 896:1024]
        outer[:, 768:896] = source[:, 448:576]
        reduced[:, 0:192] = source[:, 256:448]
        reduced[:, 192:256] = jnp.zeros((2, 64), F32)


def round_up(value, unit):
    return -(-value // unit) * unit


def spread_over(values, axis, size):
    received = [values]
    for step in range(1, size):
        perm = [(source, (source + step) % size) for source in range(size)]
        received.append(lax.ppermute(values, axis, perm))
    return received


def after(values, earlier):
    return lax.optimization_barrier((values, earlier))[0]


def shared_sum(packed, clips):
    pieces = packed.reshape(clips, packed.shape[0] // clips, 128)
    pieces = lax.all_to_all(pieces, "dp", 0, 0, tiled=True)
    return jnp.sum(pieces.astype(F32), axis=0).astype(BF16)


def gather_steps(share, parts, clips):
    column = jnp.concatenate(spread_over(share, "branch", parts), axis=0)
    columns = [column]
    for chip in range(1, clips // 2):
        perm = [(source, source ^ (2 * chip)) for source in range(clips)]
        columns.append(lax.ppermute(column, "dp", perm))
    mine = jnp.concatenate(columns, axis=0)
    other = lax.ppermute(mine, "dp", [(source, source ^ 1) for source in range(clips)])
    return (mine, other)


def on_device(frames, lengths, cotangent, pointwise, conv_mid, conv_small, gains, shifts):
    parts = lax.axis_size("branch")
    clips = lax.axis_size("dp")
    place = lax.axis_index("branch").astype(jnp.int32)
    side = frames.shape[2]
    grid, small = (Grid(side), Grid(side // 2))
    cells = side * side
    own_channels = frames.shape[-1]
    length = lengths.astype(jnp.int32)
    half_length = length // 2
    place_one = place.reshape(1)

    own = frames[0].transpose(1, 2, 0, 3).reshape(grid.rows, own_channels)
    local = -(-cells // parts)
    local_rows = local * PITCH
    split = own
    if parts * local_rows > grid.rows:
        split = jnp.pad(own, ((0, parts * local_rows - grid.rows), (0, 0)))
    by_places = lax.all_to_all(
        split.reshape(parts, local_rows, own_channels).transpose(0, 2, 1), "branch", 0, 0, tiled=True
    )
    kernel_shapes = (
        shape((9, 512, 256), BF16),
        shape((3, 512, 256), BF16),
        shape((1152, 128), BF16),
        shape((1152, 128), BF16),
    )
    prepared = call(
        functools.partial(prepare, parts),
        (
            *kernel_shapes,
            *kernel_shapes,
            shape((parts, FIRST, own_channels), BF16),
            shape((FIRST, OUTER), BF16),
            shape((2, OUTER), F32),
            shape((2, REDUCED), F32),
            shape((2, OUTER), F32),
            shape((2, REDUCED), F32),
        ),
    )(conv_mid, conv_small, pointwise.swapaxes(1, 2), gains, shifts)
    kernels = (prepared[0:4], prepared[4:8])
    point_first, point_second, outer_gain, reduced_gain, outer_shift, reduced_shift = prepared[8:]

    local_cells = jnp.clip(cells - place * local, 0, local)
    local_count = (length * local_cells).astype(F32)
    mid, rest = call(
        functools.partial(first_pointwise, parts),
        (
            shape((local_rows + PITCH, REDUCED), BF16),
            shape((local_rows + PITCH, DIRECT + POOLED), BF16),
        ),
        [pltpu.VMEM((local_rows, FIRST), F32)],
        scalars=2,
    )(length, local_count, by_places, point_first)
    mids = spread_over(mid, "branch", parts)
    rests = spread_over(after(rest, mids), "branch", parts)
    count = length.astype(F32) * float(cells)
    sums = call(
        functools.partial(first_sums, local_rows, parts),
        shape((3, REDUCED), F32),
        [pltpu.VMEM((16, REDUCED), F32)],
        scalars=2,
    )(place_one, count, *mids)
    sums = lax.all_gather(sums, "dp")
    h_reduced, taps_mid, taps_few, e, e_sums, moment = call(
        functools.partial(first_convolve, grid, 0, local_rows, parts),
        conv_outputs(grid, REDUCED),
        conv_scratch(grid),
        scalars=2,
        flops=2 * 10**10,
        far=range(5 + parts, 8 + parts),
        far_out=range(4),
    )(length, place_one, *mids, sums, reduced_gain, reduced_shift, *kernels[0][:3])
    q_rest, rest_sums = call(
        functools.partial(first_pool, grid, local_rows, parts),
        (shape((grid.rows, DIRECT + POOLED), F32), shape((2, DIRECT + POOLED), F32)),
        [
            pltpu.VMEM((parts * local_rows, DIRECT + POOLED), F32),
            pltpu.VMEM((grid.rows + 2 * grid.line_rows, POOLED), F32),
            pltpu.VMEM((16, DIRECT), F32),
            pltpu.VMEM((16, POOLED), F32),
        ],
        scalars=2,
    )(length, place_one, *rests)
    second_sums = lax.all_gather(jnp.concatenate([e_sums, rest_sums], axis=1), "dp")
    pair = 2 * grid.line_rows
    pooled, h_outer, slope, outer, pooled_slope, pooled_product = call(
        functools.partial(first_output, grid, small, 0),
        (
            shape((small.rows, OUTER), BF16),
            shape((grid.rows, OUTER), BF16),
            shape((grid.rows, OUTER), BF16),
            shape((3, OUTER), F32),
            shape((small.rows, OUTER), BF16),
            shape((small.rows, OUTER), BF16),
        ),
        [
            pltpu.VMEM((2, pair, DIRECT + POOLED), F32),
            pltpu.VMEM((2, pair, SECOND), F32),
            pltpu.VMEM((2, pair, OUTER), BF16),
            pltpu.VMEM((2, pair, OUTER), BF16),
            *[pltpu.SemaphoreType.DMA((2,))] * 4,
        ],
        scalars=1,
        far=(1, 2),
        far_out=(1, 2),
    )(length, q_rest, e, moment, second_sums[:, :, :SECOND], second_sums[:, :, SECOND:], outer_gain, outer_shift)

    small_count = half_length.astype(F32) * float(small.side * small.side)
    q_small, sums_small = call(
        functools.partial(second_pointwise, small),
        (shape((small.rows, FIRST), F32), shape((3, FIRST), F32)),
        [
            pltpu.VMEM((small.rows + 2 * small.line_rows, POOLED), F32),
            pltpu.VMEM((16, SECOND), F32),
            pltpu.VMEM((16, POOLED), F32),
        ],
        scalars=2,
    )(half_length, small_count, pooled, point_second)
    sums_small = lax.all_gather(sums_small, "dp")
    h_reduced_small, taps_mid_small, taps_few_small, e_small, e_sums_small, moment_small = call(
        functools.partial(second_convolve, small, 1),
        conv_outputs(small, FIRST),
        conv_scratch(small),
        scalars=1,
        far=range(5, 8),
        far_out=range(4),
    )(half_length, q_small, sums_small, reduced_gain, reduced_shift, *kernels[1][:3])
    e_sums_small = lax.all_gather(e_sums_small, "dp")
    cot = cotangent[0].transpose(1, 2, 0, 3).reshape(small.side**2, cotangent.shape[1], CHANNELS)
    act, h_outer_small, error_small, outer_small, outer_sums_small = call(
        functools.partial(second_output, small, 1),
        (
            shape(cot.shape, BF16),
            shape((small.rows, OUTER), BF16),
            shape((small.rows, OUTER), BF16),
            shape((3, OUTER), F32),
            shape((2, OUTER), F32),
        ),
        [pltpu.VMEM((16, OUTER), F32)],
        scalars=1,
    )(half_length, q_small, e_small, moment_small, e_sums_small, outer_gain, outer_shift, cot)

    slots = -(-TAPS // parts)
    tap_rows = round_up(slots * TAP_ROWS, 16 * clips)
    first_tap = place_one * slots

    def back(at, coarse, block, span, h_out, outer_moment, outer_sums, slopes, grads, h_red, taps, moment_of, x, point, kept, pooled_pair):
        first = coarse is not None
        gathered = lax.all_gather(outer_sums, "dp")
        d_low, total, packed_taps = call(
            functools.partial(second_back, at, coarse, block, slots),
            (
                shape((at.padded, SECOND), BF16),
                shape((2, OUTER), F32),
                shape((tap_rows, 128), BF16),
            ),
            second_back_scratch(at, slots),
            scalars=2,
            far=(2, 6, 7 + len(grads), 8 + len(grads)),
            far_out=(0,),
        )(span, first_tap, h_out, outer_moment, gathered, outer_gain, slopes, *grads, *taps)
        r_low, sums_low = call(
            functools.partial(conv_back, at, block),
            (shape((at.rows, REDUCED), BF16), shape((2, REDUCED), F32)),
            [
                pltpu.VMEM((9, 512, 256), BF16),
                pltpu.VMEM((3, 512, 256), BF16),
                pltpu.VMEM((1152, 128), BF16),
                pltpu.VMEM((at.padded, 256), BF16),
                pltpu.VMEM((at.group * at.pitch, FIRST), F32),
                pltpu.VMEM((16, REDUCED), F32),
                pltpu.SemaphoreType.DMA((3,)),
            ],
            scalars=1,
            flops=2 * 10**10 if first else 10**9,
            far=(5, 6, 7),
        )(span, d_low, h_red, reduced_gain, reduced_shift, *kernels[block][:2], kernels[block][3])
        gathered = lax.all_gather(sums_low, "dp")
        point_rows = round_up(kept * (FIRST // 128), 16 * clips)
        step = Lines.rows(at)
        wide = x.shape[1]
        moment_of = moment_of if first else moment_of[:, DIRECT:SECOND]
        dx, packed_point, reduced_total, *next_sums = call(
            functools.partial(point_back, at, coarse, block, kept),
            (
                shape((at.rows, wide), BF16),
                shape((point_rows, 128), BF16),
                shape((2, REDUCED), F32),
                *(() if first else (shape((2, OUTER), F32),)),
            ),
            [
                pltpu.VMEM((2, step, DIRECT + POOLED), BF16),
                pltpu.VMEM((2, step, DIRECT + POOLED), BF16),
                pltpu.VMEM((2, step, REDUCED), BF16),
                pltpu.VMEM((2, step, REDUCED), BF16),
                pltpu.VMEM((at.rows, wide), BF16),
                pltpu.VMEM((FIRST, wide), BF16),
                pltpu.VMEM((at.rows, SECOND), BF16),
                pltpu.VMEM((at.rows + 2 * at.line_rows, POOLED), F32),
                pltpu.VMEM((wide, FIRST), F32),
                pltpu.SemaphoreType.DMA((6, 2)),
                pltpu.SemaphoreType.DMA((2,)),
                *([] if first else [pltpu.VMEM((16, OUTER), F32)]),
            ],
            scalars=2,
            far=(2, 6, 7 + len(grads), 8 + len(grads), 12 + len(grads), 13 + len(grads)),
        )(
            span,
            place_one,
            h_out,
            outer_moment,
            total,
            outer_gain,
            slopes,
            *grads,
            h_red,
            r_low,
            moment_of,
            gathered,
            reduced_gain,
            x,
            point,
            *pooled_pair,
        )
        return (dx, packed_taps, packed_point, (total, reduced_total), next_sums)

    dx_small, taps_packed_small, point_packed_small, totals_small, (outer_sums,) = back(
        small, None, 1, half_length, h_outer_small, outer_small, outer_sums_small, error_small, (),
        h_reduced_small, (taps_mid_small, taps_few_small), moment_small, pooled, point_second,
        OUTER // parts, (pooled_slope, pooled_product),
    )
    share_small = shared_sum(
        jnp.concatenate(
            [
                taps_packed_small.reshape(clips, -1, 128),
                point_packed_small.reshape(clips, -1, 128),
            ],
            axis=1,
        ).reshape(-1, 128),
        clips,
    )
    whole_small = lax.all_gather(share_small, ("branch", "dp"), axis=0, tiled=True)
    dx, taps_packed, point_packed, totals, _ = back(
        grid, small, 0, length, h_outer, outer, outer_sums, slope, (dx_small,),
        h_reduced, (taps_mid, taps_few), moment, own, point_first, own_channels, (),
    )
    taps_mine, taps_other = gather_steps(shared_sum(taps_packed, clips), parts, clips)
    point_mine, point_other = gather_steps(shared_sum(point_packed, clips), parts, clips)

    outs = (
        shape((2, TAPS, MID_IN, MID_OUT), F32),
        shape((2, TAPS, SMALL_IN, SMALL_OUT), F32),
        shape((2, SQUEEZED, CHANNELS), F32),
    )
    mid_scratch = pltpu.VMEM((TAPS, MID_IN, MID_OUT), F32)
    small_scratch = pltpu.VMEM((TAPS, SMALL_IN, SMALL_OUT), F32)
    point_scratch = [pltpu.VMEM((SQUEEZED, CHANNELS), F32), pltpu.VMEM((CHANNELS, 128), F32)]
    point_rows = point_packed.shape[0]
    tap_share = tap_rows // clips
    mid_grad, small_grad, point_grad = call(
        functools.partial(unpack_second, parts, clips, slots, tap_share),
        outs,
        [
            pltpu.VMEM((parts, tap_rows, 128), BF16),
            pltpu.VMEM((parts, point_packed_small.shape[0], 128), BF16),
            mid_scratch,
            small_scratch,
            *point_scratch,
            pltpu.SemaphoreType.DMA((3,)),
        ],
        out_space=pl.ANY,
    )(whole_small.reshape(parts * clips, -1, 128))
    clip_one = lax.axis_index("dp").astype(jnp.int32).reshape(1)
    norms = shape((2, 1024), F32)
    mid_grad, small_grad, gain_grad, shift_grad = call(
        functools.partial(unpack_taps, parts, clips, slots, tap_share),
        (*outs[:2], norms, norms),
        [
            pltpu.VMEM((parts, tap_rows, 128), BF16),
            mid_scratch,
            small_scratch,
            pltpu.SemaphoreType.DMA((2,)),
        ],
        scalars=2,
        far_out=(0, 1),
        aliases={8: 0, 9: 1},
    )(place_one, clip_one, taps_mine, taps_other, *totals, *totals_small, mid_grad, small_grad)
    point_grad = call(
        functools.partial(unpack_point, parts, clips, point_rows // clips),
        outs[2],
        [
            pltpu.VMEM((parts, point_rows, 128), BF16),
            *point_scratch,
            pltpu.SemaphoreType.DMA((1,)),
        ],
        scalars=2,
        out_space=pl.ANY,
        aliases={4: 0},
    )(place_one, clip_one, point_mine, point_other, point_grad)
    act = act.reshape(small.side, small.side, cotangent.shape[1], CHANNELS).transpose(2, 0, 1, 3)
    input_grad = dx.reshape(side, side, PITCH, own_channels).transpose(2, 0, 1, 3)
    return (
        act[None],
        input_grad[None],
        point_grad.swapaxes(1, 2),
        mid_grad,
        small_grad,
        gain_grad,
        shift_grad,
    )


def solution(mesh):
    split = P("dp", None, None, None, "branch")
    whole = P("dp", None, None, None, None)
    return jax.shard_map(
        on_device,
        mesh=mesh,
        in_specs=(split, P("dp"), whole, P(), P(), P(), P(), P()),
        out_specs=(whole, split, P(), P(), P(), P(), P()),
        check_vma=False,
    )
```

```python
import functools

import jax
import jax.numpy as jnp
from jax import lax
from jax.experimental import pallas as pl
from jax.experimental.pallas import tpu as pltpu
from jax.sharding import PartitionSpec as P

DIRECT = 256
MID_IN = 160
MID_OUT = 320
SMALL_IN = 32
SMALL_OUT = 128
TAPS = 27
CHANNELS = 832
SQUEEZED = 576
PITCH = 16
REDUCED = 256
POOLED = 128
FIRST = 640
SECOND = 512
OUTER = 896
TAP_ROWS = 432
EPSILON = 1e-05
F32 = jnp.float32
BF16 = jnp.bfloat16
VMEM_BYTES = 58 * 2**20


def call(body, out_shape, scratch=(), scalars=0, cost=5, out_space=pltpu.VMEM, aliases=None, far=(), far_out=()):
    aliases = aliases or {}

    def run(*operands):
        specs = [
            pl.BlockSpec(
                memory_space=pl.ANY
                if number in aliases or number in far
                else pltpu.SMEM
                if number < scalars
                else pltpu.VMEM
            )
            for number in range(len(operands))
        ]
        if isinstance(out_shape, tuple):
            out_specs = tuple(
                pl.BlockSpec(memory_space=pl.ANY if number in far_out else out_space)
                for number in range(len(out_shape))
            )
        else:
            out_specs = pl.BlockSpec(memory_space=out_space)
        return pl.pallas_call(
            body,
            out_shape=out_shape,
            in_specs=specs,
            out_specs=out_specs,
            input_output_aliases=aliases,
            scratch_shapes=list(scratch),
            compiler_params=pltpu.CompilerParams(vmem_limit_bytes=VMEM_BYTES),
            cost_estimate=pl.CostEstimate(
                flops=0, bytes_accessed=int(cost * 3 * 10**6), transcendentals=0
            ),
        )(*operands)

    return run


def shape(dims, dtype):
    return jax.ShapeDtypeStruct(tuple(dims), dtype)


def rows_at(start, size):
    return pl.ds(pl.multiple_of(start, 16), size)


def frames_of(rows, width=128):
    return lax.broadcasted_iota(jnp.int32, (rows, width), 0) & (PITCH - 1)


def frame_mask(rows, length, width=128):
    mask = jnp.where(frames_of(rows) < length, 1.0, 0.0)
    return jnp.concatenate([mask] * (width // 128), axis=1) if width > 128 else mask


def earlier(values):
    return jnp.where(frames_of(*values.shape) > 0, pltpu.roll(values, 1, 0), 0.0)


def later(values):
    rows = values.shape[0]
    return jnp.where(frames_of(*values.shape) < PITCH - 1, pltpu.roll(values, rows - 1, 0), 0.0)


def plane_box(values):
    across = values + earlier(values) + later(values)
    edge = jnp.zeros((PITCH, values.shape[1]), values.dtype)
    return (
        across
        + jnp.concatenate([across[PITCH:], edge], axis=0)
        + jnp.concatenate([edge, across[:-PITCH]], axis=0)
    )


def box_window(side, length):
    frame = frames_of(side * PITCH)
    place = lax.broadcasted_iota(jnp.int32, (side * PITCH, 128), 0) >> 4

    def one(condition):
        return jnp.where(condition, 1.0, 0.0)

    count = one(frame < length) + one(frame + 1 < length) + one((frame > 0) & (frame - 1 < length))
    return count * (3.0 - one(place == 0) - one(place == side - 1))


def box_scale(line, side, window):
    lines = 3.0 - jnp.where(line == 0, 1.0, 0.0) - jnp.where(line == side - 1, 1.0, 0.0)
    return 1.0 / jnp.maximum(window * lines, 1.0)


def sigmoid(value):
    return 0.5 * jnp.tanh(0.5 * value) + 0.5


def silu(value):
    return value * sigmoid(value)


def silu_slope(value):
    gate = sigmoid(value)
    return gate * (1.0 + value * (1.0 - gate))


def partial_sum(values):
    rows, width = values.shape
    return jnp.sum(values.reshape(rows // 8, 8, width), axis=0)


def moments(total, square, count):
    center = total / count
    return (center, lax.rsqrt(square / count - center * center + EPSILON))


def total_of(gathered):
    count = len(gathered) if isinstance(gathered, (list, tuple)) else gathered.shape[0]
    total = gathered[0][...]
    for number in range(1, count):
        total = total + gathered[number][...]
    return total


def pool_matrix(side, transposed):
    line = 2 * side * PITCH
    few, many = (side * PITCH, 2 * line)
    dims = (many, few) if transposed else (few, many)
    coarse = lax.broadcasted_iota(jnp.int32, dims, 1 if transposed else 0)
    fine = lax.broadcasted_iota(jnp.int32, dims, 0 if transposed else 1)
    fine = jnp.where(fine >= line, fine - line, fine)
    same = (fine >> 5 == coarse >> 4) & ((fine & (PITCH - 1)) >> 1 == coarse & (PITCH - 1))
    return jnp.where(same, 0.125, 0.0).astype(BF16)


class Grid:
    def __init__(self, side):
        self.side = side
        self.line_rows = side * PITCH
        self.rows = side * self.line_rows
        self.pitch = (side + 1) * PITCH
        self.lead = self.pitch + PITCH
        self.padded = (side + 2) * self.pitch + 2 * PITCH
        self.group = 2 if side % 2 == 0 else side


class Slots:
    def __init__(self, grid, parts):
        self.pairs = grid.side // 2
        self.parts = parts
        self.each = -(-self.pairs // parts)
        self.empty = parts * self.each - self.pairs
        self.gap = parts * self.each // 2 - 1
        self.pair_rows = 2 * grid.line_rows
        self.rows = self.each * self.pair_rows

    def slot_of(self, pair):
        return pair + jnp.where(pair >= self.gap, self.empty, 0)

    def pair_of(self, slot):
        return slot - jnp.where(slot >= self.gap, self.empty, 0)

    def used(self, slot):
        return (slot < self.gap) | (slot >= self.gap + self.empty)

    def held(self, place):
        count = jnp.zeros((), jnp.int32)
        for number in range(self.each):
            count = count + jnp.where(self.used(place * self.each + number), 1, 0)
        return count


def zero_rows(ref):
    rows = ref.shape[0]
    step = 16
    while rows % (step * 2) == 0 and step < 256:
        step = step * 2

    @pl.loop(0, rows // step)
    def _(number):
        ref[rows_at(number * step, step), :] = jnp.zeros((step, ref.shape[1]), ref.dtype)


def store_taps(mid_ref, small_ref, at, act):
    before, after_ = (earlier(act), later(act))
    mid_ref[at, 0:128] = before[:, :128].astype(BF16)
    mid_ref[at, 128:256] = act[:, :128].astype(BF16)
    mid_ref[at, 256:384] = after_[:, :128].astype(BF16)
    before, act, after_ = (before[:, 128:], act[:, 128:], after_[:, 128:])
    lane = lax.broadcasted_iota(jnp.int32, act.shape, 1)
    mid_ref[at, 384:512] = jnp.where(
        lane < 32, before, jnp.where(lane < 64, pltpu.roll(act, 32, 1), pltpu.roll(after_, 64, 1))
    ).astype(BF16)
    small_ref[at, :] = jnp.where(
        lane < 32, pltpu.roll(before, 96, 1), jnp.where(lane < 64, act, pltpu.roll(after_, 32, 1))
    ).astype(BF16)


def tap_start(grid, base, tap, sign):
    return base + sign * ((tap // 3 - 1) * grid.pitch + (tap % 3 - 1) * PITCH)


def convolve(grid, taps, kernels, rest_ref, acc_ref, stage_ref, e_ref, stage_sem, sums_ref, length):
    mid_ref, small_ref = taps
    main_ref, last_ref, small_kernel_ref = kernels
    group_rows = grid.group * grid.pitch
    stage_rows = grid.group * grid.line_rows
    groups = grid.side // grid.group
    sums_ref[...] = jnp.zeros_like(sums_ref)
    mask = frame_mask(grid.line_rows, length, SECOND)
    edge = jnp.zeros((grid.pitch, 256), F32)
    rest_ref[PITCH : grid.lead, :] = edge
    end = grid.lead + grid.side * grid.pitch
    rest_ref[end : end + grid.pitch, :] = edge

    @pl.loop(0, groups)
    def _(group):
        base = grid.lead + group * group_rows
        total = None
        for place in range(3):
            part = jnp.dot(
                mid_ref[rows_at(base + (place - 1) * PITCH, group_rows), :],
                last_ref[place],
                preferred_element_type=F32,
            )
            total = part if total is None else total + part
        rest_ref[rows_at(base, group_rows), :] = total

    lane = lax.broadcasted_iota(jnp.int32, (grid.line_rows, 128), 1)

    def staged(group, slot):
        return pltpu.make_async_copy(
            stage_ref.at[slot],
            e_ref.at[rows_at(group * stage_rows, stage_rows), :],
            stage_sem.at[slot],
        )

    @pl.loop(0, groups)
    def _(group):
        base = grid.lead + group * group_rows
        slot = lax.rem(group, 2)
        for tap in range(9):
            part = jnp.dot(
                mid_ref[rows_at(tap_start(grid, base, tap, 1), group_rows), :],
                main_ref[tap],
                preferred_element_type=F32,
            )
            acc_ref[:, 0:256] = part if tap == 0 else acc_ref[:, 0:256] + part
        near = [small_ref[rows_at(tap_start(grid, base, tap, 1), group_rows), :] for tap in range(9)]
        acc_ref[:, 256:384] = jnp.dot(
            jnp.concatenate(near, axis=1), small_kernel_ref[...], preferred_element_type=F32
        )

        @pl.when(group >= 2)
        def _():
            staged(group - 2, slot).wait()

        for number in range(grid.group):
            rows = grid.line_rows
            start = base + number * grid.pitch
            last = (
                rest_ref[rows_at(start - grid.pitch, rows), 0:128]
                + pltpu.roll(rest_ref[rows_at(start, rows), 0:128], 64, 1)
                + rest_ref[rows_at(start + grid.pitch, rows), 128:256]
            )
            lines = slice(number * grid.pitch, number * grid.pitch + rows)
            values = jnp.concatenate(
                [acc_ref[lines, 0:256], jnp.where(lane < 64, last, 0.0), acc_ref[lines, 256:384]],
                axis=1,
            )
            stage_ref[slot, number * rows : (number + 1) * rows, :] = values
            masked = values * mask
            sums_ref[0:8] += partial_sum(masked)
            sums_ref[8:16] += partial_sum(masked * values)
        staged(group, slot).start()

    for group in range(max(groups - 2, 0), groups):
        staged(group, group % 2).wait()


def conv_scratch(grid):
    group_rows = grid.group * grid.pitch
    return [
        pltpu.VMEM((9, 512, 256), BF16),
        pltpu.VMEM((3, 512, 256), BF16),
        pltpu.VMEM((1152, 128), BF16),
        pltpu.VMEM((grid.padded, 512), BF16),
        pltpu.VMEM((grid.padded, 128), BF16),
        pltpu.VMEM((grid.rows, REDUCED), BF16),
        pltpu.VMEM((grid.padded, 256), F32),
        pltpu.VMEM((group_rows, 384), F32),
        pltpu.VMEM((2, grid.group * grid.line_rows, SECOND), F32),
        pltpu.VMEM((16, SECOND), F32),
        pltpu.SemaphoreType.DMA((3,)),
        pltpu.SemaphoreType.DMA((3,)),
        pltpu.SemaphoreType.DMA((2,)),
    ]


def conv_outputs(grid):
    return (
        shape((grid.rows, REDUCED), BF16),
        shape((grid.padded, 512), BF16),
        shape((grid.padded, 128), BF16),
        shape((grid.rows, SECOND), F32),
        shape((2, SECOND), F32),
    )


def copies(sources, targets, sem_ref):
    return [
        pltpu.make_async_copy(source, target, sem_ref.at[number])
        for number, (source, target) in enumerate(zip(sources, targets))
    ]


def run_convolution(grid, length, far_kernels, outputs, scratch, fill):
    h_out, mid_out, small_out, e_out, sums_out = outputs
    kernels, (mid_ref, small_ref, h_ref), rest = (scratch[:3], scratch[3:6], scratch[6:])
    rest_ref, acc_ref, stage_ref, sums_ref, in_sem, out_sem, stage_sem = rest
    arriving = copies(far_kernels, kernels, in_sem)
    for copy in arriving:
        copy.start()
    zero_rows(mid_ref)
    zero_rows(small_ref)
    fill(h_ref, mid_ref, small_ref)
    leaving = copies((mid_ref, small_ref, h_ref), (mid_out, small_out, h_out), out_sem)
    for copy in leaving:
        copy.start()
    for copy in arriving:
        copy.wait()
    convolve(
        grid, (mid_ref, small_ref), kernels, rest_ref, acc_ref, stage_ref, e_out, stage_sem, sums_ref, length
    )
    write_sums(sums_out, sums_ref, 0, SECOND)
    for copy in leaving:
        copy.wait()


def write_sums(out_ref, sums_ref, lo, hi):
    for number in range(2):
        out_ref[number : number + 1, lo:hi] = jnp.sum(
            sums_ref[8 * number : 8 * number + 8], axis=0, keepdims=True
        )


def turn(slots, x_ref, out_ref):
    for slot in range(slots.parts * slots.each):
        part, number = divmod(slot, slots.each)
        lanes = slice(number * slots.pair_rows, (number + 1) * slots.pair_rows)
        if slots.gap <= slot < slots.gap + slots.empty:
            out_ref[part, :, lanes] = jnp.zeros((out_ref.shape[1], slots.pair_rows), BF16)
            continue
        pair = slot - (slots.empty if slot >= slots.gap else 0)
        rows = slice(pair * slots.pair_rows, (pair + 1) * slots.pair_rows)
        out_ref[part, :, lanes] = x_ref[rows, :].T


def first_pointwise(slots, length_ref, count_ref, x_ref, p_ref, mid_ref, pool_ref, direct_ref, sums_ref, u_ref):
    rows, step = (slots.rows, 112)
    length, count = (length_ref[0], count_ref[0])
    for part in range(slots.parts):
        product = lax.dot_general(
            x_ref[part], p_ref[part], (((0,), (1,)), ((), ())), preferred_element_type=F32
        )
        u_ref[...] = product if part == 0 else u_ref[...] + product
    mask = frame_mask(step, length, FIRST)

    def summed(number, carry):
        values = u_ref[rows_at(number * step, step), :] * mask
        u_ref[rows_at(number * step, step), :] = values
        few = values[:, :SECOND]
        return (carry[0] + partial_sum(values), carry[1] + partial_sum(few * few))

    zero = (jnp.zeros((8, FIRST), F32), jnp.zeros((8, SECOND), F32))
    total, square = lax.fori_loop(0, rows // step, summed, zero)
    total = jnp.sum(total, axis=0, keepdims=True)
    sums_ref[0:1, :] = total[:, :SECOND]
    sums_ref[1:2, :] = jnp.sum(square, axis=0, keepdims=True)
    sums_ref[2:3, :] = jnp.full((1, SECOND), count, F32)
    offset = (total / jnp.full((1, FIRST), jnp.maximum(count, 1.0), F32)).astype(BF16)
    wide_offset = offset.astype(F32)
    tail = jnp.broadcast_to(wide_offset, (PITCH, FIRST)).astype(BF16)
    pool_ref[rows : rows + PITCH, :] = tail[:, SECOND:]
    shared = mid_ref.shape[0] - 2 * PITCH
    mid_ref[shared : shared + PITCH, :] = tail[:, 256:384]
    mid_ref[shared + PITCH :, :] = tail[:, 384:512]

    @pl.loop(0, rows // step)
    def _(number):
        at = rows_at(number * step, step)
        values = u_ref[at, :]
        direct_ref[at, :] = values[:, :DIRECT]
        values = values[:, DIRECT:] - wide_offset[:, DIRECT:]
        mid_ref[at, :] = values[:, :128].astype(BF16)
        pool_ref[at, :] = values[:, 256:].astype(BF16)

    lane = lax.broadcasted_iota(jnp.int32, (step, 128), 1)
    for couple in range(0, slots.each, 2):

        @pl.loop(0, slots.pair_rows // step)
        def _(number):
            start = couple * slots.pair_rows + number * step
            values = u_ref[rows_at(start, step), 384:512] - wide_offset[:, 384:512]
            if couple + 1 < slots.each:
                other = u_ref[rows_at(start + slots.pair_rows, step), 384:512]
                other = pltpu.roll(other - wide_offset[:, 384:512], 64, 1)
                values = jnp.where(lane < 64, values, other)
            place = rows + couple // 2 * slots.pair_rows + number * step
            mid_ref[rows_at(place, step), :] = values.astype(BF16)


def mid_rows(slots):
    return slots.rows + -(-slots.each // 2) * slots.pair_rows + 2 * PITCH


def each_pair(slots, place, refs, visit):
    for step, ref in enumerate(refs):
        source = lax.rem(place - step + slots.parts, slots.parts)
        for number in range(slots.each):
            slot = source * slots.each + number

            @pl.when(slots.used(slot))
            def _():
                visit(slots.pair_of(slot), ref, number)


def set_moments(total, moment_ref):
    count = total[2:3]
    center, inverse = moments(total[0:1], total[1:2], count)
    moment_ref[0:1, :] = center
    moment_ref[1:2, :] = inverse
    moment_ref[2:3, :] = count
    return (center, inverse)


def first_convolve(grid, slots, block, length_ref, place_ref, *refs):
    parts = slots.parts
    mids, (moment_ref, gain_ref, shift_ref), refs = (refs[:parts], refs[parts : parts + 3], refs[parts + 3 :])
    far_kernels, outputs, scratch = (refs[:3], refs[3:8], refs[8:])
    length = length_ref[0]
    center, inverse = (moment_ref[0:1, DIRECT:], moment_ref[1:2, DIRECT:])
    gain, shift = (gain_ref[block : block + 1], shift_ref[block : block + 1])
    step = 112
    mask = frame_mask(step, length, REDUCED)
    lane = lax.broadcasted_iota(jnp.int32, (step, 128), 1)

    def fill(h_ref, mid_ref, small_ref):
        def visit(pair, ref, number):
            shared = ref.shape[0] - 2 * PITCH
            offset = jnp.concatenate(
                [
                    ref[at : at + PITCH, :].astype(F32)[0:1]
                    for at in (shared, shared + PITCH)
                ],
                axis=1,
            )
            other = slots.rows + number // 2 * slots.pair_rows

            @pl.loop(0, slots.pair_rows // step)
            def _(chunk):
                values = ref[rows_at(number * slots.pair_rows + chunk * step, step), :].astype(F32)
                few = ref[rows_at(other + chunk * step, step), :].astype(F32)
                if number % 2 == 1:
                    few = pltpu.roll(few, 64, 1)
                few = jnp.where(lane < 64, few, 0.0)
                values = jnp.concatenate([values, few], axis=1) + offset
                scaled = (values - center) * inverse
                row = pair * slots.pair_rows + chunk * step
                h_ref[rows_at(row, step), :] = scaled.astype(BF16)
                act = silu(gain * scaled + shift) * mask
                line = row // grid.line_rows
                at = grid.lead + line * grid.pitch + row - line * grid.line_rows
                store_taps(mid_ref, small_ref, rows_at(at, step), act)

        each_pair(slots, place_ref[0], mids, visit)

    run_convolution(grid, length, far_kernels, outputs, scratch, fill)


def pool_planes(grid, plane_ref, q_ref, lo, sums_ref, length, window):
    rows = grid.line_rows
    mask = frame_mask(rows, length)
    sums_ref[...] = jnp.zeros_like(sums_ref)

    @pl.loop(0, grid.side)
    def _(line):
        start = line * rows
        values = (
            plane_ref[rows_at(start, rows), :]
            + plane_ref[rows_at(start + rows, rows), :]
            + plane_ref[rows_at(start + 2 * rows, rows), :]
        ) * box_scale(line, grid.side, window)
        q_ref[rows_at(start, rows), lo : lo + POOLED] = values
        masked = values * mask
        sums_ref[0:8] += partial_sum(masked)
        sums_ref[8:16] += partial_sum(masked * values)


def clear_edges(grid, plane_ref):
    rows = grid.line_rows
    plane_ref[0:rows] = jnp.zeros((rows, POOLED), F32)
    plane_ref[grid.rows + rows : grid.rows + 2 * rows] = jnp.zeros((rows, POOLED), F32)


def first_pool(grid, slots, length_ref, place_ref, *refs):
    pools, refs = (refs[: slots.parts], refs[slots.parts :])
    q_ref, out_sums_ref, plane_ref, sums_ref = refs
    length = length_ref[0]
    rows = grid.line_rows
    clear_edges(grid, plane_ref)

    def visit(pair, ref, number):
        offset = ref[slots.rows : slots.rows + PITCH, :].astype(F32)[0:1]
        for line in range(2):
            at = rows_at(number * slots.pair_rows + line * rows, rows)
            plane_ref[rows_at((2 * pair + line + 1) * rows, rows), :] = plane_box(
                ref[at, :].astype(F32) + offset
            )

    each_pair(slots, place_ref[0], pools, visit)
    pool_planes(grid, plane_ref, q_ref, 0, sums_ref, length, box_window(grid.side, length))
    write_sums(out_sums_ref, sums_ref, 0, POOLED)


def normalize(values, center, inverse, gain, shift, mask):
    scaled = (values - center) * inverse
    shifted = gain * scaled + shift
    gate = sigmoid(shifted)
    gate_mask = gate * mask
    act = shifted * gate_mask
    return (scaled, act, gate_mask + act * (1.0 - gate))


def pool_pieces(matrix, pieces):
    return jnp.dot(
        matrix, jnp.concatenate(pieces, axis=0), preferred_element_type=F32
    ).astype(BF16)


def first_direct(grid, small, slots, block, length_ref, u_ref, gain_ref, shift_ref, *refs):
    sums, (pooled_ref, kept_ref, moment_ref) = (refs[: slots.parts], refs[slots.parts :])
    rows = grid.line_rows
    mask = frame_mask(rows, length_ref[0], DIRECT)
    center, inverse = set_moments(total_of(sums), moment_ref)
    center, inverse = (center[:, :DIRECT], inverse[:, :DIRECT])
    gain, shift = (gain_ref[block : block + 1, :DIRECT], shift_ref[block : block + 1, :DIRECT])
    matrix = pool_matrix(small.side, False)

    @pl.loop(0, slots.each)
    def _(number):
        acts, slopes, products = ([], [], [])
        for line in range(2):
            at = rows_at(number * slots.pair_rows + line * rows, rows)
            scaled, act, slope = normalize(u_ref[at, :], center, inverse, gain, shift, mask)
            kept_ref[at, 0:DIRECT] = scaled.astype(BF16)
            kept_ref[at, DIRECT : 2 * DIRECT] = slope.astype(BF16)
            acts.append(act.astype(BF16))
            slopes.append(slope.astype(BF16))
            products.append((slope * scaled).astype(BF16))
        size = small.line_rows
        pooled_ref[rows_at(number * size, size), :] = pool_pieces(matrix, acts)
        at = rows_at(slots.rows + number * size, size)
        kept_ref[at, 0:DIRECT] = pool_pieces(matrix, slopes)
        kept_ref[at, DIRECT : 2 * DIRECT] = pool_pieces(matrix, products)


def outer_moments(center, inverse, count, outer_ref):
    outer_ref[0:1, :] = center
    outer_ref[1:2, :] = inverse
    outer_ref[2:3, :] = jnp.concatenate([count[:, 0:128]] * (OUTER // 128), axis=1)


def first_output(grid, small, block, length_ref, q_far, e_far, moment_ref, e_sums_ref, pool_sums_ref, gain_ref, shift_ref, *refs):
    pooled_ref, h_far, slope_far, outer_ref, pooled_slope_ref, pooled_product_ref, *refs = refs
    q_ref, e_ref, h_ref, slope_ref, q_sem, e_sem, h_sem, slope_sem = refs
    rows = grid.line_rows
    wide = 2 * rows
    pairs = grid.side // 2

    def arriving(pair, slot):
        at = rows_at(pair * wide, wide)
        return [
            pltpu.make_async_copy(q_far.at[at, :], q_ref.at[slot], q_sem.at[slot]),
            pltpu.make_async_copy(e_far.at[at, :], e_ref.at[slot], e_sem.at[slot]),
        ]

    def leaving(pair, slot):
        at = rows_at(pair * wide, wide)
        return [
            pltpu.make_async_copy(h_ref.at[slot], h_far.at[at, :], h_sem.at[slot]),
            pltpu.make_async_copy(slope_ref.at[slot], slope_far.at[at, :], slope_sem.at[slot]),
        ]

    for copy in arriving(0, 0):
        copy.start()
    mask = frame_mask(rows, length_ref[0], FIRST)
    total = jnp.concatenate([total_of(e_sums_ref), total_of(pool_sums_ref)], axis=1)
    count = jnp.concatenate([moment_ref[2:3, 0:128]] * (FIRST // 128), axis=1)
    center, inverse = moments(total[0:1], total[1:2], count)
    outer_moments(
        jnp.concatenate([moment_ref[0:1, :DIRECT], center], axis=1),
        jnp.concatenate([moment_ref[1:2, :DIRECT], inverse], axis=1),
        count,
        outer_ref,
    )
    matrix = pool_matrix(small.side, False)
    gain, shift = (gain_ref[block : block + 1, DIRECT:], shift_ref[block : block + 1, DIRECT:])

    @pl.loop(0, pairs)
    def _(pair):
        slot = lax.rem(pair, 2)

        @pl.when(pair + 1 < pairs)
        def _():
            for copy in arriving(pair + 1, 1 - slot):
                copy.start()

        for copy in arriving(pair, slot):
            copy.wait()

        @pl.when(pair >= 2)
        def _():
            for copy in leaving(pair - 2, slot):
                copy.wait()

        acts, slopes, products = ([], [], [])
        for number in range(2):
            lines = slice(number * rows, (number + 1) * rows)
            values = jnp.concatenate([e_ref[slot, lines, :], q_ref[slot, lines, :]], axis=1)
            scaled, act, slope = normalize(values, center, inverse, gain, shift, mask)
            h_ref[slot, lines, :] = scaled.astype(BF16)
            low_slope = slope.astype(BF16)
            slope_ref[slot, lines, :] = low_slope
            acts.append(act.astype(BF16))
            slopes.append(low_slope)
            products.append((slope * scaled).astype(BF16))
        for copy in leaving(pair, slot):
            copy.start()
        at = rows_at(pair * small.line_rows, small.line_rows)
        pooled_ref[at, :] = pool_pieces(matrix, acts)
        pooled_slope_ref[at, :] = pool_pieces(matrix, slopes)
        pooled_product_ref[at, :] = pool_pieces(matrix, products)

    for pair in range(max(pairs - 2, 0), pairs):
        for copy in leaving(pair, pair % 2):
            copy.wait()


def second_pointwise(grid, slots, length_ref, place_ref, count_ref, *refs):
    directs, refs = (refs[: slots.parts], refs[slots.parts :])
    rest_ref, p_ref, q_ref, out_sums_ref, x_ref, plane_ref, sums_ref, pool_sums_ref = refs
    length = length_ref[0]
    rows = grid.line_rows
    sums_ref[...] = jnp.zeros_like(sums_ref)
    clear_edges(grid, plane_ref)
    x_ref[:, DIRECT:] = rest_ref[...]

    def visit(pair, ref, number):
        x_ref[rows_at(pair * rows, rows), 0:DIRECT] = ref[number * rows : (number + 1) * rows, :]

    each_pair(slots, place_ref[0], directs, visit)
    q_ref[...] = lax.dot_general(
        x_ref[...], p_ref[...], (((1,), (1,)), ((), ())), preferred_element_type=F32
    )

    @pl.loop(0, grid.side)
    def _(line):
        values = q_ref[rows_at(line * rows, rows), :]
        sums_ref[0:8] += partial_sum(values[:, :SECOND])
        sums_ref[8:16] += partial_sum(values[:, :SECOND] * values[:, :SECOND])
        plane_ref[rows_at((line + 1) * rows, rows), :] = plane_box(values[:, SECOND:])

    pool_planes(grid, plane_ref, q_ref, SECOND, pool_sums_ref, length, box_window(grid.side, length))
    write_sums(out_sums_ref, sums_ref, 0, SECOND)
    write_sums(out_sums_ref, pool_sums_ref, SECOND, FIRST)
    out_sums_ref[2:3, :] = jnp.full((1, FIRST), count_ref[0], F32)


def second_convolve(grid, block, length_ref, q_ref, sums_in_ref, gain_ref, shift_ref, *refs):
    far_kernels, outputs, moment_ref, scratch = (refs[:3], refs[3:8], refs[8], refs[9:])
    length = length_ref[0]
    center, inverse = set_moments(total_of(sums_in_ref), moment_ref)
    center, inverse = (center[:, DIRECT:SECOND], inverse[:, DIRECT:SECOND])
    gain, shift = (gain_ref[block : block + 1], shift_ref[block : block + 1])
    mask = frame_mask(grid.line_rows, length, REDUCED)

    def fill(h_ref, mid_ref, small_ref):
        @pl.loop(0, grid.side)
        def _(line):
            at = rows_at(line * grid.line_rows, grid.line_rows)
            scaled = (q_ref[at, DIRECT:SECOND] - center) * inverse
            h_ref[at, :] = scaled.astype(BF16)
            act = silu(gain * scaled + shift) * mask
            store_taps(
                mid_ref, small_ref, rows_at(grid.lead + line * grid.pitch, grid.line_rows), act
            )

    run_convolution(grid, length, far_kernels, outputs, scratch, fill)


def second_output(grid, block, length_ref, q_ref, e_ref, moment_ref, sums_in_ref, gain_ref, shift_ref, cot_ref, act_ref, h_ref, error_ref, outer_ref, out_sums_ref, sums_ref):
    rows = grid.line_rows
    side, frames = (grid.side, cot_ref.shape[1])
    mask = frame_mask(rows, length_ref[0], OUTER)
    total = total_of(sums_in_ref)
    count = moment_ref[2:3, 0:SECOND]
    center, inverse = moments(total[0:1], total[1:2], count)
    center = jnp.concatenate([moment_ref[0:1, :DIRECT], center, moment_ref[0:1, SECOND:]], axis=1)
    inverse = jnp.concatenate([moment_ref[1:2, :DIRECT], inverse, moment_ref[1:2, SECOND:]], axis=1)
    outer_moments(center, inverse, count, outer_ref)
    sums_ref[...] = jnp.zeros_like(sums_ref)
    gain, shift = (gain_ref[block : block + 1], shift_ref[block : block + 1])
    gap = jnp.zeros((rows, 64), F32)
    unused = jnp.zeros((side, PITCH - frames, CHANNELS), F32)

    @pl.loop(0, side)
    def _(line):
        at = rows_at(line * rows, rows)
        places = pl.ds(line * side, side)
        values = jnp.concatenate([q_ref[at, :DIRECT], e_ref[at, :], q_ref[at, SECOND:]], axis=1)
        scaled = (values - center) * inverse
        h_ref[at, :] = scaled.astype(BF16)
        shifted = gain * scaled + shift
        gate = sigmoid(shifted)
        act = (shifted * gate * mask).reshape(side, PITCH, OUTER)[:, :frames].astype(BF16)
        act_ref[places, :, 0:576] = act[:, :, 0:576]
        act_ref[places, :, 576:CHANNELS] = act[:, :, 640:OUTER]
        slope = gate * (1.0 + shifted * (1.0 - gate))
        grad = jnp.concatenate([cot_ref[places].astype(F32), unused], axis=1)
        grad = grad.reshape(rows, CHANNELS)
        grad = jnp.concatenate([grad[:, :576], gap, grad[:, 576:]], axis=1)
        error = grad * slope * mask
        error_ref[at, :] = error.astype(BF16)
        sums_ref[0:8] += partial_sum(error)
        sums_ref[8:16] += partial_sum(error * scaled)

    write_sums(out_sums_ref, sums_ref, 0, OUTER)


def spread_matrix(grid, small):
    return None if small is None else pool_matrix(small.side, True)[: grid.line_rows]


def outer_error(slopes, small, grad_ref, matrix, line, lo, hi):
    values = slopes.astype(F32)
    if small is None:
        return values
    coarse = grad_ref[rows_at((line // 2) * small.line_rows, small.line_rows), lo:hi]
    return values * jnp.dot(matrix, coarse, preferred_element_type=F32)


class Lines:
    def __init__(self, grid, sources, buffers, sem_ref):
        self.step = 2 if grid.side % 2 == 0 else 1
        self.size = self.step * grid.line_rows
        self.steps = grid.side // self.step
        self.sources, self.buffers, self.sem = (sources, buffers, sem_ref)

    def copies(self, step, slot):
        at = rows_at(step * self.size, self.size)
        copies = []
        for number, ((ref, lo, hi), (buffer, place)) in enumerate(zip(self.sources, self.buffers)):
            source = ref(step, lo, hi) if callable(ref) else ref.at[at, pl.ds(lo, hi - lo)]
            copies.append(
                pltpu.make_async_copy(
                    source, buffer.at[slot, :, pl.ds(place, hi - lo)], self.sem.at[number, slot]
                )
            )
        return copies

    def first(self):
        for copy in self.copies(0, 0):
            copy.start()

    def run(self, visit):
        @pl.loop(0, self.steps)
        def _(step):
            slot = lax.rem(step, 2)

            @pl.when(step + 1 < self.steps)
            def _():
                for copy in self.copies(step + 1, 1 - slot):
                    copy.start()

            for copy in self.copies(step, slot):
                copy.wait()
            visit(step, slot)

    @staticmethod
    def rows(grid):
        return (2 if grid.side % 2 == 0 else 1) * grid.line_rows


def second_back(grid, small, block, slots, length_ref, first_ref, h_far, outer_ref, sums_in_ref, gain_ref, slope_far, *refs):
    grad_ref, refs = (refs[0], refs[1:]) if small is not None else (None, refs)
    mid_far, few_far, d_far, total_ref, out_ref, *refs = refs
    d_ref, h_ref, slope_ref, mid_ref, few_ref, mid_acc_ref, small_acc_ref, turned_ref, sem_ref, in_sem, out_sem = refs
    lo, hi = (DIRECT, DIRECT + SECOND)
    at = 0 if small is not None else DIRECT
    lines = Lines(
        grid,
        ((h_far, at, at + SECOND), (slope_far, at, at + SECOND)),
        ((h_ref, 0), (slope_ref, 0)),
        sem_ref,
    )
    lines.first()
    arriving = copies((mid_far, few_far), (mid_ref, few_ref), in_sem)
    for copy in arriving:
        copy.start()
    total = total_of(sums_in_ref)
    total_ref[...] = total
    count = outer_ref[2:3, lo:hi]
    mean_r = total[0:1, lo:hi] / count
    mean_rh = total[1:2, lo:hi] / count
    factor = gain_ref[block : block + 1, lo:hi] * outer_ref[1:2, lo:hi]
    mask = frame_mask(grid.line_rows, length_ref[0], SECOND)
    matrix = spread_matrix(grid, small)
    zero_rows(d_ref)
    rows = grid.line_rows

    def visit(step, slot):
        for number in range(lines.step):
            line = step * lines.step + number
            here = slice(number * rows, (number + 1) * rows)
            scaled = h_ref[slot, here, :].astype(F32)
            error = outer_error(slope_ref[slot, here, :], small, grad_ref, matrix, line, lo, hi)
            back = factor * (error - mean_r - scaled * mean_rh) * mask
            d_ref[rows_at(grid.lead + line * grid.pitch, rows), :] = back.astype(BF16)

    lines.run(visit)
    leaving = pltpu.make_async_copy(d_ref, d_far, out_sem.at[0])
    leaving.start()
    for copy in arriving:
        copy.wait()
    kernel_grads(grid, slots, first_ref, mid_ref, few_ref, d_ref, out_ref, mid_acc_ref, small_acc_ref, turned_ref)
    leaving.wait()


def second_back_scratch(grid, slots):
    rows = Lines.rows(grid)
    return [
        pltpu.VMEM((grid.padded, SECOND), BF16),
        pltpu.VMEM((2, rows, SECOND), BF16),
        pltpu.VMEM((2, rows, SECOND), BF16),
        pltpu.VMEM((grid.padded, 512), BF16),
        pltpu.VMEM((grid.padded, 128), BF16),
        pltpu.VMEM((slots, 384, 256), F32),
        pltpu.VMEM((slots, 128, 128), F32),
        pltpu.VMEM((MID_IN + 128, 128), F32),
        pltpu.SemaphoreType.DMA((2, 2)),
        pltpu.SemaphoreType.DMA((2,)),
        pltpu.SemaphoreType.DMA((1,)),
    ]


def conv_back(grid, block, length_ref, d_ref, reduced_ref, reduced_gain_ref, reduced_shift_ref, *refs):
    far_kernels, (r_ref, out_sums_ref), refs = (refs[:3], refs[3:5], refs[5:])
    kernels, (last_ref, acc_ref, sums_ref, in_sem) = (refs[:3], refs[3:])
    main_ref, rest_ref, small_ref = kernels
    arriving = copies(far_kernels, kernels, in_sem)
    for copy in arriving:
        copy.start()
    rows = grid.line_rows
    group_rows = grid.group * grid.pitch
    sums_ref[...] = jnp.zeros_like(sums_ref)
    mask = frame_mask(rows, length_ref[0], REDUCED)
    gain, shift = (reduced_gain_ref[block : block + 1], reduced_shift_ref[block : block + 1])
    turned = (((1,), (1,)), ((), ()))
    lane = lax.broadcasted_iota(jnp.int32, (rows, 128), 1)
    wide_lane = lax.broadcasted_iota(jnp.int32, (grid.pitch, 128), 1)

    @pl.loop(0, grid.side)
    def _(line):
        place = grid.lead + line * grid.pitch
        here = d_ref[rows_at(place, grid.pitch), 256:384].astype(F32)
        further = d_ref[rows_at(place + grid.pitch, grid.pitch), 256:384].astype(F32)
        at = rows_at(place, grid.pitch)
        last_ref[at, 0:128] = jnp.where(wide_lane < 64, further, pltpu.roll(here, 64, 1)).astype(
            BF16
        )
        last_ref[at, 128:256] = d_ref[rows_at(place - grid.pitch, grid.pitch), 256:384]

    last_ref[grid.lead - PITCH : grid.lead, :] = jnp.zeros((PITCH, 256), BF16)
    end = grid.lead + grid.side * grid.pitch
    last_ref[end : end + PITCH, :] = jnp.zeros((PITCH, 256), BF16)
    for copy in arriving:
        copy.wait()

    @pl.loop(0, grid.side // grid.group)
    def _(group):
        base = grid.lead + group * group_rows
        for tap in range(9):
            part = lax.dot_general(
                d_ref[rows_at(tap_start(grid, base, tap, -1), group_rows), 0:256],
                main_ref[tap],
                turned,
                preferred_element_type=F32,
            )
            acc_ref[:, 0:512] = part if tap == 0 else acc_ref[:, 0:512] + part
        for place in range(3):
            acc_ref[:, 0:512] += lax.dot_general(
                last_ref[rows_at(base - (place - 1) * PITCH, group_rows), :],
                rest_ref[place],
                turned,
                preferred_element_type=F32,
            )
        near = [
            d_ref[rows_at(tap_start(grid, base, tap, -1), group_rows), 384:512] for tap in range(9)
        ]
        acc_ref[:, 512:640] = jnp.dot(
            jnp.concatenate(near, axis=1), small_ref[...], preferred_element_type=F32
        )
        for number in range(grid.group):
            line = group * grid.group + number
            lines = slice(number * grid.pitch, number * grid.pitch + rows)
            rest, small = (acc_ref[lines, 384:512], acc_ref[lines, 512:640])
            one = jnp.where(lane < 32, rest, pltpu.roll(small, 32, 1))
            two = jnp.where(lane < 32, pltpu.roll(rest, 96, 1), small)
            three = jnp.where(lane < 32, pltpu.roll(rest, 64, 1), pltpu.roll(small, 96, 1))
            wide = later(acc_ref[lines, 0:128]) + acc_ref[lines, 128:256]
            wide = wide + earlier(acc_ref[lines, 256:384])
            narrow = jnp.where(lane < 64, later(one) + two + earlier(three), 0.0)
            back = jnp.concatenate([wide, narrow], axis=1)
            at = rows_at(line * rows, rows)
            scaled = reduced_ref[at, :].astype(F32)
            error = back * silu_slope(gain * scaled + shift) * mask
            r_ref[at, :] = error.astype(BF16)
            sums_ref[0:8] += partial_sum(error)
            sums_ref[8:16] += partial_sum(error * scaled)

    write_sums(out_sums_ref, sums_ref, 0, REDUCED)


def kernel_grads(grid, slots, first_ref, mid_ref, small_ref, d_ref, out_ref, mid_acc_ref, small_acc_ref, turned_ref):
    group_rows = grid.group * grid.pitch
    mid_acc_ref[...] = jnp.zeros_like(mid_acc_ref)
    small_acc_ref[...] = jnp.zeros_like(small_acc_ref)

    def neighbour(slot):
        return jnp.minimum(first_ref[0] + slot, TAPS - 1) // 9

    @pl.loop(0, grid.side // grid.group)
    def _(group):
        base = grid.lead + group * group_rows
        left = d_ref[rows_at(base, group_rows), :].T
        for slot in range(slots):
            tap = lax.rem(jnp.minimum(first_ref[0] + slot, TAPS - 1), 9)
            at = rows_at(
                base + (tap // 3 - 1) * grid.pitch + (lax.rem(tap, 3) - 1) * PITCH, group_rows
            )
            lanes = pl.ds(pl.multiple_of(neighbour(slot) * 128, 128), 128)
            right = jnp.concatenate([mid_ref[at, lanes], mid_ref[at, 384:512]], axis=1)
            mid_acc_ref[slot] += jnp.dot(left[0:384], right, preferred_element_type=F32)
            small_acc_ref[slot] += jnp.dot(
                left[384:512], small_ref[at, :], preferred_element_type=F32
            )

    half = MID_IN // 2
    for slot in range(slots):
        base = slot * TAP_ROWS
        rest = pl.ds(pl.multiple_of(neighbour(slot) * 32, 32), 32)
        for tile in range(3):
            lines = slice(128 * tile, 128 * (tile + 1))
            turned_ref[0:128, :] = mid_acc_ref[slot, lines, 0:128].T
            turned_ref[MID_IN : MID_IN + 128, :] = mid_acc_ref[slot, lines, 128:256].T
            turned_ref[128:MID_IN, :] = turned_ref[
                pl.ds(pl.multiple_of(MID_IN + neighbour(slot) * 32, 32), 32), :
            ]
            if tile < 2:
                out_ref[base + MID_IN * tile : base + MID_IN * (tile + 1), :] = turned_ref[
                    0:MID_IN, :
                ].astype(BF16)
            else:
                folded = turned_ref[0:half, :] + pltpu.roll(turned_ref[half:MID_IN, :], 64, 1)
                out_ref[base + 2 * MID_IN : base + 2 * MID_IN + half, :] = folded.astype(BF16)
        turned_ref[0:128, :] = small_acc_ref[slot].T
        base = base + 2 * MID_IN + half
        out_ref[base : base + SMALL_IN, :] = turned_ref[rest, :].astype(BF16)
    used = slots * TAP_ROWS
    if out_ref.shape[0] > used:
        out_ref[used:, :] = jnp.zeros((out_ref.shape[0] - used, 128), BF16)


def point_back(grid, small, slots, block, kept, length_ref, place_ref, h_far, outer_ref, total_ref, gain_ref, slope_far, *refs):
    first = small is not None
    (grad_ref, direct_far), refs = (refs[:2], refs[2:]) if first else ((None, None), refs)
    reduced_far, r_far, moment_ref, sums_in_ref, reduced_gain_ref, x_far, p_far, *refs = refs
    pooled_refs, refs = ((), refs) if first else (refs[:3], refs[3:])
    dx_ref, dp_ref, reduced_total_ref, *refs = refs
    outer_sums_ref, refs = (None, refs) if first else (refs[0], refs[1:])
    h_ref, slope_ref, reduced_ref, r_ref, x_ref, p_ref, du_ref, plane_ref, acc_ref, sem_ref, in_sem, *refs = refs
    rows = grid.line_rows
    pool = OUTER - POOLED

    def direct_part(step, lo, hi):
        slot = slots.slot_of(step)
        at = rows_at(lax.rem(slot, slots.each) * slots.pair_rows, slots.pair_rows)
        return direct_far.at[slot // slots.each, at, pl.ds(lo, hi - lo)]

    pool_lanes = (SECOND, FIRST) if first else (pool, OUTER)
    lines = Lines(
        grid,
        (
            (direct_part if first else h_far, 0, DIRECT),
            (h_far, *pool_lanes),
            (direct_part, DIRECT, 2 * DIRECT) if first else (slope_far, 0, DIRECT),
            (slope_far, *pool_lanes),
            (reduced_far, 0, REDUCED),
            (r_far, 0, REDUCED),
        ),
        ((h_ref, 0), (h_ref, DIRECT), (slope_ref, 0), (slope_ref, DIRECT), (reduced_ref, 0), (r_ref, 0)),
        sem_ref,
    )
    lines.first()
    arriving = copies((x_far, p_far.at[place_ref[0]] if first else p_far), (x_ref, p_ref), in_sem)
    for copy in arriving:
        copy.start()
    length = length_ref[0]
    matrix = spread_matrix(grid, small)
    total = total_of(sums_in_ref)
    reduced_total_ref[...] = total
    count = outer_ref[2:3, 0:REDUCED]
    mid_r, mid_rh = (total[0:1] / count, total[1:2] / count)
    mid_factor = reduced_gain_ref[block : block + 1] * moment_ref[1:2]
    mask = frame_mask(rows, length, REDUCED)
    window = box_window(grid.side, length)
    clear_edges(grid, plane_ref)

    def constants(lo, hi):
        size = outer_ref[2:3, lo:hi]
        return (
            total_ref[0:1, lo:hi] / size,
            total_ref[1:2, lo:hi] / size,
            gain_ref[block : block + 1, lo:hi] * outer_ref[1:2, lo:hi],
        )

    direct_constants, pool_constants = (constants(0, DIRECT), constants(pool, OUTER))

    def visit(step, slot):
        for number in range(lines.step):
            line = step * lines.step + number
            here = slice(number * rows, (number + 1) * rows)
            at = rows_at(line * rows, rows)

            def section(lo, hi, kept_lo, kept_hi, constant):
                scaled = h_ref[slot, here, kept_lo:kept_hi].astype(F32)
                error = outer_error(
                    slope_ref[slot, here, kept_lo:kept_hi], small, grad_ref, matrix, line, lo, hi
                )
                inner = error - constant[0] - scaled * constant[1]
                return constant[2] * inner * mask[:, : hi - lo]

            du_ref[at, 0:DIRECT] = section(0, DIRECT, 0, DIRECT, direct_constants).astype(BF16)
            scaled = reduced_ref[slot, here, :].astype(F32)
            inner = r_ref[slot, here, :].astype(F32) - mid_r - scaled * mid_rh
            du_ref[at, DIRECT:SECOND] = (mid_factor * inner * mask).astype(BF16)
            pooled = section(pool, OUTER, DIRECT, DIRECT + POOLED, pool_constants)
            plane_ref[rows_at((line + 1) * rows, rows), :] = plane_box(
                pooled * box_scale(line, grid.side, window)
            )

    lines.run(visit)
    for copy in arriving:
        copy.wait()
    if first:
        acc_ref[...] = jnp.zeros_like(acc_ref)
    else:
        sums_ref, pooled_slope_ref, pooled_product_ref = refs
        sums_ref[...] = jnp.zeros_like(sums_ref)
        pooled_slope_ref[:, DIRECT:] = pooled_refs[0][...]
        pooled_product_ref[:, DIRECT:] = pooled_refs[1][...]
        for pair in range(slots.pairs):
            slot = pair + (slots.empty if pair >= slots.gap else 0)
            at = slice(pair * rows, (pair + 1) * rows)
            start = slot % slots.each * rows
            values = pooled_refs[2][slot // slots.each, start : start + rows, :]
            pooled_slope_ref[at, 0:DIRECT] = values[:, :DIRECT]
            pooled_product_ref[at, 0:DIRECT] = values[:, DIRECT:]
    wide = lines.size
    pool_mask = frame_mask(wide, length)

    @pl.loop(0, lines.steps)
    def _(step):
        start = step * wide
        at = rows_at(start, wide)
        pooled = (
            plane_ref[at, :]
            + plane_ref[rows_at(start + rows, wide), :]
            + plane_ref[rows_at(start + 2 * rows, wide), :]
        ) * pool_mask
        du = jnp.concatenate([du_ref[at, 0:SECOND], pooled.astype(BF16)], axis=1)
        dx = jnp.dot(du, p_ref[...], preferred_element_type=F32).astype(BF16)
        dx_ref[at, :] = dx
        if not first:
            for number, ref in enumerate((pooled_slope_ref, pooled_product_ref)):
                sums_ref[8 * number : 8 * number + 8] += partial_sum(
                    dx.astype(F32) * ref[at, :].astype(F32)
                )
        if first:
            acc_ref[...] += lax.dot_general(
                x_ref[at, :], du, (((0,), (0,)), ((), ())), preferred_element_type=F32
            )
        else:
            du_ref[at, SECOND:] = pooled.astype(BF16)

    if not first:
        write_sums(outer_sums_ref, sums_ref, 0, OUTER)
        acc_ref[...] = lax.dot_general(
            x_ref[...], du_ref[...], (((0,), (0,)), ((), ())), preferred_element_type=F32
        )
    start = pl.multiple_of(place_ref[0] * kept, 16) if kept < acc_ref.shape[0] else 0
    own = acc_ref[pl.ds(start, kept), :]
    for tile in range(FIRST // 128):
        dp_ref[kept * tile : kept * (tile + 1), :] = own[:, 128 * tile : 128 * (tile + 1)].astype(
            BF16
        )
    used = (FIRST // 128) * kept
    if dp_ref.shape[0] > used:
        dp_ref[used:, :] = jnp.zeros((dp_ref.shape[0] - used, 128), BF16)


def write_taps(buffer_ref, parts, slots, mid_ref, small_ref):
    half = MID_IN // 2

    @pl.loop(0, TAPS)
    def _(tap):
        base = lax.rem(tap, slots) * TAP_ROWS
        part = tap // slots

        def piece(start, size):
            return buffer_ref[part, rows_at(base + start, size), :].astype(F32)

        folded = piece(2 * MID_IN, half)
        mid_ref[tap, :, 0:128] = piece(0, MID_IN)
        mid_ref[tap, :, 128:256] = piece(MID_IN, MID_IN)
        mid_ref[tap, 0:half, 256:320] = folded[:, 0:64]
        mid_ref[tap, half:MID_IN, 256:320] = pltpu.roll(folded, 64, 1)[:, 0:64]
        small_ref[tap] = piece(2 * MID_IN + half, SMALL_IN)


def write_point(read, parts, kept, point_ref, wide_ref):
    for tile in range(FIRST // 128):
        for part in range(parts):
            start, stop = (kept * part, kept * (part + 1))
            values = read(part, kept * tile, kept)
            if kept * parts == CHANNELS:
                wide_ref[start:stop, :] = values
                continue
            for lo, hi, moved in ((0, 576, 0), (640, OUTER, 64)):
                lo, hi = (max(lo, start), min(hi, stop))
                if lo < hi:
                    wide_ref[lo - moved : hi - moved, :] = values[lo - start : hi - start]
        turned = wide_ref[...].T
        if tile < 3:
            point_ref[128 * tile : 128 * (tile + 1), :] = turned
        elif tile == 3:
            point_ref[384:448, :] = turned[0:64]
        else:
            point_ref[448:576, :] = turned


def copy_out(pairs, sem_ref):
    copies = [
        pltpu.make_async_copy(source, target, sem_ref.at[number])
        for number, (source, target) in enumerate(pairs)
    ]
    for copy in copies:
        copy.start()
    for copy in copies:
        copy.wait()


def unpack_second(parts, slots, shares_ref, mid_out, small_out, mid_ref, small_ref, sem_ref):
    write_taps(shares_ref, parts, slots, mid_ref, small_ref)
    copy_out([(mid_ref, mid_out.at[1]), (small_ref, small_out.at[1])], sem_ref)


def reorder(parts, clips, place, clip, mine_ref, other_ref, targets):
    total = sum(rows for _, rows in targets)
    for chip in range(clips // 2):
        for step in range(parts):
            part = lax.rem(place - step + parts, parts)
            for swapped, ref in enumerate((mine_ref, other_ref)):
                owner = clip ^ (2 * chip) ^ swapped
                source = (chip * parts + step) * total
                for target, rows in targets:
                    target[part, rows_at(owner * rows, rows), :] = ref[source : source + rows, :]
                    source = source + rows


def unpack_first(parts, clips, slots, share, point_share, place_ref, clip_ref, mine_ref, other_ref, *refs):
    totals, refs = (refs[:4], refs[4:])
    mid_in, small_in, mid_out, small_out, point_out, gain_out, shift_out, *refs = refs
    buffer_ref, rows_ref, mid_ref, small_ref, point_ref, wide_ref, sem_ref = refs
    for block in range(2):
        outer_ref, reduced_ref = totals[2 * block : 2 * block + 2]
        for row, out in enumerate((shift_out, gain_out)):
            at, line = (slice(block, block + 1), slice(row, row + 1))
            out[at, 0:256] = outer_ref[line, 0:256]
            out[at, 256:448] = reduced_ref[line, 0:192]
            out[at, 448:576] = outer_ref[line, 768:896]
            out[at, 576:896] = outer_ref[line, 256:576]
            out[at, 896:1024] = outer_ref[line, 640:768]
    targets = ((buffer_ref, share), (rows_ref, point_share))
    reorder(parts, clips, place_ref[0], clip_ref[0], mine_ref, other_ref, targets)

    def read(part, start, size):
        return rows_ref[part, start : start + size, :].astype(F32)

    write_taps(buffer_ref, parts, slots, mid_ref, small_ref)
    leaving = copies((mid_ref, small_ref), (mid_out.at[0], small_out.at[0]), sem_ref)
    for copy in leaving:
        copy.start()
    write_point(read, parts, OUTER // parts, point_ref, wide_ref)
    last = pltpu.make_async_copy(point_ref, point_out.at[1], sem_ref.at[2])
    last.start()
    for copy in (*leaving, last):
        copy.wait()


def unpack_point(parts, clips, share, place_ref, clip_ref, mine_ref, other_ref, point_in, point_out, buffer_ref, point_ref, wide_ref, sem_ref):
    reorder(parts, clips, place_ref[0], clip_ref[0], mine_ref, other_ref, ((buffer_ref, share),))

    def read(part, start, size):
        return buffer_ref[part, start : start + size, :].astype(F32)

    write_point(read, parts, CHANNELS // parts, point_ref, wide_ref)
    copy_out([(point_ref, point_out.at[0])], sem_ref)


def prepare(parts, mid_in, small_in, point_in, gain_in, shift_in, *refs):
    kernels, (point_ref, second_ref, *vectors) = (refs[:8], refs[8:14])
    for block in range(2):
        main_ref, last_ref, few_ref, back_ref = kernels[4 * block : 4 * block + 4]

        @pl.loop(0, 9)
        def _(tap):
            for number in range(3):
                source = 9 * number + tap
                main_ref[tap, 128 * number : 128 * (number + 1), :] = mid_in[block, source, 0:128, 0:256]
                main_ref[tap, 384 + 32 * number : 416 + 32 * number, :] = mid_in[
                    block, source, 128:MID_IN, 0:256
                ]
            main_ref[tap, 480:512, :] = jnp.zeros((32, 256), BF16)
            small = jnp.concatenate(
                [small_in[block, 9 * number + tap] for number in range(3)]
                + [jnp.zeros((32, 128), BF16)],
                axis=0,
            )
            at = pl.ds(pl.multiple_of(tap * 128, 128), 128)
            few_ref[at, :] = small
            back_ref[at, :] = small.astype(F32).T.astype(BF16)

        @pl.loop(0, 3)
        def _(place):
            for number in range(3):
                for rows, start, size in (
                    (slice(0, 128), 128 * number, 128),
                    (slice(128, MID_IN), 384 + 32 * number, 32),
                ):
                    pieces = [
                        mid_in[block, 9 * number + 3 * line + place, rows, 256:MID_OUT].astype(F32)
                        for line in range(3)
                    ]
                    pieces.append(jnp.zeros((size, 64), F32))
                    last_ref[place, start : start + size, :] = jnp.concatenate(
                        pieces, axis=1
                    ).astype(BF16)
            last_ref[place, 480:512, :] = jnp.zeros((32, 256), BF16)

    own = point_ref.shape[2]
    for lo, hi, at in ((0, 448, 0), (448, SQUEEZED, SECOND)):
        values = point_in[0, lo:hi, :].astype(F32)
        for part in range(parts):
            point_ref[part, at : at + hi - lo, :] = values[:, own * part : own * (part + 1)].astype(
                BF16
            )
        values = point_in[1, lo:hi, :].astype(F32)
        gap = jnp.zeros((hi - lo, 64), F32)
        second_ref[at : at + hi - lo, :] = jnp.concatenate(
            [values[:, :576], gap, values[:, 576:]], axis=1
        ).astype(BF16)
    for part in range(parts):
        point_ref[part, 448:SECOND, :] = jnp.zeros((64, own), BF16)
    second_ref[448:SECOND, :] = jnp.zeros((64, OUTER), BF16)
    for source, outer, reduced in ((gain_in, vectors[0], vectors[1]), (shift_in, vectors[2], vectors[3])):
        outer[:, 0:256] = source[:, 0:256]
        outer[:, 256:576] = source[:, 576:896]
        outer[:, 576:640] = jnp.zeros((2, 64), F32)
        outer[:, 640:768] = source[:, 896:1024]
        outer[:, 768:896] = source[:, 448:576]
        reduced[:, 0:192] = source[:, 256:448]
        reduced[:, 192:256] = jnp.zeros((2, 64), F32)


def round_up(value, unit):
    return -(-value // unit) * unit


def spread_over(values, axis, size):
    received = [values]
    for step in range(1, size):
        perm = [(source, (source + step) % size) for source in range(size)]
        received.append(lax.ppermute(values, axis, perm))
    return received


def after(values, earlier):
    return lax.optimization_barrier((values, earlier))[0]


def shared_sum(packed, clips):
    pieces = packed.reshape(clips, packed.shape[0] // clips, 128)
    pieces = lax.all_to_all(pieces, "dp", 0, 0, tiled=True)
    return jnp.sum(pieces.astype(F32), axis=0).astype(BF16)


def join(taps, rows, clips):
    if rows is None:
        return taps
    pieces = [values.reshape(clips, -1, 128) for values in (taps, rows)]
    return jnp.concatenate(pieces, axis=1).reshape(-1, 128)


def gather_chips(column, clips, work=None):
    columns = [column]
    for chip in range(1, clips // 2):
        perm = [(source, source ^ (2 * chip)) for source in range(clips)]
        columns.append(lax.ppermute(column, "dp", perm))
    if work is not None:
        columns = after(columns, work)
    mine = jnp.concatenate(columns, axis=0)
    other = lax.ppermute(mine, "dp", [(source, source ^ 1) for source in range(clips)])
    return (mine, other)


def on_device(frames, lengths, cotangent, pointwise, conv_mid, conv_small, gains, shifts):
    parts = lax.axis_size("branch")
    clips = lax.axis_size("dp")
    place = lax.axis_index("branch").astype(jnp.int32)
    side = frames.shape[2]
    grid, small = (Grid(side), Grid(side // 2))
    slots = Slots(grid, parts)
    cells = side * side
    own_channels = frames.shape[-1]
    length = lengths.astype(jnp.int32)
    half_length = length // 2
    place_one = place.reshape(1)

    own = frames[0].transpose(1, 2, 0, 3).reshape(grid.rows, own_channels)
    turned = call(functools.partial(turn, slots), shape((parts, own_channels, slots.rows), BF16))(own)
    by_pairs = lax.all_to_all(turned, "branch", 0, 0, tiled=True)
    kernel_shapes = (
        shape((9, 512, 256), BF16),
        shape((3, 512, 256), BF16),
        shape((1152, 128), BF16),
        shape((1152, 128), BF16),
    )
    prepared = call(
        functools.partial(prepare, parts),
        (
            *kernel_shapes,
            *kernel_shapes,
            shape((parts, FIRST, own_channels), BF16),
            shape((FIRST, OUTER), BF16),
            shape((2, OUTER), F32),
            shape((2, REDUCED), F32),
            shape((2, OUTER), F32),
            shape((2, REDUCED), F32),
        ),
    )(conv_mid, conv_small, pointwise.swapaxes(1, 2), gains, shifts)
    kernels = (prepared[0:4], prepared[4:8])
    point_first, point_second, outer_gain, reduced_gain, outer_shift, reduced_shift = prepared[8:]

    local_count = (length * (slots.held(place) * 2 * side)).astype(F32)
    mid, pool, direct, sums = call(
        functools.partial(first_pointwise, slots),
        (
            shape((mid_rows(slots), 128), BF16),
            shape((slots.rows + PITCH, POOLED), BF16),
            shape((slots.rows, DIRECT), F32),
            shape((3, SECOND), F32),
        ),
        [pltpu.VMEM((slots.rows, FIRST), F32)],
        scalars=2,
    )(length, local_count, by_pairs, point_first)
    mids = spread_over(mid, "branch", parts)
    sums = spread_over(jnp.sum(lax.all_gather(sums, "dp"), axis=0), "branch", parts)
    pooled_direct, kept_direct, moment = call(
        functools.partial(first_direct, grid, small, slots, 0),
        (
            shape((slots.each * small.line_rows, DIRECT), BF16),
            shape((slots.rows + slots.each * small.line_rows, 2 * DIRECT), BF16),
            shape((3, SECOND), F32),
        ),
        scalars=1,
        cost=3,
    )(length, direct, outer_gain, outer_shift, *sums)
    pool, pooled_direct = after((pool, pooled_direct), mids)
    pools = spread_over(pool, "branch", parts)
    h_reduced, taps_mid, taps_few, e, e_sums = call(
        functools.partial(first_convolve, grid, slots, 0),
        conv_outputs(grid),
        conv_scratch(grid),
        scalars=2,
        cost=40,
        far=range(5 + parts, 8 + parts),
        far_out=range(4),
    )(length, place_one, *mids, moment, reduced_gain, reduced_shift, *kernels[0][:3])
    pooled_directs = spread_over(after(pooled_direct, (pools, e_sums)), "branch", parts)
    kept_direct = lax.all_gather(after(kept_direct, pooled_directs), "branch", axis=0)
    q_pool, pool_sums = call(
        functools.partial(first_pool, grid, slots),
        (shape((grid.rows, POOLED), F32), shape((2, POOLED), F32)),
        [
            pltpu.VMEM((grid.rows + 2 * grid.line_rows, POOLED), F32),
            pltpu.VMEM((16, POOLED), F32),
        ],
        scalars=2,
    )(length, place_one, *pools)
    second_sums = lax.all_gather(jnp.concatenate([e_sums, pool_sums], axis=1), "dp")
    pair = 2 * grid.line_rows
    pooled, h_outer, slope, outer, pooled_slope, pooled_product = call(
        functools.partial(first_output, grid, small, 0),
        (
            shape((small.rows, FIRST), BF16),
            shape((grid.rows, FIRST), BF16),
            shape((grid.rows, FIRST), BF16),
            shape((3, OUTER), F32),
            shape((small.rows, FIRST), BF16),
            shape((small.rows, FIRST), BF16),
        ),
        [
            pltpu.VMEM((2, pair, POOLED), F32),
            pltpu.VMEM((2, pair, SECOND), F32),
            pltpu.VMEM((2, pair, FIRST), BF16),
            pltpu.VMEM((2, pair, FIRST), BF16),
            *[pltpu.SemaphoreType.DMA((2,))] * 4,
        ],
        scalars=1,
        far=(1, 2),
        far_out=(1, 2),
    )(
        length,
        q_pool,
        e,
        moment,
        second_sums[:, :, :SECOND],
        second_sums[:, :, SECOND:],
        outer_gain,
        outer_shift,
    )

    small_count = half_length.astype(F32) * float(small.side * small.side)
    q_small, sums_small, pooled = call(
        functools.partial(second_pointwise, small, slots),
        (
            shape((small.rows, FIRST), F32),
            shape((3, FIRST), F32),
            shape((small.rows, OUTER), BF16),
        ),
        [
            pltpu.VMEM((small.rows + 2 * small.line_rows, POOLED), F32),
            pltpu.VMEM((16, SECOND), F32),
            pltpu.VMEM((16, POOLED), F32),
        ],
        scalars=3,
    )(half_length, place_one, small_count, *pooled_directs, pooled, point_second)
    sums_small = lax.all_gather(sums_small, "dp")
    h_reduced_small, taps_mid_small, taps_few_small, e_small, e_sums_small, moment_small = call(
        functools.partial(second_convolve, small, 1),
        (*conv_outputs(small), shape((3, FIRST), F32)),
        conv_scratch(small),
        scalars=1,
        far=range(5, 8),
        far_out=range(4),
    )(half_length, q_small, sums_small, reduced_gain, reduced_shift, *kernels[1][:3])
    e_sums_small = lax.all_gather(e_sums_small, "dp")
    cot = cotangent[0].transpose(1, 2, 0, 3).reshape(small.side**2, cotangent.shape[1], CHANNELS)
    act, h_outer_small, error_small, outer_small, outer_sums_small = call(
        functools.partial(second_output, small, 1),
        (
            shape(cot.shape, BF16),
            shape((small.rows, OUTER), BF16),
            shape((small.rows, OUTER), BF16),
            shape((3, OUTER), F32),
            shape((2, OUTER), F32),
        ),
        [pltpu.VMEM((16, OUTER), F32)],
        scalars=1,
    )(half_length, q_small, e_small, moment_small, e_sums_small, outer_gain, outer_shift, cot)

    taps_each = -(-TAPS // parts)
    tap_rows = round_up(taps_each * TAP_ROWS, 16 * clips)
    first_tap = place_one * taps_each

    def back(at, coarse, block, span, h_out, outer_moment, outer_sums, slopes, grads, kept_direct, h_red, taps, moment_of, x, point, kept, pooled_pair, earlier_rows):
        first = coarse is not None
        gathered = lax.all_gather(outer_sums, "dp")
        d_low, total, packed_taps = call(
            functools.partial(second_back, at, coarse, block, taps_each),
            (
                shape((at.padded, SECOND), BF16),
                shape((2, OUTER), F32),
                shape((tap_rows, 128), BF16),
            ),
            second_back_scratch(at, taps_each),
            scalars=2,
            far=(2, 6, 7 + len(grads), 8 + len(grads)),
            far_out=(0,),
        )(span, first_tap, h_out, outer_moment, gathered, outer_gain, slopes, *grads, *taps)
        r_low, sums_low = call(
            functools.partial(conv_back, at, block),
            (shape((at.rows, REDUCED), BF16), shape((2, REDUCED), F32)),
            [
                pltpu.VMEM((9, 512, 256), BF16),
                pltpu.VMEM((3, 512, 256), BF16),
                pltpu.VMEM((1152, 128), BF16),
                pltpu.VMEM((at.padded, 256), BF16),
                pltpu.VMEM((at.group * at.pitch, FIRST), F32),
                pltpu.VMEM((16, REDUCED), F32),
                pltpu.SemaphoreType.DMA((3,)),
            ],
            scalars=1,
            cost=21 if first else 8,
            far=(5, 6, 7),
        )(span, d_low, h_red, reduced_gain, reduced_shift, *kernels[block][:2], kernels[block][3])
        share = shared_sum(join(packed_taps, earlier_rows, clips), clips)
        sums_low, share = lax.optimization_barrier((sums_low, share))
        gathered = lax.all_gather(sums_low, "dp")
        if first:
            share = jnp.concatenate(spread_over(share, "branch", parts), axis=0)
            gathered, share = lax.optimization_barrier((gathered, share))
        point_rows = round_up(kept * (FIRST // 128), 16 * clips)
        step = Lines.rows(at)
        wide = x.shape[1]
        moment_of = moment_of[:, DIRECT:SECOND]
        dx, packed_point, reduced_total, *next_sums = call(
            functools.partial(point_back, at, coarse, slots, block, kept),
            (
                shape((at.rows, wide), BF16),
                shape((point_rows, 128), BF16),
                shape((2, REDUCED), F32),
                *(() if first else (shape((2, OUTER), F32),)),
            ),
            [
                pltpu.VMEM((2, step, DIRECT + POOLED), BF16),
                pltpu.VMEM((2, step, DIRECT + POOLED), BF16),
                pltpu.VMEM((2, step, REDUCED), BF16),
                pltpu.VMEM((2, step, REDUCED), BF16),
                pltpu.VMEM((at.rows, wide), BF16),
                pltpu.VMEM((FIRST, wide), BF16),
                pltpu.VMEM((at.rows, SECOND if first else FIRST), BF16),
                pltpu.VMEM((at.rows + 2 * at.line_rows, POOLED), F32),
                pltpu.VMEM((wide, FIRST), F32),
                pltpu.SemaphoreType.DMA((6, 2)),
                pltpu.SemaphoreType.DMA((2,)),
                *(
                    []
                    if first
                    else [
                        pltpu.VMEM((16, OUTER), F32),
                        pltpu.VMEM((at.rows, OUTER), BF16),
                        pltpu.VMEM((at.rows, OUTER), BF16),
                    ]
                ),
            ],
            scalars=2,
            far=(2, 6, 8, 9, 10, 14, 15) if first else (2, 6, 7, 8, 12, 13),
        )(
            span,
            place_one,
            h_out,
            outer_moment,
            total,
            outer_gain,
            slopes,
            *grads,
            *kept_direct,
            h_red,
            r_low,
            moment_of,
            gathered,
            reduced_gain,
            x,
            point,
            *pooled_pair,
        )
        return (dx, share, packed_point, (total, reduced_total), next_sums)

    dx_small, share_small, point_packed_small, totals_small, (outer_sums,) = back(
        small, None, 1, half_length, h_outer_small, outer_small, outer_sums_small, error_small, (), (),
        h_reduced_small, (taps_mid_small, taps_few_small), moment_small, pooled, point_second,
        OUTER // parts, (pooled_slope, pooled_product, kept_direct[:, slots.rows :]), None,
    )
    whole_small = lax.all_gather(share_small, ("branch", "dp"), axis=0, tiled=True)
    dx, taps_column, point_packed, totals, _ = back(
        grid, small, 0, length, h_outer, outer, outer_sums, slope, (dx_small,), (kept_direct,),
        h_reduced, (taps_mid, taps_few), moment, own, point_first, own_channels, (), point_packed_small,
    )
    column_mine, column_other = gather_chips(taps_column, clips, point_packed)

    outs = (
        shape((2, TAPS, MID_IN, MID_OUT), F32),
        shape((2, TAPS, SMALL_IN, SMALL_OUT), F32),
        shape((2, SQUEEZED, CHANNELS), F32),
    )
    tap_scratch = [
        pltpu.VMEM((TAPS, MID_IN, MID_OUT), F32),
        pltpu.VMEM((TAPS, SMALL_IN, SMALL_OUT), F32),
    ]
    point_scratch = [pltpu.VMEM((SQUEEZED, CHANNELS), F32), pltpu.VMEM((CHANNELS, 128), F32)]
    point_rows, point_rows_small = (point_packed.shape[0], point_packed_small.shape[0])
    mid_grad, small_grad = call(
        functools.partial(unpack_second, parts, taps_each),
        outs[:2],
        [*tap_scratch, pltpu.SemaphoreType.DMA((2,))],
        out_space=pl.ANY,
        cost=8,
    )(whole_small.reshape(parts, tap_rows, 128))
    clip_one = lax.axis_index("dp").astype(jnp.int32).reshape(1)
    norms = shape((2, 1024), F32)
    pieces = point_packed.reshape(clips, point_rows // clips, 128)
    pieces = lax.all_to_all(pieces, "dp", 0, 0, tiled=True)
    pieces, mid_grad, small_grad = lax.optimization_barrier((pieces, mid_grad, small_grad))
    point_share = jnp.sum(pieces.astype(F32), axis=0).astype(BF16)
    received = spread_over(point_share, "branch", parts)
    mid_grad, small_grad, point_grad, gain_grad, shift_grad = call(
        functools.partial(unpack_first, parts, clips, taps_each, tap_rows // clips, point_rows_small // clips),
        (*outs, norms, norms),
        [
            pltpu.VMEM((parts, tap_rows, 128), BF16),
            pltpu.VMEM((parts, point_rows_small, 128), BF16),
            *tap_scratch,
            *point_scratch,
            pltpu.SemaphoreType.DMA((3,)),
        ],
        scalars=2,
        far_out=(0, 1, 2),
        aliases={8: 0, 9: 1},
        cost=8,
    )(place_one, clip_one, column_mine, column_other, *totals, *totals_small, mid_grad, small_grad)
    received, point_grad = lax.optimization_barrier((received, point_grad))
    point_mine, point_other = gather_chips(jnp.concatenate(received, axis=0), clips)
    point_grad = call(
        functools.partial(unpack_point, parts, clips, point_rows // clips),
        outs[2],
        [
            pltpu.VMEM((parts, point_rows, 128), BF16),
            *point_scratch,
            pltpu.SemaphoreType.DMA((1,)),
        ],
        scalars=2,
        out_space=pl.ANY,
        aliases={4: 0},
        cost=3,
    )(place_one, clip_one, point_mine, point_other, point_grad)
    act = act.reshape(small.side, small.side, cotangent.shape[1], CHANNELS).transpose(2, 0, 1, 3)
    input_grad = dx.reshape(side, side, PITCH, own_channels).transpose(2, 0, 1, 3)
    return (
        act[None],
        input_grad[None],
        point_grad.swapaxes(1, 2),
        mid_grad,
        small_grad,
        gain_grad,
        shift_grad,
    )


def solution(mesh):
    split = P("dp", None, None, None, "branch")
    whole = P("dp", None, None, None, None)
    return jax.shard_map(
        on_device,
        mesh=mesh,
        in_specs=(split, P("dp"), whole, P(), P(), P(), P(), P()),
        out_specs=(whole, split, P(), P(), P(), P(), P()),
        check_vma=False,
    )
```

```python
import functools

import jax
import jax.numpy as jnp
from jax import lax
from jax.experimental import pallas as pl
from jax.experimental.pallas import tpu as pltpu
from jax.sharding import PartitionSpec as P

DIRECT = 256
MID_IN = 160
MID_OUT = 320
SMALL_IN = 32
SMALL_OUT = 128
TAPS = 27
CHANNELS = 832
SQUEEZED = 576
PITCH = 16
REDUCED = 256
POOLED = 128
FIRST = 640
SECOND = 512
OUTER = 896
TAP_ROWS = 432
EPSILON = 1e-05
F32 = jnp.float32
BF16 = jnp.bfloat16
VMEM_BYTES = 58 * 2**20


def call(body, out_shape, scratch=(), scalars=0, cost=5, out_space=pltpu.VMEM, aliases=None, far=(), far_out=()):
    aliases = aliases or {}

    def run(*operands):
        specs = [
            pl.BlockSpec(
                memory_space=pl.ANY
                if number in aliases or number in far
                else pltpu.SMEM
                if number < scalars
                else pltpu.VMEM
            )
            for number in range(len(operands))
        ]
        if isinstance(out_shape, tuple):
            out_specs = tuple(
                pl.BlockSpec(memory_space=pl.ANY if number in far_out else out_space)
                for number in range(len(out_shape))
            )
        else:
            out_specs = pl.BlockSpec(memory_space=out_space)
        return pl.pallas_call(
            body,
            out_shape=out_shape,
            in_specs=specs,
            out_specs=out_specs,
            input_output_aliases=aliases,
            scratch_shapes=list(scratch),
            compiler_params=pltpu.CompilerParams(vmem_limit_bytes=VMEM_BYTES),
            cost_estimate=pl.CostEstimate(
                flops=0, bytes_accessed=int(cost * 3 * 10**6), transcendentals=0
            ),
        )(*operands)

    return run


def shape(dims, dtype):
    return jax.ShapeDtypeStruct(tuple(dims), dtype)


def rows_at(start, size):
    return pl.ds(pl.multiple_of(start, 16), size)


def frames_of(rows, width=128):
    return lax.broadcasted_iota(jnp.int32, (rows, width), 0) & (PITCH - 1)


def frame_mask(rows, length, width=128):
    mask = jnp.where(frames_of(rows) < length, 1.0, 0.0)
    return jnp.concatenate([mask] * (width // 128), axis=1) if width > 128 else mask


def earlier(values):
    return jnp.where(frames_of(*values.shape) > 0, pltpu.roll(values, 1, 0), 0.0)


def later(values):
    rows = values.shape[0]
    return jnp.where(frames_of(*values.shape) < PITCH - 1, pltpu.roll(values, rows - 1, 0), 0.0)


def plane_box(values):
    across = values + earlier(values) + later(values)
    edge = jnp.zeros((PITCH, values.shape[1]), values.dtype)
    return (
        across
        + jnp.concatenate([across[PITCH:], edge], axis=0)
        + jnp.concatenate([edge, across[:-PITCH]], axis=0)
    )


def box_window(side, length):
    frame = frames_of(side * PITCH)
    place = lax.broadcasted_iota(jnp.int32, (side * PITCH, 128), 0) >> 4

    def one(condition):
        return jnp.where(condition, 1.0, 0.0)

    count = one(frame < length) + one(frame + 1 < length) + one((frame > 0) & (frame - 1 < length))
    return count * (3.0 - one(place == 0) - one(place == side - 1))


def box_scale(line, side, window):
    lines = 3.0 - jnp.where(line == 0, 1.0, 0.0) - jnp.where(line == side - 1, 1.0, 0.0)
    return 1.0 / jnp.maximum(window * lines, 1.0)


def sigmoid(value):
    return 0.5 * jnp.tanh(0.5 * value) + 0.5


def silu(value):
    return value * sigmoid(value)


def silu_slope(value):
    gate = sigmoid(value)
    return gate * (1.0 + value * (1.0 - gate))


def partial_sum(values):
    rows, width = values.shape
    return jnp.sum(values.reshape(rows // 8, 8, width), axis=0)


def moments(total, square, count):
    center = total / count
    return (center, lax.rsqrt(square / count - center * center + EPSILON))


def total_of(gathered):
    count = len(gathered) if isinstance(gathered, (list, tuple)) else gathered.shape[0]
    total = gathered[0][...]
    for number in range(1, count):
        total = total + gathered[number][...]
    return total


def pool_matrix(side, transposed):
    line = 2 * side * PITCH
    few, many = (side * PITCH, 2 * line)
    dims = (many, few) if transposed else (few, many)
    coarse = lax.broadcasted_iota(jnp.int32, dims, 1 if transposed else 0)
    fine = lax.broadcasted_iota(jnp.int32, dims, 0 if transposed else 1)
    fine = jnp.where(fine >= line, fine - line, fine)
    same = (fine >> 5 == coarse >> 4) & ((fine & (PITCH - 1)) >> 1 == coarse & (PITCH - 1))
    return jnp.where(same, 0.125, 0.0).astype(BF16)


class Grid:
    def __init__(self, side):
        self.side = side
        self.line_rows = side * PITCH
        self.rows = side * self.line_rows
        self.pitch = (side + 1) * PITCH
        self.lead = self.pitch + PITCH
        self.padded = (side + 2) * self.pitch + 2 * PITCH
        self.group = 2 if side % 2 == 0 else side


class Slots:
    def __init__(self, grid, parts):
        self.pairs = grid.side // 2
        self.parts = parts
        self.each = -(-self.pairs // parts)
        self.empty = parts * self.each - self.pairs
        self.gap = parts * self.each // 2 - 1
        self.pair_rows = 2 * grid.line_rows
        self.rows = self.each * self.pair_rows

    def slot_of(self, pair):
        return pair + jnp.where(pair >= self.gap, self.empty, 0)

    def pair_of(self, slot):
        return slot - jnp.where(slot >= self.gap, self.empty, 0)

    def used(self, slot):
        return (slot < self.gap) | (slot >= self.gap + self.empty)

    def held(self, place):
        count = jnp.zeros((), jnp.int32)
        for number in range(self.each):
            count = count + jnp.where(self.used(place * self.each + number), 1, 0)
        return count


def clear_empty(grid, ref):
    width = ref.shape[1]
    ref[0 : grid.lead, :] = jnp.zeros((grid.lead, width), ref.dtype)
    end = grid.lead + grid.side * grid.pitch
    ref[end:, :] = jnp.zeros((ref.shape[0] - end, width), ref.dtype)

    @pl.loop(0, grid.side)
    def _(line):
        at = rows_at(grid.lead + line * grid.pitch + grid.line_rows, PITCH)
        ref[at, :] = jnp.zeros((PITCH, width), ref.dtype)


def store_taps(mid_ref, small_ref, at, act):
    before, after_ = (earlier(act), later(act))
    mid_ref[at, 0:128] = before[:, :128].astype(BF16)
    mid_ref[at, 128:256] = act[:, :128].astype(BF16)
    mid_ref[at, 256:384] = after_[:, :128].astype(BF16)
    before, act, after_ = (before[:, 128:], act[:, 128:], after_[:, 128:])
    lane = lax.broadcasted_iota(jnp.int32, act.shape, 1)
    mid_ref[at, 384:512] = jnp.where(
        lane < 32, before, jnp.where(lane < 64, pltpu.roll(act, 32, 1), pltpu.roll(after_, 64, 1))
    ).astype(BF16)
    small_ref[at, :] = jnp.where(
        lane < 32, pltpu.roll(before, 96, 1), jnp.where(lane < 64, act, pltpu.roll(after_, 32, 1))
    ).astype(BF16)


def tap_start(grid, base, tap, sign):
    return base + sign * ((tap // 3 - 1) * grid.pitch + (tap % 3 - 1) * PITCH)


def convolve(grid, taps, kernels, rest_ref, acc_ref, stage_ref, e_ref, stage_sem, sums_ref, length):
    mid_ref, small_ref = taps
    main_ref, last_ref, small_kernel_ref = kernels
    group_rows = grid.group * grid.pitch
    stage_rows = grid.group * grid.line_rows
    groups = grid.side // grid.group
    sums_ref[...] = jnp.zeros_like(sums_ref)
    mask = frame_mask(grid.line_rows, length, SECOND)
    edge = jnp.zeros((grid.pitch, 256), F32)
    rest_ref[PITCH : grid.lead, :] = edge
    end = grid.lead + grid.side * grid.pitch
    rest_ref[end : end + grid.pitch, :] = edge

    @pl.loop(0, groups)
    def _(group):
        base = grid.lead + group * group_rows
        total = None
        for place in range(3):
            part = jnp.dot(
                mid_ref[rows_at(base + (place - 1) * PITCH, group_rows), :],
                last_ref[place],
                preferred_element_type=F32,
            )
            total = part if total is None else total + part
        rest_ref[rows_at(base, group_rows), :] = total

    lane = lax.broadcasted_iota(jnp.int32, (grid.line_rows, 128), 1)

    def staged(group, slot):
        return pltpu.make_async_copy(
            stage_ref.at[slot],
            e_ref.at[rows_at(group * stage_rows, stage_rows), :],
            stage_sem.at[slot],
        )

    @pl.loop(0, groups)
    def _(group):
        base = grid.lead + group * group_rows
        slot = lax.rem(group, 2)
        for tap in range(9):
            part = jnp.dot(
                mid_ref[rows_at(tap_start(grid, base, tap, 1), group_rows), :],
                main_ref[tap],
                preferred_element_type=F32,
            )
            acc_ref[:, 0:256] = part if tap == 0 else acc_ref[:, 0:256] + part
        near = [small_ref[rows_at(tap_start(grid, base, tap, 1), group_rows), :] for tap in range(9)]
        acc_ref[:, 256:384] = jnp.dot(
            jnp.concatenate(near, axis=1), small_kernel_ref[...], preferred_element_type=F32
        )

        @pl.when(group >= 2)
        def _():
            staged(group - 2, slot).wait()

        for number in range(grid.group):
            rows = grid.line_rows
            start = base + number * grid.pitch
            last = (
                rest_ref[rows_at(start - grid.pitch, rows), 0:128]
                + pltpu.roll(rest_ref[rows_at(start, rows), 0:128], 64, 1)
                + rest_ref[rows_at(start + grid.pitch, rows), 128:256]
            )
            lines = slice(number * grid.pitch, number * grid.pitch + rows)
            values = jnp.concatenate(
                [acc_ref[lines, 0:256], jnp.where(lane < 64, last, 0.0), acc_ref[lines, 256:384]],
                axis=1,
            )
            stage_ref[slot, number * rows : (number + 1) * rows, :] = values
            masked = values * mask
            sums_ref[0:8] += partial_sum(masked)
            sums_ref[8:16] += partial_sum(masked * values)
        staged(group, slot).start()

    for group in range(max(groups - 2, 0), groups):
        staged(group, group % 2).wait()


def conv_scratch(grid):
    group_rows = grid.group * grid.pitch
    return [
        pltpu.VMEM((9, 512, 256), BF16),
        pltpu.VMEM((3, 512, 256), BF16),
        pltpu.VMEM((1152, 128), BF16),
        pltpu.VMEM((grid.padded, 512), BF16),
        pltpu.VMEM((grid.padded, 128), BF16),
        pltpu.VMEM((grid.rows, REDUCED), BF16),
        pltpu.VMEM((grid.padded, 256), F32),
        pltpu.VMEM((group_rows, 384), F32),
        pltpu.VMEM((2, grid.group * grid.line_rows, SECOND), F32),
        pltpu.VMEM((16, SECOND), F32),
        pltpu.SemaphoreType.DMA((3,)),
        pltpu.SemaphoreType.DMA((3,)),
        pltpu.SemaphoreType.DMA((2,)),
    ]


def conv_outputs(grid):
    return (
        shape((grid.rows, REDUCED), BF16),
        shape((grid.padded, 512), BF16),
        shape((grid.padded, 128), BF16),
        shape((grid.rows, SECOND), F32),
        shape((2, SECOND), F32),
    )


def copies(sources, targets, sem_ref):
    return [
        pltpu.make_async_copy(source, target, sem_ref.at[number])
        for number, (source, target) in enumerate(zip(sources, targets))
    ]


def run_convolution(grid, length, far_kernels, outputs, scratch, fill):
    h_out, mid_out, small_out, e_out, sums_out = outputs
    kernels, (mid_ref, small_ref, h_ref), rest = (scratch[:3], scratch[3:6], scratch[6:])
    rest_ref, acc_ref, stage_ref, sums_ref, in_sem, out_sem, stage_sem = rest
    arriving = copies(far_kernels, kernels, in_sem)
    for copy in arriving:
        copy.start()
    clear_empty(grid, mid_ref)
    clear_empty(grid, small_ref)
    fill(h_ref, mid_ref, small_ref)
    leaving = copies((mid_ref, small_ref, h_ref), (mid_out, small_out, h_out), out_sem)
    for copy in leaving:
        copy.start()
    for copy in arriving:
        copy.wait()
    convolve(
        grid, (mid_ref, small_ref), kernels, rest_ref, acc_ref, stage_ref, e_out, stage_sem, sums_ref, length
    )
    write_sums(sums_out, sums_ref, 0, SECOND)
    for copy in leaving:
        copy.wait()


def write_sums(out_ref, sums_ref, lo, hi):
    for number in range(2):
        out_ref[number : number + 1, lo:hi] = jnp.sum(
            sums_ref[8 * number : 8 * number + 8], axis=0, keepdims=True
        )


def turn(slots, x_ref, out_ref):
    for slot in range(slots.parts * slots.each):
        part, number = divmod(slot, slots.each)
        lanes = slice(number * slots.pair_rows, (number + 1) * slots.pair_rows)
        if slots.gap <= slot < slots.gap + slots.empty:
            out_ref[part, :, lanes] = jnp.zeros((out_ref.shape[1], slots.pair_rows), BF16)
            continue
        pair = slot - (slots.empty if slot >= slots.gap else 0)
        rows = slice(pair * slots.pair_rows, (pair + 1) * slots.pair_rows)
        out_ref[part, :, lanes] = x_ref[rows, :].T


def first_pointwise(slots, length_ref, count_ref, x_ref, p_ref, mid_ref, pool_ref, direct_ref, sums_ref, u_ref):
    rows, step = (slots.rows, 112)
    length, count = (length_ref[0], count_ref[0])
    for part in range(slots.parts):
        product = lax.dot_general(
            x_ref[part], p_ref[part], (((0,), (1,)), ((), ())), preferred_element_type=F32
        )
        u_ref[...] = product if part == 0 else u_ref[...] + product
    mask = frame_mask(step, length, FIRST)

    def summed(number, carry):
        values = u_ref[rows_at(number * step, step), :] * mask
        u_ref[rows_at(number * step, step), :] = values
        few = values[:, :SECOND]
        return (carry[0] + partial_sum(values), carry[1] + partial_sum(few * few))

    zero = (jnp.zeros((8, FIRST), F32), jnp.zeros((8, SECOND), F32))
    total, square = lax.fori_loop(0, rows // step, summed, zero)
    total = jnp.sum(total, axis=0, keepdims=True)
    sums_ref[0:1, :] = total[:, :SECOND]
    sums_ref[1:2, :] = jnp.sum(square, axis=0, keepdims=True)
    sums_ref[2:3, :] = jnp.full((1, SECOND), count, F32)
    offset = (total / jnp.full((1, FIRST), jnp.maximum(count, 1.0), F32)).astype(BF16)
    wide_offset = offset.astype(F32)
    tail = jnp.broadcast_to(wide_offset, (PITCH, FIRST)).astype(BF16)
    pool_ref[rows : rows + PITCH, :] = tail[:, SECOND:]
    shared = mid_ref.shape[0] - 2 * PITCH
    mid_ref[shared : shared + PITCH, :] = tail[:, 256:384]
    mid_ref[shared + PITCH :, :] = tail[:, 384:512]

    @pl.loop(0, rows // step)
    def _(number):
        at = rows_at(number * step, step)
        values = u_ref[at, :]
        direct_ref[at, :] = values[:, :DIRECT]
        values = values[:, DIRECT:] - wide_offset[:, DIRECT:]
        mid_ref[at, :] = values[:, :128].astype(BF16)
        pool_ref[at, :] = values[:, 256:].astype(BF16)

    lane = lax.broadcasted_iota(jnp.int32, (step, 128), 1)
    for couple in range(0, slots.each, 2):

        @pl.loop(0, slots.pair_rows // step)
        def _(number):
            start = couple * slots.pair_rows + number * step
            values = u_ref[rows_at(start, step), 384:512] - wide_offset[:, 384:512]
            if couple + 1 < slots.each:
                other = u_ref[rows_at(start + slots.pair_rows, step), 384:512]
                other = pltpu.roll(other - wide_offset[:, 384:512], 64, 1)
                values = jnp.where(lane < 64, values, other)
            place = rows + couple // 2 * slots.pair_rows + number * step
            mid_ref[rows_at(place, step), :] = values.astype(BF16)


def mid_rows(slots):
    return slots.rows + -(-slots.each // 2) * slots.pair_rows + 2 * PITCH


def each_pair(slots, place, refs, visit):
    for step, ref in enumerate(refs):
        source = lax.rem(place - step + slots.parts, slots.parts)
        for number in range(slots.each):
            slot = source * slots.each + number

            @pl.when(slots.used(slot))
            def _():
                visit(slots.pair_of(slot), ref, number)


def set_moments(total, moment_ref):
    count = total[2:3]
    center, inverse = moments(total[0:1], total[1:2], count)
    moment_ref[0:1, :] = center
    moment_ref[1:2, :] = inverse
    moment_ref[2:3, :] = count
    return (center, inverse)


def first_convolve(grid, slots, block, length_ref, place_ref, *refs):
    parts = slots.parts
    mids, (moment_ref, gain_ref, shift_ref), refs = (refs[:parts], refs[parts : parts + 3], refs[parts + 3 :])
    far_kernels, outputs, scratch = (refs[:3], refs[3:8], refs[8:])
    length = length_ref[0]
    center, inverse = (moment_ref[0:1, DIRECT:], moment_ref[1:2, DIRECT:])
    gain, shift = (gain_ref[block : block + 1], shift_ref[block : block + 1])
    step = 112
    mask = frame_mask(step, length, REDUCED)
    lane = lax.broadcasted_iota(jnp.int32, (step, 128), 1)

    def fill(h_ref, mid_ref, small_ref):
        def visit(pair, ref, number):
            shared = ref.shape[0] - 2 * PITCH
            offset = jnp.concatenate(
                [
                    ref[at : at + PITCH, :].astype(F32)[0:1]
                    for at in (shared, shared + PITCH)
                ],
                axis=1,
            )
            other = slots.rows + number // 2 * slots.pair_rows

            @pl.loop(0, slots.pair_rows // step)
            def _(chunk):
                values = ref[rows_at(number * slots.pair_rows + chunk * step, step), :].astype(F32)
                few = ref[rows_at(other + chunk * step, step), :].astype(F32)
                if number % 2 == 1:
                    few = pltpu.roll(few, 64, 1)
                few = jnp.where(lane < 64, few, 0.0)
                values = jnp.concatenate([values, few], axis=1) + offset
                scaled = (values - center) * inverse
                row = pair * slots.pair_rows + chunk * step
                h_ref[rows_at(row, step), :] = scaled.astype(BF16)
                act = silu(gain * scaled + shift) * mask
                line = row // grid.line_rows
                at = grid.lead + line * grid.pitch + row - line * grid.line_rows
                store_taps(mid_ref, small_ref, rows_at(at, step), act)

        each_pair(slots, place_ref[0], mids, visit)

    run_convolution(grid, length, far_kernels, outputs, scratch, fill)


def pool_planes(grid, plane_ref, q_ref, lo, sums_ref, length, window):
    rows = grid.line_rows
    mask = frame_mask(rows, length)
    sums_ref[...] = jnp.zeros_like(sums_ref)

    @pl.loop(0, grid.side)
    def _(line):
        start = line * rows
        values = (
            plane_ref[rows_at(start, rows), :]
            + plane_ref[rows_at(start + rows, rows), :]
            + plane_ref[rows_at(start + 2 * rows, rows), :]
        ) * box_scale(line, grid.side, window)
        q_ref[rows_at(start, rows), lo : lo + POOLED] = values
        masked = values * mask
        sums_ref[0:8] += partial_sum(masked)
        sums_ref[8:16] += partial_sum(masked * values)


def clear_edges(grid, plane_ref):
    rows = grid.line_rows
    plane_ref[0:rows] = jnp.zeros((rows, POOLED), F32)
    plane_ref[grid.rows + rows : grid.rows + 2 * rows] = jnp.zeros((rows, POOLED), F32)


def first_pool(grid, slots, length_ref, place_ref, *refs):
    pools, refs = (refs[: slots.parts], refs[slots.parts :])
    q_ref, out_sums_ref, plane_ref, sums_ref = refs
    length = length_ref[0]
    rows = grid.line_rows
    clear_edges(grid, plane_ref)

    def visit(pair, ref, number):
        offset = ref[slots.rows : slots.rows + PITCH, :].astype(F32)[0:1]
        for line in range(2):
            at = rows_at(number * slots.pair_rows + line * rows, rows)
            plane_ref[rows_at((2 * pair + line + 1) * rows, rows), :] = plane_box(
                ref[at, :].astype(F32) + offset
            )

    each_pair(slots, place_ref[0], pools, visit)
    pool_planes(grid, plane_ref, q_ref, 0, sums_ref, length, box_window(grid.side, length))
    write_sums(out_sums_ref, sums_ref, 0, POOLED)


def normalize(values, center, inverse, gain, shift, mask):
    scaled = (values - center) * inverse
    shifted = gain * scaled + shift
    gate = sigmoid(shifted)
    gate_mask = gate * mask
    act = shifted * gate_mask
    return (scaled, act, gate_mask + act * (1.0 - gate))


def pool_pieces(matrix, pieces):
    return jnp.dot(
        matrix, jnp.concatenate(pieces, axis=0), preferred_element_type=F32
    ).astype(BF16)


def first_direct(grid, small, slots, block, length_ref, u_ref, gain_ref, shift_ref, *refs):
    sums, (pooled_ref, kept_ref, moment_ref) = (refs[: slots.parts], refs[slots.parts :])
    rows = grid.line_rows
    mask = frame_mask(rows, length_ref[0], DIRECT)
    center, inverse = set_moments(total_of(sums), moment_ref)
    center, inverse = (center[:, :DIRECT], inverse[:, :DIRECT])
    gain, shift = (gain_ref[block : block + 1, :DIRECT], shift_ref[block : block + 1, :DIRECT])
    matrix = pool_matrix(small.side, False)

    @pl.loop(0, slots.each)
    def _(number):
        acts, slopes, products = ([], [], [])
        for line in range(2):
            at = rows_at(number * slots.pair_rows + line * rows, rows)
            scaled, act, slope = normalize(u_ref[at, :], center, inverse, gain, shift, mask)
            kept_ref[at, 0:DIRECT] = scaled.astype(BF16)
            kept_ref[at, DIRECT : 2 * DIRECT] = slope.astype(BF16)
            acts.append(act.astype(BF16))
            slopes.append(slope.astype(BF16))
            products.append((slope * scaled).astype(BF16))
        size = small.line_rows
        pooled_ref[rows_at(number * size, size), :] = pool_pieces(matrix, acts)
        at = rows_at(slots.rows + number * size, size)
        kept_ref[at, 0:DIRECT] = pool_pieces(matrix, slopes)
        kept_ref[at, DIRECT : 2 * DIRECT] = pool_pieces(matrix, products)


def outer_moments(center, inverse, count, outer_ref):
    outer_ref[0:1, :] = center
    outer_ref[1:2, :] = inverse
    outer_ref[2:3, :] = jnp.concatenate([count[:, 0:128]] * (OUTER // 128), axis=1)


def first_output(grid, small, block, length_ref, q_far, e_far, moment_ref, e_sums_ref, pool_sums_ref, gain_ref, shift_ref, *refs):
    pooled_ref, h_far, slope_far, outer_ref, pooled_slope_ref, pooled_product_ref, *refs = refs
    q_ref, e_ref, h_ref, slope_ref, q_sem, e_sem, h_sem, slope_sem = refs
    rows = grid.line_rows
    wide = 2 * rows
    pairs = grid.side // 2

    def arriving(pair, slot):
        at = rows_at(pair * wide, wide)
        return [
            pltpu.make_async_copy(q_far.at[at, :], q_ref.at[slot], q_sem.at[slot]),
            pltpu.make_async_copy(e_far.at[at, :], e_ref.at[slot], e_sem.at[slot]),
        ]

    def leaving(pair, slot):
        at = rows_at(pair * wide, wide)
        return [
            pltpu.make_async_copy(h_ref.at[slot], h_far.at[at, :], h_sem.at[slot]),
            pltpu.make_async_copy(slope_ref.at[slot], slope_far.at[at, :], slope_sem.at[slot]),
        ]

    for copy in arriving(0, 0):
        copy.start()
    mask = frame_mask(rows, length_ref[0], FIRST)
    total = jnp.concatenate([total_of(e_sums_ref), total_of(pool_sums_ref)], axis=1)
    count = jnp.concatenate([moment_ref[2:3, 0:128]] * (FIRST // 128), axis=1)
    center, inverse = moments(total[0:1], total[1:2], count)
    outer_moments(
        jnp.concatenate([moment_ref[0:1, :DIRECT], center], axis=1),
        jnp.concatenate([moment_ref[1:2, :DIRECT], inverse], axis=1),
        count,
        outer_ref,
    )
    matrix = pool_matrix(small.side, False)
    gain, shift = (gain_ref[block : block + 1, DIRECT:], shift_ref[block : block + 1, DIRECT:])

    @pl.loop(0, pairs)
    def _(pair):
        slot = lax.rem(pair, 2)

        @pl.when(pair + 1 < pairs)
        def _():
            for copy in arriving(pair + 1, 1 - slot):
                copy.start()

        for copy in arriving(pair, slot):
            copy.wait()

        @pl.when(pair >= 2)
        def _():
            for copy in leaving(pair - 2, slot):
                copy.wait()

        acts, slopes, products = ([], [], [])
        for number in range(2):
            lines = slice(number * rows, (number + 1) * rows)
            values = jnp.concatenate([e_ref[slot, lines, :], q_ref[slot, lines, :]], axis=1)
            scaled, act, slope = normalize(values, center, inverse, gain, shift, mask)
            h_ref[slot, lines, :] = scaled.astype(BF16)
            low_slope = slope.astype(BF16)
            slope_ref[slot, lines, :] = low_slope
            acts.append(act.astype(BF16))
            slopes.append(low_slope)
            products.append((slope * scaled).astype(BF16))
        for copy in leaving(pair, slot):
            copy.start()
        at = rows_at(pair * small.line_rows, small.line_rows)
        pooled_ref[at, :] = pool_pieces(matrix, acts)
        pooled_slope_ref[at, :] = pool_pieces(matrix, slopes)
        pooled_product_ref[at, :] = pool_pieces(matrix, products)

    for pair in range(max(pairs - 2, 0), pairs):
        for copy in leaving(pair, pair % 2):
            copy.wait()


def second_pointwise(grid, slots, length_ref, place_ref, count_ref, *refs):
    directs, refs = (refs[: slots.parts], refs[slots.parts :])
    rest_ref, p_ref, q_ref, out_sums_ref, x_ref, plane_ref, sums_ref, pool_sums_ref = refs
    length = length_ref[0]
    rows = grid.line_rows
    sums_ref[...] = jnp.zeros_like(sums_ref)
    clear_edges(grid, plane_ref)
    x_ref[:, DIRECT:] = rest_ref[...]

    def visit(pair, ref, number):
        x_ref[rows_at(pair * rows, rows), 0:DIRECT] = ref[number * rows : (number + 1) * rows, :]

    each_pair(slots, place_ref[0], directs, visit)
    q_ref[...] = lax.dot_general(
        x_ref[...], p_ref[...], (((1,), (1,)), ((), ())), preferred_element_type=F32
    )

    @pl.loop(0, grid.side)
    def _(line):
        values = q_ref[rows_at(line * rows, rows), :]
        sums_ref[0:8] += partial_sum(values[:, :SECOND])
        sums_ref[8:16] += partial_sum(values[:, :SECOND] * values[:, :SECOND])
        plane_ref[rows_at((line + 1) * rows, rows), :] = plane_box(values[:, SECOND:])

    pool_planes(grid, plane_ref, q_ref, SECOND, pool_sums_ref, length, box_window(grid.side, length))
    write_sums(out_sums_ref, sums_ref, 0, SECOND)
    write_sums(out_sums_ref, pool_sums_ref, SECOND, FIRST)
    out_sums_ref[2:3, :] = jnp.full((1, FIRST), count_ref[0], F32)


def second_convolve(grid, block, length_ref, q_ref, sums_in_ref, gain_ref, shift_ref, *refs):
    far_kernels, outputs, moment_ref, scratch = (refs[:3], refs[3:8], refs[8], refs[9:])
    length = length_ref[0]
    center, inverse = set_moments(total_of(sums_in_ref), moment_ref)
    center, inverse = (center[:, DIRECT:SECOND], inverse[:, DIRECT:SECOND])
    gain, shift = (gain_ref[block : block + 1], shift_ref[block : block + 1])
    mask = frame_mask(grid.line_rows, length, REDUCED)

    def fill(h_ref, mid_ref, small_ref):
        @pl.loop(0, grid.side)
        def _(line):
            at = rows_at(line * grid.line_rows, grid.line_rows)
            scaled = (q_ref[at, DIRECT:SECOND] - center) * inverse
            h_ref[at, :] = scaled.astype(BF16)
            act = silu(gain * scaled + shift) * mask
            store_taps(
                mid_ref, small_ref, rows_at(grid.lead + line * grid.pitch, grid.line_rows), act
            )

    run_convolution(grid, length, far_kernels, outputs, scratch, fill)


def second_output(grid, block, length_ref, q_ref, e_ref, moment_ref, sums_in_ref, gain_ref, shift_ref, cot_ref, act_ref, h_ref, error_ref, outer_ref, out_sums_ref, sums_ref):
    rows = grid.line_rows
    side, frames = (grid.side, cot_ref.shape[1])
    mask = frame_mask(rows, length_ref[0], OUTER)
    total = total_of(sums_in_ref)
    count = moment_ref[2:3, 0:SECOND]
    center, inverse = moments(total[0:1], total[1:2], count)
    center = jnp.concatenate([moment_ref[0:1, :DIRECT], center, moment_ref[0:1, SECOND:]], axis=1)
    inverse = jnp.concatenate([moment_ref[1:2, :DIRECT], inverse, moment_ref[1:2, SECOND:]], axis=1)
    outer_moments(center, inverse, count, outer_ref)
    sums_ref[...] = jnp.zeros_like(sums_ref)
    gain, shift = (gain_ref[block : block + 1], shift_ref[block : block + 1])
    gap = jnp.zeros((rows, 64), F32)
    unused = jnp.zeros((side, PITCH - frames, CHANNELS), F32)

    @pl.loop(0, side)
    def _(line):
        at = rows_at(line * rows, rows)
        places = pl.ds(line * side, side)
        values = jnp.concatenate([q_ref[at, :DIRECT], e_ref[at, :], q_ref[at, SECOND:]], axis=1)
        scaled = (values - center) * inverse
        h_ref[at, :] = scaled.astype(BF16)
        shifted = gain * scaled + shift
        gate = sigmoid(shifted)
        act = (shifted * gate * mask).reshape(side, PITCH, OUTER)[:, :frames].astype(BF16)
        act_ref[places, :, 0:576] = act[:, :, 0:576]
        act_ref[places, :, 576:CHANNELS] = act[:, :, 640:OUTER]
        slope = gate * (1.0 + shifted * (1.0 - gate))
        grad = jnp.concatenate([cot_ref[places].astype(F32), unused], axis=1)
        grad = grad.reshape(rows, CHANNELS)
        grad = jnp.concatenate([grad[:, :576], gap, grad[:, 576:]], axis=1)
        error = grad * slope * mask
        error_ref[at, :] = error.astype(BF16)
        sums_ref[0:8] += partial_sum(error)
        sums_ref[8:16] += partial_sum(error * scaled)

    write_sums(out_sums_ref, sums_ref, 0, OUTER)


def spread_matrix(grid, small):
    return None if small is None else pool_matrix(small.side, True)[: grid.line_rows]


def outer_error(slopes, small, grad_ref, matrix, line, lo, hi):
    values = slopes.astype(F32)
    if small is None:
        return values
    coarse = grad_ref[rows_at((line // 2) * small.line_rows, small.line_rows), lo:hi]
    return values * jnp.dot(matrix, coarse, preferred_element_type=F32)


class Lines:
    def __init__(self, grid, sources, buffers, sem_ref):
        self.step = 2 if grid.side % 2 == 0 else 1
        self.size = self.step * grid.line_rows
        self.steps = grid.side // self.step
        self.sources, self.buffers, self.sem = (sources, buffers, sem_ref)

    def copies(self, step):
        at = rows_at(step * self.size, self.size)
        copies = []
        for number, ((ref, lo, hi), (buffer, place)) in enumerate(zip(self.sources, self.buffers)):
            source = ref(step, lo, hi) if callable(ref) else ref.at[at, pl.ds(lo, hi - lo)]
            target = buffer.at[at, pl.ds(place, hi - lo)]
            copies.append(pltpu.make_async_copy(source, target, self.sem.at[number, step]))
        return copies

    def first(self):
        @pl.loop(0, self.steps)
        def _(step):
            for copy in self.copies(step):
                copy.start()

    def run(self, visit):
        @pl.loop(0, self.steps)
        def _(step):
            for copy in self.copies(step):
                copy.wait()
            visit(step)

    @staticmethod
    def semaphores(grid, count):
        return pltpu.SemaphoreType.DMA((count, grid.side // 2 if grid.side % 2 == 0 else grid.side))


def second_back(grid, small, block, slots, length_ref, first_ref, h_far, outer_ref, sums_in_ref, gain_ref, slope_far, *refs):
    first = small is not None
    (grad_ref, carried_ref), refs = (refs[:2], refs[2:]) if first else ((None, None), refs)
    mid_far, few_far, d_far, total_ref, out_ref, *refs = refs
    d_ref, h_ref, slope_ref, mid_ref, few_ref, mid_acc_ref, small_acc_ref, turned_ref, sem_ref, in_sem, out_sem = refs
    lo, hi = (DIRECT, DIRECT + SECOND)
    at = 0 if first else DIRECT
    lines = Lines(
        grid,
        ((h_far, at, at + SECOND), (slope_far, at, at + SECOND)),
        ((h_ref, 0), (slope_ref, 0)),
        sem_ref,
    )
    lines.first()
    arriving = copies((mid_far, few_far), (mid_ref, few_ref), in_sem)
    for copy in arriving:
        copy.start()
    total = total_of(sums_in_ref)
    total_ref[...] = total
    a, b, c = before_norm(
        gain_ref[block : block + 1, lo:hi], outer_ref[1:2, lo:hi], total[:, lo:hi], outer_ref[2:3, lo:hi]
    )
    mask = frame_mask(grid.line_rows, length_ref[0], SECOND)
    matrix = spread_matrix(grid, small)
    clear_empty(grid, d_ref)
    rows = grid.line_rows
    if first:
        share = out_ref.shape[1] - carried_ref.shape[1]
        for clip in range(out_ref.shape[0]):
            out_ref[clip, share:, :] = carried_ref[clip]

    def visit(step):
        for number in range(lines.step):
            line = step * lines.step + number
            here = rows_at(line * rows, rows)
            scaled = h_ref[here, :].astype(F32)
            error = outer_error(slope_ref[here, :], small, grad_ref, matrix, line, lo, hi)
            back = (a * error - b - c * scaled) * mask
            d_ref[rows_at(grid.lead + line * grid.pitch, rows), :] = back.astype(BF16)

    lines.run(visit)
    leaving = pltpu.make_async_copy(d_ref, d_far, out_sem.at[0])
    leaving.start()
    for copy in arriving:
        copy.wait()
    kernel_grads(grid, slots, first_ref, mid_ref, few_ref, d_ref, out_ref, mid_acc_ref, small_acc_ref, turned_ref)
    leaving.wait()


def before_norm(gain, inverse, sums, count):
    factor = gain * inverse
    return (factor, factor * sums[0:1] / count, factor * sums[1:2] / count)


def second_back_scratch(grid, slots):
    return [
        pltpu.VMEM((grid.padded, SECOND), BF16),
        pltpu.VMEM((grid.rows, SECOND), BF16),
        pltpu.VMEM((grid.rows, SECOND), BF16),
        pltpu.VMEM((grid.padded, 512), BF16),
        pltpu.VMEM((grid.padded, 128), BF16),
        pltpu.VMEM((slots, 384, 256), F32),
        pltpu.VMEM((slots, 128, 128), F32),
        pltpu.VMEM((MID_IN + 128, 128), F32),
        Lines.semaphores(grid, 2),
        pltpu.SemaphoreType.DMA((2,)),
        pltpu.SemaphoreType.DMA((1,)),
    ]


def conv_back(grid, block, length_ref, d_ref, reduced_ref, reduced_gain_ref, reduced_shift_ref, *refs):
    far_kernels, refs = (refs[:3], refs[3:])
    first = len(refs) > 9
    (x_far, rest_product_ref), refs = (refs[:2], refs[2:]) if first else ((None, None), refs)
    r_ref, out_sums_ref, *refs = refs
    product_out, refs = (refs[0], refs[1:]) if first else (None, refs)
    kernels, (last_ref, acc_ref, sums_ref, in_sem, *refs) = (refs[:3], refs[3:])
    if first:
        x_ref, product_ref, x_sem = refs
        x_copy = pltpu.make_async_copy(x_far, x_ref, x_sem.at[0])
        x_copy.start()
    main_ref, rest_ref, small_ref = kernels
    arriving = copies(far_kernels, kernels, in_sem)
    for copy in arriving:
        copy.start()
    rows = grid.line_rows
    group_rows = grid.group * grid.pitch
    sums_ref[...] = jnp.zeros_like(sums_ref)
    mask = frame_mask(rows, length_ref[0], REDUCED)
    gain, shift = (reduced_gain_ref[block : block + 1], reduced_shift_ref[block : block + 1])
    turned = (((1,), (1,)), ((), ()))
    lane = lax.broadcasted_iota(jnp.int32, (rows, 128), 1)
    wide_lane = lax.broadcasted_iota(jnp.int32, (grid.pitch, 128), 1)

    @pl.loop(0, grid.side)
    def _(line):
        place = grid.lead + line * grid.pitch
        here = d_ref[rows_at(place, grid.pitch), 256:384].astype(F32)
        further = d_ref[rows_at(place + grid.pitch, grid.pitch), 256:384].astype(F32)
        at = rows_at(place, grid.pitch)
        last_ref[at, 0:128] = jnp.where(wide_lane < 64, further, pltpu.roll(here, 64, 1)).astype(
            BF16
        )
        last_ref[at, 128:256] = d_ref[rows_at(place - grid.pitch, grid.pitch), 256:384]

    last_ref[grid.lead - PITCH : grid.lead, :] = jnp.zeros((PITCH, 256), BF16)
    end = grid.lead + grid.side * grid.pitch
    last_ref[end : end + PITCH, :] = jnp.zeros((PITCH, 256), BF16)
    for copy in arriving:
        copy.wait()

    @pl.loop(0, grid.side // grid.group)
    def _(group):
        base = grid.lead + group * group_rows
        for tap in range(9):
            part = lax.dot_general(
                d_ref[rows_at(tap_start(grid, base, tap, -1), group_rows), 0:256],
                main_ref[tap],
                turned,
                preferred_element_type=F32,
            )
            acc_ref[:, 0:512] = part if tap == 0 else acc_ref[:, 0:512] + part
        for place in range(3):
            acc_ref[:, 0:512] += lax.dot_general(
                last_ref[rows_at(base - (place - 1) * PITCH, group_rows), :],
                rest_ref[place],
                turned,
                preferred_element_type=F32,
            )
        near = [
            d_ref[rows_at(tap_start(grid, base, tap, -1), group_rows), 384:512] for tap in range(9)
        ]
        acc_ref[:, 512:640] = jnp.dot(
            jnp.concatenate(near, axis=1), small_ref[...], preferred_element_type=F32
        )
        for number in range(grid.group):
            line = group * grid.group + number
            lines = slice(number * grid.pitch, number * grid.pitch + rows)
            rest, small = (acc_ref[lines, 384:512], acc_ref[lines, 512:640])
            one = jnp.where(lane < 32, rest, pltpu.roll(small, 32, 1))
            two = jnp.where(lane < 32, pltpu.roll(rest, 96, 1), small)
            three = jnp.where(lane < 32, pltpu.roll(rest, 64, 1), pltpu.roll(small, 96, 1))
            wide = later(acc_ref[lines, 0:128]) + acc_ref[lines, 128:256]
            wide = wide + earlier(acc_ref[lines, 256:384])
            narrow = jnp.where(lane < 64, later(one) + two + earlier(three), 0.0)
            back = jnp.concatenate([wide, narrow], axis=1)
            at = rows_at(line * rows, rows)
            scaled = reduced_ref[at, :].astype(F32)
            error = back * silu_slope(gain * scaled + shift) * mask
            r_ref[at, :] = error.astype(BF16)
            sums_ref[0:8] += partial_sum(error)
            sums_ref[8:16] += partial_sum(error * scaled)

    write_sums(out_sums_ref, sums_ref, 0, REDUCED)
    if first:
        x_copy.wait()
        wide = 2 * rows
        product_ref[...] = jnp.zeros_like(product_ref)
        ones = frame_mask(wide, length_ref[0])
        low_ones = ones.astype(BF16)
        two_ones = jnp.concatenate([ones, ones], axis=1)

        @pl.loop(0, grid.side // 2)
        def _(pair):
            at = rows_at(pair * wide, wide)
            scaled = (reduced_ref[at, :].astype(F32) * two_ones).astype(BF16)
            right = jnp.concatenate([r_ref[at, :], scaled, low_ones], axis=1)
            product_ref[0 : x_ref.shape[1], :] += lax.dot_general(
                x_ref[at, :], right, (((0,), (0,)), ((), ())), preferred_element_type=F32
            )

        clips, _, size, _ = product_out.shape
        for clip in range(clips):
            at = slice(clip * size, (clip + 1) * size)
            for tile in range(3):
                product_out[clip, tile] = rest_product_ref[at, 128 * tile : 128 * (tile + 1)]
            for tile in range(5):
                product_out[clip, 3 + tile] = product_ref[at, 128 * tile : 128 * (tile + 1)]


def kernel_grads(grid, slots, first_ref, mid_ref, small_ref, d_ref, out_ref, mid_acc_ref, small_acc_ref, turned_ref):
    group_rows = grid.group * grid.pitch
    mid_acc_ref[...] = jnp.zeros_like(mid_acc_ref)
    small_acc_ref[...] = jnp.zeros_like(small_acc_ref)

    def neighbour(slot):
        return jnp.minimum(first_ref[0] + slot, TAPS - 1) // 9

    @pl.loop(0, grid.side // grid.group)
    def _(group):
        base = grid.lead + group * group_rows
        left = d_ref[rows_at(base, group_rows), :].T
        for slot in range(slots):
            tap = lax.rem(jnp.minimum(first_ref[0] + slot, TAPS - 1), 9)
            at = rows_at(
                base + (tap // 3 - 1) * grid.pitch + (lax.rem(tap, 3) - 1) * PITCH, group_rows
            )
            lanes = pl.ds(pl.multiple_of(neighbour(slot) * 128, 128), 128)
            right = jnp.concatenate([mid_ref[at, lanes], mid_ref[at, 384:512]], axis=1)
            mid_acc_ref[slot] += jnp.dot(left[0:384], right, preferred_element_type=F32)
            small_acc_ref[slot] += jnp.dot(
                left[384:512], small_ref[at, :], preferred_element_type=F32
            )

    share = round_up(slots * TAP_ROWS, 16 * out_ref.shape[0]) // out_ref.shape[0]

    def put(start, values):
        done = 0
        while done < values.shape[0]:
            clip, at = divmod(start + done, share)
            size = min(values.shape[0] - done, share - at)
            out_ref[clip, at : at + size, :] = values[done : done + size].astype(BF16)
            done = done + size

    half = MID_IN // 2
    for slot in range(slots):
        base = slot * TAP_ROWS
        rest = pl.ds(pl.multiple_of(neighbour(slot) * 32, 32), 32)
        for tile in range(3):
            lines = slice(128 * tile, 128 * (tile + 1))
            turned_ref[0:128, :] = mid_acc_ref[slot, lines, 0:128].T
            turned_ref[MID_IN : MID_IN + 128, :] = mid_acc_ref[slot, lines, 128:256].T
            turned_ref[128:MID_IN, :] = turned_ref[
                pl.ds(pl.multiple_of(MID_IN + neighbour(slot) * 32, 32), 32), :
            ]
            if tile < 2:
                put(base + MID_IN * tile, turned_ref[0:MID_IN, :])
            else:
                folded = turned_ref[0:half, :] + pltpu.roll(turned_ref[half:MID_IN, :], 64, 1)
                put(base + 2 * MID_IN, folded)
        turned_ref[0:128, :] = small_acc_ref[slot].T
        put(base + 2 * MID_IN + half, turned_ref[rest, :])
    used = slots * TAP_ROWS
    put(used, jnp.zeros((share * out_ref.shape[0] - used, 128), F32))


class Spread:
    def __init__(self, grid, plane_ref, across_ref, scale_ref, length):
        self.grid, self.plane, self.across, self.scale = (grid, plane_ref, across_ref, scale_ref)
        clear_edges(grid, plane_ref)
        window = box_window(grid.side, length)
        scale_ref[0] = box_scale(0, grid.side, window)
        scale_ref[1] = box_scale(1, grid.side, window)
        edge = jnp.zeros((PITCH, POOLED), F32)
        across_ref[0:PITCH, :] = edge
        across_ref[PITCH + grid.line_rows :, :] = edge

    def put(self, line, values):
        rows = self.grid.line_rows
        inner = jnp.where((line == 0) | (line == self.grid.side - 1), 0, 1)
        values = values * self.scale[inner]
        across = self.across
        across[PITCH : PITCH + rows, :] = values + earlier(values) + later(values)
        self.plane[rows_at((line + 1) * rows, rows), :] = (
            across[0:rows, :] + across[PITCH : PITCH + rows, :] + across[2 * PITCH :, :]
        )

    def get(self, start, size):
        rows = self.grid.line_rows
        return (
            self.plane[rows_at(start, size), :]
            + self.plane[rows_at(start + rows, size), :]
            + self.plane[rows_at(start + 2 * rows, size), :]
        )

    @staticmethod
    def scratch(grid):
        return [
            pltpu.VMEM((grid.rows + 2 * grid.line_rows, POOLED), F32),
            pltpu.VMEM((grid.line_rows + 2 * PITCH, POOLED), F32),
            pltpu.VMEM((2, grid.line_rows, POOLED), F32),
        ]


def rest_constants(outer_ref, total_ref, gain_ref, block):
    pool = OUTER - POOLED

    def pick(ref, lo, hi):
        return jnp.concatenate([ref[lo:hi, 0:DIRECT], ref[lo:hi, pool:]], axis=1)

    return before_norm(
        pick(gain_ref, block, block + 1), pick(outer_ref, 1, 2), pick(total_ref, 0, 2), pick(outer_ref, 2, 3)
    )


def point_back(grid, slots, block, kept, length_ref, place_ref, h_far, outer_ref, total_ref, gain_ref, error_far, reduced_far, r_far, moment_ref, sums_in_ref, reduced_gain_ref, x_far, p_far, *refs):
    pooled_slope_in, pooled_product_in, kept_far, *refs = refs
    dx_ref, dp_ref, reduced_total_ref, outer_sums_ref, *refs = refs
    h_ref, error_ref, reduced_ref, r_ref, x_ref, p_ref, du_ref, acc_ref, *refs = refs
    plane_ref, across_ref, scale_ref, sums_ref, pooled_slope_ref, pooled_product_ref, kept_ref, *refs = refs
    sem_ref, in_sem = refs
    rows = grid.line_rows
    pool = OUTER - POOLED
    lines = Lines(
        grid,
        (
            (h_far, 0, DIRECT),
            (h_far, pool, OUTER),
            (error_far, 0, DIRECT),
            (error_far, pool, OUTER),
            (reduced_far, 0, REDUCED),
            (r_far, 0, REDUCED),
        ),
        ((h_ref, 0), (h_ref, DIRECT), (error_ref, 0), (error_ref, DIRECT), (reduced_ref, 0), (r_ref, 0)),
        sem_ref,
    )
    lines.first()
    kept_rows = kept_ref.shape[1]
    arriving = copies(
        (x_far, p_far, kept_far.at[:, pl.ds(slots.rows, kept_rows), :]), (x_ref, p_ref, kept_ref), in_sem
    )
    for copy in arriving:
        copy.start()
    length = length_ref[0]
    total = total_of(sums_in_ref)
    reduced_total_ref[...] = total
    mid = before_norm(
        reduced_gain_ref[block : block + 1], moment_ref[1:2], total, outer_ref[2:3, 0:REDUCED]
    )
    rest = rest_constants(outer_ref, total_ref, gain_ref, block)
    mask = frame_mask(rows, length, DIRECT + POOLED)
    spread = Spread(grid, plane_ref, across_ref, scale_ref, length)

    def visit(line):
        at = rows_at(line * rows, rows)
        back = rest[0] * error_ref[at, :].astype(F32) - rest[1] - rest[2] * h_ref[at, :].astype(F32)
        back = back * mask
        du_ref[at, 0:DIRECT] = back[:, :DIRECT].astype(BF16)
        spread.put(line, back[:, DIRECT:])
        back = mid[0] * r_ref[at, :].astype(F32) - mid[1] - mid[2] * reduced_ref[at, :].astype(F32)
        du_ref[at, DIRECT:SECOND] = (back * mask[:, :REDUCED]).astype(BF16)

    lines.run(visit)
    for copy in arriving:
        copy.wait()
    sums_ref[...] = jnp.zeros_like(sums_ref)
    pooled_slope_ref[:, DIRECT:] = pooled_slope_in[...]
    pooled_product_ref[:, DIRECT:] = pooled_product_in[...]
    for pair in range(slots.pairs):
        slot = pair + (slots.empty if pair >= slots.gap else 0)
        at = slice(pair * rows, (pair + 1) * rows)
        start = slot % slots.each * rows
        values = kept_ref[slot // slots.each, start : start + rows, :]
        pooled_slope_ref[at, 0:DIRECT] = values[:, :DIRECT]
        pooled_product_ref[at, 0:DIRECT] = values[:, DIRECT:]

    @pl.loop(0, grid.side)
    def _(line):
        at = rows_at(line * rows, rows)
        du_ref[at, SECOND:] = (spread.get(line * rows, rows) * mask[:, :POOLED]).astype(BF16)
        dx = jnp.dot(du_ref[at, :], p_ref[...], preferred_element_type=F32).astype(BF16)
        dx_ref[at, :] = dx
        for number, ref in enumerate((pooled_slope_ref, pooled_product_ref)):
            sums_ref[8 * number : 8 * number + 8] += partial_sum(
                dx.astype(F32) * ref[at, :].astype(F32)
            )

    write_sums(outer_sums_ref, sums_ref, 0, OUTER)
    acc_ref[...] = lax.dot_general(
        x_ref[...], du_ref[...], (((0,), (0,)), ((), ())), preferred_element_type=F32
    )
    start = pl.multiple_of(place_ref[0] * kept, 16) if kept < acc_ref.shape[0] else 0
    clips, size, _ = dp_ref.shape
    for tile in range(FIRST // 128):
        values = acc_ref[pl.ds(start, kept), 128 * tile : 128 * (tile + 1)].astype(BF16)
        done = 0
        while done < kept:
            clip, at = divmod(kept * tile + done, size)
            few = min(kept - done, size - at)
            dp_ref[clip, at : at + few, :] = values[done : done + few]
            done = done + few
    used = (FIRST // 128) * kept
    while used < clips * size:
        clip, at = divmod(used, size)
        dp_ref[clip, at:, :] = jnp.zeros((size - at, 128), BF16)
        used = used + size - at


def rest_back(grid, small, slots, block, length_ref, outer_ref, total_ref, gain_ref, grad_ref, h_far, slope_far, kept_far, x_far, du_far, product_ref, *refs):
    h_ref, slope_ref, x_ref, du_ref, plane_ref, across_ref, scale_ref, sem_ref, x_sem, du_sem = refs
    rows = grid.line_rows
    pool = OUTER - POOLED

    def direct(step, lo, hi):
        slot = slots.slot_of(step)
        at = rows_at(lax.rem(slot, slots.each) * slots.pair_rows, slots.pair_rows)
        return kept_far.at[slot // slots.each, at, pl.ds(lo, hi - lo)]

    lines = Lines(
        grid,
        (
            (direct, 0, DIRECT),
            (h_far, SECOND, FIRST),
            (direct, DIRECT, 2 * DIRECT),
            (slope_far, SECOND, FIRST),
        ),
        ((h_ref, 0), (h_ref, DIRECT), (slope_ref, 0), (slope_ref, DIRECT)),
        sem_ref,
    )
    lines.first()
    x_copy = pltpu.make_async_copy(x_far, x_ref, x_sem.at[0])
    x_copy.start()
    length = length_ref[0]
    matrix = spread_matrix(grid, small)
    a, b, c = rest_constants(outer_ref, total_ref, gain_ref, block)
    mask = frame_mask(rows, length, DIRECT + POOLED)
    spread = Spread(grid, plane_ref, across_ref, scale_ref, length)

    def visit(step):
        for number in range(lines.step):
            line = step * lines.step + number
            at = rows_at(line * rows, rows)
            coarse = grad_ref[rows_at((line // 2) * small.line_rows, small.line_rows), :]
            grad = jnp.dot(
                matrix,
                jnp.concatenate([coarse[:, :DIRECT], coarse[:, pool:]], axis=1),
                preferred_element_type=F32,
            )
            back = a * (grad * slope_ref[at, :].astype(F32)) - b - c * h_ref[at, :].astype(F32)
            back = back * mask
            du_ref[at, 0:DIRECT] = back[:, :DIRECT].astype(BF16)
            spread.put(line, back[:, DIRECT:])

    lines.run(visit)
    x_copy.wait()
    product_ref[...] = jnp.zeros_like(product_ref)
    wide = lines.size
    pool_mask = frame_mask(wide, length)

    def leaving(step):
        at = rows_at(step * wide, wide)
        return pltpu.make_async_copy(du_ref.at[at, :], du_far.at[at, :], du_sem.at[0])

    @pl.loop(0, lines.steps)
    def _(step):
        at = rows_at(step * wide, wide)
        du_ref[at, DIRECT:] = (spread.get(step * wide, wide) * pool_mask).astype(BF16)
        leaving(step).start()
        product_ref[0 : x_ref.shape[1], :] += lax.dot_general(
            x_ref[at, :], du_ref[at, :], (((0,), (0,)), ((), ())), preferred_element_type=F32
        )

    pltpu.make_async_copy(du_ref, du_far, du_sem.at[0]).wait()


def mid_back(grid, block, length_ref, place_ref, moment_ref, sums_in_ref, gain_ref, du_far, h_far, r_far, p_far, dx_far, total_ref, *refs):
    du_ref, h_ref, r_ref, p_ref, dx_ref, sem_ref, p_sem, dx_sem = refs
    lines = Lines(
        grid,
        ((du_far, 0, DIRECT + POOLED), (h_far, 0, REDUCED), (r_far, 0, REDUCED)),
        ((du_ref, 0), (h_ref, 0), (r_ref, 0)),
        sem_ref,
    )
    lines.first()
    p_copy = pltpu.make_async_copy(p_far.at[place_ref[0]], p_ref, p_sem.at[0])
    p_copy.start()
    total = total_of(sums_in_ref)
    total_ref[...] = total
    a, b, c = before_norm(gain_ref[block : block + 1], moment_ref[1:2], total, moment_ref[2:3])
    mask = frame_mask(lines.size, length_ref[0], REDUCED)
    p_copy.wait()

    def leaving(step):
        at = rows_at(step * lines.size, lines.size)
        return pltpu.make_async_copy(dx_ref.at[at, :], dx_far.at[at, :], dx_sem.at[0])

    def visit(step):
        at = rows_at(step * lines.size, lines.size)
        back = a * r_ref[at, :].astype(F32) - b - c * h_ref[at, :].astype(F32)
        du = jnp.concatenate(
            [du_ref[at, :DIRECT], (back * mask).astype(BF16), du_ref[at, DIRECT:]], axis=1
        )
        dx_ref[at, :] = jnp.dot(du, p_ref[...], preferred_element_type=F32).astype(BF16)
        leaving(step).start()

    lines.run(visit)
    pltpu.make_async_copy(dx_ref, dx_far, dx_sem.at[0]).wait()


def combine(block, pieces_ref, moment_ref, sums_in_ref, gain_ref, out_ref):
    total = total_of(sums_in_ref)
    a, b, c = before_norm(gain_ref[block : block + 1], moment_ref[1:2], total, moment_ref[2:3])
    size = out_ref.shape[0] // 5
    products = total_of(pieces_ref)
    for tile in range(2):
        out_ref[size * tile : size * (tile + 1), :] = products[tile].astype(BF16)
        lanes = slice(128 * tile, 128 * (tile + 1))
        mid = a[:, lanes] * products[3 + tile] - b[:, lanes] * products[7] - c[:, lanes] * products[5 + tile]
        out_ref[size * (2 + tile) : size * (3 + tile), :] = mid.astype(BF16)
    out_ref[4 * size :, :] = products[2].astype(BF16)


def write_taps(read, slots, mid_ref, small_ref, mid_out, small_out, sem_ref):
    half = MID_IN // 2

    def leaving(tap):
        return (
            pltpu.make_async_copy(mid_ref.at[tap], mid_out.at[tap], sem_ref.at[0]),
            pltpu.make_async_copy(small_ref.at[tap], small_out.at[tap], sem_ref.at[1]),
        )

    for tap in range(TAPS):
        part, slot = divmod(tap, slots)
        base = slot * TAP_ROWS
        folded = read(part, base + 2 * MID_IN, half)
        mid_ref[tap, :, 0:128] = read(part, base, MID_IN)
        mid_ref[tap, :, 128:256] = read(part, base + MID_IN, MID_IN)
        mid_ref[tap, 0:half, 256:320] = folded[:, 0:64]
        mid_ref[tap, half:MID_IN, 256:320] = pltpu.roll(folded, 64, 1)[:, 0:64]
        small_ref[tap] = read(part, base + 2 * MID_IN + half, SMALL_IN)
        for copy in leaving(tap):
            copy.start()
    pltpu.make_async_copy(mid_ref, mid_out, sem_ref.at[0]).wait()
    pltpu.make_async_copy(small_ref, small_out, sem_ref.at[1]).wait()


def write_point(read, parts, kept, point_ref, wide_ref):
    for tile in range(FIRST // 128):
        for part in range(parts):
            start, stop = (kept * part, kept * (part + 1))
            values = read(part, kept * tile, kept)
            if kept * parts == CHANNELS:
                wide_ref[start:stop, :] = values
                continue
            for lo, hi, moved in ((0, 576, 0), (640, OUTER, 64)):
                lo, hi = (max(lo, start), min(hi, stop))
                if lo < hi:
                    wide_ref[lo - moved : hi - moved, :] = values[lo - start : hi - start]
        turned = wide_ref[...].T
        if tile < 3:
            point_ref[128 * tile : 128 * (tile + 1), :] = turned
        elif tile == 3:
            point_ref[384:448, :] = turned[0:64]
        else:
            point_ref[448:576, :] = turned


def copy_out(pairs, sem_ref):
    copies = [
        pltpu.make_async_copy(source, target, sem_ref.at[number])
        for number, (source, target) in enumerate(pairs)
    ]
    for copy in copies:
        copy.start()
    for copy in copies:
        copy.wait()


def share_reader(ref, clips, lo, share):
    def read(part, start, size):
        pieces, done = ([], 0)
        while done < size:
            clip, at = divmod(start + done, share)
            few = min(size - done, share - at)
            pieces.append(ref[part * clips + clip, lo + at : lo + at + few, :].astype(F32))
            done = done + few
        return pieces[0] if len(pieces) == 1 else jnp.concatenate(pieces, axis=0)

    return read


def unpack_second(clips, slots, shares_ref, mid_out, small_out, mid_ref, small_ref, sem_ref):
    read = share_reader(shares_ref, clips, 0, shares_ref.shape[1])
    write_taps(read, slots, mid_ref, small_ref, mid_out.at[1], small_out.at[1], sem_ref)


def unpack_first(parts, clips, slots, share, shares_ref, *refs):
    totals, refs = (refs[:4], refs[4:])
    mid_in, small_in, mid_out, small_out, point_out, gain_out, shift_out, *refs = refs
    mid_ref, small_ref, point_ref, wide_ref, sem_ref = refs
    for block in range(2):
        outer_ref, reduced_ref = totals[2 * block : 2 * block + 2]
        for row, out in enumerate((shift_out, gain_out)):
            at, line = (slice(block, block + 1), slice(row, row + 1))
            out[at, 0:256] = outer_ref[line, 0:256]
            out[at, 256:448] = reduced_ref[line, 0:192]
            out[at, 448:576] = outer_ref[line, 768:896]
            out[at, 576:896] = outer_ref[line, 256:576]
            out[at, 896:1024] = outer_ref[line, 640:768]
    read = share_reader(shares_ref, clips, share, shares_ref.shape[1] - share)
    write_point(read, parts, OUTER // parts, point_ref, wide_ref)
    last = pltpu.make_async_copy(point_ref, point_out.at[1], sem_ref.at[2])
    last.start()
    read = share_reader(shares_ref, clips, 0, share)
    write_taps(read, slots, mid_ref, small_ref, mid_out.at[0], small_out.at[0], sem_ref)
    last.wait()


def unpack_point(parts, clips, kept, place_ref, clip_ref, mine_ref, other_ref, point_in, point_out, buffer_ref, point_ref, wide_ref, sem_ref):
    tiles = FIRST // 128
    size = buffer_ref.shape[2] // clips
    for chip in range(clips // 2):
        for step in range(parts):
            part = lax.rem(place_ref[0] - step + parts, parts)
            for swapped, ref in enumerate((mine_ref, other_ref)):
                owner = clip_ref[0] ^ (2 * chip) ^ swapped
                source = (chip * parts + step) * tiles * size
                for tile in range(tiles):
                    buffer_ref[part, tile, rows_at(owner * size, size), :] = ref[
                        source + tile * size : source + (tile + 1) * size, :
                    ]

    def read(part, start, size):
        tile, at = divmod(start, kept)
        return buffer_ref[part, tile, at : at + size, :].astype(F32)

    write_point(read, parts, kept, point_ref, wide_ref)
    last = pltpu.make_async_copy(point_ref, point_out.at[0], sem_ref.at[0])
    last.start()
    last.wait()


def prepare(parts, mid_in, small_in, point_in, gain_in, shift_in, *refs):
    kernels, (point_ref, second_ref, *vectors) = (refs[:8], refs[8:14])
    for block in range(2):
        main_ref, last_ref, few_ref, back_ref = kernels[4 * block : 4 * block + 4]

        @pl.loop(0, 9)
        def _(tap):
            for number in range(3):
                source = 9 * number + tap
                main_ref[tap, 128 * number : 128 * (number + 1), :] = mid_in[block, source, 0:128, 0:256]
                main_ref[tap, 384 + 32 * number : 416 + 32 * number, :] = mid_in[
                    block, source, 128:MID_IN, 0:256
                ]
            main_ref[tap, 480:512, :] = jnp.zeros((32, 256), BF16)
            small = jnp.concatenate(
                [small_in[block, 9 * number + tap] for number in range(3)]
                + [jnp.zeros((32, 128), BF16)],
                axis=0,
            )
            at = pl.ds(pl.multiple_of(tap * 128, 128), 128)
            few_ref[at, :] = small
            back_ref[at, :] = small.astype(F32).T.astype(BF16)

        @pl.loop(0, 3)
        def _(place):
            for number in range(3):
                for rows, start, size in (
                    (slice(0, 128), 128 * number, 128),
                    (slice(128, MID_IN), 384 + 32 * number, 32),
                ):
                    pieces = [
                        mid_in[block, 9 * number + 3 * line + place, rows, 256:MID_OUT].astype(F32)
                        for line in range(3)
                    ]
                    pieces.append(jnp.zeros((size, 64), F32))
                    last_ref[place, start : start + size, :] = jnp.concatenate(
                        pieces, axis=1
                    ).astype(BF16)
            last_ref[place, 480:512, :] = jnp.zeros((32, 256), BF16)

    own = point_ref.shape[2]
    for lo, hi, at in ((0, 448, 0), (448, SQUEEZED, SECOND)):
        values = point_in[0, lo:hi, :].astype(F32)
        for part in range(parts):
            point_ref[part, at : at + hi - lo, :] = values[:, own * part : own * (part + 1)].astype(
                BF16
            )
        values = point_in[1, lo:hi, :].astype(F32)
        gap = jnp.zeros((hi - lo, 64), F32)
        second_ref[at : at + hi - lo, :] = jnp.concatenate(
            [values[:, :576], gap, values[:, 576:]], axis=1
        ).astype(BF16)
    for part in range(parts):
        point_ref[part, 448:SECOND, :] = jnp.zeros((64, own), BF16)
    second_ref[448:SECOND, :] = jnp.zeros((64, OUTER), BF16)
    for source, outer, reduced in ((gain_in, vectors[0], vectors[1]), (shift_in, vectors[2], vectors[3])):
        outer[:, 0:256] = source[:, 0:256]
        outer[:, 256:576] = source[:, 576:896]
        outer[:, 576:640] = jnp.zeros((2, 64), F32)
        outer[:, 640:768] = source[:, 896:1024]
        outer[:, 768:896] = source[:, 448:576]
        reduced[:, 0:192] = source[:, 256:448]
        reduced[:, 192:256] = jnp.zeros((2, 64), F32)


def round_up(value, unit):
    return -(-value // unit) * unit


def spread_over(values, axis, size):
    received = [values]
    for step in range(1, size):
        perm = [(source, (source + step) % size) for source in range(size)]
        received.append(lax.ppermute(values, axis, perm))
    return received


def after(values, earlier):
    return lax.optimization_barrier((values, earlier))[0]


def summed(pieces):
    pieces = lax.all_to_all(pieces, "dp", 0, 0, tiled=True)
    return jnp.sum(pieces.astype(F32), axis=0).astype(BF16)


def gather_chips(column, clips, work=None):
    columns = [column]
    for chip in range(1, clips // 2):
        perm = [(source, source ^ (2 * chip)) for source in range(clips)]
        columns.append(lax.ppermute(column, "dp", perm))
    if work is not None:
        columns = after(columns, work)
    mine = jnp.concatenate(columns, axis=0)
    other = lax.ppermute(mine, "dp", [(source, source ^ 1) for source in range(clips)])
    return (mine, other)


def on_device(frames, lengths, cotangent, pointwise, conv_mid, conv_small, gains, shifts):
    parts = lax.axis_size("branch")
    clips = lax.axis_size("dp")
    place = lax.axis_index("branch").astype(jnp.int32)
    side = frames.shape[2]
    grid, small = (Grid(side), Grid(side // 2))
    slots = Slots(grid, parts)
    cells = side * side
    own_channels = frames.shape[-1]
    length = lengths.astype(jnp.int32)
    half_length = length // 2
    place_one = place.reshape(1)

    own = frames[0].transpose(1, 2, 0, 3).reshape(grid.rows, own_channels)
    turned = call(functools.partial(turn, slots), shape((parts, own_channels, slots.rows), BF16))(own)
    by_pairs = lax.all_to_all(turned, "branch", 0, 0, tiled=True)
    kernel_shapes = (
        shape((9, 512, 256), BF16),
        shape((3, 512, 256), BF16),
        shape((1152, 128), BF16),
        shape((1152, 128), BF16),
    )
    prepared = call(
        functools.partial(prepare, parts),
        (
            *kernel_shapes,
            *kernel_shapes,
            shape((parts, FIRST, own_channels), BF16),
            shape((FIRST, OUTER), BF16),
            shape((2, OUTER), F32),
            shape((2, REDUCED), F32),
            shape((2, OUTER), F32),
            shape((2, REDUCED), F32),
        ),
    )(conv_mid, conv_small, pointwise.swapaxes(1, 2), gains, shifts)
    kernels = (prepared[0:4], prepared[4:8])
    point_first, point_second, outer_gain, reduced_gain, outer_shift, reduced_shift = prepared[8:]

    local_count = (length * (slots.held(place) * 2 * side)).astype(F32)
    mid, pool, direct, sums = call(
        functools.partial(first_pointwise, slots),
        (
            shape((mid_rows(slots), 128), BF16),
            shape((slots.rows + PITCH, POOLED), BF16),
            shape((slots.rows, DIRECT), F32),
            shape((3, SECOND), F32),
        ),
        [pltpu.VMEM((slots.rows, FIRST), F32)],
        scalars=2,
    )(length, local_count, by_pairs, point_first)
    mids = spread_over(mid, "branch", parts)
    sums = spread_over(jnp.sum(lax.all_gather(sums, "dp"), axis=0), "branch", parts)
    pooled_direct, kept_direct, moment = call(
        functools.partial(first_direct, grid, small, slots, 0),
        (
            shape((slots.each * small.line_rows, DIRECT), BF16),
            shape((slots.rows + slots.each * small.line_rows, 2 * DIRECT), BF16),
            shape((3, SECOND), F32),
        ),
        scalars=1,
        cost=3,
    )(length, direct, outer_gain, outer_shift, *sums)
    pool, pooled_direct = after((pool, pooled_direct), mids)
    pools = spread_over(pool, "branch", parts)
    h_reduced, taps_mid, taps_few, e, e_sums = call(
        functools.partial(first_convolve, grid, slots, 0),
        conv_outputs(grid),
        conv_scratch(grid),
        scalars=2,
        cost=40,
        far=range(5 + parts, 8 + parts),
        far_out=range(4),
    )(length, place_one, *mids, moment, reduced_gain, reduced_shift, *kernels[0][:3])
    pooled_directs = spread_over(after(pooled_direct, (pools, e_sums)), "branch", parts)
    kept_direct = lax.all_gather(after(kept_direct, pooled_directs), "branch", axis=0)
    q_pool, pool_sums = call(
        functools.partial(first_pool, grid, slots),
        (shape((grid.rows, POOLED), F32), shape((2, POOLED), F32)),
        [
            pltpu.VMEM((grid.rows + 2 * grid.line_rows, POOLED), F32),
            pltpu.VMEM((16, POOLED), F32),
        ],
        scalars=2,
    )(length, place_one, *pools)
    second_sums = lax.all_gather(jnp.concatenate([e_sums, pool_sums], axis=1), "dp")
    pair = 2 * grid.line_rows
    pooled, h_outer, slope, outer, pooled_slope, pooled_product = call(
        functools.partial(first_output, grid, small, 0),
        (
            shape((small.rows, FIRST), BF16),
            shape((grid.rows, FIRST), BF16),
            shape((grid.rows, FIRST), BF16),
            shape((3, OUTER), F32),
            shape((small.rows, FIRST), BF16),
            shape((small.rows, FIRST), BF16),
        ),
        [
            pltpu.VMEM((2, pair, POOLED), F32),
            pltpu.VMEM((2, pair, SECOND), F32),
            pltpu.VMEM((2, pair, FIRST), BF16),
            pltpu.VMEM((2, pair, FIRST), BF16),
            *[pltpu.SemaphoreType.DMA((2,))] * 4,
        ],
        scalars=1,
        far=(1, 2),
        far_out=(1, 2),
    )(
        length,
        q_pool,
        e,
        moment,
        second_sums[:, :, :SECOND],
        second_sums[:, :, SECOND:],
        outer_gain,
        outer_shift,
    )

    small_count = half_length.astype(F32) * float(small.side * small.side)
    q_small, sums_small, pooled = call(
        functools.partial(second_pointwise, small, slots),
        (
            shape((small.rows, FIRST), F32),
            shape((3, FIRST), F32),
            shape((small.rows, OUTER), BF16),
        ),
        [
            pltpu.VMEM((small.rows + 2 * small.line_rows, POOLED), F32),
            pltpu.VMEM((16, SECOND), F32),
            pltpu.VMEM((16, POOLED), F32),
        ],
        scalars=3,
    )(half_length, place_one, small_count, *pooled_directs, pooled, point_second)
    sums_small = lax.all_gather(sums_small, "dp")
    h_reduced_small, taps_mid_small, taps_few_small, e_small, e_sums_small, moment_small = call(
        functools.partial(second_convolve, small, 1),
        (*conv_outputs(small), shape((3, FIRST), F32)),
        conv_scratch(small),
        scalars=1,
        far=range(5, 8),
        far_out=range(4),
    )(half_length, q_small, sums_small, reduced_gain, reduced_shift, *kernels[1][:3])
    e_sums_small = lax.all_gather(e_sums_small, "dp")
    cot = cotangent[0].transpose(1, 2, 0, 3).reshape(small.side**2, cotangent.shape[1], CHANNELS)
    act, h_outer_small, error_small, outer_small, outer_sums_small = call(
        functools.partial(second_output, small, 1),
        (
            shape(cot.shape, BF16),
            shape((small.rows, OUTER), BF16),
            shape((small.rows, OUTER), BF16),
            shape((3, OUTER), F32),
            shape((2, OUTER), F32),
        ),
        [pltpu.VMEM((16, OUTER), F32)],
        scalars=1,
    )(half_length, q_small, e_small, moment_small, e_sums_small, outer_gain, outer_shift, cot)

    taps_each = -(-TAPS // parts)
    tap_share = round_up(taps_each * TAP_ROWS, 16 * clips) // clips
    first_tap = place_one * taps_each

    def conv_back_scratch(at):
        return [
            pltpu.VMEM((9, 512, 256), BF16),
            pltpu.VMEM((3, 512, 256), BF16),
            pltpu.VMEM((1152, 128), BF16),
            pltpu.VMEM((at.padded, 256), BF16),
            pltpu.VMEM((at.group * at.pitch, FIRST), F32),
            pltpu.VMEM((16, REDUCED), F32),
            pltpu.SemaphoreType.DMA((3,)),
        ]

    gathered = lax.all_gather(outer_sums_small, "dp")
    d_low, total_small, packed_small = call(
        functools.partial(second_back, small, None, 1, taps_each),
        (
            shape((small.padded, SECOND), BF16),
            shape((2, OUTER), F32),
            shape((clips, tap_share, 128), BF16),
        ),
        second_back_scratch(small, taps_each),
        scalars=2,
        cost=8,
        far=(2, 6, 7, 8),
        far_out=(0,),
    )(
        half_length,
        first_tap,
        h_outer_small,
        outer_small,
        gathered,
        outer_gain,
        error_small,
        taps_mid_small,
        taps_few_small,
    )
    r_low, sums_low = call(
        functools.partial(conv_back, small, 1),
        (shape((small.rows, REDUCED), BF16), shape((2, REDUCED), F32)),
        conv_back_scratch(small),
        scalars=1,
        cost=8,
        far=(5, 6, 7),
    )(
        half_length,
        d_low,
        h_reduced_small,
        reduced_gain,
        reduced_shift,
        *kernels[1][:2],
        kernels[1][3],
    )
    share_small = summed(packed_small)
    sums_low, share_small = lax.optimization_barrier((sums_low, share_small))
    gathered = lax.all_gather(sums_low, "dp")
    kept = OUTER // parts
    point_share = round_up(kept * (FIRST // 128), 16 * clips) // clips
    coarse_rows = slots.each * small.line_rows
    dx_small, point_packed, reduced_total_small, outer_sums = call(
        functools.partial(point_back, small, slots, 1, kept),
        (
            shape((small.rows, OUTER), BF16),
            shape((clips, point_share, 128), BF16),
            shape((2, REDUCED), F32),
            shape((2, OUTER), F32),
        ),
        [
            pltpu.VMEM((small.rows, DIRECT + POOLED), BF16),
            pltpu.VMEM((small.rows, DIRECT + POOLED), BF16),
            pltpu.VMEM((small.rows, REDUCED), BF16),
            pltpu.VMEM((small.rows, REDUCED), BF16),
            pltpu.VMEM((small.rows, OUTER), BF16),
            pltpu.VMEM((FIRST, OUTER), BF16),
            pltpu.VMEM((small.rows, FIRST), BF16),
            pltpu.VMEM((OUTER, FIRST), F32),
            *Spread.scratch(small),
            pltpu.VMEM((16, OUTER), F32),
            pltpu.VMEM((small.rows, OUTER), BF16),
            pltpu.VMEM((small.rows, OUTER), BF16),
            pltpu.VMEM((parts, coarse_rows, 2 * DIRECT), BF16),
            Lines.semaphores(small, 6),
            pltpu.SemaphoreType.DMA((3,)),
        ],
        scalars=2,
        cost=10,
        far=(2, 6, 7, 8, 12, 13, 16),
    )(
        half_length,
        place_one,
        h_outer_small,
        outer_small,
        total_small,
        outer_gain,
        error_small,
        h_reduced_small,
        r_low,
        moment_small[:, DIRECT:SECOND],
        gathered,
        reduced_gain,
        pooled,
        point_second,
        pooled_slope,
        pooled_product,
        kept_direct,
    )
    whole_small = lax.all_gather(share_small, ("branch", "dp"), axis=0)

    gathered = lax.all_gather(outer_sums, "dp")
    d_low, total, packed = call(
        functools.partial(second_back, grid, small, 0, taps_each),
        (
            shape((grid.padded, SECOND), BF16),
            shape((2, OUTER), F32),
            shape((clips, tap_share + point_share, 128), BF16),
        ),
        second_back_scratch(grid, taps_each),
        scalars=2,
        cost=18,
        far=(2, 6, 9, 10),
        far_out=(0,),
    )(length, first_tap, h_outer, outer, gathered, outer_gain, slope, dx_small, point_packed, taps_mid, taps_few)
    product_rows = round_up(own_channels, 16 * clips)
    du_rest, rest_product = call(
        functools.partial(rest_back, grid, small, slots, 0),
        (shape((grid.rows, DIRECT + POOLED), BF16), shape((product_rows, DIRECT + POOLED), F32)),
        [
            pltpu.VMEM((grid.rows, DIRECT + POOLED), BF16),
            pltpu.VMEM((grid.rows, DIRECT + POOLED), BF16),
            pltpu.VMEM((grid.rows, own_channels), BF16),
            pltpu.VMEM((grid.rows, DIRECT + POOLED), BF16),
            *Spread.scratch(grid),
            Lines.semaphores(grid, 4),
            pltpu.SemaphoreType.DMA((1,)),
            pltpu.SemaphoreType.DMA((1,)),
        ],
        scalars=1,
        cost=8,
        far=(5, 6, 7, 8),
        far_out=(0,),
    )(length, outer, after(total, packed), outer_gain, dx_small, h_outer, slope, kept_direct, own)
    share = summed(packed)
    d_low, share = lax.optimization_barrier((after(d_low, rest_product), share))
    r_low, sums_low, products = call(
        functools.partial(conv_back, grid, 0),
        (
            shape((grid.rows, REDUCED), BF16),
            shape((2, REDUCED), F32),
            shape((clips, 8, product_rows // clips, 128), F32),
        ),
        [
            *conv_back_scratch(grid),
            pltpu.VMEM((grid.rows, own_channels), BF16),
            pltpu.VMEM((product_rows, FIRST), F32),
            pltpu.SemaphoreType.DMA((1,)),
        ],
        scalars=1,
        cost=22,
        far=(5, 6, 7, 8),
    )(
        length,
        d_low,
        h_reduced,
        reduced_gain,
        reduced_shift,
        *kernels[0][:2],
        kernels[0][3],
        own,
        rest_product,
    )
    whole = lax.all_gather(share, ("branch", "dp"), axis=0)
    gathered = lax.all_gather(sums_low, "dp")
    pieces = lax.all_to_all(products, "dp", 0, 0, tiled=True)
    mid_moment = moment[:, DIRECT:]
    dx, reduced_total = call(
        functools.partial(mid_back, grid, 0),
        (shape((grid.rows, own_channels), BF16), shape((2, REDUCED), F32)),
        [
            pltpu.VMEM((grid.rows, DIRECT + POOLED), BF16),
            pltpu.VMEM((grid.rows, REDUCED), BF16),
            pltpu.VMEM((grid.rows, REDUCED), BF16),
            pltpu.VMEM((FIRST, own_channels), BF16),
            pltpu.VMEM((grid.rows, own_channels), BF16),
            Lines.semaphores(grid, 3),
            pltpu.SemaphoreType.DMA((1,)),
            pltpu.SemaphoreType.DMA((1,)),
        ],
        scalars=2,
        cost=8,
        far=(5, 6, 7, 8),
        far_out=(0,),
    )(length, place_one, mid_moment, gathered, reduced_gain, du_rest, h_reduced, r_low, point_first)
    pieces, dx = lax.optimization_barrier((pieces, dx))
    point_sum = call(
        functools.partial(combine, 0),
        shape((5 * product_rows // clips, 128), BF16),
        cost=1,
    )(pieces, mid_moment, gathered, reduced_gain)
    received = spread_over(point_sum, "branch", parts)

    outs = (
        shape((2, TAPS, MID_IN, MID_OUT), F32),
        shape((2, TAPS, SMALL_IN, SMALL_OUT), F32),
        shape((2, SQUEEZED, CHANNELS), F32),
    )
    tap_scratch = [
        pltpu.VMEM((TAPS, MID_IN, MID_OUT), F32),
        pltpu.VMEM((TAPS, SMALL_IN, SMALL_OUT), F32),
    ]
    point_scratch = [pltpu.VMEM((SQUEEZED, CHANNELS), F32), pltpu.VMEM((CHANNELS, 128), F32)]
    mid_grad, small_grad = call(
        functools.partial(unpack_second, clips, taps_each),
        outs[:2],
        [*tap_scratch, pltpu.SemaphoreType.DMA((2,))],
        out_space=pl.ANY,
        cost=5,
    )(whole_small)
    received, mid_grad, small_grad = lax.optimization_barrier((received, mid_grad, small_grad))
    point_mine, point_other = gather_chips(jnp.concatenate(received, axis=0), clips)
    norms = shape((2, 1024), F32)
    mid_grad, small_grad, point_grad, gain_grad, shift_grad = call(
        functools.partial(unpack_first, parts, clips, taps_each, tap_share),
        (*outs, norms, norms),
        [*tap_scratch, *point_scratch, pltpu.SemaphoreType.DMA((3,))],
        far_out=(0, 1, 2),
        aliases={5: 0, 6: 1},
        cost=6,
    )(whole, total, reduced_total, total_small, reduced_total_small, mid_grad, small_grad)
    clip_one = lax.axis_index("dp").astype(jnp.int32).reshape(1)
    point_grad = call(
        functools.partial(unpack_point, parts, clips, own_channels),
        outs[2],
        [
            pltpu.VMEM((parts, FIRST // 128, product_rows, 128), BF16),
            *point_scratch,
            pltpu.SemaphoreType.DMA((1,)),
        ],
        scalars=2,
        out_space=pl.ANY,
        aliases={4: 0},
        cost=3,
    )(place_one, clip_one, point_mine, point_other, point_grad)
    act = act.reshape(small.side, small.side, cotangent.shape[1], CHANNELS).transpose(2, 0, 1, 3)
    input_grad = dx.reshape(side, side, PITCH, own_channels).transpose(2, 0, 1, 3)
    return (
        act[None],
        input_grad[None],
        point_grad.swapaxes(1, 2),
        mid_grad,
        small_grad,
        gain_grad,
        shift_grad,
    )


def solution(mesh):
    split = P("dp", None, None, None, "branch")
    whole = P("dp", None, None, None, None)
    return jax.shard_map(
        on_device,
        mesh=mesh,
        in_specs=(split, P("dp"), whole, P(), P(), P(), P(), P()),
        out_specs=(whole, split, P(), P(), P(), P(), P()),
        check_vma=False,
    )
```

```python
import functools

import jax
import jax.numpy as jnp
from jax import lax
from jax.experimental import pallas as pl
from jax.experimental.pallas import tpu as pltpu
from jax.sharding import PartitionSpec as P

DIRECT = 256
MID_IN = 160
MID_OUT = 320
SMALL_IN = 32
SMALL_OUT = 128
TAPS = 27
CHANNELS = 832
SQUEEZED = 576
PITCH = 16
REDUCED = 256
POOLED = 128
FIRST = 640
SECOND = 512
OUTER = 896
TAP_ROWS = 432
EPSILON = 1e-05
F32 = jnp.float32
BF16 = jnp.bfloat16
VMEM_BYTES = 58 * 2**20
LARGE = 2200 * 2**10


def call(body, out_shape, scratch=(), scalars=0, cost=5, aliases=None, far=(), far_out=()):
    aliases = aliases or {}

    def large(values):
        size = values.dtype.itemsize
        for extent in values.shape:
            size = size * extent
        return size > LARGE

    def placed(out):
        return pltpu.HBM(out.shape, out.dtype) if large(out) else out

    def run(*operands):
        specs = [
            pl.BlockSpec(
                memory_space=pl.ANY
                if number in aliases or number in far
                else pltpu.SMEM
                if number < scalars
                else pltpu.VMEM
            )
            for number in range(len(operands))
        ]
        operands = [
            pltpu.with_memory_space_constraint(operand, pltpu.HBM) if large(operand) else operand
            for operand in operands
        ]
        if isinstance(out_shape, tuple):
            out_specs = tuple(
                pl.BlockSpec(memory_space=pl.ANY if number in far_out else pltpu.VMEM)
                for number in range(len(out_shape))
            )
        else:
            out_specs = pl.BlockSpec(memory_space=pl.ANY if 0 in far_out else pltpu.VMEM)
        return pl.pallas_call(
            body,
            out_shape=jax.tree.map(placed, out_shape),
            in_specs=specs,
            out_specs=out_specs,
            input_output_aliases=aliases,
            scratch_shapes=list(scratch),
            compiler_params=pltpu.CompilerParams(vmem_limit_bytes=VMEM_BYTES),
            cost_estimate=pl.CostEstimate(
                flops=0, bytes_accessed=int(cost * 3 * 10**6), transcendentals=0
            ),
        )(*operands)

    return run


def shape(dims, dtype):
    return jax.ShapeDtypeStruct(tuple(dims), dtype)


def rows_at(start, size):
    return pl.ds(pl.multiple_of(start, 16), size)


def frames_of(rows, width=128):
    return lax.broadcasted_iota(jnp.int32, (rows, width), 0) & (PITCH - 1)


def frame_mask(rows, length, width=128):
    mask = jnp.where(frames_of(rows) < length, 1.0, 0.0)
    return jnp.concatenate([mask] * (width // 128), axis=1) if width > 128 else mask


def earlier(values):
    return jnp.where(frames_of(*values.shape) > 0, pltpu.roll(values, 1, 0), 0.0)


def later(values):
    rows = values.shape[0]
    return jnp.where(frames_of(*values.shape) < PITCH - 1, pltpu.roll(values, rows - 1, 0), 0.0)


def plane_box(values):
    across = values + earlier(values) + later(values)
    edge = jnp.zeros((PITCH, values.shape[1]), values.dtype)
    return (
        across
        + jnp.concatenate([across[PITCH:], edge], axis=0)
        + jnp.concatenate([edge, across[:-PITCH]], axis=0)
    )


def box_window(side, length):
    frame = frames_of(side * PITCH)
    place = lax.broadcasted_iota(jnp.int32, (side * PITCH, 128), 0) >> 4

    def one(condition):
        return jnp.where(condition, 1.0, 0.0)

    count = one(frame < length) + one(frame + 1 < length) + one((frame > 0) & (frame - 1 < length))
    return count * (3.0 - one(place == 0) - one(place == side - 1))


def box_scale(line, side, window):
    lines = 3.0 - jnp.where(line == 0, 1.0, 0.0) - jnp.where(line == side - 1, 1.0, 0.0)
    return 1.0 / jnp.maximum(window * lines, 1.0)


def sigmoid(value):
    return 0.5 * jnp.tanh(0.5 * value) + 0.5


def silu(value):
    return value * sigmoid(value)


def silu_slope(value):
    gate = sigmoid(value)
    return gate * (1.0 + value * (1.0 - gate))


def partial_sum(values):
    rows, width = values.shape
    return jnp.sum(values.reshape(rows // 8, 8, width), axis=0)


def moments(total, square, count):
    center = total / count
    return (center, lax.rsqrt(square / count - center * center + EPSILON))


def total_of(gathered):
    count = len(gathered) if isinstance(gathered, (list, tuple)) else gathered.shape[0]
    total = gathered[0][...]
    for number in range(1, count):
        total = total + gathered[number][...]
    return total


def pool_matrix(side, transposed):
    line = 2 * side * PITCH
    few, many = (side * PITCH, 2 * line)
    dims = (many, few) if transposed else (few, many)
    coarse = lax.broadcasted_iota(jnp.int32, dims, 1 if transposed else 0)
    fine = lax.broadcasted_iota(jnp.int32, dims, 0 if transposed else 1)
    fine = jnp.where(fine >= line, fine - line, fine)
    same = (fine >> 5 == coarse >> 4) & ((fine & (PITCH - 1)) >> 1 == coarse & (PITCH - 1))
    return jnp.where(same, 0.125, 0.0).astype(BF16)


class Grid:
    def __init__(self, side):
        self.side = side
        self.line_rows = side * PITCH
        self.rows = side * self.line_rows
        self.pitch = (side + 1) * PITCH
        self.lead = self.pitch + PITCH
        self.padded = (side + 2) * self.pitch + 2 * PITCH
        self.group = 2 if side % 2 == 0 else side


class Slots:
    def __init__(self, grid, parts):
        self.pairs = grid.side // 2
        self.parts = parts
        self.each = -(-self.pairs // parts)
        self.empty = parts * self.each - self.pairs
        self.gap = parts * self.each // 2 - 1
        self.pair_rows = 2 * grid.line_rows
        self.rows = self.each * self.pair_rows

    def slot_of(self, pair):
        return pair + jnp.where(pair >= self.gap, self.empty, 0)

    def pair_of(self, slot):
        return slot - jnp.where(slot >= self.gap, self.empty, 0)

    def used(self, slot):
        return (slot < self.gap) | (slot >= self.gap + self.empty)

    def held(self, place):
        count = jnp.zeros((), jnp.int32)
        for number in range(self.each):
            count = count + jnp.where(self.used(place * self.each + number), 1, 0)
        return count


def clear_empty(grid, ref):
    width = ref.shape[1]
    ref[0 : grid.lead, :] = jnp.zeros((grid.lead, width), ref.dtype)
    end = grid.lead + grid.side * grid.pitch
    ref[end:, :] = jnp.zeros((ref.shape[0] - end, width), ref.dtype)

    @pl.loop(0, grid.side)
    def _(line):
        at = rows_at(grid.lead + line * grid.pitch + grid.line_rows, PITCH)
        ref[at, :] = jnp.zeros((PITCH, width), ref.dtype)


def store_taps(mid_ref, small_ref, at, act):
    before, after_ = (earlier(act), later(act))
    mid_ref[at, 0:128] = before[:, :128].astype(BF16)
    mid_ref[at, 128:256] = act[:, :128].astype(BF16)
    mid_ref[at, 256:384] = after_[:, :128].astype(BF16)
    before, act, after_ = (before[:, 128:], act[:, 128:], after_[:, 128:])
    lane = lax.broadcasted_iota(jnp.int32, act.shape, 1)
    mid_ref[at, 384:512] = jnp.where(
        lane < 32, before, jnp.where(lane < 64, pltpu.roll(act, 32, 1), pltpu.roll(after_, 64, 1))
    ).astype(BF16)
    small_ref[at, :] = jnp.where(
        lane < 32, pltpu.roll(before, 96, 1), jnp.where(lane < 64, act, pltpu.roll(after_, 32, 1))
    ).astype(BF16)


def tap_start(grid, base, tap, sign):
    return base + sign * ((tap // 3 - 1) * grid.pitch + (tap % 3 - 1) * PITCH)


def convolve(grid, taps, kernels, rest_ref, acc_ref, stage_ref, e_ref, stage_sem, sums_ref, length):
    mid_ref, small_ref = taps
    main_ref, last_ref, small_kernel_ref = kernels
    group_rows = grid.group * grid.pitch
    stage_rows = grid.group * grid.line_rows
    groups = grid.side // grid.group
    sums_ref[...] = jnp.zeros_like(sums_ref)
    mask = frame_mask(grid.line_rows, length, SECOND)
    edge = jnp.zeros((grid.pitch, 256), F32)
    rest_ref[PITCH : grid.lead, :] = edge
    end = grid.lead + grid.side * grid.pitch
    rest_ref[end : end + grid.pitch, :] = edge

    @pl.loop(0, groups)
    def _(group):
        base = grid.lead + group * group_rows
        total = None
        for place in range(3):
            part = jnp.dot(
                mid_ref[rows_at(base + (place - 1) * PITCH, group_rows), :],
                last_ref[place],
                preferred_element_type=F32,
            )
            total = part if total is None else total + part
        rest_ref[rows_at(base, group_rows), :] = total

    lane = lax.broadcasted_iota(jnp.int32, (grid.line_rows, 128), 1)

    def staged(group, slot):
        return pltpu.make_async_copy(
            stage_ref.at[slot],
            e_ref.at[rows_at(group * stage_rows, stage_rows), :],
            stage_sem.at[slot],
        )

    @pl.loop(0, groups)
    def _(group):
        base = grid.lead + group * group_rows
        slot = lax.rem(group, 2)
        for tap in range(9):
            part = jnp.dot(
                mid_ref[rows_at(tap_start(grid, base, tap, 1), group_rows), :],
                main_ref[tap],
                preferred_element_type=F32,
            )
            acc_ref[:, 0:256] = part if tap == 0 else acc_ref[:, 0:256] + part
        near = [small_ref[rows_at(tap_start(grid, base, tap, 1), group_rows), :] for tap in range(9)]
        acc_ref[:, 256:384] = jnp.dot(
            jnp.concatenate(near, axis=1), small_kernel_ref[...], preferred_element_type=F32
        )

        @pl.when(group >= 2)
        def _():
            staged(group - 2, slot).wait()

        for number in range(grid.group):
            rows = grid.line_rows
            start = base + number * grid.pitch
            last = (
                rest_ref[rows_at(start - grid.pitch, rows), 0:128]
                + pltpu.roll(rest_ref[rows_at(start, rows), 0:128], 64, 1)
                + rest_ref[rows_at(start + grid.pitch, rows), 128:256]
            )
            lines = slice(number * grid.pitch, number * grid.pitch + rows)
            values = jnp.concatenate(
                [acc_ref[lines, 0:256], jnp.where(lane < 64, last, 0.0), acc_ref[lines, 256:384]],
                axis=1,
            )
            stage_ref[slot, number * rows : (number + 1) * rows, :] = values
            masked = values * mask
            sums_ref[0:8] += partial_sum(masked)
            sums_ref[8:16] += partial_sum(masked * values)
        staged(group, slot).start()

    for group in range(max(groups - 2, 0), groups):
        staged(group, group % 2).wait()


def conv_scratch(grid):
    group_rows = grid.group * grid.pitch
    return [
        pltpu.VMEM((9, 512, 256), BF16),
        pltpu.VMEM((3, 512, 256), BF16),
        pltpu.VMEM((1152, 128), BF16),
        pltpu.VMEM((grid.padded, 512), BF16),
        pltpu.VMEM((grid.padded, 128), BF16),
        pltpu.VMEM((grid.rows, REDUCED), BF16),
        pltpu.VMEM((grid.padded, 256), F32),
        pltpu.VMEM((group_rows, 384), F32),
        pltpu.VMEM((2, grid.group * grid.line_rows, SECOND), F32),
        pltpu.VMEM((16, SECOND), F32),
        pltpu.SemaphoreType.DMA((3,)),
        pltpu.SemaphoreType.DMA((3,)),
        pltpu.SemaphoreType.DMA((2,)),
    ]


def conv_outputs(grid, *clips):
    return (
        shape((grid.rows, REDUCED), BF16),
        shape((grid.padded, 512), BF16),
        shape((grid.padded, 128), BF16),
        shape((grid.rows, SECOND), F32),
        shape((*clips, 2, SECOND), F32),
    )


def copies(sources, targets, sem_ref):
    return [
        pltpu.make_async_copy(source, target, sem_ref.at[number])
        for number, (source, target) in enumerate(zip(sources, targets))
    ]


def run_convolution(grid, length, far_kernels, outputs, scratch, fill):
    h_out, mid_out, small_out, e_out, sums_out = outputs
    kernels, (mid_ref, small_ref, h_ref), rest = (scratch[:3], scratch[3:6], scratch[6:])
    rest_ref, acc_ref, stage_ref, sums_ref, in_sem, out_sem, stage_sem = rest
    arriving = copies(far_kernels, kernels, in_sem)
    for copy in arriving:
        copy.start()
    clear_empty(grid, mid_ref)
    clear_empty(grid, small_ref)
    fill(h_ref, mid_ref, small_ref)
    leaving = copies((mid_ref, small_ref, h_ref), (mid_out, small_out, h_out), out_sem)
    for copy in leaving:
        copy.start()
    for copy in arriving:
        copy.wait()
    convolve(
        grid, (mid_ref, small_ref), kernels, rest_ref, acc_ref, stage_ref, e_out, stage_sem, sums_ref, length
    )
    write_sums(sums_out, sums_ref, 0, SECOND)
    for copy in leaving:
        copy.wait()


def write_row(out_ref, row, lo, hi, values):
    if len(out_ref.shape) == 2:
        out_ref[row : row + 1, lo:hi] = values
    else:
        for clip in range(out_ref.shape[0]):
            out_ref[clip, row : row + 1, lo:hi] = values


def write_sums(out_ref, sums_ref, lo, hi):
    for number in range(2):
        values = jnp.sum(sums_ref[8 * number : 8 * number + 8], axis=0, keepdims=True)
        write_row(out_ref, number, lo, hi, values)


def turn(slots, x_ref, out_ref):
    for slot in range(slots.parts * slots.each):
        part, number = divmod(slot, slots.each)
        lanes = slice(number * slots.pair_rows, (number + 1) * slots.pair_rows)
        if slots.gap <= slot < slots.gap + slots.empty:
            out_ref[part, :, lanes] = jnp.zeros((out_ref.shape[1], slots.pair_rows), BF16)
            continue
        pair = slot - (slots.empty if slot >= slots.gap else 0)
        rows = slice(pair * slots.pair_rows, (pair + 1) * slots.pair_rows)
        out_ref[part, :, lanes] = x_ref[rows, :].T


def first_pointwise(slots, length_ref, count_ref, x_ref, p_ref, mid_ref, pool_ref, direct_ref, sums_ref, u_ref):
    rows, step = (slots.rows, 112)
    length, count = (length_ref[0], count_ref[0])
    for part in range(slots.parts):
        product = lax.dot_general(
            x_ref[part], p_ref[part], (((0,), (1,)), ((), ())), preferred_element_type=F32
        )
        u_ref[...] = product if part == 0 else u_ref[...] + product
    mask = frame_mask(step, length, FIRST)

    def summed(number, carry):
        values = u_ref[rows_at(number * step, step), :] * mask
        u_ref[rows_at(number * step, step), :] = values
        few = values[:, :SECOND]
        return (carry[0] + partial_sum(values), carry[1] + partial_sum(few * few))

    zero = (jnp.zeros((8, FIRST), F32), jnp.zeros((8, SECOND), F32))
    total, square = lax.fori_loop(0, rows // step, summed, zero)
    total = jnp.sum(total, axis=0, keepdims=True)
    write_row(sums_ref, 0, 0, SECOND, total[:, :SECOND])
    write_row(sums_ref, 1, 0, SECOND, jnp.sum(square, axis=0, keepdims=True))
    write_row(sums_ref, 2, 0, SECOND, jnp.full((1, SECOND), count, F32))
    offset = (total / jnp.full((1, FIRST), jnp.maximum(count, 1.0), F32)).astype(BF16)
    wide_offset = offset.astype(F32)
    tail = jnp.broadcast_to(wide_offset, (PITCH, FIRST)).astype(BF16)
    pool_ref[rows : rows + PITCH, :] = tail[:, SECOND:]
    shared = mid_ref.shape[0] - 2 * PITCH
    mid_ref[shared : shared + PITCH, :] = tail[:, 256:384]
    mid_ref[shared + PITCH :, :] = tail[:, 384:512]

    @pl.loop(0, rows // step)
    def _(number):
        at = rows_at(number * step, step)
        values = u_ref[at, :]
        direct_ref[at, :] = values[:, :DIRECT]
        values = values[:, DIRECT:] - wide_offset[:, DIRECT:]
        mid_ref[at, :] = values[:, :128].astype(BF16)
        pool_ref[at, :] = values[:, 256:].astype(BF16)

    lane = lax.broadcasted_iota(jnp.int32, (step, 128), 1)
    for couple in range(0, slots.each, 2):

        @pl.loop(0, slots.pair_rows // step)
        def _(number):
            start = couple * slots.pair_rows + number * step
            values = u_ref[rows_at(start, step), 384:512] - wide_offset[:, 384:512]
            if couple + 1 < slots.each:
                other = u_ref[rows_at(start + slots.pair_rows, step), 384:512]
                other = pltpu.roll(other - wide_offset[:, 384:512], 64, 1)
                values = jnp.where(lane < 64, values, other)
            place = rows + couple // 2 * slots.pair_rows + number * step
            mid_ref[rows_at(place, step), :] = values.astype(BF16)


def mid_rows(slots):
    return slots.rows + -(-slots.each // 2) * slots.pair_rows + 2 * PITCH


def each_pair(slots, place, refs, visit):
    for step, ref in enumerate(refs):
        source = lax.rem(place - step + slots.parts, slots.parts)
        for number in range(slots.each):
            slot = source * slots.each + number

            @pl.when(slots.used(slot))
            def _():
                visit(slots.pair_of(slot), ref, number)


def set_moments(total, moment_ref):
    count = total[2:3]
    center, inverse = moments(total[0:1], total[1:2], count)
    moment_ref[0:1, :] = center
    moment_ref[1:2, :] = inverse
    moment_ref[2:3, :] = count
    return (center, inverse)


def first_convolve(grid, slots, block, length_ref, place_ref, *refs):
    parts = slots.parts
    mids, (moment_ref, gain_ref, shift_ref), refs = (refs[:parts], refs[parts : parts + 3], refs[parts + 3 :])
    far_kernels, outputs, scratch = (refs[:3], refs[3:8], refs[8:])
    length = length_ref[0]
    center, inverse = (moment_ref[0:1, DIRECT:], moment_ref[1:2, DIRECT:])
    gain, shift = (gain_ref[block : block + 1], shift_ref[block : block + 1])
    step = 112
    mask = frame_mask(step, length, REDUCED)
    lane = lax.broadcasted_iota(jnp.int32, (step, 128), 1)

    def fill(h_ref, mid_ref, small_ref):
        def visit(pair, ref, number):
            shared = ref.shape[0] - 2 * PITCH
            offset = jnp.concatenate(
                [
                    ref[at : at + PITCH, :].astype(F32)[0:1]
                    for at in (shared, shared + PITCH)
                ],
                axis=1,
            )
            other = slots.rows + number // 2 * slots.pair_rows

            @pl.loop(0, slots.pair_rows // step)
            def _(chunk):
                values = ref[rows_at(number * slots.pair_rows + chunk * step, step), :].astype(F32)
                few = ref[rows_at(other + chunk * step, step), :].astype(F32)
                if number % 2 == 1:
                    few = pltpu.roll(few, 64, 1)
                few = jnp.where(lane < 64, few, 0.0)
                values = jnp.concatenate([values, few], axis=1) + offset
                scaled = (values - center) * inverse
                row = pair * slots.pair_rows + chunk * step
                h_ref[rows_at(row, step), :] = scaled.astype(BF16)
                act = silu(gain * scaled + shift) * mask
                line = row // grid.line_rows
                at = grid.lead + line * grid.pitch + row - line * grid.line_rows
                store_taps(mid_ref, small_ref, rows_at(at, step), act)

        each_pair(slots, place_ref[0], mids, visit)

    run_convolution(grid, length, far_kernels, outputs, scratch, fill)


def pool_planes(grid, plane_ref, q_ref, lo, sums_ref, length, window):
    rows = grid.line_rows
    mask = frame_mask(rows, length)
    sums_ref[...] = jnp.zeros_like(sums_ref)

    @pl.loop(0, grid.side)
    def _(line):
        start = line * rows
        values = (
            plane_ref[rows_at(start, rows), :]
            + plane_ref[rows_at(start + rows, rows), :]
            + plane_ref[rows_at(start + 2 * rows, rows), :]
        ) * box_scale(line, grid.side, window)
        q_ref[rows_at(start, rows), lo : lo + POOLED] = values
        masked = values * mask
        sums_ref[0:8] += partial_sum(masked)
        sums_ref[8:16] += partial_sum(masked * values)


def clear_edges(grid, plane_ref):
    rows = grid.line_rows
    plane_ref[0:rows] = jnp.zeros((rows, POOLED), F32)
    plane_ref[grid.rows + rows : grid.rows + 2 * rows] = jnp.zeros((rows, POOLED), F32)


def first_pool(grid, slots, length_ref, place_ref, *refs):
    pools, refs = (refs[: slots.parts], refs[slots.parts :])
    e_sums_ref, q_ref, out_sums_ref, plane_ref, sums_ref = refs
    length = length_ref[0]
    rows = grid.line_rows
    for row in range(2):
        write_row(out_sums_ref, row, 0, SECOND, e_sums_ref[row : row + 1, :])
    clear_edges(grid, plane_ref)

    def visit(pair, ref, number):
        offset = ref[slots.rows : slots.rows + PITCH, :].astype(F32)[0:1]
        for line in range(2):
            at = rows_at(number * slots.pair_rows + line * rows, rows)
            plane_ref[rows_at((2 * pair + line + 1) * rows, rows), :] = plane_box(
                ref[at, :].astype(F32) + offset
            )

    each_pair(slots, place_ref[0], pools, visit)
    pool_planes(grid, plane_ref, q_ref, 0, sums_ref, length, box_window(grid.side, length))
    write_sums(out_sums_ref, sums_ref, SECOND, FIRST)


def normalize(values, center, inverse, gain, shift, mask):
    scaled = (values - center) * inverse
    shifted = gain * scaled + shift
    gate = sigmoid(shifted)
    gate_mask = gate * mask
    act = shifted * gate_mask
    return (scaled, act, gate_mask + act * (1.0 - gate))


def pool_pieces(matrix, pieces):
    return jnp.dot(
        matrix, jnp.concatenate(pieces, axis=0), preferred_element_type=F32
    ).astype(BF16)


def first_direct(grid, small, slots, block, length_ref, u_ref, gain_ref, shift_ref, *refs):
    sums, (pooled_ref, kept_ref, moment_ref) = (refs[: slots.parts], refs[slots.parts :])
    rows = grid.line_rows
    mask = frame_mask(rows, length_ref[0], DIRECT)
    center, inverse = set_moments(total_of(sums), moment_ref)
    center, inverse = (center[:, :DIRECT], inverse[:, :DIRECT])
    gain, shift = (gain_ref[block : block + 1, :DIRECT], shift_ref[block : block + 1, :DIRECT])
    matrix = pool_matrix(small.side, False)

    @pl.loop(0, slots.each)
    def _(number):
        acts, slopes, products = ([], [], [])
        for line in range(2):
            at = rows_at(number * slots.pair_rows + line * rows, rows)
            scaled, act, slope = normalize(u_ref[at, :], center, inverse, gain, shift, mask)
            kept_ref[at, 0:DIRECT] = scaled.astype(BF16)
            kept_ref[at, DIRECT : 2 * DIRECT] = slope.astype(BF16)
            acts.append(act.astype(BF16))
            slopes.append(slope.astype(BF16))
            products.append((slope * scaled).astype(BF16))
        size = small.line_rows
        pooled_ref[rows_at(number * size, size), :] = pool_pieces(matrix, acts)
        at = rows_at(slots.rows + number * size, size)
        kept_ref[at, 0:DIRECT] = pool_pieces(matrix, slopes)
        kept_ref[at, DIRECT : 2 * DIRECT] = pool_pieces(matrix, products)


def outer_moments(center, inverse, count, outer_ref):
    outer_ref[0:1, :] = center
    outer_ref[1:2, :] = inverse
    outer_ref[2:3, :] = jnp.concatenate([count[:, 0:128]] * (OUTER // 128), axis=1)


def first_output(grid, small, block, length_ref, q_far, e_far, moment_ref, sums_in_ref, gain_ref, shift_ref, *refs):
    pooled_ref, h_far, slope_far, outer_ref, pooled_slope_ref, pooled_product_ref, *refs = refs
    q_ref, e_ref, h_ref, slope_ref, q_sem, e_sem, h_sem, slope_sem = refs
    rows = grid.line_rows
    wide = 2 * rows
    pairs = grid.side // 2

    def arriving(pair, slot):
        at = rows_at(pair * wide, wide)
        return [
            pltpu.make_async_copy(q_far.at[at, :], q_ref.at[slot], q_sem.at[slot]),
            pltpu.make_async_copy(e_far.at[at, :], e_ref.at[slot], e_sem.at[slot]),
        ]

    def leaving(pair, slot):
        at = rows_at(pair * wide, wide)
        return [
            pltpu.make_async_copy(h_ref.at[slot], h_far.at[at, :], h_sem.at[slot]),
            pltpu.make_async_copy(slope_ref.at[slot], slope_far.at[at, :], slope_sem.at[slot]),
        ]

    for copy in arriving(0, 0):
        copy.start()
    mask = frame_mask(rows, length_ref[0], FIRST)
    total = total_of(sums_in_ref)
    count = jnp.concatenate([moment_ref[2:3, 0:128]] * (FIRST // 128), axis=1)
    center, inverse = moments(total[0:1], total[1:2], count)
    outer_moments(
        jnp.concatenate([moment_ref[0:1, :DIRECT], center], axis=1),
        jnp.concatenate([moment_ref[1:2, :DIRECT], inverse], axis=1),
        count,
        outer_ref,
    )
    matrix = pool_matrix(small.side, False)
    gain, shift = (gain_ref[block : block + 1, DIRECT:], shift_ref[block : block + 1, DIRECT:])

    @pl.loop(0, pairs)
    def _(pair):
        slot = lax.rem(pair, 2)

        @pl.when(pair + 1 < pairs)
        def _():
            for copy in arriving(pair + 1, 1 - slot):
                copy.start()

        for copy in arriving(pair, slot):
            copy.wait()

        @pl.when(pair >= 2)
        def _():
            for copy in leaving(pair - 2, slot):
                copy.wait()

        acts, slopes, products = ([], [], [])
        for number in range(2):
            lines = slice(number * rows, (number + 1) * rows)
            values = jnp.concatenate([e_ref[slot, lines, :], q_ref[slot, lines, :]], axis=1)
            scaled, act, slope = normalize(values, center, inverse, gain, shift, mask)
            h_ref[slot, lines, :] = scaled.astype(BF16)
            low_slope = slope.astype(BF16)
            slope_ref[slot, lines, :] = low_slope
            acts.append(act.astype(BF16))
            slopes.append(low_slope)
            products.append((slope * scaled).astype(BF16))
        for copy in leaving(pair, slot):
            copy.start()
        at = rows_at(pair * small.line_rows, small.line_rows)
        pooled_ref[at, :] = pool_pieces(matrix, acts)
        pooled_slope_ref[at, :] = pool_pieces(matrix, slopes)
        pooled_product_ref[at, :] = pool_pieces(matrix, products)

    for pair in range(max(pairs - 2, 0), pairs):
        for copy in leaving(pair, pair % 2):
            copy.wait()


def second_pointwise(grid, slots, length_ref, place_ref, count_ref, *refs):
    directs, refs = (refs[: slots.parts], refs[slots.parts :])
    rest_ref, p_ref, q_ref, out_sums_ref, x_ref, plane_ref, sums_ref, pool_sums_ref = refs
    length = length_ref[0]
    rows = grid.line_rows
    sums_ref[...] = jnp.zeros_like(sums_ref)
    clear_edges(grid, plane_ref)
    x_ref[:, DIRECT:] = rest_ref[...]

    def visit(pair, ref, number):
        x_ref[rows_at(pair * rows, rows), 0:DIRECT] = ref[number * rows : (number + 1) * rows, :]

    each_pair(slots, place_ref[0], directs, visit)
    q_ref[...] = lax.dot_general(
        x_ref[...], p_ref[...], (((1,), (1,)), ((), ())), preferred_element_type=F32
    )

    @pl.loop(0, grid.side)
    def _(line):
        values = q_ref[rows_at(line * rows, rows), :]
        sums_ref[0:8] += partial_sum(values[:, :SECOND])
        sums_ref[8:16] += partial_sum(values[:, :SECOND] * values[:, :SECOND])
        plane_ref[rows_at((line + 1) * rows, rows), :] = plane_box(values[:, SECOND:])

    pool_planes(grid, plane_ref, q_ref, SECOND, pool_sums_ref, length, box_window(grid.side, length))
    write_sums(out_sums_ref, sums_ref, 0, SECOND)
    write_sums(out_sums_ref, pool_sums_ref, SECOND, FIRST)
    write_row(out_sums_ref, 2, 0, FIRST, jnp.full((1, FIRST), count_ref[0], F32))


def second_convolve(grid, block, length_ref, q_ref, sums_in_ref, gain_ref, shift_ref, *refs):
    far_kernels, outputs, moment_ref, scratch = (refs[:3], refs[3:8], refs[8], refs[9:])
    length = length_ref[0]
    center, inverse = set_moments(total_of(sums_in_ref), moment_ref)
    center, inverse = (center[:, DIRECT:SECOND], inverse[:, DIRECT:SECOND])
    gain, shift = (gain_ref[block : block + 1], shift_ref[block : block + 1])
    mask = frame_mask(grid.line_rows, length, REDUCED)

    def fill(h_ref, mid_ref, small_ref):
        @pl.loop(0, grid.side)
        def _(line):
            at = rows_at(line * grid.line_rows, grid.line_rows)
            scaled = (q_ref[at, DIRECT:SECOND] - center) * inverse
            h_ref[at, :] = scaled.astype(BF16)
            act = silu(gain * scaled + shift) * mask
            store_taps(
                mid_ref, small_ref, rows_at(grid.lead + line * grid.pitch, grid.line_rows), act
            )

    run_convolution(grid, length, far_kernels, outputs, scratch, fill)


def second_output(grid, block, length_ref, q_ref, e_ref, moment_ref, sums_in_ref, gain_ref, shift_ref, cot_ref, act_ref, h_ref, error_ref, outer_ref, out_sums_ref, sums_ref):
    rows = grid.line_rows
    side, frames = (grid.side, cot_ref.shape[1])
    mask = frame_mask(rows, length_ref[0], OUTER)
    total = total_of(sums_in_ref)
    count = moment_ref[2:3, 0:SECOND]
    center, inverse = moments(total[0:1], total[1:2], count)
    center = jnp.concatenate([moment_ref[0:1, :DIRECT], center, moment_ref[0:1, SECOND:]], axis=1)
    inverse = jnp.concatenate([moment_ref[1:2, :DIRECT], inverse, moment_ref[1:2, SECOND:]], axis=1)
    outer_moments(center, inverse, count, outer_ref)
    sums_ref[...] = jnp.zeros_like(sums_ref)
    gain, shift = (gain_ref[block : block + 1], shift_ref[block : block + 1])
    gap = jnp.zeros((rows, 64), F32)
    unused = jnp.zeros((side, PITCH - frames, CHANNELS), F32)

    @pl.loop(0, side)
    def _(line):
        at = rows_at(line * rows, rows)
        places = pl.ds(line * side, side)
        values = jnp.concatenate([q_ref[at, :DIRECT], e_ref[at, :], q_ref[at, SECOND:]], axis=1)
        scaled = (values - center) * inverse
        h_ref[at, :] = scaled.astype(BF16)
        shifted = gain * scaled + shift
        gate = sigmoid(shifted)
        act = (shifted * gate * mask).reshape(side, PITCH, OUTER)[:, :frames].astype(BF16)
        act_ref[places, :, 0:576] = act[:, :, 0:576]
        act_ref[places, :, 576:CHANNELS] = act[:, :, 640:OUTER]
        slope = gate * (1.0 + shifted * (1.0 - gate))
        grad = jnp.concatenate([cot_ref[places].astype(F32), unused], axis=1)
        grad = grad.reshape(rows, CHANNELS)
        grad = jnp.concatenate([grad[:, :576], gap, grad[:, 576:]], axis=1)
        error = grad * slope * mask
        error_ref[at, :] = error.astype(BF16)
        sums_ref[0:8] += partial_sum(error)
        sums_ref[8:16] += partial_sum(error * scaled)

    write_sums(out_sums_ref, sums_ref, 0, OUTER)


def spread_matrix(grid, small):
    return None if small is None else pool_matrix(small.side, True)[: grid.line_rows]


def outer_error(slopes, small, grad_ref, matrix, line, lo, hi):
    values = slopes.astype(F32)
    if small is None:
        return values
    coarse = grad_ref[rows_at((line // 2) * small.line_rows, small.line_rows), lo:hi]
    return values * jnp.dot(matrix, coarse, preferred_element_type=F32)


class Lines:
    def __init__(self, grid, sources, buffers, sem_ref):
        self.step = 2 if grid.side % 2 == 0 else 1
        self.size = self.step * grid.line_rows
        self.steps = grid.side // self.step
        self.sources, self.buffers, self.sem = (sources, buffers, sem_ref)

    def copies(self, step):
        at = rows_at(step * self.size, self.size)
        copies = []
        for number, ((ref, lo, hi), (buffer, place)) in enumerate(zip(self.sources, self.buffers)):
            source = ref(step, lo, hi) if callable(ref) else ref.at[at, pl.ds(lo, hi - lo)]
            target = buffer.at[at, pl.ds(place, hi - lo)]
            copies.append(pltpu.make_async_copy(source, target, self.sem.at[number, step]))
        return copies

    def first(self):
        @pl.loop(0, self.steps)
        def _(step):
            for copy in self.copies(step):
                copy.start()

    def run(self, visit):
        @pl.loop(0, self.steps)
        def _(step):
            for copy in self.copies(step):
                copy.wait()
            visit(step)

    @staticmethod
    def semaphores(grid, count):
        return pltpu.SemaphoreType.DMA((count, grid.side // 2 if grid.side % 2 == 0 else grid.side))


def second_back(grid, small, block, slots, length_ref, first_ref, h_far, outer_ref, sums_in_ref, gain_ref, slope_far, *refs):
    first = small is not None
    (grad_ref, carried_ref), refs = (refs[:2], refs[2:]) if first else ((None, None), refs)
    mid_far, few_far, d_far, total_ref, out_ref, *refs = refs
    d_ref, h_ref, slope_ref, mid_ref, few_ref, mid_acc_ref, small_acc_ref, turned_ref, sem_ref, in_sem, out_sem = refs
    lo, hi = (DIRECT, DIRECT + SECOND)
    at = 0 if first else DIRECT
    lines = Lines(
        grid,
        ((h_far, at, at + SECOND), (slope_far, at, at + SECOND)),
        ((h_ref, 0), (slope_ref, 0)),
        sem_ref,
    )
    lines.first()
    arriving = copies((mid_far, few_far), (mid_ref, few_ref), in_sem)
    for copy in arriving:
        copy.start()
    total = total_of(sums_in_ref)
    total_ref[...] = total
    a, b, c = before_norm(
        gain_ref[block : block + 1, lo:hi], outer_ref[1:2, lo:hi], total[:, lo:hi], outer_ref[2:3, lo:hi]
    )
    mask = frame_mask(grid.line_rows, length_ref[0], SECOND)
    matrix = spread_matrix(grid, small)
    clear_empty(grid, d_ref)
    rows = grid.line_rows
    if first:
        share = out_ref.shape[1] - carried_ref.shape[1]
        for clip in range(out_ref.shape[0]):
            out_ref[clip, share:, :] = carried_ref[clip]

    def visit(step):
        for number in range(lines.step):
            line = step * lines.step + number
            here = rows_at(line * rows, rows)
            scaled = h_ref[here, :].astype(F32)
            error = outer_error(slope_ref[here, :], small, grad_ref, matrix, line, lo, hi)
            back = (a * error - b - c * scaled) * mask
            d_ref[rows_at(grid.lead + line * grid.pitch, rows), :] = back.astype(BF16)

    lines.run(visit)
    leaving = pltpu.make_async_copy(d_ref, d_far, out_sem.at[0])
    leaving.start()
    for copy in arriving:
        copy.wait()
    kernel_grads(grid, slots, first_ref, mid_ref, few_ref, d_ref, out_ref, mid_acc_ref, small_acc_ref, turned_ref)
    leaving.wait()


def before_norm(gain, inverse, sums, count):
    factor = gain * inverse
    return (factor, factor * sums[0:1] / count, factor * sums[1:2] / count)


def second_back_scratch(grid, slots):
    return [
        pltpu.VMEM((grid.padded, SECOND), BF16),
        pltpu.VMEM((grid.rows, SECOND), BF16),
        pltpu.VMEM((grid.rows, SECOND), BF16),
        pltpu.VMEM((grid.padded, 512), BF16),
        pltpu.VMEM((grid.padded, 128), BF16),
        pltpu.VMEM((slots, 384, 256), F32),
        pltpu.VMEM((slots, 128, 128), F32),
        pltpu.VMEM((MID_IN + 128, 128), F32),
        Lines.semaphores(grid, 2),
        pltpu.SemaphoreType.DMA((2,)),
        pltpu.SemaphoreType.DMA((1,)),
    ]


def conv_back(grid, slots, block, length_ref, d_ref, reduced_ref, reduced_gain_ref, reduced_shift_ref, *refs):
    far_kernels, refs = (refs[:3], refs[3:])
    first = len(refs) > 9
    (x_far, rest_product_ref), refs = (refs[:2], refs[2:]) if first else ((None, None), refs)
    r_ref, out_sums_ref, *refs = refs
    product_out, refs = (refs[0], refs[1:]) if first else (None, refs)
    kernels, (last_ref, acc_ref, sums_ref, in_sem, *refs) = (refs[:3], refs[3:])
    if first:
        x_ref, product_ref, x_sem = refs
        x_copy = pltpu.make_async_copy(x_far, x_ref, x_sem.at[0])
        x_copy.start()
    main_ref, rest_ref, small_ref = kernels
    arriving = copies(far_kernels, kernels, in_sem)
    for copy in arriving:
        copy.start()
    rows = grid.line_rows
    group_rows = grid.group * grid.pitch
    sums_ref[...] = jnp.zeros_like(sums_ref)
    mask = frame_mask(rows, length_ref[0], REDUCED)
    gain, shift = (reduced_gain_ref[block : block + 1], reduced_shift_ref[block : block + 1])
    turned = (((1,), (1,)), ((), ()))
    lane = lax.broadcasted_iota(jnp.int32, (rows, 128), 1)
    wide_lane = lax.broadcasted_iota(jnp.int32, (grid.pitch, 128), 1)

    @pl.loop(0, grid.side)
    def _(line):
        place = grid.lead + line * grid.pitch
        here = d_ref[rows_at(place, grid.pitch), 256:384].astype(F32)
        further = d_ref[rows_at(place + grid.pitch, grid.pitch), 256:384].astype(F32)
        at = rows_at(place, grid.pitch)
        last_ref[at, 0:128] = jnp.where(wide_lane < 64, further, pltpu.roll(here, 64, 1)).astype(
            BF16
        )
        last_ref[at, 128:256] = d_ref[rows_at(place - grid.pitch, grid.pitch), 256:384]

    last_ref[grid.lead - PITCH : grid.lead, :] = jnp.zeros((PITCH, 256), BF16)
    end = grid.lead + grid.side * grid.pitch
    last_ref[end : end + PITCH, :] = jnp.zeros((PITCH, 256), BF16)
    for copy in arriving:
        copy.wait()

    @pl.loop(0, grid.side // grid.group)
    def _(group):
        base = grid.lead + group * group_rows
        for tap in range(9):
            part = lax.dot_general(
                d_ref[rows_at(tap_start(grid, base, tap, -1), group_rows), 0:256],
                main_ref[tap],
                turned,
                preferred_element_type=F32,
            )
            acc_ref[:, 0:512] = part if tap == 0 else acc_ref[:, 0:512] + part
        for place in range(3):
            acc_ref[:, 0:512] += lax.dot_general(
                last_ref[rows_at(base - (place - 1) * PITCH, group_rows), :],
                rest_ref[place],
                turned,
                preferred_element_type=F32,
            )
        near = [
            d_ref[rows_at(tap_start(grid, base, tap, -1), group_rows), 384:512] for tap in range(9)
        ]
        acc_ref[:, 512:640] = jnp.dot(
            jnp.concatenate(near, axis=1), small_ref[...], preferred_element_type=F32
        )
        for number in range(grid.group):
            line = group * grid.group + number
            lines = slice(number * grid.pitch, number * grid.pitch + rows)
            rest, small = (acc_ref[lines, 384:512], acc_ref[lines, 512:640])
            one = jnp.where(lane < 32, rest, pltpu.roll(small, 32, 1))
            two = jnp.where(lane < 32, pltpu.roll(rest, 96, 1), small)
            three = jnp.where(lane < 32, pltpu.roll(rest, 64, 1), pltpu.roll(small, 96, 1))
            wide = later(acc_ref[lines, 0:128]) + acc_ref[lines, 128:256]
            wide = wide + earlier(acc_ref[lines, 256:384])
            narrow = jnp.where(lane < 64, later(one) + two + earlier(three), 0.0)
            back = jnp.concatenate([wide, narrow], axis=1)
            at = rows_at(line * rows, rows)
            scaled = reduced_ref[at, :].astype(F32)
            error = back * silu_slope(gain * scaled + shift) * mask
            r_ref[at, :] = error.astype(BF16)
            sums_ref[0:8] += partial_sum(error)
            sums_ref[8:16] += partial_sum(error * scaled)

    write_sums(out_sums_ref, sums_ref, 0, REDUCED)
    if first:
        x_copy.wait()
        ones = frame_mask(slots.rows, length_ref[0])
        low_ones = ones.astype(BF16)
        two_ones = jnp.concatenate([ones, ones], axis=1)

        def right_of(start, size):
            at = slice(start, start + size)
            scaled = (reduced_ref[at, :].astype(F32) * two_ones).astype(BF16)
            return jnp.concatenate([r_ref[at, :], scaled, low_ones], axis=1)

        channels = x_ref.shape[1]
        product_ref[0:channels, :] = channel_products(slots, x_ref, right_of)
        product_ref[channels:, :] = jnp.zeros((product_ref.shape[0] - channels, FIRST), F32)
        clips, _, size, _ = product_out.shape
        for clip in range(clips):
            at = slice(clip * size, (clip + 1) * size)
            for tile in range(3):
                product_out[clip, tile] = rest_product_ref[at, 128 * tile : 128 * (tile + 1)]
            for tile in range(5):
                product_out[clip, 3 + tile] = product_ref[at, 128 * tile : 128 * (tile + 1)]


def kernel_grads(grid, slots, first_ref, mid_ref, small_ref, d_ref, out_ref, mid_acc_ref, small_acc_ref, turned_ref):
    group_rows = grid.group * grid.pitch
    mid_acc_ref[...] = jnp.zeros_like(mid_acc_ref)
    small_acc_ref[...] = jnp.zeros_like(small_acc_ref)

    def neighbour(slot):
        return jnp.minimum(first_ref[0] + slot, TAPS - 1) // 9

    @pl.loop(0, grid.side // grid.group)
    def _(group):
        base = grid.lead + group * group_rows
        left = d_ref[rows_at(base, group_rows), :].T
        for slot in range(slots):
            tap = lax.rem(jnp.minimum(first_ref[0] + slot, TAPS - 1), 9)
            at = rows_at(
                base + (tap // 3 - 1) * grid.pitch + (lax.rem(tap, 3) - 1) * PITCH, group_rows
            )
            lanes = pl.ds(pl.multiple_of(neighbour(slot) * 128, 128), 128)
            right = jnp.concatenate([mid_ref[at, lanes], mid_ref[at, 384:512]], axis=1)
            mid_acc_ref[slot] += jnp.dot(left[0:384], right, preferred_element_type=F32)
            small_acc_ref[slot] += jnp.dot(
                left[384:512], small_ref[at, :], preferred_element_type=F32
            )

    share = round_up(slots * TAP_ROWS, 16 * out_ref.shape[0]) // out_ref.shape[0]

    def put(start, values):
        done = 0
        while done < values.shape[0]:
            clip, at = divmod(start + done, share)
            size = min(values.shape[0] - done, share - at)
            out_ref[clip, at : at + size, :] = values[done : done + size].astype(BF16)
            done = done + size

    half = MID_IN // 2
    for slot in range(slots):
        base = slot * TAP_ROWS
        rest = pl.ds(pl.multiple_of(neighbour(slot) * 32, 32), 32)
        for tile in range(3):
            lines = slice(128 * tile, 128 * (tile + 1))
            turned_ref[0:128, :] = mid_acc_ref[slot, lines, 0:128].T
            turned_ref[MID_IN : MID_IN + 128, :] = mid_acc_ref[slot, lines, 128:256].T
            turned_ref[128:MID_IN, :] = turned_ref[
                pl.ds(pl.multiple_of(MID_IN + neighbour(slot) * 32, 32), 32), :
            ]
            if tile < 2:
                put(base + MID_IN * tile, turned_ref[0:MID_IN, :])
            else:
                folded = turned_ref[0:half, :] + pltpu.roll(turned_ref[half:MID_IN, :], 64, 1)
                put(base + 2 * MID_IN, folded)
        turned_ref[0:128, :] = small_acc_ref[slot].T
        put(base + 2 * MID_IN + half, turned_ref[rest, :])
    used = slots * TAP_ROWS
    put(used, jnp.zeros((share * out_ref.shape[0] - used, 128), F32))


class Spread:
    def __init__(self, grid, plane_ref, across_ref, scale_ref, length):
        self.grid, self.plane, self.across, self.scale = (grid, plane_ref, across_ref, scale_ref)
        clear_edges(grid, plane_ref)
        window = box_window(grid.side, length)
        scale_ref[0] = box_scale(0, grid.side, window)
        scale_ref[1] = box_scale(1, grid.side, window)
        edge = jnp.zeros((PITCH, POOLED), F32)
        across_ref[0:PITCH, :] = edge
        across_ref[PITCH + grid.line_rows :, :] = edge

    def put(self, line, values):
        rows = self.grid.line_rows
        inner = jnp.where((line == 0) | (line == self.grid.side - 1), 0, 1)
        values = values * self.scale[inner]
        across = self.across
        across[PITCH : PITCH + rows, :] = values + earlier(values) + later(values)
        self.plane[rows_at((line + 1) * rows, rows), :] = (
            across[0:rows, :] + across[PITCH : PITCH + rows, :] + across[2 * PITCH :, :]
        )

    def get(self, start, size):
        rows = self.grid.line_rows
        return (
            self.plane[rows_at(start, size), :]
            + self.plane[rows_at(start + rows, size), :]
            + self.plane[rows_at(start + 2 * rows, size), :]
        )

    @staticmethod
    def scratch(grid):
        return [
            pltpu.VMEM((grid.rows + 2 * grid.line_rows, POOLED), F32),
            pltpu.VMEM((grid.line_rows + 2 * PITCH, POOLED), F32),
            pltpu.VMEM((2, grid.line_rows, POOLED), F32),
        ]


def channel_products(slots, x_ref, right_of):
    total = None
    for part in range(slots.parts):
        slot = part * slots.each
        pair = slot - (slots.empty if slot >= slots.gap + slots.empty else 0)
        pair = min(pair, slots.pairs - slots.each)
        product = jnp.dot(
            x_ref[part], right_of(pair * slots.pair_rows, slots.rows), preferred_element_type=F32
        )
        total = product if total is None else total + product
    return total


def rest_constants(outer_ref, total_ref, gain_ref, block):
    pool = OUTER - POOLED

    def pick(ref, lo, hi):
        return jnp.concatenate([ref[lo:hi, 0:DIRECT], ref[lo:hi, pool:]], axis=1)

    return before_norm(
        pick(gain_ref, block, block + 1), pick(outer_ref, 1, 2), pick(total_ref, 0, 2), pick(outer_ref, 2, 3)
    )


def point_back(grid, slots, block, kept, length_ref, place_ref, h_far, outer_ref, total_ref, gain_ref, error_far, reduced_far, r_far, moment_ref, sums_in_ref, reduced_gain_ref, x_far, p_far, *refs):
    pooled_slope_in, pooled_product_in, kept_far, *refs = refs
    dx_ref, dp_ref, reduced_total_ref, outer_sums_ref, *refs = refs
    h_ref, error_ref, reduced_ref, r_ref, x_ref, p_ref, du_ref, acc_ref, *refs = refs
    plane_ref, across_ref, scale_ref, sums_ref, pooled_slope_ref, pooled_product_ref, kept_ref, *refs = refs
    sem_ref, in_sem = refs
    rows = grid.line_rows
    pool = OUTER - POOLED
    lines = Lines(
        grid,
        (
            (h_far, 0, DIRECT),
            (h_far, pool, OUTER),
            (error_far, 0, DIRECT),
            (error_far, pool, OUTER),
            (reduced_far, 0, REDUCED),
            (r_far, 0, REDUCED),
        ),
        ((h_ref, 0), (h_ref, DIRECT), (error_ref, 0), (error_ref, DIRECT), (reduced_ref, 0), (r_ref, 0)),
        sem_ref,
    )
    lines.first()
    kept_rows = kept_ref.shape[1]
    arriving = copies(
        (x_far, p_far, kept_far.at[:, pl.ds(slots.rows, kept_rows), :]), (x_ref, p_ref, kept_ref), in_sem
    )
    for copy in arriving:
        copy.start()
    length = length_ref[0]
    total = total_of(sums_in_ref)
    reduced_total_ref[...] = total
    mid = before_norm(
        reduced_gain_ref[block : block + 1],
        moment_ref[1:2, DIRECT:SECOND],
        total,
        outer_ref[2:3, 0:REDUCED],
    )
    rest = rest_constants(outer_ref, total_ref, gain_ref, block)
    mask = frame_mask(rows, length, DIRECT + POOLED)
    spread = Spread(grid, plane_ref, across_ref, scale_ref, length)

    def visit(line):
        at = rows_at(line * rows, rows)
        back = rest[0] * error_ref[at, :].astype(F32) - rest[1] - rest[2] * h_ref[at, :].astype(F32)
        back = back * mask
        du_ref[at, 0:DIRECT] = back[:, :DIRECT].astype(BF16)
        spread.put(line, back[:, DIRECT:])
        back = mid[0] * r_ref[at, :].astype(F32) - mid[1] - mid[2] * reduced_ref[at, :].astype(F32)
        du_ref[at, DIRECT:SECOND] = (back * mask[:, :REDUCED]).astype(BF16)

    lines.run(visit)
    for copy in arriving:
        copy.wait()
    sums_ref[...] = jnp.zeros_like(sums_ref)
    pooled_slope_ref[:, DIRECT:] = pooled_slope_in[...]
    pooled_product_ref[:, DIRECT:] = pooled_product_in[...]
    for pair in range(slots.pairs):
        slot = pair + (slots.empty if pair >= slots.gap else 0)
        at = slice(pair * rows, (pair + 1) * rows)
        start = slot % slots.each * rows
        values = kept_ref[slot // slots.each, start : start + rows, :]
        pooled_slope_ref[at, 0:DIRECT] = values[:, :DIRECT]
        pooled_product_ref[at, 0:DIRECT] = values[:, DIRECT:]

    @pl.loop(0, grid.side)
    def _(line):
        at = rows_at(line * rows, rows)
        du_ref[at, SECOND:] = (spread.get(line * rows, rows) * mask[:, :POOLED]).astype(BF16)
        dx = jnp.dot(du_ref[at, :], p_ref[...], preferred_element_type=F32).astype(BF16)
        dx_ref[at, :] = dx
        for number, ref in enumerate((pooled_slope_ref, pooled_product_ref)):
            sums_ref[8 * number : 8 * number + 8] += partial_sum(
                dx.astype(F32) * ref[at, :].astype(F32)
            )

    write_sums(outer_sums_ref, sums_ref, 0, OUTER)
    acc_ref[...] = lax.dot_general(
        x_ref[...], du_ref[...], (((0,), (0,)), ((), ())), preferred_element_type=F32
    )
    start = pl.multiple_of(place_ref[0] * kept, 16) if kept < acc_ref.shape[0] else 0
    clips, size, _ = dp_ref.shape
    for tile in range(FIRST // 128):
        values = acc_ref[pl.ds(start, kept), 128 * tile : 128 * (tile + 1)].astype(BF16)
        done = 0
        while done < kept:
            clip, at = divmod(kept * tile + done, size)
            few = min(kept - done, size - at)
            dp_ref[clip, at : at + few, :] = values[done : done + few]
            done = done + few
    used = (FIRST // 128) * kept
    while used < clips * size:
        clip, at = divmod(used, size)
        dp_ref[clip, at:, :] = jnp.zeros((size - at, 128), BF16)
        used = used + size - at


def rest_back(grid, small, slots, block, length_ref, outer_ref, total_ref, gain_ref, grad_ref, h_far, slope_far, kept_far, x_far, du_far, product_ref, *refs):
    h_ref, slope_ref, x_ref, du_ref, plane_ref, across_ref, scale_ref, sem_ref, x_sem, du_sem = refs
    rows = grid.line_rows
    pool = OUTER - POOLED

    def direct(step, lo, hi):
        slot = slots.slot_of(step)
        at = rows_at(lax.rem(slot, slots.each) * slots.pair_rows, slots.pair_rows)
        return kept_far.at[slot // slots.each, at, pl.ds(lo, hi - lo)]

    lines = Lines(
        grid,
        (
            (direct, 0, DIRECT),
            (h_far, SECOND, FIRST),
            (direct, DIRECT, 2 * DIRECT),
            (slope_far, SECOND, FIRST),
        ),
        ((h_ref, 0), (h_ref, DIRECT), (slope_ref, 0), (slope_ref, DIRECT)),
        sem_ref,
    )
    lines.first()
    x_copy = pltpu.make_async_copy(x_far, x_ref, x_sem.at[0])
    x_copy.start()
    length = length_ref[0]
    matrix = spread_matrix(grid, small)
    a, b, c = rest_constants(outer_ref, total_ref, gain_ref, block)
    mask = frame_mask(rows, length, DIRECT + POOLED)
    spread = Spread(grid, plane_ref, across_ref, scale_ref, length)

    def visit(step):
        for number in range(lines.step):
            line = step * lines.step + number
            at = rows_at(line * rows, rows)
            coarse = grad_ref[rows_at((line // 2) * small.line_rows, small.line_rows), :]
            grad = jnp.dot(
                matrix,
                jnp.concatenate([coarse[:, :DIRECT], coarse[:, pool:]], axis=1),
                preferred_element_type=F32,
            )
            back = a * (grad * slope_ref[at, :].astype(F32)) - b - c * h_ref[at, :].astype(F32)
            back = back * mask
            du_ref[at, 0:DIRECT] = back[:, :DIRECT].astype(BF16)
            spread.put(line, back[:, DIRECT:])

    lines.run(visit)
    x_copy.wait()
    wide = lines.size
    pool_mask = frame_mask(wide, length)

    def leaving(step):
        at = rows_at(step * wide, wide)
        return pltpu.make_async_copy(du_ref.at[at, :], du_far.at[at, :], du_sem.at[0])

    @pl.loop(0, lines.steps)
    def _(step):
        at = rows_at(step * wide, wide)
        du_ref[at, DIRECT:] = (spread.get(step * wide, wide) * pool_mask).astype(BF16)
        leaving(step).start()

    channels = x_ref.shape[1]
    product_ref[0:channels, :] = channel_products(
        slots, x_ref, lambda start, size: du_ref[start : start + size, :]
    )
    product_ref[channels:, :] = jnp.zeros((product_ref.shape[0] - channels, DIRECT + POOLED), F32)
    pltpu.make_async_copy(du_ref, du_far, du_sem.at[0]).wait()


def mid_back(grid, block, length_ref, place_ref, moment_ref, sums_in_ref, gain_ref, du_far, h_far, r_far, p_far, dx_far, total_ref, *refs):
    du_ref, h_ref, r_ref, p_ref, dx_ref, sem_ref, p_sem, dx_sem = refs
    lines = Lines(
        grid,
        ((du_far, 0, DIRECT + POOLED), (h_far, 0, REDUCED), (r_far, 0, REDUCED)),
        ((du_ref, 0), (h_ref, 0), (r_ref, 0)),
        sem_ref,
    )
    lines.first()
    p_copy = pltpu.make_async_copy(p_far.at[place_ref[0]], p_ref, p_sem.at[0])
    p_copy.start()
    total = total_of(sums_in_ref)
    total_ref[...] = total
    a, b, c = before_norm(
        gain_ref[block : block + 1], moment_ref[1:2, DIRECT:], total, moment_ref[2:3, DIRECT:]
    )
    mask = frame_mask(lines.size, length_ref[0], REDUCED)
    p_copy.wait()

    def leaving(step):
        at = rows_at(step * lines.size, lines.size)
        return pltpu.make_async_copy(dx_ref.at[at, :], dx_far.at[at, :], dx_sem.at[0])

    def visit(step):
        at = rows_at(step * lines.size, lines.size)
        back = a * r_ref[at, :].astype(F32) - b - c * h_ref[at, :].astype(F32)
        du = jnp.concatenate(
            [du_ref[at, :DIRECT], (back * mask).astype(BF16), du_ref[at, DIRECT:]], axis=1
        )
        dx_ref[at, :] = jnp.dot(du, p_ref[...], preferred_element_type=F32).astype(BF16)
        leaving(step).start()

    lines.run(visit)
    pltpu.make_async_copy(dx_ref, dx_far, dx_sem.at[0]).wait()


def combine(block, pieces_ref, moment_ref, sums_in_ref, gain_ref, out_ref):
    total = total_of(sums_in_ref)
    a, b, c = before_norm(
        gain_ref[block : block + 1], moment_ref[1:2, DIRECT:], total, moment_ref[2:3, DIRECT:]
    )
    size = out_ref.shape[0] // 5
    products = total_of(pieces_ref)
    for tile in range(2):
        out_ref[size * tile : size * (tile + 1), :] = products[tile].astype(BF16)
        lanes = slice(128 * tile, 128 * (tile + 1))
        mid = a[:, lanes] * products[3 + tile] - b[:, lanes] * products[7] - c[:, lanes] * products[5 + tile]
        out_ref[size * (2 + tile) : size * (3 + tile), :] = mid.astype(BF16)
    out_ref[4 * size :, :] = products[2].astype(BF16)


def write_taps(read, slots, mid_ref, small_ref, mid_out, small_out, sem_ref):
    half = MID_IN // 2

    def leaving(tap):
        return (
            pltpu.make_async_copy(mid_ref.at[tap], mid_out.at[tap], sem_ref.at[0]),
            pltpu.make_async_copy(small_ref.at[tap], small_out.at[tap], sem_ref.at[1]),
        )

    for tap in range(TAPS):
        part, slot = divmod(tap, slots)
        base = slot * TAP_ROWS
        folded = read(part, base + 2 * MID_IN, half)
        mid_ref[tap, :, 0:128] = read(part, base, MID_IN)
        mid_ref[tap, :, 128:256] = read(part, base + MID_IN, MID_IN)
        mid_ref[tap, 0:half, 256:320] = folded[:, 0:64]
        mid_ref[tap, half:MID_IN, 256:320] = pltpu.roll(folded, 64, 1)[:, 0:64]
        small_ref[tap] = read(part, base + 2 * MID_IN + half, SMALL_IN)
        for copy in leaving(tap):
            copy.start()
    pltpu.make_async_copy(mid_ref, mid_out, sem_ref.at[0]).wait()
    pltpu.make_async_copy(small_ref, small_out, sem_ref.at[1]).wait()


def write_point(read, parts, kept, point_ref, wide_ref):
    for tile in range(FIRST // 128):
        for part in range(parts):
            start, stop = (kept * part, kept * (part + 1))
            values = read(part, kept * tile, kept)
            if kept * parts == CHANNELS:
                wide_ref[start:stop, :] = values
                continue
            for lo, hi, moved in ((0, 576, 0), (640, OUTER, 64)):
                lo, hi = (max(lo, start), min(hi, stop))
                if lo < hi:
                    wide_ref[lo - moved : hi - moved, :] = values[lo - start : hi - start]
        turned = wide_ref[...].T
        if tile < 3:
            point_ref[128 * tile : 128 * (tile + 1), :] = turned
        elif tile == 3:
            point_ref[384:448, :] = turned[0:64]
        else:
            point_ref[448:576, :] = turned


def copy_out(pairs, sem_ref):
    copies = [
        pltpu.make_async_copy(source, target, sem_ref.at[number])
        for number, (source, target) in enumerate(pairs)
    ]
    for copy in copies:
        copy.start()
    for copy in copies:
        copy.wait()


def share_reader(ref, clips, lo, share):
    def read(part, start, size):
        pieces, done = ([], 0)
        while done < size:
            clip, at = divmod(start + done, share)
            few = min(size - done, share - at)
            pieces.append(ref[part * clips + clip, lo + at : lo + at + few, :].astype(F32))
            done = done + few
        return pieces[0] if len(pieces) == 1 else jnp.concatenate(pieces, axis=0)

    return read


def unpack_second(clips, slots, shares_ref, mid_out, small_out, mid_ref, small_ref, sem_ref):
    read = share_reader(shares_ref, clips, 0, shares_ref.shape[1])
    write_taps(read, slots, mid_ref, small_ref, mid_out.at[1], small_out.at[1], sem_ref)


def unpack_first(parts, clips, slots, share, shares_ref, *refs):
    totals, refs = (refs[:4], refs[4:])
    mid_in, small_in, mid_out, small_out, point_out, gain_out, shift_out, *refs = refs
    mid_ref, small_ref, point_ref, wide_ref, sem_ref = refs
    for block in range(2):
        outer_ref, reduced_ref = totals[2 * block : 2 * block + 2]
        for row, out in enumerate((shift_out, gain_out)):
            at, line = (slice(block, block + 1), slice(row, row + 1))
            out[at, 0:256] = outer_ref[line, 0:256]
            out[at, 256:448] = reduced_ref[line, 0:192]
            out[at, 448:576] = outer_ref[line, 768:896]
            out[at, 576:896] = outer_ref[line, 256:576]
            out[at, 896:1024] = outer_ref[line, 640:768]
    read = share_reader(shares_ref, clips, share, shares_ref.shape[1] - share)
    write_point(read, parts, OUTER // parts, point_ref, wide_ref)
    last = pltpu.make_async_copy(point_ref, point_out.at[1], sem_ref.at[2])
    last.start()
    read = share_reader(shares_ref, clips, 0, share)
    write_taps(read, slots, mid_ref, small_ref, mid_out.at[0], small_out.at[0], sem_ref)
    last.wait()


def unpack_point(parts, clips, kept, place_ref, clip_ref, mine_ref, other_ref, point_in, point_out, buffer_ref, point_ref, wide_ref, sem_ref):
    tiles = FIRST // 128
    size = buffer_ref.shape[2] // clips
    for chip in range(clips // 2):
        for step in range(parts):
            part = lax.rem(place_ref[0] - step + parts, parts)
            for swapped, ref in enumerate((mine_ref, other_ref)):
                owner = clip_ref[0] ^ (2 * chip) ^ swapped
                source = (chip * parts + step) * tiles * size
                for tile in range(tiles):
                    buffer_ref[part, tile, rows_at(owner * size, size), :] = ref[
                        source + tile * size : source + (tile + 1) * size, :
                    ]

    def read(part, start, size):
        tile, at = divmod(start, kept)
        return buffer_ref[part, tile, at : at + size, :].astype(F32)

    write_point(read, parts, kept, point_ref, wide_ref)
    last = pltpu.make_async_copy(point_ref, point_out.at[0], sem_ref.at[0])
    last.start()
    last.wait()


def prepare(parts, mid_in, small_in, point_in, gain_in, shift_in, *refs):
    kernels, (point_ref, second_ref, *vectors) = (refs[:8], refs[8:14])
    for block in range(2):
        main_ref, last_ref, few_ref, back_ref = kernels[4 * block : 4 * block + 4]

        @pl.loop(0, 9)
        def _(tap):
            for number in range(3):
                source = 9 * number + tap
                main_ref[tap, 128 * number : 128 * (number + 1), :] = mid_in[block, source, 0:128, 0:256]
                main_ref[tap, 384 + 32 * number : 416 + 32 * number, :] = mid_in[
                    block, source, 128:MID_IN, 0:256
                ]
            main_ref[tap, 480:512, :] = jnp.zeros((32, 256), BF16)
            small = jnp.concatenate(
                [small_in[block, 9 * number + tap] for number in range(3)]
                + [jnp.zeros((32, 128), BF16)],
                axis=0,
            )
            at = pl.ds(pl.multiple_of(tap * 128, 128), 128)
            few_ref[at, :] = small
            back_ref[at, :] = small.astype(F32).T.astype(BF16)

        @pl.loop(0, 3)
        def _(place):
            for number in range(3):
                for rows, start, size in (
                    (slice(0, 128), 128 * number, 128),
                    (slice(128, MID_IN), 384 + 32 * number, 32),
                ):
                    pieces = [
                        mid_in[block, 9 * number + 3 * line + place, rows, 256:MID_OUT].astype(F32)
                        for line in range(3)
                    ]
                    pieces.append(jnp.zeros((size, 64), F32))
                    last_ref[place, start : start + size, :] = jnp.concatenate(
                        pieces, axis=1
                    ).astype(BF16)
            last_ref[place, 480:512, :] = jnp.zeros((32, 256), BF16)

    own = point_ref.shape[2]
    for lo, hi, at in ((0, 448, 0), (448, SQUEEZED, SECOND)):
        values = point_in[0, lo:hi, :].astype(F32)
        for part in range(parts):
            point_ref[part, at : at + hi - lo, :] = values[:, own * part : own * (part + 1)].astype(
                BF16
            )
        values = point_in[1, lo:hi, :].astype(F32)
        gap = jnp.zeros((hi - lo, 64), F32)
        second_ref[at : at + hi - lo, :] = jnp.concatenate(
            [values[:, :576], gap, values[:, 576:]], axis=1
        ).astype(BF16)
    for part in range(parts):
        point_ref[part, 448:SECOND, :] = jnp.zeros((64, own), BF16)
    second_ref[448:SECOND, :] = jnp.zeros((64, OUTER), BF16)
    for source, outer, reduced in ((gain_in, vectors[0], vectors[1]), (shift_in, vectors[2], vectors[3])):
        outer[:, 0:256] = source[:, 0:256]
        outer[:, 256:576] = source[:, 576:896]
        outer[:, 576:640] = jnp.zeros((2, 64), F32)
        outer[:, 640:768] = source[:, 896:1024]
        outer[:, 768:896] = source[:, 448:576]
        reduced[:, 0:192] = source[:, 256:448]
        reduced[:, 192:256] = jnp.zeros((2, 64), F32)


def round_up(value, unit):
    return -(-value // unit) * unit


def spread_over(values, axis, size):
    received = [values]
    for step in range(1, size):
        perm = [(source, (source + step) % size) for source in range(size)]
        received.append(lax.ppermute(values, axis, perm))
    return received


def after(values, earlier):
    return lax.optimization_barrier((values, earlier))[0]


def exchange(values):
    return lax.all_to_all(values, "dp", 0, 0, tiled=True)


def summed(pieces):
    pieces = exchange(pieces)
    return jnp.sum(pieces.astype(F32), axis=0).astype(BF16)


def gather_chips(column, clips, work=None):
    columns = [column]
    for chip in range(1, clips // 2):
        perm = [(source, source ^ (2 * chip)) for source in range(clips)]
        columns.append(lax.ppermute(column, "dp", perm))
    if work is not None:
        columns = after(columns, work)
    mine = jnp.concatenate(columns, axis=0)
    other = lax.ppermute(mine, "dp", [(source, source ^ 1) for source in range(clips)])
    return (mine, other)


def on_device(frames, lengths, cotangent, pointwise, conv_mid, conv_small, gains, shifts):
    parts = lax.axis_size("branch")
    clips = lax.axis_size("dp")
    place = lax.axis_index("branch").astype(jnp.int32)
    side = frames.shape[2]
    grid, small = (Grid(side), Grid(side // 2))
    slots = Slots(grid, parts)
    cells = side * side
    own_channels = frames.shape[-1]
    length = lengths.astype(jnp.int32)
    half_length = length // 2
    place_one = place.reshape(1)

    own = frames[0].transpose(1, 2, 0, 3).reshape(grid.rows, own_channels)
    turned = call(functools.partial(turn, slots), shape((parts, own_channels, slots.rows), BF16))(own)
    by_pairs = lax.all_to_all(turned, "branch", 0, 0, tiled=True)
    kernel_shapes = (
        shape((9, 512, 256), BF16),
        shape((3, 512, 256), BF16),
        shape((1152, 128), BF16),
        shape((1152, 128), BF16),
    )
    prepared = call(
        functools.partial(prepare, parts),
        (
            *kernel_shapes,
            *kernel_shapes,
            shape((parts, FIRST, own_channels), BF16),
            shape((FIRST, OUTER), BF16),
            shape((2, OUTER), F32),
            shape((2, REDUCED), F32),
            shape((2, OUTER), F32),
            shape((2, REDUCED), F32),
        ),
    )(conv_mid, conv_small, pointwise.swapaxes(1, 2), gains, shifts)
    kernels = (prepared[0:4], prepared[4:8])
    point_first, point_second, outer_gain, reduced_gain, outer_shift, reduced_shift = prepared[8:]

    local_count = (length * (slots.held(place) * 2 * side)).astype(F32)
    mid, pool, direct, sums = call(
        functools.partial(first_pointwise, slots),
        (
            shape((mid_rows(slots), 128), BF16),
            shape((slots.rows + PITCH, POOLED), BF16),
            shape((slots.rows, DIRECT), F32),
            shape((clips, 3, SECOND), F32),
        ),
        [pltpu.VMEM((slots.rows, FIRST), F32)],
        scalars=2,
    )(length, local_count, by_pairs, point_first)
    mids = spread_over(mid, "branch", parts)
    sums = spread_over(jnp.sum(exchange(sums), axis=0), "branch", parts)
    pooled_direct, kept_direct, moment = call(
        functools.partial(first_direct, grid, small, slots, 0),
        (
            shape((slots.each * small.line_rows, DIRECT), BF16),
            shape((slots.rows + slots.each * small.line_rows, 2 * DIRECT), BF16),
            shape((3, SECOND), F32),
        ),
        scalars=1,
        cost=3,
    )(length, direct, outer_gain, outer_shift, *sums)
    pool, pooled_direct = after((pool, pooled_direct), mids)
    pools = spread_over(pool, "branch", parts)
    h_reduced, taps_mid, taps_few, e, e_sums = call(
        functools.partial(first_convolve, grid, slots, 0),
        conv_outputs(grid),
        conv_scratch(grid),
        scalars=2,
        cost=40,
        far=range(5 + parts, 8 + parts),
        far_out=range(4),
    )(length, place_one, *mids, moment, reduced_gain, reduced_shift, *kernels[0][:3])
    pooled_directs = spread_over(after(pooled_direct, (pools, e_sums)), "branch", parts)
    kept_direct = lax.all_gather(after(kept_direct, pooled_directs), "branch", axis=0)
    q_pool, second_sums = call(
        functools.partial(first_pool, grid, slots),
        (shape((grid.rows, POOLED), F32), shape((clips, 2, FIRST), F32)),
        [
            pltpu.VMEM((grid.rows + 2 * grid.line_rows, POOLED), F32),
            pltpu.VMEM((16, POOLED), F32),
        ],
        scalars=2,
    )(length, place_one, *pools, e_sums)
    second_sums = exchange(second_sums)
    pair = 2 * grid.line_rows
    pooled, h_outer, slope, outer, pooled_slope, pooled_product = call(
        functools.partial(first_output, grid, small, 0),
        (
            shape((small.rows, FIRST), BF16),
            shape((grid.rows, FIRST), BF16),
            shape((grid.rows, FIRST), BF16),
            shape((3, OUTER), F32),
            shape((small.rows, FIRST), BF16),
            shape((small.rows, FIRST), BF16),
        ),
        [
            pltpu.VMEM((2, pair, POOLED), F32),
            pltpu.VMEM((2, pair, SECOND), F32),
            pltpu.VMEM((2, pair, FIRST), BF16),
            pltpu.VMEM((2, pair, FIRST), BF16),
            *[pltpu.SemaphoreType.DMA((2,))] * 4,
        ],
        scalars=1,
        far=(1, 2),
        far_out=(1, 2),
    )(
        length,
        q_pool,
        e,
        moment,
        second_sums,
        outer_gain,
        outer_shift,
    )

    small_count = half_length.astype(F32) * float(small.side * small.side)
    q_small, sums_small, pooled = call(
        functools.partial(second_pointwise, small, slots),
        (
            shape((small.rows, FIRST), F32),
            shape((clips, 3, FIRST), F32),
            shape((small.rows, OUTER), BF16),
        ),
        [
            pltpu.VMEM((small.rows + 2 * small.line_rows, POOLED), F32),
            pltpu.VMEM((16, SECOND), F32),
            pltpu.VMEM((16, POOLED), F32),
        ],
        scalars=3,
    )(half_length, place_one, small_count, *pooled_directs, pooled, point_second)
    sums_small = exchange(sums_small)
    h_reduced_small, taps_mid_small, taps_few_small, e_small, e_sums_small, moment_small = call(
        functools.partial(second_convolve, small, 1),
        (*conv_outputs(small, clips), shape((3, FIRST), F32)),
        conv_scratch(small),
        scalars=1,
        far=range(5, 8),
        far_out=range(4),
    )(half_length, q_small, sums_small, reduced_gain, reduced_shift, *kernels[1][:3])
    e_sums_small = exchange(e_sums_small)
    cot = cotangent[0].transpose(1, 2, 0, 3).reshape(small.side**2, cotangent.shape[1], CHANNELS)
    act, h_outer_small, error_small, outer_small, outer_sums_small = call(
        functools.partial(second_output, small, 1),
        (
            shape(cot.shape, BF16),
            shape((small.rows, OUTER), BF16),
            shape((small.rows, OUTER), BF16),
            shape((3, OUTER), F32),
            shape((clips, 2, OUTER), F32),
        ),
        [pltpu.VMEM((16, OUTER), F32)],
        scalars=1,
    )(half_length, q_small, e_small, moment_small, e_sums_small, outer_gain, outer_shift, cot)

    taps_each = -(-TAPS // parts)
    tap_share = round_up(taps_each * TAP_ROWS, 16 * clips) // clips
    first_tap = place_one * taps_each

    def conv_back_scratch(at):
        return [
            pltpu.VMEM((9, 512, 256), BF16),
            pltpu.VMEM((3, 512, 256), BF16),
            pltpu.VMEM((1152, 128), BF16),
            pltpu.VMEM((at.padded, 256), BF16),
            pltpu.VMEM((at.group * at.pitch, FIRST), F32),
            pltpu.VMEM((16, REDUCED), F32),
            pltpu.SemaphoreType.DMA((3,)),
        ]

    gathered = exchange(outer_sums_small)
    d_low, total_small, packed_small = call(
        functools.partial(second_back, small, None, 1, taps_each),
        (
            shape((small.padded, SECOND), BF16),
            shape((2, OUTER), F32),
            shape((clips, tap_share, 128), BF16),
        ),
        second_back_scratch(small, taps_each),
        scalars=2,
        cost=8,
        far=(2, 6, 7, 8),
        far_out=(0,),
    )(
        half_length,
        first_tap,
        h_outer_small,
        outer_small,
        gathered,
        outer_gain,
        error_small,
        taps_mid_small,
        taps_few_small,
    )
    r_low, sums_low = call(
        functools.partial(conv_back, small, None, 1),
        (shape((small.rows, REDUCED), BF16), shape((clips, 2, REDUCED), F32)),
        conv_back_scratch(small),
        scalars=1,
        cost=8,
        far=(5, 6, 7),
    )(
        half_length,
        d_low,
        h_reduced_small,
        reduced_gain,
        reduced_shift,
        *kernels[1][:2],
        kernels[1][3],
    )
    share_small = summed(packed_small)
    sums_low, share_small = lax.optimization_barrier((sums_low, share_small))
    gathered = exchange(sums_low)
    kept = OUTER // parts
    point_share = round_up(kept * (FIRST // 128), 16 * clips) // clips
    coarse_rows = slots.each * small.line_rows
    dx_small, point_packed, reduced_total_small, outer_sums = call(
        functools.partial(point_back, small, slots, 1, kept),
        (
            shape((small.rows, OUTER), BF16),
            shape((clips, point_share, 128), BF16),
            shape((2, REDUCED), F32),
            shape((clips, 2, OUTER), F32),
        ),
        [
            pltpu.VMEM((small.rows, DIRECT + POOLED), BF16),
            pltpu.VMEM((small.rows, DIRECT + POOLED), BF16),
            pltpu.VMEM((small.rows, REDUCED), BF16),
            pltpu.VMEM((small.rows, REDUCED), BF16),
            pltpu.VMEM((small.rows, OUTER), BF16),
            pltpu.VMEM((FIRST, OUTER), BF16),
            pltpu.VMEM((small.rows, FIRST), BF16),
            pltpu.VMEM((OUTER, FIRST), F32),
            *Spread.scratch(small),
            pltpu.VMEM((16, OUTER), F32),
            pltpu.VMEM((small.rows, OUTER), BF16),
            pltpu.VMEM((small.rows, OUTER), BF16),
            pltpu.VMEM((parts, coarse_rows, 2 * DIRECT), BF16),
            Lines.semaphores(small, 6),
            pltpu.SemaphoreType.DMA((3,)),
        ],
        scalars=2,
        cost=10,
        far=(2, 6, 7, 8, 12, 13, 16),
    )(
        half_length,
        place_one,
        h_outer_small,
        outer_small,
        total_small,
        outer_gain,
        error_small,
        h_reduced_small,
        r_low,
        moment_small,
        gathered,
        reduced_gain,
        pooled,
        point_second,
        pooled_slope,
        pooled_product,
        kept_direct,
    )
    whole_small = lax.all_gather(share_small, ("branch", "dp"), axis=0)

    gathered = exchange(outer_sums)
    d_low, total, packed = call(
        functools.partial(second_back, grid, small, 0, taps_each),
        (
            shape((grid.padded, SECOND), BF16),
            shape((2, OUTER), F32),
            shape((clips, tap_share + point_share, 128), BF16),
        ),
        second_back_scratch(grid, taps_each),
        scalars=2,
        cost=18,
        far=(2, 6, 9, 10),
        far_out=(0,),
    )(length, first_tap, h_outer, outer, gathered, outer_gain, slope, dx_small, point_packed, taps_mid, taps_few)
    product_rows = round_up(own_channels, 16 * clips)
    du_rest, rest_product = call(
        functools.partial(rest_back, grid, small, slots, 0),
        (shape((grid.rows, DIRECT + POOLED), BF16), shape((product_rows, DIRECT + POOLED), F32)),
        [
            pltpu.VMEM((grid.rows, DIRECT + POOLED), BF16),
            pltpu.VMEM((grid.rows, DIRECT + POOLED), BF16),
            pltpu.VMEM(turned.shape, BF16),
            pltpu.VMEM((grid.rows, DIRECT + POOLED), BF16),
            *Spread.scratch(grid),
            Lines.semaphores(grid, 4),
            pltpu.SemaphoreType.DMA((1,)),
            pltpu.SemaphoreType.DMA((1,)),
        ],
        scalars=1,
        cost=8,
        far=(5, 6, 7, 8),
        far_out=(0,),
    )(length, outer, after(total, packed), outer_gain, dx_small, h_outer, slope, kept_direct, turned)
    share = summed(packed)
    d_low, share = lax.optimization_barrier((after(d_low, rest_product), share))
    r_low, sums_low, products = call(
        functools.partial(conv_back, grid, slots, 0),
        (
            shape((grid.rows, REDUCED), BF16),
            shape((clips, 2, REDUCED), F32),
            shape((clips, 8, product_rows // clips, 128), F32),
        ),
        [
            *conv_back_scratch(grid),
            pltpu.VMEM(turned.shape, BF16),
            pltpu.VMEM((product_rows, FIRST), F32),
            pltpu.SemaphoreType.DMA((1,)),
        ],
        scalars=1,
        cost=22,
        far=(5, 6, 7, 8),
    )(
        length,
        d_low,
        h_reduced,
        reduced_gain,
        reduced_shift,
        *kernels[0][:2],
        kernels[0][3],
        turned,
        rest_product,
    )
    whole = lax.all_gather(share, ("branch", "dp"), axis=0)
    gathered = exchange(sums_low)
    pieces = exchange(products)
    dx, reduced_total = call(
        functools.partial(mid_back, grid, 0),
        (shape((grid.rows, own_channels), BF16), shape((2, REDUCED), F32)),
        [
            pltpu.VMEM((grid.rows, DIRECT + POOLED), BF16),
            pltpu.VMEM((grid.rows, REDUCED), BF16),
            pltpu.VMEM((grid.rows, REDUCED), BF16),
            pltpu.VMEM((FIRST, own_channels), BF16),
            pltpu.VMEM((grid.rows, own_channels), BF16),
            Lines.semaphores(grid, 3),
            pltpu.SemaphoreType.DMA((1,)),
            pltpu.SemaphoreType.DMA((1,)),
        ],
        scalars=2,
        cost=8,
        far=(5, 6, 7, 8),
        far_out=(0,),
    )(length, place_one, moment, gathered, reduced_gain, du_rest, h_reduced, r_low, point_first)
    pieces, dx = lax.optimization_barrier((pieces, dx))
    point_sum = call(
        functools.partial(combine, 0),
        shape((5 * product_rows // clips, 128), BF16),
        cost=1,
    )(pieces, moment, gathered, reduced_gain)
    received = spread_over(point_sum, "branch", parts)

    outs = (
        shape((2, TAPS, MID_IN, MID_OUT), F32),
        shape((2, TAPS, SMALL_IN, SMALL_OUT), F32),
        shape((2, SQUEEZED, CHANNELS), F32),
    )
    tap_scratch = [
        pltpu.VMEM((TAPS, MID_IN, MID_OUT), F32),
        pltpu.VMEM((TAPS, SMALL_IN, SMALL_OUT), F32),
    ]
    point_scratch = [pltpu.VMEM((SQUEEZED, CHANNELS), F32), pltpu.VMEM((CHANNELS, 128), F32)]
    mid_grad, small_grad = call(
        functools.partial(unpack_second, clips, taps_each),
        outs[:2],
        [*tap_scratch, pltpu.SemaphoreType.DMA((2,))],
        far_out=(0, 1),
        cost=5,
    )(whole_small)
    received, mid_grad, small_grad = lax.optimization_barrier((received, mid_grad, small_grad))
    norms = shape((2, 1024), F32)
    mid_grad, small_grad, point_grad, gain_grad, shift_grad = call(
        functools.partial(unpack_first, parts, clips, taps_each, tap_share),
        (*outs, norms, norms),
        [*tap_scratch, *point_scratch, pltpu.SemaphoreType.DMA((3,))],
        far_out=(0, 1, 2),
        aliases={5: 0, 6: 1},
        cost=6,
    )(whole, total, reduced_total, total_small, reduced_total_small, mid_grad, small_grad)
    point_mine, point_other = gather_chips(
        jnp.concatenate(received, axis=0), clips, (mid_grad, small_grad)
    )
    clip_one = lax.axis_index("dp").astype(jnp.int32).reshape(1)
    point_grad = call(
        functools.partial(unpack_point, parts, clips, own_channels),
        outs[2],
        [
            pltpu.VMEM((parts, FIRST // 128, product_rows, 128), BF16),
            *point_scratch,
            pltpu.SemaphoreType.DMA((1,)),
        ],
        scalars=2,
        far_out=(0,),
        aliases={4: 0},
        cost=3,
    )(place_one, clip_one, point_mine, point_other, point_grad)
    act = act.reshape(small.side, small.side, cotangent.shape[1], CHANNELS).transpose(2, 0, 1, 3)
    input_grad = dx.reshape(side, side, PITCH, own_channels).transpose(2, 0, 1, 3)
    return (
        act[None],
        input_grad[None],
        point_grad.swapaxes(1, 2),
        mid_grad,
        small_grad,
        gain_grad,
        shift_grad,
    )


def solution(mesh):
    split = P("dp", None, None, None, "branch")
    whole = P("dp", None, None, None, None)
    return jax.shard_map(
        on_device,
        mesh=mesh,
        in_specs=(split, P("dp"), whole, P(), P(), P(), P(), P()),
        out_specs=(whole, split, P(), P(), P(), P(), P()),
        check_vma=False,
    )
```

```python
import functools

import jax
import jax.numpy as jnp
from jax import lax
from jax.experimental import pallas as pl
from jax.experimental.pallas import tpu as pltpu
from jax.sharding import PartitionSpec as P

DIRECT = 256
MID_IN = 160
MID_OUT = 320
SMALL_IN = 32
SMALL_OUT = 128
TAPS = 27
CHANNELS = 832
SQUEEZED = 576
TILE = 16
REDUCED = 256
POOLED = 128
FIRST = 640
SECOND = 512
OUTER = 896
TAP_ROWS = 432
EPSILON = 1e-05
F32 = jnp.float32
BF16 = jnp.bfloat16
VMEM_BYTES = 58 * 2**20
LARGE = 2200 * 2**10


def call(body, out_shape, scratch=(), scalars=0, cost=5, aliases=None, far=(), far_out=()):
    aliases = aliases or {}

    def large(values):
        size = values.dtype.itemsize
        for extent in values.shape:
            size = size * extent
        return size > LARGE

    def placed(out):
        return pltpu.HBM(out.shape, out.dtype) if large(out) else out

    def run(*operands):
        specs = [
            pl.BlockSpec(
                memory_space=pl.ANY
                if number in aliases or number in far
                else pltpu.SMEM
                if number < scalars
                else pltpu.VMEM
            )
            for number in range(len(operands))
        ]
        operands = [
            pltpu.with_memory_space_constraint(operand, pltpu.HBM) if large(operand) else operand
            for operand in operands
        ]
        if isinstance(out_shape, tuple):
            out_specs = tuple(
                pl.BlockSpec(memory_space=pl.ANY if number in far_out else pltpu.VMEM)
                for number in range(len(out_shape))
            )
        else:
            out_specs = pl.BlockSpec(memory_space=pl.ANY if 0 in far_out else pltpu.VMEM)
        return pl.pallas_call(
            body,
            out_shape=jax.tree.map(placed, out_shape),
            in_specs=specs,
            out_specs=out_specs,
            input_output_aliases=aliases,
            scratch_shapes=list(scratch),
            compiler_params=pltpu.CompilerParams(vmem_limit_bytes=VMEM_BYTES),
            cost_estimate=pl.CostEstimate(
                flops=0, bytes_accessed=int(cost * 3 * 10**6), transcendentals=0
            ),
        )(*operands)

    return run


def shape(dims, dtype):
    return jax.ShapeDtypeStruct(tuple(dims), dtype)


def rows_at(start, size):
    return pl.ds(pl.multiple_of(start, 16), size)


def frames_of(values_or_rows, unit):
    dims = values_or_rows if isinstance(values_or_rows, tuple) else (values_or_rows, 128)
    return lax.broadcasted_iota(jnp.int32, dims, 0) & (unit - 1)


def earlier(values, unit):
    return jnp.where(frames_of(values.shape, unit) > 0, pltpu.roll(values, 1, 0), 0.0)


def later(values, unit):
    rows = values.shape[0]
    shifted = pltpu.roll(values, rows - 1, 0)
    return jnp.where(frames_of(values.shape, unit) < unit - 1, shifted, 0.0)


def plane_box(values, unit):
    across = values + earlier(values, unit) + later(values, unit)
    edge = jnp.zeros((unit, values.shape[1]), values.dtype)
    return (
        across
        + jnp.concatenate([across[unit:], edge], axis=0)
        + jnp.concatenate([edge, across[:-unit]], axis=0)
    )


def box_window(grid, length):
    frame, place = (frames_of(grid.line_rows, grid.unit), grid.places_of(grid.line_rows))

    def one(condition):
        return jnp.where(condition, 1.0, 0.0)

    count = one(frame < length) + one(frame + 1 < length) + one((frame > 0) & (frame - 1 < length))
    return count * (3.0 - one(place == 0) - one(place == grid.side - 1))


def box_scale(line, side, window):
    lines = 3.0 - jnp.where(line == 0, 1.0, 0.0) - jnp.where(line == side - 1, 1.0, 0.0)
    return 1.0 / jnp.maximum(window * lines, 1.0)


def sigmoid(value):
    return 0.5 * jnp.tanh(0.5 * value) + 0.5


def silu(value):
    return value * sigmoid(value)


def silu_slope(value):
    gate = sigmoid(value)
    return gate * (1.0 + value * (1.0 - gate))


def partial_sum(values):
    rows, width = values.shape
    return jnp.sum(values.reshape(rows // 8, 8, width), axis=0)


def moments(total, square, count):
    center = total / count
    return (center, lax.rsqrt(square / count - center * center + EPSILON))


def total_of(gathered):
    count = len(gathered) if isinstance(gathered, (list, tuple)) else gathered.shape[0]
    total = gathered[0][...]
    for number in range(1, count):
        total = total + gathered[number][...]
    return total


def pool_matrix(grid, small, transposed):
    line = grid.line_rows
    few, many = (small.line_rows, 2 * line)
    dims = (many, few) if transposed else (few, many)
    coarse = lax.broadcasted_iota(jnp.int32, dims, 1 if transposed else 0)
    fine = lax.broadcasted_iota(jnp.int32, dims, 0 if transposed else 1)
    fine = jnp.where(fine >= line, fine - line, fine)
    same = (fine >> (grid.bits + 1) == coarse >> small.bits) & (
        (fine & (grid.unit - 1)) >> 1 == coarse & (small.unit - 1)
    )
    return jnp.where(same, 0.125, 0.0).astype(BF16)


class Grid:
    def __init__(self, side, unit):
        self.side, self.unit = (side, unit)
        self.bits = unit.bit_length() - 1
        self.copies = TILE // unit
        self.line_rows = side * unit if self.copies == 1 else (side + 1) * unit
        self.rows = side * self.line_rows
        self.pitch = (side + 1) * unit
        margin = 1 if self.copies == 1 else 2
        self.lead = margin * self.pitch + TILE
        self.padded = (side + 2 * margin) * self.pitch + 2 * TILE
        self.group = 2 if side % 2 == 0 else side

    def places_of(self, rows):
        place = lax.broadcasted_iota(jnp.int32, (rows, 128), 0) >> self.bits
        return place if self.copies == 1 else place & self.side

    def mask(self, rows, length, width=128):
        valid = frames_of(rows, self.unit) < length
        if self.copies > 1:
            valid = valid & (self.places_of(rows) < self.side)
        mask = jnp.where(valid, 1.0, 0.0)
        return jnp.concatenate([mask] * (width // 128), axis=1) if width > 128 else mask

    def near(self, ref, base, lines, places, size, lanes=slice(None)):
        start = base + lines * self.pitch
        if self.copies == 1:
            return ref[0, rows_at(start + places * TILE, size), lanes]
        copy = 0 if places == 0 else 1
        return ref[copy, rows_at(start - (TILE if places < 0 else 0), size), lanes]


class Slots:
    def __init__(self, grid, parts):
        self.pairs = grid.side // 2
        self.parts = parts
        self.each = -(-self.pairs // parts)
        self.empty = parts * self.each - self.pairs
        self.gap = parts * self.each // 2 - 1
        self.pair_rows = 2 * grid.line_rows
        self.grid = grid
        self.rows = self.each * self.pair_rows

    def slot_of(self, pair):
        return pair + jnp.where(pair >= self.gap, self.empty, 0)

    def pair_of(self, slot):
        return slot - jnp.where(slot >= self.gap, self.empty, 0)

    def used(self, slot):
        return (slot < self.gap) | (slot >= self.gap + self.empty)

    def held(self, place):
        count = jnp.zeros((), jnp.int32)
        for number in range(self.each):
            count = count + jnp.where(self.used(place * self.each + number), 1, 0)
        return count


def clear_empty(grid, ref):
    width = ref.shape[2]
    if grid.copies > 1:
        ref[...] = jnp.zeros_like(ref)
        return
    ref[0, 0 : grid.lead, :] = jnp.zeros((grid.lead, width), ref.dtype)
    end = grid.lead + grid.side * grid.pitch
    ref[0, end:, :] = jnp.zeros((ref.shape[1] - end, width), ref.dtype)

    @pl.loop(0, grid.side)
    def _(line):
        at = rows_at(grid.lead + line * grid.pitch + grid.line_rows, TILE)
        ref[0, at, :] = jnp.zeros((TILE, width), ref.dtype)


def store_taps(unit, mid_ref, small_ref, copy, at, act):
    before, after_ = (earlier(act, unit), later(act, unit))
    mid_ref[copy, at, 0:128] = before[:, :128].astype(BF16)
    mid_ref[copy, at, 128:256] = act[:, :128].astype(BF16)
    mid_ref[copy, at, 256:384] = after_[:, :128].astype(BF16)
    before, act, after_ = (before[:, 128:], act[:, 128:], after_[:, 128:])
    lane = lax.broadcasted_iota(jnp.int32, act.shape, 1)
    mid_ref[copy, at, 384:512] = jnp.where(
        lane < 32, before, jnp.where(lane < 64, pltpu.roll(act, 32, 1), pltpu.roll(after_, 64, 1))
    ).astype(BF16)
    small_ref[copy, at, :] = jnp.where(
        lane < 32, pltpu.roll(before, 96, 1), jnp.where(lane < 64, act, pltpu.roll(after_, 32, 1))
    ).astype(BF16)


def near_tap(grid, ref, base, tap, sign, size, lanes=slice(None)):
    return grid.near(ref, base, sign * (tap // 3 - 1), sign * (tap % 3 - 1), size, lanes)


def convolve(grid, taps, kernels, rest_ref, acc_ref, stage_ref, e_ref, stage_sem, sums_ref, length):
    mid_ref, small_ref = taps
    main_ref, last_ref, small_kernel_ref = kernels
    group_rows = grid.group * grid.pitch
    stage_rows = grid.group * grid.line_rows
    groups = grid.side // grid.group
    sums_ref[...] = jnp.zeros_like(sums_ref)
    mask = grid.mask(grid.line_rows, length, SECOND)
    edge = jnp.zeros((grid.pitch, 256), F32)
    rest_ref[grid.lead - grid.pitch : grid.lead, :] = edge
    end = grid.lead + grid.side * grid.pitch
    rest_ref[end : end + grid.pitch, :] = edge

    @pl.loop(0, groups)
    def _(group):
        base = grid.lead + group * group_rows
        total = None
        for place in range(3):
            part = jnp.dot(
                grid.near(mid_ref, base, 0, place - 1, group_rows),
                last_ref[place],
                preferred_element_type=F32,
            )
            total = part if total is None else total + part
        rest_ref[rows_at(base, group_rows), :] = total

    lane = lax.broadcasted_iota(jnp.int32, (grid.line_rows, 128), 1)

    def staged(group, slot):
        return pltpu.make_async_copy(
            stage_ref.at[slot],
            e_ref.at[rows_at(group * stage_rows, stage_rows), :],
            stage_sem.at[slot],
        )

    @pl.loop(0, groups)
    def _(group):
        base = grid.lead + group * group_rows
        slot = lax.rem(group, 2)
        for tap in range(9):
            part = jnp.dot(
                near_tap(grid, mid_ref, base, tap, 1, group_rows),
                main_ref[tap],
                preferred_element_type=F32,
            )
            acc_ref[:, 0:256] = part if tap == 0 else acc_ref[:, 0:256] + part
        near = [near_tap(grid, small_ref, base, tap, 1, group_rows) for tap in range(9)]
        acc_ref[:, 256:384] = jnp.dot(
            jnp.concatenate(near, axis=1), small_kernel_ref[...], preferred_element_type=F32
        )

        @pl.when(group >= 2)
        def _():
            staged(group - 2, slot).wait()

        for number in range(grid.group):
            rows = grid.line_rows
            start = base + number * grid.pitch
            last = (
                rest_ref[rows_at(start - grid.pitch, rows), 0:128]
                + pltpu.roll(rest_ref[rows_at(start, rows), 0:128], 64, 1)
                + rest_ref[rows_at(start + grid.pitch, rows), 128:256]
            )
            lines = slice(number * grid.pitch, number * grid.pitch + rows)
            values = jnp.concatenate(
                [acc_ref[lines, 0:256], jnp.where(lane < 64, last, 0.0), acc_ref[lines, 256:384]],
                axis=1,
            )
            stage_ref[slot, number * rows : (number + 1) * rows, :] = values
            masked = values * mask
            sums_ref[0:8] += partial_sum(masked)
            sums_ref[8:16] += partial_sum(masked * values)
        staged(group, slot).start()

    for group in range(max(groups - 2, 0), groups):
        staged(group, group % 2).wait()


def conv_scratch(grid):
    group_rows = grid.group * grid.pitch
    return [
        pltpu.VMEM((9, 512, 256), BF16),
        pltpu.VMEM((3, 512, 256), BF16),
        pltpu.VMEM((1152, 128), BF16),
        pltpu.VMEM((grid.copies, grid.padded, 512), BF16),
        pltpu.VMEM((grid.copies, grid.padded, 128), BF16),
        pltpu.VMEM((grid.rows, REDUCED), BF16),
        pltpu.VMEM((grid.padded, 256), F32),
        pltpu.VMEM((group_rows, 384), F32),
        pltpu.VMEM((2, grid.group * grid.line_rows, SECOND), F32),
        pltpu.VMEM((16, SECOND), F32),
        pltpu.SemaphoreType.DMA((3,)),
        pltpu.SemaphoreType.DMA((3,)),
        pltpu.SemaphoreType.DMA((2,)),
    ]


def conv_outputs(grid, *clips):
    return (
        shape((grid.rows, REDUCED), BF16),
        shape((grid.copies, grid.padded, 512), BF16),
        shape((grid.copies, grid.padded, 128), BF16),
        shape((grid.rows, SECOND), F32),
        shape((*clips, 2, SECOND), F32),
    )


def copies(sources, targets, sem_ref):
    return [
        pltpu.make_async_copy(source, target, sem_ref.at[number])
        for number, (source, target) in enumerate(zip(sources, targets))
    ]


def run_convolution(grid, length, far_kernels, outputs, scratch, fill):
    h_out, mid_out, small_out, e_out, sums_out = outputs
    kernels, (mid_ref, small_ref, h_ref), rest = (scratch[:3], scratch[3:6], scratch[6:])
    rest_ref, acc_ref, stage_ref, sums_ref, in_sem, out_sem, stage_sem = rest
    arriving = copies(far_kernels, kernels, in_sem)
    for copy in arriving:
        copy.start()
    clear_empty(grid, mid_ref)
    clear_empty(grid, small_ref)
    fill(h_ref, mid_ref, small_ref)
    leaving = copies((mid_ref, small_ref, h_ref), (mid_out, small_out, h_out), out_sem)
    for copy in leaving:
        copy.start()
    for copy in arriving:
        copy.wait()
    convolve(
        grid, (mid_ref, small_ref), kernels, rest_ref, acc_ref, stage_ref, e_out, stage_sem, sums_ref, length
    )
    write_sums(sums_out, sums_ref, 0, SECOND)
    for copy in leaving:
        copy.wait()


def write_row(out_ref, row, lo, hi, values):
    if len(out_ref.shape) == 2:
        out_ref[row : row + 1, lo:hi] = values
    else:
        for clip in range(out_ref.shape[0]):
            out_ref[clip, row : row + 1, lo:hi] = values


def write_sums(out_ref, sums_ref, lo, hi):
    for number in range(2):
        values = jnp.sum(sums_ref[8 * number : 8 * number + 8], axis=0, keepdims=True)
        write_row(out_ref, number, lo, hi, values)


def turn(slots, x_ref, out_ref):
    for slot in range(slots.parts * slots.each):
        part, number = divmod(slot, slots.each)
        lanes = slice(number * slots.pair_rows, (number + 1) * slots.pair_rows)
        if slots.gap <= slot < slots.gap + slots.empty:
            out_ref[part, :, lanes] = jnp.zeros((out_ref.shape[1], slots.pair_rows), BF16)
            continue
        pair = slot - (slots.empty if slot >= slots.gap else 0)
        rows = slice(pair * slots.pair_rows, (pair + 1) * slots.pair_rows)
        out_ref[part, :, lanes] = x_ref[rows, :].T


def first_pointwise(slots, length_ref, count_ref, x_ref, p_ref, mid_ref, pool_ref, direct_ref, sums_ref, u_ref):
    rows, step = (slots.rows, 112)
    length, count = (length_ref[0], count_ref[0])
    for part in range(slots.parts):
        product = lax.dot_general(
            x_ref[part], p_ref[part], (((0,), (1,)), ((), ())), preferred_element_type=F32
        )
        u_ref[...] = product if part == 0 else u_ref[...] + product
    mask = slots.grid.mask(step, length, FIRST)

    def summed(number, carry):
        values = u_ref[rows_at(number * step, step), :] * mask
        u_ref[rows_at(number * step, step), :] = values
        few = values[:, :SECOND]
        return (carry[0] + partial_sum(values), carry[1] + partial_sum(few * few))

    zero = (jnp.zeros((8, FIRST), F32), jnp.zeros((8, SECOND), F32))
    total, square = lax.fori_loop(0, rows // step, summed, zero)
    total = jnp.sum(total, axis=0, keepdims=True)
    write_row(sums_ref, 0, 0, SECOND, total[:, :SECOND])
    write_row(sums_ref, 1, 0, SECOND, jnp.sum(square, axis=0, keepdims=True))
    write_row(sums_ref, 2, 0, SECOND, jnp.full((1, SECOND), count, F32))
    offset = (total / jnp.full((1, FIRST), jnp.maximum(count, 1.0), F32)).astype(BF16)
    wide_offset = offset.astype(F32)
    tail = jnp.broadcast_to(wide_offset, (TILE, FIRST)).astype(BF16)
    pool_ref[rows : rows + TILE, :] = tail[:, SECOND:]
    shared = mid_ref.shape[0] - 2 * TILE
    mid_ref[shared : shared + TILE, :] = tail[:, 256:384]
    mid_ref[shared + TILE :, :] = tail[:, 384:512]

    @pl.loop(0, rows // step)
    def _(number):
        at = rows_at(number * step, step)
        values = u_ref[at, :]
        direct_ref[at, :] = values[:, :DIRECT]
        values = values[:, DIRECT:] - wide_offset[:, DIRECT:]
        mid_ref[at, :] = values[:, :128].astype(BF16)
        pool_ref[at, :] = values[:, 256:].astype(BF16)

    lane = lax.broadcasted_iota(jnp.int32, (step, 128), 1)
    for couple in range(0, slots.each, 2):

        @pl.loop(0, slots.pair_rows // step)
        def _(number):
            start = couple * slots.pair_rows + number * step
            values = u_ref[rows_at(start, step), 384:512] - wide_offset[:, 384:512]
            if couple + 1 < slots.each:
                other = u_ref[rows_at(start + slots.pair_rows, step), 384:512]
                other = pltpu.roll(other - wide_offset[:, 384:512], 64, 1)
                values = jnp.where(lane < 64, values, other)
            place = rows + couple // 2 * slots.pair_rows + number * step
            mid_ref[rows_at(place, step), :] = values.astype(BF16)


def mid_rows(slots):
    return slots.rows + -(-slots.each // 2) * slots.pair_rows + 2 * TILE


def each_pair(slots, place, refs, visit):
    for step, ref in enumerate(refs):
        source = lax.rem(place - step + slots.parts, slots.parts)
        for number in range(slots.each):
            slot = source * slots.each + number

            @pl.when(slots.used(slot))
            def _():
                visit(slots.pair_of(slot), ref, number)


def set_moments(total, moment_ref):
    count = total[2:3]
    center, inverse = moments(total[0:1], total[1:2], count)
    moment_ref[0:1, :] = center
    moment_ref[1:2, :] = inverse
    moment_ref[2:3, :] = count
    return (center, inverse)


def first_convolve(grid, slots, block, length_ref, place_ref, *refs):
    parts = slots.parts
    mids, (moment_ref, gain_ref, shift_ref), refs = (refs[:parts], refs[parts : parts + 3], refs[parts + 3 :])
    far_kernels, outputs, scratch = (refs[:3], refs[3:8], refs[8:])
    length = length_ref[0]
    center, inverse = (moment_ref[0:1, DIRECT:], moment_ref[1:2, DIRECT:])
    gain, shift = (gain_ref[block : block + 1], shift_ref[block : block + 1])
    step = 112
    mask = grid.mask(step, length, REDUCED)
    lane = lax.broadcasted_iota(jnp.int32, (step, 128), 1)

    def fill(h_ref, mid_ref, small_ref):
        def visit(pair, ref, number):
            shared = ref.shape[0] - 2 * TILE
            offset = jnp.concatenate(
                [
                    ref[at : at + TILE, :].astype(F32)[0:1]
                    for at in (shared, shared + TILE)
                ],
                axis=1,
            )
            other = slots.rows + number // 2 * slots.pair_rows

            @pl.loop(0, slots.pair_rows // step)
            def _(chunk):
                values = ref[rows_at(number * slots.pair_rows + chunk * step, step), :].astype(F32)
                few = ref[rows_at(other + chunk * step, step), :].astype(F32)
                if number % 2 == 1:
                    few = pltpu.roll(few, 64, 1)
                few = jnp.where(lane < 64, few, 0.0)
                values = jnp.concatenate([values, few], axis=1) + offset
                scaled = (values - center) * inverse
                row = pair * slots.pair_rows + chunk * step
                h_ref[rows_at(row, step), :] = scaled.astype(BF16)
                act = silu(gain * scaled + shift) * mask
                line = row // grid.line_rows
                at = grid.lead + line * grid.pitch + row - line * grid.line_rows
                store_taps(grid.unit, mid_ref, small_ref, 0, rows_at(at, step), act)

        each_pair(slots, place_ref[0], mids, visit)

    run_convolution(grid, length, far_kernels, outputs, scratch, fill)


def pool_planes(grid, plane_ref, q_ref, lo, sums_ref, length, window):
    rows = grid.line_rows
    mask = grid.mask(rows, length)
    sums_ref[...] = jnp.zeros_like(sums_ref)

    @pl.loop(0, grid.side)
    def _(line):
        start = line * rows
        values = (
            plane_ref[rows_at(start, rows), :]
            + plane_ref[rows_at(start + rows, rows), :]
            + plane_ref[rows_at(start + 2 * rows, rows), :]
        ) * box_scale(line, grid.side, window)
        q_ref[rows_at(start, rows), lo : lo + POOLED] = values
        masked = values * mask
        sums_ref[0:8] += partial_sum(masked)
        sums_ref[8:16] += partial_sum(masked * values)


def clear_edges(grid, plane_ref):
    rows = grid.line_rows
    plane_ref[0:rows] = jnp.zeros((rows, POOLED), F32)
    plane_ref[grid.rows + rows : grid.rows + 2 * rows] = jnp.zeros((rows, POOLED), F32)


def first_pool(grid, slots, length_ref, place_ref, *refs):
    pools, refs = (refs[: slots.parts], refs[slots.parts :])
    e_sums_ref, q_ref, out_sums_ref, plane_ref, sums_ref = refs
    length = length_ref[0]
    rows = grid.line_rows
    for row in range(2):
        write_row(out_sums_ref, row, 0, SECOND, e_sums_ref[row : row + 1, :])
    clear_edges(grid, plane_ref)

    def visit(pair, ref, number):
        offset = ref[slots.rows : slots.rows + TILE, :].astype(F32)[0:1]
        for line in range(2):
            at = rows_at(number * slots.pair_rows + line * rows, rows)
            plane_ref[rows_at((2 * pair + line + 1) * rows, rows), :] = plane_box(
                ref[at, :].astype(F32) + offset, grid.unit
            )

    each_pair(slots, place_ref[0], pools, visit)
    pool_planes(grid, plane_ref, q_ref, 0, sums_ref, length, box_window(grid, length))
    write_sums(out_sums_ref, sums_ref, SECOND, FIRST)


def normalize(values, center, inverse, gain, shift, mask):
    scaled = (values - center) * inverse
    shifted = gain * scaled + shift
    gate = sigmoid(shifted)
    gate_mask = gate * mask
    act = shifted * gate_mask
    return (scaled, act, gate_mask + act * (1.0 - gate))


def pool_pieces(matrix, pieces):
    return jnp.dot(
        matrix, jnp.concatenate(pieces, axis=0), preferred_element_type=F32
    ).astype(BF16)


def first_direct(grid, small, slots, block, length_ref, u_ref, gain_ref, shift_ref, *refs):
    sums, (pooled_ref, kept_ref, moment_ref) = (refs[: slots.parts], refs[slots.parts :])
    rows = grid.line_rows
    mask = grid.mask(rows, length_ref[0], DIRECT)
    center, inverse = set_moments(total_of(sums), moment_ref)
    center, inverse = (center[:, :DIRECT], inverse[:, :DIRECT])
    gain, shift = (gain_ref[block : block + 1, :DIRECT], shift_ref[block : block + 1, :DIRECT])
    matrix = pool_matrix(grid, small, False)

    @pl.loop(0, slots.each)
    def _(number):
        acts, slopes, products = ([], [], [])
        for line in range(2):
            at = rows_at(number * slots.pair_rows + line * rows, rows)
            scaled, act, slope = normalize(u_ref[at, :], center, inverse, gain, shift, mask)
            kept_ref[at, 0:DIRECT] = scaled.astype(BF16)
            kept_ref[at, DIRECT : 2 * DIRECT] = slope.astype(BF16)
            acts.append(act.astype(BF16))
            slopes.append(slope.astype(BF16))
            products.append((slope * scaled).astype(BF16))
        size = small.line_rows
        pooled_ref[rows_at(number * size, size), :] = pool_pieces(matrix, acts)
        at = rows_at(slots.rows + number * size, size)
        kept_ref[at, 0:DIRECT] = pool_pieces(matrix, slopes)
        kept_ref[at, DIRECT : 2 * DIRECT] = pool_pieces(matrix, products)


def outer_moments(center, inverse, count, outer_ref):
    outer_ref[0:1, :] = center
    outer_ref[1:2, :] = inverse
    outer_ref[2:3, :] = jnp.concatenate([count[:, 0:128]] * (OUTER // 128), axis=1)


def first_output(grid, small, block, length_ref, q_far, e_far, moment_ref, sums_in_ref, gain_ref, shift_ref, *refs):
    pooled_ref, h_far, slope_far, outer_ref, pooled_slope_ref, pooled_product_ref, *refs = refs
    q_ref, e_ref, h_ref, slope_ref, q_sem, e_sem, h_sem, slope_sem = refs
    rows = grid.line_rows
    wide = 2 * rows
    pairs = grid.side // 2

    def arriving(pair, slot):
        at = rows_at(pair * wide, wide)
        return [
            pltpu.make_async_copy(q_far.at[at, :], q_ref.at[slot], q_sem.at[slot]),
            pltpu.make_async_copy(e_far.at[at, :], e_ref.at[slot], e_sem.at[slot]),
        ]

    def leaving(pair, slot):
        at = rows_at(pair * wide, wide)
        return [
            pltpu.make_async_copy(h_ref.at[slot], h_far.at[at, :], h_sem.at[slot]),
            pltpu.make_async_copy(slope_ref.at[slot], slope_far.at[at, :], slope_sem.at[slot]),
        ]

    for copy in arriving(0, 0):
        copy.start()
    mask = grid.mask(rows, length_ref[0], FIRST)
    total = total_of(sums_in_ref)
    count = jnp.concatenate([moment_ref[2:3, 0:128]] * (FIRST // 128), axis=1)
    center, inverse = moments(total[0:1], total[1:2], count)
    outer_moments(
        jnp.concatenate([moment_ref[0:1, :DIRECT], center], axis=1),
        jnp.concatenate([moment_ref[1:2, :DIRECT], inverse], axis=1),
        count,
        outer_ref,
    )
    matrix = pool_matrix(grid, small, False)
    gain, shift = (gain_ref[block : block + 1, DIRECT:], shift_ref[block : block + 1, DIRECT:])

    @pl.loop(0, pairs)
    def _(pair):
        slot = lax.rem(pair, 2)

        @pl.when(pair + 1 < pairs)
        def _():
            for copy in arriving(pair + 1, 1 - slot):
                copy.start()

        for copy in arriving(pair, slot):
            copy.wait()

        @pl.when(pair >= 2)
        def _():
            for copy in leaving(pair - 2, slot):
                copy.wait()

        acts, slopes, products = ([], [], [])
        for number in range(2):
            lines = slice(number * rows, (number + 1) * rows)
            values = jnp.concatenate([e_ref[slot, lines, :], q_ref[slot, lines, :]], axis=1)
            scaled, act, slope = normalize(values, center, inverse, gain, shift, mask)
            h_ref[slot, lines, :] = scaled.astype(BF16)
            low_slope = slope.astype(BF16)
            slope_ref[slot, lines, :] = low_slope
            acts.append(act.astype(BF16))
            slopes.append(low_slope)
            products.append((slope * scaled).astype(BF16))
        for copy in leaving(pair, slot):
            copy.start()
        at = rows_at(pair * small.line_rows, small.line_rows)
        pooled_ref[at, :] = pool_pieces(matrix, acts)
        pooled_slope_ref[at, :] = pool_pieces(matrix, slopes)
        pooled_product_ref[at, :] = pool_pieces(matrix, products)

    for pair in range(max(pairs - 2, 0), pairs):
        for copy in leaving(pair, pair % 2):
            copy.wait()


def second_pointwise(grid, slots, length_ref, place_ref, count_ref, *refs):
    directs, refs = (refs[: slots.parts], refs[slots.parts :])
    rest_ref, p_ref, q_ref, out_sums_ref, x_ref, plane_ref, sums_ref, pool_sums_ref = refs
    length = length_ref[0]
    rows = grid.line_rows
    sums_ref[...] = jnp.zeros_like(sums_ref)
    clear_edges(grid, plane_ref)
    x_ref[:, DIRECT:] = rest_ref[...]

    def visit(pair, ref, number):
        x_ref[rows_at(pair * rows, rows), 0:DIRECT] = ref[number * rows : (number + 1) * rows, :]

    each_pair(slots, place_ref[0], directs, visit)
    q_ref[...] = lax.dot_general(
        x_ref[...], p_ref[...], (((1,), (1,)), ((), ())), preferred_element_type=F32
    )

    @pl.loop(0, grid.side)
    def _(line):
        values = q_ref[rows_at(line * rows, rows), :]
        sums_ref[0:8] += partial_sum(values[:, :SECOND])
        sums_ref[8:16] += partial_sum(values[:, :SECOND] * values[:, :SECOND])
        plane_ref[rows_at((line + 1) * rows, rows), :] = plane_box(
            values[:, SECOND:], grid.unit
        )

    pool_planes(grid, plane_ref, q_ref, SECOND, pool_sums_ref, length, box_window(grid, length))
    write_sums(out_sums_ref, sums_ref, 0, SECOND)
    write_sums(out_sums_ref, pool_sums_ref, SECOND, FIRST)
    write_row(out_sums_ref, 2, 0, FIRST, jnp.full((1, FIRST), count_ref[0], F32))


def clear_ends(grid, ref):
    edge = jnp.zeros((grid.line_rows, ref.shape[1]), F32)
    ref[0 : grid.line_rows, :] = edge
    ref[grid.rows + grid.line_rows :, :] = edge


def store_copies(grid, ref, store):
    @pl.loop(0, grid.side + 1)
    def _(number):
        start = number * grid.line_rows
        at = rows_at(grid.lead + (number - 1) * grid.pitch, grid.line_rows)
        store(0, at, ref[rows_at(start, grid.line_rows), :])
        moved = pl.ds(pl.multiple_of(start + grid.unit, grid.unit), grid.line_rows)
        store(1, at, ref[moved, :])


def second_convolve(grid, block, length_ref, q_ref, sums_in_ref, gain_ref, shift_ref, *refs):
    far_kernels, outputs, moment_ref, scratch = (refs[:3], refs[3:8], refs[8], refs[9:])
    length = length_ref[0]
    center, inverse = set_moments(total_of(sums_in_ref), moment_ref)
    center, inverse = (center[:, DIRECT:SECOND], inverse[:, DIRECT:SECOND])
    gain, shift = (gain_ref[block : block + 1], shift_ref[block : block + 1])
    rows = grid.line_rows
    mask = grid.mask(rows, length, REDUCED)
    scratch, act_ref = (scratch[:-1], scratch[-1])

    def fill(h_ref, mid_ref, small_ref):
        clear_ends(grid, act_ref)

        @pl.loop(0, grid.side)
        def _(line):
            at = rows_at(line * rows, rows)
            scaled = (q_ref[at, DIRECT:SECOND] - center) * inverse
            h_ref[at, :] = scaled.astype(BF16)
            act_ref[rows_at((line + 1) * rows, rows), :] = silu(gain * scaled + shift) * mask

        def store(copy, at, values):
            store_taps(grid.unit, mid_ref, small_ref, copy, at, values)

        store_copies(grid, act_ref, store)

    run_convolution(grid, length, far_kernels, outputs, scratch, fill)


def second_output(grid, block, length_ref, q_ref, e_ref, moment_ref, sums_in_ref, gain_ref, shift_ref, cot_ref, act_ref, h_ref, error_ref, outer_ref, out_sums_ref, sums_ref):
    rows = grid.line_rows
    side, frames = (grid.side, cot_ref.shape[1])
    mask = grid.mask(rows, length_ref[0], OUTER)
    total = total_of(sums_in_ref)
    count = moment_ref[2:3, 0:SECOND]
    center, inverse = moments(total[0:1], total[1:2], count)
    center = jnp.concatenate([moment_ref[0:1, :DIRECT], center, moment_ref[0:1, SECOND:]], axis=1)
    inverse = jnp.concatenate([moment_ref[1:2, :DIRECT], inverse, moment_ref[1:2, SECOND:]], axis=1)
    outer_moments(center, inverse, count, outer_ref)
    sums_ref[...] = jnp.zeros_like(sums_ref)
    gain, shift = (gain_ref[block : block + 1], shift_ref[block : block + 1])
    gap = jnp.zeros((rows, 64), F32)
    unused = jnp.zeros((grid.unit, CHANNELS), F32)

    @pl.loop(0, side)
    def _(line):
        at = rows_at(line * rows, rows)
        places = pl.ds(line * side, side)
        values = jnp.concatenate([q_ref[at, :DIRECT], e_ref[at, :], q_ref[at, SECOND:]], axis=1)
        scaled = (values - center) * inverse
        h_ref[at, :] = scaled.astype(BF16)
        shifted = gain * scaled + shift
        gate = sigmoid(shifted)
        act = (shifted * gate * mask).reshape(side + 1, frames, OUTER)[:side].astype(BF16)
        act_ref[places, :, 0:576] = act[:, :, 0:576]
        act_ref[places, :, 576:CHANNELS] = act[:, :, 640:OUTER]
        slope = gate * (1.0 + shifted * (1.0 - gate))
        grad = cot_ref[places].astype(F32).reshape(side * frames, CHANNELS)
        grad = jnp.concatenate([grad, unused], axis=0)
        grad = jnp.concatenate([grad[:, :576], gap, grad[:, 576:]], axis=1)
        error = grad * slope * mask
        error_ref[at, :] = error.astype(BF16)
        sums_ref[0:8] += partial_sum(error)
        sums_ref[8:16] += partial_sum(error * scaled)

    write_sums(out_sums_ref, sums_ref, 0, OUTER)


def spread_matrix(grid, small):
    return None if small is None else pool_matrix(grid, small, True)[: grid.line_rows]


def outer_error(slopes, small, grad_ref, matrix, line, lo, hi):
    values = slopes.astype(F32)
    if small is None:
        return values
    coarse = grad_ref[rows_at((line // 2) * small.line_rows, small.line_rows), lo:hi]
    return values * jnp.dot(matrix, coarse, preferred_element_type=F32)


class Lines:
    def __init__(self, grid, sources, buffers, sem_ref):
        self.step = 2 if grid.side % 2 == 0 else 1
        self.size = self.step * grid.line_rows
        self.steps = grid.side // self.step
        self.sources, self.buffers, self.sem = (sources, buffers, sem_ref)

    def copies(self, step):
        at = rows_at(step * self.size, self.size)
        copies = []
        for number, ((ref, lo, hi), (buffer, place)) in enumerate(zip(self.sources, self.buffers)):
            source = ref(step, lo, hi) if callable(ref) else ref.at[at, pl.ds(lo, hi - lo)]
            target = buffer.at[at, pl.ds(place, hi - lo)]
            copies.append(pltpu.make_async_copy(source, target, self.sem.at[number, step]))
        return copies

    def first(self):
        @pl.loop(0, self.steps)
        def _(step):
            for copy in self.copies(step):
                copy.start()

    def run(self, visit):
        @pl.loop(0, self.steps)
        def _(step):
            for copy in self.copies(step):
                copy.wait()
            visit(step)

    @staticmethod
    def semaphores(grid, count):
        return pltpu.SemaphoreType.DMA((count, grid.side // 2 if grid.side % 2 == 0 else grid.side))


def second_back(grid, small, block, slots, length_ref, first_ref, h_far, outer_ref, sums_in_ref, gain_ref, slope_far, *refs):
    first = small is not None
    (grad_ref, carried_ref), refs = (refs[:2], refs[2:]) if first else ((None, None), refs)
    mid_far, few_far, d_far, total_ref, out_ref, *refs = refs
    d_ref, h_ref, slope_ref, mid_ref, few_ref, mid_acc_ref, small_acc_ref, turned_ref, sem_ref, in_sem, out_sem, *refs = refs
    lo, hi = (DIRECT, DIRECT + SECOND)
    at = 0 if first else DIRECT
    lines = Lines(
        grid,
        ((h_far, at, at + SECOND), (slope_far, at, at + SECOND)),
        ((h_ref, 0), (slope_ref, 0)),
        sem_ref,
    )
    lines.first()
    arriving = copies((mid_far, few_far), (mid_ref, few_ref), in_sem)
    for copy in arriving:
        copy.start()
    total = total_of(sums_in_ref)
    total_ref[...] = total
    a, b, c = before_norm(
        gain_ref[block : block + 1, lo:hi], outer_ref[1:2, lo:hi], total[:, lo:hi], outer_ref[2:3, lo:hi]
    )
    mask = grid.mask(grid.line_rows, length_ref[0], SECOND)
    matrix = spread_matrix(grid, small)
    clear_empty(grid, d_ref)
    rows = grid.line_rows
    if first:
        share = out_ref.shape[1] - carried_ref.shape[1]
        for clip in range(out_ref.shape[0]):
            out_ref[clip, share:, :] = carried_ref[clip]

    def visit(step):
        for number in range(lines.step):
            line = step * lines.step + number
            here = rows_at(line * rows, rows)
            scaled = h_ref[here, :].astype(F32)
            error = outer_error(slope_ref[here, :], small, grad_ref, matrix, line, lo, hi)
            back = (a * error - b - c * scaled) * mask
            if grid.copies == 1:
                d_ref[0, rows_at(grid.lead + line * grid.pitch, rows), :] = back.astype(BF16)
            else:
                refs[0][rows_at((line + 1) * rows, rows), :] = back

    lines.run(visit)
    if grid.copies > 1:
        clear_ends(grid, refs[0])

        def store(copy, at, values):
            d_ref[copy, at, :] = values.astype(BF16)

        store_copies(grid, refs[0], store)
    leaving = pltpu.make_async_copy(d_ref, d_far, out_sem.at[0])
    leaving.start()
    for copy in arriving:
        copy.wait()
    kernel_grads(grid, slots, first_ref, mid_ref, few_ref, d_ref, out_ref, mid_acc_ref, small_acc_ref, turned_ref)
    leaving.wait()


def before_norm(gain, inverse, sums, count):
    factor = gain * inverse
    return (factor, factor * sums[0:1] / count, factor * sums[1:2] / count)


def second_back_scratch(grid, slots):
    return [
        pltpu.VMEM((grid.copies, grid.padded, SECOND), BF16),
        pltpu.VMEM((grid.rows, SECOND), BF16),
        pltpu.VMEM((grid.rows, SECOND), BF16),
        pltpu.VMEM((grid.copies, grid.padded, 512), BF16),
        pltpu.VMEM((grid.copies, grid.padded, 128), BF16),
        pltpu.VMEM((slots, 384, 256), F32),
        pltpu.VMEM((slots, 128, 128), F32),
        pltpu.VMEM((MID_IN + 128, 128), F32),
        Lines.semaphores(grid, 2),
        pltpu.SemaphoreType.DMA((2,)),
        pltpu.SemaphoreType.DMA((1,)),
        *([pltpu.VMEM((grid.rows + 2 * grid.line_rows, SECOND), F32)] if grid.copies > 1 else []),
    ]


def conv_back(grid, slots, block, length_ref, d_ref, reduced_ref, reduced_gain_ref, reduced_shift_ref, *refs):
    far_kernels, refs = (refs[:3], refs[3:])
    first = len(refs) > 9
    (x_far, rest_product_ref), refs = (refs[:2], refs[2:]) if first else ((None, None), refs)
    r_ref, out_sums_ref, *refs = refs
    product_out, refs = (refs[0], refs[1:]) if first else (None, refs)
    kernels, (last_ref, acc_ref, sums_ref, in_sem, *refs) = (refs[:3], refs[3:])
    if first:
        x_ref, product_ref, x_sem = refs
        x_copy = pltpu.make_async_copy(x_far, x_ref, x_sem.at[0])
        x_copy.start()
    main_ref, rest_ref, small_ref = kernels
    arriving = copies(far_kernels, kernels, in_sem)
    for copy in arriving:
        copy.start()
    rows = grid.line_rows
    group_rows = grid.group * grid.pitch
    sums_ref[...] = jnp.zeros_like(sums_ref)
    mask = grid.mask(rows, length_ref[0], REDUCED)
    gain, shift = (reduced_gain_ref[block : block + 1], reduced_shift_ref[block : block + 1])
    turned = (((1,), (1,)), ((), ()))
    lane = lax.broadcasted_iota(jnp.int32, (rows, 128), 1)
    wide_lane = lax.broadcasted_iota(jnp.int32, (grid.pitch, 128), 1)

    for copy in range(grid.copies):

        @pl.loop(1 - grid.copies, grid.side)
        def _(line):
            place = grid.lead + line * grid.pitch

            def lanes(start):
                return d_ref[copy, rows_at(start, grid.pitch), 256:384]

            further, here = (lanes(place + grid.pitch).astype(F32), lanes(place).astype(F32))
            at = rows_at(place, grid.pitch)
            last_ref[copy, at, 0:128] = jnp.where(
                wide_lane < 64, further, pltpu.roll(here, 64, 1)
            ).astype(BF16)
            last_ref[copy, at, 128:256] = lanes(place - grid.pitch)

        if grid.copies == 1:
            last_ref[copy, grid.lead - TILE : grid.lead, :] = jnp.zeros((TILE, 256), BF16)
        end = grid.lead + grid.side * grid.pitch
        last_ref[copy, end : end + TILE, :] = jnp.zeros((TILE, 256), BF16)
    for copy in arriving:
        copy.wait()

    @pl.loop(0, grid.side // grid.group)
    def _(group):
        base = grid.lead + group * group_rows
        for tap in range(9):
            part = lax.dot_general(
                near_tap(grid, d_ref, base, tap, -1, group_rows, slice(0, 256)),
                main_ref[tap],
                turned,
                preferred_element_type=F32,
            )
            acc_ref[:, 0:512] = part if tap == 0 else acc_ref[:, 0:512] + part
        for place in range(3):
            acc_ref[:, 0:512] += lax.dot_general(
                grid.near(last_ref, base, 0, 1 - place, group_rows),
                rest_ref[place],
                turned,
                preferred_element_type=F32,
            )
        near = [
            near_tap(grid, d_ref, base, tap, -1, group_rows, slice(384, 512)) for tap in range(9)
        ]
        acc_ref[:, 512:640] = jnp.dot(
            jnp.concatenate(near, axis=1), small_ref[...], preferred_element_type=F32
        )
        for number in range(grid.group):
            line = group * grid.group + number
            lines = slice(number * grid.pitch, number * grid.pitch + rows)
            rest, small = (acc_ref[lines, 384:512], acc_ref[lines, 512:640])
            one = jnp.where(lane < 32, rest, pltpu.roll(small, 32, 1))
            two = jnp.where(lane < 32, pltpu.roll(rest, 96, 1), small)
            three = jnp.where(lane < 32, pltpu.roll(rest, 64, 1), pltpu.roll(small, 96, 1))
            unit = grid.unit
            wide = later(acc_ref[lines, 0:128], unit) + acc_ref[lines, 128:256]
            wide = wide + earlier(acc_ref[lines, 256:384], unit)
            narrow = jnp.where(lane < 64, later(one, unit) + two + earlier(three, unit), 0.0)
            back = jnp.concatenate([wide, narrow], axis=1)
            at = rows_at(line * rows, rows)
            scaled = reduced_ref[at, :].astype(F32)
            error = back * silu_slope(gain * scaled + shift) * mask
            r_ref[at, :] = error.astype(BF16)
            sums_ref[0:8] += partial_sum(error)
            sums_ref[8:16] += partial_sum(error * scaled)

    write_sums(out_sums_ref, sums_ref, 0, REDUCED)
    if first:
        x_copy.wait()
        ones = grid.mask(slots.rows, length_ref[0])
        low_ones = ones.astype(BF16)
        two_ones = jnp.concatenate([ones, ones], axis=1)

        def right_of(start, size):
            at = slice(start, start + size)
            scaled = (reduced_ref[at, :].astype(F32) * two_ones).astype(BF16)
            return jnp.concatenate([r_ref[at, :], scaled, low_ones], axis=1)

        channels = x_ref.shape[1]
        product_ref[0:channels, :] = channel_products(slots, x_ref, right_of)
        product_ref[channels:, :] = jnp.zeros((product_ref.shape[0] - channels, FIRST), F32)
        clips, _, size, _ = product_out.shape
        for clip in range(clips):
            at = slice(clip * size, (clip + 1) * size)
            for tile in range(3):
                product_out[clip, tile] = rest_product_ref[at, 128 * tile : 128 * (tile + 1)]
            for tile in range(5):
                product_out[clip, 3 + tile] = product_ref[at, 128 * tile : 128 * (tile + 1)]


def kernel_grads(grid, slots, first_ref, mid_ref, small_ref, d_ref, out_ref, mid_acc_ref, small_acc_ref, turned_ref):
    group_rows = grid.group * grid.pitch
    mid_acc_ref[...] = jnp.zeros_like(mid_acc_ref)
    small_acc_ref[...] = jnp.zeros_like(small_acc_ref)

    def neighbour(slot):
        return jnp.minimum(first_ref[0] + slot, TAPS - 1) // 9

    @pl.loop(0, grid.side // grid.group)
    def _(group):
        base = grid.lead + group * group_rows
        left = d_ref[0, rows_at(base, group_rows), :].T
        for slot in range(slots):
            tap = lax.rem(jnp.minimum(first_ref[0] + slot, TAPS - 1), 9)
            start = base + (tap // 3 - 1) * grid.pitch
            place = lax.rem(tap, 3) - 1
            copy = 0
            if grid.copies == 1:
                start = start + place * TILE
            else:
                copy = jnp.where(place == 0, 0, 1)
                start = start - jnp.where(place < 0, TILE, 0)
            at = rows_at(start, group_rows)
            lanes = pl.ds(pl.multiple_of(neighbour(slot) * 128, 128), 128)
            right = jnp.concatenate([mid_ref[copy, at, lanes], mid_ref[copy, at, 384:512]], axis=1)
            mid_acc_ref[slot] += jnp.dot(left[0:384], right, preferred_element_type=F32)
            small_acc_ref[slot] += jnp.dot(
                left[384:512], small_ref[copy, at, :], preferred_element_type=F32
            )

    share = round_up(slots * TAP_ROWS, 16 * out_ref.shape[0]) // out_ref.shape[0]

    def put(start, values):
        done = 0
        while done < values.shape[0]:
            clip, at = divmod(start + done, share)
            size = min(values.shape[0] - done, share - at)
            out_ref[clip, at : at + size, :] = values[done : done + size].astype(BF16)
            done = done + size

    half = MID_IN // 2
    for slot in range(slots):
        base = slot * TAP_ROWS
        rest = pl.ds(pl.multiple_of(neighbour(slot) * 32, 32), 32)
        for tile in range(3):
            lines = slice(128 * tile, 128 * (tile + 1))
            turned_ref[0:128, :] = mid_acc_ref[slot, lines, 0:128].T
            turned_ref[MID_IN : MID_IN + 128, :] = mid_acc_ref[slot, lines, 128:256].T
            turned_ref[128:MID_IN, :] = turned_ref[
                pl.ds(pl.multiple_of(MID_IN + neighbour(slot) * 32, 32), 32), :
            ]
            if tile < 2:
                put(base + MID_IN * tile, turned_ref[0:MID_IN, :])
            else:
                folded = turned_ref[0:half, :] + pltpu.roll(turned_ref[half:MID_IN, :], 64, 1)
                put(base + 2 * MID_IN, folded)
        turned_ref[0:128, :] = small_acc_ref[slot].T
        put(base + 2 * MID_IN + half, turned_ref[rest, :])
    used = slots * TAP_ROWS
    put(used, jnp.zeros((share * out_ref.shape[0] - used, 128), F32))


class Spread:
    def __init__(self, grid, plane_ref, across_ref, scale_ref, length):
        self.grid, self.plane, self.across, self.scale = (grid, plane_ref, across_ref, scale_ref)
        clear_edges(grid, plane_ref)
        window = box_window(grid, length)
        scale_ref[0] = box_scale(0, grid.side, window)
        scale_ref[1] = box_scale(1, grid.side, window)
        unit = grid.unit
        edge = jnp.zeros((unit, POOLED), F32)
        across_ref[0:unit, :] = edge
        across_ref[unit + grid.line_rows :, :] = edge

    def put(self, line, values):
        rows = self.grid.line_rows
        inner = jnp.where((line == 0) | (line == self.grid.side - 1), 0, 1)
        values = values * self.scale[inner]
        across, unit = (self.across, self.grid.unit)
        across[unit : unit + rows, :] = values + earlier(values, unit) + later(values, unit)
        self.plane[rows_at((line + 1) * rows, rows), :] = (
            across[0:rows, :] + across[unit : unit + rows, :] + across[2 * unit :, :]
        )

    def get(self, start, size):
        rows = self.grid.line_rows
        return (
            self.plane[rows_at(start, size), :]
            + self.plane[rows_at(start + rows, size), :]
            + self.plane[rows_at(start + 2 * rows, size), :]
        )

    @staticmethod
    def scratch(grid):
        return [
            pltpu.VMEM((grid.rows + 2 * grid.line_rows, POOLED), F32),
            pltpu.VMEM((grid.line_rows + 2 * grid.unit, POOLED), F32),
            pltpu.VMEM((2, grid.line_rows, POOLED), F32),
        ]


def channel_products(slots, x_ref, right_of):
    total = None
    for part in range(slots.parts):
        slot = part * slots.each
        pair = slot - (slots.empty if slot >= slots.gap + slots.empty else 0)
        pair = min(pair, slots.pairs - slots.each)
        product = jnp.dot(
            x_ref[part], right_of(pair * slots.pair_rows, slots.rows), preferred_element_type=F32
        )
        total = product if total is None else total + product
    return total


def rest_constants(outer_ref, total_ref, gain_ref, block):
    pool = OUTER - POOLED

    def pick(ref, lo, hi):
        return jnp.concatenate([ref[lo:hi, 0:DIRECT], ref[lo:hi, pool:]], axis=1)

    return before_norm(
        pick(gain_ref, block, block + 1), pick(outer_ref, 1, 2), pick(total_ref, 0, 2), pick(outer_ref, 2, 3)
    )


def point_back(grid, slots, block, kept, length_ref, place_ref, h_far, outer_ref, total_ref, gain_ref, error_far, reduced_far, r_far, moment_ref, sums_in_ref, reduced_gain_ref, x_far, p_far, *refs):
    pooled_slope_in, pooled_product_in, kept_far, *refs = refs
    dx_ref, dp_ref, reduced_total_ref, outer_sums_ref, *refs = refs
    h_ref, error_ref, reduced_ref, r_ref, x_ref, p_ref, du_ref, acc_ref, *refs = refs
    plane_ref, across_ref, scale_ref, sums_ref, pooled_slope_ref, pooled_product_ref, kept_ref, *refs = refs
    sem_ref, in_sem = refs
    rows = grid.line_rows
    pool = OUTER - POOLED
    lines = Lines(
        grid,
        (
            (h_far, 0, DIRECT),
            (h_far, pool, OUTER),
            (error_far, 0, DIRECT),
            (error_far, pool, OUTER),
            (reduced_far, 0, REDUCED),
            (r_far, 0, REDUCED),
        ),
        ((h_ref, 0), (h_ref, DIRECT), (error_ref, 0), (error_ref, DIRECT), (reduced_ref, 0), (r_ref, 0)),
        sem_ref,
    )
    lines.first()
    kept_rows = kept_ref.shape[1]
    arriving = copies(
        (x_far, p_far, kept_far.at[:, pl.ds(slots.rows, kept_rows), :]), (x_ref, p_ref, kept_ref), in_sem
    )
    for copy in arriving:
        copy.start()
    length = length_ref[0]
    total = total_of(sums_in_ref)
    reduced_total_ref[...] = total
    mid = before_norm(
        reduced_gain_ref[block : block + 1],
        moment_ref[1:2, DIRECT:SECOND],
        total,
        outer_ref[2:3, 0:REDUCED],
    )
    rest = rest_constants(outer_ref, total_ref, gain_ref, block)
    mask = grid.mask(rows, length, DIRECT + POOLED)
    spread = Spread(grid, plane_ref, across_ref, scale_ref, length)

    def visit(line):
        at = rows_at(line * rows, rows)
        back = rest[0] * error_ref[at, :].astype(F32) - rest[1] - rest[2] * h_ref[at, :].astype(F32)
        back = back * mask
        du_ref[at, 0:DIRECT] = back[:, :DIRECT].astype(BF16)
        spread.put(line, back[:, DIRECT:])
        back = mid[0] * r_ref[at, :].astype(F32) - mid[1] - mid[2] * reduced_ref[at, :].astype(F32)
        du_ref[at, DIRECT:SECOND] = (back * mask[:, :REDUCED]).astype(BF16)

    lines.run(visit)
    for copy in arriving:
        copy.wait()
    sums_ref[...] = jnp.zeros_like(sums_ref)
    pooled_slope_ref[:, DIRECT:] = pooled_slope_in[...]
    pooled_product_ref[:, DIRECT:] = pooled_product_in[...]
    for pair in range(slots.pairs):
        slot = pair + (slots.empty if pair >= slots.gap else 0)
        at = slice(pair * rows, (pair + 1) * rows)
        start = slot % slots.each * rows
        values = kept_ref[slot // slots.each, start : start + rows, :]
        pooled_slope_ref[at, 0:DIRECT] = values[:, :DIRECT]
        pooled_product_ref[at, 0:DIRECT] = values[:, DIRECT:]

    @pl.loop(0, grid.side)
    def _(line):
        at = rows_at(line * rows, rows)
        du_ref[at, SECOND:] = (spread.get(line * rows, rows) * mask[:, :POOLED]).astype(BF16)
        dx = jnp.dot(du_ref[at, :], p_ref[...], preferred_element_type=F32).astype(BF16)
        dx_ref[at, :] = dx
        for number, ref in enumerate((pooled_slope_ref, pooled_product_ref)):
            sums_ref[8 * number : 8 * number + 8] += partial_sum(
                dx.astype(F32) * ref[at, :].astype(F32)
            )

    write_sums(outer_sums_ref, sums_ref, 0, OUTER)
    acc_ref[...] = lax.dot_general(
        x_ref[...], du_ref[...], (((0,), (0,)), ((), ())), preferred_element_type=F32
    )
    start = pl.multiple_of(place_ref[0] * kept, 16) if kept < acc_ref.shape[0] else 0
    clips, size, _ = dp_ref.shape
    for tile in range(FIRST // 128):
        values = acc_ref[pl.ds(start, kept), 128 * tile : 128 * (tile + 1)].astype(BF16)
        done = 0
        while done < kept:
            clip, at = divmod(kept * tile + done, size)
            few = min(kept - done, size - at)
            dp_ref[clip, at : at + few, :] = values[done : done + few]
            done = done + few
    used = (FIRST // 128) * kept
    while used < clips * size:
        clip, at = divmod(used, size)
        dp_ref[clip, at:, :] = jnp.zeros((size - at, 128), BF16)
        used = used + size - at


def rest_back(grid, small, slots, block, length_ref, outer_ref, total_ref, gain_ref, grad_ref, h_far, slope_far, kept_far, x_far, du_far, product_ref, *refs):
    h_ref, slope_ref, x_ref, du_ref, plane_ref, across_ref, scale_ref, sem_ref, x_sem, du_sem = refs
    rows = grid.line_rows
    pool = OUTER - POOLED

    def direct(step, lo, hi):
        slot = slots.slot_of(step)
        at = rows_at(lax.rem(slot, slots.each) * slots.pair_rows, slots.pair_rows)
        return kept_far.at[slot // slots.each, at, pl.ds(lo, hi - lo)]

    lines = Lines(
        grid,
        (
            (direct, 0, DIRECT),
            (h_far, SECOND, FIRST),
            (direct, DIRECT, 2 * DIRECT),
            (slope_far, SECOND, FIRST),
        ),
        ((h_ref, 0), (h_ref, DIRECT), (slope_ref, 0), (slope_ref, DIRECT)),
        sem_ref,
    )
    lines.first()
    x_copy = pltpu.make_async_copy(x_far, x_ref, x_sem.at[0])
    x_copy.start()
    length = length_ref[0]
    matrix = spread_matrix(grid, small)
    a, b, c = rest_constants(outer_ref, total_ref, gain_ref, block)
    mask = grid.mask(rows, length, DIRECT + POOLED)
    spread = Spread(grid, plane_ref, across_ref, scale_ref, length)

    def visit(step):
        for number in range(lines.step):
            line = step * lines.step + number
            at = rows_at(line * rows, rows)
            coarse = grad_ref[rows_at((line // 2) * small.line_rows, small.line_rows), :]
            grad = jnp.dot(
                matrix,
                jnp.concatenate([coarse[:, :DIRECT], coarse[:, pool:]], axis=1),
                preferred_element_type=F32,
            )
            back = a * (grad * slope_ref[at, :].astype(F32)) - b - c * h_ref[at, :].astype(F32)
            back = back * mask
            du_ref[at, 0:DIRECT] = back[:, :DIRECT].astype(BF16)
            spread.put(line, back[:, DIRECT:])

    lines.run(visit)
    x_copy.wait()
    wide = lines.size
    pool_mask = grid.mask(wide, length)

    def leaving(step):
        at = rows_at(step * wide, wide)
        return pltpu.make_async_copy(du_ref.at[at, :], du_far.at[at, :], du_sem.at[0])

    @pl.loop(0, lines.steps)
    def _(step):
        at = rows_at(step * wide, wide)
        du_ref[at, DIRECT:] = (spread.get(step * wide, wide) * pool_mask).astype(BF16)
        leaving(step).start()

    channels = x_ref.shape[1]
    product_ref[0:channels, :] = channel_products(
        slots, x_ref, lambda start, size: du_ref[start : start + size, :]
    )
    product_ref[channels:, :] = jnp.zeros((product_ref.shape[0] - channels, DIRECT + POOLED), F32)
    pltpu.make_async_copy(du_ref, du_far, du_sem.at[0]).wait()


def mid_back(grid, block, length_ref, place_ref, moment_ref, sums_in_ref, gain_ref, du_far, h_far, r_far, p_far, dx_far, total_ref, *refs):
    du_ref, h_ref, r_ref, p_ref, dx_ref, sem_ref, p_sem, dx_sem = refs
    lines = Lines(
        grid,
        ((du_far, 0, DIRECT + POOLED), (h_far, 0, REDUCED), (r_far, 0, REDUCED)),
        ((du_ref, 0), (h_ref, 0), (r_ref, 0)),
        sem_ref,
    )
    lines.first()
    p_copy = pltpu.make_async_copy(p_far.at[place_ref[0]], p_ref, p_sem.at[0])
    p_copy.start()
    total = total_of(sums_in_ref)
    total_ref[...] = total
    a, b, c = before_norm(
        gain_ref[block : block + 1], moment_ref[1:2, DIRECT:], total, moment_ref[2:3, DIRECT:]
    )
    mask = grid.mask(lines.size, length_ref[0], REDUCED)
    p_copy.wait()

    def leaving(step):
        at = rows_at(step * lines.size, lines.size)
        return pltpu.make_async_copy(dx_ref.at[at, :], dx_far.at[at, :], dx_sem.at[0])

    def visit(step):
        at = rows_at(step * lines.size, lines.size)
        back = a * r_ref[at, :].astype(F32) - b - c * h_ref[at, :].astype(F32)
        du = jnp.concatenate(
            [du_ref[at, :DIRECT], (back * mask).astype(BF16), du_ref[at, DIRECT:]], axis=1
        )
        dx_ref[at, :] = jnp.dot(du, p_ref[...], preferred_element_type=F32).astype(BF16)
        leaving(step).start()

    lines.run(visit)
    pltpu.make_async_copy(dx_ref, dx_far, dx_sem.at[0]).wait()


def combine(block, pieces_ref, moment_ref, sums_in_ref, gain_ref, out_ref):
    total = total_of(sums_in_ref)
    a, b, c = before_norm(
        gain_ref[block : block + 1], moment_ref[1:2, DIRECT:], total, moment_ref[2:3, DIRECT:]
    )
    size = out_ref.shape[0] // 5
    products = total_of(pieces_ref)
    for tile in range(2):
        out_ref[size * tile : size * (tile + 1), :] = products[tile].astype(BF16)
        lanes = slice(128 * tile, 128 * (tile + 1))
        mid = a[:, lanes] * products[3 + tile] - b[:, lanes] * products[7] - c[:, lanes] * products[5 + tile]
        out_ref[size * (2 + tile) : size * (3 + tile), :] = mid.astype(BF16)
    out_ref[4 * size :, :] = products[2].astype(BF16)


def write_taps(read, slots, mid_ref, small_ref, mid_out, small_out, sem_ref):
    half = MID_IN // 2

    def leaving(tap):
        return (
            pltpu.make_async_copy(mid_ref.at[tap], mid_out.at[tap], sem_ref.at[0]),
            pltpu.make_async_copy(small_ref.at[tap], small_out.at[tap], sem_ref.at[1]),
        )

    for tap in range(TAPS):
        part, slot = divmod(tap, slots)
        base = slot * TAP_ROWS
        folded = read(part, base + 2 * MID_IN, half)
        mid_ref[tap, :, 0:128] = read(part, base, MID_IN)
        mid_ref[tap, :, 128:256] = read(part, base + MID_IN, MID_IN)
        mid_ref[tap, 0:half, 256:320] = folded[:, 0:64]
        mid_ref[tap, half:MID_IN, 256:320] = pltpu.roll(folded, 64, 1)[:, 0:64]
        small_ref[tap] = read(part, base + 2 * MID_IN + half, SMALL_IN)
        for copy in leaving(tap):
            copy.start()
    pltpu.make_async_copy(mid_ref, mid_out, sem_ref.at[0]).wait()
    pltpu.make_async_copy(small_ref, small_out, sem_ref.at[1]).wait()


def write_point(read, parts, kept, point_ref, wide_ref):
    for tile in range(FIRST // 128):
        for part in range(parts):
            start, stop = (kept * part, kept * (part + 1))
            values = read(part, kept * tile, kept)
            if kept * parts == CHANNELS:
                wide_ref[start:stop, :] = values
                continue
            for lo, hi, moved in ((0, 576, 0), (640, OUTER, 64)):
                lo, hi = (max(lo, start), min(hi, stop))
                if lo < hi:
                    wide_ref[lo - moved : hi - moved, :] = values[lo - start : hi - start]
        turned = wide_ref[...].T
        if tile < 3:
            point_ref[128 * tile : 128 * (tile + 1), :] = turned
        elif tile == 3:
            point_ref[384:448, :] = turned[0:64]
        else:
            point_ref[448:576, :] = turned


def copy_out(pairs, sem_ref):
    copies = [
        pltpu.make_async_copy(source, target, sem_ref.at[number])
        for number, (source, target) in enumerate(pairs)
    ]
    for copy in copies:
        copy.start()
    for copy in copies:
        copy.wait()


def share_reader(ref, clips, lo, share):
    def read(part, start, size):
        pieces, done = ([], 0)
        while done < size:
            clip, at = divmod(start + done, share)
            few = min(size - done, share - at)
            pieces.append(ref[part * clips + clip, lo + at : lo + at + few, :].astype(F32))
            done = done + few
        return pieces[0] if len(pieces) == 1 else jnp.concatenate(pieces, axis=0)

    return read


def unpack_second(clips, slots, shares_ref, mid_out, small_out, mid_ref, small_ref, sem_ref):
    read = share_reader(shares_ref, clips, 0, shares_ref.shape[1])
    write_taps(read, slots, mid_ref, small_ref, mid_out.at[1], small_out.at[1], sem_ref)


def unpack_first(parts, clips, slots, share, shares_ref, *refs):
    totals, refs = (refs[:4], refs[4:])
    mid_in, small_in, mid_out, small_out, point_out, gain_out, shift_out, *refs = refs
    mid_ref, small_ref, point_ref, wide_ref, sem_ref = refs
    for block in range(2):
        outer_ref, reduced_ref = totals[2 * block : 2 * block + 2]
        for row, out in enumerate((shift_out, gain_out)):
            at, line = (slice(block, block + 1), slice(row, row + 1))
            out[at, 0:256] = outer_ref[line, 0:256]
            out[at, 256:448] = reduced_ref[line, 0:192]
            out[at, 448:576] = outer_ref[line, 768:896]
            out[at, 576:896] = outer_ref[line, 256:576]
            out[at, 896:1024] = outer_ref[line, 640:768]
    read = share_reader(shares_ref, clips, share, shares_ref.shape[1] - share)
    write_point(read, parts, OUTER // parts, point_ref, wide_ref)
    last = pltpu.make_async_copy(point_ref, point_out.at[1], sem_ref.at[2])
    last.start()
    read = share_reader(shares_ref, clips, 0, share)
    write_taps(read, slots, mid_ref, small_ref, mid_out.at[0], small_out.at[0], sem_ref)
    last.wait()


def unpack_point(parts, clips, kept, place_ref, clip_ref, mine_ref, other_ref, point_in, point_out, buffer_ref, point_ref, wide_ref, sem_ref):
    tiles = FIRST // 128
    size = buffer_ref.shape[2] // clips
    for chip in range(clips // 2):
        for step in range(parts):
            part = lax.rem(place_ref[0] - step + parts, parts)
            for swapped, ref in enumerate((mine_ref, other_ref)):
                owner = clip_ref[0] ^ (2 * chip) ^ swapped
                source = (chip * parts + step) * tiles * size
                for tile in range(tiles):
                    buffer_ref[part, tile, rows_at(owner * size, size), :] = ref[
                        source + tile * size : source + (tile + 1) * size, :
                    ]

    def read(part, start, size):
        tile, at = divmod(start, kept)
        return buffer_ref[part, tile, at : at + size, :].astype(F32)

    write_point(read, parts, kept, point_ref, wide_ref)
    last = pltpu.make_async_copy(point_ref, point_out.at[0], sem_ref.at[0])
    last.start()
    last.wait()


def prepare(parts, mid_in, small_in, point_in, gain_in, shift_in, *refs):
    kernels, (point_ref, second_ref, *vectors) = (refs[:8], refs[8:14])
    for block in range(2):
        main_ref, last_ref, few_ref, back_ref = kernels[4 * block : 4 * block + 4]

        @pl.loop(0, 9)
        def _(tap):
            for number in range(3):
                source = 9 * number + tap
                main_ref[tap, 128 * number : 128 * (number + 1), :] = mid_in[block, source, 0:128, 0:256]
                main_ref[tap, 384 + 32 * number : 416 + 32 * number, :] = mid_in[
                    block, source, 128:MID_IN, 0:256
                ]
            main_ref[tap, 480:512, :] = jnp.zeros((32, 256), BF16)
            small = jnp.concatenate(
                [small_in[block, 9 * number + tap] for number in range(3)]
                + [jnp.zeros((32, 128), BF16)],
                axis=0,
            )
            at = pl.ds(pl.multiple_of(tap * 128, 128), 128)
            few_ref[at, :] = small
            back_ref[at, :] = small.astype(F32).T.astype(BF16)

        @pl.loop(0, 3)
        def _(place):
            for number in range(3):
                for rows, start, size in (
                    (slice(0, 128), 128 * number, 128),
                    (slice(128, MID_IN), 384 + 32 * number, 32),
                ):
                    pieces = [
                        mid_in[block, 9 * number + 3 * line + place, rows, 256:MID_OUT].astype(F32)
                        for line in range(3)
                    ]
                    pieces.append(jnp.zeros((size, 64), F32))
                    last_ref[place, start : start + size, :] = jnp.concatenate(
                        pieces, axis=1
                    ).astype(BF16)
            last_ref[place, 480:512, :] = jnp.zeros((32, 256), BF16)

    own = point_ref.shape[2]
    for lo, hi, at in ((0, 448, 0), (448, SQUEEZED, SECOND)):
        values = point_in[0, lo:hi, :].astype(F32)
        for part in range(parts):
            point_ref[part, at : at + hi - lo, :] = values[:, own * part : own * (part + 1)].astype(
                BF16
            )
        values = point_in[1, lo:hi, :].astype(F32)
        gap = jnp.zeros((hi - lo, 64), F32)
        second_ref[at : at + hi - lo, :] = jnp.concatenate(
            [values[:, :576], gap, values[:, 576:]], axis=1
        ).astype(BF16)
    for part in range(parts):
        point_ref[part, 448:SECOND, :] = jnp.zeros((64, own), BF16)
    second_ref[448:SECOND, :] = jnp.zeros((64, OUTER), BF16)
    for source, outer, reduced in ((gain_in, vectors[0], vectors[1]), (shift_in, vectors[2], vectors[3])):
        outer[:, 0:256] = source[:, 0:256]
        outer[:, 256:576] = source[:, 576:896]
        outer[:, 576:640] = jnp.zeros((2, 64), F32)
        outer[:, 640:768] = source[:, 896:1024]
        outer[:, 768:896] = source[:, 448:576]
        reduced[:, 0:192] = source[:, 256:448]
        reduced[:, 192:256] = jnp.zeros((2, 64), F32)


def round_up(value, unit):
    return -(-value // unit) * unit


def spread_over(values, axis, size):
    received = [values]
    for step in range(1, size):
        perm = [(source, (source + step) % size) for source in range(size)]
        received.append(lax.ppermute(values, axis, perm))
    return received


def after(values, earlier):
    return lax.optimization_barrier((values, earlier))[0]


def exchange(values):
    return lax.all_to_all(values, "dp", 0, 0, tiled=True)


def summed(pieces):
    pieces = exchange(pieces)
    return jnp.sum(pieces.astype(F32), axis=0).astype(BF16)


def gather_chips(column, clips, work=None):
    columns = [column]
    for chip in range(1, clips // 2):
        perm = [(source, source ^ (2 * chip)) for source in range(clips)]
        columns.append(lax.ppermute(column, "dp", perm))
    if work is not None:
        columns = after(columns, work)
    mine = jnp.concatenate(columns, axis=0)
    other = lax.ppermute(mine, "dp", [(source, source ^ 1) for source in range(clips)])
    return (mine, other)


def on_device(frames, lengths, cotangent, pointwise, conv_mid, conv_small, gains, shifts):
    parts = lax.axis_size("branch")
    clips = lax.axis_size("dp")
    place = lax.axis_index("branch").astype(jnp.int32)
    side = frames.shape[2]
    grid, small = (Grid(side, frames.shape[1]), Grid(side // 2, frames.shape[1] // 2))
    slots = Slots(grid, parts)
    cells = side * side
    own_channels = frames.shape[-1]
    length = lengths.astype(jnp.int32)
    half_length = length // 2
    place_one = place.reshape(1)

    own = frames[0].transpose(1, 2, 0, 3).reshape(grid.rows, own_channels)
    turned = call(functools.partial(turn, slots), shape((parts, own_channels, slots.rows), BF16))(own)
    by_pairs = lax.all_to_all(turned, "branch", 0, 0, tiled=True)
    kernel_shapes = (
        shape((9, 512, 256), BF16),
        shape((3, 512, 256), BF16),
        shape((1152, 128), BF16),
        shape((1152, 128), BF16),
    )
    prepared = call(
        functools.partial(prepare, parts),
        (
            *kernel_shapes,
            *kernel_shapes,
            shape((parts, FIRST, own_channels), BF16),
            shape((FIRST, OUTER), BF16),
            shape((2, OUTER), F32),
            shape((2, REDUCED), F32),
            shape((2, OUTER), F32),
            shape((2, REDUCED), F32),
        ),
    )(conv_mid, conv_small, pointwise.swapaxes(1, 2), gains, shifts)
    kernels = (prepared[0:4], prepared[4:8])
    point_first, point_second, outer_gain, reduced_gain, outer_shift, reduced_shift = prepared[8:]

    local_count = (length * (slots.held(place) * 2 * side)).astype(F32)
    mid, pool, direct, sums = call(
        functools.partial(first_pointwise, slots),
        (
            shape((mid_rows(slots), 128), BF16),
            shape((slots.rows + TILE, POOLED), BF16),
            shape((slots.rows, DIRECT), F32),
            shape((clips, 3, SECOND), F32),
        ),
        [pltpu.VMEM((slots.rows, FIRST), F32)],
        scalars=2,
    )(length, local_count, by_pairs, point_first)
    mids = spread_over(mid, "branch", parts)
    sums = spread_over(jnp.sum(exchange(sums), axis=0), "branch", parts)
    pooled_direct, kept_direct, moment = call(
        functools.partial(first_direct, grid, small, slots, 0),
        (
            shape((slots.each * small.line_rows, DIRECT), BF16),
            shape((slots.rows + slots.each * small.line_rows, 2 * DIRECT), BF16),
            shape((3, SECOND), F32),
        ),
        scalars=1,
        cost=3,
    )(length, direct, outer_gain, outer_shift, *sums)
    pool, pooled_direct = after((pool, pooled_direct), mids)
    pools = spread_over(pool, "branch", parts)
    h_reduced, taps_mid, taps_few, e, e_sums = call(
        functools.partial(first_convolve, grid, slots, 0),
        conv_outputs(grid),
        conv_scratch(grid),
        scalars=2,
        cost=40,
        far=range(5 + parts, 8 + parts),
        far_out=range(4),
    )(length, place_one, *mids, moment, reduced_gain, reduced_shift, *kernels[0][:3])
    pooled_directs = spread_over(after(pooled_direct, (pools, e_sums)), "branch", parts)
    q_pool, second_sums = call(
        functools.partial(first_pool, grid, slots),
        (shape((grid.rows, POOLED), F32), shape((clips, 2, FIRST), F32)),
        [
            pltpu.VMEM((grid.rows + 2 * grid.line_rows, POOLED), F32),
            pltpu.VMEM((16, POOLED), F32),
        ],
        scalars=2,
    )(length, place_one, *pools, e_sums)
    second_sums = exchange(second_sums)
    kept_direct = lax.all_gather(after(kept_direct, second_sums), "branch", axis=0)
    pair = 2 * grid.line_rows
    pooled, h_outer, slope, outer, pooled_slope, pooled_product = call(
        functools.partial(first_output, grid, small, 0),
        (
            shape((small.rows, FIRST), BF16),
            shape((grid.rows, FIRST), BF16),
            shape((grid.rows, FIRST), BF16),
            shape((3, OUTER), F32),
            shape((small.rows, FIRST), BF16),
            shape((small.rows, FIRST), BF16),
        ),
        [
            pltpu.VMEM((2, pair, POOLED), F32),
            pltpu.VMEM((2, pair, SECOND), F32),
            pltpu.VMEM((2, pair, FIRST), BF16),
            pltpu.VMEM((2, pair, FIRST), BF16),
            *[pltpu.SemaphoreType.DMA((2,))] * 4,
        ],
        scalars=1,
        far=(1, 2),
        far_out=(1, 2),
    )(
        length,
        q_pool,
        e,
        moment,
        second_sums,
        outer_gain,
        outer_shift,
    )

    small_count = half_length.astype(F32) * float(small.side * small.side)
    q_small, sums_small, pooled = call(
        functools.partial(second_pointwise, small, slots),
        (
            shape((small.rows, FIRST), F32),
            shape((clips, 3, FIRST), F32),
            shape((small.rows, OUTER), BF16),
        ),
        [
            pltpu.VMEM((small.rows + 2 * small.line_rows, POOLED), F32),
            pltpu.VMEM((16, SECOND), F32),
            pltpu.VMEM((16, POOLED), F32),
        ],
        scalars=3,
    )(half_length, place_one, small_count, *pooled_directs, pooled, point_second)
    sums_small = exchange(sums_small)
    h_reduced_small, taps_mid_small, taps_few_small, e_small, e_sums_small, moment_small = call(
        functools.partial(second_convolve, small, 1),
        (*conv_outputs(small, clips), shape((3, FIRST), F32)),
        [*conv_scratch(small), pltpu.VMEM((small.rows + 2 * small.line_rows, REDUCED), F32)],
        scalars=1,
        far=range(5, 8),
        far_out=range(4),
    )(half_length, q_small, sums_small, reduced_gain, reduced_shift, *kernels[1][:3])
    e_sums_small = exchange(e_sums_small)
    cot = cotangent[0].transpose(1, 2, 0, 3).reshape(small.side**2, cotangent.shape[1], CHANNELS)
    act, h_outer_small, error_small, outer_small, outer_sums_small = call(
        functools.partial(second_output, small, 1),
        (
            shape(cot.shape, BF16),
            shape((small.rows, OUTER), BF16),
            shape((small.rows, OUTER), BF16),
            shape((3, OUTER), F32),
            shape((clips, 2, OUTER), F32),
        ),
        [pltpu.VMEM((16, OUTER), F32)],
        scalars=1,
    )(half_length, q_small, e_small, moment_small, e_sums_small, outer_gain, outer_shift, cot)

    taps_each = -(-TAPS // parts)
    tap_share = round_up(taps_each * TAP_ROWS, 16 * clips) // clips
    first_tap = place_one * taps_each

    def conv_back_scratch(at):
        return [
            pltpu.VMEM((9, 512, 256), BF16),
            pltpu.VMEM((3, 512, 256), BF16),
            pltpu.VMEM((1152, 128), BF16),
            pltpu.VMEM((at.copies, at.padded, 256), BF16),
            pltpu.VMEM((at.group * at.pitch, FIRST), F32),
            pltpu.VMEM((16, REDUCED), F32),
            pltpu.SemaphoreType.DMA((3,)),
        ]

    gathered = exchange(outer_sums_small)
    d_low, total_small, packed_small = call(
        functools.partial(second_back, small, None, 1, taps_each),
        (
            shape((small.copies, small.padded, SECOND), BF16),
            shape((2, OUTER), F32),
            shape((clips, tap_share, 128), BF16),
        ),
        second_back_scratch(small, taps_each),
        scalars=2,
        cost=8,
        far=(2, 6, 7, 8),
        far_out=(0,),
    )(
        half_length,
        first_tap,
        h_outer_small,
        outer_small,
        gathered,
        outer_gain,
        error_small,
        taps_mid_small,
        taps_few_small,
    )
    r_low, sums_low = call(
        functools.partial(conv_back, small, None, 1),
        (shape((small.rows, REDUCED), BF16), shape((clips, 2, REDUCED), F32)),
        conv_back_scratch(small),
        scalars=1,
        cost=8,
        far=(5, 6, 7),
    )(
        half_length,
        d_low,
        h_reduced_small,
        reduced_gain,
        reduced_shift,
        *kernels[1][:2],
        kernels[1][3],
    )
    share_small = summed(packed_small)
    sums_low, share_small = lax.optimization_barrier((sums_low, share_small))
    gathered = exchange(sums_low)
    kept = OUTER // parts
    point_share = round_up(kept * (FIRST // 128), 16 * clips) // clips
    coarse_rows = slots.each * small.line_rows
    dx_small, point_packed, reduced_total_small, outer_sums = call(
        functools.partial(point_back, small, slots, 1, kept),
        (
            shape((small.rows, OUTER), BF16),
            shape((clips, point_share, 128), BF16),
            shape((2, REDUCED), F32),
            shape((clips, 2, OUTER), F32),
        ),
        [
            pltpu.VMEM((small.rows, DIRECT + POOLED), BF16),
            pltpu.VMEM((small.rows, DIRECT + POOLED), BF16),
            pltpu.VMEM((small.rows, REDUCED), BF16),
            pltpu.VMEM((small.rows, REDUCED), BF16),
            pltpu.VMEM((small.rows, OUTER), BF16),
            pltpu.VMEM((FIRST, OUTER), BF16),
            pltpu.VMEM((small.rows, FIRST), BF16),
            pltpu.VMEM((OUTER, FIRST), F32),
            *Spread.scratch(small),
            pltpu.VMEM((16, OUTER), F32),
            pltpu.VMEM((small.rows, OUTER), BF16),
            pltpu.VMEM((small.rows, OUTER), BF16),
            pltpu.VMEM((parts, coarse_rows, 2 * DIRECT), BF16),
            Lines.semaphores(small, 6),
            pltpu.SemaphoreType.DMA((3,)),
        ],
        scalars=2,
        cost=10,
        far=(2, 6, 7, 8, 12, 13, 16),
    )(
        half_length,
        place_one,
        h_outer_small,
        outer_small,
        total_small,
        outer_gain,
        error_small,
        h_reduced_small,
        r_low,
        moment_small,
        gathered,
        reduced_gain,
        pooled,
        point_second,
        pooled_slope,
        pooled_product,
        kept_direct,
    )
    whole_small = lax.all_gather(share_small, ("branch", "dp"), axis=0)

    gathered = exchange(outer_sums)
    d_low, total, packed = call(
        functools.partial(second_back, grid, small, 0, taps_each),
        (
            shape((grid.copies, grid.padded, SECOND), BF16),
            shape((2, OUTER), F32),
            shape((clips, tap_share + point_share, 128), BF16),
        ),
        second_back_scratch(grid, taps_each),
        scalars=2,
        cost=18,
        far=(2, 6, 9, 10),
        far_out=(0,),
    )(length, first_tap, h_outer, outer, gathered, outer_gain, slope, dx_small, point_packed, taps_mid, taps_few)
    product_rows = round_up(own_channels, 16 * clips)
    du_rest, rest_product = call(
        functools.partial(rest_back, grid, small, slots, 0),
        (shape((grid.rows, DIRECT + POOLED), BF16), shape((product_rows, DIRECT + POOLED), F32)),
        [
            pltpu.VMEM((grid.rows, DIRECT + POOLED), BF16),
            pltpu.VMEM((grid.rows, DIRECT + POOLED), BF16),
            pltpu.VMEM(turned.shape, BF16),
            pltpu.VMEM((grid.rows, DIRECT + POOLED), BF16),
            *Spread.scratch(grid),
            Lines.semaphores(grid, 4),
            pltpu.SemaphoreType.DMA((1,)),
            pltpu.SemaphoreType.DMA((1,)),
        ],
        scalars=1,
        cost=8,
        far=(5, 6, 7, 8),
        far_out=(0,),
    )(length, outer, after(total, packed), outer_gain, dx_small, h_outer, slope, kept_direct, turned)
    share = summed(packed)
    d_low, share = lax.optimization_barrier((after(d_low, rest_product), share))
    r_low, sums_low, products = call(
        functools.partial(conv_back, grid, slots, 0),
        (
            shape((grid.rows, REDUCED), BF16),
            shape((clips, 2, REDUCED), F32),
            shape((clips, 8, product_rows // clips, 128), F32),
        ),
        [
            *conv_back_scratch(grid),
            pltpu.VMEM(turned.shape, BF16),
            pltpu.VMEM((product_rows, FIRST), F32),
            pltpu.SemaphoreType.DMA((1,)),
        ],
        scalars=1,
        cost=22,
        far=(5, 6, 7, 8),
    )(
        length,
        d_low,
        h_reduced,
        reduced_gain,
        reduced_shift,
        *kernels[0][:2],
        kernels[0][3],
        turned,
        rest_product,
    )
    whole = lax.all_gather(share, ("branch", "dp"), axis=0)
    gathered = exchange(sums_low)
    pieces = exchange(products)
    dx, reduced_total = call(
        functools.partial(mid_back, grid, 0),
        (shape((grid.rows, own_channels), BF16), shape((2, REDUCED), F32)),
        [
            pltpu.VMEM((grid.rows, DIRECT + POOLED), BF16),
            pltpu.VMEM((grid.rows, REDUCED), BF16),
            pltpu.VMEM((grid.rows, REDUCED), BF16),
            pltpu.VMEM((FIRST, own_channels), BF16),
            pltpu.VMEM((grid.rows, own_channels), BF16),
            Lines.semaphores(grid, 3),
            pltpu.SemaphoreType.DMA((1,)),
            pltpu.SemaphoreType.DMA((1,)),
        ],
        scalars=2,
        cost=8,
        far=(5, 6, 7, 8),
        far_out=(0,),
    )(length, place_one, moment, gathered, reduced_gain, du_rest, h_reduced, r_low, point_first)
    outs = (
        shape((2, TAPS, MID_IN, MID_OUT), F32),
        shape((2, TAPS, SMALL_IN, SMALL_OUT), F32),
        shape((2, SQUEEZED, CHANNELS), F32),
    )
    tap_scratch = [
        pltpu.VMEM((TAPS, MID_IN, MID_OUT), F32),
        pltpu.VMEM((TAPS, SMALL_IN, SMALL_OUT), F32),
    ]
    point_scratch = [pltpu.VMEM((SQUEEZED, CHANNELS), F32), pltpu.VMEM((CHANNELS, 128), F32)]
    mid_grad, small_grad = call(
        functools.partial(unpack_second, clips, taps_each),
        outs[:2],
        [*tap_scratch, pltpu.SemaphoreType.DMA((2,))],
        far_out=(0, 1),
        cost=5,
    )(whole_small)
    pieces, mid_grad, small_grad, dx = lax.optimization_barrier((pieces, mid_grad, small_grad, dx))
    point_sum = call(
        functools.partial(combine, 0),
        shape((5 * product_rows // clips, 128), BF16),
        cost=1,
    )(pieces, moment, gathered, reduced_gain)
    received = spread_over(point_sum, "branch", parts)

    norms = shape((2, 1024), F32)
    mid_grad, small_grad, point_grad, gain_grad, shift_grad = call(
        functools.partial(unpack_first, parts, clips, taps_each, tap_share),
        (*outs, norms, norms),
        [*tap_scratch, *point_scratch, pltpu.SemaphoreType.DMA((3,))],
        far_out=(0, 1, 2),
        aliases={5: 0, 6: 1},
        cost=6,
    )(whole, total, reduced_total, total_small, reduced_total_small, mid_grad, small_grad)
    point_mine, point_other = gather_chips(
        jnp.concatenate(received, axis=0), clips, (mid_grad, small_grad)
    )
    clip_one = lax.axis_index("dp").astype(jnp.int32).reshape(1)
    point_grad = call(
        functools.partial(unpack_point, parts, clips, own_channels),
        outs[2],
        [
            pltpu.VMEM((parts, FIRST // 128, product_rows, 128), BF16),
            *point_scratch,
            pltpu.SemaphoreType.DMA((1,)),
        ],
        scalars=2,
        far_out=(0,),
        aliases={4: 0},
        cost=3,
    )(place_one, clip_one, point_mine, point_other, point_grad)
    act = act.reshape(small.side, small.side, cotangent.shape[1], CHANNELS).transpose(2, 0, 1, 3)
    input_grad = dx.reshape(side, side, grid.unit, own_channels).transpose(2, 0, 1, 3)
    return (
        act[None],
        input_grad[None],
        point_grad.swapaxes(1, 2),
        mid_grad,
        small_grad,
        gain_grad,
        shift_grad,
    )


def solution(mesh):
    split = P("dp", None, None, None, "branch")
    whole = P("dp", None, None, None, None)
    return jax.shard_map(
        on_device,
        mesh=mesh,
        in_specs=(split, P("dp"), whole, P(), P(), P(), P(), P()),
        out_specs=(whole, split, P(), P(), P(), P(), P()),
        check_vma=False,
    )
```

```python
import functools

import jax
import jax.numpy as jnp
from jax import lax
from jax.experimental import pallas as pl
from jax.experimental.pallas import tpu as pltpu
from jax.sharding import PartitionSpec as P

DIRECT = 256
MID_IN = 160
MID_OUT = 320
SMALL_IN = 32
SMALL_OUT = 128
TAPS = 27
CHANNELS = 832
SQUEEZED = 576
TILE = 16
REDUCED = 256
POOLED = 128
FIRST = 640
SECOND = 512
OUTER = 896
TAP_ROWS = 432
EPSILON = 1e-05
F32 = jnp.float32
BF16 = jnp.bfloat16
VMEM_BYTES = 58 * 2**20
LARGE = 2200 * 2**10


def call(body, out_shape, scratch=(), scalars=0, cost=5, aliases=None, far=(), far_out=()):
    aliases = aliases or {}

    def large(values):
        size = values.dtype.itemsize
        for extent in values.shape:
            size = size * extent
        return size > LARGE

    def placed(out):
        return pltpu.HBM(out.shape, out.dtype) if large(out) else out

    def run(*operands):
        specs = [
            pl.BlockSpec(
                memory_space=pl.ANY
                if number in aliases or number in far
                else pltpu.SMEM
                if number < scalars
                else pltpu.VMEM
            )
            for number in range(len(operands))
        ]
        operands = [
            pltpu.with_memory_space_constraint(operand, pltpu.HBM) if large(operand) else operand
            for operand in operands
        ]
        if isinstance(out_shape, tuple):
            out_specs = tuple(
                pl.BlockSpec(memory_space=pl.ANY if number in far_out else pltpu.VMEM)
                for number in range(len(out_shape))
            )
        else:
            out_specs = pl.BlockSpec(memory_space=pl.ANY if 0 in far_out else pltpu.VMEM)
        return pl.pallas_call(
            body,
            out_shape=jax.tree.map(placed, out_shape),
            in_specs=specs,
            out_specs=out_specs,
            input_output_aliases=aliases,
            scratch_shapes=list(scratch),
            compiler_params=pltpu.CompilerParams(vmem_limit_bytes=VMEM_BYTES),
            cost_estimate=pl.CostEstimate(
                flops=0, bytes_accessed=int(cost * 3 * 10**6), transcendentals=0
            ),
        )(*operands)

    return run


def shape(dims, dtype):
    return jax.ShapeDtypeStruct(tuple(dims), dtype)


def rows_at(start, size):
    return pl.ds(pl.multiple_of(start, 16), size)


def frames_of(values_or_rows, unit):
    dims = values_or_rows if isinstance(values_or_rows, tuple) else (values_or_rows, 128)
    return lax.broadcasted_iota(jnp.int32, dims, 0) & (unit - 1)


def earlier(values, unit):
    return jnp.where(frames_of(values.shape, unit) > 0, pltpu.roll(values, 1, 0), 0.0)


def later(values, unit):
    rows = values.shape[0]
    shifted = pltpu.roll(values, rows - 1, 0)
    return jnp.where(frames_of(values.shape, unit) < unit - 1, shifted, 0.0)


def plane_box(values, unit):
    across = values + earlier(values, unit) + later(values, unit)
    edge = jnp.zeros((unit, values.shape[1]), values.dtype)
    return (
        across
        + jnp.concatenate([across[unit:], edge], axis=0)
        + jnp.concatenate([edge, across[:-unit]], axis=0)
    )


def box_window(grid, length):
    frame, place = (frames_of(grid.line_rows, grid.unit), grid.places_of(grid.line_rows))

    def one(condition):
        return jnp.where(condition, 1.0, 0.0)

    count = one(frame < length) + one(frame + 1 < length) + one((frame > 0) & (frame - 1 < length))
    return count * (3.0 - one(place == 0) - one(place == grid.side - 1))


def box_scale(line, side, window):
    lines = 3.0 - jnp.where(line == 0, 1.0, 0.0) - jnp.where(line == side - 1, 1.0, 0.0)
    return 1.0 / jnp.maximum(window * lines, 1.0)


def sigmoid(value):
    return 0.5 * jnp.tanh(0.5 * value) + 0.5


def silu(value):
    return value * sigmoid(value)


def silu_slope(value):
    gate = sigmoid(value)
    return gate * (1.0 + value * (1.0 - gate))


def partial_sum(values):
    rows, width = values.shape
    return jnp.sum(values.reshape(rows // 8, 8, width), axis=0)


def moments(total, square, count):
    center = total / count
    return (center, lax.rsqrt(square / count - center * center + EPSILON))


def total_of(gathered):
    count = len(gathered) if isinstance(gathered, (list, tuple)) else gathered.shape[0]
    total = gathered[0][...]
    for number in range(1, count):
        total = total + gathered[number][...]
    return total


def pool_matrix(grid, small, transposed):
    line = grid.line_rows
    few, many = (small.line_rows, 2 * line)
    dims = (many, few) if transposed else (few, many)
    coarse = lax.broadcasted_iota(jnp.int32, dims, 1 if transposed else 0)
    fine = lax.broadcasted_iota(jnp.int32, dims, 0 if transposed else 1)
    fine = jnp.where(fine >= line, fine - line, fine)
    same = (fine >> (grid.bits + 1) == coarse >> small.bits) & (
        (fine & (grid.unit - 1)) >> 1 == coarse & (small.unit - 1)
    )
    return jnp.where(same, 0.125, 0.0).astype(BF16)


class Grid:
    def __init__(self, side, unit):
        self.side, self.unit = (side, unit)
        self.bits = unit.bit_length() - 1
        self.copies = TILE // unit
        self.line_rows = side * unit if self.copies == 1 else (side + 1) * unit
        self.rows = side * self.line_rows
        self.pitch = (side + 1) * unit
        margin = 1 if self.copies == 1 else 2
        self.lead = margin * self.pitch + TILE
        self.padded = (side + 2 * margin) * self.pitch + 2 * TILE
        self.group = 2 if side % 2 == 0 else side

    def places_of(self, rows):
        place = lax.broadcasted_iota(jnp.int32, (rows, 128), 0) >> self.bits
        return place if self.copies == 1 else place & self.side

    def mask(self, rows, length, width=128):
        valid = frames_of(rows, self.unit) < length
        if self.copies > 1:
            valid = valid & (self.places_of(rows) < self.side)
        mask = jnp.where(valid, 1.0, 0.0)
        return jnp.concatenate([mask] * (width // 128), axis=1) if width > 128 else mask

    def near(self, ref, base, lines, places, size, lanes=slice(None)):
        start = base + lines * self.pitch
        if self.copies == 1:
            return ref[0, rows_at(start + places * TILE, size), lanes]
        copy = 0 if places == 0 else 1
        return ref[copy, rows_at(start - (TILE if places < 0 else 0), size), lanes]


class Slots:
    def __init__(self, grid, parts):
        self.pairs = grid.side // 2
        self.parts = parts
        self.each = -(-self.pairs // parts)
        self.empty = parts * self.each - self.pairs
        self.gap = parts * self.each // 2 - 1
        self.pair_rows = 2 * grid.line_rows
        self.grid = grid
        self.rows = self.each * self.pair_rows

    def slot_of(self, pair):
        return pair + jnp.where(pair >= self.gap, self.empty, 0)

    def pair_of(self, slot):
        return slot - jnp.where(slot >= self.gap, self.empty, 0)

    def used(self, slot):
        return (slot < self.gap) | (slot >= self.gap + self.empty)

    def held(self, place):
        count = jnp.zeros((), jnp.int32)
        for number in range(self.each):
            count = count + jnp.where(self.used(place * self.each + number), 1, 0)
        return count


def clear_empty(grid, ref):
    width = ref.shape[2]
    if grid.copies > 1:
        ref[...] = jnp.zeros_like(ref)
        return
    ref[0, 0 : grid.lead, :] = jnp.zeros((grid.lead, width), ref.dtype)
    end = grid.lead + grid.side * grid.pitch
    ref[0, end:, :] = jnp.zeros((ref.shape[1] - end, width), ref.dtype)

    @pl.loop(0, grid.side)
    def _(line):
        at = rows_at(grid.lead + line * grid.pitch + grid.line_rows, TILE)
        ref[0, at, :] = jnp.zeros((TILE, width), ref.dtype)


def store_taps(unit, mid_ref, small_ref, copy, at, act):
    before, after_ = (earlier(act, unit), later(act, unit))
    mid_ref[copy, at, 0:128] = before[:, :128].astype(BF16)
    mid_ref[copy, at, 128:256] = act[:, :128].astype(BF16)
    mid_ref[copy, at, 256:384] = after_[:, :128].astype(BF16)
    before, act, after_ = (before[:, 128:], act[:, 128:], after_[:, 128:])
    lane = lax.broadcasted_iota(jnp.int32, act.shape, 1)
    mid_ref[copy, at, 384:512] = jnp.where(
        lane < 32, before, jnp.where(lane < 64, pltpu.roll(act, 32, 1), pltpu.roll(after_, 64, 1))
    ).astype(BF16)
    small_ref[copy, at, :] = jnp.where(
        lane < 32, pltpu.roll(before, 96, 1), jnp.where(lane < 64, act, pltpu.roll(after_, 32, 1))
    ).astype(BF16)


def near_tap(grid, ref, base, tap, sign, size, lanes=slice(None)):
    return grid.near(ref, base, sign * (tap // 3 - 1), sign * (tap % 3 - 1), size, lanes)


def convolve(grid, taps, kernels, rest_ref, acc_ref, stage_ref, e_ref, stage_sem, sums_ref, length):
    mid_ref, small_ref = taps
    main_ref, last_ref, small_kernel_ref = kernels
    group_rows = grid.group * grid.pitch
    stage_rows = grid.group * grid.line_rows
    groups = grid.side // grid.group
    sums_ref[...] = jnp.zeros_like(sums_ref)
    mask = grid.mask(grid.line_rows, length, SECOND)
    edge = jnp.zeros((grid.pitch, 256), F32)
    rest_ref[grid.lead - grid.pitch : grid.lead, :] = edge
    end = grid.lead + grid.side * grid.pitch
    rest_ref[end : end + grid.pitch, :] = edge

    @pl.loop(0, groups)
    def _(group):
        base = grid.lead + group * group_rows
        total = None
        for place in range(3):
            part = jnp.dot(
                grid.near(mid_ref, base, 0, place - 1, group_rows),
                last_ref[place],
                preferred_element_type=F32,
            )
            total = part if total is None else total + part
        rest_ref[rows_at(base, group_rows), :] = total

    lane = lax.broadcasted_iota(jnp.int32, (grid.line_rows, 128), 1)

    def staged(group, slot):
        return pltpu.make_async_copy(
            stage_ref.at[slot],
            e_ref.at[rows_at(group * stage_rows, stage_rows), :],
            stage_sem.at[slot],
        )

    @pl.loop(0, groups)
    def _(group):
        base = grid.lead + group * group_rows
        slot = lax.rem(group, 2)
        for tap in range(9):
            part = jnp.dot(
                near_tap(grid, mid_ref, base, tap, 1, group_rows),
                main_ref[tap],
                preferred_element_type=F32,
            )
            acc_ref[:, 0:256] = part if tap == 0 else acc_ref[:, 0:256] + part
        near = [near_tap(grid, small_ref, base, tap, 1, group_rows) for tap in range(9)]
        acc_ref[:, 256:384] = jnp.dot(
            jnp.concatenate(near, axis=1), small_kernel_ref[...], preferred_element_type=F32
        )

        @pl.when(group >= 2)
        def _():
            staged(group - 2, slot).wait()

        for number in range(grid.group):
            rows = grid.line_rows
            start = base + number * grid.pitch
            last = (
                rest_ref[rows_at(start - grid.pitch, rows), 0:128]
                + pltpu.roll(rest_ref[rows_at(start, rows), 0:128], 64, 1)
                + rest_ref[rows_at(start + grid.pitch, rows), 128:256]
            )
            lines = slice(number * grid.pitch, number * grid.pitch + rows)
            values = jnp.concatenate(
                [acc_ref[lines, 0:256], jnp.where(lane < 64, last, 0.0), acc_ref[lines, 256:384]],
                axis=1,
            )
            stage_ref[slot, number * rows : (number + 1) * rows, :] = values
            masked = values * mask
            sums_ref[0:8] += partial_sum(masked)
            sums_ref[8:16] += partial_sum(masked * values)
        staged(group, slot).start()

    for group in range(max(groups - 2, 0), groups):
        staged(group, group % 2).wait()


def conv_scratch(grid):
    group_rows = grid.group * grid.pitch
    return [
        pltpu.VMEM((9, 512, 256), BF16),
        pltpu.VMEM((3, 512, 256), BF16),
        pltpu.VMEM((1152, 128), BF16),
        pltpu.VMEM((grid.copies, grid.padded, 512), BF16),
        pltpu.VMEM((grid.copies, grid.padded, 128), BF16),
        pltpu.VMEM((grid.rows, REDUCED), BF16),
        pltpu.VMEM((grid.padded, 256), F32),
        pltpu.VMEM((group_rows, 384), F32),
        pltpu.VMEM((2, grid.group * grid.line_rows, SECOND), F32),
        pltpu.VMEM((16, SECOND), F32),
        pltpu.SemaphoreType.DMA((3,)),
        pltpu.SemaphoreType.DMA((3,)),
        pltpu.SemaphoreType.DMA((2,)),
    ]


def conv_outputs(grid, *clips):
    return (
        shape((grid.rows, REDUCED), BF16),
        shape((grid.copies, grid.padded, 512), BF16),
        shape((grid.copies, grid.padded, 128), BF16),
        shape((grid.rows, SECOND), F32),
        shape((*clips, 2, SECOND), F32),
    )


def copies(sources, targets, sem_ref):
    return [
        pltpu.make_async_copy(source, target, sem_ref.at[number])
        for number, (source, target) in enumerate(zip(sources, targets))
    ]


def run_convolution(grid, length, far_kernels, outputs, scratch, fill):
    h_out, mid_out, small_out, e_out, sums_out = outputs
    kernels, (mid_ref, small_ref, h_ref), rest = (scratch[:3], scratch[3:6], scratch[6:])
    rest_ref, acc_ref, stage_ref, sums_ref, in_sem, out_sem, stage_sem = rest
    arriving = copies(far_kernels, kernels, in_sem)
    for copy in arriving:
        copy.start()
    clear_empty(grid, mid_ref)
    clear_empty(grid, small_ref)
    fill(h_ref, mid_ref, small_ref)
    leaving = copies((mid_ref, small_ref, h_ref), (mid_out, small_out, h_out), out_sem)
    for copy in leaving:
        copy.start()
    for copy in arriving:
        copy.wait()
    convolve(
        grid, (mid_ref, small_ref), kernels, rest_ref, acc_ref, stage_ref, e_out, stage_sem, sums_ref, length
    )
    write_sums(sums_out, sums_ref, 0, SECOND)
    for copy in leaving:
        copy.wait()


def write_row(out_ref, row, lo, hi, values):
    if len(out_ref.shape) == 2:
        out_ref[row : row + 1, lo:hi] = values
    else:
        for clip in range(out_ref.shape[0]):
            out_ref[clip, row : row + 1, lo:hi] = values


def write_sums(out_ref, sums_ref, lo, hi):
    for number in range(2):
        values = jnp.sum(sums_ref[8 * number : 8 * number + 8], axis=0, keepdims=True)
        write_row(out_ref, number, lo, hi, values)


def turn(slots, x_ref, out_ref):
    for slot in range(slots.parts * slots.each):
        part, number = divmod(slot, slots.each)
        lanes = slice(number * slots.pair_rows, (number + 1) * slots.pair_rows)
        if slots.gap <= slot < slots.gap + slots.empty:
            out_ref[part, :, lanes] = jnp.zeros((out_ref.shape[1], slots.pair_rows), BF16)
            continue
        pair = slot - (slots.empty if slot >= slots.gap else 0)
        rows = slice(pair * slots.pair_rows, (pair + 1) * slots.pair_rows)
        out_ref[part, :, lanes] = x_ref[rows, :].T


def first_pointwise(slots, length_ref, count_ref, x_ref, p_ref, mid_ref, pool_ref, direct_ref, sums_ref, u_ref):
    rows, step = (slots.rows, 112)
    length, count = (length_ref[0], count_ref[0])
    for part in range(slots.parts):
        product = lax.dot_general(
            x_ref[part], p_ref[part], (((0,), (1,)), ((), ())), preferred_element_type=F32
        )
        u_ref[...] = product if part == 0 else u_ref[...] + product
    mask = slots.grid.mask(step, length, FIRST)

    def summed(number, carry):
        values = u_ref[rows_at(number * step, step), :] * mask
        u_ref[rows_at(number * step, step), :] = values
        few = values[:, :SECOND]
        return (carry[0] + partial_sum(values), carry[1] + partial_sum(few * few))

    zero = (jnp.zeros((8, FIRST), F32), jnp.zeros((8, SECOND), F32))
    total, square = lax.fori_loop(0, rows // step, summed, zero)
    total = jnp.sum(total, axis=0, keepdims=True)
    write_row(sums_ref, 0, 0, SECOND, total[:, :SECOND])
    write_row(sums_ref, 1, 0, SECOND, jnp.sum(square, axis=0, keepdims=True))
    write_row(sums_ref, 2, 0, SECOND, jnp.full((1, SECOND), count, F32))
    offset = (total / jnp.full((1, FIRST), jnp.maximum(count, 1.0), F32)).astype(BF16)
    wide_offset = offset.astype(F32)
    tail = jnp.broadcast_to(wide_offset, (TILE, FIRST)).astype(BF16)
    pool_ref[rows : rows + TILE, :] = tail[:, SECOND:]
    shared = mid_ref.shape[0] - 2 * TILE
    mid_ref[shared : shared + TILE, :] = tail[:, 256:384]
    mid_ref[shared + TILE :, :] = tail[:, 384:512]

    @pl.loop(0, rows // step)
    def _(number):
        at = rows_at(number * step, step)
        values = u_ref[at, :]
        direct_ref[at, :] = values[:, :DIRECT]
        values = values[:, DIRECT:] - wide_offset[:, DIRECT:]
        mid_ref[at, :] = values[:, :128].astype(BF16)
        pool_ref[at, :] = values[:, 256:].astype(BF16)

    lane = lax.broadcasted_iota(jnp.int32, (step, 128), 1)
    for couple in range(0, slots.each, 2):

        @pl.loop(0, slots.pair_rows // step)
        def _(number):
            start = couple * slots.pair_rows + number * step
            values = u_ref[rows_at(start, step), 384:512] - wide_offset[:, 384:512]
            if couple + 1 < slots.each:
                other = u_ref[rows_at(start + slots.pair_rows, step), 384:512]
                other = pltpu.roll(other - wide_offset[:, 384:512], 64, 1)
                values = jnp.where(lane < 64, values, other)
            place = rows + couple // 2 * slots.pair_rows + number * step
            mid_ref[rows_at(place, step), :] = values.astype(BF16)


def mid_rows(slots):
    return slots.rows + -(-slots.each // 2) * slots.pair_rows + 2 * TILE


def each_pair(slots, place, refs, visit):
    for step, ref in enumerate(refs):
        source = lax.rem(place - step + slots.parts, slots.parts)
        for number in range(slots.each):
            slot = source * slots.each + number

            @pl.when(slots.used(slot))
            def _():
                visit(slots.pair_of(slot), ref, number)


def set_moments(total, moment_ref):
    count = total[2:3]
    center, inverse = moments(total[0:1], total[1:2], count)
    moment_ref[0:1, :] = center
    moment_ref[1:2, :] = inverse
    moment_ref[2:3, :] = count
    return (center, inverse)


def first_convolve(grid, slots, block, length_ref, place_ref, *refs):
    parts = slots.parts
    mids, sums, refs = (refs[:parts], refs[parts : 2 * parts], refs[2 * parts :])
    gain_ref, shift_ref, *refs = refs
    far_kernels, outputs, scratch = (refs[:3], refs[3:8], refs[8:])
    length = length_ref[0]
    total = total_of(sums)[:, DIRECT:]
    center, inverse = moments(total[0:1], total[1:2], total[2:3])
    gain, shift = (gain_ref[block : block + 1], shift_ref[block : block + 1])
    step = 112
    mask = grid.mask(step, length, REDUCED)
    lane = lax.broadcasted_iota(jnp.int32, (step, 128), 1)

    def fill(h_ref, mid_ref, small_ref):
        def visit(pair, ref, number):
            shared = ref.shape[0] - 2 * TILE
            offset = jnp.concatenate(
                [
                    ref[at : at + TILE, :].astype(F32)[0:1]
                    for at in (shared, shared + TILE)
                ],
                axis=1,
            )
            other = slots.rows + number // 2 * slots.pair_rows

            @pl.loop(0, slots.pair_rows // step)
            def _(chunk):
                values = ref[rows_at(number * slots.pair_rows + chunk * step, step), :].astype(F32)
                few = ref[rows_at(other + chunk * step, step), :].astype(F32)
                if number % 2 == 1:
                    few = pltpu.roll(few, 64, 1)
                few = jnp.where(lane < 64, few, 0.0)
                values = jnp.concatenate([values, few], axis=1) + offset
                scaled = (values - center) * inverse
                row = pair * slots.pair_rows + chunk * step
                h_ref[rows_at(row, step), :] = scaled.astype(BF16)
                act = silu(gain * scaled + shift) * mask
                line = row // grid.line_rows
                at = grid.lead + line * grid.pitch + row - line * grid.line_rows
                store_taps(grid.unit, mid_ref, small_ref, 0, rows_at(at, step), act)

        each_pair(slots, place_ref[0], mids, visit)

    run_convolution(grid, length, far_kernels, outputs, scratch, fill)


def pool_planes(grid, plane_ref, q_ref, lo, sums_ref, length, window):
    rows = grid.line_rows
    mask = grid.mask(rows, length)
    sums_ref[...] = jnp.zeros_like(sums_ref)

    @pl.loop(0, grid.side)
    def _(line):
        start = line * rows
        values = (
            plane_ref[rows_at(start, rows), :]
            + plane_ref[rows_at(start + rows, rows), :]
            + plane_ref[rows_at(start + 2 * rows, rows), :]
        ) * box_scale(line, grid.side, window)
        q_ref[rows_at(start, rows), lo : lo + POOLED] = values
        masked = values * mask
        sums_ref[0:8] += partial_sum(masked)
        sums_ref[8:16] += partial_sum(masked * values)


def clear_edges(grid, plane_ref):
    rows = grid.line_rows
    plane_ref[0:rows] = jnp.zeros((rows, POOLED), F32)
    plane_ref[grid.rows + rows : grid.rows + 2 * rows] = jnp.zeros((rows, POOLED), F32)


def first_pool(grid, slots, length_ref, place_ref, *refs):
    pools, refs = (refs[: slots.parts], refs[slots.parts :])
    e_sums_ref, q_ref, out_sums_ref, plane_ref, sums_ref = refs
    length = length_ref[0]
    rows = grid.line_rows
    for row in range(2):
        write_row(out_sums_ref, row, 0, SECOND, e_sums_ref[row : row + 1, :])
    clear_edges(grid, plane_ref)

    def visit(pair, ref, number):
        offset = ref[slots.rows : slots.rows + TILE, :].astype(F32)[0:1]
        for line in range(2):
            at = rows_at(number * slots.pair_rows + line * rows, rows)
            plane_ref[rows_at((2 * pair + line + 1) * rows, rows), :] = plane_box(
                ref[at, :].astype(F32) + offset, grid.unit
            )

    each_pair(slots, place_ref[0], pools, visit)
    pool_planes(grid, plane_ref, q_ref, 0, sums_ref, length, box_window(grid, length))
    write_sums(out_sums_ref, sums_ref, SECOND, FIRST)


def normalize(values, center, inverse, gain, shift, mask):
    scaled = (values - center) * inverse
    shifted = gain * scaled + shift
    gate = sigmoid(shifted)
    gate_mask = gate * mask
    act = shifted * gate_mask
    return (scaled, act, gate_mask + act * (1.0 - gate))


def pool_pieces(matrix, pieces):
    return jnp.dot(
        matrix, jnp.concatenate(pieces, axis=0), preferred_element_type=F32
    ).astype(BF16)


def first_direct(grid, small, slots, block, length_ref, u_ref, gain_ref, shift_ref, *refs):
    sums, (pooled_ref, kept_ref, moment_ref) = (refs[: slots.parts], refs[slots.parts :])
    rows = grid.line_rows
    mask = grid.mask(rows, length_ref[0], DIRECT)
    center, inverse = set_moments(total_of(sums), moment_ref)
    center, inverse = (center[:, :DIRECT], inverse[:, :DIRECT])
    gain, shift = (gain_ref[block : block + 1, :DIRECT], shift_ref[block : block + 1, :DIRECT])
    matrix = pool_matrix(grid, small, False)

    @pl.loop(0, slots.each)
    def _(number):
        acts, slopes, products = ([], [], [])
        for line in range(2):
            at = rows_at(number * slots.pair_rows + line * rows, rows)
            scaled, act, slope = normalize(u_ref[at, :], center, inverse, gain, shift, mask)
            kept_ref[at, 0:DIRECT] = scaled.astype(BF16)
            kept_ref[at, DIRECT : 2 * DIRECT] = slope.astype(BF16)
            acts.append(act.astype(BF16))
            slopes.append(slope.astype(BF16))
            products.append((slope * scaled).astype(BF16))
        size = small.line_rows
        pooled_ref[rows_at(number * size, size), :] = pool_pieces(matrix, acts)
        at = rows_at(slots.rows + number * size, size)
        kept_ref[at, 0:DIRECT] = pool_pieces(matrix, slopes)
        kept_ref[at, DIRECT : 2 * DIRECT] = pool_pieces(matrix, products)


def outer_moments(center, inverse, count, outer_ref):
    outer_ref[0:1, :] = center
    outer_ref[1:2, :] = inverse
    outer_ref[2:3, :] = jnp.concatenate([count[:, 0:128]] * (OUTER // 128), axis=1)


def first_output(grid, small, block, length_ref, q_far, e_far, moment_ref, sums_in_ref, gain_ref, shift_ref, *refs):
    pooled_ref, h_far, slope_far, outer_ref, pooled_slope_ref, pooled_product_ref, *refs = refs
    q_ref, e_ref, h_ref, slope_ref, q_sem, e_sem, h_sem, slope_sem = refs
    rows = grid.line_rows
    wide = 2 * rows
    pairs = grid.side // 2

    def arriving(pair, slot):
        at = rows_at(pair * wide, wide)
        return [
            pltpu.make_async_copy(q_far.at[at, :], q_ref.at[slot], q_sem.at[slot]),
            pltpu.make_async_copy(e_far.at[at, :], e_ref.at[slot], e_sem.at[slot]),
        ]

    def leaving(pair, slot):
        at = rows_at(pair * wide, wide)
        return [
            pltpu.make_async_copy(h_ref.at[slot], h_far.at[at, :], h_sem.at[slot]),
            pltpu.make_async_copy(slope_ref.at[slot], slope_far.at[at, :], slope_sem.at[slot]),
        ]

    for copy in arriving(0, 0):
        copy.start()
    mask = grid.mask(rows, length_ref[0], FIRST)
    total = total_of(sums_in_ref)
    count = jnp.concatenate([moment_ref[2:3, 0:128]] * (FIRST // 128), axis=1)
    center, inverse = moments(total[0:1], total[1:2], count)
    outer_moments(
        jnp.concatenate([moment_ref[0:1, :DIRECT], center], axis=1),
        jnp.concatenate([moment_ref[1:2, :DIRECT], inverse], axis=1),
        count,
        outer_ref,
    )
    matrix = pool_matrix(grid, small, False)
    gain, shift = (gain_ref[block : block + 1, DIRECT:], shift_ref[block : block + 1, DIRECT:])

    @pl.loop(0, pairs)
    def _(pair):
        slot = lax.rem(pair, 2)

        @pl.when(pair + 1 < pairs)
        def _():
            for copy in arriving(pair + 1, 1 - slot):
                copy.start()

        for copy in arriving(pair, slot):
            copy.wait()

        @pl.when(pair >= 2)
        def _():
            for copy in leaving(pair - 2, slot):
                copy.wait()

        acts, slopes, products = ([], [], [])
        for number in range(2):
            lines = slice(number * rows, (number + 1) * rows)
            values = jnp.concatenate([e_ref[slot, lines, :], q_ref[slot, lines, :]], axis=1)
            scaled, act, slope = normalize(values, center, inverse, gain, shift, mask)
            h_ref[slot, lines, :] = scaled.astype(BF16)
            low_slope = slope.astype(BF16)
            slope_ref[slot, lines, :] = low_slope
            acts.append(act.astype(BF16))
            slopes.append(low_slope)
            products.append((slope * scaled).astype(BF16))
        for copy in leaving(pair, slot):
            copy.start()
        at = rows_at(pair * small.line_rows, small.line_rows)
        pooled_ref[at, :] = pool_pieces(matrix, acts)
        pooled_slope_ref[at, :] = pool_pieces(matrix, slopes)
        pooled_product_ref[at, :] = pool_pieces(matrix, products)

    for pair in range(max(pairs - 2, 0), pairs):
        for copy in leaving(pair, pair % 2):
            copy.wait()


def second_pointwise(grid, slots, length_ref, place_ref, count_ref, *refs):
    directs, refs = (refs[: slots.parts], refs[slots.parts :])
    rest_ref, p_ref, q_ref, out_sums_ref, x_ref, plane_ref, sums_ref, pool_sums_ref = refs
    length = length_ref[0]
    rows = grid.line_rows
    sums_ref[...] = jnp.zeros_like(sums_ref)
    clear_edges(grid, plane_ref)
    x_ref[:, DIRECT:] = rest_ref[...]

    def visit(pair, ref, number):
        x_ref[rows_at(pair * rows, rows), 0:DIRECT] = ref[number * rows : (number + 1) * rows, :]

    each_pair(slots, place_ref[0], directs, visit)
    q_ref[...] = lax.dot_general(
        x_ref[...], p_ref[...], (((1,), (1,)), ((), ())), preferred_element_type=F32
    )

    @pl.loop(0, grid.side)
    def _(line):
        values = q_ref[rows_at(line * rows, rows), :]
        sums_ref[0:8] += partial_sum(values[:, :SECOND])
        sums_ref[8:16] += partial_sum(values[:, :SECOND] * values[:, :SECOND])
        plane_ref[rows_at((line + 1) * rows, rows), :] = plane_box(
            values[:, SECOND:], grid.unit
        )

    pool_planes(grid, plane_ref, q_ref, SECOND, pool_sums_ref, length, box_window(grid, length))
    write_sums(out_sums_ref, sums_ref, 0, SECOND)
    write_sums(out_sums_ref, pool_sums_ref, SECOND, FIRST)
    write_row(out_sums_ref, 2, 0, FIRST, jnp.full((1, FIRST), count_ref[0], F32))


def clear_ends(grid, ref):
    edge = jnp.zeros((grid.line_rows, ref.shape[1]), F32)
    ref[0 : grid.line_rows, :] = edge
    ref[grid.rows + grid.line_rows :, :] = edge


def store_copies(grid, ref, store):
    @pl.loop(0, grid.side + 1)
    def _(number):
        start = number * grid.line_rows
        at = rows_at(grid.lead + (number - 1) * grid.pitch, grid.line_rows)
        store(0, at, ref[rows_at(start, grid.line_rows), :])
        moved = pl.ds(pl.multiple_of(start + grid.unit, grid.unit), grid.line_rows)
        store(1, at, ref[moved, :])


def second_convolve(grid, block, length_ref, q_ref, sums_in_ref, gain_ref, shift_ref, *refs):
    far_kernels, outputs, moment_ref, scratch = (refs[:3], refs[3:8], refs[8], refs[9:])
    length = length_ref[0]
    center, inverse = set_moments(total_of(sums_in_ref), moment_ref)
    center, inverse = (center[:, DIRECT:SECOND], inverse[:, DIRECT:SECOND])
    gain, shift = (gain_ref[block : block + 1], shift_ref[block : block + 1])
    rows = grid.line_rows
    mask = grid.mask(rows, length, REDUCED)
    scratch, act_ref = (scratch[:-1], scratch[-1])

    def fill(h_ref, mid_ref, small_ref):
        clear_ends(grid, act_ref)

        @pl.loop(0, grid.side)
        def _(line):
            at = rows_at(line * rows, rows)
            scaled = (q_ref[at, DIRECT:SECOND] - center) * inverse
            h_ref[at, :] = scaled.astype(BF16)
            act_ref[rows_at((line + 1) * rows, rows), :] = silu(gain * scaled + shift) * mask

        def store(copy, at, values):
            store_taps(grid.unit, mid_ref, small_ref, copy, at, values)

        store_copies(grid, act_ref, store)

    run_convolution(grid, length, far_kernels, outputs, scratch, fill)


def second_output(grid, block, length_ref, q_ref, e_ref, moment_ref, sums_in_ref, gain_ref, shift_ref, cot_ref, act_ref, h_ref, error_ref, outer_ref, out_sums_ref, sums_ref):
    rows = grid.line_rows
    side, frames = (grid.side, cot_ref.shape[1])
    mask = grid.mask(rows, length_ref[0], OUTER)
    total = total_of(sums_in_ref)
    count = moment_ref[2:3, 0:SECOND]
    center, inverse = moments(total[0:1], total[1:2], count)
    center = jnp.concatenate([moment_ref[0:1, :DIRECT], center, moment_ref[0:1, SECOND:]], axis=1)
    inverse = jnp.concatenate([moment_ref[1:2, :DIRECT], inverse, moment_ref[1:2, SECOND:]], axis=1)
    outer_moments(center, inverse, count, outer_ref)
    sums_ref[...] = jnp.zeros_like(sums_ref)
    gain, shift = (gain_ref[block : block + 1], shift_ref[block : block + 1])
    gap = jnp.zeros((rows, 64), F32)
    unused = jnp.zeros((grid.unit, CHANNELS), F32)

    @pl.loop(0, side)
    def _(line):
        at = rows_at(line * rows, rows)
        places = pl.ds(line * side, side)
        values = jnp.concatenate([q_ref[at, :DIRECT], e_ref[at, :], q_ref[at, SECOND:]], axis=1)
        scaled = (values - center) * inverse
        h_ref[at, :] = scaled.astype(BF16)
        shifted = gain * scaled + shift
        gate = sigmoid(shifted)
        act = (shifted * gate * mask).reshape(side + 1, frames, OUTER)[:side].astype(BF16)
        act_ref[places, :, 0:576] = act[:, :, 0:576]
        act_ref[places, :, 576:CHANNELS] = act[:, :, 640:OUTER]
        slope = gate * (1.0 + shifted * (1.0 - gate))
        grad = cot_ref[places].astype(F32).reshape(side * frames, CHANNELS)
        grad = jnp.concatenate([grad, unused], axis=0)
        grad = jnp.concatenate([grad[:, :576], gap, grad[:, 576:]], axis=1)
        error = grad * slope * mask
        error_ref[at, :] = error.astype(BF16)
        sums_ref[0:8] += partial_sum(error)
        sums_ref[8:16] += partial_sum(error * scaled)

    write_sums(out_sums_ref, sums_ref, 0, OUTER)


def spread_matrix(grid, small):
    return None if small is None else pool_matrix(grid, small, True)[: grid.line_rows]


def outer_error(slopes, small, grad_ref, matrix, line, lo, hi):
    values = slopes.astype(F32)
    if small is None:
        return values
    coarse = grad_ref[rows_at((line // 2) * small.line_rows, small.line_rows), lo:hi]
    return values * jnp.dot(matrix, coarse, preferred_element_type=F32)


class Lines:
    def __init__(self, grid, sources, buffers, sem_ref):
        self.step = 2 if grid.side % 2 == 0 else 1
        self.size = self.step * grid.line_rows
        self.steps = grid.side // self.step
        self.sources, self.buffers, self.sem = (sources, buffers, sem_ref)

    def copies(self, step):
        at = rows_at(step * self.size, self.size)
        copies = []
        for number, ((ref, lo, hi), (buffer, place)) in enumerate(zip(self.sources, self.buffers)):
            source = ref(step, lo, hi) if callable(ref) else ref.at[at, pl.ds(lo, hi - lo)]
            target = buffer.at[at, pl.ds(place, hi - lo)]
            copies.append(pltpu.make_async_copy(source, target, self.sem.at[number, step]))
        return copies

    def first(self):
        @pl.loop(0, self.steps)
        def _(step):
            for copy in self.copies(step):
                copy.start()

    def run(self, visit):
        @pl.loop(0, self.steps)
        def _(step):
            for copy in self.copies(step):
                copy.wait()
            visit(step)

    @staticmethod
    def semaphores(grid, count):
        return pltpu.SemaphoreType.DMA((count, grid.side // 2 if grid.side % 2 == 0 else grid.side))


def second_back(grid, small, block, slots, length_ref, first_ref, h_far, outer_ref, sums_in_ref, gain_ref, slope_far, *refs):
    first = small is not None
    (grad_ref, carried_ref), refs = (refs[:2], refs[2:]) if first else ((None, None), refs)
    mid_far, few_far, d_far, total_ref, out_ref, *refs = refs
    d_ref, h_ref, slope_ref, mid_ref, few_ref, mid_acc_ref, small_acc_ref, turned_ref, sem_ref, in_sem, out_sem, *refs = refs
    lo, hi = (DIRECT, DIRECT + SECOND)
    at = 0 if first else DIRECT
    lines = Lines(
        grid,
        ((h_far, at, at + SECOND), (slope_far, at, at + SECOND)),
        ((h_ref, 0), (slope_ref, 0)),
        sem_ref,
    )
    lines.first()
    arriving = copies((mid_far, few_far), (mid_ref, few_ref), in_sem)
    for copy in arriving:
        copy.start()
    total = total_of(sums_in_ref)
    total_ref[...] = total
    a, b, c = before_norm(
        gain_ref[block : block + 1, lo:hi], outer_ref[1:2, lo:hi], total[:, lo:hi], outer_ref[2:3, lo:hi]
    )
    mask = grid.mask(grid.line_rows, length_ref[0], SECOND)
    matrix = spread_matrix(grid, small)
    clear_empty(grid, d_ref)
    rows = grid.line_rows
    if first:
        share = out_ref.shape[1] - carried_ref.shape[1]
        for clip in range(out_ref.shape[0]):
            out_ref[clip, share:, :] = carried_ref[clip]

    def visit(step):
        for number in range(lines.step):
            line = step * lines.step + number
            here = rows_at(line * rows, rows)
            scaled = h_ref[here, :].astype(F32)
            error = outer_error(slope_ref[here, :], small, grad_ref, matrix, line, lo, hi)
            back = (a * error - b - c * scaled) * mask
            if grid.copies == 1:
                d_ref[0, rows_at(grid.lead + line * grid.pitch, rows), :] = back.astype(BF16)
            else:
                refs[0][rows_at((line + 1) * rows, rows), :] = back

    lines.run(visit)
    if grid.copies > 1:
        clear_ends(grid, refs[0])

        def store(copy, at, values):
            d_ref[copy, at, :] = values.astype(BF16)

        store_copies(grid, refs[0], store)
    leaving = pltpu.make_async_copy(d_ref, d_far, out_sem.at[0])
    leaving.start()
    for copy in arriving:
        copy.wait()
    kernel_grads(grid, slots, first_ref, mid_ref, few_ref, d_ref, out_ref, mid_acc_ref, small_acc_ref, turned_ref)
    leaving.wait()


def before_norm(gain, inverse, sums, count):
    factor = gain * inverse
    return (factor, factor * sums[0:1] / count, factor * sums[1:2] / count)


def second_back_scratch(grid, slots):
    return [
        pltpu.VMEM((grid.copies, grid.padded, SECOND), BF16),
        pltpu.VMEM((grid.rows, SECOND), BF16),
        pltpu.VMEM((grid.rows, SECOND), BF16),
        pltpu.VMEM((grid.copies, grid.padded, 512), BF16),
        pltpu.VMEM((grid.copies, grid.padded, 128), BF16),
        pltpu.VMEM((slots, 384, 256), F32),
        pltpu.VMEM((slots, 128, 128), F32),
        pltpu.VMEM((MID_IN + 128, 128), F32),
        Lines.semaphores(grid, 2),
        pltpu.SemaphoreType.DMA((2,)),
        pltpu.SemaphoreType.DMA((1,)),
        *([pltpu.VMEM((grid.rows + 2 * grid.line_rows, SECOND), F32)] if grid.copies > 1 else []),
    ]


def conv_back(grid, slots, block, length_ref, d_ref, reduced_ref, reduced_gain_ref, reduced_shift_ref, *refs):
    far_kernels, refs = (refs[:3], refs[3:])
    first = len(refs) > 9
    x_far, refs = (refs[0], refs[1:]) if first else (None, refs)
    r_ref, out_sums_ref, *refs = refs
    product_out, refs = (refs[0], refs[1:]) if first else (None, refs)
    kernels, (last_ref, acc_ref, sums_ref, in_sem, *refs) = (refs[:3], refs[3:])
    if first:
        x_ref, product_ref, x_sem = refs
        x_copy = pltpu.make_async_copy(x_far, x_ref, x_sem.at[0])
        x_copy.start()
    main_ref, rest_ref, small_ref = kernels
    arriving = copies(far_kernels, kernels, in_sem)
    for copy in arriving:
        copy.start()
    rows = grid.line_rows
    group_rows = grid.group * grid.pitch
    sums_ref[...] = jnp.zeros_like(sums_ref)
    mask = grid.mask(rows, length_ref[0], REDUCED)
    gain, shift = (reduced_gain_ref[block : block + 1], reduced_shift_ref[block : block + 1])
    turned = (((1,), (1,)), ((), ()))
    lane = lax.broadcasted_iota(jnp.int32, (rows, 128), 1)
    wide_lane = lax.broadcasted_iota(jnp.int32, (grid.pitch, 128), 1)

    for copy in range(grid.copies):

        @pl.loop(1 - grid.copies, grid.side)
        def _(line):
            place = grid.lead + line * grid.pitch

            def lanes(start):
                return d_ref[copy, rows_at(start, grid.pitch), 256:384]

            further, here = (lanes(place + grid.pitch).astype(F32), lanes(place).astype(F32))
            at = rows_at(place, grid.pitch)
            last_ref[copy, at, 0:128] = jnp.where(
                wide_lane < 64, further, pltpu.roll(here, 64, 1)
            ).astype(BF16)
            last_ref[copy, at, 128:256] = lanes(place - grid.pitch)

        if grid.copies == 1:
            last_ref[copy, grid.lead - TILE : grid.lead, :] = jnp.zeros((TILE, 256), BF16)
        end = grid.lead + grid.side * grid.pitch
        last_ref[copy, end : end + TILE, :] = jnp.zeros((TILE, 256), BF16)
    for copy in arriving:
        copy.wait()

    @pl.loop(0, grid.side // grid.group)
    def _(group):
        base = grid.lead + group * group_rows
        for tap in range(9):
            part = lax.dot_general(
                near_tap(grid, d_ref, base, tap, -1, group_rows, slice(0, 256)),
                main_ref[tap],
                turned,
                preferred_element_type=F32,
            )
            acc_ref[:, 0:512] = part if tap == 0 else acc_ref[:, 0:512] + part
        for place in range(3):
            acc_ref[:, 0:512] += lax.dot_general(
                grid.near(last_ref, base, 0, 1 - place, group_rows),
                rest_ref[place],
                turned,
                preferred_element_type=F32,
            )
        near = [
            near_tap(grid, d_ref, base, tap, -1, group_rows, slice(384, 512)) for tap in range(9)
        ]
        acc_ref[:, 512:640] = jnp.dot(
            jnp.concatenate(near, axis=1), small_ref[...], preferred_element_type=F32
        )
        for number in range(grid.group):
            line = group * grid.group + number
            lines = slice(number * grid.pitch, number * grid.pitch + rows)
            rest, small = (acc_ref[lines, 384:512], acc_ref[lines, 512:640])
            one = jnp.where(lane < 32, rest, pltpu.roll(small, 32, 1))
            two = jnp.where(lane < 32, pltpu.roll(rest, 96, 1), small)
            three = jnp.where(lane < 32, pltpu.roll(rest, 64, 1), pltpu.roll(small, 96, 1))
            unit = grid.unit
            wide = later(acc_ref[lines, 0:128], unit) + acc_ref[lines, 128:256]
            wide = wide + earlier(acc_ref[lines, 256:384], unit)
            narrow = jnp.where(lane < 64, later(one, unit) + two + earlier(three, unit), 0.0)
            back = jnp.concatenate([wide, narrow], axis=1)
            at = rows_at(line * rows, rows)
            scaled = reduced_ref[at, :].astype(F32)
            error = back * silu_slope(gain * scaled + shift) * mask
            r_ref[at, :] = error.astype(BF16)
            sums_ref[0:8] += partial_sum(error)
            sums_ref[8:16] += partial_sum(error * scaled)

    write_sums(out_sums_ref, sums_ref, 0, REDUCED)
    if first:
        x_copy.wait()
        write_products(
            slots,
            x_ref,
            lambda start, size: r_ref[start : start + size, :],
            product_ref,
            product_out,
        )


def kernel_grads(grid, slots, first_ref, mid_ref, small_ref, d_ref, out_ref, mid_acc_ref, small_acc_ref, turned_ref):
    group_rows = grid.group * grid.pitch
    mid_acc_ref[...] = jnp.zeros_like(mid_acc_ref)
    small_acc_ref[...] = jnp.zeros_like(small_acc_ref)

    def neighbour(slot):
        return jnp.minimum(first_ref[0] + slot, TAPS - 1) // 9

    @pl.loop(0, grid.side // grid.group)
    def _(group):
        base = grid.lead + group * group_rows
        left = d_ref[0, rows_at(base, group_rows), :].T
        for slot in range(slots):
            tap = lax.rem(jnp.minimum(first_ref[0] + slot, TAPS - 1), 9)
            start = base + (tap // 3 - 1) * grid.pitch
            place = lax.rem(tap, 3) - 1
            copy = 0
            if grid.copies == 1:
                start = start + place * TILE
            else:
                copy = jnp.where(place == 0, 0, 1)
                start = start - jnp.where(place < 0, TILE, 0)
            at = rows_at(start, group_rows)
            lanes = pl.ds(pl.multiple_of(neighbour(slot) * 128, 128), 128)
            right = jnp.concatenate([mid_ref[copy, at, lanes], mid_ref[copy, at, 384:512]], axis=1)
            mid_acc_ref[slot] += jnp.dot(left[0:384], right, preferred_element_type=F32)
            small_acc_ref[slot] += jnp.dot(
                left[384:512], small_ref[copy, at, :], preferred_element_type=F32
            )

    share = round_up(slots * TAP_ROWS, 16 * out_ref.shape[0]) // out_ref.shape[0]

    def put(start, values):
        done = 0
        while done < values.shape[0]:
            clip, at = divmod(start + done, share)
            size = min(values.shape[0] - done, share - at)
            out_ref[clip, at : at + size, :] = values[done : done + size].astype(BF16)
            done = done + size

    half = MID_IN // 2
    for slot in range(slots):
        base = slot * TAP_ROWS
        rest = pl.ds(pl.multiple_of(neighbour(slot) * 32, 32), 32)
        for tile in range(3):
            lines = slice(128 * tile, 128 * (tile + 1))
            turned_ref[0:128, :] = mid_acc_ref[slot, lines, 0:128].T
            turned_ref[MID_IN : MID_IN + 128, :] = mid_acc_ref[slot, lines, 128:256].T
            turned_ref[128:MID_IN, :] = turned_ref[
                pl.ds(pl.multiple_of(MID_IN + neighbour(slot) * 32, 32), 32), :
            ]
            if tile < 2:
                put(base + MID_IN * tile, turned_ref[0:MID_IN, :])
            else:
                folded = turned_ref[0:half, :] + pltpu.roll(turned_ref[half:MID_IN, :], 64, 1)
                put(base + 2 * MID_IN, folded)
        turned_ref[0:128, :] = small_acc_ref[slot].T
        put(base + 2 * MID_IN + half, turned_ref[rest, :])
    used = slots * TAP_ROWS
    put(used, jnp.zeros((share * out_ref.shape[0] - used, 128), F32))


class Spread:
    def __init__(self, grid, plane_ref, across_ref, scale_ref, length):
        self.grid, self.plane, self.across, self.scale = (grid, plane_ref, across_ref, scale_ref)
        clear_edges(grid, plane_ref)
        window = box_window(grid, length)
        scale_ref[0] = box_scale(0, grid.side, window)
        scale_ref[1] = box_scale(1, grid.side, window)
        unit = grid.unit
        edge = jnp.zeros((unit, POOLED), F32)
        across_ref[0:unit, :] = edge
        across_ref[unit + grid.line_rows :, :] = edge

    def put(self, line, values):
        rows = self.grid.line_rows
        inner = jnp.where((line == 0) | (line == self.grid.side - 1), 0, 1)
        values = values * self.scale[inner]
        across, unit = (self.across, self.grid.unit)
        across[unit : unit + rows, :] = values + earlier(values, unit) + later(values, unit)
        self.plane[rows_at((line + 1) * rows, rows), :] = (
            across[0:rows, :] + across[unit : unit + rows, :] + across[2 * unit :, :]
        )

    def get(self, start, size):
        rows = self.grid.line_rows
        return (
            self.plane[rows_at(start, size), :]
            + self.plane[rows_at(start + rows, size), :]
            + self.plane[rows_at(start + 2 * rows, size), :]
        )

    @staticmethod
    def scratch(grid):
        return [
            pltpu.VMEM((grid.rows + 2 * grid.line_rows, POOLED), F32),
            pltpu.VMEM((grid.line_rows + 2 * grid.unit, POOLED), F32),
            pltpu.VMEM((2, grid.line_rows, POOLED), F32),
        ]


def channel_products(slots, x_ref, right_of):
    total = None
    for part in range(slots.parts):
        slot = part * slots.each
        pair = slot - (slots.empty if slot >= slots.gap + slots.empty else 0)
        pair = min(pair, slots.pairs - slots.each)
        product = jnp.dot(
            x_ref[part], right_of(pair * slots.pair_rows, slots.rows), preferred_element_type=F32
        )
        total = product if total is None else total + product
    return total


def write_products(slots, x_ref, right_of, product_ref, product_out):
    channels = x_ref.shape[1]
    product_ref[0:channels, :] = channel_products(slots, x_ref, right_of)
    product_ref[channels:, :] = jnp.zeros((product_ref.shape[0] - channels, product_ref.shape[1]), F32)
    clips, tiles, size, _ = product_out.shape
    for clip in range(clips):
        for tile in range(tiles):
            product_out[clip, tile] = product_ref[
                clip * size : (clip + 1) * size, 128 * tile : 128 * (tile + 1)
            ]


def rest_constants(outer_ref, total_ref, gain_ref, block):
    pool = OUTER - POOLED

    def pick(ref, lo, hi):
        return jnp.concatenate([ref[lo:hi, 0:DIRECT], ref[lo:hi, pool:]], axis=1)

    return before_norm(
        pick(gain_ref, block, block + 1), pick(outer_ref, 1, 2), pick(total_ref, 0, 2), pick(outer_ref, 2, 3)
    )


def point_back(grid, slots, block, kept, length_ref, place_ref, h_far, outer_ref, total_ref, gain_ref, error_far, reduced_far, r_far, moment_ref, sums_in_ref, reduced_gain_ref, x_far, p_far, *refs):
    pooled_slope_in, pooled_product_in, kept_far, *refs = refs
    dx_ref, dp_ref, reduced_total_ref, outer_sums_ref, *refs = refs
    h_ref, error_ref, reduced_ref, r_ref, x_ref, p_ref, du_ref, acc_ref, *refs = refs
    plane_ref, across_ref, scale_ref, sums_ref, pooled_slope_ref, pooled_product_ref, kept_ref, *refs = refs
    sem_ref, in_sem = refs
    rows = grid.line_rows
    pool = OUTER - POOLED
    lines = Lines(
        grid,
        (
            (h_far, 0, DIRECT),
            (h_far, pool, OUTER),
            (error_far, 0, DIRECT),
            (error_far, pool, OUTER),
            (reduced_far, 0, REDUCED),
            (r_far, 0, REDUCED),
        ),
        ((h_ref, 0), (h_ref, DIRECT), (error_ref, 0), (error_ref, DIRECT), (reduced_ref, 0), (r_ref, 0)),
        sem_ref,
    )
    lines.first()
    kept_rows = kept_ref.shape[1]
    arriving = copies(
        (x_far, p_far, kept_far.at[:, pl.ds(slots.rows, kept_rows), :]), (x_ref, p_ref, kept_ref), in_sem
    )
    for copy in arriving:
        copy.start()
    length = length_ref[0]
    total = total_of(sums_in_ref)
    reduced_total_ref[...] = total
    mid = before_norm(
        reduced_gain_ref[block : block + 1],
        moment_ref[1:2, DIRECT:SECOND],
        total,
        outer_ref[2:3, 0:REDUCED],
    )
    rest = rest_constants(outer_ref, total_ref, gain_ref, block)
    mask = grid.mask(rows, length, DIRECT + POOLED)
    spread = Spread(grid, plane_ref, across_ref, scale_ref, length)

    def visit(line):
        at = rows_at(line * rows, rows)
        back = rest[0] * error_ref[at, :].astype(F32) - rest[1] - rest[2] * h_ref[at, :].astype(F32)
        back = back * mask
        du_ref[at, 0:DIRECT] = back[:, :DIRECT].astype(BF16)
        spread.put(line, back[:, DIRECT:])
        back = mid[0] * r_ref[at, :].astype(F32) - mid[1] - mid[2] * reduced_ref[at, :].astype(F32)
        du_ref[at, DIRECT:SECOND] = (back * mask[:, :REDUCED]).astype(BF16)

    lines.run(visit)
    for copy in arriving:
        copy.wait()
    sums_ref[...] = jnp.zeros_like(sums_ref)
    pooled_slope_ref[:, DIRECT:] = pooled_slope_in[...]
    pooled_product_ref[:, DIRECT:] = pooled_product_in[...]
    for pair in range(slots.pairs):
        slot = pair + (slots.empty if pair >= slots.gap else 0)
        at = slice(pair * rows, (pair + 1) * rows)
        start = slot % slots.each * rows
        values = kept_ref[slot // slots.each, start : start + rows, :]
        pooled_slope_ref[at, 0:DIRECT] = values[:, :DIRECT]
        pooled_product_ref[at, 0:DIRECT] = values[:, DIRECT:]

    @pl.loop(0, grid.side)
    def _(line):
        at = rows_at(line * rows, rows)
        du_ref[at, SECOND:] = (spread.get(line * rows, rows) * mask[:, :POOLED]).astype(BF16)
        dx = jnp.dot(du_ref[at, :], p_ref[...], preferred_element_type=F32).astype(BF16)
        dx_ref[at, :] = dx
        for number, ref in enumerate((pooled_slope_ref, pooled_product_ref)):
            sums_ref[8 * number : 8 * number + 8] += partial_sum(
                dx.astype(F32) * ref[at, :].astype(F32)
            )

    write_sums(outer_sums_ref, sums_ref, 0, OUTER)
    acc_ref[...] = lax.dot_general(
        x_ref[...], du_ref[...], (((0,), (0,)), ((), ())), preferred_element_type=F32
    )
    start = pl.multiple_of(place_ref[0] * kept, 16) if kept < acc_ref.shape[0] else 0
    clips, size, _ = dp_ref.shape
    for tile in range(FIRST // 128):
        values = acc_ref[pl.ds(start, kept), 128 * tile : 128 * (tile + 1)].astype(BF16)
        done = 0
        while done < kept:
            clip, at = divmod(kept * tile + done, size)
            few = min(kept - done, size - at)
            dp_ref[clip, at : at + few, :] = values[done : done + few]
            done = done + few
    used = (FIRST // 128) * kept
    while used < clips * size:
        clip, at = divmod(used, size)
        dp_ref[clip, at:, :] = jnp.zeros((size - at, 128), BF16)
        used = used + size - at


def rest_back(grid, small, slots, block, length_ref, outer_ref, total_ref, gain_ref, grad_ref, h_far, slope_far, kept_far, x_far, reduced_far, du_far, product_out, *refs):
    h_ref, slope_ref, x_ref, reduced_ref, du_ref, plane_ref, across_ref, scale_ref, product_ref, sem_ref, in_sem, du_sem = refs
    rows = grid.line_rows
    pool = OUTER - POOLED

    def direct(step, lo, hi):
        slot = slots.slot_of(step)
        at = rows_at(lax.rem(slot, slots.each) * slots.pair_rows, slots.pair_rows)
        return kept_far.at[slot // slots.each, at, pl.ds(lo, hi - lo)]

    lines = Lines(
        grid,
        (
            (direct, 0, DIRECT),
            (h_far, SECOND, FIRST),
            (direct, DIRECT, 2 * DIRECT),
            (slope_far, SECOND, FIRST),
        ),
        ((h_ref, 0), (h_ref, DIRECT), (slope_ref, 0), (slope_ref, DIRECT)),
        sem_ref,
    )
    lines.first()
    arriving = copies((x_far, reduced_far), (x_ref, reduced_ref), in_sem)
    for copy in arriving:
        copy.start()
    length = length_ref[0]
    matrix = spread_matrix(grid, small)
    a, b, c = rest_constants(outer_ref, total_ref, gain_ref, block)
    mask = grid.mask(rows, length, DIRECT + POOLED)
    spread = Spread(grid, plane_ref, across_ref, scale_ref, length)

    def visit(step):
        for number in range(lines.step):
            line = step * lines.step + number
            at = rows_at(line * rows, rows)
            coarse = grad_ref[rows_at((line // 2) * small.line_rows, small.line_rows), :]
            grad = jnp.dot(
                matrix,
                jnp.concatenate([coarse[:, :DIRECT], coarse[:, pool:]], axis=1),
                preferred_element_type=F32,
            )
            back = a * (grad * slope_ref[at, :].astype(F32)) - b - c * h_ref[at, :].astype(F32)
            back = back * mask
            du_ref[at, 0:DIRECT] = back[:, :DIRECT].astype(BF16)
            spread.put(line, back[:, DIRECT:])

    lines.run(visit)
    for copy in arriving:
        copy.wait()
    wide = lines.size
    pool_mask = grid.mask(wide, length)

    def leaving(step):
        at = rows_at(step * wide, wide)
        return pltpu.make_async_copy(du_ref.at[at, :], du_far.at[at, :], du_sem.at[0])

    @pl.loop(0, lines.steps)
    def _(step):
        at = rows_at(step * wide, wide)
        du_ref[at, DIRECT:] = (spread.get(step * wide, wide) * pool_mask).astype(BF16)
        leaving(step).start()

    ones = grid.mask(slots.rows, length)
    two_ones = jnp.concatenate([ones, ones], axis=1)

    def right_of(start, size):
        at = slice(start, start + size)
        scaled = (reduced_ref[at, :].astype(F32) * two_ones).astype(BF16)
        return jnp.concatenate([du_ref[at, :], scaled, ones.astype(BF16)], axis=1)

    write_products(slots, x_ref, right_of, product_ref, product_out)
    pltpu.make_async_copy(du_ref, du_far, du_sem.at[0]).wait()


def mid_back(grid, block, length_ref, place_ref, moment_ref, sums_in_ref, gain_ref, du_far, h_far, r_far, p_far, dx_far, total_ref, *refs):
    du_ref, h_ref, r_ref, p_ref, dx_ref, sem_ref, p_sem, dx_sem = refs
    lines = Lines(
        grid,
        ((du_far, 0, DIRECT + POOLED), (h_far, 0, REDUCED), (r_far, 0, REDUCED)),
        ((du_ref, 0), (h_ref, 0), (r_ref, 0)),
        sem_ref,
    )
    lines.first()
    p_copy = pltpu.make_async_copy(p_far.at[place_ref[0]], p_ref, p_sem.at[0])
    p_copy.start()
    total = total_of(sums_in_ref)
    total_ref[...] = total
    a, b, c = before_norm(
        gain_ref[block : block + 1], moment_ref[1:2, DIRECT:], total, moment_ref[2:3, DIRECT:]
    )
    mask = grid.mask(lines.size, length_ref[0], REDUCED)
    p_copy.wait()

    def leaving(step):
        at = rows_at(step * lines.size, lines.size)
        return pltpu.make_async_copy(dx_ref.at[at, :], dx_far.at[at, :], dx_sem.at[0])

    def visit(step):
        at = rows_at(step * lines.size, lines.size)
        back = a * r_ref[at, :].astype(F32) - b - c * h_ref[at, :].astype(F32)
        du = jnp.concatenate(
            [du_ref[at, :DIRECT], (back * mask).astype(BF16), du_ref[at, DIRECT:]], axis=1
        )
        dx_ref[at, :] = jnp.dot(du, p_ref[...], preferred_element_type=F32).astype(BF16)
        leaving(step).start()

    lines.run(visit)
    pltpu.make_async_copy(dx_ref, dx_far, dx_sem.at[0]).wait()


def combine(block, rest_ref, pieces_ref, moment_ref, sums_in_ref, gain_ref, out_ref):
    total = total_of(sums_in_ref)
    a, b, c = before_norm(
        gain_ref[block : block + 1], moment_ref[1:2, DIRECT:], total, moment_ref[2:3, DIRECT:]
    )
    size = out_ref.shape[0] // 5
    rest, products = (total_of(rest_ref), total_of(pieces_ref))
    for tile in range(2):
        out_ref[size * tile : size * (tile + 1), :] = rest[tile].astype(BF16)
        lanes = slice(128 * tile, 128 * (tile + 1))
        mid = a[:, lanes] * products[tile] - b[:, lanes] * rest[5] - c[:, lanes] * rest[3 + tile]
        out_ref[size * (2 + tile) : size * (3 + tile), :] = mid.astype(BF16)
    out_ref[4 * size :, :] = rest[2].astype(BF16)


def write_taps(read, slots, mid_ref, small_ref, mid_out, small_out, sem_ref):
    half = MID_IN // 2

    def leaving(tap):
        return (
            pltpu.make_async_copy(mid_ref.at[tap], mid_out.at[tap], sem_ref.at[0]),
            pltpu.make_async_copy(small_ref.at[tap], small_out.at[tap], sem_ref.at[1]),
        )

    for tap in range(TAPS):
        part, slot = divmod(tap, slots)
        base = slot * TAP_ROWS
        folded = read(part, base + 2 * MID_IN, half)
        mid_ref[tap, :, 0:128] = read(part, base, MID_IN)
        mid_ref[tap, :, 128:256] = read(part, base + MID_IN, MID_IN)
        mid_ref[tap, 0:half, 256:320] = folded[:, 0:64]
        mid_ref[tap, half:MID_IN, 256:320] = pltpu.roll(folded, 64, 1)[:, 0:64]
        small_ref[tap] = read(part, base + 2 * MID_IN + half, SMALL_IN)
        for copy in leaving(tap):
            copy.start()
    pltpu.make_async_copy(mid_ref, mid_out, sem_ref.at[0]).wait()
    pltpu.make_async_copy(small_ref, small_out, sem_ref.at[1]).wait()


def write_point(read, parts, kept, point_ref, wide_ref):
    for tile in range(FIRST // 128):
        for part in range(parts):
            start, stop = (kept * part, kept * (part + 1))
            values = read(part, kept * tile, kept)
            if kept * parts == CHANNELS:
                wide_ref[start:stop, :] = values
                continue
            for lo, hi, moved in ((0, 576, 0), (640, OUTER, 64)):
                lo, hi = (max(lo, start), min(hi, stop))
                if lo < hi:
                    wide_ref[lo - moved : hi - moved, :] = values[lo - start : hi - start]
        turned = wide_ref[...].T
        if tile < 3:
            point_ref[128 * tile : 128 * (tile + 1), :] = turned
        elif tile == 3:
            point_ref[384:448, :] = turned[0:64]
        else:
            point_ref[448:576, :] = turned


def copy_out(pairs, sem_ref):
    copies = [
        pltpu.make_async_copy(source, target, sem_ref.at[number])
        for number, (source, target) in enumerate(pairs)
    ]
    for copy in copies:
        copy.start()
    for copy in copies:
        copy.wait()


def share_reader(ref, clips, lo, share):
    def read(part, start, size):
        pieces, done = ([], 0)
        while done < size:
            clip, at = divmod(start + done, share)
            few = min(size - done, share - at)
            pieces.append(ref[part * clips + clip, lo + at : lo + at + few, :].astype(F32))
            done = done + few
        return pieces[0] if len(pieces) == 1 else jnp.concatenate(pieces, axis=0)

    return read


def unpack_second(clips, slots, shares_ref, mid_out, small_out, mid_ref, small_ref, sem_ref):
    read = share_reader(shares_ref, clips, 0, shares_ref.shape[1])
    write_taps(read, slots, mid_ref, small_ref, mid_out.at[1], small_out.at[1], sem_ref)


def unpack_first(parts, clips, slots, share, shares_ref, *refs):
    totals, refs = (refs[:4], refs[4:])
    mid_in, small_in, mid_out, small_out, point_out, gain_out, shift_out, *refs = refs
    mid_ref, small_ref, point_ref, wide_ref, sem_ref = refs
    for block in range(2):
        outer_ref, reduced_ref = totals[2 * block : 2 * block + 2]
        for row, out in enumerate((shift_out, gain_out)):
            at, line = (slice(block, block + 1), slice(row, row + 1))
            out[at, 0:256] = outer_ref[line, 0:256]
            out[at, 256:448] = reduced_ref[line, 0:192]
            out[at, 448:576] = outer_ref[line, 768:896]
            out[at, 576:896] = outer_ref[line, 256:576]
            out[at, 896:1024] = outer_ref[line, 640:768]
    read = share_reader(shares_ref, clips, share, shares_ref.shape[1] - share)
    write_point(read, parts, OUTER // parts, point_ref, wide_ref)
    last = pltpu.make_async_copy(point_ref, point_out.at[1], sem_ref.at[2])
    last.start()
    read = share_reader(shares_ref, clips, 0, share)
    write_taps(read, slots, mid_ref, small_ref, mid_out.at[0], small_out.at[0], sem_ref)
    last.wait()


def unpack_point(parts, clips, kept, place_ref, clip_ref, mine_ref, other_ref, point_in, point_out, buffer_ref, point_ref, wide_ref, sem_ref):
    tiles = FIRST // 128
    size = buffer_ref.shape[2] // clips
    for chip in range(clips // 2):
        for step in range(parts):
            part = lax.rem(place_ref[0] - step + parts, parts)
            for swapped, ref in enumerate((mine_ref, other_ref)):
                owner = clip_ref[0] ^ (2 * chip) ^ swapped
                source = (chip * parts + step) * tiles * size
                for tile in range(tiles):
                    buffer_ref[part, tile, rows_at(owner * size, size), :] = ref[
                        source + tile * size : source + (tile + 1) * size, :
                    ]

    def read(part, start, size):
        tile, at = divmod(start, kept)
        return buffer_ref[part, tile, at : at + size, :].astype(F32)

    write_point(read, parts, kept, point_ref, wide_ref)
    last = pltpu.make_async_copy(point_ref, point_out.at[0], sem_ref.at[0])
    last.start()
    last.wait()


def prepare(parts, mid_in, small_in, point_in, gain_in, shift_in, *refs):
    kernels, (point_ref, second_ref, *vectors) = (refs[:8], refs[8:14])
    for block in range(2):
        main_ref, last_ref, few_ref, back_ref = kernels[4 * block : 4 * block + 4]

        @pl.loop(0, 9)
        def _(tap):
            for number in range(3):
                source = 9 * number + tap
                main_ref[tap, 128 * number : 128 * (number + 1), :] = mid_in[block, source, 0:128, 0:256]
                main_ref[tap, 384 + 32 * number : 416 + 32 * number, :] = mid_in[
                    block, source, 128:MID_IN, 0:256
                ]
            main_ref[tap, 480:512, :] = jnp.zeros((32, 256), BF16)
            small = jnp.concatenate(
                [small_in[block, 9 * number + tap] for number in range(3)]
                + [jnp.zeros((32, 128), BF16)],
                axis=0,
            )
            at = pl.ds(pl.multiple_of(tap * 128, 128), 128)
            few_ref[at, :] = small
            back_ref[at, :] = small.astype(F32).T.astype(BF16)

        @pl.loop(0, 3)
        def _(place):
            for number in range(3):
                for rows, start, size in (
                    (slice(0, 128), 128 * number, 128),
                    (slice(128, MID_IN), 384 + 32 * number, 32),
                ):
                    pieces = [
                        mid_in[block, 9 * number + 3 * line + place, rows, 256:MID_OUT].astype(F32)
                        for line in range(3)
                    ]
                    pieces.append(jnp.zeros((size, 64), F32))
                    last_ref[place, start : start + size, :] = jnp.concatenate(
                        pieces, axis=1
                    ).astype(BF16)
            last_ref[place, 480:512, :] = jnp.zeros((32, 256), BF16)

    own = point_ref.shape[2]
    for lo, hi, at in ((0, 448, 0), (448, SQUEEZED, SECOND)):
        values = point_in[0, lo:hi, :].astype(F32)
        for part in range(parts):
            point_ref[part, at : at + hi - lo, :] = values[:, own * part : own * (part + 1)].astype(
                BF16
            )
        values = point_in[1, lo:hi, :].astype(F32)
        gap = jnp.zeros((hi - lo, 64), F32)
        second_ref[at : at + hi - lo, :] = jnp.concatenate(
            [values[:, :576], gap, values[:, 576:]], axis=1
        ).astype(BF16)
    for part in range(parts):
        point_ref[part, 448:SECOND, :] = jnp.zeros((64, own), BF16)
    second_ref[448:SECOND, :] = jnp.zeros((64, OUTER), BF16)
    for source, outer, reduced in ((gain_in, vectors[0], vectors[1]), (shift_in, vectors[2], vectors[3])):
        outer[:, 0:256] = source[:, 0:256]
        outer[:, 256:576] = source[:, 576:896]
        outer[:, 576:640] = jnp.zeros((2, 64), F32)
        outer[:, 640:768] = source[:, 896:1024]
        outer[:, 768:896] = source[:, 448:576]
        reduced[:, 0:192] = source[:, 256:448]
        reduced[:, 192:256] = jnp.zeros((2, 64), F32)


def round_up(value, unit):
    return -(-value // unit) * unit


def spread_over(values, axis, size):
    received = [values]
    for step in range(1, size):
        perm = [(source, (source + step) % size) for source in range(size)]
        received.append(lax.ppermute(values, axis, perm))
    return received


def after(values, earlier):
    return lax.optimization_barrier((values, earlier))[0]


def exchange(values):
    return lax.all_to_all(values, "dp", 0, 0, tiled=True)


def add_up(pieces):
    return jnp.sum(pieces.astype(F32), axis=0).astype(BF16)


def gather_chips(column, clips, work=None):
    columns = [column]
    for chip in range(1, clips // 2):
        perm = [(source, source ^ (2 * chip)) for source in range(clips)]
        columns.append(lax.ppermute(column, "dp", perm))
    if work is not None:
        columns = after(columns, work)
    mine = jnp.concatenate(columns, axis=0)
    other = lax.ppermute(mine, "dp", [(source, source ^ 1) for source in range(clips)])
    return (mine, other)


def on_device(frames, lengths, cotangent, pointwise, conv_mid, conv_small, gains, shifts):
    parts = lax.axis_size("branch")
    clips = lax.axis_size("dp")
    place = lax.axis_index("branch").astype(jnp.int32)
    side = frames.shape[2]
    grid, small = (Grid(side, frames.shape[1]), Grid(side // 2, frames.shape[1] // 2))
    slots = Slots(grid, parts)
    cells = side * side
    own_channels = frames.shape[-1]
    length = lengths.astype(jnp.int32)
    half_length = length // 2
    place_one = place.reshape(1)

    own = frames[0].transpose(1, 2, 0, 3).reshape(grid.rows, own_channels)
    turned = call(functools.partial(turn, slots), shape((parts, own_channels, slots.rows), BF16))(own)
    by_pairs = lax.all_to_all(turned, "branch", 0, 0, tiled=True)
    kernel_shapes = (
        shape((9, 512, 256), BF16),
        shape((3, 512, 256), BF16),
        shape((1152, 128), BF16),
        shape((1152, 128), BF16),
    )
    prepared = call(
        functools.partial(prepare, parts),
        (
            *kernel_shapes,
            *kernel_shapes,
            shape((parts, FIRST, own_channels), BF16),
            shape((FIRST, OUTER), BF16),
            shape((2, OUTER), F32),
            shape((2, REDUCED), F32),
            shape((2, OUTER), F32),
            shape((2, REDUCED), F32),
        ),
    )(conv_mid, conv_small, pointwise.swapaxes(1, 2), gains, shifts)
    kernels = (prepared[0:4], prepared[4:8])
    point_first, point_second, outer_gain, reduced_gain, outer_shift, reduced_shift = prepared[8:]

    local_count = (length * (slots.held(place) * 2 * side)).astype(F32)
    mid, pool, direct, sums = call(
        functools.partial(first_pointwise, slots),
        (
            shape((mid_rows(slots), 128), BF16),
            shape((slots.rows + TILE, POOLED), BF16),
            shape((slots.rows, DIRECT), F32),
            shape((clips, 3, SECOND), F32),
        ),
        [pltpu.VMEM((slots.rows, FIRST), F32)],
        scalars=2,
    )(length, local_count, by_pairs, point_first)
    mids = spread_over(mid, "branch", parts)
    sums = spread_over(jnp.sum(exchange(sums), axis=0), "branch", parts)
    pools = spread_over(after(pool, (mids, sums)), "branch", parts)
    h_reduced, taps_mid, taps_few, e, e_sums = call(
        functools.partial(first_convolve, grid, slots, 0),
        conv_outputs(grid),
        conv_scratch(grid),
        scalars=2,
        cost=40,
        far=range(4 + 2 * parts, 7 + 2 * parts),
        far_out=range(4),
    )(length, place_one, *mids, *sums, reduced_gain, reduced_shift, *kernels[0][:3])
    q_pool, second_sums = call(
        functools.partial(first_pool, grid, slots),
        (shape((grid.rows, POOLED), F32), shape((clips, 2, FIRST), F32)),
        [
            pltpu.VMEM((grid.rows + 2 * grid.line_rows, POOLED), F32),
            pltpu.VMEM((16, POOLED), F32),
        ],
        scalars=2,
    )(length, place_one, *pools, e_sums)
    second_sums = exchange(second_sums)
    pooled_direct, kept_direct, moment = call(
        functools.partial(first_direct, grid, small, slots, 0),
        (
            shape((slots.each * small.line_rows, DIRECT), BF16),
            shape((slots.rows + slots.each * small.line_rows, 2 * DIRECT), BF16),
            shape((3, SECOND), F32),
        ),
        scalars=1,
        cost=3,
    )(length, direct, outer_gain, outer_shift, *sums)
    second_sums, pooled_direct = lax.optimization_barrier((second_sums, pooled_direct))
    pooled_directs = spread_over(pooled_direct, "branch", parts)
    kept_direct = lax.all_gather(after(kept_direct, second_sums), "branch", axis=0)
    pair = 2 * grid.line_rows
    pooled, h_outer, slope, outer, pooled_slope, pooled_product = call(
        functools.partial(first_output, grid, small, 0),
        (
            shape((small.rows, FIRST), BF16),
            shape((grid.rows, FIRST), BF16),
            shape((grid.rows, FIRST), BF16),
            shape((3, OUTER), F32),
            shape((small.rows, FIRST), BF16),
            shape((small.rows, FIRST), BF16),
        ),
        [
            pltpu.VMEM((2, pair, POOLED), F32),
            pltpu.VMEM((2, pair, SECOND), F32),
            pltpu.VMEM((2, pair, FIRST), BF16),
            pltpu.VMEM((2, pair, FIRST), BF16),
            *[pltpu.SemaphoreType.DMA((2,))] * 4,
        ],
        scalars=1,
        far=(1, 2),
        far_out=(1, 2),
    )(
        length,
        q_pool,
        e,
        moment,
        second_sums,
        outer_gain,
        outer_shift,
    )

    small_count = half_length.astype(F32) * float(small.side * small.side)
    q_small, sums_small, pooled = call(
        functools.partial(second_pointwise, small, slots),
        (
            shape((small.rows, FIRST), F32),
            shape((clips, 3, FIRST), F32),
            shape((small.rows, OUTER), BF16),
        ),
        [
            pltpu.VMEM((small.rows + 2 * small.line_rows, POOLED), F32),
            pltpu.VMEM((16, SECOND), F32),
            pltpu.VMEM((16, POOLED), F32),
        ],
        scalars=3,
    )(half_length, place_one, small_count, *pooled_directs, pooled, point_second)
    sums_small = exchange(sums_small)
    h_reduced_small, taps_mid_small, taps_few_small, e_small, e_sums_small, moment_small = call(
        functools.partial(second_convolve, small, 1),
        (*conv_outputs(small, clips), shape((3, FIRST), F32)),
        [*conv_scratch(small), pltpu.VMEM((small.rows + 2 * small.line_rows, REDUCED), F32)],
        scalars=1,
        far=range(5, 8),
        far_out=range(4),
    )(half_length, q_small, sums_small, reduced_gain, reduced_shift, *kernels[1][:3])
    e_sums_small = exchange(e_sums_small)
    cot = cotangent[0].transpose(1, 2, 0, 3).reshape(small.side**2, cotangent.shape[1], CHANNELS)
    act, h_outer_small, error_small, outer_small, outer_sums_small = call(
        functools.partial(second_output, small, 1),
        (
            shape(cot.shape, BF16),
            shape((small.rows, OUTER), BF16),
            shape((small.rows, OUTER), BF16),
            shape((3, OUTER), F32),
            shape((clips, 2, OUTER), F32),
        ),
        [pltpu.VMEM((16, OUTER), F32)],
        scalars=1,
    )(half_length, q_small, e_small, moment_small, e_sums_small, outer_gain, outer_shift, cot)

    taps_each = -(-TAPS // parts)
    tap_share = round_up(taps_each * TAP_ROWS, 16 * clips) // clips
    first_tap = place_one * taps_each

    def conv_back_scratch(at):
        return [
            pltpu.VMEM((9, 512, 256), BF16),
            pltpu.VMEM((3, 512, 256), BF16),
            pltpu.VMEM((1152, 128), BF16),
            pltpu.VMEM((at.copies, at.padded, 256), BF16),
            pltpu.VMEM((at.group * at.pitch, FIRST), F32),
            pltpu.VMEM((16, REDUCED), F32),
            pltpu.SemaphoreType.DMA((3,)),
        ]

    gathered = exchange(outer_sums_small)
    d_low, total_small, packed_small = call(
        functools.partial(second_back, small, None, 1, taps_each),
        (
            shape((small.copies, small.padded, SECOND), BF16),
            shape((2, OUTER), F32),
            shape((clips, tap_share, 128), BF16),
        ),
        second_back_scratch(small, taps_each),
        scalars=2,
        cost=8,
        far=(2, 6, 7, 8),
        far_out=(0,),
    )(
        half_length,
        first_tap,
        h_outer_small,
        outer_small,
        gathered,
        outer_gain,
        error_small,
        taps_mid_small,
        taps_few_small,
    )
    r_low, sums_low = call(
        functools.partial(conv_back, small, None, 1),
        (shape((small.rows, REDUCED), BF16), shape((clips, 2, REDUCED), F32)),
        conv_back_scratch(small),
        scalars=1,
        cost=8,
        far=(5, 6, 7),
    )(
        half_length,
        d_low,
        h_reduced_small,
        reduced_gain,
        reduced_shift,
        *kernels[1][:2],
        kernels[1][3],
    )
    share_small = add_up(exchange(packed_small))
    sums_low, share_small = lax.optimization_barrier((sums_low, share_small))
    gathered = exchange(sums_low)
    kept = OUTER // parts
    point_share = round_up(kept * (FIRST // 128), 16 * clips) // clips
    coarse_rows = slots.each * small.line_rows
    dx_small, point_packed, reduced_total_small, outer_sums = call(
        functools.partial(point_back, small, slots, 1, kept),
        (
            shape((small.rows, OUTER), BF16),
            shape((clips, point_share, 128), BF16),
            shape((2, REDUCED), F32),
            shape((clips, 2, OUTER), F32),
        ),
        [
            pltpu.VMEM((small.rows, DIRECT + POOLED), BF16),
            pltpu.VMEM((small.rows, DIRECT + POOLED), BF16),
            pltpu.VMEM((small.rows, REDUCED), BF16),
            pltpu.VMEM((small.rows, REDUCED), BF16),
            pltpu.VMEM((small.rows, OUTER), BF16),
            pltpu.VMEM((FIRST, OUTER), BF16),
            pltpu.VMEM((small.rows, FIRST), BF16),
            pltpu.VMEM((OUTER, FIRST), F32),
            *Spread.scratch(small),
            pltpu.VMEM((16, OUTER), F32),
            pltpu.VMEM((small.rows, OUTER), BF16),
            pltpu.VMEM((small.rows, OUTER), BF16),
            pltpu.VMEM((parts, coarse_rows, 2 * DIRECT), BF16),
            Lines.semaphores(small, 6),
            pltpu.SemaphoreType.DMA((3,)),
        ],
        scalars=2,
        cost=10,
        far=(2, 6, 7, 8, 12, 13, 16),
    )(
        half_length,
        place_one,
        h_outer_small,
        outer_small,
        total_small,
        outer_gain,
        error_small,
        h_reduced_small,
        r_low,
        moment_small,
        gathered,
        reduced_gain,
        pooled,
        point_second,
        pooled_slope,
        pooled_product,
        kept_direct,
    )
    whole_small = lax.all_gather(share_small, ("branch", "dp"), axis=0)

    gathered = exchange(outer_sums)
    d_low, total, packed = call(
        functools.partial(second_back, grid, small, 0, taps_each),
        (
            shape((grid.copies, grid.padded, SECOND), BF16),
            shape((2, OUTER), F32),
            shape((clips, tap_share + point_share, 128), BF16),
        ),
        second_back_scratch(grid, taps_each),
        scalars=2,
        cost=18,
        far=(2, 6, 9, 10),
        far_out=(0,),
    )(length, first_tap, h_outer, outer, gathered, outer_gain, slope, dx_small, point_packed, taps_mid, taps_few)
    product_rows = round_up(own_channels, 16 * clips)
    du_rest, rest_product = call(
        functools.partial(rest_back, grid, small, slots, 0),
        (
            shape((grid.rows, DIRECT + POOLED), BF16),
            shape((clips, 6, product_rows // clips, 128), F32),
        ),
        [
            pltpu.VMEM((grid.rows, DIRECT + POOLED), BF16),
            pltpu.VMEM((grid.rows, DIRECT + POOLED), BF16),
            pltpu.VMEM(turned.shape, BF16),
            pltpu.VMEM((grid.rows, REDUCED), BF16),
            pltpu.VMEM((grid.rows, DIRECT + POOLED), BF16),
            *Spread.scratch(grid),
            pltpu.VMEM((product_rows, 768), F32),
            Lines.semaphores(grid, 4),
            pltpu.SemaphoreType.DMA((2,)),
            pltpu.SemaphoreType.DMA((1,)),
        ],
        scalars=1,
        cost=8,
        far=(5, 6, 7, 8, 9),
        far_out=(0,),
    )(length, outer, after(total, packed), outer_gain, dx_small, h_outer, slope, kept_direct, turned, h_reduced)
    share = add_up(exchange(packed))
    rest_pieces = exchange(rest_product)
    d_low, share = lax.optimization_barrier((after(d_low, rest_product), share))
    r_low, sums_low, products = call(
        functools.partial(conv_back, grid, slots, 0),
        (
            shape((grid.rows, REDUCED), BF16),
            shape((clips, 2, REDUCED), F32),
            shape((clips, 2, product_rows // clips, 128), F32),
        ),
        [
            *conv_back_scratch(grid),
            pltpu.VMEM(turned.shape, BF16),
            pltpu.VMEM((product_rows, REDUCED), F32),
            pltpu.SemaphoreType.DMA((1,)),
        ],
        scalars=1,
        cost=22,
        far=(5, 6, 7, 8),
    )(
        length,
        d_low,
        h_reduced,
        reduced_gain,
        reduced_shift,
        *kernels[0][:2],
        kernels[0][3],
        turned,
    )
    whole = lax.all_gather(share, ("branch", "dp"), axis=0)
    sums_low, rest_pieces = lax.optimization_barrier((sums_low, rest_pieces))
    gathered = exchange(sums_low)
    pieces = exchange(products)
    dx, reduced_total = call(
        functools.partial(mid_back, grid, 0),
        (shape((grid.rows, own_channels), BF16), shape((2, REDUCED), F32)),
        [
            pltpu.VMEM((grid.rows, DIRECT + POOLED), BF16),
            pltpu.VMEM((grid.rows, REDUCED), BF16),
            pltpu.VMEM((grid.rows, REDUCED), BF16),
            pltpu.VMEM((FIRST, own_channels), BF16),
            pltpu.VMEM((grid.rows, own_channels), BF16),
            Lines.semaphores(grid, 3),
            pltpu.SemaphoreType.DMA((1,)),
            pltpu.SemaphoreType.DMA((1,)),
        ],
        scalars=2,
        cost=8,
        far=(5, 6, 7, 8),
        far_out=(0,),
    )(length, place_one, moment, gathered, reduced_gain, du_rest, h_reduced, r_low, point_first)
    pieces, dx = lax.optimization_barrier((pieces, dx))
    point_sum = call(
        functools.partial(combine, 0),
        shape((5 * product_rows // clips, 128), BF16),
        cost=1,
    )(rest_pieces, pieces, moment, gathered, reduced_gain)
    received = spread_over(point_sum, "branch", parts)

    outs = (
        shape((2, TAPS, MID_IN, MID_OUT), F32),
        shape((2, TAPS, SMALL_IN, SMALL_OUT), F32),
        shape((2, SQUEEZED, CHANNELS), F32),
    )
    tap_scratch = [
        pltpu.VMEM((TAPS, MID_IN, MID_OUT), F32),
        pltpu.VMEM((TAPS, SMALL_IN, SMALL_OUT), F32),
    ]
    point_scratch = [pltpu.VMEM((SQUEEZED, CHANNELS), F32), pltpu.VMEM((CHANNELS, 128), F32)]
    mid_grad, small_grad = call(
        functools.partial(unpack_second, clips, taps_each),
        outs[:2],
        [*tap_scratch, pltpu.SemaphoreType.DMA((2,))],
        far_out=(0, 1),
        cost=5,
    )(whole_small)
    received, mid_grad, small_grad = lax.optimization_barrier((received, mid_grad, small_grad))
    norms = shape((2, 1024), F32)
    mid_grad, small_grad, point_grad, gain_grad, shift_grad = call(
        functools.partial(unpack_first, parts, clips, taps_each, tap_share),
        (*outs, norms, norms),
        [*tap_scratch, *point_scratch, pltpu.SemaphoreType.DMA((3,))],
        far_out=(0, 1, 2),
        aliases={5: 0, 6: 1},
        cost=6,
    )(whole, total, reduced_total, total_small, reduced_total_small, mid_grad, small_grad)
    point_mine, point_other = gather_chips(
        jnp.concatenate(received, axis=0), clips, (mid_grad, small_grad)
    )
    clip_one = lax.axis_index("dp").astype(jnp.int32).reshape(1)
    point_grad = call(
        functools.partial(unpack_point, parts, clips, own_channels),
        outs[2],
        [
            pltpu.VMEM((parts, FIRST // 128, product_rows, 128), BF16),
            *point_scratch,
            pltpu.SemaphoreType.DMA((1,)),
        ],
        scalars=2,
        far_out=(0,),
        aliases={4: 0},
        cost=3,
    )(place_one, clip_one, point_mine, point_other, point_grad)
    act = act.reshape(small.side, small.side, cotangent.shape[1], CHANNELS).transpose(2, 0, 1, 3)
    input_grad = dx.reshape(side, side, grid.unit, own_channels).transpose(2, 0, 1, 3)
    return (
        act[None],
        input_grad[None],
        point_grad.swapaxes(1, 2),
        mid_grad,
        small_grad,
        gain_grad,
        shift_grad,
    )


def solution(mesh):
    split = P("dp", None, None, None, "branch")
    whole = P("dp", None, None, None, None)
    return jax.shard_map(
        on_device,
        mesh=mesh,
        in_specs=(split, P("dp"), whole, P(), P(), P(), P(), P()),
        out_specs=(whole, split, P(), P(), P(), P(), P()),
        check_vma=False,
    )
```

```python
import functools

import jax
import jax.numpy as jnp
from jax import lax
from jax.experimental import pallas as pl
from jax.experimental.pallas import tpu as pltpu
from jax.sharding import PartitionSpec as P

DIRECT = 256
MID_IN = 160
MID_OUT = 320
SMALL_IN = 32
SMALL_OUT = 128
TAPS = 27
CHANNELS = 832
SQUEEZED = 576
TILE = 16
REDUCED = 256
POOLED = 128
FIRST = 640
SECOND = 512
OUTER = 896
TAP_ROWS = 432
EPSILON = 1e-05
F32 = jnp.float32
BF16 = jnp.bfloat16
VMEM_BYTES = 58 * 2**20
LARGE = 2200 * 2**10


def call(body, out_shape, scratch=(), scalars=0, cost=5, vmem=VMEM_BYTES, aliases=None, far=(), far_out=()):
    aliases = aliases or {}

    def large(values):
        size = values.dtype.itemsize
        for extent in values.shape:
            size = size * extent
        return size > LARGE

    def placed(out):
        return pltpu.HBM(out.shape, out.dtype) if large(out) else out

    def run(*operands):
        specs = [
            pl.BlockSpec(
                memory_space=pl.ANY
                if number in aliases or number in far
                else pltpu.SMEM
                if number < scalars
                else pltpu.VMEM
            )
            for number in range(len(operands))
        ]
        operands = [
            pltpu.with_memory_space_constraint(operand, pltpu.HBM) if large(operand) else operand
            for operand in operands
        ]
        if isinstance(out_shape, tuple):
            out_specs = tuple(
                pl.BlockSpec(memory_space=pl.ANY if number in far_out else pltpu.VMEM)
                for number in range(len(out_shape))
            )
        else:
            out_specs = pl.BlockSpec(memory_space=pl.ANY if 0 in far_out else pltpu.VMEM)
        return pl.pallas_call(
            body,
            out_shape=jax.tree.map(placed, out_shape),
            in_specs=specs,
            out_specs=out_specs,
            input_output_aliases=aliases,
            scratch_shapes=list(scratch),
            compiler_params=pltpu.CompilerParams(vmem_limit_bytes=vmem),
            cost_estimate=pl.CostEstimate(
                flops=0, bytes_accessed=int(cost * 3 * 10**6), transcendentals=0
            ),
        )(*operands)

    return run


def shape(dims, dtype):
    return jax.ShapeDtypeStruct(tuple(dims), dtype)


def rows_at(start, size):
    return pl.ds(pl.multiple_of(start, 16), size)


def frames_of(values_or_rows, unit):
    dims = values_or_rows if isinstance(values_or_rows, tuple) else (values_or_rows, 128)
    return lax.broadcasted_iota(jnp.int32, dims, 0) & (unit - 1)


def keep_frames(values, unit, lo, hi):
    rows, width = values.shape
    frame = lax.broadcasted_iota(jnp.int32, (1, unit, width), 1)
    kept = jnp.where((frame >= lo) & (frame < hi), 1.0, 0.0)
    return (values.reshape(rows // unit, unit, width) * kept).reshape(rows, width)


def earlier(values, unit):
    return keep_frames(pltpu.roll(values, 1, 0), unit, 1, unit)


def later(values, unit):
    return keep_frames(pltpu.roll(values, values.shape[0] - 1, 0), unit, 0, unit - 1)


def plane_box(values, unit):
    across = values + earlier(values, unit) + later(values, unit)
    edge = jnp.zeros((unit, values.shape[1]), values.dtype)
    return (
        across
        + jnp.concatenate([across[unit:], edge], axis=0)
        + jnp.concatenate([edge, across[:-unit]], axis=0)
    )


def box_window(grid, length):
    frame, place = (frames_of(grid.line_rows, grid.unit), grid.places_of(grid.line_rows))

    def one(condition):
        return jnp.where(condition, 1.0, 0.0)

    count = one(frame < length) + one(frame + 1 < length) + one((frame > 0) & (frame - 1 < length))
    return count * (3.0 - one(place == 0) - one(place == grid.side - 1))


def box_scale(line, side, window):
    lines = 3.0 - jnp.where(line == 0, 1.0, 0.0) - jnp.where(line == side - 1, 1.0, 0.0)
    return 1.0 / jnp.maximum(window * lines, 1.0)


def sigmoid(value):
    return 0.5 * jnp.tanh(0.5 * value) + 0.5


def silu(value):
    return value * sigmoid(value)


def silu_slope(value):
    gate = sigmoid(value)
    return gate * (1.0 + value * (1.0 - gate))


def partial_sum(values):
    rows, width = values.shape
    return jnp.sum(values.reshape(rows // 8, 8, width), axis=0)


def moments(total, square, count):
    center = total / count
    return (center, lax.rsqrt(square / count - center * center + EPSILON))


def total_of(gathered):
    count = len(gathered) if isinstance(gathered, (list, tuple)) else gathered.shape[0]
    total = gathered[0][...]
    for number in range(1, count):
        total = total + gathered[number][...]
    return total


def pool_matrix(grid, small, transposed):
    line = grid.line_rows
    few, many = (small.line_rows, 2 * line)
    dims = (many, few) if transposed else (few, many)
    coarse = lax.broadcasted_iota(jnp.int32, dims, 1 if transposed else 0)
    fine = lax.broadcasted_iota(jnp.int32, dims, 0 if transposed else 1)
    fine = jnp.where(fine >= line, fine - line, fine)
    same = (fine >> (grid.bits + 1) == coarse >> small.bits) & (
        (fine & (grid.unit - 1)) >> 1 == coarse & (small.unit - 1)
    )
    return jnp.where(same, 0.125, 0.0).astype(BF16)


class Grid:
    def __init__(self, side, unit):
        self.side, self.unit = (side, unit)
        self.bits = unit.bit_length() - 1
        self.copies = TILE // unit
        self.line_rows = side * unit if self.copies == 1 else (side + 1) * unit
        self.rows = side * self.line_rows
        self.pitch = (side + 1) * unit
        margin = 1 if self.copies == 1 else 2
        self.lead = margin * self.pitch + TILE
        self.padded = (side + 2 * margin) * self.pitch + 2 * TILE
        self.group = 2 if side % 2 == 0 else side

    def places_of(self, rows):
        place = lax.broadcasted_iota(jnp.int32, (rows, 128), 0) >> self.bits
        return place if self.copies == 1 else place & self.side

    def mask(self, rows, length, width=128):
        valid = frames_of(rows, self.unit) < length
        if self.copies > 1:
            valid = valid & (self.places_of(rows) < self.side)
        mask = jnp.where(valid, 1.0, 0.0)
        return jnp.concatenate([mask] * (width // 128), axis=1) if width > 128 else mask

    def near(self, ref, base, lines, places, size, lanes=slice(None)):
        start = base + lines * self.pitch
        if self.copies == 1:
            return ref[0, rows_at(start + places * TILE, size), lanes]
        copy = 0 if places == 0 else 1
        return ref[copy, rows_at(start - (TILE if places < 0 else 0), size), lanes]


class Slots:
    def __init__(self, grid, parts):
        self.pairs = grid.side // 2
        self.parts = parts
        self.each = -(-self.pairs // parts)
        self.empty = parts * self.each - self.pairs
        self.gap = parts * self.each // 2 - 1
        self.pair_rows = 2 * grid.line_rows
        self.grid = grid
        self.rows = self.each * self.pair_rows

    def slot_of(self, pair):
        return pair + jnp.where(pair >= self.gap, self.empty, 0)

    def pair_of(self, slot):
        return slot - jnp.where(slot >= self.gap, self.empty, 0)

    def used(self, slot):
        return (slot < self.gap) | (slot >= self.gap + self.empty)

    def held(self, place):
        count = jnp.zeros((), jnp.int32)
        for number in range(self.each):
            count = count + jnp.where(self.used(place * self.each + number), 1, 0)
        return count


def clear_empty(grid, ref):
    width = ref.shape[2]
    if grid.copies > 1:
        ref[...] = jnp.zeros_like(ref)
        return
    ref[0, 0 : grid.lead, :] = jnp.zeros((grid.lead, width), ref.dtype)
    end = grid.lead + grid.side * grid.pitch
    ref[0, end:, :] = jnp.zeros((ref.shape[1] - end, width), ref.dtype)

    @pl.loop(0, grid.side)
    def _(line):
        at = rows_at(grid.lead + line * grid.pitch + grid.line_rows, TILE)
        ref[0, at, :] = jnp.zeros((TILE, width), ref.dtype)


def store_taps(unit, mid_ref, small_ref, copy, at, act):
    before, after_ = (earlier(act, unit), later(act, unit))
    mid_ref[copy, at, 0:128] = before[:, :128].astype(BF16)
    mid_ref[copy, at, 128:256] = act[:, :128].astype(BF16)
    mid_ref[copy, at, 256:384] = after_[:, :128].astype(BF16)
    before, act, after_ = (before[:, 128:], act[:, 128:], after_[:, 128:])
    lane = lax.broadcasted_iota(jnp.int32, act.shape, 1)
    mid_ref[copy, at, 384:512] = jnp.where(
        lane < 32, before, jnp.where(lane < 64, pltpu.roll(act, 32, 1), pltpu.roll(after_, 64, 1))
    ).astype(BF16)
    small_ref[copy, at, :] = jnp.where(
        lane < 32, pltpu.roll(before, 96, 1), jnp.where(lane < 64, act, pltpu.roll(after_, 32, 1))
    ).astype(BF16)


def near_tap(grid, ref, base, tap, sign, size, lanes=slice(None)):
    return grid.near(ref, base, sign * (tap // 3 - 1), sign * (tap % 3 - 1), size, lanes)


def convolve(grid, taps, kernels, rest_ref, acc_ref, stage_ref, e_ref, stage_sem, sums_ref, length):
    mid_ref, small_ref = taps
    main_ref, last_ref, small_kernel_ref = kernels
    group_rows = grid.group * grid.pitch
    stage_rows = grid.group * grid.line_rows
    groups = grid.side // grid.group
    sums_ref[...] = jnp.zeros_like(sums_ref)
    mask = grid.mask(grid.line_rows, length, SECOND)
    edge = jnp.zeros((grid.pitch, 256), F32)
    rest_ref[grid.lead - grid.pitch : grid.lead, :] = edge
    end = grid.lead + grid.side * grid.pitch
    rest_ref[end : end + grid.pitch, :] = edge

    @pl.loop(0, groups)
    def _(group):
        base = grid.lead + group * group_rows
        total = None
        for place in range(3):
            part = jnp.dot(
                grid.near(mid_ref, base, 0, place - 1, group_rows),
                last_ref[place],
                preferred_element_type=F32,
            )
            total = part if total is None else total + part
        rest_ref[rows_at(base, group_rows), :] = total

    lane = lax.broadcasted_iota(jnp.int32, (grid.line_rows, 128), 1)

    def staged(group, slot):
        return pltpu.make_async_copy(
            stage_ref.at[slot],
            e_ref.at[rows_at(group * stage_rows, stage_rows), :],
            stage_sem.at[slot],
        )

    @pl.loop(0, groups)
    def _(group):
        base = grid.lead + group * group_rows
        slot = lax.rem(group, 2)
        for tap in range(9):
            part = jnp.dot(
                near_tap(grid, mid_ref, base, tap, 1, group_rows),
                main_ref[tap],
                preferred_element_type=F32,
            )
            acc_ref[:, 0:256] = part if tap == 0 else acc_ref[:, 0:256] + part
        near = [near_tap(grid, small_ref, base, tap, 1, group_rows) for tap in range(9)]
        acc_ref[:, 256:384] = jnp.dot(
            jnp.concatenate(near, axis=1), small_kernel_ref[...], preferred_element_type=F32
        )

        @pl.when(group >= 2)
        def _():
            staged(group - 2, slot).wait()

        for number in range(grid.group):
            rows = grid.line_rows
            start = base + number * grid.pitch
            last = (
                rest_ref[rows_at(start - grid.pitch, rows), 0:128]
                + pltpu.roll(rest_ref[rows_at(start, rows), 0:128], 64, 1)
                + rest_ref[rows_at(start + grid.pitch, rows), 128:256]
            )
            lines = slice(number * grid.pitch, number * grid.pitch + rows)
            values = jnp.concatenate(
                [acc_ref[lines, 0:256], jnp.where(lane < 64, last, 0.0), acc_ref[lines, 256:384]],
                axis=1,
            )
            stage_ref[slot, number * rows : (number + 1) * rows, :] = values
            masked = values * mask
            sums_ref[0:8] += partial_sum(masked)
            sums_ref[8:16] += partial_sum(masked * values)
        staged(group, slot).start()

    for group in range(max(groups - 2, 0), groups):
        staged(group, group % 2).wait()


def conv_scratch(grid):
    group_rows = grid.group * grid.pitch
    return [
        pltpu.VMEM((9, 512, 256), BF16),
        pltpu.VMEM((3, 512, 256), BF16),
        pltpu.VMEM((1152, 128), BF16),
        pltpu.VMEM((grid.copies, grid.padded, 512), BF16),
        pltpu.VMEM((grid.copies, grid.padded, 128), BF16),
        pltpu.VMEM((grid.rows, REDUCED), BF16),
        pltpu.VMEM((grid.padded, 256), F32),
        pltpu.VMEM((group_rows, 384), F32),
        pltpu.VMEM((2, grid.group * grid.line_rows, SECOND), F32),
        pltpu.VMEM((16, SECOND), F32),
        pltpu.SemaphoreType.DMA((3,)),
        pltpu.SemaphoreType.DMA((3,)),
        pltpu.SemaphoreType.DMA((2,)),
    ]


def conv_outputs(grid, *clips):
    return (
        shape((grid.rows, REDUCED), BF16),
        shape((grid.copies, grid.padded, 512), BF16),
        shape((grid.copies, grid.padded, 128), BF16),
        shape((grid.rows, SECOND), F32),
        shape((*clips, 2, SECOND), F32),
    )


def copies(sources, targets, sem_ref):
    return [
        pltpu.make_async_copy(source, target, sem_ref.at[number])
        for number, (source, target) in enumerate(zip(sources, targets))
    ]


def run_convolution(grid, length, far_kernels, outputs, scratch, fill):
    h_out, mid_out, small_out, e_out, sums_out = outputs
    kernels, (mid_ref, small_ref, h_ref), rest = (scratch[:3], scratch[3:6], scratch[6:])
    rest_ref, acc_ref, stage_ref, sums_ref, in_sem, out_sem, stage_sem = rest
    arriving = copies(far_kernels, kernels, in_sem)
    for copy in arriving:
        copy.start()
    clear_empty(grid, mid_ref)
    clear_empty(grid, small_ref)
    fill(h_ref, mid_ref, small_ref)
    leaving = copies((mid_ref, small_ref, h_ref), (mid_out, small_out, h_out), out_sem)
    for copy in leaving:
        copy.start()
    for copy in arriving:
        copy.wait()
    convolve(
        grid, (mid_ref, small_ref), kernels, rest_ref, acc_ref, stage_ref, e_out, stage_sem, sums_ref, length
    )
    write_sums(sums_out, sums_ref, 0, SECOND)
    for copy in leaving:
        copy.wait()


def write_row(out_ref, row, lo, hi, values):
    if len(out_ref.shape) == 2:
        out_ref[row : row + 1, lo:hi] = values
    else:
        for clip in range(out_ref.shape[0]):
            out_ref[clip, row : row + 1, lo:hi] = values


def write_sums(out_ref, sums_ref, lo, hi):
    for number in range(2):
        values = jnp.sum(sums_ref[8 * number : 8 * number + 8], axis=0, keepdims=True)
        write_row(out_ref, number, lo, hi, values)


def turn(slots, x_ref, out_ref):
    for slot in range(slots.parts * slots.each):
        part, number = divmod(slot, slots.each)
        lanes = slice(number * slots.pair_rows, (number + 1) * slots.pair_rows)
        if slots.gap <= slot < slots.gap + slots.empty:
            out_ref[part, :, lanes] = jnp.zeros((out_ref.shape[1], slots.pair_rows), BF16)
            continue
        pair = slot - (slots.empty if slot >= slots.gap else 0)
        rows = slice(pair * slots.pair_rows, (pair + 1) * slots.pair_rows)
        out_ref[part, :, lanes] = x_ref[rows, :].T


def first_pointwise(slots, length_ref, count_ref, x_ref, p_ref, mid_ref, pool_ref, direct_ref, sums_ref, u_ref):
    rows, step = (slots.rows, 112)
    length, count = (length_ref[0], count_ref[0])
    for part in range(slots.parts):
        product = lax.dot_general(
            x_ref[part], p_ref[part], (((0,), (1,)), ((), ())), preferred_element_type=F32
        )
        u_ref[...] = product if part == 0 else u_ref[...] + product
    mask = slots.grid.mask(step, length, FIRST)

    def summed(number, carry):
        values = u_ref[rows_at(number * step, step), :] * mask
        u_ref[rows_at(number * step, step), :] = values
        few = values[:, :SECOND]
        return (carry[0] + partial_sum(values), carry[1] + partial_sum(few * few))

    zero = (jnp.zeros((8, FIRST), F32), jnp.zeros((8, SECOND), F32))
    total, square = lax.fori_loop(0, rows // step, summed, zero)
    total = jnp.sum(total, axis=0, keepdims=True)
    write_row(sums_ref, 0, 0, SECOND, total[:, :SECOND])
    write_row(sums_ref, 1, 0, SECOND, jnp.sum(square, axis=0, keepdims=True))
    write_row(sums_ref, 2, 0, SECOND, jnp.full((1, SECOND), count, F32))
    offset = (total / jnp.full((1, FIRST), jnp.maximum(count, 1.0), F32)).astype(BF16)
    wide_offset = offset.astype(F32)
    tail = jnp.broadcast_to(wide_offset, (TILE, FIRST)).astype(BF16)
    pool_ref[rows : rows + TILE, :] = tail[:, SECOND:]
    shared = mid_ref.shape[0] - 2 * TILE
    mid_ref[shared : shared + TILE, :] = tail[:, 256:384]
    mid_ref[shared + TILE :, :] = tail[:, 384:512]

    @pl.loop(0, rows // step)
    def _(number):
        at = rows_at(number * step, step)
        values = u_ref[at, :]
        direct_ref[at, :] = values[:, :DIRECT]
        values = values[:, DIRECT:] - wide_offset[:, DIRECT:]
        mid_ref[at, :] = values[:, :128].astype(BF16)
        pool_ref[at, :] = values[:, 256:].astype(BF16)

    lane = lax.broadcasted_iota(jnp.int32, (step, 128), 1)
    for couple in range(0, slots.each, 2):

        @pl.loop(0, slots.pair_rows // step)
        def _(number):
            start = couple * slots.pair_rows + number * step
            values = u_ref[rows_at(start, step), 384:512] - wide_offset[:, 384:512]
            if couple + 1 < slots.each:
                other = u_ref[rows_at(start + slots.pair_rows, step), 384:512]
                other = pltpu.roll(other - wide_offset[:, 384:512], 64, 1)
                values = jnp.where(lane < 64, values, other)
            place = rows + couple // 2 * slots.pair_rows + number * step
            mid_ref[rows_at(place, step), :] = values.astype(BF16)


def mid_rows(slots):
    return slots.rows + -(-slots.each // 2) * slots.pair_rows + 2 * TILE


def each_pair(slots, place, refs, visit):
    for step, ref in enumerate(refs):
        source = lax.rem(place - step + slots.parts, slots.parts)
        for number in range(slots.each):
            slot = source * slots.each + number

            @pl.when(slots.used(slot))
            def _():
                visit(slots.pair_of(slot), ref, number)


def set_moments(total, moment_ref):
    count = total[2:3]
    center, inverse = moments(total[0:1], total[1:2], count)
    moment_ref[0:1, :] = center
    moment_ref[1:2, :] = inverse
    moment_ref[2:3, :] = count
    return (center, inverse)


def first_convolve(grid, slots, block, length_ref, place_ref, *refs):
    parts = slots.parts
    mids, sums, refs = (refs[:parts], refs[parts : 2 * parts], refs[2 * parts :])
    gain_ref, shift_ref, *refs = refs
    far_kernels, outputs, scratch = (refs[:3], refs[3:8], refs[8:])
    length = length_ref[0]
    total = total_of(sums)[:, DIRECT:]
    center, inverse = moments(total[0:1], total[1:2], total[2:3])
    gain, shift = (gain_ref[block : block + 1], shift_ref[block : block + 1])
    step = 112
    mask = grid.mask(step, length, REDUCED)
    lane = lax.broadcasted_iota(jnp.int32, (step, 128), 1)

    def fill(h_ref, mid_ref, small_ref):
        def visit(pair, ref, number):
            shared = ref.shape[0] - 2 * TILE
            offset = jnp.concatenate(
                [
                    ref[at : at + TILE, :].astype(F32)[0:1]
                    for at in (shared, shared + TILE)
                ],
                axis=1,
            )
            other = slots.rows + number // 2 * slots.pair_rows

            @pl.loop(0, slots.pair_rows // step)
            def _(chunk):
                values = ref[rows_at(number * slots.pair_rows + chunk * step, step), :].astype(F32)
                few = ref[rows_at(other + chunk * step, step), :].astype(F32)
                if number % 2 == 1:
                    few = pltpu.roll(few, 64, 1)
                few = jnp.where(lane < 64, few, 0.0)
                values = jnp.concatenate([values, few], axis=1) + offset
                scaled = (values - center) * inverse
                row = pair * slots.pair_rows + chunk * step
                h_ref[rows_at(row, step), :] = scaled.astype(BF16)
                act = silu(gain * scaled + shift) * mask
                line = row // grid.line_rows
                at = grid.lead + line * grid.pitch + row - line * grid.line_rows
                store_taps(grid.unit, mid_ref, small_ref, 0, rows_at(at, step), act)

        each_pair(slots, place_ref[0], mids, visit)

    run_convolution(grid, length, far_kernels, outputs, scratch, fill)


def pool_planes(grid, plane_ref, q_ref, lo, sums_ref, length, window):
    rows = grid.line_rows
    mask = grid.mask(rows, length)
    sums_ref[...] = jnp.zeros_like(sums_ref)

    @pl.loop(0, grid.side)
    def _(line):
        start = line * rows
        values = (
            plane_ref[rows_at(start, rows), :]
            + plane_ref[rows_at(start + rows, rows), :]
            + plane_ref[rows_at(start + 2 * rows, rows), :]
        ) * box_scale(line, grid.side, window)
        q_ref[rows_at(start, rows), lo : lo + POOLED] = values
        masked = values * mask
        sums_ref[0:8] += partial_sum(masked)
        sums_ref[8:16] += partial_sum(masked * values)


def clear_edges(grid, plane_ref):
    rows = grid.line_rows
    plane_ref[0:rows] = jnp.zeros((rows, POOLED), F32)
    plane_ref[grid.rows + rows : grid.rows + 2 * rows] = jnp.zeros((rows, POOLED), F32)


def first_pool(grid, slots, length_ref, place_ref, *refs):
    pools, refs = (refs[: slots.parts], refs[slots.parts :])
    e_sums_ref, q_ref, out_sums_ref, plane_ref, sums_ref = refs
    length = length_ref[0]
    rows = grid.line_rows
    for row in range(2):
        write_row(out_sums_ref, row, 0, SECOND, e_sums_ref[row : row + 1, :])
    clear_edges(grid, plane_ref)

    def visit(pair, ref, number):
        offset = ref[slots.rows : slots.rows + TILE, :].astype(F32)[0:1]
        for line in range(2):
            at = rows_at(number * slots.pair_rows + line * rows, rows)
            plane_ref[rows_at((2 * pair + line + 1) * rows, rows), :] = plane_box(
                ref[at, :].astype(F32) + offset, grid.unit
            )

    each_pair(slots, place_ref[0], pools, visit)
    pool_planes(grid, plane_ref, q_ref, 0, sums_ref, length, box_window(grid, length))
    write_sums(out_sums_ref, sums_ref, SECOND, FIRST)


def normalize(values, center, inverse, gain, shift, mask):
    scaled = (values - center) * inverse
    shifted = gain * scaled + shift
    gate = sigmoid(shifted)
    gate_mask = gate * mask
    act = shifted * gate_mask
    return (scaled, act, gate_mask + act * (1.0 - gate))


def pool_pieces(matrix, pieces):
    return jnp.dot(
        matrix, jnp.concatenate(pieces, axis=0), preferred_element_type=F32
    ).astype(BF16)


def first_direct(grid, small, slots, block, length_ref, u_ref, gain_ref, shift_ref, *refs):
    sums, (pooled_ref, kept_ref, moment_ref) = (refs[: slots.parts], refs[slots.parts :])
    rows = grid.line_rows
    mask = grid.mask(rows, length_ref[0], DIRECT)
    center, inverse = set_moments(total_of(sums), moment_ref)
    center, inverse = (center[:, :DIRECT], inverse[:, :DIRECT])
    gain, shift = (gain_ref[block : block + 1, :DIRECT], shift_ref[block : block + 1, :DIRECT])
    matrix = pool_matrix(grid, small, False)

    @pl.loop(0, slots.each)
    def _(number):
        acts, slopes, products = ([], [], [])
        for line in range(2):
            at = rows_at(number * slots.pair_rows + line * rows, rows)
            scaled, act, slope = normalize(u_ref[at, :], center, inverse, gain, shift, mask)
            kept_ref[at, 0:DIRECT] = scaled.astype(BF16)
            kept_ref[at, DIRECT : 2 * DIRECT] = slope.astype(BF16)
            acts.append(act.astype(BF16))
            slopes.append(slope.astype(BF16))
            products.append((slope * scaled).astype(BF16))
        size = small.line_rows
        pooled_ref[rows_at(number * size, size), :] = pool_pieces(matrix, acts)
        at = rows_at(slots.rows + number * size, size)
        kept_ref[at, 0:DIRECT] = pool_pieces(matrix, slopes)
        kept_ref[at, DIRECT : 2 * DIRECT] = pool_pieces(matrix, products)


def outer_moments(center, inverse, count, outer_ref):
    outer_ref[0:1, :] = center
    outer_ref[1:2, :] = inverse
    outer_ref[2:3, :] = jnp.concatenate([count[:, 0:128]] * (OUTER // 128), axis=1)


def first_output(grid, small, block, length_ref, q_far, e_far, moment_ref, sums_in_ref, gain_ref, shift_ref, *refs):
    pooled_ref, h_far, slope_far, outer_ref, pooled_slope_ref, pooled_product_ref, *refs = refs
    q_ref, e_ref, h_ref, slope_ref, q_sem, e_sem, h_sem, slope_sem = refs
    rows = grid.line_rows
    wide = 2 * rows
    pairs = grid.side // 2

    def arriving(pair, slot):
        at = rows_at(pair * wide, wide)
        return [
            pltpu.make_async_copy(q_far.at[at, :], q_ref.at[slot], q_sem.at[slot]),
            pltpu.make_async_copy(e_far.at[at, :], e_ref.at[slot], e_sem.at[slot]),
        ]

    def leaving(pair, slot):
        at = rows_at(pair * wide, wide)
        return [
            pltpu.make_async_copy(h_ref.at[slot], h_far.at[at, :], h_sem.at[slot]),
            pltpu.make_async_copy(slope_ref.at[slot], slope_far.at[at, :], slope_sem.at[slot]),
        ]

    for copy in arriving(0, 0):
        copy.start()
    mask = grid.mask(rows, length_ref[0], FIRST)
    total = total_of(sums_in_ref)
    count = jnp.concatenate([moment_ref[2:3, 0:128]] * (FIRST // 128), axis=1)
    center, inverse = moments(total[0:1], total[1:2], count)
    outer_moments(
        jnp.concatenate([moment_ref[0:1, :DIRECT], center], axis=1),
        jnp.concatenate([moment_ref[1:2, :DIRECT], inverse], axis=1),
        count,
        outer_ref,
    )
    matrix = pool_matrix(grid, small, False)
    gain, shift = (gain_ref[block : block + 1, DIRECT:], shift_ref[block : block + 1, DIRECT:])

    @pl.loop(0, pairs)
    def _(pair):
        slot = lax.rem(pair, 2)

        @pl.when(pair + 1 < pairs)
        def _():
            for copy in arriving(pair + 1, 1 - slot):
                copy.start()

        for copy in arriving(pair, slot):
            copy.wait()

        @pl.when(pair >= 2)
        def _():
            for copy in leaving(pair - 2, slot):
                copy.wait()

        acts, slopes, products = ([], [], [])
        for number in range(2):
            lines = slice(number * rows, (number + 1) * rows)
            values = jnp.concatenate([e_ref[slot, lines, :], q_ref[slot, lines, :]], axis=1)
            scaled, act, slope = normalize(values, center, inverse, gain, shift, mask)
            h_ref[slot, lines, :] = scaled.astype(BF16)
            low_slope = slope.astype(BF16)
            slope_ref[slot, lines, :] = low_slope
            acts.append(act.astype(BF16))
            slopes.append(low_slope)
            products.append((slope * scaled).astype(BF16))
        for copy in leaving(pair, slot):
            copy.start()
        at = rows_at(pair * small.line_rows, small.line_rows)
        pooled_ref[at, :] = pool_pieces(matrix, acts)
        pooled_slope_ref[at, :] = pool_pieces(matrix, slopes)
        pooled_product_ref[at, :] = pool_pieces(matrix, products)

    for pair in range(max(pairs - 2, 0), pairs):
        for copy in leaving(pair, pair % 2):
            copy.wait()


def second_pointwise(grid, slots, length_ref, place_ref, count_ref, *refs):
    directs, refs = (refs[: slots.parts], refs[slots.parts :])
    rest_ref, p_ref, q_ref, out_sums_ref, x_ref, plane_ref, sums_ref, pool_sums_ref = refs
    length = length_ref[0]
    rows = grid.line_rows
    sums_ref[...] = jnp.zeros_like(sums_ref)
    clear_edges(grid, plane_ref)
    x_ref[:, DIRECT:] = rest_ref[...]

    def visit(pair, ref, number):
        x_ref[rows_at(pair * rows, rows), 0:DIRECT] = ref[number * rows : (number + 1) * rows, :]

    each_pair(slots, place_ref[0], directs, visit)
    q_ref[...] = lax.dot_general(
        x_ref[...], p_ref[...], (((1,), (1,)), ((), ())), preferred_element_type=F32
    )

    @pl.loop(0, grid.side)
    def _(line):
        values = q_ref[rows_at(line * rows, rows), :]
        sums_ref[0:8] += partial_sum(values[:, :SECOND])
        sums_ref[8:16] += partial_sum(values[:, :SECOND] * values[:, :SECOND])
        plane_ref[rows_at((line + 1) * rows, rows), :] = plane_box(
            values[:, SECOND:], grid.unit
        )

    pool_planes(grid, plane_ref, q_ref, SECOND, pool_sums_ref, length, box_window(grid, length))
    write_sums(out_sums_ref, sums_ref, 0, SECOND)
    write_sums(out_sums_ref, pool_sums_ref, SECOND, FIRST)
    write_row(out_sums_ref, 2, 0, FIRST, jnp.full((1, FIRST), count_ref[0], F32))


def clear_ends(grid, ref):
    edge = jnp.zeros((grid.line_rows, ref.shape[1]), F32)
    ref[0 : grid.line_rows, :] = edge
    ref[grid.rows + grid.line_rows :, :] = edge


def store_copies(grid, ref, store):
    @pl.loop(0, grid.side + 1)
    def _(number):
        start = number * grid.line_rows
        at = rows_at(grid.lead + (number - 1) * grid.pitch, grid.line_rows)
        store(0, at, ref[rows_at(start, grid.line_rows), :])
        moved = pl.ds(pl.multiple_of(start + grid.unit, grid.unit), grid.line_rows)
        store(1, at, ref[moved, :])


def second_convolve(grid, block, length_ref, q_ref, sums_in_ref, gain_ref, shift_ref, *refs):
    far_kernels, outputs, moment_ref, scratch = (refs[:3], refs[3:8], refs[8], refs[9:])
    length = length_ref[0]
    center, inverse = set_moments(total_of(sums_in_ref), moment_ref)
    center, inverse = (center[:, DIRECT:SECOND], inverse[:, DIRECT:SECOND])
    gain, shift = (gain_ref[block : block + 1], shift_ref[block : block + 1])
    rows = grid.line_rows
    mask = grid.mask(rows, length, REDUCED)
    scratch, act_ref = (scratch[:-1], scratch[-1])

    def fill(h_ref, mid_ref, small_ref):
        clear_ends(grid, act_ref)

        @pl.loop(0, grid.side)
        def _(line):
            at = rows_at(line * rows, rows)
            scaled = (q_ref[at, DIRECT:SECOND] - center) * inverse
            h_ref[at, :] = scaled.astype(BF16)
            act_ref[rows_at((line + 1) * rows, rows), :] = silu(gain * scaled + shift) * mask

        def store(copy, at, values):
            store_taps(grid.unit, mid_ref, small_ref, copy, at, values)

        store_copies(grid, act_ref, store)

    run_convolution(grid, length, far_kernels, outputs, scratch, fill)


def second_output(grid, block, length_ref, q_ref, e_ref, moment_ref, sums_in_ref, gain_ref, shift_ref, cot_ref, act_ref, h_ref, error_ref, outer_ref, out_sums_ref, sums_ref):
    rows = grid.line_rows
    side, frames = (grid.side, cot_ref.shape[1])
    mask = grid.mask(rows, length_ref[0], OUTER)
    total = total_of(sums_in_ref)
    count = moment_ref[2:3, 0:SECOND]
    center, inverse = moments(total[0:1], total[1:2], count)
    center = jnp.concatenate([moment_ref[0:1, :DIRECT], center, moment_ref[0:1, SECOND:]], axis=1)
    inverse = jnp.concatenate([moment_ref[1:2, :DIRECT], inverse, moment_ref[1:2, SECOND:]], axis=1)
    outer_moments(center, inverse, count, outer_ref)
    sums_ref[...] = jnp.zeros_like(sums_ref)
    gain, shift = (gain_ref[block : block + 1], shift_ref[block : block + 1])
    gap = jnp.zeros((rows, 64), F32)
    unused = jnp.zeros((grid.unit, CHANNELS), F32)

    @pl.loop(0, side)
    def _(line):
        at = rows_at(line * rows, rows)
        places = pl.ds(line * side, side)
        values = jnp.concatenate([q_ref[at, :DIRECT], e_ref[at, :], q_ref[at, SECOND:]], axis=1)
        scaled = (values - center) * inverse
        h_ref[at, :] = scaled.astype(BF16)
        shifted = gain * scaled + shift
        gate = sigmoid(shifted)
        act = (shifted * gate * mask).reshape(side + 1, frames, OUTER)[:side].astype(BF16)
        act_ref[places, :, 0:576] = act[:, :, 0:576]
        act_ref[places, :, 576:CHANNELS] = act[:, :, 640:OUTER]
        slope = gate * (1.0 + shifted * (1.0 - gate))
        grad = cot_ref[places].astype(F32).reshape(side * frames, CHANNELS)
        grad = jnp.concatenate([grad, unused], axis=0)
        grad = jnp.concatenate([grad[:, :576], gap, grad[:, 576:]], axis=1)
        error = grad * slope * mask
        error_ref[at, :] = error.astype(BF16)
        sums_ref[0:8] += partial_sum(error)
        sums_ref[8:16] += partial_sum(error * scaled)

    write_sums(out_sums_ref, sums_ref, 0, OUTER)


def spread_matrix(grid, small):
    return None if small is None else pool_matrix(grid, small, True)[: grid.line_rows]


def outer_error(slopes, small, grad_ref, matrix, line, lo, hi):
    values = slopes.astype(F32)
    if small is None:
        return values
    coarse = grad_ref[rows_at((line // 2) * small.line_rows, small.line_rows), lo:hi]
    return values * jnp.dot(matrix, coarse, preferred_element_type=F32)


class Lines:
    def __init__(self, grid, sources, buffers, sem_ref):
        self.step = 2 if grid.side % 2 == 0 else 1
        self.size = self.step * grid.line_rows
        self.steps = grid.side // self.step
        self.sources, self.buffers, self.sem = (sources, buffers, sem_ref)

    def copies(self, step):
        at = rows_at(step * self.size, self.size)
        copies = []
        for number, ((ref, lo, hi), (buffer, place)) in enumerate(zip(self.sources, self.buffers)):
            source = ref(step, lo, hi) if callable(ref) else ref.at[at, pl.ds(lo, hi - lo)]
            target = buffer.at[at, pl.ds(place, hi - lo)]
            copies.append(pltpu.make_async_copy(source, target, self.sem.at[number, step]))
        return copies

    def first(self):
        @pl.loop(0, self.steps)
        def _(step):
            for copy in self.copies(step):
                copy.start()

    def run(self, visit):
        @pl.loop(0, self.steps)
        def _(step):
            for copy in self.copies(step):
                copy.wait()
            visit(step)

    @staticmethod
    def semaphores(grid, count):
        return pltpu.SemaphoreType.DMA((count, grid.side // 2 if grid.side % 2 == 0 else grid.side))


def second_back(grid, small, block, slots, length_ref, first_ref, h_far, outer_ref, sums_in_ref, gain_ref, slope_far, *refs):
    first = small is not None
    (grad_ref, carried_ref), refs = (refs[:2], refs[2:]) if first else ((None, None), refs)
    mid_far, few_far, d_far, total_ref, out_ref, *refs = refs
    d_ref, h_ref, slope_ref, mid_ref, few_ref, mid_acc_ref, small_acc_ref, turned_ref, sem_ref, in_sem, out_sem, *refs = refs
    lo, hi = (DIRECT, DIRECT + SECOND)
    at = 0 if first else DIRECT
    lines = Lines(
        grid,
        ((h_far, at, at + SECOND), (slope_far, at, at + SECOND)),
        ((h_ref, 0), (slope_ref, 0)),
        sem_ref,
    )
    lines.first()
    arriving = copies((mid_far, few_far), (mid_ref, few_ref), in_sem)
    for copy in arriving:
        copy.start()
    total = total_of(sums_in_ref)
    total_ref[...] = total
    a, b, c = before_norm(
        gain_ref[block : block + 1, lo:hi], outer_ref[1:2, lo:hi], total[:, lo:hi], outer_ref[2:3, lo:hi]
    )
    mask = grid.mask(grid.line_rows, length_ref[0], SECOND)
    matrix = spread_matrix(grid, small)
    clear_empty(grid, d_ref)
    rows = grid.line_rows
    if first:
        share = out_ref.shape[1] - carried_ref.shape[1]
        for clip in range(out_ref.shape[0]):
            out_ref[clip, share:, :] = carried_ref[clip]

    def visit(step):
        for number in range(lines.step):
            line = step * lines.step + number
            here = rows_at(line * rows, rows)
            scaled = h_ref[here, :].astype(F32)
            error = outer_error(slope_ref[here, :], small, grad_ref, matrix, line, lo, hi)
            back = (a * error - b - c * scaled) * mask
            if grid.copies == 1:
                d_ref[0, rows_at(grid.lead + line * grid.pitch, rows), :] = back.astype(BF16)
            else:
                refs[0][rows_at((line + 1) * rows, rows), :] = back

    lines.run(visit)
    if grid.copies > 1:
        clear_ends(grid, refs[0])

        def store(copy, at, values):
            d_ref[copy, at, :] = values.astype(BF16)

        store_copies(grid, refs[0], store)
    leaving = pltpu.make_async_copy(d_ref, d_far, out_sem.at[0])
    leaving.start()
    for copy in arriving:
        copy.wait()
    kernel_grads(grid, slots, first_ref, mid_ref, few_ref, d_ref, out_ref, mid_acc_ref, small_acc_ref, turned_ref)
    leaving.wait()


def before_norm(gain, inverse, sums, count):
    factor = gain * inverse
    return (factor, factor * sums[0:1] / count, factor * sums[1:2] / count)


def second_back_scratch(grid, slots):
    return [
        pltpu.VMEM((grid.copies, grid.padded, SECOND), BF16),
        pltpu.VMEM((grid.rows, SECOND), BF16),
        pltpu.VMEM((grid.rows, SECOND), BF16),
        pltpu.VMEM((grid.copies, grid.padded, 512), BF16),
        pltpu.VMEM((grid.copies, grid.padded, 128), BF16),
        pltpu.VMEM((slots, 384, 256), F32),
        pltpu.VMEM((slots, 128, 128), F32),
        pltpu.VMEM((MID_IN + 128, 128), F32),
        Lines.semaphores(grid, 2),
        pltpu.SemaphoreType.DMA((2,)),
        pltpu.SemaphoreType.DMA((1,)),
        *([pltpu.VMEM((grid.rows + 2 * grid.line_rows, SECOND), F32)] if grid.copies > 1 else []),
    ]


def conv_back(grid, slots, block, length_ref, d_ref, reduced_ref, reduced_gain_ref, reduced_shift_ref, *refs):
    far_kernels, refs = (refs[:3], refs[3:])
    first = len(refs) > 9
    x_far, refs = (refs[0], refs[1:]) if first else (None, refs)
    r_ref, out_sums_ref, *refs = refs
    product_out, refs = (refs[0], refs[1:]) if first else (None, refs)
    kernels, (last_ref, acc_ref, sums_ref, in_sem, *refs) = (refs[:3], refs[3:])
    if first:
        x_ref, product_ref, x_sem = refs
        x_copy = pltpu.make_async_copy(x_far, x_ref, x_sem.at[0])
        x_copy.start()
    main_ref, rest_ref, small_ref = kernels
    arriving = copies(far_kernels, kernels, in_sem)
    for copy in arriving:
        copy.start()
    rows = grid.line_rows
    group_rows = grid.group * grid.pitch
    sums_ref[...] = jnp.zeros_like(sums_ref)
    mask = grid.mask(rows, length_ref[0], REDUCED)
    gain, shift = (reduced_gain_ref[block : block + 1], reduced_shift_ref[block : block + 1])
    turned = (((1,), (1,)), ((), ()))
    lane = lax.broadcasted_iota(jnp.int32, (rows, 128), 1)
    wide_lane = lax.broadcasted_iota(jnp.int32, (grid.pitch, 128), 1)

    for copy in range(grid.copies):

        @pl.loop(1 - grid.copies, grid.side)
        def _(line):
            place = grid.lead + line * grid.pitch

            def lanes(start):
                return d_ref[copy, rows_at(start, grid.pitch), 256:384]

            further, here = (lanes(place + grid.pitch).astype(F32), lanes(place).astype(F32))
            at = rows_at(place, grid.pitch)
            last_ref[copy, at, 0:128] = jnp.where(
                wide_lane < 64, further, pltpu.roll(here, 64, 1)
            ).astype(BF16)
            last_ref[copy, at, 128:256] = lanes(place - grid.pitch)

        if grid.copies == 1:
            last_ref[copy, grid.lead - TILE : grid.lead, :] = jnp.zeros((TILE, 256), BF16)
        end = grid.lead + grid.side * grid.pitch
        last_ref[copy, end : end + TILE, :] = jnp.zeros((TILE, 256), BF16)
    for copy in arriving:
        copy.wait()

    @pl.loop(0, grid.side // grid.group)
    def _(group):
        base = grid.lead + group * group_rows
        for tap in range(9):
            part = lax.dot_general(
                near_tap(grid, d_ref, base, tap, -1, group_rows, slice(0, 256)),
                main_ref[tap],
                turned,
                preferred_element_type=F32,
            )
            acc_ref[:, 0:512] = part if tap == 0 else acc_ref[:, 0:512] + part
        for place in range(3):
            acc_ref[:, 0:512] += lax.dot_general(
                grid.near(last_ref, base, 0, 1 - place, group_rows),
                rest_ref[place],
                turned,
                preferred_element_type=F32,
            )
        near = [
            near_tap(grid, d_ref, base, tap, -1, group_rows, slice(384, 512)) for tap in range(9)
        ]
        acc_ref[:, 512:640] = jnp.dot(
            jnp.concatenate(near, axis=1), small_ref[...], preferred_element_type=F32
        )
        for number in range(grid.group):
            line = group * grid.group + number
            lines = slice(number * grid.pitch, number * grid.pitch + rows)
            rest, small = (acc_ref[lines, 384:512], acc_ref[lines, 512:640])
            one = jnp.where(lane < 32, rest, pltpu.roll(small, 32, 1))
            two = jnp.where(lane < 32, pltpu.roll(rest, 96, 1), small)
            three = jnp.where(lane < 32, pltpu.roll(rest, 64, 1), pltpu.roll(small, 96, 1))
            unit = grid.unit
            wide = later(acc_ref[lines, 0:128], unit) + acc_ref[lines, 128:256]
            wide = wide + earlier(acc_ref[lines, 256:384], unit)
            narrow = jnp.where(lane < 64, later(one, unit) + two + earlier(three, unit), 0.0)
            back = jnp.concatenate([wide, narrow], axis=1)
            at = rows_at(line * rows, rows)
            scaled = reduced_ref[at, :].astype(F32)
            error = back * silu_slope(gain * scaled + shift) * mask
            r_ref[at, :] = error.astype(BF16)
            sums_ref[0:8] += partial_sum(error)
            sums_ref[8:16] += partial_sum(error * scaled)

    write_sums(out_sums_ref, sums_ref, 0, REDUCED)
    if first:
        x_copy.wait()
        write_products(
            slots,
            x_ref,
            lambda start, size: r_ref[start : start + size, :],
            product_ref,
            product_out,
        )


def kernel_grads(grid, slots, first_ref, mid_ref, small_ref, d_ref, out_ref, mid_acc_ref, small_acc_ref, turned_ref):
    group_rows = grid.group * grid.pitch
    mid_acc_ref[...] = jnp.zeros_like(mid_acc_ref)
    small_acc_ref[...] = jnp.zeros_like(small_acc_ref)

    def neighbour(slot):
        return jnp.minimum(first_ref[0] + slot, TAPS - 1) // 9

    @pl.loop(0, grid.side // grid.group)
    def _(group):
        base = grid.lead + group * group_rows
        left = d_ref[0, rows_at(base, group_rows), :].T
        for slot in range(slots):
            tap = lax.rem(jnp.minimum(first_ref[0] + slot, TAPS - 1), 9)
            start = base + (tap // 3 - 1) * grid.pitch
            place = lax.rem(tap, 3) - 1
            copy = 0
            if grid.copies == 1:
                start = start + place * TILE
            else:
                copy = jnp.where(place == 0, 0, 1)
                start = start - jnp.where(place < 0, TILE, 0)
            at = rows_at(start, group_rows)
            lanes = pl.ds(pl.multiple_of(neighbour(slot) * 128, 128), 128)
            right = jnp.concatenate([mid_ref[copy, at, lanes], mid_ref[copy, at, 384:512]], axis=1)
            mid_acc_ref[slot] += jnp.dot(left[0:384], right, preferred_element_type=F32)
            small_acc_ref[slot] += jnp.dot(
                left[384:512], small_ref[copy, at, :], preferred_element_type=F32
            )

    share = round_up(slots * TAP_ROWS, 16 * out_ref.shape[0]) // out_ref.shape[0]

    def put(start, values):
        done = 0
        while done < values.shape[0]:
            clip, at = divmod(start + done, share)
            size = min(values.shape[0] - done, share - at)
            out_ref[clip, at : at + size, :] = values[done : done + size].astype(BF16)
            done = done + size

    half = MID_IN // 2
    for slot in range(slots):
        base = slot * TAP_ROWS
        rest = pl.ds(pl.multiple_of(neighbour(slot) * 32, 32), 32)
        for tile in range(3):
            lines = slice(128 * tile, 128 * (tile + 1))
            turned_ref[0:128, :] = mid_acc_ref[slot, lines, 0:128].T
            turned_ref[MID_IN : MID_IN + 128, :] = mid_acc_ref[slot, lines, 128:256].T
            turned_ref[128:MID_IN, :] = turned_ref[
                pl.ds(pl.multiple_of(MID_IN + neighbour(slot) * 32, 32), 32), :
            ]
            if tile < 2:
                put(base + MID_IN * tile, turned_ref[0:MID_IN, :])
            else:
                folded = turned_ref[0:half, :] + pltpu.roll(turned_ref[half:MID_IN, :], 64, 1)
                put(base + 2 * MID_IN, folded)
        turned_ref[0:128, :] = small_acc_ref[slot].T
        put(base + 2 * MID_IN + half, turned_ref[rest, :])
    used = slots * TAP_ROWS
    put(used, jnp.zeros((share * out_ref.shape[0] - used, 128), F32))


class Spread:
    def __init__(self, grid, plane_ref, across_ref, scale_ref, length):
        self.grid, self.plane, self.across, self.scale = (grid, plane_ref, across_ref, scale_ref)
        clear_edges(grid, plane_ref)
        window = box_window(grid, length)
        scale_ref[0] = box_scale(0, grid.side, window)
        scale_ref[1] = box_scale(1, grid.side, window)
        unit = grid.unit
        edge = jnp.zeros((unit, POOLED), F32)
        across_ref[0:unit, :] = edge
        across_ref[unit + grid.line_rows :, :] = edge

    def put(self, line, values):
        rows = self.grid.line_rows
        inner = jnp.where((line == 0) | (line == self.grid.side - 1), 0, 1)
        values = values * self.scale[inner]
        across, unit = (self.across, self.grid.unit)
        across[unit : unit + rows, :] = values + earlier(values, unit) + later(values, unit)
        self.plane[rows_at((line + 1) * rows, rows), :] = (
            across[0:rows, :] + across[unit : unit + rows, :] + across[2 * unit :, :]
        )

    def get(self, start, size):
        rows = self.grid.line_rows
        return (
            self.plane[rows_at(start, size), :]
            + self.plane[rows_at(start + rows, size), :]
            + self.plane[rows_at(start + 2 * rows, size), :]
        )

    @staticmethod
    def scratch(grid):
        return [
            pltpu.VMEM((grid.rows + 2 * grid.line_rows, POOLED), F32),
            pltpu.VMEM((grid.line_rows + 2 * grid.unit, POOLED), F32),
            pltpu.VMEM((2, grid.line_rows, POOLED), F32),
        ]


def channel_products(slots, x_ref, right_of):
    total = None
    for part in range(slots.parts):
        slot = part * slots.each
        pair = slot - (slots.empty if slot >= slots.gap + slots.empty else 0)
        pair = min(pair, slots.pairs - slots.each)
        product = jnp.dot(
            x_ref[part], right_of(pair * slots.pair_rows, slots.rows), preferred_element_type=F32
        )
        total = product if total is None else total + product
    return total


def write_products(slots, x_ref, right_of, product_ref, product_out):
    channels = x_ref.shape[1]
    product_ref[0:channels, :] = channel_products(slots, x_ref, right_of)
    product_ref[channels:, :] = jnp.zeros((product_ref.shape[0] - channels, product_ref.shape[1]), F32)
    clips, tiles, size, _ = product_out.shape
    for clip in range(clips):
        for tile in range(tiles):
            product_out[clip, tile] = product_ref[
                clip * size : (clip + 1) * size, 128 * tile : 128 * (tile + 1)
            ]


def rest_constants(outer_ref, total_ref, gain_ref, block):
    pool = OUTER - POOLED

    def pick(ref, lo, hi):
        return jnp.concatenate([ref[lo:hi, 0:DIRECT], ref[lo:hi, pool:]], axis=1)

    return before_norm(
        pick(gain_ref, block, block + 1), pick(outer_ref, 1, 2), pick(total_ref, 0, 2), pick(outer_ref, 2, 3)
    )


def point_back(grid, slots, block, kept, length_ref, place_ref, h_far, outer_ref, total_ref, gain_ref, error_far, reduced_far, r_far, moment_ref, sums_in_ref, reduced_gain_ref, x_far, p_far, *refs):
    pooled_slope_in, pooled_product_in, kept_far, *refs = refs
    dx_ref, dp_ref, reduced_total_ref, outer_sums_ref, *refs = refs
    h_ref, error_ref, reduced_ref, r_ref, x_ref, p_ref, du_ref, acc_ref, *refs = refs
    plane_ref, across_ref, scale_ref, sums_ref, pooled_slope_ref, pooled_product_ref, kept_ref, *refs = refs
    sem_ref, in_sem = refs
    rows = grid.line_rows
    pool = OUTER - POOLED
    lines = Lines(
        grid,
        (
            (h_far, 0, DIRECT),
            (h_far, pool, OUTER),
            (error_far, 0, DIRECT),
            (error_far, pool, OUTER),
            (reduced_far, 0, REDUCED),
            (r_far, 0, REDUCED),
        ),
        ((h_ref, 0), (h_ref, DIRECT), (error_ref, 0), (error_ref, DIRECT), (reduced_ref, 0), (r_ref, 0)),
        sem_ref,
    )
    lines.first()
    kept_rows = kept_ref.shape[1]
    arriving = copies(
        (x_far, p_far, kept_far.at[:, pl.ds(slots.rows, kept_rows), :]), (x_ref, p_ref, kept_ref), in_sem
    )
    for copy in arriving:
        copy.start()
    length = length_ref[0]
    total = total_of(sums_in_ref)
    reduced_total_ref[...] = total
    mid = before_norm(
        reduced_gain_ref[block : block + 1],
        moment_ref[1:2, DIRECT:SECOND],
        total,
        outer_ref[2:3, 0:REDUCED],
    )
    rest = rest_constants(outer_ref, total_ref, gain_ref, block)
    mask = grid.mask(rows, length, DIRECT + POOLED)
    spread = Spread(grid, plane_ref, across_ref, scale_ref, length)

    def visit(line):
        at = rows_at(line * rows, rows)
        back = rest[0] * error_ref[at, :].astype(F32) - rest[1] - rest[2] * h_ref[at, :].astype(F32)
        back = back * mask
        du_ref[at, 0:DIRECT] = back[:, :DIRECT].astype(BF16)
        spread.put(line, back[:, DIRECT:])
        back = mid[0] * r_ref[at, :].astype(F32) - mid[1] - mid[2] * reduced_ref[at, :].astype(F32)
        du_ref[at, DIRECT:SECOND] = (back * mask[:, :REDUCED]).astype(BF16)

    lines.run(visit)
    for copy in arriving:
        copy.wait()
    sums_ref[...] = jnp.zeros_like(sums_ref)
    pooled_slope_ref[:, DIRECT:] = pooled_slope_in[...]
    pooled_product_ref[:, DIRECT:] = pooled_product_in[...]
    for pair in range(slots.pairs):
        slot = pair + (slots.empty if pair >= slots.gap else 0)
        at = slice(pair * rows, (pair + 1) * rows)
        start = slot % slots.each * rows
        values = kept_ref[slot // slots.each, start : start + rows, :]
        pooled_slope_ref[at, 0:DIRECT] = values[:, :DIRECT]
        pooled_product_ref[at, 0:DIRECT] = values[:, DIRECT:]

    @pl.loop(0, grid.side)
    def _(line):
        at = rows_at(line * rows, rows)
        du_ref[at, SECOND:] = (spread.get(line * rows, rows) * mask[:, :POOLED]).astype(BF16)
        dx = jnp.dot(du_ref[at, :], p_ref[...], preferred_element_type=F32).astype(BF16)
        dx_ref[at, :] = dx
        for number, ref in enumerate((pooled_slope_ref, pooled_product_ref)):
            sums_ref[8 * number : 8 * number + 8] += partial_sum(
                dx.astype(F32) * ref[at, :].astype(F32)
            )

    write_sums(outer_sums_ref, sums_ref, 0, OUTER)
    acc_ref[...] = lax.dot_general(
        x_ref[...], du_ref[...], (((0,), (0,)), ((), ())), preferred_element_type=F32
    )
    start = pl.multiple_of(place_ref[0] * kept, 16) if kept < acc_ref.shape[0] else 0
    clips, size, _ = dp_ref.shape
    for tile in range(FIRST // 128):
        values = acc_ref[pl.ds(start, kept), 128 * tile : 128 * (tile + 1)].astype(BF16)
        done = 0
        while done < kept:
            clip, at = divmod(kept * tile + done, size)
            few = min(kept - done, size - at)
            dp_ref[clip, at : at + few, :] = values[done : done + few]
            done = done + few
    used = (FIRST // 128) * kept
    while used < clips * size:
        clip, at = divmod(used, size)
        dp_ref[clip, at:, :] = jnp.zeros((size - at, 128), BF16)
        used = used + size - at


def rest_back(grid, small, slots, block, length_ref, outer_ref, total_ref, gain_ref, grad_ref, h_far, slope_far, kept_far, x_far, reduced_far, du_far, product_out, *refs):
    h_ref, slope_ref, x_ref, reduced_ref, du_ref, plane_ref, across_ref, scale_ref, product_ref, sem_ref, in_sem, du_sem = refs
    rows = grid.line_rows
    pool = OUTER - POOLED

    def direct(step, lo, hi):
        slot = slots.slot_of(step)
        at = rows_at(lax.rem(slot, slots.each) * slots.pair_rows, slots.pair_rows)
        return kept_far.at[slot // slots.each, at, pl.ds(lo, hi - lo)]

    lines = Lines(
        grid,
        (
            (direct, 0, DIRECT),
            (h_far, SECOND, FIRST),
            (direct, DIRECT, 2 * DIRECT),
            (slope_far, SECOND, FIRST),
        ),
        ((h_ref, 0), (h_ref, DIRECT), (slope_ref, 0), (slope_ref, DIRECT)),
        sem_ref,
    )
    lines.first()
    arriving = copies((x_far, reduced_far), (x_ref, reduced_ref), in_sem)
    for copy in arriving:
        copy.start()
    length = length_ref[0]
    matrix = spread_matrix(grid, small)
    a, b, c = rest_constants(outer_ref, total_ref, gain_ref, block)
    mask = grid.mask(rows, length, DIRECT + POOLED)
    spread = Spread(grid, plane_ref, across_ref, scale_ref, length)

    def visit(step):
        for number in range(lines.step):
            line = step * lines.step + number
            at = rows_at(line * rows, rows)
            coarse = grad_ref[rows_at((line // 2) * small.line_rows, small.line_rows), :]
            grad = jnp.dot(
                matrix,
                jnp.concatenate([coarse[:, :DIRECT], coarse[:, pool:]], axis=1),
                preferred_element_type=F32,
            )
            back = a * (grad * slope_ref[at, :].astype(F32)) - b - c * h_ref[at, :].astype(F32)
            back = back * mask
            du_ref[at, 0:DIRECT] = back[:, :DIRECT].astype(BF16)
            spread.put(line, back[:, DIRECT:])

    lines.run(visit)
    for copy in arriving:
        copy.wait()
    wide = lines.size
    pool_mask = grid.mask(wide, length)

    def leaving(step):
        at = rows_at(step * wide, wide)
        return pltpu.make_async_copy(du_ref.at[at, :], du_far.at[at, :], du_sem.at[0])

    @pl.loop(0, lines.steps)
    def _(step):
        at = rows_at(step * wide, wide)
        du_ref[at, DIRECT:] = (spread.get(step * wide, wide) * pool_mask).astype(BF16)
        leaving(step).start()

    ones = grid.mask(slots.rows, length)
    two_ones = jnp.concatenate([ones, ones], axis=1)

    def right_of(start, size):
        at = slice(start, start + size)
        scaled = (reduced_ref[at, :].astype(F32) * two_ones).astype(BF16)
        return jnp.concatenate([du_ref[at, :], scaled, ones.astype(BF16)], axis=1)

    write_products(slots, x_ref, right_of, product_ref, product_out)
    pltpu.make_async_copy(du_ref, du_far, du_sem.at[0]).wait()


def mid_back(grid, block, length_ref, place_ref, moment_ref, sums_in_ref, gain_ref, du_far, h_far, r_far, p_far, dx_far, total_ref, *refs):
    du_ref, h_ref, r_ref, p_ref, dx_ref, sem_ref, p_sem, dx_sem = refs
    lines = Lines(
        grid,
        ((du_far, 0, DIRECT + POOLED), (h_far, 0, REDUCED), (r_far, 0, REDUCED)),
        ((du_ref, 0), (h_ref, 0), (r_ref, 0)),
        sem_ref,
    )
    lines.first()
    p_copy = pltpu.make_async_copy(p_far.at[place_ref[0]], p_ref, p_sem.at[0])
    p_copy.start()
    total = total_of(sums_in_ref)
    total_ref[...] = total
    a, b, c = before_norm(
        gain_ref[block : block + 1], moment_ref[1:2, DIRECT:], total, moment_ref[2:3, DIRECT:]
    )
    mask = grid.mask(lines.size, length_ref[0], REDUCED)
    p_copy.wait()

    def leaving(step):
        at = rows_at(step * lines.size, lines.size)
        return pltpu.make_async_copy(dx_ref.at[at, :], dx_far.at[at, :], dx_sem.at[0])

    def visit(step):
        at = rows_at(step * lines.size, lines.size)
        back = a * r_ref[at, :].astype(F32) - b - c * h_ref[at, :].astype(F32)
        du = jnp.concatenate(
            [du_ref[at, :DIRECT], (back * mask).astype(BF16), du_ref[at, DIRECT:]], axis=1
        )
        dx_ref[at, :] = jnp.dot(du, p_ref[...], preferred_element_type=F32).astype(BF16)
        leaving(step).start()

    lines.run(visit)
    pltpu.make_async_copy(dx_ref, dx_far, dx_sem.at[0]).wait()


def combine(block, rest_ref, pieces_ref, moment_ref, sums_in_ref, gain_ref, out_ref):
    total = total_of(sums_in_ref)
    a, b, c = before_norm(
        gain_ref[block : block + 1], moment_ref[1:2, DIRECT:], total, moment_ref[2:3, DIRECT:]
    )
    size = out_ref.shape[0] // 5
    rest, products = (total_of(rest_ref), total_of(pieces_ref))
    for tile in range(2):
        out_ref[size * tile : size * (tile + 1), :] = rest[tile].astype(BF16)
        lanes = slice(128 * tile, 128 * (tile + 1))
        mid = a[:, lanes] * products[tile] - b[:, lanes] * rest[5] - c[:, lanes] * rest[3 + tile]
        out_ref[size * (2 + tile) : size * (3 + tile), :] = mid.astype(BF16)
    out_ref[4 * size :, :] = rest[2].astype(BF16)


def write_taps(read, slots, mid_ref, small_ref, mid_out, small_out, sem_ref):
    half = MID_IN // 2

    def leaving(tap):
        return (
            pltpu.make_async_copy(mid_ref.at[tap], mid_out.at[tap], sem_ref.at[0]),
            pltpu.make_async_copy(small_ref.at[tap], small_out.at[tap], sem_ref.at[1]),
        )

    for tap in range(TAPS):
        part, slot = divmod(tap, slots)
        base = slot * TAP_ROWS
        folded = read(part, base + 2 * MID_IN, half)
        mid_ref[tap, :, 0:128] = read(part, base, MID_IN)
        mid_ref[tap, :, 128:256] = read(part, base + MID_IN, MID_IN)
        mid_ref[tap, 0:half, 256:320] = folded[:, 0:64]
        mid_ref[tap, half:MID_IN, 256:320] = pltpu.roll(folded, 64, 1)[:, 0:64]
        small_ref[tap] = read(part, base + 2 * MID_IN + half, SMALL_IN)
        for copy in leaving(tap):
            copy.start()
    pltpu.make_async_copy(mid_ref, mid_out, sem_ref.at[0]).wait()
    pltpu.make_async_copy(small_ref, small_out, sem_ref.at[1]).wait()


def write_point(read, parts, kept, point_ref, wide_ref):
    for tile in range(FIRST // 128):
        for part in range(parts):
            start, stop = (kept * part, kept * (part + 1))
            values = read(part, kept * tile, kept)
            if kept * parts == CHANNELS:
                wide_ref[start:stop, :] = values
                continue
            for lo, hi, moved in ((0, 576, 0), (640, OUTER, 64)):
                lo, hi = (max(lo, start), min(hi, stop))
                if lo < hi:
                    wide_ref[lo - moved : hi - moved, :] = values[lo - start : hi - start]
        turned = wide_ref[...].T
        if tile < 3:
            point_ref[128 * tile : 128 * (tile + 1), :] = turned
        elif tile == 3:
            point_ref[384:448, :] = turned[0:64]
        else:
            point_ref[448:576, :] = turned


def copy_out(pairs, sem_ref):
    copies = [
        pltpu.make_async_copy(source, target, sem_ref.at[number])
        for number, (source, target) in enumerate(pairs)
    ]
    for copy in copies:
        copy.start()
    for copy in copies:
        copy.wait()


def share_reader(ref, clips, lo, share):
    def read(part, start, size):
        pieces, done = ([], 0)
        while done < size:
            clip, at = divmod(start + done, share)
            few = min(size - done, share - at)
            pieces.append(ref[part * clips + clip, lo + at : lo + at + few, :].astype(F32))
            done = done + few
        return pieces[0] if len(pieces) == 1 else jnp.concatenate(pieces, axis=0)

    return read


def unpack_second(clips, slots, shares_ref, mid_out, small_out, mid_ref, small_ref, sem_ref):
    read = share_reader(shares_ref, clips, 0, shares_ref.shape[1])
    write_taps(read, slots, mid_ref, small_ref, mid_out.at[1], small_out.at[1], sem_ref)


def unpack_first(parts, clips, slots, share, shares_ref, *refs):
    totals, refs = (refs[:4], refs[4:])
    mid_in, small_in, mid_out, small_out, point_out, gain_out, shift_out, *refs = refs
    mid_ref, small_ref, point_ref, wide_ref, sem_ref = refs
    for block in range(2):
        outer_ref, reduced_ref = totals[2 * block : 2 * block + 2]
        for row, out in enumerate((shift_out, gain_out)):
            at, line = (slice(block, block + 1), slice(row, row + 1))
            out[at, 0:256] = outer_ref[line, 0:256]
            out[at, 256:448] = reduced_ref[line, 0:192]
            out[at, 448:576] = outer_ref[line, 768:896]
            out[at, 576:896] = outer_ref[line, 256:576]
            out[at, 896:1024] = outer_ref[line, 640:768]
    read = share_reader(shares_ref, clips, share, shares_ref.shape[1] - share)
    write_point(read, parts, OUTER // parts, point_ref, wide_ref)
    last = pltpu.make_async_copy(point_ref, point_out.at[1], sem_ref.at[2])
    last.start()
    read = share_reader(shares_ref, clips, 0, share)
    write_taps(read, slots, mid_ref, small_ref, mid_out.at[0], small_out.at[0], sem_ref)
    last.wait()


def unpack_point(parts, clips, kept, place_ref, clip_ref, mine_ref, other_ref, point_in, point_out, buffer_ref, point_ref, wide_ref, sem_ref):
    tiles = FIRST // 128
    size = buffer_ref.shape[2] // clips
    for chip in range(clips // 2):
        for step in range(parts):
            part = lax.rem(place_ref[0] - step + parts, parts)
            for swapped, ref in enumerate((mine_ref, other_ref)):
                owner = clip_ref[0] ^ (2 * chip) ^ swapped
                source = (chip * parts + step) * tiles * size
                for tile in range(tiles):
                    buffer_ref[part, tile, rows_at(owner * size, size), :] = ref[
                        source + tile * size : source + (tile + 1) * size, :
                    ]

    def read(part, start, size):
        tile, at = divmod(start, kept)
        return buffer_ref[part, tile, at : at + size, :].astype(F32)

    write_point(read, parts, kept, point_ref, wide_ref)
    last = pltpu.make_async_copy(point_ref, point_out.at[0], sem_ref.at[0])
    last.start()
    last.wait()


def prepare(parts, mid_in, small_in, point_in, gain_in, shift_in, *refs):
    kernels, (point_ref, second_ref, *vectors) = (refs[:8], refs[8:14])
    for block in range(2):
        main_ref, last_ref, few_ref, back_ref = kernels[4 * block : 4 * block + 4]

        @pl.loop(0, 9)
        def _(tap):
            for number in range(3):
                source = 9 * number + tap
                main_ref[tap, 128 * number : 128 * (number + 1), :] = mid_in[block, source, 0:128, 0:256]
                main_ref[tap, 384 + 32 * number : 416 + 32 * number, :] = mid_in[
                    block, source, 128:MID_IN, 0:256
                ]
            main_ref[tap, 480:512, :] = jnp.zeros((32, 256), BF16)
            small = jnp.concatenate(
                [small_in[block, 9 * number + tap] for number in range(3)]
                + [jnp.zeros((32, 128), BF16)],
                axis=0,
            )
            at = pl.ds(pl.multiple_of(tap * 128, 128), 128)
            few_ref[at, :] = small
            back_ref[at, :] = small.astype(F32).T.astype(BF16)

        @pl.loop(0, 3)
        def _(place):
            for number in range(3):
                for rows, start, size in (
                    (slice(0, 128), 128 * number, 128),
                    (slice(128, MID_IN), 384 + 32 * number, 32),
                ):
                    pieces = [
                        mid_in[block, 9 * number + 3 * line + place, rows, 256:MID_OUT].astype(F32)
                        for line in range(3)
                    ]
                    pieces.append(jnp.zeros((size, 64), F32))
                    last_ref[place, start : start + size, :] = jnp.concatenate(
                        pieces, axis=1
                    ).astype(BF16)
            last_ref[place, 480:512, :] = jnp.zeros((32, 256), BF16)

    own = point_ref.shape[2]
    for lo, hi, at in ((0, 448, 0), (448, SQUEEZED, SECOND)):
        values = point_in[0, lo:hi, :].astype(F32)
        for part in range(parts):
            point_ref[part, at : at + hi - lo, :] = values[:, own * part : own * (part + 1)].astype(
                BF16
            )
        values = point_in[1, lo:hi, :].astype(F32)
        gap = jnp.zeros((hi - lo, 64), F32)
        second_ref[at : at + hi - lo, :] = jnp.concatenate(
            [values[:, :576], gap, values[:, 576:]], axis=1
        ).astype(BF16)
    for part in range(parts):
        point_ref[part, 448:SECOND, :] = jnp.zeros((64, own), BF16)
    second_ref[448:SECOND, :] = jnp.zeros((64, OUTER), BF16)
    for source, outer, reduced in ((gain_in, vectors[0], vectors[1]), (shift_in, vectors[2], vectors[3])):
        outer[:, 0:256] = source[:, 0:256]
        outer[:, 256:576] = source[:, 576:896]
        outer[:, 576:640] = jnp.zeros((2, 64), F32)
        outer[:, 640:768] = source[:, 896:1024]
        outer[:, 768:896] = source[:, 448:576]
        reduced[:, 0:192] = source[:, 256:448]
        reduced[:, 192:256] = jnp.zeros((2, 64), F32)


def round_up(value, unit):
    return -(-value // unit) * unit


def spread_over(values, axis, size):
    received = [values]
    for step in range(1, size):
        perm = [(source, (source + step) % size) for source in range(size)]
        received.append(lax.ppermute(values, axis, perm))
    return received


def after(values, earlier):
    return lax.optimization_barrier((values, earlier))[0]


def exchange(values):
    return lax.all_to_all(values, "dp", 0, 0, tiled=True)


def add_up(pieces):
    return jnp.sum(pieces.astype(F32), axis=0).astype(BF16)


def gather_chips(column, clips, work=None):
    columns = [column]
    for chip in range(1, clips // 2):
        perm = [(source, source ^ (2 * chip)) for source in range(clips)]
        columns.append(lax.ppermute(column, "dp", perm))
    if work is not None:
        columns = after(columns, work)
    mine = jnp.concatenate(columns, axis=0)
    other = lax.ppermute(mine, "dp", [(source, source ^ 1) for source in range(clips)])
    return (mine, other)


def on_device(frames, lengths, cotangent, pointwise, conv_mid, conv_small, gains, shifts):
    parts = lax.axis_size("branch")
    clips = lax.axis_size("dp")
    place = lax.axis_index("branch").astype(jnp.int32)
    side = frames.shape[2]
    grid, small = (Grid(side, frames.shape[1]), Grid(side // 2, frames.shape[1] // 2))
    slots = Slots(grid, parts)
    cells = side * side
    own_channels = frames.shape[-1]
    length = lengths.astype(jnp.int32)
    half_length = length // 2
    place_one = place.reshape(1)

    own = frames[0].transpose(1, 2, 0, 3).reshape(grid.rows, own_channels)
    turned = call(functools.partial(turn, slots), shape((parts, own_channels, slots.rows), BF16))(own)
    by_pairs = lax.all_to_all(turned, "branch", 0, 0, tiled=True)
    kernel_shapes = (
        shape((9, 512, 256), BF16),
        shape((3, 512, 256), BF16),
        shape((1152, 128), BF16),
        shape((1152, 128), BF16),
    )
    prepared = call(
        functools.partial(prepare, parts),
        (
            *kernel_shapes,
            *kernel_shapes,
            shape((parts, FIRST, own_channels), BF16),
            shape((FIRST, OUTER), BF16),
            shape((2, OUTER), F32),
            shape((2, REDUCED), F32),
            shape((2, OUTER), F32),
            shape((2, REDUCED), F32),
        ),
    )(conv_mid, conv_small, pointwise.swapaxes(1, 2), gains, shifts)
    kernels = (prepared[0:4], prepared[4:8])
    point_first, point_second, outer_gain, reduced_gain, outer_shift, reduced_shift = prepared[8:]

    local_count = (length * (slots.held(place) * 2 * side)).astype(F32)
    mid, pool, direct, sums = call(
        functools.partial(first_pointwise, slots),
        (
            shape((mid_rows(slots), 128), BF16),
            shape((slots.rows + TILE, POOLED), BF16),
            shape((slots.rows, DIRECT), F32),
            shape((clips, 3, SECOND), F32),
        ),
        [pltpu.VMEM((slots.rows, FIRST), F32)],
        scalars=2,
        vmem=VMEM_BYTES // 3,
    )(length, local_count, by_pairs, point_first)
    mids = spread_over(mid, "branch", parts)
    sums = spread_over(jnp.sum(exchange(sums), axis=0), "branch", parts)
    pools = spread_over(after(pool, (mids, sums)), "branch", parts)
    h_reduced, taps_mid, taps_few, e, e_sums = call(
        functools.partial(first_convolve, grid, slots, 0),
        conv_outputs(grid),
        conv_scratch(grid),
        scalars=2,
        cost=40,
        far=range(4 + 2 * parts, 7 + 2 * parts),
        far_out=range(4),
    )(length, place_one, *mids, *sums, reduced_gain, reduced_shift, *kernels[0][:3])
    q_pool, second_sums = call(
        functools.partial(first_pool, grid, slots),
        (shape((grid.rows, POOLED), F32), shape((clips, 2, FIRST), F32)),
        [
            pltpu.VMEM((grid.rows + 2 * grid.line_rows, POOLED), F32),
            pltpu.VMEM((16, POOLED), F32),
        ],
        scalars=2,
    )(length, place_one, *pools, e_sums)
    second_sums = exchange(second_sums)
    pooled_direct, kept_direct, moment = call(
        functools.partial(first_direct, grid, small, slots, 0),
        (
            shape((slots.each * small.line_rows, DIRECT), BF16),
            shape((slots.rows + slots.each * small.line_rows, 2 * DIRECT), BF16),
            shape((3, SECOND), F32),
        ),
        scalars=1,
        cost=3,
    )(length, direct, outer_gain, outer_shift, *sums)
    second_sums, pooled_direct = lax.optimization_barrier((second_sums, pooled_direct))
    pooled_directs = spread_over(pooled_direct, "branch", parts)
    kept_direct = lax.all_gather(after(kept_direct, second_sums), "branch", axis=0)
    pair = 2 * grid.line_rows
    pooled, h_outer, slope, outer, pooled_slope, pooled_product = call(
        functools.partial(first_output, grid, small, 0),
        (
            shape((small.rows, FIRST), BF16),
            shape((grid.rows, FIRST), BF16),
            shape((grid.rows, FIRST), BF16),
            shape((3, OUTER), F32),
            shape((small.rows, FIRST), BF16),
            shape((small.rows, FIRST), BF16),
        ),
        [
            pltpu.VMEM((2, pair, POOLED), F32),
            pltpu.VMEM((2, pair, SECOND), F32),
            pltpu.VMEM((2, pair, FIRST), BF16),
            pltpu.VMEM((2, pair, FIRST), BF16),
            *[pltpu.SemaphoreType.DMA((2,))] * 4,
        ],
        scalars=1,
        far=(1, 2),
        far_out=(1, 2),
    )(
        length,
        q_pool,
        e,
        moment,
        second_sums,
        outer_gain,
        outer_shift,
    )

    small_count = half_length.astype(F32) * float(small.side * small.side)
    q_small, sums_small, pooled = call(
        functools.partial(second_pointwise, small, slots),
        (
            shape((small.rows, FIRST), F32),
            shape((clips, 3, FIRST), F32),
            shape((small.rows, OUTER), BF16),
        ),
        [
            pltpu.VMEM((small.rows + 2 * small.line_rows, POOLED), F32),
            pltpu.VMEM((16, SECOND), F32),
            pltpu.VMEM((16, POOLED), F32),
        ],
        scalars=3,
    )(half_length, place_one, small_count, *pooled_directs, pooled, point_second)
    sums_small = exchange(sums_small)
    h_reduced_small, taps_mid_small, taps_few_small, e_small, e_sums_small, moment_small = call(
        functools.partial(second_convolve, small, 1),
        (*conv_outputs(small, clips), shape((3, FIRST), F32)),
        [*conv_scratch(small), pltpu.VMEM((small.rows + 2 * small.line_rows, REDUCED), F32)],
        scalars=1,
        far=range(5, 8),
        far_out=range(4),
    )(half_length, q_small, sums_small, reduced_gain, reduced_shift, *kernels[1][:3])
    e_sums_small = exchange(e_sums_small)
    cot = cotangent[0].transpose(1, 2, 0, 3).reshape(small.side**2, cotangent.shape[1], CHANNELS)
    act, h_outer_small, error_small, outer_small, outer_sums_small = call(
        functools.partial(second_output, small, 1),
        (
            shape(cot.shape, BF16),
            shape((small.rows, OUTER), BF16),
            shape((small.rows, OUTER), BF16),
            shape((3, OUTER), F32),
            shape((clips, 2, OUTER), F32),
        ),
        [pltpu.VMEM((16, OUTER), F32)],
        scalars=1,
    )(half_length, q_small, e_small, moment_small, e_sums_small, outer_gain, outer_shift, cot)

    taps_each = -(-TAPS // parts)
    tap_share = round_up(taps_each * TAP_ROWS, 16 * clips) // clips
    first_tap = place_one * taps_each

    def conv_back_scratch(at):
        return [
            pltpu.VMEM((9, 512, 256), BF16),
            pltpu.VMEM((3, 512, 256), BF16),
            pltpu.VMEM((1152, 128), BF16),
            pltpu.VMEM((at.copies, at.padded, 256), BF16),
            pltpu.VMEM((at.group * at.pitch, FIRST), F32),
            pltpu.VMEM((16, REDUCED), F32),
            pltpu.SemaphoreType.DMA((3,)),
        ]

    gathered = exchange(outer_sums_small)
    d_low, total_small, packed_small = call(
        functools.partial(second_back, small, None, 1, taps_each),
        (
            shape((small.copies, small.padded, SECOND), BF16),
            shape((2, OUTER), F32),
            shape((clips, tap_share, 128), BF16),
        ),
        second_back_scratch(small, taps_each),
        scalars=2,
        cost=8,
        far=(2, 6, 7, 8),
        far_out=(0,),
    )(
        half_length,
        first_tap,
        h_outer_small,
        outer_small,
        gathered,
        outer_gain,
        error_small,
        taps_mid_small,
        taps_few_small,
    )
    r_low, sums_low = call(
        functools.partial(conv_back, small, None, 1),
        (shape((small.rows, REDUCED), BF16), shape((clips, 2, REDUCED), F32)),
        conv_back_scratch(small),
        scalars=1,
        cost=8,
        far=(5, 6, 7),
    )(
        half_length,
        d_low,
        h_reduced_small,
        reduced_gain,
        reduced_shift,
        *kernels[1][:2],
        kernels[1][3],
    )
    share_small = add_up(exchange(packed_small))
    sums_low, share_small = lax.optimization_barrier((sums_low, share_small))
    gathered = exchange(sums_low)
    kept = OUTER // parts
    point_share = round_up(kept * (FIRST // 128), 16 * clips) // clips
    coarse_rows = slots.each * small.line_rows
    dx_small, point_packed, reduced_total_small, outer_sums = call(
        functools.partial(point_back, small, slots, 1, kept),
        (
            shape((small.rows, OUTER), BF16),
            shape((clips, point_share, 128), BF16),
            shape((2, REDUCED), F32),
            shape((clips, 2, OUTER), F32),
        ),
        [
            pltpu.VMEM((small.rows, DIRECT + POOLED), BF16),
            pltpu.VMEM((small.rows, DIRECT + POOLED), BF16),
            pltpu.VMEM((small.rows, REDUCED), BF16),
            pltpu.VMEM((small.rows, REDUCED), BF16),
            pltpu.VMEM((small.rows, OUTER), BF16),
            pltpu.VMEM((FIRST, OUTER), BF16),
            pltpu.VMEM((small.rows, FIRST), BF16),
            pltpu.VMEM((OUTER, FIRST), F32),
            *Spread.scratch(small),
            pltpu.VMEM((16, OUTER), F32),
            pltpu.VMEM((small.rows, OUTER), BF16),
            pltpu.VMEM((small.rows, OUTER), BF16),
            pltpu.VMEM((parts, coarse_rows, 2 * DIRECT), BF16),
            Lines.semaphores(small, 6),
            pltpu.SemaphoreType.DMA((3,)),
        ],
        scalars=2,
        cost=10,
        far=(2, 6, 7, 8, 12, 13, 16),
    )(
        half_length,
        place_one,
        h_outer_small,
        outer_small,
        total_small,
        outer_gain,
        error_small,
        h_reduced_small,
        r_low,
        moment_small,
        gathered,
        reduced_gain,
        pooled,
        point_second,
        pooled_slope,
        pooled_product,
        kept_direct,
    )
    whole_small = lax.all_gather(share_small, ("branch", "dp"), axis=0)

    gathered = exchange(outer_sums)
    d_low, total, packed = call(
        functools.partial(second_back, grid, small, 0, taps_each),
        (
            shape((grid.copies, grid.padded, SECOND), BF16),
            shape((2, OUTER), F32),
            shape((clips, tap_share + point_share, 128), BF16),
        ),
        second_back_scratch(grid, taps_each),
        scalars=2,
        cost=18,
        far=(2, 6, 9, 10),
        far_out=(0,),
    )(length, first_tap, h_outer, outer, gathered, outer_gain, slope, dx_small, point_packed, taps_mid, taps_few)
    product_rows = round_up(own_channels, 16 * clips)
    du_rest, rest_product = call(
        functools.partial(rest_back, grid, small, slots, 0),
        (
            shape((grid.rows, DIRECT + POOLED), BF16),
            shape((clips, 6, product_rows // clips, 128), F32),
        ),
        [
            pltpu.VMEM((grid.rows, DIRECT + POOLED), BF16),
            pltpu.VMEM((grid.rows, DIRECT + POOLED), BF16),
            pltpu.VMEM(turned.shape, BF16),
            pltpu.VMEM((grid.rows, REDUCED), BF16),
            pltpu.VMEM((grid.rows, DIRECT + POOLED), BF16),
            *Spread.scratch(grid),
            pltpu.VMEM((product_rows, 768), F32),
            Lines.semaphores(grid, 4),
            pltpu.SemaphoreType.DMA((2,)),
            pltpu.SemaphoreType.DMA((1,)),
        ],
        scalars=1,
        cost=8,
        far=(5, 6, 7, 8, 9),
        far_out=(0,),
    )(length, outer, after(total, packed), outer_gain, dx_small, h_outer, slope, kept_direct, turned, h_reduced)
    share = add_up(exchange(packed))
    rest_pieces = exchange(rest_product)
    d_low, share = lax.optimization_barrier((after(d_low, rest_product), share))
    r_low, sums_low, products = call(
        functools.partial(conv_back, grid, slots, 0),
        (
            shape((grid.rows, REDUCED), BF16),
            shape((clips, 2, REDUCED), F32),
            shape((clips, 2, product_rows // clips, 128), F32),
        ),
        [
            *conv_back_scratch(grid),
            pltpu.VMEM(turned.shape, BF16),
            pltpu.VMEM((product_rows, REDUCED), F32),
            pltpu.SemaphoreType.DMA((1,)),
        ],
        scalars=1,
        cost=22,
        far=(5, 6, 7, 8),
    )(
        length,
        d_low,
        h_reduced,
        reduced_gain,
        reduced_shift,
        *kernels[0][:2],
        kernels[0][3],
        turned,
    )
    whole = lax.all_gather(share, ("branch", "dp"), axis=0)
    sums_low, rest_pieces = lax.optimization_barrier((sums_low, rest_pieces))
    gathered = exchange(sums_low)
    pieces = exchange(products)
    dx, reduced_total = call(
        functools.partial(mid_back, grid, 0),
        (shape((grid.rows, own_channels), BF16), shape((2, REDUCED), F32)),
        [
            pltpu.VMEM((grid.rows, DIRECT + POOLED), BF16),
            pltpu.VMEM((grid.rows, REDUCED), BF16),
            pltpu.VMEM((grid.rows, REDUCED), BF16),
            pltpu.VMEM((FIRST, own_channels), BF16),
            pltpu.VMEM((grid.rows, own_channels), BF16),
            Lines.semaphores(grid, 3),
            pltpu.SemaphoreType.DMA((1,)),
            pltpu.SemaphoreType.DMA((1,)),
        ],
        scalars=2,
        cost=8,
        far=(5, 6, 7, 8),
        far_out=(0,),
    )(length, place_one, moment, gathered, reduced_gain, du_rest, h_reduced, r_low, point_first)
    pieces, dx = lax.optimization_barrier((pieces, dx))
    point_sum = call(
        functools.partial(combine, 0),
        shape((5 * product_rows // clips, 128), BF16),
        cost=1,
        vmem=VMEM_BYTES // 3,
    )(rest_pieces, pieces, moment, gathered, reduced_gain)
    received = spread_over(point_sum, "branch", parts)

    outs = (
        shape((2, TAPS, MID_IN, MID_OUT), F32),
        shape((2, TAPS, SMALL_IN, SMALL_OUT), F32),
        shape((2, SQUEEZED, CHANNELS), F32),
    )
    tap_scratch = [
        pltpu.VMEM((TAPS, MID_IN, MID_OUT), F32),
        pltpu.VMEM((TAPS, SMALL_IN, SMALL_OUT), F32),
    ]
    point_scratch = [pltpu.VMEM((SQUEEZED, CHANNELS), F32), pltpu.VMEM((CHANNELS, 128), F32)]
    mid_grad, small_grad = call(
        functools.partial(unpack_second, clips, taps_each),
        outs[:2],
        [*tap_scratch, pltpu.SemaphoreType.DMA((2,))],
        far_out=(0, 1),
        cost=5,
    )(whole_small)
    received, mid_grad, small_grad = lax.optimization_barrier((received, mid_grad, small_grad))
    norms = shape((2, 1024), F32)
    mid_grad, small_grad, point_grad, gain_grad, shift_grad = call(
        functools.partial(unpack_first, parts, clips, taps_each, tap_share),
        (*outs, norms, norms),
        [*tap_scratch, *point_scratch, pltpu.SemaphoreType.DMA((3,))],
        far_out=(0, 1, 2),
        aliases={5: 0, 6: 1},
        cost=6,
    )(whole, total, reduced_total, total_small, reduced_total_small, mid_grad, small_grad)
    point_mine, point_other = gather_chips(
        jnp.concatenate(received, axis=0), clips, (mid_grad, small_grad)
    )
    clip_one = lax.axis_index("dp").astype(jnp.int32).reshape(1)
    point_grad = call(
        functools.partial(unpack_point, parts, clips, own_channels),
        outs[2],
        [
            pltpu.VMEM((parts, FIRST // 128, product_rows, 128), BF16),
            *point_scratch,
            pltpu.SemaphoreType.DMA((1,)),
        ],
        scalars=2,
        far_out=(0,),
        aliases={4: 0},
        cost=3,
        vmem=VMEM_BYTES // 2,
    )(place_one, clip_one, point_mine, point_other, point_grad)
    act = act.reshape(small.side, small.side, cotangent.shape[1], CHANNELS).transpose(2, 0, 1, 3)
    input_grad = dx.reshape(side, side, grid.unit, own_channels).transpose(2, 0, 1, 3)
    return (
        act[None],
        input_grad[None],
        point_grad.swapaxes(1, 2),
        mid_grad,
        small_grad,
        gain_grad,
        shift_grad,
    )


def solution(mesh):
    split = P("dp", None, None, None, "branch")
    whole = P("dp", None, None, None, None)
    return jax.shard_map(
        on_device,
        mesh=mesh,
        in_specs=(split, P("dp"), whole, P(), P(), P(), P(), P()),
        out_specs=(whole, split, P(), P(), P(), P(), P()),
        check_vma=False,
    )
```

```python
import functools

import jax
import jax.numpy as jnp
from jax import lax
from jax.experimental import pallas as pl
from jax.experimental.pallas import tpu as pltpu
from jax.sharding import PartitionSpec as P

DIRECT = 256
MID_IN = 160
MID_OUT = 320
SMALL_IN = 32
SMALL_OUT = 128
TAPS = 27
CHANNELS = 832
SQUEEZED = 576
TILE = 16
REDUCED = 256
POOLED = 128
FIRST = 640
SECOND = 512
OUTER = 896
TAP_ROWS = 432
EPSILON = 1e-05
F32 = jnp.float32
BF16 = jnp.bfloat16
VMEM_BYTES = 58 * 2**20
LARGE = 2200 * 2**10


def call(body, out_shape, scratch=(), scalars=0, cost=5, vmem=VMEM_BYTES, aliases=None, far=(), far_out=()):
    aliases = aliases or {}

    def large(values):
        size = values.dtype.itemsize
        for extent in values.shape:
            size = size * extent
        return size > LARGE

    def placed(out):
        return pltpu.HBM(out.shape, out.dtype) if large(out) else out

    def run(*operands):
        specs = [
            pl.BlockSpec(
                memory_space=pl.ANY
                if number in aliases or number in far
                else pltpu.SMEM
                if number < scalars
                else pltpu.VMEM
            )
            for number in range(len(operands))
        ]
        operands = [
            pltpu.with_memory_space_constraint(operand, pltpu.HBM) if large(operand) else operand
            for operand in operands
        ]
        if isinstance(out_shape, tuple):
            out_specs = tuple(
                pl.BlockSpec(memory_space=pl.ANY if number in far_out else pltpu.VMEM)
                for number in range(len(out_shape))
            )
        else:
            out_specs = pl.BlockSpec(memory_space=pl.ANY if 0 in far_out else pltpu.VMEM)
        return pl.pallas_call(
            body,
            out_shape=jax.tree.map(placed, out_shape),
            in_specs=specs,
            out_specs=out_specs,
            input_output_aliases=aliases,
            scratch_shapes=list(scratch),
            compiler_params=pltpu.CompilerParams(vmem_limit_bytes=vmem),
            cost_estimate=pl.CostEstimate(
                flops=0, bytes_accessed=int(cost * 3 * 10**6), transcendentals=0
            ),
        )(*operands)

    return run


def shape(dims, dtype):
    return jax.ShapeDtypeStruct(tuple(dims), dtype)


def rows_at(start, size):
    return pl.ds(pl.multiple_of(start, 16), size)


def frames_of(values_or_rows, unit):
    dims = values_or_rows if isinstance(values_or_rows, tuple) else (values_or_rows, 128)
    return lax.broadcasted_iota(jnp.int32, dims, 0) & (unit - 1)


def keep_frames(values, unit, lo, hi):
    rows, width = values.shape
    frame = lax.broadcasted_iota(jnp.int32, (1, unit, width), 1)
    kept = jnp.where((frame >= lo) & (frame < hi), 1.0, 0.0)
    return (values.reshape(rows // unit, unit, width) * kept).reshape(rows, width)


def earlier(values, unit):
    return keep_frames(pltpu.roll(values, 1, 0), unit, 1, unit)


def later(values, unit):
    return keep_frames(pltpu.roll(values, values.shape[0] - 1, 0), unit, 0, unit - 1)


def plane_box(values, unit):
    across = values + earlier(values, unit) + later(values, unit)
    edge = jnp.zeros((unit, values.shape[1]), values.dtype)
    return (
        across
        + jnp.concatenate([across[unit:], edge], axis=0)
        + jnp.concatenate([edge, across[:-unit]], axis=0)
    )


def box_window(grid, length):
    frame, place = (frames_of(grid.line_rows, grid.unit), grid.places_of(grid.line_rows))

    def one(condition):
        return jnp.where(condition, 1.0, 0.0)

    count = one(frame < length) + one(frame + 1 < length) + one((frame > 0) & (frame - 1 < length))
    return count * (3.0 - one(place == 0) - one(place == grid.side - 1))


def box_scale(line, side, window):
    lines = 3.0 - jnp.where(line == 0, 1.0, 0.0) - jnp.where(line == side - 1, 1.0, 0.0)
    return 1.0 / jnp.maximum(window * lines, 1.0)


def sigmoid(value):
    return 0.5 * jnp.tanh(0.5 * value) + 0.5


def silu(value):
    return value * sigmoid(value)


def silu_slope(value):
    gate = sigmoid(value)
    return gate * (1.0 + value * (1.0 - gate))


def partial_sum(values):
    rows, width = values.shape
    return jnp.sum(values.reshape(rows // 8, 8, width), axis=0)


def moments(total, square, count):
    center = total / count
    return (center, lax.rsqrt(square / count - center * center + EPSILON))


def total_of(gathered):
    count = len(gathered) if isinstance(gathered, (list, tuple)) else gathered.shape[0]
    total = gathered[0][...]
    for number in range(1, count):
        total = total + gathered[number][...]
    return total


def pool_matrix(grid, small, transposed):
    line = grid.line_rows
    few, many = (small.line_rows, 2 * line)
    dims = (many, few) if transposed else (few, many)
    coarse = lax.broadcasted_iota(jnp.int32, dims, 1 if transposed else 0)
    fine = lax.broadcasted_iota(jnp.int32, dims, 0 if transposed else 1)
    fine = jnp.where(fine >= line, fine - line, fine)
    same = (fine >> (grid.bits + 1) == coarse >> small.bits) & (
        (fine & (grid.unit - 1)) >> 1 == coarse & (small.unit - 1)
    )
    return jnp.where(same, 0.125, 0.0).astype(BF16)


class Grid:
    def __init__(self, side, unit):
        self.side, self.unit = (side, unit)
        self.bits = unit.bit_length() - 1
        self.copies = TILE // unit
        self.line_rows = side * unit if self.copies == 1 else (side + 1) * unit
        self.rows = side * self.line_rows
        self.pitch = (side + 1) * unit
        margin = 1 if self.copies == 1 else 2
        self.lead = margin * self.pitch + TILE
        self.padded = (side + 2 * margin) * self.pitch + 2 * TILE
        self.group = 2 if side % 2 == 0 else side

    def places_of(self, rows):
        place = lax.broadcasted_iota(jnp.int32, (rows, 128), 0) >> self.bits
        return place if self.copies == 1 else place & self.side

    def mask(self, rows, length, width=128):
        valid = frames_of(rows, self.unit) < length
        if self.copies > 1:
            valid = valid & (self.places_of(rows) < self.side)
        mask = jnp.where(valid, 1.0, 0.0)
        return jnp.concatenate([mask] * (width // 128), axis=1) if width > 128 else mask

    def near(self, ref, base, lines, places, size, lanes=slice(None)):
        start = base + lines * self.pitch
        if self.copies == 1:
            return ref[0, rows_at(start + places * TILE, size), lanes]
        copy = 0 if places == 0 else 1
        return ref[copy, rows_at(start - (TILE if places < 0 else 0), size), lanes]


class Slots:
    def __init__(self, grid, parts):
        self.pairs = grid.side // 2
        self.parts = parts
        self.each = -(-self.pairs // parts)
        self.empty = parts * self.each - self.pairs
        self.gap = parts * self.each // 2 - 1
        self.pair_rows = 2 * grid.line_rows
        self.grid = grid
        self.rows = self.each * self.pair_rows

    def slot_of(self, pair):
        return pair + jnp.where(pair >= self.gap, self.empty, 0)

    def pair_of(self, slot):
        return slot - jnp.where(slot >= self.gap, self.empty, 0)

    def used(self, slot):
        return (slot < self.gap) | (slot >= self.gap + self.empty)

    def held(self, place):
        count = jnp.zeros((), jnp.int32)
        for number in range(self.each):
            count = count + jnp.where(self.used(place * self.each + number), 1, 0)
        return count


def clear_empty(grid, ref):
    width = ref.shape[2]
    if grid.copies > 1:
        ref[...] = jnp.zeros_like(ref)
        return
    ref[0, 0 : grid.lead, :] = jnp.zeros((grid.lead, width), ref.dtype)
    end = grid.lead + grid.side * grid.pitch
    ref[0, end:, :] = jnp.zeros((ref.shape[1] - end, width), ref.dtype)

    @pl.loop(0, grid.side)
    def _(line):
        at = rows_at(grid.lead + line * grid.pitch + grid.line_rows, TILE)
        ref[0, at, :] = jnp.zeros((TILE, width), ref.dtype)


def store_taps(unit, mid_ref, small_ref, copy, at, act):
    before, after_ = (earlier(act, unit), later(act, unit))
    mid_ref[copy, at, 0:128] = before[:, :128].astype(BF16)
    mid_ref[copy, at, 128:256] = act[:, :128].astype(BF16)
    mid_ref[copy, at, 256:384] = after_[:, :128].astype(BF16)
    before, act, after_ = (before[:, 128:], act[:, 128:], after_[:, 128:])
    lane = lax.broadcasted_iota(jnp.int32, act.shape, 1)
    mid_ref[copy, at, 384:512] = jnp.where(
        lane < 32, before, jnp.where(lane < 64, pltpu.roll(act, 32, 1), pltpu.roll(after_, 64, 1))
    ).astype(BF16)
    small_ref[copy, at, :] = jnp.where(
        lane < 32, pltpu.roll(before, 96, 1), jnp.where(lane < 64, act, pltpu.roll(after_, 32, 1))
    ).astype(BF16)


def near_tap(grid, ref, base, tap, sign, size, lanes=slice(None)):
    return grid.near(ref, base, sign * (tap // 3 - 1), sign * (tap % 3 - 1), size, lanes)


def convolve(grid, taps, kernels, rest_ref, acc_ref, stage_ref, e_ref, stage_sem, sums_ref, length):
    mid_ref, small_ref = taps
    main_ref, last_ref, small_kernel_ref = kernels
    group_rows = grid.group * grid.pitch
    stage_rows = grid.group * grid.line_rows
    groups = grid.side // grid.group
    sums_ref[...] = jnp.zeros_like(sums_ref)
    mask = grid.mask(grid.line_rows, length, SECOND)
    edge = jnp.zeros((grid.pitch, 256), F32)
    rest_ref[grid.lead - grid.pitch : grid.lead, :] = edge
    end = grid.lead + grid.side * grid.pitch
    rest_ref[end : end + grid.pitch, :] = edge

    @pl.loop(0, groups)
    def _(group):
        base = grid.lead + group * group_rows
        total = None
        for place in range(3):
            part = jnp.dot(
                grid.near(mid_ref, base, 0, place - 1, group_rows),
                last_ref[place],
                preferred_element_type=F32,
            )
            total = part if total is None else total + part
        rest_ref[rows_at(base, group_rows), :] = total

    lane = lax.broadcasted_iota(jnp.int32, (grid.line_rows, 128), 1)

    def staged(group, slot):
        return pltpu.make_async_copy(
            stage_ref.at[slot],
            e_ref.at[rows_at(group * stage_rows, stage_rows), :],
            stage_sem.at[slot],
        )

    @pl.loop(0, groups)
    def _(group):
        base = grid.lead + group * group_rows
        slot = lax.rem(group, 2)
        for tap in range(9):
            part = jnp.dot(
                near_tap(grid, mid_ref, base, tap, 1, group_rows),
                main_ref[tap],
                preferred_element_type=F32,
            )
            acc_ref[:, 0:256] = part if tap == 0 else acc_ref[:, 0:256] + part
        near = [near_tap(grid, small_ref, base, tap, 1, group_rows) for tap in range(9)]
        acc_ref[:, 256:384] = jnp.dot(
            jnp.concatenate(near, axis=1), small_kernel_ref[...], preferred_element_type=F32
        )

        @pl.when(group >= 2)
        def _():
            staged(group - 2, slot).wait()

        for number in range(grid.group):
            rows = grid.line_rows
            start = base + number * grid.pitch
            last = (
                rest_ref[rows_at(start - grid.pitch, rows), 0:128]
                + pltpu.roll(rest_ref[rows_at(start, rows), 0:128], 64, 1)
                + rest_ref[rows_at(start + grid.pitch, rows), 128:256]
            )
            lines = slice(number * grid.pitch, number * grid.pitch + rows)
            values = jnp.concatenate(
                [acc_ref[lines, 0:256], jnp.where(lane < 64, last, 0.0), acc_ref[lines, 256:384]],
                axis=1,
            )
            stage_ref[slot, number * rows : (number + 1) * rows, :] = values
            masked = values * mask
            sums_ref[0:8] += partial_sum(masked)
            sums_ref[8:16] += partial_sum(masked * values)
        staged(group, slot).start()

    for group in range(max(groups - 2, 0), groups):
        staged(group, group % 2).wait()


def conv_scratch(grid):
    group_rows = grid.group * grid.pitch
    return [
        pltpu.VMEM((9, 512, 256), BF16),
        pltpu.VMEM((3, 512, 256), BF16),
        pltpu.VMEM((1152, 128), BF16),
        pltpu.VMEM((grid.copies, grid.padded, 512), BF16),
        pltpu.VMEM((grid.copies, grid.padded, 128), BF16),
        pltpu.VMEM((grid.rows, REDUCED), BF16),
        pltpu.VMEM((grid.padded, 256), F32),
        pltpu.VMEM((group_rows, 384), F32),
        pltpu.VMEM((2, grid.group * grid.line_rows, SECOND), F32),
        pltpu.VMEM((16, SECOND), F32),
        pltpu.SemaphoreType.DMA((3,)),
        pltpu.SemaphoreType.DMA((3,)),
        pltpu.SemaphoreType.DMA((2,)),
    ]


def conv_outputs(grid, *clips):
    return (
        shape((grid.rows, REDUCED), BF16),
        shape((grid.copies, grid.padded, 512), BF16),
        shape((grid.copies, grid.padded, 128), BF16),
        shape((grid.rows, SECOND), F32),
        shape((*clips, 2, SECOND), F32),
    )


def copies(sources, targets, sem_ref):
    return [
        pltpu.make_async_copy(source, target, sem_ref.at[number])
        for number, (source, target) in enumerate(zip(sources, targets))
    ]


def run_convolution(grid, length, far_kernels, outputs, scratch, fill):
    h_out, mid_out, small_out, e_out, sums_out = outputs
    kernels, (mid_ref, small_ref, h_ref), rest = (scratch[:3], scratch[3:6], scratch[6:])
    rest_ref, acc_ref, stage_ref, sums_ref, in_sem, out_sem, stage_sem = rest
    arriving = copies(far_kernels, kernels, in_sem)
    for copy in arriving:
        copy.start()
    clear_empty(grid, mid_ref)
    clear_empty(grid, small_ref)
    fill(h_ref, mid_ref, small_ref)
    leaving = copies((mid_ref, small_ref, h_ref), (mid_out, small_out, h_out), out_sem)
    for copy in leaving:
        copy.start()
    for copy in arriving:
        copy.wait()
    convolve(
        grid, (mid_ref, small_ref), kernels, rest_ref, acc_ref, stage_ref, e_out, stage_sem, sums_ref, length
    )
    write_sums(sums_out, sums_ref, 0, SECOND)
    for copy in leaving:
        copy.wait()


def write_row(out_ref, row, lo, hi, values):
    if len(out_ref.shape) == 2:
        out_ref[row : row + 1, lo:hi] = values
    else:
        for clip in range(out_ref.shape[0]):
            out_ref[clip, row : row + 1, lo:hi] = values


def write_sums(out_ref, sums_ref, lo, hi):
    for number in range(2):
        values = jnp.sum(sums_ref[8 * number : 8 * number + 8], axis=0, keepdims=True)
        write_row(out_ref, number, lo, hi, values)


def turn(slots, x_ref, out_ref):
    for slot in range(slots.parts * slots.each):
        part, number = divmod(slot, slots.each)
        lanes = slice(number * slots.pair_rows, (number + 1) * slots.pair_rows)
        if slots.gap <= slot < slots.gap + slots.empty:
            out_ref[part, :, lanes] = jnp.zeros((out_ref.shape[1], slots.pair_rows), BF16)
            continue
        pair = slot - (slots.empty if slot >= slots.gap else 0)
        rows = slice(pair * slots.pair_rows, (pair + 1) * slots.pair_rows)
        out_ref[part, :, lanes] = x_ref[rows, :].T


def first_pointwise(slots, length_ref, count_ref, x_ref, p_ref, mid_ref, pool_ref, direct_ref, sums_ref, u_ref):
    rows, step = (slots.rows, 112)
    length, count = (length_ref[0], count_ref[0])
    for part in range(slots.parts):
        product = lax.dot_general(
            x_ref[part], p_ref[part], (((0,), (1,)), ((), ())), preferred_element_type=F32
        )
        u_ref[...] = product if part == 0 else u_ref[...] + product
    mask = slots.grid.mask(step, length, FIRST)

    def summed(number, carry):
        values = u_ref[rows_at(number * step, step), :] * mask
        u_ref[rows_at(number * step, step), :] = values
        few = values[:, :SECOND]
        return (carry[0] + partial_sum(values), carry[1] + partial_sum(few * few))

    zero = (jnp.zeros((8, FIRST), F32), jnp.zeros((8, SECOND), F32))
    total, square = lax.fori_loop(0, rows // step, summed, zero)
    total = jnp.sum(total, axis=0, keepdims=True)
    write_row(sums_ref, 0, 0, SECOND, total[:, :SECOND])
    write_row(sums_ref, 1, 0, SECOND, jnp.sum(square, axis=0, keepdims=True))
    write_row(sums_ref, 2, 0, SECOND, jnp.full((1, SECOND), count, F32))
    offset = (total / jnp.full((1, FIRST), jnp.maximum(count, 1.0), F32)).astype(BF16)
    wide_offset = offset.astype(F32)
    tail = jnp.broadcast_to(wide_offset, (TILE, FIRST)).astype(BF16)
    pool_ref[rows : rows + TILE, :] = tail[:, SECOND:]
    shared = mid_ref.shape[0] - 2 * TILE
    mid_ref[shared : shared + TILE, :] = tail[:, 256:384]
    mid_ref[shared + TILE :, :] = tail[:, 384:512]

    @pl.loop(0, rows // step)
    def _(number):
        at = rows_at(number * step, step)
        values = u_ref[at, :]
        direct_ref[at, :] = values[:, :DIRECT]
        values = values[:, DIRECT:] - wide_offset[:, DIRECT:]
        mid_ref[at, :] = values[:, :128].astype(BF16)
        pool_ref[at, :] = values[:, 256:].astype(BF16)

    lane = lax.broadcasted_iota(jnp.int32, (step, 128), 1)
    for couple in range(0, slots.each, 2):

        @pl.loop(0, slots.pair_rows // step)
        def _(number):
            start = couple * slots.pair_rows + number * step
            values = u_ref[rows_at(start, step), 384:512] - wide_offset[:, 384:512]
            if couple + 1 < slots.each:
                other = u_ref[rows_at(start + slots.pair_rows, step), 384:512]
                other = pltpu.roll(other - wide_offset[:, 384:512], 64, 1)
                values = jnp.where(lane < 64, values, other)
            place = rows + couple // 2 * slots.pair_rows + number * step
            mid_ref[rows_at(place, step), :] = values.astype(BF16)


def mid_rows(slots):
    return slots.rows + -(-slots.each // 2) * slots.pair_rows + 2 * TILE


def each_pair(slots, place, refs, visit):
    for step, ref in enumerate(refs):
        source = lax.rem(place - step + slots.parts, slots.parts)
        for number in range(slots.each):
            slot = source * slots.each + number

            @pl.when(slots.used(slot))
            def _():
                visit(slots.pair_of(slot), ref, number)


def set_moments(total, moment_ref):
    count = total[2:3]
    center, inverse = moments(total[0:1], total[1:2], count)
    moment_ref[0:1, :] = center
    moment_ref[1:2, :] = inverse
    moment_ref[2:3, :] = count
    return (center, inverse)


def first_convolve(grid, slots, block, length_ref, place_ref, *refs):
    parts = slots.parts
    mids, sums, refs = (refs[:parts], refs[parts : 2 * parts], refs[2 * parts :])
    gain_ref, shift_ref, *refs = refs
    far_kernels, outputs, scratch = (refs[:3], refs[3:8], refs[8:])
    length = length_ref[0]
    total = total_of(sums)[:, DIRECT:]
    center, inverse = moments(total[0:1], total[1:2], total[2:3])
    gain, shift = (gain_ref[block : block + 1], shift_ref[block : block + 1])
    step = 112
    mask = grid.mask(step, length, REDUCED)
    lane = lax.broadcasted_iota(jnp.int32, (step, 128), 1)

    def fill(h_ref, mid_ref, small_ref):
        def visit(pair, ref, number):
            shared = ref.shape[0] - 2 * TILE
            offset = jnp.concatenate(
                [
                    ref[at : at + TILE, :].astype(F32)[0:1]
                    for at in (shared, shared + TILE)
                ],
                axis=1,
            )
            other = slots.rows + number // 2 * slots.pair_rows

            @pl.loop(0, slots.pair_rows // step)
            def _(chunk):
                values = ref[rows_at(number * slots.pair_rows + chunk * step, step), :].astype(F32)
                few = ref[rows_at(other + chunk * step, step), :].astype(F32)
                if number % 2 == 1:
                    few = pltpu.roll(few, 64, 1)
                few = jnp.where(lane < 64, few, 0.0)
                values = jnp.concatenate([values, few], axis=1) + offset
                scaled = (values - center) * inverse
                row = pair * slots.pair_rows + chunk * step
                h_ref[rows_at(row, step), :] = scaled.astype(BF16)
                act = silu(gain * scaled + shift) * mask
                line = row // grid.line_rows
                at = grid.lead + line * grid.pitch + row - line * grid.line_rows
                store_taps(grid.unit, mid_ref, small_ref, 0, rows_at(at, step), act)

        each_pair(slots, place_ref[0], mids, visit)

    run_convolution(grid, length, far_kernels, outputs, scratch, fill)


def pool_planes(grid, plane_ref, q_ref, lo, sums_ref, length, window):
    rows = grid.line_rows
    mask = grid.mask(rows, length)
    sums_ref[...] = jnp.zeros_like(sums_ref)

    @pl.loop(0, grid.side)
    def _(line):
        start = line * rows
        values = (
            plane_ref[rows_at(start, rows), :]
            + plane_ref[rows_at(start + rows, rows), :]
            + plane_ref[rows_at(start + 2 * rows, rows), :]
        ) * box_scale(line, grid.side, window)
        q_ref[rows_at(start, rows), lo : lo + POOLED] = values
        masked = values * mask
        sums_ref[0:8] += partial_sum(masked)
        sums_ref[8:16] += partial_sum(masked * values)


def clear_edges(grid, plane_ref):
    rows = grid.line_rows
    plane_ref[0:rows] = jnp.zeros((rows, POOLED), F32)
    plane_ref[grid.rows + rows : grid.rows + 2 * rows] = jnp.zeros((rows, POOLED), F32)


def first_pool(grid, slots, length_ref, place_ref, *refs):
    pools, refs = (refs[: slots.parts], refs[slots.parts :])
    e_sums_ref, q_ref, out_sums_ref, plane_ref, sums_ref = refs
    length = length_ref[0]
    rows = grid.line_rows
    for row in range(2):
        write_row(out_sums_ref, row, 0, SECOND, e_sums_ref[row : row + 1, :])
    clear_edges(grid, plane_ref)

    def visit(pair, ref, number):
        offset = ref[slots.rows : slots.rows + TILE, :].astype(F32)[0:1]
        for line in range(2):
            at = rows_at(number * slots.pair_rows + line * rows, rows)
            plane_ref[rows_at((2 * pair + line + 1) * rows, rows), :] = plane_box(
                ref[at, :].astype(F32) + offset, grid.unit
            )

    each_pair(slots, place_ref[0], pools, visit)
    pool_planes(grid, plane_ref, q_ref, 0, sums_ref, length, box_window(grid, length))
    write_sums(out_sums_ref, sums_ref, SECOND, FIRST)


def normalize(values, center, inverse, gain, shift, mask):
    scaled = (values - center) * inverse
    shifted = gain * scaled + shift
    gate = sigmoid(shifted)
    gate_mask = gate * mask
    act = shifted * gate_mask
    return (scaled, act, gate_mask + act * (1.0 - gate))


def pool_pieces(matrix, pieces):
    return jnp.dot(
        matrix, jnp.concatenate(pieces, axis=0), preferred_element_type=F32
    ).astype(BF16)


def first_direct(grid, small, slots, block, length_ref, u_ref, gain_ref, shift_ref, *refs):
    sums, (pooled_ref, kept_ref, moment_ref) = (refs[: slots.parts], refs[slots.parts :])
    rows = grid.line_rows
    mask = grid.mask(rows, length_ref[0], DIRECT)
    center, inverse = set_moments(total_of(sums), moment_ref)
    center, inverse = (center[:, :DIRECT], inverse[:, :DIRECT])
    gain, shift = (gain_ref[block : block + 1, :DIRECT], shift_ref[block : block + 1, :DIRECT])
    matrix = pool_matrix(grid, small, False)

    @pl.loop(0, slots.each)
    def _(number):
        acts, slopes, products = ([], [], [])
        for line in range(2):
            at = rows_at(number * slots.pair_rows + line * rows, rows)
            scaled, act, slope = normalize(u_ref[at, :], center, inverse, gain, shift, mask)
            kept_ref[at, 0:DIRECT] = scaled.astype(BF16)
            kept_ref[at, DIRECT : 2 * DIRECT] = slope.astype(BF16)
            acts.append(act.astype(BF16))
            slopes.append(slope.astype(BF16))
            products.append((slope * scaled).astype(BF16))
        size = small.line_rows
        pooled_ref[rows_at(number * size, size), :] = pool_pieces(matrix, acts)
        at = rows_at(slots.rows + number * size, size)
        kept_ref[at, 0:DIRECT] = pool_pieces(matrix, slopes)
        kept_ref[at, DIRECT : 2 * DIRECT] = pool_pieces(matrix, products)


def outer_moments(center, inverse, count, outer_ref):
    outer_ref[0:1, :] = center
    outer_ref[1:2, :] = inverse
    outer_ref[2:3, :] = jnp.concatenate([count[:, 0:128]] * (OUTER // 128), axis=1)


def first_output(grid, small, block, length_ref, q_far, e_far, moment_ref, sums_in_ref, gain_ref, shift_ref, *refs):
    pooled_ref, h_far, slope_far, outer_ref, pooled_slope_ref, pooled_product_ref, *refs = refs
    q_ref, e_ref, h_ref, slope_ref, q_sem, e_sem, h_sem, slope_sem = refs
    rows = grid.line_rows
    wide = 2 * rows
    pairs = grid.side // 2

    def arriving(pair, slot):
        at = rows_at(pair * wide, wide)
        return [
            pltpu.make_async_copy(q_far.at[at, :], q_ref.at[slot], q_sem.at[slot]),
            pltpu.make_async_copy(e_far.at[at, :], e_ref.at[slot], e_sem.at[slot]),
        ]

    def leaving(pair, slot):
        at = rows_at(pair * wide, wide)
        return [
            pltpu.make_async_copy(h_ref.at[slot], h_far.at[at, :], h_sem.at[slot]),
            pltpu.make_async_copy(slope_ref.at[slot], slope_far.at[at, :], slope_sem.at[slot]),
        ]

    for copy in arriving(0, 0):
        copy.start()
    mask = grid.mask(rows, length_ref[0], FIRST)
    total = total_of(sums_in_ref)
    count = jnp.concatenate([moment_ref[2:3, 0:128]] * (FIRST // 128), axis=1)
    center, inverse = moments(total[0:1], total[1:2], count)
    outer_moments(
        jnp.concatenate([moment_ref[0:1, :DIRECT], center], axis=1),
        jnp.concatenate([moment_ref[1:2, :DIRECT], inverse], axis=1),
        count,
        outer_ref,
    )
    matrix = pool_matrix(grid, small, False)
    gain, shift = (gain_ref[block : block + 1, DIRECT:], shift_ref[block : block + 1, DIRECT:])

    @pl.loop(0, pairs)
    def _(pair):
        slot = lax.rem(pair, 2)

        @pl.when(pair + 1 < pairs)
        def _():
            for copy in arriving(pair + 1, 1 - slot):
                copy.start()

        for copy in arriving(pair, slot):
            copy.wait()

        @pl.when(pair >= 2)
        def _():
            for copy in leaving(pair - 2, slot):
                copy.wait()

        acts, slopes, products = ([], [], [])
        for number in range(2):
            lines = slice(number * rows, (number + 1) * rows)
            values = jnp.concatenate([e_ref[slot, lines, :], q_ref[slot, lines, :]], axis=1)
            scaled, act, slope = normalize(values, center, inverse, gain, shift, mask)
            h_ref[slot, lines, :] = scaled.astype(BF16)
            low_slope = slope.astype(BF16)
            slope_ref[slot, lines, :] = low_slope
            acts.append(act.astype(BF16))
            slopes.append(low_slope)
            products.append((slope * scaled).astype(BF16))
        for copy in leaving(pair, slot):
            copy.start()
        at = rows_at(pair * small.line_rows, small.line_rows)
        pooled_ref[at, :] = pool_pieces(matrix, acts)
        pooled_slope_ref[at, :] = pool_pieces(matrix, slopes)
        pooled_product_ref[at, :] = pool_pieces(matrix, products)

    for pair in range(max(pairs - 2, 0), pairs):
        for copy in leaving(pair, pair % 2):
            copy.wait()


def second_pointwise(grid, slots, length_ref, place_ref, count_ref, *refs):
    directs, refs = (refs[: slots.parts], refs[slots.parts :])
    rest_ref, p_ref, q_ref, out_sums_ref, x_ref, plane_ref, sums_ref, pool_sums_ref = refs
    length = length_ref[0]
    rows = grid.line_rows
    sums_ref[...] = jnp.zeros_like(sums_ref)
    clear_edges(grid, plane_ref)
    x_ref[:, DIRECT:] = rest_ref[...]

    def visit(pair, ref, number):
        x_ref[rows_at(pair * rows, rows), 0:DIRECT] = ref[number * rows : (number + 1) * rows, :]

    each_pair(slots, place_ref[0], directs, visit)
    q_ref[...] = lax.dot_general(
        x_ref[...], p_ref[...], (((1,), (1,)), ((), ())), preferred_element_type=F32
    )

    @pl.loop(0, grid.side)
    def _(line):
        values = q_ref[rows_at(line * rows, rows), :]
        sums_ref[0:8] += partial_sum(values[:, :SECOND])
        sums_ref[8:16] += partial_sum(values[:, :SECOND] * values[:, :SECOND])
        plane_ref[rows_at((line + 1) * rows, rows), :] = plane_box(
            values[:, SECOND:], grid.unit
        )

    pool_planes(grid, plane_ref, q_ref, SECOND, pool_sums_ref, length, box_window(grid, length))
    write_sums(out_sums_ref, sums_ref, 0, SECOND)
    write_sums(out_sums_ref, pool_sums_ref, SECOND, FIRST)
    write_row(out_sums_ref, 2, 0, FIRST, jnp.full((1, FIRST), count_ref[0], F32))


def clear_ends(grid, ref):
    edge = jnp.zeros((grid.line_rows, ref.shape[1]), F32)
    ref[0 : grid.line_rows, :] = edge
    ref[grid.rows + grid.line_rows :, :] = edge


def store_copies(grid, ref, store):
    @pl.loop(0, grid.side + 1)
    def _(number):
        start = number * grid.line_rows
        at = rows_at(grid.lead + (number - 1) * grid.pitch, grid.line_rows)
        store(0, at, ref[rows_at(start, grid.line_rows), :])
        moved = pl.ds(pl.multiple_of(start + grid.unit, grid.unit), grid.line_rows)
        store(1, at, ref[moved, :])


def second_convolve(grid, block, length_ref, q_ref, sums_in_ref, gain_ref, shift_ref, *refs):
    far_kernels, outputs, moment_ref, scratch = (refs[:3], refs[3:8], refs[8], refs[9:])
    length = length_ref[0]
    center, inverse = set_moments(total_of(sums_in_ref), moment_ref)
    center, inverse = (center[:, DIRECT:SECOND], inverse[:, DIRECT:SECOND])
    gain, shift = (gain_ref[block : block + 1], shift_ref[block : block + 1])
    rows = grid.line_rows
    mask = grid.mask(rows, length, REDUCED)
    scratch, act_ref = (scratch[:-1], scratch[-1])

    def fill(h_ref, mid_ref, small_ref):
        clear_ends(grid, act_ref)

        @pl.loop(0, grid.side)
        def _(line):
            at = rows_at(line * rows, rows)
            scaled = (q_ref[at, DIRECT:SECOND] - center) * inverse
            h_ref[at, :] = scaled.astype(BF16)
            act_ref[rows_at((line + 1) * rows, rows), :] = silu(gain * scaled + shift) * mask

        def store(copy, at, values):
            store_taps(grid.unit, mid_ref, small_ref, copy, at, values)

        store_copies(grid, act_ref, store)

    run_convolution(grid, length, far_kernels, outputs, scratch, fill)


def second_output(grid, block, length_ref, q_ref, e_ref, moment_ref, sums_in_ref, gain_ref, shift_ref, cot_ref, act_ref, h_ref, error_ref, outer_ref, out_sums_ref, sums_ref):
    rows = grid.line_rows
    side, frames = (grid.side, cot_ref.shape[1])
    mask = grid.mask(rows, length_ref[0], OUTER)
    total = total_of(sums_in_ref)
    count = moment_ref[2:3, 0:SECOND]
    center, inverse = moments(total[0:1], total[1:2], count)
    center = jnp.concatenate([moment_ref[0:1, :DIRECT], center, moment_ref[0:1, SECOND:]], axis=1)
    inverse = jnp.concatenate([moment_ref[1:2, :DIRECT], inverse, moment_ref[1:2, SECOND:]], axis=1)
    outer_moments(center, inverse, count, outer_ref)
    sums_ref[...] = jnp.zeros_like(sums_ref)
    gain, shift = (gain_ref[block : block + 1], shift_ref[block : block + 1])
    gap = jnp.zeros((rows, 64), F32)
    unused = jnp.zeros((grid.unit, CHANNELS), F32)

    @pl.loop(0, side)
    def _(line):
        at = rows_at(line * rows, rows)
        places = pl.ds(line * side, side)
        values = jnp.concatenate([q_ref[at, :DIRECT], e_ref[at, :], q_ref[at, SECOND:]], axis=1)
        scaled = (values - center) * inverse
        h_ref[at, :] = scaled.astype(BF16)
        shifted = gain * scaled + shift
        gate = sigmoid(shifted)
        act = (shifted * gate * mask).reshape(side + 1, frames, OUTER)[:side].astype(BF16)
        act_ref[places, :, 0:576] = act[:, :, 0:576]
        act_ref[places, :, 576:CHANNELS] = act[:, :, 640:OUTER]
        slope = gate * (1.0 + shifted * (1.0 - gate))
        grad = cot_ref[places].astype(F32).reshape(side * frames, CHANNELS)
        grad = jnp.concatenate([grad, unused], axis=0)
        grad = jnp.concatenate([grad[:, :576], gap, grad[:, 576:]], axis=1)
        error = grad * slope * mask
        error_ref[at, :] = error.astype(BF16)
        sums_ref[0:8] += partial_sum(error)
        sums_ref[8:16] += partial_sum(error * scaled)

    write_sums(out_sums_ref, sums_ref, 0, OUTER)


def spread_matrix(grid, small):
    return None if small is None else pool_matrix(grid, small, True)[: grid.line_rows]


def outer_error(slopes, small, grad_ref, matrix, line, lo, hi):
    values = slopes.astype(F32)
    if small is None:
        return values
    coarse = grad_ref[rows_at((line // 2) * small.line_rows, small.line_rows), lo:hi]
    return values * jnp.dot(matrix, coarse, preferred_element_type=F32)


class Lines:
    def __init__(self, grid, sources, buffers, sem_ref):
        self.step = 2 if grid.side % 2 == 0 else 1
        self.size = self.step * grid.line_rows
        self.steps = grid.side // self.step
        self.sources, self.buffers, self.sem = (sources, buffers, sem_ref)

    def copies(self, step):
        at = rows_at(step * self.size, self.size)
        copies = []
        for number, ((ref, lo, hi), (buffer, place)) in enumerate(zip(self.sources, self.buffers)):
            source = ref(step, lo, hi) if callable(ref) else ref.at[at, pl.ds(lo, hi - lo)]
            target = buffer.at[at, pl.ds(place, hi - lo)]
            copies.append(pltpu.make_async_copy(source, target, self.sem.at[number, step]))
        return copies

    def first(self):
        @pl.loop(0, self.steps)
        def _(step):
            for copy in self.copies(step):
                copy.start()

    def run(self, visit):
        @pl.loop(0, self.steps)
        def _(step):
            for copy in self.copies(step):
                copy.wait()
            visit(step)

    @staticmethod
    def semaphores(grid, count):
        return pltpu.SemaphoreType.DMA((count, grid.side // 2 if grid.side % 2 == 0 else grid.side))


def second_back(grid, small, block, slots, length_ref, first_ref, h_far, outer_ref, sums_in_ref, gain_ref, slope_far, *refs):
    first = small is not None
    (grad_ref, carried_ref), refs = (refs[:2], refs[2:]) if first else ((None, None), refs)
    mid_far, few_far, d_far, total_ref, out_ref, *refs = refs
    d_ref, h_ref, slope_ref, mid_ref, few_ref, mid_acc_ref, small_acc_ref, turned_ref, sem_ref, in_sem, out_sem, *refs = refs
    lo, hi = (DIRECT, DIRECT + SECOND)
    at = 0 if first else DIRECT
    lines = Lines(
        grid,
        ((h_far, at, at + SECOND), (slope_far, at, at + SECOND)),
        ((h_ref, 0), (slope_ref, 0)),
        sem_ref,
    )
    lines.first()
    arriving = copies((mid_far, few_far), (mid_ref, few_ref), in_sem)
    for copy in arriving:
        copy.start()
    total = total_of(sums_in_ref)
    total_ref[...] = total
    a, b, c = before_norm(
        gain_ref[block : block + 1, lo:hi], outer_ref[1:2, lo:hi], total[:, lo:hi], outer_ref[2:3, lo:hi]
    )
    mask = grid.mask(grid.line_rows, length_ref[0], SECOND)
    matrix = spread_matrix(grid, small)
    clear_empty(grid, d_ref)
    rows = grid.line_rows
    if first:
        share = out_ref.shape[1] - carried_ref.shape[1]
        for clip in range(out_ref.shape[0]):
            out_ref[clip, share:, :] = carried_ref[clip]

    def visit(step):
        for number in range(lines.step):
            line = step * lines.step + number
            here = rows_at(line * rows, rows)
            scaled = h_ref[here, :].astype(F32)
            error = outer_error(slope_ref[here, :], small, grad_ref, matrix, line, lo, hi)
            back = (a * error - b - c * scaled) * mask
            if grid.copies == 1:
                d_ref[0, rows_at(grid.lead + line * grid.pitch, rows), :] = back.astype(BF16)
            else:
                refs[0][rows_at((line + 1) * rows, rows), :] = back

    lines.run(visit)
    if grid.copies > 1:
        clear_ends(grid, refs[0])

        def store(copy, at, values):
            d_ref[copy, at, :] = values.astype(BF16)

        store_copies(grid, refs[0], store)
    leaving = pltpu.make_async_copy(d_ref, d_far, out_sem.at[0])
    leaving.start()
    for copy in arriving:
        copy.wait()
    kernel_grads(grid, slots, first_ref, mid_ref, few_ref, d_ref, out_ref, mid_acc_ref, small_acc_ref, turned_ref)
    leaving.wait()


def before_norm(gain, inverse, sums, count):
    factor = gain * inverse
    return (factor, factor * sums[0:1] / count, factor * sums[1:2] / count)


def second_back_scratch(grid, slots):
    return [
        pltpu.VMEM((grid.copies, grid.padded, SECOND), BF16),
        pltpu.VMEM((grid.rows, SECOND), BF16),
        pltpu.VMEM((grid.rows, SECOND), BF16),
        pltpu.VMEM((grid.copies, grid.padded, 512), BF16),
        pltpu.VMEM((grid.copies, grid.padded, 128), BF16),
        pltpu.VMEM((slots, 384, 256), F32),
        pltpu.VMEM((slots, 128, 128), F32),
        pltpu.VMEM((MID_IN + 128, 128), F32),
        Lines.semaphores(grid, 2),
        pltpu.SemaphoreType.DMA((2,)),
        pltpu.SemaphoreType.DMA((1,)),
        *([pltpu.VMEM((grid.rows + 2 * grid.line_rows, SECOND), F32)] if grid.copies > 1 else []),
    ]


def conv_back(grid, slots, block, length_ref, d_ref, reduced_ref, reduced_gain_ref, reduced_shift_ref, *refs):
    far_kernels, refs = (refs[:3], refs[3:])
    first = len(refs) > 9
    x_far, refs = (refs[0], refs[1:]) if first else (None, refs)
    r_ref, out_sums_ref, *refs = refs
    product_out, refs = (refs[0], refs[1:]) if first else (None, refs)
    kernels, (last_ref, acc_ref, sums_ref, in_sem, *refs) = (refs[:3], refs[3:])
    if first:
        x_ref, product_ref, x_sem = refs
        x_copy = pltpu.make_async_copy(x_far, x_ref, x_sem.at[0])
        x_copy.start()
    main_ref, rest_ref, small_ref = kernels
    arriving = copies(far_kernels, kernels, in_sem)
    for copy in arriving:
        copy.start()
    rows = grid.line_rows
    group_rows = grid.group * grid.pitch
    sums_ref[...] = jnp.zeros_like(sums_ref)
    mask = grid.mask(rows, length_ref[0], REDUCED)
    gain, shift = (reduced_gain_ref[block : block + 1], reduced_shift_ref[block : block + 1])
    turned = (((1,), (1,)), ((), ()))
    lane = lax.broadcasted_iota(jnp.int32, (rows, 128), 1)
    wide_lane = lax.broadcasted_iota(jnp.int32, (grid.pitch, 128), 1)

    for copy in range(grid.copies):

        @pl.loop(1 - grid.copies, grid.side)
        def _(line):
            place = grid.lead + line * grid.pitch

            def lanes(start):
                return d_ref[copy, rows_at(start, grid.pitch), 256:384]

            further, here = (lanes(place + grid.pitch).astype(F32), lanes(place).astype(F32))
            at = rows_at(place, grid.pitch)
            last_ref[copy, at, 0:128] = jnp.where(
                wide_lane < 64, further, pltpu.roll(here, 64, 1)
            ).astype(BF16)
            last_ref[copy, at, 128:256] = lanes(place - grid.pitch)

        if grid.copies == 1:
            last_ref[copy, grid.lead - TILE : grid.lead, :] = jnp.zeros((TILE, 256), BF16)
        end = grid.lead + grid.side * grid.pitch
        last_ref[copy, end : end + TILE, :] = jnp.zeros((TILE, 256), BF16)
    for copy in arriving:
        copy.wait()

    @pl.loop(0, grid.side // grid.group)
    def _(group):
        base = grid.lead + group * group_rows
        for tap in range(9):
            part = lax.dot_general(
                near_tap(grid, d_ref, base, tap, -1, group_rows, slice(0, 256)),
                main_ref[tap],
                turned,
                preferred_element_type=F32,
            )
            acc_ref[:, 0:512] = part if tap == 0 else acc_ref[:, 0:512] + part
        for place in range(3):
            acc_ref[:, 0:512] += lax.dot_general(
                grid.near(last_ref, base, 0, 1 - place, group_rows),
                rest_ref[place],
                turned,
                preferred_element_type=F32,
            )
        near = [
            near_tap(grid, d_ref, base, tap, -1, group_rows, slice(384, 512)) for tap in range(9)
        ]
        acc_ref[:, 512:640] = jnp.dot(
            jnp.concatenate(near, axis=1), small_ref[...], preferred_element_type=F32
        )
        for number in range(grid.group):
            line = group * grid.group + number
            lines = slice(number * grid.pitch, number * grid.pitch + rows)
            rest, small = (acc_ref[lines, 384:512], acc_ref[lines, 512:640])
            one = jnp.where(lane < 32, rest, pltpu.roll(small, 32, 1))
            two = jnp.where(lane < 32, pltpu.roll(rest, 96, 1), small)
            three = jnp.where(lane < 32, pltpu.roll(rest, 64, 1), pltpu.roll(small, 96, 1))
            unit = grid.unit
            wide = later(acc_ref[lines, 0:128], unit) + acc_ref[lines, 128:256]
            wide = wide + earlier(acc_ref[lines, 256:384], unit)
            narrow = jnp.where(lane < 64, later(one, unit) + two + earlier(three, unit), 0.0)
            back = jnp.concatenate([wide, narrow], axis=1)
            at = rows_at(line * rows, rows)
            scaled = reduced_ref[at, :].astype(F32)
            error = back * silu_slope(gain * scaled + shift) * mask
            r_ref[at, :] = error.astype(BF16)
            sums_ref[0:8] += partial_sum(error)
            sums_ref[8:16] += partial_sum(error * scaled)

    write_sums(out_sums_ref, sums_ref, 0, REDUCED)
    if first:
        x_copy.wait()
        write_products(
            slots,
            x_ref,
            lambda start, size: r_ref[start : start + size, :],
            product_ref,
            product_out,
        )


def kernel_grads(grid, slots, first_ref, mid_ref, small_ref, d_ref, out_ref, mid_acc_ref, small_acc_ref, turned_ref):
    group_rows = grid.group * grid.pitch
    mid_acc_ref[...] = jnp.zeros_like(mid_acc_ref)
    small_acc_ref[...] = jnp.zeros_like(small_acc_ref)

    def neighbour(slot):
        return jnp.minimum(first_ref[0] + slot, TAPS - 1) // 9

    @pl.loop(0, grid.side // grid.group)
    def _(group):
        base = grid.lead + group * group_rows
        left = d_ref[0, rows_at(base, group_rows), :].T
        for slot in range(slots):
            tap = lax.rem(jnp.minimum(first_ref[0] + slot, TAPS - 1), 9)
            start = base + (tap // 3 - 1) * grid.pitch
            place = lax.rem(tap, 3) - 1
            copy = 0
            if grid.copies == 1:
                start = start + place * TILE
            else:
                copy = jnp.where(place == 0, 0, 1)
                start = start - jnp.where(place < 0, TILE, 0)
            at = rows_at(start, group_rows)
            lanes = pl.ds(pl.multiple_of(neighbour(slot) * 128, 128), 128)
            right = jnp.concatenate([mid_ref[copy, at, lanes], mid_ref[copy, at, 384:512]], axis=1)
            mid_acc_ref[slot] += jnp.dot(left[0:384], right, preferred_element_type=F32)
            small_acc_ref[slot] += jnp.dot(
                left[384:512], small_ref[copy, at, :], preferred_element_type=F32
            )

    share = round_up(slots * TAP_ROWS, 16 * out_ref.shape[0]) // out_ref.shape[0]

    def put(start, values):
        done = 0
        while done < values.shape[0]:
            clip, at = divmod(start + done, share)
            size = min(values.shape[0] - done, share - at)
            out_ref[clip, at : at + size, :] = values[done : done + size].astype(BF16)
            done = done + size

    half = MID_IN // 2
    for slot in range(slots):
        base = slot * TAP_ROWS
        rest = pl.ds(pl.multiple_of(neighbour(slot) * 32, 32), 32)
        for tile in range(3):
            lines = slice(128 * tile, 128 * (tile + 1))
            turned_ref[0:128, :] = mid_acc_ref[slot, lines, 0:128].T
            turned_ref[MID_IN : MID_IN + 128, :] = mid_acc_ref[slot, lines, 128:256].T
            turned_ref[128:MID_IN, :] = turned_ref[
                pl.ds(pl.multiple_of(MID_IN + neighbour(slot) * 32, 32), 32), :
            ]
            if tile < 2:
                put(base + MID_IN * tile, turned_ref[0:MID_IN, :])
            else:
                folded = turned_ref[0:half, :] + pltpu.roll(turned_ref[half:MID_IN, :], 64, 1)
                put(base + 2 * MID_IN, folded)
        turned_ref[0:128, :] = small_acc_ref[slot].T
        put(base + 2 * MID_IN + half, turned_ref[rest, :])
    used = slots * TAP_ROWS
    put(used, jnp.zeros((share * out_ref.shape[0] - used, 128), F32))


class Spread:
    def __init__(self, grid, plane_ref, across_ref, scale_ref, length):
        self.grid, self.plane, self.across, self.scale = (grid, plane_ref, across_ref, scale_ref)
        clear_edges(grid, plane_ref)
        window = box_window(grid, length)
        scale_ref[0] = box_scale(0, grid.side, window)
        scale_ref[1] = box_scale(1, grid.side, window)
        unit = grid.unit
        edge = jnp.zeros((unit, POOLED), F32)
        across_ref[0:unit, :] = edge
        across_ref[unit + grid.line_rows :, :] = edge

    def put(self, line, values):
        rows = self.grid.line_rows
        inner = jnp.where((line == 0) | (line == self.grid.side - 1), 0, 1)
        values = values * self.scale[inner]
        across, unit = (self.across, self.grid.unit)
        across[unit : unit + rows, :] = values + earlier(values, unit) + later(values, unit)
        self.plane[rows_at((line + 1) * rows, rows), :] = (
            across[0:rows, :] + across[unit : unit + rows, :] + across[2 * unit :, :]
        )

    def get(self, start, size):
        rows = self.grid.line_rows
        return (
            self.plane[rows_at(start, size), :]
            + self.plane[rows_at(start + rows, size), :]
            + self.plane[rows_at(start + 2 * rows, size), :]
        )

    @staticmethod
    def scratch(grid):
        return [
            pltpu.VMEM((grid.rows + 2 * grid.line_rows, POOLED), F32),
            pltpu.VMEM((grid.line_rows + 2 * grid.unit, POOLED), F32),
            pltpu.VMEM((2, grid.line_rows, POOLED), F32),
        ]


def channel_products(slots, x_ref, right_of):
    total = None
    for part in range(slots.parts):
        slot = part * slots.each
        pair = slot - (slots.empty if slot >= slots.gap + slots.empty else 0)
        pair = min(pair, slots.pairs - slots.each)
        product = jnp.dot(
            x_ref[part], right_of(pair * slots.pair_rows, slots.rows), preferred_element_type=F32
        )
        total = product if total is None else total + product
    return total


def write_products(slots, x_ref, right_of, product_ref, product_out):
    channels = x_ref.shape[1]
    product_ref[0:channels, :] = channel_products(slots, x_ref, right_of)
    product_ref[channels:, :] = jnp.zeros((product_ref.shape[0] - channels, product_ref.shape[1]), F32)
    clips, tiles, size, _ = product_out.shape
    for clip in range(clips):
        for tile in range(tiles):
            product_out[clip, tile] = product_ref[
                clip * size : (clip + 1) * size, 128 * tile : 128 * (tile + 1)
            ]


def rest_constants(outer_ref, total_ref, gain_ref, block):
    pool = OUTER - POOLED

    def pick(ref, lo, hi):
        return jnp.concatenate([ref[lo:hi, 0:DIRECT], ref[lo:hi, pool:]], axis=1)

    return before_norm(
        pick(gain_ref, block, block + 1), pick(outer_ref, 1, 2), pick(total_ref, 0, 2), pick(outer_ref, 2, 3)
    )


def point_back(grid, slots, block, kept, length_ref, place_ref, h_far, outer_ref, total_ref, gain_ref, error_far, reduced_far, r_far, moment_ref, sums_in_ref, reduced_gain_ref, x_far, p_far, *refs):
    pooled_slope_in, pooled_product_in, kept_far, *refs = refs
    dx_ref, dp_ref, reduced_total_ref, outer_sums_ref, *refs = refs
    h_ref, error_ref, reduced_ref, r_ref, x_ref, p_ref, du_ref, acc_ref, *refs = refs
    plane_ref, across_ref, scale_ref, sums_ref, pooled_slope_ref, pooled_product_ref, kept_ref, *refs = refs
    sem_ref, in_sem = refs
    rows = grid.line_rows
    pool = OUTER - POOLED
    lines = Lines(
        grid,
        (
            (h_far, 0, DIRECT),
            (h_far, pool, OUTER),
            (error_far, 0, DIRECT),
            (error_far, pool, OUTER),
            (reduced_far, 0, REDUCED),
            (r_far, 0, REDUCED),
        ),
        ((h_ref, 0), (h_ref, DIRECT), (error_ref, 0), (error_ref, DIRECT), (reduced_ref, 0), (r_ref, 0)),
        sem_ref,
    )
    lines.first()
    kept_rows = kept_ref.shape[1]
    arriving = copies(
        (x_far, p_far, kept_far.at[:, pl.ds(slots.rows, kept_rows), :]), (x_ref, p_ref, kept_ref), in_sem
    )
    for copy in arriving:
        copy.start()
    length = length_ref[0]
    total = total_of(sums_in_ref)
    reduced_total_ref[...] = total
    mid = before_norm(
        reduced_gain_ref[block : block + 1],
        moment_ref[1:2, DIRECT:SECOND],
        total,
        outer_ref[2:3, 0:REDUCED],
    )
    rest = rest_constants(outer_ref, total_ref, gain_ref, block)
    mask = grid.mask(rows, length, DIRECT + POOLED)
    spread = Spread(grid, plane_ref, across_ref, scale_ref, length)

    def visit(line):
        at = rows_at(line * rows, rows)
        back = rest[0] * error_ref[at, :].astype(F32) - rest[1] - rest[2] * h_ref[at, :].astype(F32)
        back = back * mask
        du_ref[at, 0:DIRECT] = back[:, :DIRECT].astype(BF16)
        spread.put(line, back[:, DIRECT:])
        back = mid[0] * r_ref[at, :].astype(F32) - mid[1] - mid[2] * reduced_ref[at, :].astype(F32)
        du_ref[at, DIRECT:SECOND] = (back * mask[:, :REDUCED]).astype(BF16)

    lines.run(visit)
    for copy in arriving:
        copy.wait()
    sums_ref[...] = jnp.zeros_like(sums_ref)
    pooled_slope_ref[:, DIRECT:] = pooled_slope_in[...]
    pooled_product_ref[:, DIRECT:] = pooled_product_in[...]
    for pair in range(slots.pairs):
        slot = pair + (slots.empty if pair >= slots.gap else 0)
        at = slice(pair * rows, (pair + 1) * rows)
        start = slot % slots.each * rows
        values = kept_ref[slot // slots.each, start : start + rows, :]
        pooled_slope_ref[at, 0:DIRECT] = values[:, :DIRECT]
        pooled_product_ref[at, 0:DIRECT] = values[:, DIRECT:]

    @pl.loop(0, grid.side)
    def _(line):
        at = rows_at(line * rows, rows)
        du_ref[at, SECOND:] = (spread.get(line * rows, rows) * mask[:, :POOLED]).astype(BF16)
        dx = jnp.dot(du_ref[at, :], p_ref[...], preferred_element_type=F32).astype(BF16)
        dx_ref[at, :] = dx
        for number, ref in enumerate((pooled_slope_ref, pooled_product_ref)):
            sums_ref[8 * number : 8 * number + 8] += partial_sum(
                dx.astype(F32) * ref[at, :].astype(F32)
            )

    write_sums(outer_sums_ref, sums_ref, 0, OUTER)
    acc_ref[...] = lax.dot_general(
        x_ref[...], du_ref[...], (((0,), (0,)), ((), ())), preferred_element_type=F32
    )
    start = pl.multiple_of(place_ref[0] * kept, 16) if kept < acc_ref.shape[0] else 0
    clips, size, _ = dp_ref.shape
    for tile in range(FIRST // 128):
        values = acc_ref[pl.ds(start, kept), 128 * tile : 128 * (tile + 1)].astype(BF16)
        done = 0
        while done < kept:
            clip, at = divmod(kept * tile + done, size)
            few = min(kept - done, size - at)
            dp_ref[clip, at : at + few, :] = values[done : done + few]
            done = done + few
    used = (FIRST // 128) * kept
    while used < clips * size:
        clip, at = divmod(used, size)
        dp_ref[clip, at:, :] = jnp.zeros((size - at, 128), BF16)
        used = used + size - at


def rest_back(grid, small, slots, block, length_ref, outer_ref, total_ref, gain_ref, grad_ref, h_far, slope_far, kept_far, x_far, reduced_far, du_far, product_out, *refs):
    h_ref, slope_ref, x_ref, reduced_ref, du_ref, plane_ref, across_ref, scale_ref, product_ref, sem_ref, in_sem, du_sem = refs
    rows = grid.line_rows
    pool = OUTER - POOLED

    def direct(step, lo, hi):
        slot = slots.slot_of(step)
        at = rows_at(lax.rem(slot, slots.each) * slots.pair_rows, slots.pair_rows)
        return kept_far.at[slot // slots.each, at, pl.ds(lo, hi - lo)]

    lines = Lines(
        grid,
        (
            (direct, 0, DIRECT),
            (h_far, SECOND, FIRST),
            (direct, DIRECT, 2 * DIRECT),
            (slope_far, SECOND, FIRST),
        ),
        ((h_ref, 0), (h_ref, DIRECT), (slope_ref, 0), (slope_ref, DIRECT)),
        sem_ref,
    )
    lines.first()
    arriving = copies((x_far, reduced_far), (x_ref, reduced_ref), in_sem)
    for copy in arriving:
        copy.start()
    length = length_ref[0]
    matrix = spread_matrix(grid, small)
    a, b, c = rest_constants(outer_ref, total_ref, gain_ref, block)
    mask = grid.mask(rows, length, DIRECT + POOLED)
    spread = Spread(grid, plane_ref, across_ref, scale_ref, length)

    def visit(step):
        for number in range(lines.step):
            line = step * lines.step + number
            at = rows_at(line * rows, rows)
            coarse = grad_ref[rows_at((line // 2) * small.line_rows, small.line_rows), :]
            grad = jnp.dot(
                matrix,
                jnp.concatenate([coarse[:, :DIRECT], coarse[:, pool:]], axis=1),
                preferred_element_type=F32,
            )
            back = a * (grad * slope_ref[at, :].astype(F32)) - b - c * h_ref[at, :].astype(F32)
            back = back * mask
            du_ref[at, 0:DIRECT] = back[:, :DIRECT].astype(BF16)
            spread.put(line, back[:, DIRECT:])

    lines.run(visit)
    for copy in arriving:
        copy.wait()
    wide = lines.size
    pool_mask = grid.mask(wide, length)

    def leaving(step):
        at = rows_at(step * wide, wide)
        return pltpu.make_async_copy(du_ref.at[at, :], du_far.at[at, :], du_sem.at[0])

    @pl.loop(0, lines.steps)
    def _(step):
        at = rows_at(step * wide, wide)
        du_ref[at, DIRECT:] = (spread.get(step * wide, wide) * pool_mask).astype(BF16)
        leaving(step).start()

    ones = grid.mask(slots.rows, length)
    two_ones = jnp.concatenate([ones, ones], axis=1)

    def right_of(start, size):
        at = slice(start, start + size)
        scaled = (reduced_ref[at, :].astype(F32) * two_ones).astype(BF16)
        return jnp.concatenate([du_ref[at, :], scaled, ones.astype(BF16)], axis=1)

    write_products(slots, x_ref, right_of, product_ref, product_out)
    pltpu.make_async_copy(du_ref, du_far, du_sem.at[0]).wait()


def mid_back(grid, block, length_ref, place_ref, moment_ref, sums_in_ref, gain_ref, du_far, h_far, r_far, p_far, dx_far, total_ref, *refs):
    du_ref, h_ref, r_ref, p_ref, dx_ref, sem_ref, p_sem, dx_sem = refs
    lines = Lines(
        grid,
        ((du_far, 0, DIRECT + POOLED), (h_far, 0, REDUCED), (r_far, 0, REDUCED)),
        ((du_ref, 0), (h_ref, 0), (r_ref, 0)),
        sem_ref,
    )
    lines.first()
    p_copy = pltpu.make_async_copy(p_far.at[place_ref[0]], p_ref, p_sem.at[0])
    p_copy.start()
    total = total_of(sums_in_ref)
    total_ref[...] = total
    a, b, c = before_norm(
        gain_ref[block : block + 1], moment_ref[1:2, DIRECT:], total, moment_ref[2:3, DIRECT:]
    )
    mask = grid.mask(lines.size, length_ref[0], REDUCED)
    p_copy.wait()

    def leaving(step):
        at = rows_at(step * lines.size, lines.size)
        return pltpu.make_async_copy(dx_ref.at[at, :], dx_far.at[at, :], dx_sem.at[0])

    def visit(step):
        at = rows_at(step * lines.size, lines.size)
        back = a * r_ref[at, :].astype(F32) - b - c * h_ref[at, :].astype(F32)
        du = jnp.concatenate(
            [du_ref[at, :DIRECT], (back * mask).astype(BF16), du_ref[at, DIRECT:]], axis=1
        )
        dx_ref[at, :] = jnp.dot(du, p_ref[...], preferred_element_type=F32).astype(BF16)
        leaving(step).start()

    lines.run(visit)
    pltpu.make_async_copy(dx_ref, dx_far, dx_sem.at[0]).wait()


def combine(block, rest_ref, pieces_ref, moment_ref, sums_in_ref, gain_ref, out_ref):
    total = total_of(sums_in_ref)
    a, b, c = before_norm(
        gain_ref[block : block + 1], moment_ref[1:2, DIRECT:], total, moment_ref[2:3, DIRECT:]
    )
    size = out_ref.shape[0] // 5
    rest, products = (total_of(rest_ref), total_of(pieces_ref))
    for tile in range(2):
        out_ref[size * tile : size * (tile + 1), :] = rest[tile].astype(BF16)
        lanes = slice(128 * tile, 128 * (tile + 1))
        mid = a[:, lanes] * products[tile] - b[:, lanes] * rest[5] - c[:, lanes] * rest[3 + tile]
        out_ref[size * (2 + tile) : size * (3 + tile), :] = mid.astype(BF16)
    out_ref[4 * size :, :] = rest[2].astype(BF16)


def write_taps(read, slots, arriving, mid_ref, small_ref, mid_out, small_out, sem_ref):
    half = MID_IN // 2

    def leaving(tap):
        return (
            pltpu.make_async_copy(mid_ref.at[tap], mid_out.at[tap], sem_ref.at[0]),
            pltpu.make_async_copy(small_ref.at[tap], small_out.at[tap], sem_ref.at[1]),
        )

    for tap in range(TAPS):
        part, slot = divmod(tap, slots)
        if slot == 0:
            arriving[part].wait()
        base = slot * TAP_ROWS
        folded = read(part, base + 2 * MID_IN, half)
        mid_ref[tap, :, 0:128] = read(part, base, MID_IN)
        mid_ref[tap, :, 128:256] = read(part, base + MID_IN, MID_IN)
        mid_ref[tap, 0:half, 256:320] = folded[:, 0:64]
        mid_ref[tap, half:MID_IN, 256:320] = pltpu.roll(folded, 64, 1)[:, 0:64]
        small_ref[tap] = read(part, base + 2 * MID_IN + half, SMALL_IN)
        for copy in leaving(tap):
            copy.start()
    for copy in arriving[-(-TAPS // slots) :]:
        copy.wait()
    return [
        pltpu.make_async_copy(mid_ref, mid_out, sem_ref.at[0]),
        pltpu.make_async_copy(small_ref, small_out, sem_ref.at[1]),
    ]


def parts_of(clips, far, ref, sem_ref):
    copies = []
    for part in range(far.shape[0] // clips):
        at = pl.ds(part * clips, clips)
        copies.append(pltpu.make_async_copy(far.at[at], ref.at[at], sem_ref.at[part]))
    for copy in copies:
        copy.start()
    return copies


def write_point(read, parts, kept, point_ref, wide_ref):
    for tile in range(FIRST // 128):
        for part in range(parts):
            start, stop = (kept * part, kept * (part + 1))
            values = read(part, kept * tile, kept)
            if kept * parts == CHANNELS:
                wide_ref[start:stop, :] = values
                continue
            for lo, hi, moved in ((0, 576, 0), (640, OUTER, 64)):
                lo, hi = (max(lo, start), min(hi, stop))
                if lo < hi:
                    wide_ref[lo - moved : hi - moved, :] = values[lo - start : hi - start]
        turned = wide_ref[...].T
        if tile < 3:
            point_ref[128 * tile : 128 * (tile + 1), :] = turned
        elif tile == 3:
            point_ref[384:448, :] = turned[0:64]
        else:
            point_ref[448:576, :] = turned


def copy_out(pairs, sem_ref):
    copies = [
        pltpu.make_async_copy(source, target, sem_ref.at[number])
        for number, (source, target) in enumerate(pairs)
    ]
    for copy in copies:
        copy.start()
    for copy in copies:
        copy.wait()


def share_reader(ref, clips, lo, share):
    def read(part, start, size):
        pieces, done = ([], 0)
        while done < size:
            clip, at = divmod(start + done, share)
            few = min(size - done, share - at)
            pieces.append(ref[part * clips + clip, lo + at : lo + at + few, :].astype(F32))
            done = done + few
        return pieces[0] if len(pieces) == 1 else jnp.concatenate(pieces, axis=0)

    return read


def unpack_second(clips, slots, far, mid_out, small_out, shares_ref, mid_ref, small_ref, sem_ref, in_sem):
    arriving = parts_of(clips, far, shares_ref, in_sem)
    read = share_reader(shares_ref, clips, 0, shares_ref.shape[1])
    leaving = write_taps(
        read, slots, arriving, mid_ref, small_ref, mid_out.at[1], small_out.at[1], sem_ref
    )
    for copy in leaving:
        copy.wait()


def unpack_first(parts, clips, slots, share, far, *refs):
    totals, refs = (refs[:4], refs[4:])
    mid_in, small_in, mid_out, small_out, point_out, gain_out, shift_out, *refs = refs
    shares_ref, mid_ref, small_ref, point_ref, wide_ref, sem_ref, in_sem = refs
    arriving = parts_of(clips, far, shares_ref, in_sem)
    for block in range(2):
        outer_ref, reduced_ref = totals[2 * block : 2 * block + 2]
        for row, out in enumerate((shift_out, gain_out)):
            at, line = (slice(block, block + 1), slice(row, row + 1))
            out[at, 0:256] = outer_ref[line, 0:256]
            out[at, 256:448] = reduced_ref[line, 0:192]
            out[at, 448:576] = outer_ref[line, 768:896]
            out[at, 576:896] = outer_ref[line, 256:576]
            out[at, 896:1024] = outer_ref[line, 640:768]
    read = share_reader(shares_ref, clips, 0, share)
    leaving = write_taps(
        read, slots, arriving, mid_ref, small_ref, mid_out.at[0], small_out.at[0], sem_ref
    )
    read = share_reader(shares_ref, clips, share, shares_ref.shape[1] - share)
    write_point(read, parts, OUTER // parts, point_ref, wide_ref)
    last = pltpu.make_async_copy(point_ref, point_out.at[1], sem_ref.at[2])
    last.start()
    for copy in (*leaving, last):
        copy.wait()


def unpack_point(parts, clips, kept, place_ref, clip_ref, mine_ref, other_ref, point_in, point_out, buffer_ref, point_ref, wide_ref, sem_ref):
    tiles = FIRST // 128
    size = buffer_ref.shape[2] // clips
    for chip in range(clips // 2):
        for step in range(parts):
            part = lax.rem(place_ref[0] - step + parts, parts)
            for swapped, ref in enumerate((mine_ref, other_ref)):
                owner = clip_ref[0] ^ (2 * chip) ^ swapped
                source = (chip * parts + step) * tiles * size
                for tile in range(tiles):
                    buffer_ref[part, tile, rows_at(owner * size, size), :] = ref[
                        source + tile * size : source + (tile + 1) * size, :
                    ]

    def read(part, start, size):
        tile, at = divmod(start, kept)
        return buffer_ref[part, tile, at : at + size, :].astype(F32)

    write_point(read, parts, kept, point_ref, wide_ref)
    last = pltpu.make_async_copy(point_ref, point_out.at[0], sem_ref.at[0])
    last.start()
    last.wait()


def prepare(parts, mid_in, small_in, point_in, gain_in, shift_in, *refs):
    kernels, (point_ref, second_ref, *vectors) = (refs[:8], refs[8:14])
    for block in range(2):
        main_ref, last_ref, few_ref, back_ref = kernels[4 * block : 4 * block + 4]

        @pl.loop(0, 9)
        def _(tap):
            for number in range(3):
                source = 9 * number + tap
                main_ref[tap, 128 * number : 128 * (number + 1), :] = mid_in[block, source, 0:128, 0:256]
                main_ref[tap, 384 + 32 * number : 416 + 32 * number, :] = mid_in[
                    block, source, 128:MID_IN, 0:256
                ]
            main_ref[tap, 480:512, :] = jnp.zeros((32, 256), BF16)
            small = jnp.concatenate(
                [small_in[block, 9 * number + tap] for number in range(3)]
                + [jnp.zeros((32, 128), BF16)],
                axis=0,
            )
            at = pl.ds(pl.multiple_of(tap * 128, 128), 128)
            few_ref[at, :] = small
            back_ref[at, :] = small.astype(F32).T.astype(BF16)

        @pl.loop(0, 3)
        def _(place):
            for number in range(3):
                for rows, start, size in (
                    (slice(0, 128), 128 * number, 128),
                    (slice(128, MID_IN), 384 + 32 * number, 32),
                ):
                    pieces = [
                        mid_in[block, 9 * number + 3 * line + place, rows, 256:MID_OUT].astype(F32)
                        for line in range(3)
                    ]
                    pieces.append(jnp.zeros((size, 64), F32))
                    last_ref[place, start : start + size, :] = jnp.concatenate(
                        pieces, axis=1
                    ).astype(BF16)
            last_ref[place, 480:512, :] = jnp.zeros((32, 256), BF16)

    own = point_ref.shape[2]
    for lo, hi, at in ((0, 448, 0), (448, SQUEEZED, SECOND)):
        values = point_in[0, lo:hi, :].astype(F32)
        for part in range(parts):
            point_ref[part, at : at + hi - lo, :] = values[:, own * part : own * (part + 1)].astype(
                BF16
            )
        values = point_in[1, lo:hi, :].astype(F32)
        gap = jnp.zeros((hi - lo, 64), F32)
        second_ref[at : at + hi - lo, :] = jnp.concatenate(
            [values[:, :576], gap, values[:, 576:]], axis=1
        ).astype(BF16)
    for part in range(parts):
        point_ref[part, 448:SECOND, :] = jnp.zeros((64, own), BF16)
    second_ref[448:SECOND, :] = jnp.zeros((64, OUTER), BF16)
    for source, outer, reduced in ((gain_in, vectors[0], vectors[1]), (shift_in, vectors[2], vectors[3])):
        outer[:, 0:256] = source[:, 0:256]
        outer[:, 256:576] = source[:, 576:896]
        outer[:, 576:640] = jnp.zeros((2, 64), F32)
        outer[:, 640:768] = source[:, 896:1024]
        outer[:, 768:896] = source[:, 448:576]
        reduced[:, 0:192] = source[:, 256:448]
        reduced[:, 192:256] = jnp.zeros((2, 64), F32)


def round_up(value, unit):
    return -(-value // unit) * unit


def spread_over(values, axis, size):
    received = [values]
    for step in range(1, size):
        perm = [(source, (source + step) % size) for source in range(size)]
        received.append(lax.ppermute(values, axis, perm))
    return received


def after(values, earlier):
    return lax.optimization_barrier((values, earlier))[0]


def exchange(values):
    return lax.all_to_all(values, "dp", 0, 0, tiled=True)


def add_up(pieces):
    return jnp.sum(pieces.astype(F32), axis=0).astype(BF16)


def gather_chips(column, clips, work=None):
    columns = [column]
    for chip in range(1, clips // 2):
        perm = [(source, source ^ (2 * chip)) for source in range(clips)]
        columns.append(lax.ppermute(column, "dp", perm))
    if work is not None:
        columns = after(columns, work)
    mine = jnp.concatenate(columns, axis=0)
    other = lax.ppermute(mine, "dp", [(source, source ^ 1) for source in range(clips)])
    return (mine, other)


def on_device(frames, lengths, cotangent, pointwise, conv_mid, conv_small, gains, shifts):
    parts = lax.axis_size("branch")
    clips = lax.axis_size("dp")
    place = lax.axis_index("branch").astype(jnp.int32)
    side = frames.shape[2]
    grid, small = (Grid(side, frames.shape[1]), Grid(side // 2, frames.shape[1] // 2))
    slots = Slots(grid, parts)
    cells = side * side
    own_channels = frames.shape[-1]
    length = lengths.astype(jnp.int32)
    half_length = length // 2
    place_one = place.reshape(1)

    own = frames[0].transpose(1, 2, 0, 3).reshape(grid.rows, own_channels)
    turned = call(functools.partial(turn, slots), shape((parts, own_channels, slots.rows), BF16))(own)
    by_pairs = lax.all_to_all(turned, "branch", 0, 0, tiled=True)
    kernel_shapes = (
        shape((9, 512, 256), BF16),
        shape((3, 512, 256), BF16),
        shape((1152, 128), BF16),
        shape((1152, 128), BF16),
    )
    prepared = call(
        functools.partial(prepare, parts),
        (
            *kernel_shapes,
            *kernel_shapes,
            shape((parts, FIRST, own_channels), BF16),
            shape((FIRST, OUTER), BF16),
            shape((2, OUTER), F32),
            shape((2, REDUCED), F32),
            shape((2, OUTER), F32),
            shape((2, REDUCED), F32),
        ),
    )(conv_mid, conv_small, pointwise.swapaxes(1, 2), gains, shifts)
    kernels = (prepared[0:4], prepared[4:8])
    point_first, point_second, outer_gain, reduced_gain, outer_shift, reduced_shift = prepared[8:]

    local_count = (length * (slots.held(place) * 2 * side)).astype(F32)
    mid, pool, direct, sums = call(
        functools.partial(first_pointwise, slots),
        (
            shape((mid_rows(slots), 128), BF16),
            shape((slots.rows + TILE, POOLED), BF16),
            shape((slots.rows, DIRECT), F32),
            shape((clips, 3, SECOND), F32),
        ),
        [pltpu.VMEM((slots.rows, FIRST), F32)],
        scalars=2,
        vmem=VMEM_BYTES // 3,
    )(length, local_count, by_pairs, point_first)
    mids = spread_over(mid, "branch", parts)
    sums = spread_over(jnp.sum(exchange(sums), axis=0), "branch", parts)
    pools = spread_over(after(pool, (mids, sums)), "branch", parts)
    h_reduced, taps_mid, taps_few, e, e_sums = call(
        functools.partial(first_convolve, grid, slots, 0),
        conv_outputs(grid),
        conv_scratch(grid),
        scalars=2,
        cost=40,
        far=range(4 + 2 * parts, 7 + 2 * parts),
        far_out=range(4),
    )(length, place_one, *mids, *sums, reduced_gain, reduced_shift, *kernels[0][:3])
    q_pool, second_sums = call(
        functools.partial(first_pool, grid, slots),
        (shape((grid.rows, POOLED), F32), shape((clips, 2, FIRST), F32)),
        [
            pltpu.VMEM((grid.rows + 2 * grid.line_rows, POOLED), F32),
            pltpu.VMEM((16, POOLED), F32),
        ],
        scalars=2,
    )(length, place_one, *pools, e_sums)
    second_sums = exchange(second_sums)
    pooled_direct, kept_direct, moment = call(
        functools.partial(first_direct, grid, small, slots, 0),
        (
            shape((slots.each * small.line_rows, DIRECT), BF16),
            shape((slots.rows + slots.each * small.line_rows, 2 * DIRECT), BF16),
            shape((3, SECOND), F32),
        ),
        scalars=1,
        cost=3,
    )(length, direct, outer_gain, outer_shift, *sums)
    second_sums, pooled_direct = lax.optimization_barrier((second_sums, pooled_direct))
    pooled_directs = spread_over(pooled_direct, "branch", parts)
    kept_direct = lax.all_gather(after(kept_direct, second_sums), "branch", axis=0)
    pair = 2 * grid.line_rows
    pooled, h_outer, slope, outer, pooled_slope, pooled_product = call(
        functools.partial(first_output, grid, small, 0),
        (
            shape((small.rows, FIRST), BF16),
            shape((grid.rows, FIRST), BF16),
            shape((grid.rows, FIRST), BF16),
            shape((3, OUTER), F32),
            shape((small.rows, FIRST), BF16),
            shape((small.rows, FIRST), BF16),
        ),
        [
            pltpu.VMEM((2, pair, POOLED), F32),
            pltpu.VMEM((2, pair, SECOND), F32),
            pltpu.VMEM((2, pair, FIRST), BF16),
            pltpu.VMEM((2, pair, FIRST), BF16),
            *[pltpu.SemaphoreType.DMA((2,))] * 4,
        ],
        scalars=1,
        far=(1, 2),
        far_out=(1, 2),
    )(
        length,
        q_pool,
        e,
        moment,
        second_sums,
        outer_gain,
        outer_shift,
    )

    small_count = half_length.astype(F32) * float(small.side * small.side)
    q_small, sums_small, pooled = call(
        functools.partial(second_pointwise, small, slots),
        (
            shape((small.rows, FIRST), F32),
            shape((clips, 3, FIRST), F32),
            shape((small.rows, OUTER), BF16),
        ),
        [
            pltpu.VMEM((small.rows + 2 * small.line_rows, POOLED), F32),
            pltpu.VMEM((16, SECOND), F32),
            pltpu.VMEM((16, POOLED), F32),
        ],
        scalars=3,
    )(half_length, place_one, small_count, *pooled_directs, pooled, point_second)
    sums_small = exchange(sums_small)
    h_reduced_small, taps_mid_small, taps_few_small, e_small, e_sums_small, moment_small = call(
        functools.partial(second_convolve, small, 1),
        (*conv_outputs(small, clips), shape((3, FIRST), F32)),
        [*conv_scratch(small), pltpu.VMEM((small.rows + 2 * small.line_rows, REDUCED), F32)],
        scalars=1,
        far=range(5, 8),
        far_out=range(4),
    )(half_length, q_small, sums_small, reduced_gain, reduced_shift, *kernels[1][:3])
    e_sums_small = exchange(e_sums_small)
    cot = cotangent[0].transpose(1, 2, 0, 3).reshape(small.side**2, cotangent.shape[1], CHANNELS)
    act, h_outer_small, error_small, outer_small, outer_sums_small = call(
        functools.partial(second_output, small, 1),
        (
            shape(cot.shape, BF16),
            shape((small.rows, OUTER), BF16),
            shape((small.rows, OUTER), BF16),
            shape((3, OUTER), F32),
            shape((clips, 2, OUTER), F32),
        ),
        [pltpu.VMEM((16, OUTER), F32)],
        scalars=1,
    )(half_length, q_small, e_small, moment_small, e_sums_small, outer_gain, outer_shift, cot)

    taps_each = -(-TAPS // parts)
    tap_share = round_up(taps_each * TAP_ROWS, 16 * clips) // clips
    first_tap = place_one * taps_each

    def conv_back_scratch(at):
        return [
            pltpu.VMEM((9, 512, 256), BF16),
            pltpu.VMEM((3, 512, 256), BF16),
            pltpu.VMEM((1152, 128), BF16),
            pltpu.VMEM((at.copies, at.padded, 256), BF16),
            pltpu.VMEM((at.group * at.pitch, FIRST), F32),
            pltpu.VMEM((16, REDUCED), F32),
            pltpu.SemaphoreType.DMA((3,)),
        ]

    gathered = exchange(outer_sums_small)
    d_low, total_small, packed_small = call(
        functools.partial(second_back, small, None, 1, taps_each),
        (
            shape((small.copies, small.padded, SECOND), BF16),
            shape((2, OUTER), F32),
            shape((clips, tap_share, 128), BF16),
        ),
        second_back_scratch(small, taps_each),
        scalars=2,
        cost=8,
        far=(2, 6, 7, 8),
        far_out=(0,),
    )(
        half_length,
        first_tap,
        h_outer_small,
        outer_small,
        gathered,
        outer_gain,
        error_small,
        taps_mid_small,
        taps_few_small,
    )
    r_low, sums_low = call(
        functools.partial(conv_back, small, None, 1),
        (shape((small.rows, REDUCED), BF16), shape((clips, 2, REDUCED), F32)),
        conv_back_scratch(small),
        scalars=1,
        cost=8,
        far=(5, 6, 7),
    )(
        half_length,
        d_low,
        h_reduced_small,
        reduced_gain,
        reduced_shift,
        *kernels[1][:2],
        kernels[1][3],
    )
    share_small = add_up(exchange(packed_small))
    sums_low, share_small = lax.optimization_barrier((sums_low, share_small))
    gathered = exchange(sums_low)
    kept = OUTER // parts
    point_share = round_up(kept * (FIRST // 128), 16 * clips) // clips
    coarse_rows = slots.each * small.line_rows
    dx_small, point_packed, reduced_total_small, outer_sums = call(
        functools.partial(point_back, small, slots, 1, kept),
        (
            shape((small.rows, OUTER), BF16),
            shape((clips, point_share, 128), BF16),
            shape((2, REDUCED), F32),
            shape((clips, 2, OUTER), F32),
        ),
        [
            pltpu.VMEM((small.rows, DIRECT + POOLED), BF16),
            pltpu.VMEM((small.rows, DIRECT + POOLED), BF16),
            pltpu.VMEM((small.rows, REDUCED), BF16),
            pltpu.VMEM((small.rows, REDUCED), BF16),
            pltpu.VMEM((small.rows, OUTER), BF16),
            pltpu.VMEM((FIRST, OUTER), BF16),
            pltpu.VMEM((small.rows, FIRST), BF16),
            pltpu.VMEM((OUTER, FIRST), F32),
            *Spread.scratch(small),
            pltpu.VMEM((16, OUTER), F32),
            pltpu.VMEM((small.rows, OUTER), BF16),
            pltpu.VMEM((small.rows, OUTER), BF16),
            pltpu.VMEM((parts, coarse_rows, 2 * DIRECT), BF16),
            Lines.semaphores(small, 6),
            pltpu.SemaphoreType.DMA((3,)),
        ],
        scalars=2,
        cost=10,
        far=(2, 6, 7, 8, 12, 13, 16),
    )(
        half_length,
        place_one,
        h_outer_small,
        outer_small,
        total_small,
        outer_gain,
        error_small,
        h_reduced_small,
        r_low,
        moment_small,
        gathered,
        reduced_gain,
        pooled,
        point_second,
        pooled_slope,
        pooled_product,
        kept_direct,
    )
    whole_small = lax.all_gather(share_small, ("branch", "dp"), axis=0)

    gathered = exchange(outer_sums)
    d_low, total, packed = call(
        functools.partial(second_back, grid, small, 0, taps_each),
        (
            shape((grid.copies, grid.padded, SECOND), BF16),
            shape((2, OUTER), F32),
            shape((clips, tap_share + point_share, 128), BF16),
        ),
        second_back_scratch(grid, taps_each),
        scalars=2,
        cost=18,
        far=(2, 6, 9, 10),
        far_out=(0,),
    )(length, first_tap, h_outer, outer, gathered, outer_gain, slope, dx_small, point_packed, taps_mid, taps_few)
    product_rows = round_up(own_channels, 16 * clips)
    du_rest, rest_product = call(
        functools.partial(rest_back, grid, small, slots, 0),
        (
            shape((grid.rows, DIRECT + POOLED), BF16),
            shape((clips, 6, product_rows // clips, 128), F32),
        ),
        [
            pltpu.VMEM((grid.rows, DIRECT + POOLED), BF16),
            pltpu.VMEM((grid.rows, DIRECT + POOLED), BF16),
            pltpu.VMEM(turned.shape, BF16),
            pltpu.VMEM((grid.rows, REDUCED), BF16),
            pltpu.VMEM((grid.rows, DIRECT + POOLED), BF16),
            *Spread.scratch(grid),
            pltpu.VMEM((product_rows, 768), F32),
            Lines.semaphores(grid, 4),
            pltpu.SemaphoreType.DMA((2,)),
            pltpu.SemaphoreType.DMA((1,)),
        ],
        scalars=1,
        cost=8,
        far=(5, 6, 7, 8, 9),
        far_out=(0,),
    )(length, outer, after(total, packed), outer_gain, dx_small, h_outer, slope, kept_direct, turned, h_reduced)
    share = add_up(exchange(packed))
    rest_pieces = exchange(rest_product)
    d_low, share = lax.optimization_barrier((after(d_low, rest_product), share))
    r_low, sums_low, products = call(
        functools.partial(conv_back, grid, slots, 0),
        (
            shape((grid.rows, REDUCED), BF16),
            shape((clips, 2, REDUCED), F32),
            shape((clips, 2, product_rows // clips, 128), F32),
        ),
        [
            *conv_back_scratch(grid),
            pltpu.VMEM(turned.shape, BF16),
            pltpu.VMEM((product_rows, REDUCED), F32),
            pltpu.SemaphoreType.DMA((1,)),
        ],
        scalars=1,
        cost=22,
        far=(5, 6, 7, 8),
    )(
        length,
        d_low,
        h_reduced,
        reduced_gain,
        reduced_shift,
        *kernels[0][:2],
        kernels[0][3],
        turned,
    )
    whole = lax.all_gather(share, ("branch", "dp"), axis=0)
    sums_low, rest_pieces = lax.optimization_barrier((sums_low, rest_pieces))
    gathered = exchange(sums_low)
    pieces = exchange(products)
    dx, reduced_total = call(
        functools.partial(mid_back, grid, 0),
        (shape((grid.rows, own_channels), BF16), shape((2, REDUCED), F32)),
        [
            pltpu.VMEM((grid.rows, DIRECT + POOLED), BF16),
            pltpu.VMEM((grid.rows, REDUCED), BF16),
            pltpu.VMEM((grid.rows, REDUCED), BF16),
            pltpu.VMEM((FIRST, own_channels), BF16),
            pltpu.VMEM((grid.rows, own_channels), BF16),
            Lines.semaphores(grid, 3),
            pltpu.SemaphoreType.DMA((1,)),
            pltpu.SemaphoreType.DMA((1,)),
        ],
        scalars=2,
        cost=8,
        far=(5, 6, 7, 8),
        far_out=(0,),
    )(length, place_one, moment, gathered, reduced_gain, du_rest, h_reduced, r_low, point_first)
    pieces, dx = lax.optimization_barrier((pieces, dx))
    point_sum = call(
        functools.partial(combine, 0),
        shape((5 * product_rows // clips, 128), BF16),
        cost=1,
        vmem=VMEM_BYTES // 3,
    )(rest_pieces, pieces, moment, gathered, reduced_gain)
    received = spread_over(point_sum, "branch", parts)

    outs = (
        shape((2, TAPS, MID_IN, MID_OUT), F32),
        shape((2, TAPS, SMALL_IN, SMALL_OUT), F32),
        shape((2, SQUEEZED, CHANNELS), F32),
    )
    tap_scratch = [
        pltpu.VMEM((TAPS, MID_IN, MID_OUT), F32),
        pltpu.VMEM((TAPS, SMALL_IN, SMALL_OUT), F32),
    ]
    point_scratch = [pltpu.VMEM((SQUEEZED, CHANNELS), F32), pltpu.VMEM((CHANNELS, 128), F32)]
    mid_grad, small_grad = call(
        functools.partial(unpack_second, clips, taps_each),
        outs[:2],
        [
            pltpu.VMEM(whole_small.shape, BF16),
            *tap_scratch,
            pltpu.SemaphoreType.DMA((2,)),
            pltpu.SemaphoreType.DMA((parts,)),
        ],
        far=(0,),
        far_out=(0, 1),
        cost=5,
    )(whole_small)
    received, mid_grad, small_grad = lax.optimization_barrier((received, mid_grad, small_grad))
    norms = shape((2, 1024), F32)
    mid_grad, small_grad, point_grad, gain_grad, shift_grad = call(
        functools.partial(unpack_first, parts, clips, taps_each, tap_share),
        (*outs, norms, norms),
        [
            pltpu.VMEM(whole.shape, BF16),
            *tap_scratch,
            *point_scratch,
            pltpu.SemaphoreType.DMA((3,)),
            pltpu.SemaphoreType.DMA((parts,)),
        ],
        far=(0,),
        far_out=(0, 1, 2),
        aliases={5: 0, 6: 1},
        cost=6,
    )(whole, total, reduced_total, total_small, reduced_total_small, mid_grad, small_grad)
    point_mine, point_other = gather_chips(
        jnp.concatenate(received, axis=0), clips, (mid_grad, small_grad)
    )
    clip_one = lax.axis_index("dp").astype(jnp.int32).reshape(1)
    point_grad = call(
        functools.partial(unpack_point, parts, clips, own_channels),
        outs[2],
        [
            pltpu.VMEM((parts, FIRST // 128, product_rows, 128), BF16),
            *point_scratch,
            pltpu.SemaphoreType.DMA((1,)),
        ],
        scalars=2,
        far_out=(0,),
        aliases={4: 0},
        cost=3,
        vmem=VMEM_BYTES // 2,
    )(place_one, clip_one, point_mine, point_other, point_grad)
    act = act.reshape(small.side, small.side, cotangent.shape[1], CHANNELS).transpose(2, 0, 1, 3)
    input_grad = dx.reshape(side, side, grid.unit, own_channels).transpose(2, 0, 1, 3)
    return (
        act[None],
        input_grad[None],
        point_grad.swapaxes(1, 2),
        mid_grad,
        small_grad,
        gain_grad,
        shift_grad,
    )


def solution(mesh):
    split = P("dp", None, None, None, "branch")
    whole = P("dp", None, None, None, None)
    return jax.shard_map(
        on_device,
        mesh=mesh,
        in_specs=(split, P("dp"), whole, P(), P(), P(), P(), P()),
        out_specs=(whole, split, P(), P(), P(), P(), P()),
        check_vma=False,
    )
```

```python
import functools

import jax
import jax.numpy as jnp
from jax import lax
from jax.experimental import pallas as pl
from jax.experimental.pallas import tpu as pltpu
from jax.sharding import PartitionSpec as P

DIRECT = 256
MID_IN = 160
MID_OUT = 320
SMALL_IN = 32
SMALL_OUT = 128
TAPS = 27
CHANNELS = 832
SQUEEZED = 576
TILE = 16
REDUCED = 256
POOLED = 128
FIRST = 640
SECOND = 512
OUTER = 896
TAP_ROWS = 432
EPSILON = 1e-05
F32 = jnp.float32
BF16 = jnp.bfloat16
VMEM_BYTES = 58 * 2**20
LARGE = 2200 * 2**10


def call(body, out_shape, scratch=(), scalars=0, cost=5, vmem=VMEM_BYTES, aliases=None, far=(), far_out=()):
    aliases = aliases or {}

    def large(values):
        size = values.dtype.itemsize
        for extent in values.shape:
            size = size * extent
        return size > LARGE

    def placed(out):
        return pltpu.HBM(out.shape, out.dtype) if large(out) else out

    def run(*operands):
        specs = [
            pl.BlockSpec(
                memory_space=pl.ANY
                if number in aliases or number in far
                else pltpu.SMEM
                if number < scalars
                else pltpu.VMEM
            )
            for number in range(len(operands))
        ]
        operands = [
            pltpu.with_memory_space_constraint(operand, pltpu.HBM) if large(operand) else operand
            for operand in operands
        ]
        if isinstance(out_shape, tuple):
            out_specs = tuple(
                pl.BlockSpec(memory_space=pl.ANY if number in far_out else pltpu.VMEM)
                for number in range(len(out_shape))
            )
        else:
            out_specs = pl.BlockSpec(memory_space=pl.ANY if 0 in far_out else pltpu.VMEM)
        return pl.pallas_call(
            body,
            out_shape=jax.tree.map(placed, out_shape),
            in_specs=specs,
            out_specs=out_specs,
            input_output_aliases=aliases,
            scratch_shapes=list(scratch),
            compiler_params=pltpu.CompilerParams(vmem_limit_bytes=vmem),
            cost_estimate=pl.CostEstimate(
                flops=0, bytes_accessed=int(cost * 3 * 10**6), transcendentals=0
            ),
        )(*operands)

    return run


def shape(dims, dtype):
    return jax.ShapeDtypeStruct(tuple(dims), dtype)


def rows_at(start, size):
    return pl.ds(pl.multiple_of(start, 16), size)


def frames_of(values_or_rows, unit):
    dims = values_or_rows if isinstance(values_or_rows, tuple) else (values_or_rows, 128)
    return lax.broadcasted_iota(jnp.int32, dims, 0) & (unit - 1)


def keep_frames(values, unit, lo, hi):
    rows, width = values.shape
    frame = lax.broadcasted_iota(jnp.int32, (1, unit, width), 1)
    kept = jnp.where((frame >= lo) & (frame < hi), 1.0, 0.0)
    return (values.reshape(rows // unit, unit, width) * kept).reshape(rows, width)


def earlier(values, unit):
    return keep_frames(pltpu.roll(values, 1, 0), unit, 1, unit)


def later(values, unit):
    return keep_frames(pltpu.roll(values, values.shape[0] - 1, 0), unit, 0, unit - 1)


def plane_box(values, unit):
    across = values + earlier(values, unit) + later(values, unit)
    edge = jnp.zeros((unit, values.shape[1]), values.dtype)
    return (
        across
        + jnp.concatenate([across[unit:], edge], axis=0)
        + jnp.concatenate([edge, across[:-unit]], axis=0)
    )


def box_window(grid, length):
    frame, place = (frames_of(grid.line_rows, grid.unit), grid.places_of(grid.line_rows))

    def one(condition):
        return jnp.where(condition, 1.0, 0.0)

    count = one(frame < length) + one(frame + 1 < length) + one((frame > 0) & (frame - 1 < length))
    return count * (3.0 - one(place == 0) - one(place == grid.side - 1))


def box_scale(line, side, window):
    lines = 3.0 - jnp.where(line == 0, 1.0, 0.0) - jnp.where(line == side - 1, 1.0, 0.0)
    return 1.0 / jnp.maximum(window * lines, 1.0)


def sigmoid(value):
    return 0.5 * jnp.tanh(0.5 * value) + 0.5


def silu(value):
    return value * sigmoid(value)


def silu_slope(value):
    gate = sigmoid(value)
    return gate * (1.0 + value * (1.0 - gate))


def partial_sum(values):
    rows, width = values.shape
    return jnp.sum(values.reshape(rows // 8, 8, width), axis=0)


def moments(total, square, count):
    center = total / count
    return (center, lax.rsqrt(square / count - center * center + EPSILON))


def total_of(gathered):
    count = len(gathered) if isinstance(gathered, (list, tuple)) else gathered.shape[0]
    total = gathered[0][...]
    for number in range(1, count):
        total = total + gathered[number][...]
    return total


def pool_matrix(grid, small, transposed):
    line = grid.line_rows
    few, many = (small.line_rows, 2 * line)
    dims = (many, few) if transposed else (few, many)
    coarse = lax.broadcasted_iota(jnp.int32, dims, 1 if transposed else 0)
    fine = lax.broadcasted_iota(jnp.int32, dims, 0 if transposed else 1)
    fine = jnp.where(fine >= line, fine - line, fine)
    same = (fine >> (grid.bits + 1) == coarse >> small.bits) & (
        (fine & (grid.unit - 1)) >> 1 == coarse & (small.unit - 1)
    )
    return jnp.where(same, 0.125, 0.0).astype(BF16)


class Grid:
    def __init__(self, side, unit):
        self.side, self.unit = (side, unit)
        self.bits = unit.bit_length() - 1
        self.copies = TILE // unit
        self.line_rows = side * unit if self.copies == 1 else (side + 1) * unit
        self.rows = side * self.line_rows
        self.pitch = (side + 1) * unit
        margin = 1 if self.copies == 1 else 2
        self.lead = margin * self.pitch + TILE
        self.padded = (side + 2 * margin) * self.pitch + 2 * TILE
        self.group = 2 if side % 2 == 0 else side

    def places_of(self, rows):
        place = lax.broadcasted_iota(jnp.int32, (rows, 128), 0) >> self.bits
        return place if self.copies == 1 else place & self.side

    def mask(self, rows, length, width=128):
        valid = frames_of(rows, self.unit) < length
        if self.copies > 1:
            valid = valid & (self.places_of(rows) < self.side)
        mask = jnp.where(valid, 1.0, 0.0)
        return jnp.concatenate([mask] * (width // 128), axis=1) if width > 128 else mask

    def near(self, ref, base, lines, places, size, lanes=slice(None)):
        start = base + lines * self.pitch
        if self.copies == 1:
            return ref[0, rows_at(start + places * TILE, size), lanes]
        copy = 0 if places == 0 else 1
        return ref[copy, rows_at(start - (TILE if places < 0 else 0), size), lanes]


class Slots:
    def __init__(self, grid, parts):
        self.pairs = grid.side // 2
        self.parts = parts
        self.each = -(-self.pairs // parts)
        self.empty = parts * self.each - self.pairs
        self.gap = parts * self.each // 2 - 1
        self.pair_rows = 2 * grid.line_rows
        self.grid = grid
        self.rows = self.each * self.pair_rows

    def slot_of(self, pair):
        return pair + jnp.where(pair >= self.gap, self.empty, 0)

    def pair_of(self, slot):
        return slot - jnp.where(slot >= self.gap, self.empty, 0)

    def used(self, slot):
        return (slot < self.gap) | (slot >= self.gap + self.empty)

    def held(self, place):
        count = jnp.zeros((), jnp.int32)
        for number in range(self.each):
            count = count + jnp.where(self.used(place * self.each + number), 1, 0)
        return count


def clear_empty(grid, ref):
    width = ref.shape[2]
    if grid.copies > 1:
        ref[...] = jnp.zeros_like(ref)
        return
    ref[0, 0 : grid.lead, :] = jnp.zeros((grid.lead, width), ref.dtype)
    end = grid.lead + grid.side * grid.pitch
    ref[0, end:, :] = jnp.zeros((ref.shape[1] - end, width), ref.dtype)

    @pl.loop(0, grid.side)
    def _(line):
        at = rows_at(grid.lead + line * grid.pitch + grid.line_rows, TILE)
        ref[0, at, :] = jnp.zeros((TILE, width), ref.dtype)


def store_taps(unit, mid_ref, small_ref, copy, at, act):
    before, after_ = (earlier(act, unit), later(act, unit))
    mid_ref[copy, at, 0:128] = before[:, :128].astype(BF16)
    mid_ref[copy, at, 128:256] = act[:, :128].astype(BF16)
    mid_ref[copy, at, 256:384] = after_[:, :128].astype(BF16)
    before, act, after_ = (before[:, 128:], act[:, 128:], after_[:, 128:])
    lane = lax.broadcasted_iota(jnp.int32, act.shape, 1)
    mid_ref[copy, at, 384:512] = jnp.where(
        lane < 32, before, jnp.where(lane < 64, pltpu.roll(act, 32, 1), pltpu.roll(after_, 64, 1))
    ).astype(BF16)
    small_ref[copy, at, :] = jnp.where(
        lane < 32, pltpu.roll(before, 96, 1), jnp.where(lane < 64, act, pltpu.roll(after_, 32, 1))
    ).astype(BF16)


def near_tap(grid, ref, base, tap, sign, size, lanes=slice(None)):
    return grid.near(ref, base, sign * (tap // 3 - 1), sign * (tap % 3 - 1), size, lanes)


def convolve(grid, taps, kernels, rest_ref, acc_ref, stage_ref, e_ref, stage_sem, sums_ref, length):
    mid_ref, small_ref = taps
    main_ref, last_ref, small_kernel_ref = kernels
    group_rows = grid.group * grid.pitch
    stage_rows = grid.group * grid.line_rows
    groups = grid.side // grid.group
    sums_ref[...] = jnp.zeros_like(sums_ref)
    mask = grid.mask(grid.line_rows, length, SECOND)
    edge = jnp.zeros((grid.pitch, 256), F32)
    rest_ref[grid.lead - grid.pitch : grid.lead, :] = edge
    end = grid.lead + grid.side * grid.pitch
    rest_ref[end : end + grid.pitch, :] = edge

    @pl.loop(0, groups)
    def _(group):
        base = grid.lead + group * group_rows
        total = None
        for place in range(3):
            part = jnp.dot(
                grid.near(mid_ref, base, 0, place - 1, group_rows),
                last_ref[place],
                preferred_element_type=F32,
            )
            total = part if total is None else total + part
        rest_ref[rows_at(base, group_rows), :] = total

    lane = lax.broadcasted_iota(jnp.int32, (grid.line_rows, 128), 1)

    def staged(group, slot):
        return pltpu.make_async_copy(
            stage_ref.at[slot],
            e_ref.at[rows_at(group * stage_rows, stage_rows), :],
            stage_sem.at[slot],
        )

    @pl.loop(0, groups)
    def _(group):
        base = grid.lead + group * group_rows
        slot = lax.rem(group, 2)
        for tap in range(9):
            part = jnp.dot(
                near_tap(grid, mid_ref, base, tap, 1, group_rows),
                main_ref[tap],
                preferred_element_type=F32,
            )
            acc_ref[:, 0:256] = part if tap == 0 else acc_ref[:, 0:256] + part
        near = [near_tap(grid, small_ref, base, tap, 1, group_rows) for tap in range(9)]
        acc_ref[:, 256:384] = jnp.dot(
            jnp.concatenate(near, axis=1), small_kernel_ref[...], preferred_element_type=F32
        )

        @pl.when(group >= 2)
        def _():
            staged(group - 2, slot).wait()

        for number in range(grid.group):
            rows = grid.line_rows
            start = base + number * grid.pitch
            last = (
                rest_ref[rows_at(start - grid.pitch, rows), 0:128]
                + pltpu.roll(rest_ref[rows_at(start, rows), 0:128], 64, 1)
                + rest_ref[rows_at(start + grid.pitch, rows), 128:256]
            )
            lines = slice(number * grid.pitch, number * grid.pitch + rows)
            values = jnp.concatenate(
                [acc_ref[lines, 0:256], jnp.where(lane < 64, last, 0.0), acc_ref[lines, 256:384]],
                axis=1,
            )
            stage_ref[slot, number * rows : (number + 1) * rows, :] = values
            masked = values * mask
            sums_ref[0:8] += partial_sum(masked)
            sums_ref[8:16] += partial_sum(masked * values)
        staged(group, slot).start()

    for group in range(max(groups - 2, 0), groups):
        staged(group, group % 2).wait()


def conv_scratch(grid):
    group_rows = grid.group * grid.pitch
    return [
        pltpu.VMEM((9, 512, 256), BF16),
        pltpu.VMEM((3, 512, 256), BF16),
        pltpu.VMEM((1152, 128), BF16),
        pltpu.VMEM((grid.copies, grid.padded, 512), BF16),
        pltpu.VMEM((grid.copies, grid.padded, 128), BF16),
        pltpu.VMEM((grid.rows, REDUCED), BF16),
        pltpu.VMEM((grid.padded, 256), F32),
        pltpu.VMEM((group_rows, 384), F32),
        pltpu.VMEM((2, grid.group * grid.line_rows, SECOND), F32),
        pltpu.VMEM((16, SECOND), F32),
        pltpu.SemaphoreType.DMA((3,)),
        pltpu.SemaphoreType.DMA((3,)),
        pltpu.SemaphoreType.DMA((2,)),
    ]


def conv_outputs(grid, *clips):
    return (
        shape((grid.rows, REDUCED), BF16),
        shape((grid.copies, grid.padded, 512), BF16),
        shape((grid.copies, grid.padded, 128), BF16),
        shape((grid.rows, SECOND), F32),
        shape((*clips, 2, SECOND), F32),
    )


def copies(sources, targets, sem_ref):
    return [
        pltpu.make_async_copy(source, target, sem_ref.at[number])
        for number, (source, target) in enumerate(zip(sources, targets))
    ]


def run_convolution(grid, length, far_kernels, outputs, scratch, fill):
    h_out, mid_out, small_out, e_out, sums_out = outputs
    kernels, (mid_ref, small_ref, h_ref), rest = (scratch[:3], scratch[3:6], scratch[6:])
    rest_ref, acc_ref, stage_ref, sums_ref, in_sem, out_sem, stage_sem = rest
    arriving = copies(far_kernels, kernels, in_sem)
    for copy in arriving:
        copy.start()
    clear_empty(grid, mid_ref)
    clear_empty(grid, small_ref)
    fill(h_ref, mid_ref, small_ref)
    leaving = copies((mid_ref, small_ref, h_ref), (mid_out, small_out, h_out), out_sem)
    for copy in leaving:
        copy.start()
    for copy in arriving:
        copy.wait()
    convolve(
        grid, (mid_ref, small_ref), kernels, rest_ref, acc_ref, stage_ref, e_out, stage_sem, sums_ref, length
    )
    write_sums(sums_out, sums_ref, 0, SECOND)
    for copy in leaving:
        copy.wait()


def write_row(out_ref, row, lo, hi, values):
    if len(out_ref.shape) == 2:
        out_ref[row : row + 1, lo:hi] = values
    else:
        for clip in range(out_ref.shape[0]):
            out_ref[clip, row : row + 1, lo:hi] = values


def write_sums(out_ref, sums_ref, lo, hi):
    for number in range(2):
        values = jnp.sum(sums_ref[8 * number : 8 * number + 8], axis=0, keepdims=True)
        write_row(out_ref, number, lo, hi, values)


def turn(slots, x_ref, out_ref):
    for slot in range(slots.parts * slots.each):
        part, number = divmod(slot, slots.each)
        lanes = slice(number * slots.pair_rows, (number + 1) * slots.pair_rows)
        if slots.gap <= slot < slots.gap + slots.empty:
            out_ref[part, :, lanes] = jnp.zeros((out_ref.shape[1], slots.pair_rows), BF16)
            continue
        pair = slot - (slots.empty if slot >= slots.gap else 0)
        rows = slice(pair * slots.pair_rows, (pair + 1) * slots.pair_rows)
        out_ref[part, :, lanes] = x_ref[rows, :].T


def first_pointwise(slots, length_ref, count_ref, x_ref, p_ref, mid_ref, pool_ref, direct_ref, sums_ref, u_ref):
    rows, step = (slots.rows, 112)
    length, count = (length_ref[0], count_ref[0])
    for part in range(slots.parts):
        product = lax.dot_general(
            x_ref[part], p_ref[part], (((0,), (1,)), ((), ())), preferred_element_type=F32
        )
        u_ref[...] = product if part == 0 else u_ref[...] + product
    mask = slots.grid.mask(step, length, FIRST)

    def summed(number, carry):
        values = u_ref[rows_at(number * step, step), :] * mask
        u_ref[rows_at(number * step, step), :] = values
        few = values[:, :SECOND]
        return (carry[0] + partial_sum(values), carry[1] + partial_sum(few * few))

    zero = (jnp.zeros((8, FIRST), F32), jnp.zeros((8, SECOND), F32))
    total, square = lax.fori_loop(0, rows // step, summed, zero)
    total = jnp.sum(total, axis=0, keepdims=True)
    write_row(sums_ref, 0, 0, SECOND, total[:, :SECOND])
    write_row(sums_ref, 1, 0, SECOND, jnp.sum(square, axis=0, keepdims=True))
    write_row(sums_ref, 2, 0, SECOND, jnp.full((1, SECOND), count, F32))
    offset = (total / jnp.full((1, FIRST), jnp.maximum(count, 1.0), F32)).astype(BF16)
    wide_offset = offset.astype(F32)
    tail = jnp.broadcast_to(wide_offset, (TILE, FIRST)).astype(BF16)
    pool_ref[rows : rows + TILE, :] = tail[:, SECOND:]
    shared = mid_ref.shape[0] - 2 * TILE
    mid_ref[shared : shared + TILE, :] = tail[:, 256:384]
    mid_ref[shared + TILE :, :] = tail[:, 384:512]

    @pl.loop(0, rows // step)
    def _(number):
        at = rows_at(number * step, step)
        values = u_ref[at, :]
        direct_ref[at, :] = values[:, :DIRECT]
        values = values[:, DIRECT:] - wide_offset[:, DIRECT:]
        mid_ref[at, :] = values[:, :128].astype(BF16)
        pool_ref[at, :] = values[:, 256:].astype(BF16)

    lane = lax.broadcasted_iota(jnp.int32, (step, 128), 1)
    for couple in range(0, slots.each, 2):

        @pl.loop(0, slots.pair_rows // step)
        def _(number):
            start = couple * slots.pair_rows + number * step
            values = u_ref[rows_at(start, step), 384:512] - wide_offset[:, 384:512]
            if couple + 1 < slots.each:
                other = u_ref[rows_at(start + slots.pair_rows, step), 384:512]
                other = pltpu.roll(other - wide_offset[:, 384:512], 64, 1)
                values = jnp.where(lane < 64, values, other)
            place = rows + couple // 2 * slots.pair_rows + number * step
            mid_ref[rows_at(place, step), :] = values.astype(BF16)


def mid_rows(slots):
    return slots.rows + -(-slots.each // 2) * slots.pair_rows + 2 * TILE


def each_pair(slots, place, refs, visit):
    for step, ref in enumerate(refs):
        source = lax.rem(place - step + slots.parts, slots.parts)
        for number in range(slots.each):
            slot = source * slots.each + number

            @pl.when(slots.used(slot))
            def _():
                visit(slots.pair_of(slot), ref, number)


def set_moments(total, moment_ref):
    count = total[2:3]
    center, inverse = moments(total[0:1], total[1:2], count)
    moment_ref[0:1, :] = center
    moment_ref[1:2, :] = inverse
    moment_ref[2:3, :] = count
    return (center, inverse)


def first_convolve(grid, slots, block, length_ref, place_ref, *refs):
    parts = slots.parts
    mids, sums, refs = (refs[:parts], refs[parts : 2 * parts], refs[2 * parts :])
    gain_ref, shift_ref, *refs = refs
    far_kernels, outputs, scratch = (refs[:3], refs[3:8], refs[8:])
    length = length_ref[0]
    total = total_of(sums)[:, DIRECT:]
    center, inverse = moments(total[0:1], total[1:2], total[2:3])
    gain, shift = (gain_ref[block : block + 1], shift_ref[block : block + 1])
    step = 112
    mask = grid.mask(step, length, REDUCED)
    lane = lax.broadcasted_iota(jnp.int32, (step, 128), 1)

    def fill(h_ref, mid_ref, small_ref):
        def visit(pair, ref, number):
            shared = ref.shape[0] - 2 * TILE
            offset = jnp.concatenate(
                [
                    ref[at : at + TILE, :].astype(F32)[0:1]
                    for at in (shared, shared + TILE)
                ],
                axis=1,
            )
            other = slots.rows + number // 2 * slots.pair_rows

            @pl.loop(0, slots.pair_rows // step)
            def _(chunk):
                values = ref[rows_at(number * slots.pair_rows + chunk * step, step), :].astype(F32)
                few = ref[rows_at(other + chunk * step, step), :].astype(F32)
                if number % 2 == 1:
                    few = pltpu.roll(few, 64, 1)
                few = jnp.where(lane < 64, few, 0.0)
                values = jnp.concatenate([values, few], axis=1) + offset
                scaled = (values - center) * inverse
                row = pair * slots.pair_rows + chunk * step
                h_ref[rows_at(row, step), :] = scaled.astype(BF16)
                act = silu(gain * scaled + shift) * mask
                line = row // grid.line_rows
                at = grid.lead + line * grid.pitch + row - line * grid.line_rows
                store_taps(grid.unit, mid_ref, small_ref, 0, rows_at(at, step), act)

        each_pair(slots, place_ref[0], mids, visit)

    run_convolution(grid, length, far_kernels, outputs, scratch, fill)


def pool_planes(grid, plane_ref, q_ref, lo, sums_ref, length, window):
    rows = grid.line_rows
    mask = grid.mask(rows, length)
    sums_ref[...] = jnp.zeros_like(sums_ref)

    @pl.loop(0, grid.side)
    def _(line):
        start = line * rows
        values = (
            plane_ref[rows_at(start, rows), :]
            + plane_ref[rows_at(start + rows, rows), :]
            + plane_ref[rows_at(start + 2 * rows, rows), :]
        ) * box_scale(line, grid.side, window)
        q_ref[rows_at(start, rows), lo : lo + POOLED] = values
        masked = values * mask
        sums_ref[0:8] += partial_sum(masked)
        sums_ref[8:16] += partial_sum(masked * values)


def clear_edges(grid, plane_ref):
    rows = grid.line_rows
    plane_ref[0:rows] = jnp.zeros((rows, POOLED), F32)
    plane_ref[grid.rows + rows : grid.rows + 2 * rows] = jnp.zeros((rows, POOLED), F32)


def first_pool(grid, slots, length_ref, place_ref, *refs):
    pools, refs = (refs[: slots.parts], refs[slots.parts :])
    e_sums_ref, q_ref, out_sums_ref, plane_ref, sums_ref = refs
    length = length_ref[0]
    rows = grid.line_rows
    for row in range(2):
        write_row(out_sums_ref, row, 0, SECOND, e_sums_ref[row : row + 1, :])
    clear_edges(grid, plane_ref)

    def visit(pair, ref, number):
        offset = ref[slots.rows : slots.rows + TILE, :].astype(F32)[0:1]
        for line in range(2):
            at = rows_at(number * slots.pair_rows + line * rows, rows)
            plane_ref[rows_at((2 * pair + line + 1) * rows, rows), :] = plane_box(
                ref[at, :].astype(F32) + offset, grid.unit
            )

    each_pair(slots, place_ref[0], pools, visit)
    pool_planes(grid, plane_ref, q_ref, 0, sums_ref, length, box_window(grid, length))
    write_sums(out_sums_ref, sums_ref, SECOND, FIRST)


def normalize(values, center, inverse, gain, shift, mask):
    scaled = (values - center) * inverse
    shifted = gain * scaled + shift
    gate = sigmoid(shifted)
    gate_mask = gate * mask
    act = shifted * gate_mask
    return (scaled, act, gate_mask + act * (1.0 - gate))


def pool_pieces(matrix, pieces):
    return jnp.dot(
        matrix, jnp.concatenate(pieces, axis=0), preferred_element_type=F32
    ).astype(BF16)


def first_direct(grid, small, slots, block, length_ref, u_ref, gain_ref, shift_ref, *refs):
    sums, (pooled_ref, kept_ref, moment_ref) = (refs[: slots.parts], refs[slots.parts :])
    rows = grid.line_rows
    mask = grid.mask(rows, length_ref[0], DIRECT)
    center, inverse = set_moments(total_of(sums), moment_ref)
    center, inverse = (center[:, :DIRECT], inverse[:, :DIRECT])
    gain, shift = (gain_ref[block : block + 1, :DIRECT], shift_ref[block : block + 1, :DIRECT])
    matrix = pool_matrix(grid, small, False)

    @pl.loop(0, slots.each)
    def _(number):
        acts, slopes, products = ([], [], [])
        for line in range(2):
            at = rows_at(number * slots.pair_rows + line * rows, rows)
            scaled, act, slope = normalize(u_ref[at, :], center, inverse, gain, shift, mask)
            kept_ref[at, :] = scaled.astype(BF16)
            acts.append(act.astype(BF16))
            slopes.append(slope.astype(BF16))
            products.append((slope * scaled).astype(BF16))
        size = small.line_rows
        pooled_ref[rows_at(number * size, size), :] = pool_pieces(matrix, acts)
        at = slots.rows + number * size
        kept_ref[rows_at(at, size), :] = pool_pieces(matrix, slopes)
        kept_ref[rows_at(at + slots.each * size, size), :] = pool_pieces(matrix, products)


def outer_moments(center, inverse, count, outer_ref):
    outer_ref[0:1, :] = center
    outer_ref[1:2, :] = inverse
    outer_ref[2:3, :] = jnp.concatenate([count[:, 0:128]] * (OUTER // 128), axis=1)


def first_output(grid, small, block, length_ref, q_far, e_far, moment_ref, sums_in_ref, gain_ref, shift_ref, *refs):
    pooled_ref, h_far, slope_far, outer_ref, pooled_slope_ref, pooled_product_ref, *refs = refs
    q_ref, e_ref, h_ref, slope_ref, q_sem, e_sem, h_sem, slope_sem = refs
    rows = grid.line_rows
    wide = 2 * rows
    pairs = grid.side // 2

    def arriving(pair, slot):
        at = rows_at(pair * wide, wide)
        return [
            pltpu.make_async_copy(q_far.at[at, :], q_ref.at[slot], q_sem.at[slot]),
            pltpu.make_async_copy(e_far.at[at, :], e_ref.at[slot], e_sem.at[slot]),
        ]

    def leaving(pair, slot):
        at = rows_at(pair * wide, wide)
        return [
            pltpu.make_async_copy(h_ref.at[slot], h_far.at[at, :], h_sem.at[slot]),
            pltpu.make_async_copy(slope_ref.at[slot], slope_far.at[at, :], slope_sem.at[slot]),
        ]

    for copy in arriving(0, 0):
        copy.start()
    mask = grid.mask(rows, length_ref[0], FIRST)
    total = total_of(sums_in_ref)
    count = jnp.concatenate([moment_ref[2:3, 0:128]] * (FIRST // 128), axis=1)
    center, inverse = moments(total[0:1], total[1:2], count)
    outer_moments(
        jnp.concatenate([moment_ref[0:1, :DIRECT], center], axis=1),
        jnp.concatenate([moment_ref[1:2, :DIRECT], inverse], axis=1),
        count,
        outer_ref,
    )
    matrix = pool_matrix(grid, small, False)
    gain, shift = (gain_ref[block : block + 1, DIRECT:], shift_ref[block : block + 1, DIRECT:])

    @pl.loop(0, pairs)
    def _(pair):
        slot = lax.rem(pair, 2)

        @pl.when(pair + 1 < pairs)
        def _():
            for copy in arriving(pair + 1, 1 - slot):
                copy.start()

        for copy in arriving(pair, slot):
            copy.wait()

        @pl.when(pair >= 2)
        def _():
            for copy in leaving(pair - 2, slot):
                copy.wait()

        acts, slopes, products = ([], [], [])
        for number in range(2):
            lines = slice(number * rows, (number + 1) * rows)
            values = jnp.concatenate([e_ref[slot, lines, :], q_ref[slot, lines, :]], axis=1)
            scaled, act, slope = normalize(values, center, inverse, gain, shift, mask)
            h_ref[slot, lines, :] = scaled.astype(BF16)
            low_slope = slope.astype(BF16)
            slope_ref[slot, lines, :] = low_slope
            acts.append(act.astype(BF16))
            slopes.append(low_slope)
            products.append((slope * scaled).astype(BF16))
        for copy in leaving(pair, slot):
            copy.start()
        at = rows_at(pair * small.line_rows, small.line_rows)
        pooled_ref[at, :] = pool_pieces(matrix, acts)
        pooled_slope_ref[at, :] = pool_pieces(matrix, slopes)
        pooled_product_ref[at, :] = pool_pieces(matrix, products)

    for pair in range(max(pairs - 2, 0), pairs):
        for copy in leaving(pair, pair % 2):
            copy.wait()


def second_pointwise(grid, slots, length_ref, place_ref, count_ref, *refs):
    directs, refs = (refs[: slots.parts], refs[slots.parts :])
    rest_ref, p_ref, q_ref, out_sums_ref, x_ref, plane_ref, sums_ref, pool_sums_ref = refs
    length = length_ref[0]
    rows = grid.line_rows
    sums_ref[...] = jnp.zeros_like(sums_ref)
    clear_edges(grid, plane_ref)
    x_ref[:, DIRECT:] = rest_ref[...]

    def visit(pair, ref, number):
        x_ref[rows_at(pair * rows, rows), 0:DIRECT] = ref[number * rows : (number + 1) * rows, :]

    each_pair(slots, place_ref[0], directs, visit)
    q_ref[...] = lax.dot_general(
        x_ref[...], p_ref[...], (((1,), (1,)), ((), ())), preferred_element_type=F32
    )

    @pl.loop(0, grid.side)
    def _(line):
        values = q_ref[rows_at(line * rows, rows), :]
        sums_ref[0:8] += partial_sum(values[:, :SECOND])
        sums_ref[8:16] += partial_sum(values[:, :SECOND] * values[:, :SECOND])
        plane_ref[rows_at((line + 1) * rows, rows), :] = plane_box(
            values[:, SECOND:], grid.unit
        )

    pool_planes(grid, plane_ref, q_ref, SECOND, pool_sums_ref, length, box_window(grid, length))
    write_sums(out_sums_ref, sums_ref, 0, SECOND)
    write_sums(out_sums_ref, pool_sums_ref, SECOND, FIRST)
    write_row(out_sums_ref, 2, 0, FIRST, jnp.full((1, FIRST), count_ref[0], F32))


def clear_ends(grid, ref):
    edge = jnp.zeros((grid.line_rows, ref.shape[1]), F32)
    ref[0 : grid.line_rows, :] = edge
    ref[grid.rows + grid.line_rows :, :] = edge


def store_copies(grid, ref, store):
    @pl.loop(0, grid.side + 1)
    def _(number):
        start = number * grid.line_rows
        at = rows_at(grid.lead + (number - 1) * grid.pitch, grid.line_rows)
        store(0, at, ref[rows_at(start, grid.line_rows), :])
        moved = pl.ds(pl.multiple_of(start + grid.unit, grid.unit), grid.line_rows)
        store(1, at, ref[moved, :])


def second_convolve(grid, block, length_ref, q_ref, sums_in_ref, gain_ref, shift_ref, *refs):
    far_kernels, outputs, moment_ref, scratch = (refs[:3], refs[3:8], refs[8], refs[9:])
    length = length_ref[0]
    center, inverse = set_moments(total_of(sums_in_ref), moment_ref)
    center, inverse = (center[:, DIRECT:SECOND], inverse[:, DIRECT:SECOND])
    gain, shift = (gain_ref[block : block + 1], shift_ref[block : block + 1])
    rows = grid.line_rows
    mask = grid.mask(rows, length, REDUCED)
    scratch, act_ref = (scratch[:-1], scratch[-1])

    def fill(h_ref, mid_ref, small_ref):
        clear_ends(grid, act_ref)

        @pl.loop(0, grid.side)
        def _(line):
            at = rows_at(line * rows, rows)
            scaled = (q_ref[at, DIRECT:SECOND] - center) * inverse
            h_ref[at, :] = scaled.astype(BF16)
            act_ref[rows_at((line + 1) * rows, rows), :] = silu(gain * scaled + shift) * mask

        def store(copy, at, values):
            store_taps(grid.unit, mid_ref, small_ref, copy, at, values)

        store_copies(grid, act_ref, store)

    run_convolution(grid, length, far_kernels, outputs, scratch, fill)


def second_output(grid, block, length_ref, q_ref, e_ref, moment_ref, sums_in_ref, gain_ref, shift_ref, cot_ref, act_ref, h_ref, error_ref, outer_ref, out_sums_ref, sums_ref):
    rows = grid.line_rows
    side, frames = (grid.side, cot_ref.shape[1])
    mask = grid.mask(rows, length_ref[0], OUTER)
    total = total_of(sums_in_ref)
    count = moment_ref[2:3, 0:SECOND]
    center, inverse = moments(total[0:1], total[1:2], count)
    center = jnp.concatenate([moment_ref[0:1, :DIRECT], center, moment_ref[0:1, SECOND:]], axis=1)
    inverse = jnp.concatenate([moment_ref[1:2, :DIRECT], inverse, moment_ref[1:2, SECOND:]], axis=1)
    outer_moments(center, inverse, count, outer_ref)
    sums_ref[...] = jnp.zeros_like(sums_ref)
    gain, shift = (gain_ref[block : block + 1], shift_ref[block : block + 1])
    gap = jnp.zeros((rows, 64), F32)
    unused = jnp.zeros((grid.unit, CHANNELS), F32)

    @pl.loop(0, side)
    def _(line):
        at = rows_at(line * rows, rows)
        places = pl.ds(line * side, side)
        values = jnp.concatenate([q_ref[at, :DIRECT], e_ref[at, :], q_ref[at, SECOND:]], axis=1)
        scaled = (values - center) * inverse
        h_ref[at, :] = scaled.astype(BF16)
        shifted = gain * scaled + shift
        gate = sigmoid(shifted)
        act = (shifted * gate * mask).reshape(side + 1, frames, OUTER)[:side].astype(BF16)
        act_ref[places, :, 0:576] = act[:, :, 0:576]
        act_ref[places, :, 576:CHANNELS] = act[:, :, 640:OUTER]
        slope = gate * (1.0 + shifted * (1.0 - gate))
        grad = cot_ref[places].astype(F32).reshape(side * frames, CHANNELS)
        grad = jnp.concatenate([grad, unused], axis=0)
        grad = jnp.concatenate([grad[:, :576], gap, grad[:, 576:]], axis=1)
        error = grad * slope * mask
        error_ref[at, :] = error.astype(BF16)
        sums_ref[0:8] += partial_sum(error)
        sums_ref[8:16] += partial_sum(error * scaled)

    write_sums(out_sums_ref, sums_ref, 0, OUTER)


def spread_matrix(grid, small):
    return None if small is None else pool_matrix(grid, small, True)[: grid.line_rows]


def outer_error(slopes, small, grad_ref, matrix, line, lo, hi):
    values = slopes.astype(F32)
    if small is None:
        return values
    coarse = grad_ref[rows_at((line // 2) * small.line_rows, small.line_rows), lo:hi]
    return values * jnp.dot(matrix, coarse, preferred_element_type=F32)


class Lines:
    def __init__(self, grid, sources, buffers, sem_ref):
        self.step = 2 if grid.side % 2 == 0 else 1
        self.size = self.step * grid.line_rows
        self.steps = grid.side // self.step
        self.sources, self.buffers, self.sem = (sources, buffers, sem_ref)

    def copies(self, step):
        at = rows_at(step * self.size, self.size)
        copies = []
        for number, ((ref, lo, hi), (buffer, place)) in enumerate(zip(self.sources, self.buffers)):
            source = ref(step, lo, hi) if callable(ref) else ref.at[at, pl.ds(lo, hi - lo)]
            target = buffer.at[at, pl.ds(place, hi - lo)]
            copies.append(pltpu.make_async_copy(source, target, self.sem.at[number, step]))
        return copies

    def first(self):
        @pl.loop(0, self.steps)
        def _(step):
            for copy in self.copies(step):
                copy.start()

    def run(self, visit):
        @pl.loop(0, self.steps)
        def _(step):
            for copy in self.copies(step):
                copy.wait()
            visit(step)

    @staticmethod
    def semaphores(grid, count):
        return pltpu.SemaphoreType.DMA((count, grid.side // 2 if grid.side % 2 == 0 else grid.side))


def second_back(grid, small, block, slots, length_ref, first_ref, h_far, outer_ref, sums_in_ref, gain_ref, slope_far, *refs):
    first = small is not None
    (grad_ref, carried_ref), refs = (refs[:2], refs[2:]) if first else ((None, None), refs)
    mid_far, few_far, d_far, total_ref, out_ref, *refs = refs
    d_ref, h_ref, slope_ref, mid_ref, few_ref, mid_acc_ref, small_acc_ref, turned_ref, sem_ref, in_sem, out_sem, *refs = refs
    lo, hi = (DIRECT, DIRECT + SECOND)
    at = 0 if first else DIRECT
    lines = Lines(
        grid,
        ((h_far, at, at + SECOND), (slope_far, at, at + SECOND)),
        ((h_ref, 0), (slope_ref, 0)),
        sem_ref,
    )
    lines.first()
    arriving = copies((mid_far, few_far), (mid_ref, few_ref), in_sem)
    for copy in arriving:
        copy.start()
    total = total_of(sums_in_ref)
    total_ref[...] = total
    a, b, c = before_norm(
        gain_ref[block : block + 1, lo:hi], outer_ref[1:2, lo:hi], total[:, lo:hi], outer_ref[2:3, lo:hi]
    )
    mask = grid.mask(grid.line_rows, length_ref[0], SECOND)
    matrix = spread_matrix(grid, small)
    clear_empty(grid, d_ref)
    rows = grid.line_rows
    if first:
        share = out_ref.shape[1] - carried_ref.shape[1]
        for clip in range(out_ref.shape[0]):
            out_ref[clip, share:, :] = carried_ref[clip]

    def visit(step):
        for number in range(lines.step):
            line = step * lines.step + number
            here = rows_at(line * rows, rows)
            scaled = h_ref[here, :].astype(F32)
            error = outer_error(slope_ref[here, :], small, grad_ref, matrix, line, lo, hi)
            back = (a * error - b - c * scaled) * mask
            if grid.copies == 1:
                d_ref[0, rows_at(grid.lead + line * grid.pitch, rows), :] = back.astype(BF16)
            else:
                refs[0][rows_at((line + 1) * rows, rows), :] = back

    lines.run(visit)
    if grid.copies > 1:
        clear_ends(grid, refs[0])

        def store(copy, at, values):
            d_ref[copy, at, :] = values.astype(BF16)

        store_copies(grid, refs[0], store)
    leaving = pltpu.make_async_copy(d_ref, d_far, out_sem.at[0])
    leaving.start()
    for copy in arriving:
        copy.wait()
    kernel_grads(grid, slots, first_ref, mid_ref, few_ref, d_ref, out_ref, mid_acc_ref, small_acc_ref, turned_ref)
    leaving.wait()


def before_norm(gain, inverse, sums, count):
    factor = gain * inverse
    return (factor, factor * sums[0:1] / count, factor * sums[1:2] / count)


def second_back_scratch(grid, slots):
    return [
        pltpu.VMEM((grid.copies, grid.padded, SECOND), BF16),
        pltpu.VMEM((grid.rows, SECOND), BF16),
        pltpu.VMEM((grid.rows, SECOND), BF16),
        pltpu.VMEM((grid.copies, grid.padded, 512), BF16),
        pltpu.VMEM((grid.copies, grid.padded, 128), BF16),
        pltpu.VMEM((slots, 384, 256), F32),
        pltpu.VMEM((slots, 128, 128), F32),
        pltpu.VMEM((MID_IN + 128, 128), F32),
        Lines.semaphores(grid, 2),
        pltpu.SemaphoreType.DMA((2,)),
        pltpu.SemaphoreType.DMA((1,)),
        *([pltpu.VMEM((grid.rows + 2 * grid.line_rows, SECOND), F32)] if grid.copies > 1 else []),
    ]


def conv_back(grid, slots, block, length_ref, d_ref, reduced_ref, reduced_gain_ref, reduced_shift_ref, *refs):
    far_kernels, refs = (refs[:3], refs[3:])
    first = len(refs) > 9
    x_far, refs = (refs[0], refs[1:]) if first else (None, refs)
    r_ref, out_sums_ref, *refs = refs
    product_out, refs = (refs[0], refs[1:]) if first else (None, refs)
    kernels, (last_ref, acc_ref, sums_ref, in_sem, *refs) = (refs[:3], refs[3:])
    if first:
        x_ref, product_ref, x_sem = refs
        x_copy = pltpu.make_async_copy(x_far, x_ref, x_sem.at[0])
        x_copy.start()
    main_ref, rest_ref, small_ref = kernels
    arriving = copies(far_kernels, kernels, in_sem)
    for copy in arriving:
        copy.start()
    rows = grid.line_rows
    group_rows = grid.group * grid.pitch
    sums_ref[...] = jnp.zeros_like(sums_ref)
    mask = grid.mask(rows, length_ref[0], REDUCED)
    gain, shift = (reduced_gain_ref[block : block + 1], reduced_shift_ref[block : block + 1])
    turned = (((1,), (1,)), ((), ()))
    lane = lax.broadcasted_iota(jnp.int32, (rows, 128), 1)
    wide_lane = lax.broadcasted_iota(jnp.int32, (grid.pitch, 128), 1)

    for copy in range(grid.copies):

        @pl.loop(1 - grid.copies, grid.side)
        def _(line):
            place = grid.lead + line * grid.pitch

            def lanes(start):
                return d_ref[copy, rows_at(start, grid.pitch), 256:384]

            further, here = (lanes(place + grid.pitch).astype(F32), lanes(place).astype(F32))
            at = rows_at(place, grid.pitch)
            last_ref[copy, at, 0:128] = jnp.where(
                wide_lane < 64, further, pltpu.roll(here, 64, 1)
            ).astype(BF16)
            last_ref[copy, at, 128:256] = lanes(place - grid.pitch)

        if grid.copies == 1:
            last_ref[copy, grid.lead - TILE : grid.lead, :] = jnp.zeros((TILE, 256), BF16)
        end = grid.lead + grid.side * grid.pitch
        last_ref[copy, end : end + TILE, :] = jnp.zeros((TILE, 256), BF16)
    for copy in arriving:
        copy.wait()

    @pl.loop(0, grid.side // grid.group)
    def _(group):
        base = grid.lead + group * group_rows
        for tap in range(9):
            part = lax.dot_general(
                near_tap(grid, d_ref, base, tap, -1, group_rows, slice(0, 256)),
                main_ref[tap],
                turned,
                preferred_element_type=F32,
            )
            acc_ref[:, 0:512] = part if tap == 0 else acc_ref[:, 0:512] + part
        for place in range(3):
            acc_ref[:, 0:512] += lax.dot_general(
                grid.near(last_ref, base, 0, 1 - place, group_rows),
                rest_ref[place],
                turned,
                preferred_element_type=F32,
            )
        near = [
            near_tap(grid, d_ref, base, tap, -1, group_rows, slice(384, 512)) for tap in range(9)
        ]
        acc_ref[:, 512:640] = jnp.dot(
            jnp.concatenate(near, axis=1), small_ref[...], preferred_element_type=F32
        )
        for number in range(grid.group):
            line = group * grid.group + number
            lines = slice(number * grid.pitch, number * grid.pitch + rows)
            rest, small = (acc_ref[lines, 384:512], acc_ref[lines, 512:640])
            one = jnp.where(lane < 32, rest, pltpu.roll(small, 32, 1))
            two = jnp.where(lane < 32, pltpu.roll(rest, 96, 1), small)
            three = jnp.where(lane < 32, pltpu.roll(rest, 64, 1), pltpu.roll(small, 96, 1))
            unit = grid.unit
            wide = later(acc_ref[lines, 0:128], unit) + acc_ref[lines, 128:256]
            wide = wide + earlier(acc_ref[lines, 256:384], unit)
            narrow = jnp.where(lane < 64, later(one, unit) + two + earlier(three, unit), 0.0)
            back = jnp.concatenate([wide, narrow], axis=1)
            at = rows_at(line * rows, rows)
            scaled = reduced_ref[at, :].astype(F32)
            error = back * silu_slope(gain * scaled + shift) * mask
            r_ref[at, :] = error.astype(BF16)
            sums_ref[0:8] += partial_sum(error)
            sums_ref[8:16] += partial_sum(error * scaled)

    write_sums(out_sums_ref, sums_ref, 0, REDUCED)
    if first:
        x_copy.wait()
        write_products(
            slots,
            x_ref,
            lambda start, size: r_ref[start : start + size, :],
            product_ref,
            product_out,
        )


def kernel_grads(grid, slots, first_ref, mid_ref, small_ref, d_ref, out_ref, mid_acc_ref, small_acc_ref, turned_ref):
    group_rows = grid.group * grid.pitch
    mid_acc_ref[...] = jnp.zeros_like(mid_acc_ref)
    small_acc_ref[...] = jnp.zeros_like(small_acc_ref)

    def neighbour(slot):
        return jnp.minimum(first_ref[0] + slot, TAPS - 1) // 9

    @pl.loop(0, grid.side // grid.group)
    def _(group):
        base = grid.lead + group * group_rows
        left = d_ref[0, rows_at(base, group_rows), :].T
        for slot in range(slots):
            tap = lax.rem(jnp.minimum(first_ref[0] + slot, TAPS - 1), 9)
            start = base + (tap // 3 - 1) * grid.pitch
            place = lax.rem(tap, 3) - 1
            copy = 0
            if grid.copies == 1:
                start = start + place * TILE
            else:
                copy = jnp.where(place == 0, 0, 1)
                start = start - jnp.where(place < 0, TILE, 0)
            at = rows_at(start, group_rows)
            lanes = pl.ds(pl.multiple_of(neighbour(slot) * 128, 128), 128)
            right = jnp.concatenate([mid_ref[copy, at, lanes], mid_ref[copy, at, 384:512]], axis=1)
            mid_acc_ref[slot] += jnp.dot(left[0:384], right, preferred_element_type=F32)
            small_acc_ref[slot] += jnp.dot(
                left[384:512], small_ref[copy, at, :], preferred_element_type=F32
            )

    share = round_up(slots * TAP_ROWS, 16 * out_ref.shape[0]) // out_ref.shape[0]

    def put(start, values):
        done = 0
        while done < values.shape[0]:
            clip, at = divmod(start + done, share)
            size = min(values.shape[0] - done, share - at)
            out_ref[clip, at : at + size, :] = values[done : done + size].astype(BF16)
            done = done + size

    half = MID_IN // 2
    for slot in range(slots):
        base = slot * TAP_ROWS
        rest = pl.ds(pl.multiple_of(neighbour(slot) * 32, 32), 32)
        for tile in range(3):
            lines = slice(128 * tile, 128 * (tile + 1))
            turned_ref[0:128, :] = mid_acc_ref[slot, lines, 0:128].T
            turned_ref[MID_IN : MID_IN + 128, :] = mid_acc_ref[slot, lines, 128:256].T
            turned_ref[128:MID_IN, :] = turned_ref[
                pl.ds(pl.multiple_of(MID_IN + neighbour(slot) * 32, 32), 32), :
            ]
            if tile < 2:
                put(base + MID_IN * tile, turned_ref[0:MID_IN, :])
            else:
                folded = turned_ref[0:half, :] + pltpu.roll(turned_ref[half:MID_IN, :], 64, 1)
                put(base + 2 * MID_IN, folded)
        turned_ref[0:128, :] = small_acc_ref[slot].T
        put(base + 2 * MID_IN + half, turned_ref[rest, :])
    used = slots * TAP_ROWS
    put(used, jnp.zeros((share * out_ref.shape[0] - used, 128), F32))


class Spread:
    def __init__(self, grid, plane_ref, across_ref, scale_ref, length):
        self.grid, self.plane, self.across, self.scale = (grid, plane_ref, across_ref, scale_ref)
        clear_edges(grid, plane_ref)
        window = box_window(grid, length)
        scale_ref[0] = box_scale(0, grid.side, window)
        scale_ref[1] = box_scale(1, grid.side, window)
        unit = grid.unit
        edge = jnp.zeros((unit, POOLED), F32)
        across_ref[0:unit, :] = edge
        across_ref[unit + grid.line_rows :, :] = edge

    def put(self, line, values):
        rows = self.grid.line_rows
        inner = jnp.where((line == 0) | (line == self.grid.side - 1), 0, 1)
        values = values * self.scale[inner]
        across, unit = (self.across, self.grid.unit)
        across[unit : unit + rows, :] = values + earlier(values, unit) + later(values, unit)
        self.plane[rows_at((line + 1) * rows, rows), :] = (
            across[0:rows, :] + across[unit : unit + rows, :] + across[2 * unit :, :]
        )

    def get(self, start, size):
        rows = self.grid.line_rows
        return (
            self.plane[rows_at(start, size), :]
            + self.plane[rows_at(start + rows, size), :]
            + self.plane[rows_at(start + 2 * rows, size), :]
        )

    @staticmethod
    def scratch(grid):
        return [
            pltpu.VMEM((grid.rows + 2 * grid.line_rows, POOLED), F32),
            pltpu.VMEM((grid.line_rows + 2 * grid.unit, POOLED), F32),
            pltpu.VMEM((2, grid.line_rows, POOLED), F32),
        ]


def channel_products(slots, x_ref, right_of):
    total = None
    for part in range(slots.parts):
        slot = part * slots.each
        pair = slot - (slots.empty if slot >= slots.gap + slots.empty else 0)
        pair = min(pair, slots.pairs - slots.each)
        product = jnp.dot(
            x_ref[part], right_of(pair * slots.pair_rows, slots.rows), preferred_element_type=F32
        )
        total = product if total is None else total + product
    return total


def write_products(slots, x_ref, right_of, product_ref, product_out):
    channels = x_ref.shape[1]
    product_ref[0:channels, :] = channel_products(slots, x_ref, right_of)
    product_ref[channels:, :] = jnp.zeros((product_ref.shape[0] - channels, product_ref.shape[1]), F32)
    clips, tiles, size, _ = product_out.shape
    for clip in range(clips):
        for tile in range(tiles):
            product_out[clip, tile] = product_ref[
                clip * size : (clip + 1) * size, 128 * tile : 128 * (tile + 1)
            ]


def rest_constants(outer_ref, total_ref, gain_ref, block):
    pool = OUTER - POOLED

    def pick(ref, lo, hi):
        return jnp.concatenate([ref[lo:hi, 0:DIRECT], ref[lo:hi, pool:]], axis=1)

    return before_norm(
        pick(gain_ref, block, block + 1), pick(outer_ref, 1, 2), pick(total_ref, 0, 2), pick(outer_ref, 2, 3)
    )


def point_back(grid, slots, block, kept, length_ref, place_ref, h_far, outer_ref, total_ref, gain_ref, error_far, reduced_far, r_far, moment_ref, sums_in_ref, reduced_gain_ref, x_far, p_far, *refs):
    pooled_slope_in, pooled_product_in, kept_far, *refs = refs
    dx_ref, dp_ref, reduced_total_ref, outer_sums_ref, *refs = refs
    h_ref, error_ref, reduced_ref, r_ref, x_ref, p_ref, du_ref, acc_ref, *refs = refs
    plane_ref, across_ref, scale_ref, sums_ref, pooled_slope_ref, pooled_product_ref, kept_ref, *refs = refs
    sem_ref, in_sem = refs
    rows = grid.line_rows
    pool = OUTER - POOLED
    lines = Lines(
        grid,
        (
            (h_far, 0, DIRECT),
            (h_far, pool, OUTER),
            (error_far, 0, DIRECT),
            (error_far, pool, OUTER),
            (reduced_far, 0, REDUCED),
            (r_far, 0, REDUCED),
        ),
        ((h_ref, 0), (h_ref, DIRECT), (error_ref, 0), (error_ref, DIRECT), (reduced_ref, 0), (r_ref, 0)),
        sem_ref,
    )
    lines.first()
    kept_rows = kept_ref.shape[1]
    arriving = copies(
        (x_far, p_far, kept_far.at[:, pl.ds(slots.rows, kept_rows), :]), (x_ref, p_ref, kept_ref), in_sem
    )
    for copy in arriving:
        copy.start()
    length = length_ref[0]
    total = total_of(sums_in_ref)
    reduced_total_ref[...] = total
    mid = before_norm(
        reduced_gain_ref[block : block + 1],
        moment_ref[1:2, DIRECT:SECOND],
        total,
        outer_ref[2:3, 0:REDUCED],
    )
    rest = rest_constants(outer_ref, total_ref, gain_ref, block)
    mask = grid.mask(rows, length, DIRECT + POOLED)
    spread = Spread(grid, plane_ref, across_ref, scale_ref, length)

    def visit(line):
        at = rows_at(line * rows, rows)
        back = rest[0] * error_ref[at, :].astype(F32) - rest[1] - rest[2] * h_ref[at, :].astype(F32)
        back = back * mask
        du_ref[at, 0:DIRECT] = back[:, :DIRECT].astype(BF16)
        spread.put(line, back[:, DIRECT:])
        back = mid[0] * r_ref[at, :].astype(F32) - mid[1] - mid[2] * reduced_ref[at, :].astype(F32)
        du_ref[at, DIRECT:SECOND] = (back * mask[:, :REDUCED]).astype(BF16)

    lines.run(visit)
    for copy in arriving:
        copy.wait()
    sums_ref[...] = jnp.zeros_like(sums_ref)
    pooled_slope_ref[:, DIRECT:] = pooled_slope_in[...]
    pooled_product_ref[:, DIRECT:] = pooled_product_in[...]
    for pair in range(slots.pairs):
        slot = pair + (slots.empty if pair >= slots.gap else 0)
        at = slice(pair * rows, (pair + 1) * rows)
        start = slot % slots.each * rows
        other = start + slots.each * rows
        pooled_slope_ref[at, 0:DIRECT] = kept_ref[slot // slots.each, start : start + rows, :]
        pooled_product_ref[at, 0:DIRECT] = kept_ref[slot // slots.each, other : other + rows, :]

    @pl.loop(0, grid.side)
    def _(line):
        at = rows_at(line * rows, rows)
        du_ref[at, SECOND:] = (spread.get(line * rows, rows) * mask[:, :POOLED]).astype(BF16)
        dx = jnp.dot(du_ref[at, :], p_ref[...], preferred_element_type=F32).astype(BF16)
        dx_ref[at, :] = dx
        for number, ref in enumerate((pooled_slope_ref, pooled_product_ref)):
            sums_ref[8 * number : 8 * number + 8] += partial_sum(
                dx.astype(F32) * ref[at, :].astype(F32)
            )

    write_sums(outer_sums_ref, sums_ref, 0, OUTER)
    acc_ref[...] = lax.dot_general(
        x_ref[...], du_ref[...], (((0,), (0,)), ((), ())), preferred_element_type=F32
    )
    start = pl.multiple_of(place_ref[0] * kept, 16) if kept < acc_ref.shape[0] else 0
    clips, size, _ = dp_ref.shape
    for tile in range(FIRST // 128):
        values = acc_ref[pl.ds(start, kept), 128 * tile : 128 * (tile + 1)].astype(BF16)
        done = 0
        while done < kept:
            clip, at = divmod(kept * tile + done, size)
            few = min(kept - done, size - at)
            dp_ref[clip, at : at + few, :] = values[done : done + few]
            done = done + few
    used = (FIRST // 128) * kept
    while used < clips * size:
        clip, at = divmod(used, size)
        dp_ref[clip, at:, :] = jnp.zeros((size - at, 128), BF16)
        used = used + size - at


def rest_back(grid, small, slots, block, length_ref, outer_ref, total_ref, gain_ref, shift_ref, grad_ref, h_far, slope_far, kept_far, x_far, reduced_far, du_far, product_out, *refs):
    h_ref, slope_ref, x_ref, reduced_ref, du_ref, plane_ref, across_ref, scale_ref, product_ref, sem_ref, in_sem, du_sem = refs
    rows = grid.line_rows
    pool = OUTER - POOLED

    def direct(step, lo, hi):
        slot = slots.slot_of(step)
        at = rows_at(lax.rem(slot, slots.each) * slots.pair_rows, slots.pair_rows)
        return kept_far.at[slot // slots.each, at, pl.ds(lo, hi - lo)]

    lines = Lines(
        grid,
        (
            (direct, 0, DIRECT),
            (h_far, SECOND, FIRST),
            (slope_far, SECOND, FIRST),
        ),
        ((h_ref, 0), (h_ref, DIRECT), (slope_ref, 0)),
        sem_ref,
    )
    lines.first()
    arriving = copies((x_far, reduced_far), (x_ref, reduced_ref), in_sem)
    for copy in arriving:
        copy.start()
    length = length_ref[0]
    matrix = spread_matrix(grid, small)
    a, b, c = rest_constants(outer_ref, total_ref, gain_ref, block)
    mask = grid.mask(rows, length, DIRECT + POOLED)
    gain = gain_ref[block : block + 1, 0:DIRECT]
    shift = shift_ref[block : block + 1, 0:DIRECT]
    spread = Spread(grid, plane_ref, across_ref, scale_ref, length)

    def visit(step):
        for number in range(lines.step):
            line = step * lines.step + number
            at = rows_at(line * rows, rows)
            coarse = grad_ref[rows_at((line // 2) * small.line_rows, small.line_rows), :]
            grad = jnp.dot(
                matrix,
                jnp.concatenate([coarse[:, :DIRECT], coarse[:, pool:]], axis=1),
                preferred_element_type=F32,
            )
            scaled = h_ref[at, :].astype(F32)
            slope = silu_slope(gain * scaled[:, :DIRECT] + shift)
            slope = jnp.concatenate([slope, slope_ref[at, :].astype(F32)], axis=1)
            back = a * (grad * slope) - b - c * scaled
            back = back * mask
            du_ref[at, 0:DIRECT] = back[:, :DIRECT].astype(BF16)
            spread.put(line, back[:, DIRECT:])

    lines.run(visit)
    for copy in arriving:
        copy.wait()
    wide = lines.size
    pool_mask = grid.mask(wide, length)

    def leaving(step):
        at = rows_at(step * wide, wide)
        return pltpu.make_async_copy(du_ref.at[at, :], du_far.at[at, :], du_sem.at[0])

    @pl.loop(0, lines.steps)
    def _(step):
        at = rows_at(step * wide, wide)
        du_ref[at, DIRECT:] = (spread.get(step * wide, wide) * pool_mask).astype(BF16)
        leaving(step).start()

    ones = grid.mask(slots.rows, length)
    two_ones = jnp.concatenate([ones, ones], axis=1)

    def right_of(start, size):
        at = slice(start, start + size)
        scaled = (reduced_ref[at, :].astype(F32) * two_ones).astype(BF16)
        return jnp.concatenate([du_ref[at, :], scaled, ones.astype(BF16)], axis=1)

    write_products(slots, x_ref, right_of, product_ref, product_out)
    pltpu.make_async_copy(du_ref, du_far, du_sem.at[0]).wait()


def mid_back(grid, block, length_ref, place_ref, moment_ref, sums_in_ref, gain_ref, du_far, h_far, r_far, p_far, dx_far, total_ref, *refs):
    du_ref, h_ref, r_ref, p_ref, dx_ref, sem_ref, p_sem, dx_sem = refs
    lines = Lines(
        grid,
        ((du_far, 0, DIRECT + POOLED), (h_far, 0, REDUCED), (r_far, 0, REDUCED)),
        ((du_ref, 0), (h_ref, 0), (r_ref, 0)),
        sem_ref,
    )
    lines.first()
    p_copy = pltpu.make_async_copy(p_far.at[place_ref[0]], p_ref, p_sem.at[0])
    p_copy.start()
    total = total_of(sums_in_ref)
    total_ref[...] = total
    a, b, c = before_norm(
        gain_ref[block : block + 1], moment_ref[1:2, DIRECT:], total, moment_ref[2:3, DIRECT:]
    )
    mask = grid.mask(lines.size, length_ref[0], REDUCED)
    p_copy.wait()

    def leaving(step):
        at = rows_at(step * lines.size, lines.size)
        return pltpu.make_async_copy(dx_ref.at[at, :], dx_far.at[at, :], dx_sem.at[0])

    def visit(step):
        at = rows_at(step * lines.size, lines.size)
        back = a * r_ref[at, :].astype(F32) - b - c * h_ref[at, :].astype(F32)
        du = jnp.concatenate(
            [du_ref[at, :DIRECT], (back * mask).astype(BF16), du_ref[at, DIRECT:]], axis=1
        )
        dx_ref[at, :] = jnp.dot(du, p_ref[...], preferred_element_type=F32).astype(BF16)
        leaving(step).start()

    lines.run(visit)
    pltpu.make_async_copy(dx_ref, dx_far, dx_sem.at[0]).wait()


def combine(block, rest_ref, pieces_ref, moment_ref, sums_in_ref, gain_ref, out_ref):
    total = total_of(sums_in_ref)
    a, b, c = before_norm(
        gain_ref[block : block + 1], moment_ref[1:2, DIRECT:], total, moment_ref[2:3, DIRECT:]
    )
    size = out_ref.shape[0] // 5
    rest, products = (total_of(rest_ref), total_of(pieces_ref))
    for tile in range(2):
        out_ref[size * tile : size * (tile + 1), :] = rest[tile].astype(BF16)
        lanes = slice(128 * tile, 128 * (tile + 1))
        mid = a[:, lanes] * products[tile] - b[:, lanes] * rest[5] - c[:, lanes] * rest[3 + tile]
        out_ref[size * (2 + tile) : size * (3 + tile), :] = mid.astype(BF16)
    out_ref[4 * size :, :] = rest[2].astype(BF16)


def write_taps(read, slots, arriving, mid_ref, small_ref, mid_out, small_out, sem_ref):
    half = MID_IN // 2

    def leaving(tap):
        return (
            pltpu.make_async_copy(mid_ref.at[tap], mid_out.at[tap], sem_ref.at[0]),
            pltpu.make_async_copy(small_ref.at[tap], small_out.at[tap], sem_ref.at[1]),
        )

    for tap in range(TAPS):
        part, slot = divmod(tap, slots)
        if slot == 0:
            arriving[part].wait()
        base = slot * TAP_ROWS
        folded = read(part, base + 2 * MID_IN, half)
        mid_ref[tap, :, 0:128] = read(part, base, MID_IN)
        mid_ref[tap, :, 128:256] = read(part, base + MID_IN, MID_IN)
        mid_ref[tap, 0:half, 256:320] = folded[:, 0:64]
        mid_ref[tap, half:MID_IN, 256:320] = pltpu.roll(folded, 64, 1)[:, 0:64]
        small_ref[tap] = read(part, base + 2 * MID_IN + half, SMALL_IN)
        for copy in leaving(tap):
            copy.start()
    for copy in arriving[-(-TAPS // slots) :]:
        copy.wait()
    return [
        pltpu.make_async_copy(mid_ref, mid_out, sem_ref.at[0]),
        pltpu.make_async_copy(small_ref, small_out, sem_ref.at[1]),
    ]


def parts_of(clips, far, ref, sem_ref):
    copies = []
    for part in range(far.shape[0] // clips):
        at = pl.ds(part * clips, clips)
        copies.append(pltpu.make_async_copy(far.at[at], ref.at[at], sem_ref.at[part]))
    for copy in copies:
        copy.start()
    return copies


def write_point(read, parts, kept, point_ref, wide_ref):
    for tile in range(FIRST // 128):
        for part in range(parts):
            start, stop = (kept * part, kept * (part + 1))
            values = read(part, kept * tile, kept)
            if kept * parts == CHANNELS:
                wide_ref[start:stop, :] = values
                continue
            for lo, hi, moved in ((0, 576, 0), (640, OUTER, 64)):
                lo, hi = (max(lo, start), min(hi, stop))
                if lo < hi:
                    wide_ref[lo - moved : hi - moved, :] = values[lo - start : hi - start]
        turned = wide_ref[...].T
        if tile < 3:
            point_ref[128 * tile : 128 * (tile + 1), :] = turned
        elif tile == 3:
            point_ref[384:448, :] = turned[0:64]
        else:
            point_ref[448:576, :] = turned


def copy_out(pairs, sem_ref):
    copies = [
        pltpu.make_async_copy(source, target, sem_ref.at[number])
        for number, (source, target) in enumerate(pairs)
    ]
    for copy in copies:
        copy.start()
    for copy in copies:
        copy.wait()


def share_reader(ref, clips, lo, share):
    def read(part, start, size):
        pieces, done = ([], 0)
        while done < size:
            clip, at = divmod(start + done, share)
            few = min(size - done, share - at)
            pieces.append(ref[part * clips + clip, lo + at : lo + at + few, :].astype(F32))
            done = done + few
        return pieces[0] if len(pieces) == 1 else jnp.concatenate(pieces, axis=0)

    return read


def unpack_second(clips, slots, far, mid_out, small_out, shares_ref, mid_ref, small_ref, sem_ref, in_sem):
    arriving = parts_of(clips, far, shares_ref, in_sem)
    read = share_reader(shares_ref, clips, 0, shares_ref.shape[1])
    leaving = write_taps(
        read, slots, arriving, mid_ref, small_ref, mid_out.at[1], small_out.at[1], sem_ref
    )
    for copy in leaving:
        copy.wait()


def unpack_first(parts, clips, slots, share, far, *refs):
    totals, refs = (refs[:4], refs[4:])
    mid_in, small_in, mid_out, small_out, point_out, gain_out, shift_out, *refs = refs
    shares_ref, mid_ref, small_ref, point_ref, wide_ref, sem_ref, in_sem = refs
    arriving = parts_of(clips, far, shares_ref, in_sem)
    for block in range(2):
        outer_ref, reduced_ref = totals[2 * block : 2 * block + 2]
        for row, out in enumerate((shift_out, gain_out)):
            at, line = (slice(block, block + 1), slice(row, row + 1))
            out[at, 0:256] = outer_ref[line, 0:256]
            out[at, 256:448] = reduced_ref[line, 0:192]
            out[at, 448:576] = outer_ref[line, 768:896]
            out[at, 576:896] = outer_ref[line, 256:576]
            out[at, 896:1024] = outer_ref[line, 640:768]
    read = share_reader(shares_ref, clips, 0, share)
    leaving = write_taps(
        read, slots, arriving, mid_ref, small_ref, mid_out.at[0], small_out.at[0], sem_ref
    )
    read = share_reader(shares_ref, clips, share, shares_ref.shape[1] - share)
    write_point(read, parts, OUTER // parts, point_ref, wide_ref)
    last = pltpu.make_async_copy(point_ref, point_out.at[1], sem_ref.at[2])
    last.start()
    for copy in (*leaving, last):
        copy.wait()


def unpack_point(parts, clips, kept, place_ref, clip_ref, mine_ref, other_ref, point_in, point_out, buffer_ref, point_ref, wide_ref, sem_ref):
    tiles = FIRST // 128
    size = buffer_ref.shape[2] // clips
    for chip in range(clips // 2):
        for step in range(parts):
            part = lax.rem(place_ref[0] - step + parts, parts)
            for swapped, ref in enumerate((mine_ref, other_ref)):
                owner = clip_ref[0] ^ (2 * chip) ^ swapped
                source = (chip * parts + step) * tiles * size
                for tile in range(tiles):
                    buffer_ref[part, tile, rows_at(owner * size, size), :] = ref[
                        source + tile * size : source + (tile + 1) * size, :
                    ]

    def read(part, start, size):
        tile, at = divmod(start, kept)
        return buffer_ref[part, tile, at : at + size, :].astype(F32)

    write_point(read, parts, kept, point_ref, wide_ref)
    last = pltpu.make_async_copy(point_ref, point_out.at[0], sem_ref.at[0])
    last.start()
    last.wait()


def prepare(parts, mid_in, small_in, point_in, gain_in, shift_in, *refs):
    kernels, (point_ref, second_ref, *vectors) = (refs[:8], refs[8:14])
    for block in range(2):
        main_ref, last_ref, few_ref, back_ref = kernels[4 * block : 4 * block + 4]

        @pl.loop(0, 9)
        def _(tap):
            for number in range(3):
                source = 9 * number + tap
                main_ref[tap, 128 * number : 128 * (number + 1), :] = mid_in[block, source, 0:128, 0:256]
                main_ref[tap, 384 + 32 * number : 416 + 32 * number, :] = mid_in[
                    block, source, 128:MID_IN, 0:256
                ]
            main_ref[tap, 480:512, :] = jnp.zeros((32, 256), BF16)
            small = jnp.concatenate(
                [small_in[block, 9 * number + tap] for number in range(3)]
                + [jnp.zeros((32, 128), BF16)],
                axis=0,
            )
            at = pl.ds(pl.multiple_of(tap * 128, 128), 128)
            few_ref[at, :] = small
            back_ref[at, :] = small.astype(F32).T.astype(BF16)

        @pl.loop(0, 3)
        def _(place):
            for number in range(3):
                for rows, start, size in (
                    (slice(0, 128), 128 * number, 128),
                    (slice(128, MID_IN), 384 + 32 * number, 32),
                ):
                    pieces = [
                        mid_in[block, 9 * number + 3 * line + place, rows, 256:MID_OUT].astype(F32)
                        for line in range(3)
                    ]
                    pieces.append(jnp.zeros((size, 64), F32))
                    last_ref[place, start : start + size, :] = jnp.concatenate(
                        pieces, axis=1
                    ).astype(BF16)
            last_ref[place, 480:512, :] = jnp.zeros((32, 256), BF16)

    own = point_ref.shape[2]
    for lo, hi, at in ((0, 448, 0), (448, SQUEEZED, SECOND)):
        values = point_in[0, lo:hi, :].astype(F32)
        for part in range(parts):
            point_ref[part, at : at + hi - lo, :] = values[:, own * part : own * (part + 1)].astype(
                BF16
            )
        values = point_in[1, lo:hi, :].astype(F32)
        gap = jnp.zeros((hi - lo, 64), F32)
        second_ref[at : at + hi - lo, :] = jnp.concatenate(
            [values[:, :576], gap, values[:, 576:]], axis=1
        ).astype(BF16)
    for part in range(parts):
        point_ref[part, 448:SECOND, :] = jnp.zeros((64, own), BF16)
    second_ref[448:SECOND, :] = jnp.zeros((64, OUTER), BF16)
    for source, outer, reduced in ((gain_in, vectors[0], vectors[1]), (shift_in, vectors[2], vectors[3])):
        outer[:, 0:256] = source[:, 0:256]
        outer[:, 256:576] = source[:, 576:896]
        outer[:, 576:640] = jnp.zeros((2, 64), F32)
        outer[:, 640:768] = source[:, 896:1024]
        outer[:, 768:896] = source[:, 448:576]
        reduced[:, 0:192] = source[:, 256:448]
        reduced[:, 192:256] = jnp.zeros((2, 64), F32)


def round_up(value, unit):
    return -(-value // unit) * unit


def spread_over(values, axis, size):
    received = [values]
    for step in range(1, size):
        perm = [(source, (source + step) % size) for source in range(size)]
        received.append(lax.ppermute(values, axis, perm))
    return received


def after(values, earlier):
    return lax.optimization_barrier((values, earlier))[0]


def exchange(values):
    return lax.all_to_all(values, "dp", 0, 0, tiled=True)


def add_up(pieces):
    return jnp.sum(pieces.astype(F32), axis=0).astype(BF16)


def gather_chips(column, clips, work=None):
    columns = [column]
    for chip in range(1, clips // 2):
        perm = [(source, source ^ (2 * chip)) for source in range(clips)]
        columns.append(lax.ppermute(column, "dp", perm))
    if work is not None:
        columns = after(columns, work)
    mine = jnp.concatenate(columns, axis=0)
    other = lax.ppermute(mine, "dp", [(source, source ^ 1) for source in range(clips)])
    return (mine, other)


def on_device(frames, lengths, cotangent, pointwise, conv_mid, conv_small, gains, shifts):
    parts = lax.axis_size("branch")
    clips = lax.axis_size("dp")
    place = lax.axis_index("branch").astype(jnp.int32)
    side = frames.shape[2]
    grid, small = (Grid(side, frames.shape[1]), Grid(side // 2, frames.shape[1] // 2))
    slots = Slots(grid, parts)
    cells = side * side
    own_channels = frames.shape[-1]
    length = lengths.astype(jnp.int32)
    half_length = length // 2
    place_one = place.reshape(1)

    own = frames[0].transpose(1, 2, 0, 3).reshape(grid.rows, own_channels)
    turned = call(functools.partial(turn, slots), shape((parts, own_channels, slots.rows), BF16))(own)
    by_pairs = lax.all_to_all(turned, "branch", 0, 0, tiled=True)
    kernel_shapes = (
        shape((9, 512, 256), BF16),
        shape((3, 512, 256), BF16),
        shape((1152, 128), BF16),
        shape((1152, 128), BF16),
    )
    prepared = call(
        functools.partial(prepare, parts),
        (
            *kernel_shapes,
            *kernel_shapes,
            shape((parts, FIRST, own_channels), BF16),
            shape((FIRST, OUTER), BF16),
            shape((2, OUTER), F32),
            shape((2, REDUCED), F32),
            shape((2, OUTER), F32),
            shape((2, REDUCED), F32),
        ),
    )(conv_mid, conv_small, pointwise.swapaxes(1, 2), gains, shifts)
    kernels = (prepared[0:4], prepared[4:8])
    point_first, point_second, outer_gain, reduced_gain, outer_shift, reduced_shift = prepared[8:]

    local_count = (length * (slots.held(place) * 2 * side)).astype(F32)
    mid, pool, direct, sums = call(
        functools.partial(first_pointwise, slots),
        (
            shape((mid_rows(slots), 128), BF16),
            shape((slots.rows + TILE, POOLED), BF16),
            shape((slots.rows, DIRECT), F32),
            shape((clips, 3, SECOND), F32),
        ),
        [pltpu.VMEM((slots.rows, FIRST), F32)],
        scalars=2,
        vmem=VMEM_BYTES // 3,
    )(length, local_count, by_pairs, point_first)
    mids = spread_over(mid, "branch", parts)
    sums = spread_over(jnp.sum(exchange(sums), axis=0), "branch", parts)
    pools = spread_over(after(pool, (mids, sums)), "branch", parts)
    h_reduced, taps_mid, taps_few, e, e_sums = call(
        functools.partial(first_convolve, grid, slots, 0),
        conv_outputs(grid),
        conv_scratch(grid),
        scalars=2,
        cost=40,
        far=range(4 + 2 * parts, 7 + 2 * parts),
        far_out=range(4),
    )(length, place_one, *mids, *sums, reduced_gain, reduced_shift, *kernels[0][:3])
    q_pool, second_sums = call(
        functools.partial(first_pool, grid, slots),
        (shape((grid.rows, POOLED), F32), shape((clips, 2, FIRST), F32)),
        [
            pltpu.VMEM((grid.rows + 2 * grid.line_rows, POOLED), F32),
            pltpu.VMEM((16, POOLED), F32),
        ],
        scalars=2,
    )(length, place_one, *pools, e_sums)
    second_sums = exchange(second_sums)
    pooled_direct, kept_direct, moment = call(
        functools.partial(first_direct, grid, small, slots, 0),
        (
            shape((slots.each * small.line_rows, DIRECT), BF16),
            shape((slots.rows + 2 * slots.each * small.line_rows, DIRECT), BF16),
            shape((3, SECOND), F32),
        ),
        scalars=1,
        cost=3,
    )(length, direct, outer_gain, outer_shift, *sums)
    second_sums, pooled_direct = lax.optimization_barrier((second_sums, pooled_direct))
    pooled_directs = spread_over(pooled_direct, "branch", parts)
    kept_direct = lax.all_gather(after(kept_direct, second_sums), "branch", axis=0)
    pair = 2 * grid.line_rows
    pooled, h_outer, slope, outer, pooled_slope, pooled_product = call(
        functools.partial(first_output, grid, small, 0),
        (
            shape((small.rows, FIRST), BF16),
            shape((grid.rows, FIRST), BF16),
            shape((grid.rows, FIRST), BF16),
            shape((3, OUTER), F32),
            shape((small.rows, FIRST), BF16),
            shape((small.rows, FIRST), BF16),
        ),
        [
            pltpu.VMEM((2, pair, POOLED), F32),
            pltpu.VMEM((2, pair, SECOND), F32),
            pltpu.VMEM((2, pair, FIRST), BF16),
            pltpu.VMEM((2, pair, FIRST), BF16),
            *[pltpu.SemaphoreType.DMA((2,))] * 4,
        ],
        scalars=1,
        far=(1, 2),
        far_out=(1, 2),
    )(
        length,
        q_pool,
        e,
        moment,
        second_sums,
        outer_gain,
        outer_shift,
    )

    small_count = half_length.astype(F32) * float(small.side * small.side)
    q_small, sums_small, pooled = call(
        functools.partial(second_pointwise, small, slots),
        (
            shape((small.rows, FIRST), F32),
            shape((clips, 3, FIRST), F32),
            shape((small.rows, OUTER), BF16),
        ),
        [
            pltpu.VMEM((small.rows + 2 * small.line_rows, POOLED), F32),
            pltpu.VMEM((16, SECOND), F32),
            pltpu.VMEM((16, POOLED), F32),
        ],
        scalars=3,
    )(half_length, place_one, small_count, *pooled_directs, pooled, point_second)
    sums_small = exchange(sums_small)
    h_reduced_small, taps_mid_small, taps_few_small, e_small, e_sums_small, moment_small = call(
        functools.partial(second_convolve, small, 1),
        (*conv_outputs(small, clips), shape((3, FIRST), F32)),
        [*conv_scratch(small), pltpu.VMEM((small.rows + 2 * small.line_rows, REDUCED), F32)],
        scalars=1,
        far=range(5, 8),
        far_out=range(4),
    )(half_length, q_small, sums_small, reduced_gain, reduced_shift, *kernels[1][:3])
    e_sums_small = exchange(e_sums_small)
    cot = cotangent[0].transpose(1, 2, 0, 3).reshape(small.side**2, cotangent.shape[1], CHANNELS)
    act, h_outer_small, error_small, outer_small, outer_sums_small = call(
        functools.partial(second_output, small, 1),
        (
            shape(cot.shape, BF16),
            shape((small.rows, OUTER), BF16),
            shape((small.rows, OUTER), BF16),
            shape((3, OUTER), F32),
            shape((clips, 2, OUTER), F32),
        ),
        [pltpu.VMEM((16, OUTER), F32)],
        scalars=1,
    )(half_length, q_small, e_small, moment_small, e_sums_small, outer_gain, outer_shift, cot)

    taps_each = -(-TAPS // parts)
    tap_share = round_up(taps_each * TAP_ROWS, 16 * clips) // clips
    first_tap = place_one * taps_each

    def conv_back_scratch(at):
        return [
            pltpu.VMEM((9, 512, 256), BF16),
            pltpu.VMEM((3, 512, 256), BF16),
            pltpu.VMEM((1152, 128), BF16),
            pltpu.VMEM((at.copies, at.padded, 256), BF16),
            pltpu.VMEM((at.group * at.pitch, FIRST), F32),
            pltpu.VMEM((16, REDUCED), F32),
            pltpu.SemaphoreType.DMA((3,)),
        ]

    gathered = exchange(outer_sums_small)
    d_low, total_small, packed_small = call(
        functools.partial(second_back, small, None, 1, taps_each),
        (
            shape((small.copies, small.padded, SECOND), BF16),
            shape((2, OUTER), F32),
            shape((clips, tap_share, 128), BF16),
        ),
        second_back_scratch(small, taps_each),
        scalars=2,
        cost=8,
        far=(2, 6, 7, 8),
        far_out=(0,),
    )(
        half_length,
        first_tap,
        h_outer_small,
        outer_small,
        gathered,
        outer_gain,
        error_small,
        taps_mid_small,
        taps_few_small,
    )
    r_low, sums_low = call(
        functools.partial(conv_back, small, None, 1),
        (shape((small.rows, REDUCED), BF16), shape((clips, 2, REDUCED), F32)),
        conv_back_scratch(small),
        scalars=1,
        cost=8,
        far=(5, 6, 7),
    )(
        half_length,
        d_low,
        h_reduced_small,
        reduced_gain,
        reduced_shift,
        *kernels[1][:2],
        kernels[1][3],
    )
    share_small = add_up(exchange(packed_small))
    sums_low, share_small = lax.optimization_barrier((sums_low, share_small))
    gathered = exchange(sums_low)
    kept = OUTER // parts
    point_share = round_up(kept * (FIRST // 128), 16 * clips) // clips
    coarse_rows = slots.each * small.line_rows
    dx_small, point_packed, reduced_total_small, outer_sums = call(
        functools.partial(point_back, small, slots, 1, kept),
        (
            shape((small.rows, OUTER), BF16),
            shape((clips, point_share, 128), BF16),
            shape((2, REDUCED), F32),
            shape((clips, 2, OUTER), F32),
        ),
        [
            pltpu.VMEM((small.rows, DIRECT + POOLED), BF16),
            pltpu.VMEM((small.rows, DIRECT + POOLED), BF16),
            pltpu.VMEM((small.rows, REDUCED), BF16),
            pltpu.VMEM((small.rows, REDUCED), BF16),
            pltpu.VMEM((small.rows, OUTER), BF16),
            pltpu.VMEM((FIRST, OUTER), BF16),
            pltpu.VMEM((small.rows, FIRST), BF16),
            pltpu.VMEM((OUTER, FIRST), F32),
            *Spread.scratch(small),
            pltpu.VMEM((16, OUTER), F32),
            pltpu.VMEM((small.rows, OUTER), BF16),
            pltpu.VMEM((small.rows, OUTER), BF16),
            pltpu.VMEM((parts, 2 * coarse_rows, DIRECT), BF16),
            Lines.semaphores(small, 6),
            pltpu.SemaphoreType.DMA((3,)),
        ],
        scalars=2,
        cost=10,
        far=(2, 6, 7, 8, 12, 13, 16),
    )(
        half_length,
        place_one,
        h_outer_small,
        outer_small,
        total_small,
        outer_gain,
        error_small,
        h_reduced_small,
        r_low,
        moment_small,
        gathered,
        reduced_gain,
        pooled,
        point_second,
        pooled_slope,
        pooled_product,
        kept_direct,
    )
    whole_small = lax.all_gather(share_small, ("branch", "dp"), axis=0)

    gathered = exchange(outer_sums)
    d_low, total, packed = call(
        functools.partial(second_back, grid, small, 0, taps_each),
        (
            shape((grid.copies, grid.padded, SECOND), BF16),
            shape((2, OUTER), F32),
            shape((clips, tap_share + point_share, 128), BF16),
        ),
        second_back_scratch(grid, taps_each),
        scalars=2,
        cost=18,
        far=(2, 6, 9, 10),
        far_out=(0,),
    )(length, first_tap, h_outer, outer, gathered, outer_gain, slope, dx_small, point_packed, taps_mid, taps_few)
    product_rows = round_up(own_channels, 16 * clips)
    du_rest, rest_product = call(
        functools.partial(rest_back, grid, small, slots, 0),
        (
            shape((grid.rows, DIRECT + POOLED), BF16),
            shape((clips, 6, product_rows // clips, 128), F32),
        ),
        [
            pltpu.VMEM((grid.rows, DIRECT + POOLED), BF16),
            pltpu.VMEM((grid.rows, POOLED), BF16),
            pltpu.VMEM(turned.shape, BF16),
            pltpu.VMEM((grid.rows, REDUCED), BF16),
            pltpu.VMEM((grid.rows, DIRECT + POOLED), BF16),
            *Spread.scratch(grid),
            pltpu.VMEM((product_rows, 768), F32),
            Lines.semaphores(grid, 3),
            pltpu.SemaphoreType.DMA((2,)),
            pltpu.SemaphoreType.DMA((1,)),
        ],
        scalars=1,
        cost=8,
        far=(6, 7, 8, 9, 10),
        far_out=(0,),
    )(length, outer, after(total, packed), outer_gain, outer_shift, dx_small, h_outer, slope, kept_direct, turned, h_reduced)
    share = add_up(exchange(packed))
    rest_pieces = exchange(rest_product)
    d_low, share = lax.optimization_barrier((after(d_low, rest_product), share))
    r_low, sums_low, products = call(
        functools.partial(conv_back, grid, slots, 0),
        (
            shape((grid.rows, REDUCED), BF16),
            shape((clips, 2, REDUCED), F32),
            shape((clips, 2, product_rows // clips, 128), F32),
        ),
        [
            *conv_back_scratch(grid),
            pltpu.VMEM(turned.shape, BF16),
            pltpu.VMEM((product_rows, REDUCED), F32),
            pltpu.SemaphoreType.DMA((1,)),
        ],
        scalars=1,
        cost=22,
        far=(5, 6, 7, 8),
    )(
        length,
        d_low,
        h_reduced,
        reduced_gain,
        reduced_shift,
        *kernels[0][:2],
        kernels[0][3],
        turned,
    )
    whole = lax.all_gather(share, ("branch", "dp"), axis=0)
    sums_low, rest_pieces = lax.optimization_barrier((sums_low, rest_pieces))
    gathered = exchange(sums_low)
    pieces = exchange(products)
    dx, reduced_total = call(
        functools.partial(mid_back, grid, 0),
        (shape((grid.rows, own_channels), BF16), shape((2, REDUCED), F32)),
        [
            pltpu.VMEM((grid.rows, DIRECT + POOLED), BF16),
            pltpu.VMEM((grid.rows, REDUCED), BF16),
            pltpu.VMEM((grid.rows, REDUCED), BF16),
            pltpu.VMEM((FIRST, own_channels), BF16),
            pltpu.VMEM((grid.rows, own_channels), BF16),
            Lines.semaphores(grid, 3),
            pltpu.SemaphoreType.DMA((1,)),
            pltpu.SemaphoreType.DMA((1,)),
        ],
        scalars=2,
        cost=8,
        far=(5, 6, 7, 8),
        far_out=(0,),
    )(length, place_one, moment, gathered, reduced_gain, du_rest, h_reduced, r_low, point_first)
    pieces, dx = lax.optimization_barrier((pieces, dx))
    point_sum = call(
        functools.partial(combine, 0),
        shape((5 * product_rows // clips, 128), BF16),
        cost=1,
        vmem=VMEM_BYTES // 3,
    )(rest_pieces, pieces, moment, gathered, reduced_gain)
    received = spread_over(point_sum, "branch", parts)

    outs = (
        shape((2, TAPS, MID_IN, MID_OUT), F32),
        shape((2, TAPS, SMALL_IN, SMALL_OUT), F32),
        shape((2, SQUEEZED, CHANNELS), F32),
    )
    tap_scratch = [
        pltpu.VMEM((TAPS, MID_IN, MID_OUT), F32),
        pltpu.VMEM((TAPS, SMALL_IN, SMALL_OUT), F32),
    ]
    point_scratch = [pltpu.VMEM((SQUEEZED, CHANNELS), F32), pltpu.VMEM((CHANNELS, 128), F32)]
    mid_grad, small_grad = call(
        functools.partial(unpack_second, clips, taps_each),
        outs[:2],
        [
            pltpu.VMEM(whole_small.shape, BF16),
            *tap_scratch,
            pltpu.SemaphoreType.DMA((2,)),
            pltpu.SemaphoreType.DMA((parts,)),
        ],
        far=(0,),
        far_out=(0, 1),
        cost=5,
    )(whole_small)
    received, mid_grad, small_grad = lax.optimization_barrier((received, mid_grad, small_grad))
    norms = shape((2, 1024), F32)
    mid_grad, small_grad, point_grad, gain_grad, shift_grad = call(
        functools.partial(unpack_first, parts, clips, taps_each, tap_share),
        (*outs, norms, norms),
        [
            pltpu.VMEM(whole.shape, BF16),
            *tap_scratch,
            *point_scratch,
            pltpu.SemaphoreType.DMA((3,)),
            pltpu.SemaphoreType.DMA((parts,)),
        ],
        far=(0,),
        far_out=(0, 1, 2),
        aliases={5: 0, 6: 1},
        cost=6,
    )(whole, total, reduced_total, total_small, reduced_total_small, mid_grad, small_grad)
    point_mine, point_other = gather_chips(
        jnp.concatenate(received, axis=0), clips, (mid_grad, small_grad)
    )
    clip_one = lax.axis_index("dp").astype(jnp.int32).reshape(1)
    point_grad = call(
        functools.partial(unpack_point, parts, clips, own_channels),
        outs[2],
        [
            pltpu.VMEM((parts, FIRST // 128, product_rows, 128), BF16),
            *point_scratch,
            pltpu.SemaphoreType.DMA((1,)),
        ],
        scalars=2,
        far_out=(0,),
        aliases={4: 0},
        cost=3,
        vmem=VMEM_BYTES // 2,
    )(place_one, clip_one, point_mine, point_other, point_grad)
    act = act.reshape(small.side, small.side, cotangent.shape[1], CHANNELS).transpose(2, 0, 1, 3)
    input_grad = dx.reshape(side, side, grid.unit, own_channels).transpose(2, 0, 1, 3)
    return (
        act[None],
        input_grad[None],
        point_grad.swapaxes(1, 2),
        mid_grad,
        small_grad,
        gain_grad,
        shift_grad,
    )


def solution(mesh):
    split = P("dp", None, None, None, "branch")
    whole = P("dp", None, None, None, None)
    return jax.shard_map(
        on_device,
        mesh=mesh,
        in_specs=(split, P("dp"), whole, P(), P(), P(), P(), P()),
        out_specs=(whole, split, P(), P(), P(), P(), P()),
        check_vma=False,
    )
```
